128 devices in a mesh: head: 4 (over z), blk: 32 (over y, x, core).
Axes of the slice: x: 4, y: 4, z: 4, core: 2. Of those that a mesh axis runs over, the one named last changes fastest.
Arguments:
- tokens: bfloat16 [32, 512, 2048], P('blk', 'head'), may hold values from -6 to 6
- segments: int32 [32, 512], replicated, may hold values from 0 to 15, as said below
- w_query: bfloat16 [2048, 2048], P('blk', 'head'), may hold values from -0.125 to 0.125
- key_projection: bfloat16 [2048, 256], P('blk', 'head'), may hold values from -0.125 to 0.125
- value_projection: bfloat16 [2048, 256], P('blk', 'head'), may hold values from -0.125 to 0.125
- w_out: bfloat16 [2048, 2048], P('head', 'blk'), may hold values from -1.5 to 1.5
- w_gate: bfloat16 [2048, 5632], P('blk', 'head'), may hold values from -0.125 to 0.125
- w_up: bfloat16 [2048, 5632], P('blk', 'head'), may hold values from -0.125 to 0.125
- w_down: bfloat16 [5632, 2048], P('head', 'blk'), may hold values from -0.078125 to 0.078125
- norm_attn: bfloat16 [2048], replicated, may hold values from 0.099609375 to 1.8984375
- norm_ffn: bfloat16 [2048], replicated, may hold values from 0.099609375 to 1.8984375
- cotangent: bfloat16 [32, 512, 2048], P('blk', 'head'), may hold values from -6 to 6
Outputs:
- output: bfloat16 [32, 512, 2048], P('blk', 'head')
- grad_tokens: bfloat16 [32, 512, 2048], P('blk', 'head')
- grad_w_query: float32 [2048, 2048], P('blk', 'head')
- grad_w_key: float32 [2048, 256], P('blk', 'head')
- grad_w_value: float32 [2048, 256], P('blk', 'head')
- grad_w_out: float32 [2048, 2048], P('head', 'blk')
- grad_w_gate: float32 [2048, 5632], P('blk', 'head')
- grad_w_up: float32 [2048, 5632], P('blk', 'head')
- grad_w_down: float32 [5632, 2048], P('head', 'blk')
- grad_norm_attn: float32 [2048], replicated
- grad_norm_ffn: float32 [2048], replicated
The draws below stay inside these ranges and needn't reach their ends.
Inputs may be any that keep to these rules, and one draw needn't show every extreme that they name: `segments`: read in order of blocks and rows, the document numbers never fall; they begin at 0 and end at 15.
All inputs are finite; a program needn't handle non-finite values.
Results may differ from the reference program's by a relative error of at most 0.025.
Values may be sent and summed in bfloat16 or wider, within the bound.
No kernel may reach another device: no remote copies, remote signals or barrier semaphores. Data moves between devices by JAX's collectives and lax.ppermute only.
A program may use at most 192 MiB of HBM per device.

```python
import jax
import jax.numpy as jnp
from jax import lax

MODEL_WIDTH = 2048
QUERY_HEAD_COUNT = 32
KEY_VALUE_HEADS = 4
HEAD_SIZE = 64
FF = 5632
WINDOW = 1024
BLOCKS = 32
BLOCK = 512
PACKED_TOKENS = 16384
DOCS = 16
REACH = 2


def draw_segments(key, part):
    key = jax.random.fold_in(key, 7)
    order = jax.random.permutation(key, PACKED_TOKENS - 1).astype(jnp.int32)
    cuts = order[:DOCS - 1] + 1
    token_positions = jnp.arange(PACKED_TOKENS, dtype=jnp.int32)
    numbers = jnp.sum((token_positions[:, None] >= cuts[None, :]).astype(jnp.int32), 1)
    return numbers.reshape(BLOCKS, BLOCK)


def levels(rng, dims, cuts, smallest, high):
    factor_of, own = 1.0, jax.random.fold_in(rng, 6)
    for position, blocks in cuts:
        draws = jnp.exp(jax.random.uniform(jax.random.fold_in(own, position), (blocks,), jnp.float32, smallest / len(cuts), high / len(cuts)))
        factor_of = factor_of * jnp.repeat(draws, dims[position] // blocks).reshape([-1 if axis == position else 1 for axis in range(len(dims))])
    return factor_of


def noise(own_key, shape, width, reach, split=(), kind=jnp.bfloat16):
    values = jax.random.normal(own_key, shape, jnp.float32) * width
    if len(split) > 0:
        values = levels(own_key, shape, split, -0.22, 0.18) * values
    return jnp.clip(values, min=-reach, max=reach).astype(kind)


def setup_inputs(seed: int = 0) -> dict:
    seeds = jax.random.split(jax.random.key(seed), 13)
    return {
        "tokens": noise(seeds[0], (BLOCKS, BLOCK, MODEL_WIDTH), 1.0, 6.0, ((0, 32), (1, 4))),
        "segments": draw_segments(jax.random.fold_in(seeds[12], 71), 0),
        "w_query": noise(seeds[2], (MODEL_WIDTH, QUERY_HEAD_COUNT * HEAD_SIZE), MODEL_WIDTH ** -0.5, 0.125, ((0, 32), (1, 4))),
        "key_projection": noise(seeds[3], (MODEL_WIDTH, KEY_VALUE_HEADS * HEAD_SIZE), MODEL_WIDTH ** -0.5, 0.125, ((0, 32), (1, 4))),
        "value_projection": noise(seeds[4], (MODEL_WIDTH, KEY_VALUE_HEADS * HEAD_SIZE), MODEL_WIDTH ** -0.5, 0.125, ((0, 32), (1, 4))),
        "w_out": noise(seeds[5], (QUERY_HEAD_COUNT * HEAD_SIZE, MODEL_WIDTH), 16 ** -0.5, 1.5, ((0, 4), (1, 32))),
        "w_gate": noise(seeds[6], (MODEL_WIDTH, FF), MODEL_WIDTH ** -0.5, 0.125, ((0, 32), (1, 4))),
        "w_up": noise(seeds[7], (MODEL_WIDTH, FF), MODEL_WIDTH ** -0.5, 0.125, ((0, 32), (1, 4))),
        "w_down": noise(seeds[8], (FF, MODEL_WIDTH), FF ** -0.5, 0.078125, ((0, 4), (1, 32))),
        "norm_attn": jnp.clip(1.0 + 0.18 * jax.random.normal(seeds[9], (MODEL_WIDTH,), jnp.float32), 0.099609375, 1.8984375).astype(jnp.bfloat16),
        "norm_ffn": jnp.clip(1.0 + 0.18 * jax.random.normal(seeds[10], (MODEL_WIDTH,), jnp.float32), 0.099609375, 1.8984375).astype(jnp.bfloat16),
        "cotangent": noise(seeds[11], (BLOCKS, BLOCK, MODEL_WIDTH), 1.0, 6.0, ((0, 32), (1, 4))),
    }


epsilon = 1e-05

@jax.custom_vjp
def reduced_precision(v):
    return lax.optimization_barrier(v.astype(jnp.bfloat16)).astype(jnp.float32)

@jax.custom_vjp
def reduced_backward(v):
    return v

def low_keep(v):
    return (reduced_precision(v), None)

def low_pass(kept, grad):
    return (grad,)

def back_keep(v):
    return (v, None)

def back_low(kept, grad):
    return (reduced_precision(grad),)
reduced_precision.defvjp(low_keep, low_pass)
reduced_backward.defvjp(back_keep, back_low)

def matrix_multiply(former, latter):
    return jnp.dot(former, latter, precision=lax.Precision.HIGHEST)

def normalize(value_vectors, gain_vector):
    inv_root = lax.rsqrt(lax.optimization_barrier(jnp.mean(value_vectors * value_vectors, -1, keepdims=True)) + epsilon)
    return value_vectors * inv_root * gain_vector

def apply_rotary(value_vectors, token_positions):
    half_size = HEAD_SIZE // 2
    frequency = 10000.0 ** (-jnp.arange(half_size, dtype=jnp.float32) * 2.0 / HEAD_SIZE)
    angles = token_positions.astype(jnp.float32)[:, None] * frequency[None, :]
    cosine_table = jnp.cos(angles)[:, None, :]
    sine_table = jnp.sin(angles)[:, None, :]
    first_half = value_vectors[..., :half_size]
    second_half = value_vectors[..., half_size:]
    return jnp.concatenate([first_half * cosine_table - second_half * sine_table, second_half * cosine_table + first_half * sine_table], -1)

def attention(queries, key_vectors, value_vectors, segments):
    heads_per_group = QUERY_HEAD_COUNT // KEY_VALUE_HEADS
    scale_factor = HEAD_SIZE ** (-0.5)
    padding_rows = REACH * BLOCK
    key_rows = (REACH + 1) * BLOCK
    padded_keys = jnp.concatenate([jnp.zeros((padding_rows, KEY_VALUE_HEADS, HEAD_SIZE), jnp.float32), key_vectors], 0)
    padded_values = jnp.concatenate([jnp.zeros((padding_rows, KEY_VALUE_HEADS, HEAD_SIZE), jnp.float32), value_vectors], 0)
    flat_segments = segments.reshape(-1).astype(jnp.int32)
    segments_pad = jnp.concatenate([jnp.full((padding_rows,), -1, jnp.int32), flat_segments])

    def one_block(block_number):
        offset = block_number * BLOCK
        query_block = lax.dynamic_slice_in_dim(queries, offset, BLOCK, 0)
        key_block = jnp.repeat(lax.dynamic_slice_in_dim(padded_keys, offset, key_rows, 0), heads_per_group, axis=1)
        value_block = jnp.repeat(lax.dynamic_slice_in_dim(padded_values, offset, key_rows, 0), heads_per_group, axis=1)
        scores = reduced_backward(jnp.einsum('qhd,khd->hqk', query_block, key_block, precision=lax.Precision.HIGHEST) * scale_factor)
        query_positions = offset + jnp.arange(BLOCK, dtype=jnp.int32)
        key_positions = offset - padding_rows + jnp.arange(key_rows, dtype=jnp.int32)
        query_segments = lax.dynamic_slice_in_dim(flat_segments, offset, BLOCK, 0)
        key_segments = lax.dynamic_slice_in_dim(segments_pad, offset, key_rows, 0)
        distance = query_positions[:, None] - key_positions[None, :]
        mask_table = (distance >= 0) & (distance < WINDOW) & (query_segments[:, None] == key_segments[None, :])
        scores = jnp.where(mask_table[None], scores, -jnp.inf)
        maximum = lax.optimization_barrier(jnp.max(scores, -1, keepdims=True))
        exponents = jnp.exp(scores - maximum)
        probabilities = exponents / lax.optimization_barrier(jnp.sum(exponents, -1, keepdims=True))
        result = jnp.einsum('hqk,khd->qhd', reduced_precision(probabilities), value_block, precision=lax.Precision.HIGHEST)
        return result.reshape(BLOCK, QUERY_HEAD_COUNT * HEAD_SIZE)
    blocks = lax.map(jax.checkpoint(one_block), jnp.arange(PACKED_TOKENS // BLOCK, dtype=jnp.int32))
    return blocks.reshape(PACKED_TOKENS, QUERY_HEAD_COUNT * HEAD_SIZE)

def reference(tokens, segments, w_query, key_projection, value_projection, w_out, w_gate, w_up, w_down, norm_attn, norm_ffn, cotangent):
    token_positions = jnp.arange(PACKED_TOKENS, dtype=jnp.int32)

    def forward(inputs, query_weight, key_matrix, value_matrix, out_weight, gate_weight, up_weight, down_weight, gain_one, gain_two):
        first_normed = reduced_precision(normalize(inputs, gain_one))
        queries = reduced_precision(apply_rotary(reduced_backward(matrix_multiply(first_normed, query_weight)).reshape(PACKED_TOKENS, QUERY_HEAD_COUNT, HEAD_SIZE), token_positions))
        key_vectors = reduced_precision(apply_rotary(reduced_backward(matrix_multiply(first_normed, key_matrix)).reshape(PACKED_TOKENS, KEY_VALUE_HEADS, HEAD_SIZE), token_positions))
        value_vectors = reduced_precision(reduced_backward(matrix_multiply(first_normed, value_matrix))).reshape(PACKED_TOKENS, KEY_VALUE_HEADS, HEAD_SIZE)
        attended = reduced_backward(reduced_precision(attention(queries, key_vectors, value_vectors, segments)))
        hidden_one = inputs + reduced_backward(matrix_multiply(attended, out_weight))
        normed_two = reduced_precision(normalize(hidden_one, gain_two))
        gate_value = reduced_backward(matrix_multiply(normed_two, gate_weight))
        up_value = reduced_backward(matrix_multiply(normed_two, up_weight))
        product = reduced_precision(jax.nn.silu(gate_value) * up_value)
        return hidden_one + reduced_backward(matrix_multiply(product, down_weight))
    primals = (tokens.reshape(PACKED_TOKENS, MODEL_WIDTH).astype(jnp.float32), w_query.astype(jnp.float32), key_projection.astype(jnp.float32), value_projection.astype(jnp.float32), w_out.astype(jnp.float32), w_gate.astype(jnp.float32), w_up.astype(jnp.float32), w_down.astype(jnp.float32), norm_attn.astype(jnp.float32), norm_ffn.astype(jnp.float32))
    result, pullback = jax.vjp(forward, *primals)
    grads = pullback(cotangent.reshape(PACKED_TOKENS, MODEL_WIDTH).astype(jnp.float32))
    return (result.reshape(BLOCKS, BLOCK, MODEL_WIDTH).astype(jnp.bfloat16), grads[0].reshape(BLOCKS, BLOCK, MODEL_WIDTH).astype(jnp.bfloat16), grads[1], grads[2], grads[3], grads[4], grads[5], grads[6], grads[7], grads[8], grads[9])
```

```python
import functools

import jax
import jax.numpy as jnp
from jax import lax
from jax.experimental import pallas as pl
from jax.experimental.pallas import tpu as pltpu
from jax.sharding import Mesh
from jax.sharding import PartitionSpec as P

HEAD_SIZE = 64
WINDOW = 1024
EPSILON = 1e-05
BF16 = jnp.bfloat16
F32 = jnp.float32
BLK = ("y", "x", "core")
VMEM_LIMIT = 56 * 1024 * 1024


def dot_nn(a, b):
    return jnp.dot(a, b, preferred_element_type=F32)


def dot_nt(a, b):
    return lax.dot_general(a, b, (((1,), (1,)), ((), ())), preferred_element_type=F32)


def dot_tn(a, b):
    return lax.dot_general(a, b, (((0,), (0,)), ((), ())), preferred_element_type=F32)


def shift(value, axis, distance):
    size = lax.axis_size(axis)
    return lax.ppermute(value, axis, [(i, (i + distance) % size) for i in range(size)])


def add_low(a, b):
    return (a.astype(F32) + b.astype(F32)).astype(BF16)


def gather_head(rows):
    half = rows.shape[0] // 2
    top, bottom = rows[:half], rows[half:]
    behind_top = shift(top, "head", 1)
    ahead_bottom = shift(bottom, "head", -1)
    behind_bottom = shift(bottom, "head", 1)
    ahead_top = shift(top, "head", -1)
    far_top = shift(behind_top, "head", 1)
    far_bottom = shift(ahead_bottom, "head", -1)
    return jnp.concatenate(
        [rows, ahead_top, ahead_bottom, far_top, far_bottom, behind_top, behind_bottom], 0
    )


def scatter_head(partial):
    n = partial.shape[0] // 4
    half = n // 2
    own, ahead, far, behind = (partial[k * n : (k + 1) * n] for k in range(4))
    far_top = shift(far[:half], "head", 1)
    far_bottom = shift(far[half:], "head", -1)
    from_behind_bottom = shift(ahead[half:], "head", 1)
    from_ahead_top = shift(behind[:half], "head", -1)
    from_behind_top = shift(add_low(ahead[:half], far_top), "head", 1)
    from_ahead_bottom = shift(add_low(behind[half:], far_bottom), "head", -1)
    own = own.astype(F32)
    top = own[:half] + from_behind_top.astype(F32) + from_ahead_top.astype(F32)
    bottom = own[half:] + from_behind_bottom.astype(F32) + from_ahead_bottom.astype(F32)
    return jnp.concatenate([top, bottom], 0)


def scatter_axis(value, axis, dim):
    index = lax.axis_index(axis)

    def pick(distance):
        return lax.dynamic_index_in_dim(value, (index + distance) % 4, dim, False)

    ahead, behind, far = (
        shift(pick(1), axis, 1),
        shift(pick(3), axis, -1),
        shift(pick(2), axis, 2),
    )
    return pick(0).astype(F32) + ahead.astype(F32) + behind.astype(F32) + far.astype(F32)


def scatter_blocks(value):
    rows = value.shape[0] // 32
    half = rows // 2
    core = lax.axis_index("core")
    shaped = value.reshape(16, 2, rows, value.shape[1])
    other = shift(lax.dynamic_index_in_dim(shaped, 1 - core, 1, False), "core", 1)
    pair = add_low(lax.dynamic_index_in_dim(shaped, core, 1, False), other)
    pair = pair.reshape(4, 4, rows, value.shape[1])
    first = scatter_axis(pair[:, :, :half], "x", 1).astype(BF16)
    second = scatter_axis(pair[:, :, half:], "y", 0).astype(BF16)
    first = scatter_axis(first, "y", 0)
    second = scatter_axis(second, "x", 0)
    return jnp.concatenate([first, second], 0)


def sum_everywhere(value):
    for axis in ("head", "y", "x"):
        value = (value + shift(value, axis, 1)) + (shift(value, axis, -1) + shift(value, axis, 2))
    return value + shift(value, "core", 1)


def from_block(value, distance):
    route = [(i, i + distance) for i in range(32) if 0 <= i + distance < 32]
    return lax.ppermute(value, BLK, route)


def scale_of(values):
    return lax.rsqrt(jnp.mean(values * values, -1, keepdims=True) + EPSILON)


def norm_backward(values, scale, gain, grad):
    weighted = grad * gain
    inner = jnp.mean(weighted * values, -1, keepdims=True)
    return scale * weighted - values * (scale * scale * scale * inner)


def lane_is_low(shape, period):
    return lax.broadcasted_iota(jnp.int32, shape, len(shape) - 1) % period < period // 2


def turn(values, cosine, sine):
    swapped = jnp.where(
        lane_is_low(values.shape, 64), pltpu.roll(values, 96, 1), pltpu.roll(values, 32, 1)
    )
    return values * cosine + swapped * sine


def project_kernel(x_ref, w_ref, cos_ref, sin_ref, q_ref, kv_ref):
    cosine, sine = cos_ref[...], sin_ref[...]
    x = x_ref[...]
    for start in (0, 256):
        wide = dot_nn(x, w_ref[:, start : start + 256])
        for part in (0, 128):
            turned = turn(wide[:, part : part + 128], cosine, sine)
            q_ref[:, start + part : start + part + 128] = (turned * HEAD_SIZE**-0.5).astype(BF16)
    last = dot_nn(x, w_ref[:, 512:640])
    kv_ref[...] = jnp.where(lane_is_low(last.shape, 128), turn(last, cosine, sine), last).astype(BF16)


def project(normed, weights, cosine, sine):
    rows, width = normed.shape
    return pl.pallas_call(
        project_kernel,
        out_shape=(
            jax.ShapeDtypeStruct((rows, 512), BF16),
            jax.ShapeDtypeStruct((rows, 128), BF16),
        ),
        grid=(1,),
        in_specs=[
            pl.BlockSpec((rows, width), lambda i: (0, 0)),
            pl.BlockSpec((width, 640), lambda i: (0, 0)),
            pl.BlockSpec((rows, 128), lambda i: (0, 0)),
            pl.BlockSpec((rows, 128), lambda i: (0, 0)),
        ],
        out_specs=(
            pl.BlockSpec((rows, 512), lambda i: (0, 0)),
            pl.BlockSpec((rows, 128), lambda i: (0, 0)),
        ),
        compiler_params=pltpu.CompilerParams(vmem_limit_bytes=VMEM_LIMIT),
        cost_estimate=pl.CostEstimate(
            flops=2 * rows * width * 640, bytes_accessed=6 * 1024 * 1024, transcendentals=0
        ),
    )(normed, weights, cosine, sine)


def set_up(place, kv0_ref, kv1_ref, kv2_ref, qseg_ref, kseg_ref, kk, vv, kvt, bias):
    low = lane_is_low((128, 128), 128)
    for block, ref in enumerate((kv0_ref, kv1_ref, kv2_ref)):
        for group in range(4):
            at = pl.multiple_of(lax.rem(group - place + 4, 4) * 128, 128)
            piece = ref[pl.ds(at, 128), :].astype(F32)
            rolled = pltpu.roll(piece, 64, 1)
            to = block * 512 + group * 128
            kk[to : to + 128, :] = jnp.where(low, piece, rolled).astype(BF16)
            vv[to : to + 128, :] = jnp.where(low, rolled, piece).astype(BF16)
            kvt[:, to : to + 128] = piece.T.astype(BF16)
    for tile in range(2):
        key = lax.broadcasted_iota(jnp.int32, (1280, 256), 0)
        query = lax.broadcasted_iota(jnp.int32, (1280, 256), 1)
        distance = query - key + WINDOW
        same = kseg_ref[256 * tile : 256 * tile + 1280, :] == qseg_ref[:, 256 * tile : 256 * tile + 256]
        seen = (distance >= 0) & (distance < WINDOW) & same
        bias[tile] = jnp.where(seen, 0.0, -jnp.inf)


def true_rows(ref, place, tile):
    pieces = []
    for group in (0, 1):
        at = pl.multiple_of(lax.rem(2 * tile + group - place + 4, 4) * 128, 128)
        pieces.append(ref[pl.ds(at, 128), :])
    return jnp.concatenate(pieces, 0)


def put_rows(ref, place, tile, value):
    for group in (0, 1):
        at = pl.multiple_of(lax.rem(2 * tile + group - place + 4, 4) * 128, 128)
        ref[pl.ds(at, 128), :] = value[128 * group : 128 * group + 128]


def attend_kernel(
    place_ref, q_ref, kv0_ref, kv1_ref, kv2_ref, qseg_ref, kseg_ref, o_ref, lse_ref, kk, vv, kvt, bias
):
    place = place_ref[0]

    @pl.when(pl.program_id(0) == 0)
    def _():
        set_up(place, kv0_ref, kv1_ref, kv2_ref, qseg_ref, kseg_ref, kk, vv, kvt, bias)

    low = lane_is_low((256, 128), 128)
    for tile in range(2):
        keys = slice(256 * tile, 256 * tile + 1280)
        pair = true_rows(q_ref, place, tile)
        results = []
        for head in range(2):
            query = jnp.where(low if head == 0 else ~low, pair, jnp.zeros_like(pair))
            scores = dot_nt(kk[keys, :], query) + bias[tile]
            top = jnp.max(scores, 0, keepdims=True)
            weights = jnp.exp(scores - top)
            total = jnp.sum(weights, 0, keepdims=True)
            results.append(dot_nn(kvt[64:128, keys], weights.astype(BF16)) / total)
            lse_ref[0, head : head + 1, 256 * tile : 256 * tile + 256] = top + jnp.log(total)
        put_rows(o_ref, place, tile, jnp.concatenate(results, 0).T.astype(BF16))


ATTENTION_SCRATCH = [
    pltpu.VMEM((1536, 128), BF16),
    pltpu.VMEM((1536, 128), BF16),
    pltpu.VMEM((128, 1536), BF16),
    pltpu.VMEM((2, 1280, 256), F32),
]


def attend(place, queries, kv, qseg, kseg):
    whole = lambda p, s: (0, 0)
    grid = pltpu.PrefetchScalarGridSpec(
        num_scalar_prefetch=1,
        grid=(4,),
        in_specs=[
            pl.BlockSpec((512, 128), lambda p, s: (0, p)),
            pl.BlockSpec((512, 128), whole),
            pl.BlockSpec((512, 128), whole),
            pl.BlockSpec((512, 128), whole),
            pl.BlockSpec((1, 512), whole),
            pl.BlockSpec((1536, 1), whole),
        ],
        out_specs=(
            pl.BlockSpec((512, 128), lambda p, s: (0, p)),
            pl.BlockSpec((1, 2, 512), lambda p, s: (p, 0, 0)),
        ),
        scratch_shapes=ATTENTION_SCRATCH,
    )
    return pl.pallas_call(
        attend_kernel,
        grid_spec=grid,
        out_shape=(
            jax.ShapeDtypeStruct((512, 512), BF16),
            jax.ShapeDtypeStruct((4, 2, 512), F32),
        ),
        compiler_params=pltpu.CompilerParams(vmem_limit_bytes=VMEM_LIMIT),
        cost_estimate=pl.CostEstimate(
            flops=8 * 512 * 1280 * 256 * 2, bytes_accessed=4 * 1024 * 1024, transcendentals=8 * 512 * 1280
        ),
    )(place, queries, *kv, qseg, kseg)


def attend_back_kernel(
    place_ref,
    q_ref,
    do_ref,
    lse_ref,
    kv0_ref,
    kv1_ref,
    kv2_ref,
    qseg_ref,
    kseg_ref,
    cos_ref,
    sin_ref,
    dq_ref,
    dkv_ref,
    kk,
    vv,
    kvt,
    bias,
    dk,
    dv,
):
    place = place_ref[0]

    @pl.when(pl.program_id(0) == 0)
    def _():
        set_up(place, kv0_ref, kv1_ref, kv2_ref, qseg_ref, kseg_ref, kk, vv, kvt, bias)
        dk[...] = jnp.zeros_like(dk)
        dv[...] = jnp.zeros_like(dv)

    low = lane_is_low((256, 128), 128)
    for tile in range(2):
        keys = slice(256 * tile, 256 * tile + 1280)
        pair = true_rows(q_ref, place, tile)
        grad_pair = true_rows(do_ref, place, tile)
        results = []
        for head in range(2):
            mask = low if head == 0 else ~low
            query = jnp.where(mask, pair, jnp.zeros_like(pair))
            grad = jnp.where(mask, grad_pair, jnp.zeros_like(pair))
            scores = dot_nt(kk[keys, :], query) + bias[tile]
            weights = jnp.exp(scores - lse_ref[0, head : head + 1, 256 * tile : 256 * tile + 256])
            grad_weights = dot_nt(vv[keys, :], grad)
            dv[keys, :] += dot_nn(weights.astype(BF16), grad)
            inner = jnp.sum(weights * grad_weights, 0, keepdims=True)
            grad_scores = (weights * (grad_weights - inner)).astype(BF16)
            dk[keys, :] += dot_nn(grad_scores, query)
            results.append(dot_nn(kvt[0:64, keys], grad_scores))
        grad_query = jnp.concatenate(results, 0).T * HEAD_SIZE**-0.5
        turned = turn(
            grad_query, true_rows(cos_ref, place, tile), -true_rows(sin_ref, place, tile)
        )
        put_rows(dq_ref, place, tile, turned.astype(BF16))

    @pl.when(pl.program_id(0) == 3)
    def _():
        half = lane_is_low((128, 128), 128)
        for block in range(3):
            for group in range(4):
                at = pl.multiple_of(lax.rem(group - place + 4, 4) * 128, 128)
                frm = slice(block * 512 + group * 128, block * 512 + group * 128 + 128)
                key, value = dk[frm, :], dv[frm, :]
                key = key + pltpu.roll(key, 64, 1)
                value = value + pltpu.roll(value, 64, 1)
                dkv_ref[block, pl.ds(at, 128), :] = jnp.where(half, key, value)


def attend_back(place, queries, grad_attended, lse, kv, qseg, kseg, cosine, sine):
    whole = lambda p, s: (0, 0)
    grid = pltpu.PrefetchScalarGridSpec(
        num_scalar_prefetch=1,
        grid=(4,),
        in_specs=[
            pl.BlockSpec((512, 128), lambda p, s: (0, p)),
            pl.BlockSpec((512, 128), lambda p, s: (0, p)),
            pl.BlockSpec((1, 2, 512), lambda p, s: (p, 0, 0)),
            pl.BlockSpec((512, 128), whole),
            pl.BlockSpec((512, 128), whole),
            pl.BlockSpec((512, 128), whole),
            pl.BlockSpec((1, 512), whole),
            pl.BlockSpec((1536, 1), whole),
            pl.BlockSpec((512, 128), whole),
            pl.BlockSpec((512, 128), whole),
        ],
        out_specs=(
            pl.BlockSpec((512, 128), lambda p, s: (0, p)),
            pl.BlockSpec((3, 512, 128), lambda p, s: (0, 0, 0)),
        ),
        scratch_shapes=ATTENTION_SCRATCH
        + [pltpu.VMEM((1536, 128), F32), pltpu.VMEM((1536, 128), F32)],
    )
    return pl.pallas_call(
        attend_back_kernel,
        grid_spec=grid,
        out_shape=(
            jax.ShapeDtypeStruct((512, 512), BF16),
            jax.ShapeDtypeStruct((3, 512, 128), F32),
        ),
        compiler_params=pltpu.CompilerParams(vmem_limit_bytes=VMEM_LIMIT),
        cost_estimate=pl.CostEstimate(
            flops=8 * 512 * 1280 * 640 * 2, bytes_accessed=6 * 1024 * 1024, transcendentals=8 * 512 * 1280
        ),
    )(place, queries, grad_attended, lse, *kv, qseg, kseg, cosine, sine)


def weight_grad_kernel(normed_ref, dy_ref, dgu_ref, act_ref, out_ref):
    part = pl.program_id(0)

    @pl.when(part < 2)
    def _():
        out_ref[...] = dot_tn(normed_ref[...], dgu_ref[...]).astype(BF16)

    @pl.when(part == 2)
    def _():
        out_ref[...] = dot_tn(dy_ref[...], act_ref[...]).astype(BF16)


def weight_grads(normed, dy, dgu, act):
    rows, width = normed.shape
    hidden = act.shape[1]
    tile = 256
    return pl.pallas_call(
        weight_grad_kernel,
        out_shape=jax.ShapeDtypeStruct((width, 3 * hidden), BF16),
        grid=(3, width // tile),
        in_specs=[
            pl.BlockSpec((rows, tile), lambda j, i: (0, i)),
            pl.BlockSpec((rows, tile), lambda j, i: (0, i)),
            pl.BlockSpec((rows, hidden), lambda j, i: (0, jnp.minimum(j, 1))),
            pl.BlockSpec((rows, hidden), lambda j, i: (0, 0)),
        ],
        out_specs=pl.BlockSpec((tile, hidden), lambda j, i: (i, j)),
        compiler_params=pltpu.CompilerParams(vmem_limit_bytes=VMEM_LIMIT),
        cost_estimate=pl.CostEstimate(
            flops=2 * 3 * rows * width * hidden, bytes_accessed=30 * 1024 * 1024, transcendentals=0
        ),
    )(normed, dy, dgu, act)


def per_device(
    tokens,
    segments,
    w_query,
    key_projection,
    value_projection,
    w_out,
    w_gate,
    w_up,
    w_down,
    norm_attn,
    norm_ffn,
    cotangent,
):
    place = lax.axis_index("head")
    block = (lax.axis_index("y") * 4 + lax.axis_index("x")) * 2 + lax.axis_index("core")
    place_array = place.astype(jnp.int32).reshape(1)

    attention_weights = lax.all_gather(
        jnp.concatenate([w_query, key_projection, value_projection, w_out.T], 1), BLK, axis=0, tiled=True
    )
    ffn_weights = lax.all_gather(
        jnp.concatenate([w_gate, w_up, w_down.T], 1), BLK, axis=0, tiled=True
    )
    out_t = attention_weights[:, 640:]

    gain_one, gain_two = norm_attn.astype(F32), norm_ffn.astype(F32)
    x_rows = tokens[0].astype(F32)
    scale_one = scale_of(x_rows)
    normed_one = gather_head((x_rows * scale_one * gain_one).astype(BF16))

    row = jnp.arange(512, dtype=jnp.int32)
    positions = block * 512 + ((row // 128 + place) % 4) * 128 + row % 128
    frequency = 10000.0 ** (-jnp.arange(32, dtype=F32) * 2.0 / HEAD_SIZE)
    angles = positions.astype(F32)[:, None] * frequency[None, :]
    cosine, sine = jnp.cos(angles), jnp.sin(angles)
    cosine = jnp.concatenate([cosine] * 4, 1)
    sine = jnp.concatenate([-sine, sine, -sine, sine], 1)

    queries, kv_own = project(normed_one, attention_weights, cosine, sine)
    kv = (from_block(kv_own, 2), from_block(kv_own, 1), kv_own)

    flat = segments.reshape(-1)
    padded = jnp.concatenate([jnp.full((1024,), -1, jnp.int32), flat])
    qseg = lax.dynamic_slice_in_dim(flat, block * 512, 512, 0).reshape(1, 512)
    kseg = lax.dynamic_slice_in_dim(padded, block * 512, 1536, 0).reshape(1536, 1)

    attended, lse = attend(place_array, queries, kv, qseg, kseg)
    h1 = x_rows + scatter_head(dot_nt(attended, out_t).astype(BF16))
    scale_two = scale_of(h1)
    normed_two = gather_head((h1 * scale_two * gain_two).astype(BF16))

    dy = gather_head(cotangent[0])
    gate = dot_nn(normed_two, ffn_weights[:, :1408])
    up = dot_nn(normed_two, ffn_weights[:, 1408:2816])
    dact = dot_nn(dy, ffn_weights[:, 2816:])
    sig = jax.nn.sigmoid(gate)
    silu = gate * sig
    act = (silu * up).astype(BF16)
    dgate = (dact * up * (sig * (1.0 + gate * (1.0 - sig)))).astype(BF16)
    dup = (dact * silu).astype(BF16)
    dgu = jnp.concatenate([dgate, dup], 1)
    output = h1 + scatter_head(dot_nt(act, ffn_weights[:, 2816:]).astype(BF16))
    dnormed_two = scatter_head(dot_nt(dgu, ffn_weights[:, :2816]).astype(BF16))

    ffn_grads = lax.psum_scatter(
        weight_grads(normed_two, dy, dgu, act), BLK, scatter_dimension=0, tiled=True
    )

    dh1 = cotangent[0].astype(F32) + norm_backward(h1, scale_two, gain_two, dnormed_two)
    grad_gain_two = jnp.sum(dnormed_two * h1 * scale_two, 0)
    dh1_low = gather_head(dh1.astype(BF16))
    dattended = dot_nn(dh1_low, out_t).astype(BF16)
    grad_out_t = dot_tn(dh1_low, attended).astype(BF16)

    dq, dkv = attend_back(place_array, queries, dattended, lse, kv, qseg, kseg, cosine, sine)
    dkv_own = (
        dkv[2]
        + from_block(dkv[1].astype(BF16), -1).astype(F32)
        + from_block(dkv[0].astype(BF16), -2).astype(F32)
    )
    dk_own = dkv_own[:, :64]
    swapped = jnp.concatenate([dk_own[:, 32:], dk_own[:, :32]], 1)
    dk_own = dk_own * cosine[:, :64] - swapped * sine[:, :64]
    dqkv = jnp.concatenate([dq, dk_own.astype(BF16), dkv_own[:, 64:].astype(BF16)], 1)

    qkv_weights = attention_weights[:, :640]
    dnormed_one = scatter_head(dot_nt(dqkv, qkv_weights).astype(BF16))
    grad_inputs = dh1 + norm_backward(x_rows, scale_one, gain_one, dnormed_one)
    grad_qkv = dot_tn(normed_one, dqkv)
    grad_gain_one = jnp.sum(grad_qkv * qkv_weights.astype(F32), 1) / gain_one
    gains = sum_everywhere(jnp.stack([grad_gain_one, grad_gain_two]))
    attention_grads = scatter_blocks(jnp.concatenate([grad_qkv.astype(BF16), grad_out_t], 1))

    return (
        output.astype(BF16)[None],
        grad_inputs.astype(BF16)[None],
        attention_grads[:, :512],
        attention_grads[:, 512:576],
        attention_grads[:, 576:640],
        attention_grads[:, 640:].T,
        ffn_grads[:, :1408].astype(F32),
        ffn_grads[:, 1408:2816].astype(F32),
        ffn_grads[:, 2816:].T.astype(F32),
        gains[0],
        gains[1],
    )


def solution(mesh):
    grid = Mesh(mesh.devices.reshape(4, 4, 4, 2), ("head", "y", "x", "core"))
    rows, up, down = P(BLK, "head", None), P(BLK, "head"), P("head", BLK)
    return jax.shard_map(
        per_device,
        mesh=grid,
        in_specs=(rows, P(), up, up, up, down, up, up, down, P(), P(), rows),
        out_specs=(rows, rows, up, up, up, down, up, up, down, P(), P()),
        check_vma=False,
    )
```

```python
import functools

import jax
import jax.numpy as jnp
from jax import lax
from jax.experimental import pallas as pl
from jax.experimental.pallas import tpu as pltpu
from jax.sharding import Mesh
from jax.sharding import PartitionSpec as P

HEAD_SIZE = 64
WINDOW = 1024
EPSILON = 1e-05
BF16 = jnp.bfloat16
F32 = jnp.float32
BLK = ("y", "x", "core")
VMEM_LIMIT = 56 * 1024 * 1024


def dot_nn(a, b):
    return jnp.dot(a, b, preferred_element_type=F32)


def dot_nt(a, b):
    return lax.dot_general(a, b, (((1,), (1,)), ((), ())), preferred_element_type=F32)


def dot_tn(a, b):
    return lax.dot_general(a, b, (((0,), (0,)), ((), ())), preferred_element_type=F32)


def shift(value, axis, distance):
    size = lax.axis_size(axis)
    return lax.ppermute(value, axis, [(i, (i + distance) % size) for i in range(size)])


def add_low(a, b):
    return (a.astype(F32) + b.astype(F32)).astype(BF16)


def gather_head(rows):
    half = rows.shape[0] // 2
    top, bottom = rows[:half], rows[half:]
    behind_top = shift(top, "head", 1)
    ahead_bottom = shift(bottom, "head", -1)
    behind_bottom = shift(bottom, "head", 1)
    ahead_top = shift(top, "head", -1)
    far_top = shift(behind_top, "head", 1)
    far_bottom = shift(ahead_bottom, "head", -1)
    return jnp.concatenate(
        [rows, ahead_top, ahead_bottom, far_top, far_bottom, behind_top, behind_bottom], 0
    )


def scatter_head(partial):
    n = partial.shape[0] // 4
    half = n // 2
    own, ahead, far, behind = (partial[k * n : (k + 1) * n] for k in range(4))
    far_top = shift(far[:half], "head", 1)
    far_bottom = shift(far[half:], "head", -1)
    from_behind_bottom = shift(ahead[half:], "head", 1)
    from_ahead_top = shift(behind[:half], "head", -1)
    from_behind_top = shift(add_low(ahead[:half], far_top), "head", 1)
    from_ahead_bottom = shift(add_low(behind[half:], far_bottom), "head", -1)
    own = own.astype(F32)
    top = own[:half] + from_behind_top.astype(F32) + from_ahead_top.astype(F32)
    bottom = own[half:] + from_behind_bottom.astype(F32) + from_ahead_bottom.astype(F32)
    return jnp.concatenate([top, bottom], 0)


def gather_head_direct(rows):
    ahead, behind, far = shift(rows, "head", -1), shift(rows, "head", 1), shift(rows, "head", 2)
    return jnp.concatenate([rows, ahead, far, behind], 0)


def scatter_head_direct(partial):
    n = partial.shape[0] // 4
    own, ahead, far, behind = (partial[k * n : (k + 1) * n] for k in range(4))
    ahead, behind, far = shift(ahead, "head", 1), shift(behind, "head", -1), shift(far, "head", 2)
    return (own.astype(F32) + far.astype(F32)) + (ahead.astype(F32) + behind.astype(F32))


def scatter_axis(value, extra, axis):
    index = lax.axis_index(axis)
    rows = value.shape[1]

    def send(distance):
        piece = lax.dynamic_index_in_dim(value, (index + distance) % 4, 0, False)
        moved = shift(jnp.concatenate([piece, extra], 0), axis, 2 if distance == 2 else distance)
        return moved.astype(F32)

    own = jnp.concatenate([lax.dynamic_index_in_dim(value, index, 0, False), extra], 0)
    total = (own.astype(F32) + send(1)) + (send(-1) + send(2))
    return total[:rows], total[rows:]


def scatter_blocks(value, extra):
    columns = value.shape[1]
    core = lax.axis_index("core")
    shaped = value.reshape(16, 2, 64, columns)
    other = shift(lax.dynamic_index_in_dim(shaped, 1 - core, 1, False), "core", 1)
    pair = add_low(lax.dynamic_index_in_dim(shaped, core, 1, False), other)
    extra = extra + shift(extra, "core", 1)
    pair = pair.reshape(4, 4, 64, columns).transpose(1, 0, 2, 3).reshape(4, 256, columns)
    part, extra = scatter_axis(pair, extra.astype(BF16), "x")
    part = part.astype(BF16).reshape(4, 64, columns)
    return scatter_axis(part, extra.astype(BF16), "y")


def sum_head(value):
    return (value + shift(value, "head", 1)) + (shift(value, "head", -1) + shift(value, "head", 2))


def from_block(value, distance):
    route = [(i, i + distance) for i in range(32) if 0 <= i + distance < 32]
    return lax.ppermute(value, BLK, route)


def scale_of(values):
    return lax.rsqrt(jnp.mean(values * values, -1, keepdims=True) + EPSILON)


def norm_backward(values, scale, gain, grad):
    weighted = grad * gain
    inner = jnp.mean(weighted * values, -1, keepdims=True)
    return scale * weighted - values * (scale * scale * scale * inner)


def lane_is_low(shape, period):
    return lax.broadcasted_iota(jnp.int32, shape, len(shape) - 1) % period < period // 2


def turn(values, cosine, sine):
    swapped = jnp.where(
        lane_is_low(values.shape, 64), pltpu.roll(values, 96, 1), pltpu.roll(values, 32, 1)
    )
    return values * cosine + swapped * sine


def project_kv_kernel(x_ref, w_ref, cos_ref, sin_ref, kv_ref):
    flat = dot_nn(x_ref[...], w_ref[...])
    turned = turn(flat, cos_ref[...], sin_ref[...])
    kv_ref[...] = jnp.where(lane_is_low(flat.shape, 128), turned, flat).astype(BF16)


def project_q_kernel(x_ref, w_ref, cos_ref, sin_ref, q_ref):
    cosine, sine = cos_ref[...], sin_ref[...]
    wide = dot_nn(x_ref[...], w_ref[...])
    for part in (0, 128):
        turned = turn(wide[:, part : part + 128], cosine, sine)
        q_ref[:, part : part + 128] = (turned * HEAD_SIZE**-0.5).astype(BF16)


def project(kernel, normed, weights, cosine, sine, start, columns, tile):
    rows, width = normed.shape
    whole = lambda i: (0, 0)
    return pl.pallas_call(
        kernel,
        out_shape=jax.ShapeDtypeStruct((rows, columns), BF16),
        grid=(columns // tile,),
        in_specs=[
            pl.BlockSpec((rows, width), whole),
            pl.BlockSpec((width, tile), lambda i: (0, start // tile + i)),
            pl.BlockSpec((rows, 128), whole),
            pl.BlockSpec((rows, 128), whole),
        ],
        out_specs=pl.BlockSpec((rows, tile), lambda i: (0, i)),
        compiler_params=pltpu.CompilerParams(vmem_limit_bytes=VMEM_LIMIT),
        cost_estimate=pl.CostEstimate(
            flops=2 * rows * width * columns,
            bytes_accessed=2 * (rows * width + width * columns + rows * columns),
            transcendentals=0,
        ),
    )(normed, weights, cosine, sine)


def set_up(place, kv0_ref, kv1_ref, kv2_ref, qseg_ref, kseg_ref, kk, vv, kvt, bias):
    low = lane_is_low((128, 128), 128)
    for block, ref in enumerate((kv0_ref, kv1_ref, kv2_ref)):
        for group in range(4):
            at = pl.multiple_of(lax.rem(group - place + 4, 4) * 128, 128)
            piece = ref[pl.ds(at, 128), :].astype(F32)
            rolled = pltpu.roll(piece, 64, 1)
            to = block * 512 + group * 128
            kk[to : to + 128, :] = jnp.where(low, piece, rolled).astype(BF16)
            vv[to : to + 128, :] = jnp.where(low, rolled, piece).astype(BF16)
            kvt[:, to : to + 128] = piece.T.astype(BF16)
    for tile in range(2):
        key = lax.broadcasted_iota(jnp.int32, (1280, 256), 0)
        query = lax.broadcasted_iota(jnp.int32, (1280, 256), 1)
        distance = query - key + WINDOW
        same = kseg_ref[256 * tile : 256 * tile + 1280, :] == qseg_ref[:, 256 * tile : 256 * tile + 256]
        seen = (distance >= 0) & (distance < WINDOW) & same
        bias[tile] = jnp.where(seen, 0.0, -jnp.inf)


def true_rows(ref, place, tile):
    pieces = []
    for group in (0, 1):
        at = pl.multiple_of(lax.rem(2 * tile + group - place + 4, 4) * 128, 128)
        pieces.append(ref[pl.ds(at, 128), :])
    return jnp.concatenate(pieces, 0)


def put_rows(ref, place, tile, value):
    for group in (0, 1):
        at = pl.multiple_of(lax.rem(2 * tile + group - place + 4, 4) * 128, 128)
        ref[pl.ds(at, 128), :] = value[128 * group : 128 * group + 128]


def attend_kernel(
    place_ref, q_ref, kv0_ref, kv1_ref, kv2_ref, qseg_ref, kseg_ref, o_ref, lse_ref, kk, vv, kvt, bias
):
    place = place_ref[0]

    @pl.when(pl.program_id(0) == 0)
    def _():
        set_up(place, kv0_ref, kv1_ref, kv2_ref, qseg_ref, kseg_ref, kk, vv, kvt, bias)

    low = lane_is_low((256, 128), 128)
    for tile in range(2):
        keys = slice(256 * tile, 256 * tile + 1280)
        pair = true_rows(q_ref, place, tile)
        results = []
        for head in range(2):
            query = jnp.where(low if head == 0 else ~low, pair, jnp.zeros_like(pair))
            scores = dot_nt(kk[keys, :], query) + bias[tile]
            top = jnp.max(scores, 0, keepdims=True)
            weights = jnp.exp(scores - top)
            total = jnp.sum(weights, 0, keepdims=True)
            results.append(dot_nn(kvt[64:128, keys], weights.astype(BF16)) / total)
            lse_ref[0, head : head + 1, 256 * tile : 256 * tile + 256] = top + jnp.log(total)
        put_rows(o_ref, place, tile, jnp.concatenate(results, 0).T.astype(BF16))


ATTENTION_SCRATCH = [
    pltpu.VMEM((1536, 128), BF16),
    pltpu.VMEM((1536, 128), BF16),
    pltpu.VMEM((128, 1536), BF16),
    pltpu.VMEM((2, 1280, 256), F32),
]


def attend(place, queries, kv, qseg, kseg):
    whole = lambda p, s: (0, 0)
    grid = pltpu.PrefetchScalarGridSpec(
        num_scalar_prefetch=1,
        grid=(4,),
        in_specs=[
            pl.BlockSpec((512, 128), lambda p, s: (0, p)),
            pl.BlockSpec((512, 128), whole),
            pl.BlockSpec((512, 128), whole),
            pl.BlockSpec((512, 128), whole),
            pl.BlockSpec((1, 512), whole),
            pl.BlockSpec((1536, 1), whole),
        ],
        out_specs=(
            pl.BlockSpec((512, 128), lambda p, s: (0, p)),
            pl.BlockSpec((1, 2, 512), lambda p, s: (p, 0, 0)),
        ),
        scratch_shapes=ATTENTION_SCRATCH,
    )
    return pl.pallas_call(
        attend_kernel,
        grid_spec=grid,
        out_shape=(
            jax.ShapeDtypeStruct((512, 512), BF16),
            jax.ShapeDtypeStruct((4, 2, 512), F32),
        ),
        compiler_params=pltpu.CompilerParams(vmem_limit_bytes=VMEM_LIMIT),
        cost_estimate=pl.CostEstimate(
            flops=8 * 512 * 1280 * 256 * 2, bytes_accessed=4 * 1024 * 1024, transcendentals=8 * 512 * 1280
        ),
    )(place, queries, *kv, qseg, kseg)


def attend_back_kernel(
    place_ref,
    q_ref,
    do_ref,
    lse_ref,
    kv0_ref,
    kv1_ref,
    kv2_ref,
    qseg_ref,
    kseg_ref,
    cos_ref,
    sin_ref,
    dq_ref,
    own_ref,
    earlier_ref,
    kk,
    vv,
    kvt,
    bias,
    dk,
    dv,
):
    place = place_ref[0]

    @pl.when(pl.program_id(0) == 0)
    def _():
        set_up(place, kv0_ref, kv1_ref, kv2_ref, qseg_ref, kseg_ref, kk, vv, kvt, bias)
        dk[...] = jnp.zeros_like(dk)
        dv[...] = jnp.zeros_like(dv)

    low = lane_is_low((256, 128), 128)
    for tile in range(2):
        keys = slice(256 * tile, 256 * tile + 1280)
        pair = true_rows(q_ref, place, tile)
        grad_pair = true_rows(do_ref, place, tile)
        results = []
        for head in range(2):
            mask = low if head == 0 else ~low
            query = jnp.where(mask, pair, jnp.zeros_like(pair))
            grad = jnp.where(mask, grad_pair, jnp.zeros_like(pair))
            scores = dot_nt(kk[keys, :], query) + bias[tile]
            weights = jnp.exp(scores - lse_ref[0, head : head + 1, 256 * tile : 256 * tile + 256])
            grad_weights = dot_nt(vv[keys, :], grad)
            dv[keys, :] += dot_nn(weights.astype(BF16), grad)
            inner = jnp.sum(weights * grad_weights, 0, keepdims=True)
            grad_scores = (weights * (grad_weights - inner)).astype(BF16)
            dk[keys, :] += dot_nn(grad_scores, query)
            results.append(dot_nn(kvt[0:64, keys], grad_scores))
        grad_query = jnp.concatenate(results, 0).T * HEAD_SIZE**-0.5
        turned = turn(
            grad_query, true_rows(cos_ref, place, tile), -true_rows(sin_ref, place, tile)
        )
        put_rows(dq_ref, place, tile, turned.astype(BF16))

    @pl.when(pl.program_id(0) == 3)
    def _():
        half = lane_is_low((128, 128), 128)
        for block in range(3):
            for group in range(4):
                at = pl.multiple_of(lax.rem(group - place + 4, 4) * 128, 128)
                frm = slice(block * 512 + group * 128, block * 512 + group * 128 + 128)
                key, value = dk[frm, :], dv[frm, :]
                key = key + pltpu.roll(key, 64, 1)
                value = value + pltpu.roll(value, 64, 1)
                both = jnp.where(half, key, value)
                if block == 2:
                    own_ref[pl.ds(at, 128), :] = both
                else:
                    earlier_ref[block, pl.ds(at, 128), :] = both.astype(BF16)


def attend_back(place, queries, grad_attended, lse, kv, qseg, kseg, cosine, sine):
    whole = lambda p, s: (0, 0)
    grid = pltpu.PrefetchScalarGridSpec(
        num_scalar_prefetch=1,
        grid=(4,),
        in_specs=[
            pl.BlockSpec((512, 128), lambda p, s: (0, p)),
            pl.BlockSpec((512, 128), lambda p, s: (0, p)),
            pl.BlockSpec((1, 2, 512), lambda p, s: (p, 0, 0)),
            pl.BlockSpec((512, 128), whole),
            pl.BlockSpec((512, 128), whole),
            pl.BlockSpec((512, 128), whole),
            pl.BlockSpec((1, 512), whole),
            pl.BlockSpec((1536, 1), whole),
            pl.BlockSpec((512, 128), whole),
            pl.BlockSpec((512, 128), whole),
        ],
        out_specs=(
            pl.BlockSpec((512, 128), lambda p, s: (0, p)),
            pl.BlockSpec((512, 128), whole),
            pl.BlockSpec((2, 512, 128), lambda p, s: (0, 0, 0)),
        ),
        scratch_shapes=ATTENTION_SCRATCH
        + [pltpu.VMEM((1536, 128), F32), pltpu.VMEM((1536, 128), F32)],
    )
    return pl.pallas_call(
        attend_back_kernel,
        grid_spec=grid,
        out_shape=(
            jax.ShapeDtypeStruct((512, 512), BF16),
            jax.ShapeDtypeStruct((512, 128), F32),
            jax.ShapeDtypeStruct((2, 512, 128), BF16),
        ),
        compiler_params=pltpu.CompilerParams(vmem_limit_bytes=VMEM_LIMIT),
        cost_estimate=pl.CostEstimate(
            flops=8 * 512 * 1280 * 640 * 2, bytes_accessed=6 * 1024 * 1024, transcendentals=8 * 512 * 1280
        ),
    )(place, queries, grad_attended, lse, *kv, qseg, kseg, cosine, sine)


HIDDEN = 1408
GROUPS = [(0, 256), (256, 256), (512, 256), (768, 256), (1024, 256), (1280, 128)]


def ffn_kernel(x_ref, dy_ref, w_ref, act_ref, dgu_ref, dx_ref, held, sems):
    copies = []
    for number, (start, width) in enumerate(GROUPS):
        for part in range(3):
            columns = pl.ds(part * HIDDEN + start, width)
            copy = pltpu.make_async_copy(
                w_ref.at[:, columns], held.at[:, columns], sems.at[3 * number + part]
            )
            copy.start()
            copies.append(copy)
    x, dy = x_ref[...], dy_ref[...]
    for number, (start, width) in enumerate(GROUPS):
        for part in range(3):
            copies[3 * number + part].wait()
        gate = dot_nn(x, held[:, start : start + width])
        up = dot_nn(x, held[:, HIDDEN + start : HIDDEN + start + width])
        dact = dot_nn(dy, held[:, 2 * HIDDEN + start : 2 * HIDDEN + start + width])
        sig = jax.nn.sigmoid(gate)
        silu = gate * sig
        act_ref[:, start : start + width] = (silu * up).astype(BF16)
        dgate = dact * up * (sig * (1.0 + gate * (1.0 - sig)))
        dgu_ref[:, start : start + width] = dgate.astype(BF16)
        dgu_ref[:, HIDDEN + start : HIDDEN + start + width] = (dact * silu).astype(BF16)
    dgu = dgu_ref[...]
    for start in range(0, 2048, 512):
        dx = dot_nt(dgu, held[start : start + 512, : 2 * HIDDEN])
        dx_ref[:, start : start + 512] = dx.astype(BF16)


def ffn(normed, dy, weights):
    rows, width = normed.shape
    vmem = pl.BlockSpec(memory_space=pltpu.VMEM)
    return pl.pallas_call(
        ffn_kernel,
        out_shape=(
            jax.ShapeDtypeStruct((rows, HIDDEN), BF16),
            jax.ShapeDtypeStruct((rows, 2 * HIDDEN), BF16),
            jax.ShapeDtypeStruct((rows, width), BF16),
        ),
        in_specs=[vmem, vmem, pl.BlockSpec(memory_space=pl.ANY)],
        out_specs=(vmem, vmem, vmem),
        scratch_shapes=[pltpu.VMEM((width, 3 * HIDDEN), BF16), pltpu.SemaphoreType.DMA((18,))],
        compiler_params=pltpu.CompilerParams(vmem_limit_bytes=VMEM_LIMIT),
        cost_estimate=pl.CostEstimate(
            flops=10 * rows * width * HIDDEN,
            bytes_accessed=28 * 1024 * 1024,
            transcendentals=rows * HIDDEN,
        ),
    )(normed, dy, weights)


def weight_grad_kernel(*refs):
    left_ref, right_ref, out_ref = refs[-3:]
    out_ref[...] = dot_tn(left_ref[...], right_ref[...]).astype(BF16)


def weight_grad(held, left, right, right_part, part):
    rows, width = left.shape
    tile = 512
    specs = [
        pl.BlockSpec((rows, tile), lambda i: (0, i)),
        pl.BlockSpec((rows, HIDDEN), lambda i: (0, right_part)),
    ]
    operands = (left, right)
    if held is not None:
        specs = [pl.BlockSpec(memory_space=pl.ANY)] + specs
        operands = (held,) + operands
    return pl.pallas_call(
        weight_grad_kernel,
        out_shape=jax.ShapeDtypeStruct((width, 3 * HIDDEN), BF16),
        grid=(width // tile,),
        in_specs=specs,
        out_specs=pl.BlockSpec((tile, HIDDEN), lambda i: (i, part)),
        input_output_aliases={} if held is None else {0: 0},
        compiler_params=pltpu.CompilerParams(vmem_limit_bytes=VMEM_LIMIT),
        cost_estimate=pl.CostEstimate(
            flops=2 * rows * width * HIDDEN, bytes_accessed=10 * 1024 * 1024, transcendentals=0
        ),
    )(*operands)


def rows_times_kernel(left_ref, right_ref, out_ref):
    out_ref[...] = dot_nt(left_ref[...], right_ref[...]).astype(BF16)


def rows_times(left, right, right_part):
    rows, depth = left.shape
    width = right.shape[0]
    tile = 512
    return pl.pallas_call(
        rows_times_kernel,
        out_shape=jax.ShapeDtypeStruct((rows, width), BF16),
        grid=(width // tile,),
        in_specs=[
            pl.BlockSpec((rows, depth), lambda i: (0, 0)),
            pl.BlockSpec((tile, depth), lambda i: (i, right_part)),
        ],
        out_specs=pl.BlockSpec((rows, tile), lambda i: (0, i)),
        compiler_params=pltpu.CompilerParams(vmem_limit_bytes=VMEM_LIMIT),
        cost_estimate=pl.CostEstimate(
            flops=2 * rows * depth * width,
            bytes_accessed=2 * (rows * depth + width * depth + rows * width),
            transcendentals=0,
        ),
    )(left, right)


def finish_kernel(
    x_ref, w_ref, dq_ref, own_ref, one_ref, two_ref, cos_ref, sin_ref, grad_ref, dx_ref, gain_ref, dqkv
):
    dqkv[:, :512] = dq_ref[...]
    dkv = own_ref[...] + one_ref[...].astype(F32) + two_ref[...].astype(F32)
    turned = turn(dkv, cos_ref[...], -sin_ref[...])
    dqkv[:, 512:] = jnp.where(lane_is_low(dkv.shape, 128), turned, dkv).astype(BF16)
    grads = dqkv[...]
    for start in range(0, 2048, 512):
        columns = slice(start, start + 512)
        x = x_ref[:, columns]
        dx = dot_nt(grads, w_ref[columns, :])
        dx_ref[:, columns] = dx.astype(BF16)
        gain_ref[:, columns] = jnp.sum(dx * x.astype(F32), 0, keepdims=True)
        grad_ref[columns, :] = dot_tn(x, grads).astype(BF16)


def finish(normed, weights, dq, own, one, two, cosine, sine):
    rows, width = normed.shape
    whole = lambda i: (0, 0)
    return pl.pallas_call(
        finish_kernel,
        out_shape=(
            jax.ShapeDtypeStruct((width, 640), BF16),
            jax.ShapeDtypeStruct((rows, width), BF16),
            jax.ShapeDtypeStruct((1, width), F32),
        ),
        grid=(1,),
        in_specs=[
            pl.BlockSpec((rows, width), whole),
            pl.BlockSpec((width, 640), whole),
            pl.BlockSpec((rows, 512), whole),
            pl.BlockSpec((rows, 128), whole),
            pl.BlockSpec((rows, 128), whole),
            pl.BlockSpec((rows, 128), whole),
            pl.BlockSpec((rows, 128), whole),
            pl.BlockSpec((rows, 128), whole),
        ],
        out_specs=(
            pl.BlockSpec((width, 640), whole),
            pl.BlockSpec((rows, width), whole),
            pl.BlockSpec((1, width), whole),
        ),
        scratch_shapes=[pltpu.VMEM((rows, 640), BF16)],
        compiler_params=pltpu.CompilerParams(vmem_limit_bytes=VMEM_LIMIT),
        cost_estimate=pl.CostEstimate(
            flops=4 * rows * width * 640, bytes_accessed=11 * 1024 * 1024, transcendentals=0
        ),
    )(normed, weights, dq, own, one, two, cosine, sine)


def per_device(
    tokens,
    segments,
    w_query,
    key_projection,
    value_projection,
    w_out,
    w_gate,
    w_up,
    w_down,
    norm_attn,
    norm_ffn,
    cotangent,
):
    place = lax.axis_index("head")
    block = (lax.axis_index("y") * 4 + lax.axis_index("x")) * 2 + lax.axis_index("core")
    place_array = place.astype(jnp.int32).reshape(1)

    attention_weights = lax.all_gather(
        jnp.concatenate([w_query, key_projection, value_projection, w_out.T], 1), BLK, axis=0, tiled=True
    )
    ffn_weights = lax.all_gather(
        jnp.concatenate([w_gate, w_up, w_down.T], 1), BLK, axis=0, tiled=True
    )
    out_t = attention_weights[:, 640:]

    gain_one, gain_two = norm_attn.astype(F32), norm_ffn.astype(F32)
    x_rows = tokens[0].astype(F32)
    scale_one = scale_of(x_rows)
    normed_one = gather_head((x_rows * scale_one * gain_one).astype(BF16))

    row = jnp.arange(512, dtype=jnp.int32)
    positions = block * 512 + ((row // 128 + place) % 4) * 128 + row % 128
    frequency = 10000.0 ** (-jnp.arange(32, dtype=F32) * 2.0 / HEAD_SIZE)
    angles = positions.astype(F32)[:, None] * frequency[None, :]
    cosine, sine = jnp.cos(angles), jnp.sin(angles)
    cosine = jnp.concatenate([cosine] * 4, 1)
    sine = jnp.concatenate([-sine, sine, -sine, sine], 1)

    kv_own = project(project_kv_kernel, normed_one, attention_weights, cosine, sine, 512, 128, 128)
    kv = (from_block(kv_own, 2), from_block(kv_own, 1), kv_own)
    queries = project(project_q_kernel, normed_one, attention_weights, cosine, sine, 0, 512, 256)

    flat = segments.reshape(-1)
    padded = jnp.concatenate([jnp.full((1024,), -1, jnp.int32), flat])
    qseg = lax.dynamic_slice_in_dim(flat, block * 512, 512, 0).reshape(1, 512)
    kseg = lax.dynamic_slice_in_dim(padded, block * 512, 1536, 0).reshape(1536, 1)

    cotangent_rows, queries = lax.optimization_barrier((cotangent[0], queries))
    dy = gather_head_direct(cotangent_rows)
    attended, lse = attend(place_array, queries, kv, qseg, kseg)
    attended, dy = lax.optimization_barrier((attended, dy))
    h1 = x_rows + scatter_head(dot_nt(attended, out_t).astype(BF16))
    scale_two = scale_of(h1)
    normed_two = gather_head((h1 * scale_two * gain_two).astype(BF16))

    act, dgu, dnormed_two = ffn(normed_two, dy, ffn_weights)
    dnormed_two = scatter_head(dnormed_two)
    held = weight_grad(None, normed_two, dgu, 0, 0)
    held = weight_grad(held, normed_two, dgu, 1, 1)
    held = weight_grad(held, dy, act, 0, 2)
    ffn_grads = lax.psum_scatter(held, BLK, scatter_dimension=0, tiled=True)

    dh1 = cotangent[0].astype(F32) + norm_backward(h1, scale_two, gain_two, dnormed_two)
    grad_gain_two = jnp.sum(dnormed_two * h1 * scale_two, 0)
    dh1_low = gather_head(dh1.astype(BF16))
    dattended = dot_nn(dh1_low, out_t).astype(BF16)

    late_act, dattended = lax.optimization_barrier((act, dattended))
    output = h1 + scatter_head_direct(rows_times(late_act, ffn_weights, 2))
    dq, dkv_own, dkv_earlier = attend_back(
        place_array, queries, dattended, lse, kv, qseg, kseg, cosine, sine
    )
    dq, output = lax.optimization_barrier((dq, output))
    dkv_one = from_block(dkv_earlier[1], -1)
    dkv_two = from_block(dkv_earlier[0], -2)
    grad_out_t = dot_tn(dh1_low, attended).astype(BF16)

    grad_qkv, dnormed_one, grad_gain_one = finish(
        normed_one, attention_weights, dq, dkv_own, dkv_one, dkv_two, cosine, sine
    )
    grad_gain_one = grad_gain_one[0] / gain_one
    dnormed_one = scatter_head(dnormed_one)
    grad_inputs = dh1 + norm_backward(x_rows, scale_one, gain_one, dnormed_one)
    gains = jnp.pad(jnp.concatenate([grad_gain_one, grad_gain_two]), (0, 16 * 1152 - 4096))
    attention_grads, gains = scatter_blocks(
        jnp.concatenate([grad_qkv, grad_out_t], 1), gains.reshape(16, 1152)
    )
    gains = sum_head(gains.reshape(-1)[:4096].reshape(2, 2048))

    return (
        output.astype(BF16)[None],
        grad_inputs.astype(BF16)[None],
        attention_grads[:, :512],
        attention_grads[:, 512:576],
        attention_grads[:, 576:640],
        attention_grads[:, 640:].T,
        ffn_grads[:, :1408].astype(F32),
        ffn_grads[:, 1408:2816].astype(F32),
        ffn_grads[:, 2816:].T.astype(F32),
        gains[0],
        gains[1],
    )


def solution(mesh):
    grid = Mesh(mesh.devices.reshape(4, 4, 4, 2), ("head", "y", "x", "core"))
    rows, up, down = P(BLK, "head", None), P(BLK, "head"), P("head", BLK)
    return jax.shard_map(
        per_device,
        mesh=grid,
        in_specs=(rows, P(), up, up, up, down, up, up, down, P(), P(), rows),
        out_specs=(rows, rows, up, up, up, down, up, up, down, P(), P()),
        check_vma=False,
    )
```

```python
import jax
import jax.numpy as jnp
from jax import lax
from jax.experimental import pallas as pl
from jax.experimental.pallas import tpu as pltpu
from jax.sharding import Mesh
from jax.sharding import PartitionSpec as P

HEAD_SIZE = 64
WINDOW = 1024
EPSILON = 1e-05
BF16 = jnp.bfloat16
F32 = jnp.float32
BLK = ("y", "x", "core")
CORE_FIRST = ("core", "y", "x")
VMEM_LIMIT = 56 * 1024 * 1024


def dot_nn(a, b):
    return jnp.dot(a, b, preferred_element_type=F32)


def dot_nt(a, b):
    return lax.dot_general(a, b, (((1,), (1,)), ((), ())), preferred_element_type=F32)


def dot_tn(a, b):
    return lax.dot_general(a, b, (((0,), (0,)), ((), ())), preferred_element_type=F32)


def shift(value, axis, distance):
    size = lax.axis_size(axis)
    return lax.ppermute(value, axis, [(i, (i + distance) % size) for i in range(size)])


def add_low(a, b):
    return (a.astype(F32) + b.astype(F32)).astype(BF16)


def gather_head(rows):
    half = rows.shape[0] // 2
    ahead, behind = shift(rows, "head", -1), shift(rows, "head", 1)
    far_top = shift(behind[:half], "head", 1)
    far_bottom = shift(ahead[half:], "head", -1)
    return jnp.concatenate([rows, ahead, far_top, far_bottom, behind], 0)


def scatter_head(partial, beside=None):
    n = partial.shape[0] // 4
    half = n // 2
    own, ahead, far, behind = (partial[k * n : (k + 1) * n] for k in range(4))
    far_top = shift(far[:half], "head", 1)
    far_bottom = shift(far[half:], "head", -1)
    if beside is not None:
        far_top, far_bottom, beside = lax.optimization_barrier((far_top, far_bottom, beside))
    ahead = jnp.concatenate([add_low(ahead[:half], far_top), ahead[half:]], 0)
    behind = jnp.concatenate([behind[:half], add_low(behind[half:], far_bottom)], 0)
    ahead, behind = shift(ahead, "head", 1), shift(behind, "head", -1)
    total = own.astype(F32) + (ahead.astype(F32) + behind.astype(F32))
    return total if beside is None else (total, beside)


def swap_half(value, core):
    width = value.shape[1] // 2
    return shift(lax.dynamic_slice_in_dim(value, (1 - core) * width, width, 1), "core", 1)


def gather_head_direct(rows):
    ahead, behind, far = shift(rows, "head", -1), shift(rows, "head", 1), shift(rows, "head", 2)
    return jnp.concatenate([rows, ahead, far, behind], 0)


def scatter_head_direct(partial):
    n = partial.shape[0] // 4
    own, ahead, far, behind = (partial[k * n : (k + 1) * n] for k in range(4))
    ahead, behind, far = shift(ahead, "head", 1), shift(behind, "head", -1), shift(far, "head", 2)
    return (own.astype(F32) + far.astype(F32)) + (ahead.astype(F32) + behind.astype(F32))


def scatter_axis(value, extra, axis):
    index = lax.axis_index(axis)
    rows = value.shape[1]

    def send(distance):
        piece = lax.dynamic_index_in_dim(value, (index + distance) % 4, 0, False)
        moved = shift(jnp.concatenate([piece, extra], 0), axis, 2 if distance == 2 else distance)
        return moved.astype(F32)

    own = jnp.concatenate([lax.dynamic_index_in_dim(value, index, 0, False), extra], 0)
    total = (own.astype(F32) + send(1)) + (send(-1) + send(2))
    return total[:rows], total[rows:]


def scatter_blocks(value, extra):
    columns = value.shape[1]
    core = lax.axis_index("core")
    other = shift(lax.dynamic_slice_in_dim(value, (1 - core) * 1024, 1024, 0), "core", 1)
    extra = extra + shift(extra, "core", 1)
    pair = add_low(lax.dynamic_slice_in_dim(value, core * 1024, 1024, 0), other)
    pair = pair.reshape(4, 4, 64, columns).transpose(1, 0, 2, 3).reshape(4, 256, columns)
    part, extra = scatter_axis(pair, extra.astype(BF16), "x")
    part = part.astype(BF16).reshape(4, 64, columns)
    return scatter_axis(part, extra.astype(BF16), "y")


def sum_head(value):
    return (value + shift(value, "head", 1)) + (shift(value, "head", -1) + shift(value, "head", 2))


def from_block(value, distance):
    route = [(i, i + distance) for i in range(32) if 0 <= i + distance < 32]
    return lax.ppermute(value, BLK, route)


def scale_of(values):
    return lax.rsqrt(jnp.mean(values * values, -1, keepdims=True) + EPSILON)


def norm_backward(values, scale, gain, grad):
    weighted = grad * gain
    inner = jnp.mean(weighted * values, -1, keepdims=True)
    return scale * weighted - values * (scale * scale * scale * inner)


def lane_is_low(shape, period):
    return lax.broadcasted_iota(jnp.int32, shape, len(shape) - 1) % period < period // 2


def turn(values, cosine, sine):
    swapped = jnp.where(
        lane_is_low(values.shape, 64), pltpu.roll(values, 96, 1), pltpu.roll(values, 32, 1)
    )
    return values * cosine + swapped * sine


def core_major_tiles(tiles):
    low = lane_is_low(tiles[0].shape, 128)
    rolled = [pltpu.roll(tile, 64, 1) for tile in tiles]
    first = [jnp.where(low, tiles[2 * k], rolled[2 * k + 1]) for k in range(8)]
    second = [jnp.where(low, rolled[2 * k], tiles[2 * k + 1]) for k in range(8)]
    return first + second


def block_major_tiles(tiles):
    low = lane_is_low(tiles[0].shape, 128)
    rolled = [pltpu.roll(tile, 64, 1) for tile in tiles]
    result = []
    for k in range(8):
        result.append(jnp.where(low, tiles[k], rolled[8 + k]))
        result.append(jnp.where(low, rolled[k], tiles[8 + k]))
    return result


def in_tiles(value):
    return [value[:, 128 * k : 128 * k + 128] for k in range(16)]


def prepare_kernel(x_ref, dy_ref, gain_one_ref, gain_two_ref, x_out, dy_out, normed_out, one_out, two_out):
    def convert(ref):
        return jnp.concatenate(core_major_tiles(in_tiles(ref[...].astype(F32))), 1)

    x, gain = convert(x_ref), convert(gain_one_ref)
    one_out[...], two_out[...] = gain, convert(gain_two_ref)
    x_out[...] = x
    dy_out[...] = convert(dy_ref).astype(BF16)
    normed_out[...] = (x * scale_of(x) * gain[:1]).astype(BF16)


def prepare(x, dy, gain_one, gain_two):
    rows, width = x.shape
    return pl.pallas_call(
        prepare_kernel,
        out_shape=(
            jax.ShapeDtypeStruct((rows, width), F32),
            jax.ShapeDtypeStruct((rows, width), BF16),
            jax.ShapeDtypeStruct((rows, width), BF16),
            jax.ShapeDtypeStruct((16, width), F32),
            jax.ShapeDtypeStruct((16, width), F32),
        ),
        compiler_params=pltpu.CompilerParams(vmem_limit_bytes=VMEM_LIMIT),
        cost_estimate=pl.CostEstimate(
            flops=10 * rows * width, bytes_accessed=10 * rows * width, transcendentals=rows
        ),
    )(x, dy, gain_one, gain_two)


def to_blocks_kernel(value_ref, out_ref):
    out_ref[...] = jnp.concatenate(block_major_tiles(in_tiles(value_ref[...])), 1).astype(out_ref.dtype)


def to_blocks(value, dtype):
    return pl.pallas_call(
        to_blocks_kernel,
        out_shape=jax.ShapeDtypeStruct(value.shape, dtype),
        compiler_params=pltpu.CompilerParams(vmem_limit_bytes=VMEM_LIMIT),
        cost_estimate=pl.CostEstimate(flops=2 * value.size, bytes_accessed=6 * value.size, transcendentals=0),
    )(value)


def project_kv_kernel(x_ref, w_ref, cos_ref, sin_ref, kv_ref):
    flat = dot_nn(x_ref[...], w_ref[...])
    turned = turn(flat, cos_ref[...], sin_ref[...])
    kv_ref[...] = jnp.where(lane_is_low(flat.shape, 128), turned, flat).astype(BF16)


def project_q_kernel(x_ref, w_ref, cos_ref, sin_ref, q_ref):
    cosine, sine = cos_ref[...], sin_ref[...]
    wide = dot_nn(x_ref[...], w_ref[...])
    for part in (0, 128):
        turned = turn(wide[:, part : part + 128], cosine, sine)
        q_ref[:, part : part + 128] = (turned * HEAD_SIZE**-0.5).astype(BF16)


def project(kernel, normed, weights, cosine, sine, start, columns, tile):
    rows, width = normed.shape
    whole = lambda i: (0, 0)
    return pl.pallas_call(
        kernel,
        out_shape=jax.ShapeDtypeStruct((rows, columns), BF16),
        grid=(columns // tile,),
        in_specs=[
            pl.BlockSpec((rows, width), whole),
            pl.BlockSpec((width, tile), lambda i: (0, start // tile + i)),
            pl.BlockSpec((rows, 128), whole),
            pl.BlockSpec((rows, 128), whole),
        ],
        out_specs=pl.BlockSpec((rows, tile), lambda i: (0, i)),
        compiler_params=pltpu.CompilerParams(vmem_limit_bytes=VMEM_LIMIT),
        cost_estimate=pl.CostEstimate(
            flops=2 * rows * width * columns,
            bytes_accessed=2 * (rows * width + width * columns + rows * columns),
            transcendentals=0,
        ),
    )(normed, weights, cosine, sine)


def set_up(place, kv0_ref, kv1_ref, kv2_ref, qseg_ref, kseg_ref, kk, vv, kvt, bias):
    low = lane_is_low((128, 128), 128)
    for block, ref in enumerate((kv0_ref, kv1_ref, kv2_ref)):
        for group in range(4):
            at = pl.multiple_of(lax.rem(group - place + 4, 4) * 128, 128)
            piece = ref[pl.ds(at, 128), :].astype(F32)
            rolled = pltpu.roll(piece, 64, 1)
            to = block * 512 + group * 128
            kk[to : to + 128, :] = jnp.where(low, piece, rolled).astype(BF16)
            vv[to : to + 128, :] = jnp.where(low, rolled, piece).astype(BF16)
            kvt[:, to : to + 128] = piece.T.astype(BF16)
    for tile in range(2):
        key = lax.broadcasted_iota(jnp.int32, (1280, 256), 0)
        query = lax.broadcasted_iota(jnp.int32, (1280, 256), 1)
        distance = query - key + WINDOW
        same = kseg_ref[256 * tile : 256 * tile + 1280, :] == qseg_ref[:, 256 * tile : 256 * tile + 256]
        seen = (distance >= 0) & (distance < WINDOW) & same
        bias[tile] = jnp.where(seen, 0.0, -jnp.inf)


def true_rows(ref, place, tile):
    pieces = []
    for group in (0, 1):
        at = pl.multiple_of(lax.rem(2 * tile + group - place + 4, 4) * 128, 128)
        pieces.append(ref[pl.ds(at, 128), :])
    return jnp.concatenate(pieces, 0)


def put_rows(ref, place, tile, value):
    for group in (0, 1):
        at = pl.multiple_of(lax.rem(2 * tile + group - place + 4, 4) * 128, 128)
        ref[pl.ds(at, 128), :] = value[128 * group : 128 * group + 128]


def attend_kernel(
    place_ref, q_ref, kv0_ref, kv1_ref, kv2_ref, qseg_ref, kseg_ref, o_ref, lse_ref, kk, vv, kvt, bias
):
    place = place_ref[0]

    @pl.when(pl.program_id(0) == 0)
    def _():
        set_up(place, kv0_ref, kv1_ref, kv2_ref, qseg_ref, kseg_ref, kk, vv, kvt, bias)

    low = lane_is_low((256, 128), 128)
    for tile in range(2):
        keys = slice(256 * tile, 256 * tile + 1280)
        pair = true_rows(q_ref, place, tile)
        results = []
        for head in range(2):
            query = jnp.where(low if head == 0 else ~low, pair, jnp.zeros_like(pair))
            scores = dot_nt(kk[keys, :], query) + bias[tile]
            top = jnp.max(scores, 0, keepdims=True)
            weights = jnp.exp(scores - top)
            total = jnp.sum(weights, 0, keepdims=True)
            results.append(dot_nn(kvt[64:128, keys], weights.astype(BF16)) / total)
            lse_ref[0, head : head + 1, 256 * tile : 256 * tile + 256] = top + jnp.log(total)
        put_rows(o_ref, place, tile, jnp.concatenate(results, 0).T.astype(BF16))


ATTENTION_SCRATCH = [
    pltpu.VMEM((1536, 128), BF16),
    pltpu.VMEM((1536, 128), BF16),
    pltpu.VMEM((128, 1536), BF16),
    pltpu.VMEM((2, 1280, 256), F32),
]


def attend(place, queries, kv, qseg, kseg):
    whole = lambda p, s: (0, 0)
    grid = pltpu.PrefetchScalarGridSpec(
        num_scalar_prefetch=1,
        grid=(4,),
        in_specs=[
            pl.BlockSpec((512, 128), lambda p, s: (0, p)),
            pl.BlockSpec((512, 128), whole),
            pl.BlockSpec((512, 128), whole),
            pl.BlockSpec((512, 128), whole),
            pl.BlockSpec((1, 512), whole),
            pl.BlockSpec((1536, 1), whole),
        ],
        out_specs=(
            pl.BlockSpec((512, 128), lambda p, s: (0, p)),
            pl.BlockSpec((1, 2, 512), lambda p, s: (p, 0, 0)),
        ),
        scratch_shapes=ATTENTION_SCRATCH,
    )
    return pl.pallas_call(
        attend_kernel,
        grid_spec=grid,
        out_shape=(
            jax.ShapeDtypeStruct((512, 512), BF16),
            jax.ShapeDtypeStruct((4, 2, 512), F32),
        ),
        compiler_params=pltpu.CompilerParams(vmem_limit_bytes=VMEM_LIMIT),
        cost_estimate=pl.CostEstimate(
            flops=8 * 512 * 1280 * 256 * 2, bytes_accessed=4 * 1024 * 1024, transcendentals=8 * 512 * 1280
        ),
    )(place, queries, *kv, qseg, kseg)


def attend_back_kernel(
    place_ref,
    q_ref,
    do_ref,
    lse_ref,
    kv0_ref,
    kv1_ref,
    kv2_ref,
    qseg_ref,
    kseg_ref,
    cos_ref,
    sin_ref,
    dq_ref,
    own_ref,
    earlier_ref,
    kk,
    vv,
    kvt,
    bias,
    dk,
    dv,
):
    place = place_ref[0]

    @pl.when(pl.program_id(0) == 0)
    def _():
        set_up(place, kv0_ref, kv1_ref, kv2_ref, qseg_ref, kseg_ref, kk, vv, kvt, bias)
        dk[...] = jnp.zeros_like(dk)
        dv[...] = jnp.zeros_like(dv)

    low = lane_is_low((256, 128), 128)
    for tile in range(2):
        keys = slice(256 * tile, 256 * tile + 1280)
        pair = true_rows(q_ref, place, tile)
        grad_pair = true_rows(do_ref, place, tile)
        results = []
        for head in range(2):
            mask = low if head == 0 else ~low
            query = jnp.where(mask, pair, jnp.zeros_like(pair))
            grad = jnp.where(mask, grad_pair, jnp.zeros_like(pair))
            scores = dot_nt(kk[keys, :], query) + bias[tile]
            weights = jnp.exp(scores - lse_ref[0, head : head + 1, 256 * tile : 256 * tile + 256])
            grad_weights = dot_nt(vv[keys, :], grad)
            dv[keys, :] += dot_nn(weights.astype(BF16), grad)
            inner = jnp.sum(weights * grad_weights, 0, keepdims=True)
            grad_scores = (weights * (grad_weights - inner)).astype(BF16)
            dk[keys, :] += dot_nn(grad_scores, query)
            results.append(dot_nn(kvt[0:64, keys], grad_scores))
        grad_query = jnp.concatenate(results, 0).T * HEAD_SIZE**-0.5
        turned = turn(
            grad_query, true_rows(cos_ref, place, tile), -true_rows(sin_ref, place, tile)
        )
        put_rows(dq_ref, place, tile, turned.astype(BF16))

    @pl.when(pl.program_id(0) == 3)
    def _():
        half = lane_is_low((128, 128), 128)
        for block in range(3):
            for group in range(4):
                at = pl.multiple_of(lax.rem(group - place + 4, 4) * 128, 128)
                frm = slice(block * 512 + group * 128, block * 512 + group * 128 + 128)
                key, value = dk[frm, :], dv[frm, :]
                key = key + pltpu.roll(key, 64, 1)
                value = value + pltpu.roll(value, 64, 1)
                both = jnp.where(half, key, value)
                if block == 2:
                    own_ref[pl.ds(at, 128), :] = both
                else:
                    earlier_ref[block, pl.ds(at, 128), :] = both.astype(BF16)


def attend_back(place, queries, grad_attended, lse, kv, qseg, kseg, cosine, sine):
    whole = lambda p, s: (0, 0)
    grid = pltpu.PrefetchScalarGridSpec(
        num_scalar_prefetch=1,
        grid=(4,),
        in_specs=[
            pl.BlockSpec((512, 128), lambda p, s: (0, p)),
            pl.BlockSpec((512, 128), lambda p, s: (0, p)),
            pl.BlockSpec((1, 2, 512), lambda p, s: (p, 0, 0)),
            pl.BlockSpec((512, 128), whole),
            pl.BlockSpec((512, 128), whole),
            pl.BlockSpec((512, 128), whole),
            pl.BlockSpec((1, 512), whole),
            pl.BlockSpec((1536, 1), whole),
            pl.BlockSpec((512, 128), whole),
            pl.BlockSpec((512, 128), whole),
        ],
        out_specs=(
            pl.BlockSpec((512, 128), lambda p, s: (0, p)),
            pl.BlockSpec((512, 128), whole),
            pl.BlockSpec((2, 512, 128), lambda p, s: (0, 0, 0)),
        ),
        scratch_shapes=ATTENTION_SCRATCH
        + [pltpu.VMEM((1536, 128), F32), pltpu.VMEM((1536, 128), F32)],
    )
    return pl.pallas_call(
        attend_back_kernel,
        grid_spec=grid,
        out_shape=(
            jax.ShapeDtypeStruct((512, 512), BF16),
            jax.ShapeDtypeStruct((512, 128), F32),
            jax.ShapeDtypeStruct((2, 512, 128), BF16),
        ),
        compiler_params=pltpu.CompilerParams(vmem_limit_bytes=VMEM_LIMIT),
        cost_estimate=pl.CostEstimate(
            flops=8 * 512 * 1280 * 640 * 2, bytes_accessed=6 * 1024 * 1024, transcendentals=8 * 512 * 1280
        ),
    )(place, queries, grad_attended, lse, *kv, qseg, kseg, cosine, sine)


HIDDEN = 1408
GROUPS = [(0, 128), (128, 256), (384, 512), (896, 512)]


def columns_times_kernel(left_ref, right_ref, out_ref):
    out_ref[...] = dot_nn(left_ref[...], right_ref[...])


def columns_times(left, right, part):
    rows, width = left.shape
    return pl.pallas_call(
        columns_times_kernel,
        out_shape=jax.ShapeDtypeStruct((rows, HIDDEN), F32),
        grid=(1,),
        in_specs=[
            pl.BlockSpec((rows, width), lambda i: (0, 0)),
            pl.BlockSpec((width, HIDDEN), lambda i: (0, part)),
        ],
        out_specs=pl.BlockSpec((rows, HIDDEN), lambda i: (0, 0)),
        compiler_params=pltpu.CompilerParams(vmem_limit_bytes=VMEM_LIMIT),
        cost_estimate=pl.CostEstimate(
            flops=2 * rows * width * HIDDEN, bytes_accessed=11 * 1024 * 1024, transcendentals=0
        ),
    )(left, right)


def ffn_kernel(x_ref, dact_ref, w_ref, gua_ref, dx_ref, x_held, dact_held, w_held, gua, dx, sems, out_sems):
    x_copy = pltpu.make_async_copy(x_ref, x_held, sems.at[12])
    x_copy.start()
    copies = []
    for number, (start, width) in enumerate(GROUPS):
        for part in range(3):
            if part < 2:
                columns = pl.ds(part * HIDDEN + start, width)
                copy = pltpu.make_async_copy(
                    w_ref.at[:, columns], w_held.at[:, columns], sems.at[3 * number + part]
                )
            else:
                columns = pl.ds(start, width)
                copy = pltpu.make_async_copy(
                    dact_ref.at[:, columns], dact_held.at[:, columns], sems.at[3 * number + part]
                )
            copy.start()
            copies.append(copy)
    x_copy.wait()
    x = x_held[...]
    results = []
    for number, (start, width) in enumerate(GROUPS):
        for part in range(3):
            copies[3 * number + part].wait()
        gate = dot_nn(x, w_held[:, start : start + width])
        up = dot_nn(x, w_held[:, HIDDEN + start : HIDDEN + start + width])
        dact = dact_held[:, start : start + width]
        sig = jax.nn.sigmoid(gate)
        silu = gate * sig
        dgate = dact * up * (sig * (1.0 + gate * (1.0 - sig)))
        gua[:, start : start + width] = dgate.astype(BF16)
        gua[:, HIDDEN + start : HIDDEN + start + width] = (dact * silu).astype(BF16)
        gua[:, 2 * HIDDEN + start : 2 * HIDDEN + start + width] = (silu * up).astype(BF16)
    copy = pltpu.make_async_copy(gua, gua_ref, out_sems.at[4])
    copy.start()
    results.append(copy)
    dgu = gua[:, : 2 * HIDDEN]
    for number in range(4):
        columns = slice(512 * number, 512 * number + 512)
        dx[:, columns] = dot_nt(dgu, w_held[columns, : 2 * HIDDEN]).astype(BF16)
        copy = pltpu.make_async_copy(
            dx.at[:, pl.ds(512 * number, 512)],
            dx_ref.at[:, pl.ds(512 * number, 512)],
            out_sems.at[number],
        )
        copy.start()
        results.append(copy)
    for copy in results:
        copy.wait()


def ffn(normed, dact, weights):
    rows, width = normed.shape
    anywhere = pl.BlockSpec(memory_space=pl.ANY)
    return pl.pallas_call(
        ffn_kernel,
        out_shape=(
            jax.ShapeDtypeStruct((rows, 3 * HIDDEN), BF16),
            jax.ShapeDtypeStruct((rows, width), BF16),
        ),
        in_specs=[anywhere, anywhere, anywhere],
        out_specs=(anywhere, anywhere),
        scratch_shapes=[
            pltpu.VMEM((rows, width), BF16),
            pltpu.VMEM((rows, HIDDEN), F32),
            pltpu.VMEM((width, 2 * HIDDEN), BF16),
            pltpu.VMEM((rows, 3 * HIDDEN), BF16),
            pltpu.VMEM((rows, width), BF16),
            pltpu.SemaphoreType.DMA((13,)),
            pltpu.SemaphoreType.DMA((5,)),
        ],
        compiler_params=pltpu.CompilerParams(vmem_limit_bytes=VMEM_LIMIT),
        cost_estimate=pl.CostEstimate(
            flops=8 * rows * width * HIDDEN,
            bytes_accessed=25 * 1024 * 1024,
            transcendentals=rows * HIDDEN,
        ),
    )(normed, dact, weights)


OUT_COLUMNS = 512
GRAD_COLUMNS = 3 * HIDDEN + OUT_COLUMNS


def weight_grads_kernel(core_ref, x_ref, x2_ref, dy_ref, dy2_ref, right_ref, right2_ref, out_ref):
    part = pl.program_id(0)

    @pl.when(part < 2)
    def _():
        total = dot_tn(x_ref[...], right_ref[...]) + dot_tn(x2_ref[...], right2_ref[...])
        out_ref[...] = total.astype(BF16)

    @pl.when(part == 2)
    def _():
        total = dot_tn(dy_ref[...], right_ref[...]) + dot_tn(dy2_ref[...], right2_ref[...])
        out_ref[...] = total.astype(BF16)


def weight_grads(core, x, x2, dy, dy2, right, right2):
    rows = x.shape[0]
    tile = 512
    half = x2.shape[1]
    tiles = half // tile
    own = lambda j, i, c: (0, c[0] * tiles + i)
    other = lambda j, i, c: (0, i)
    side = lambda j, i, c: (0, j)
    grid = pltpu.PrefetchScalarGridSpec(
        num_scalar_prefetch=1,
        grid=(3, tiles),
        in_specs=[
            pl.BlockSpec((rows, tile), own),
            pl.BlockSpec((rows, tile), other),
            pl.BlockSpec((rows, tile), own),
            pl.BlockSpec((rows, tile), other),
            pl.BlockSpec((rows, HIDDEN), side),
            pl.BlockSpec((rows, HIDDEN), side),
        ],
        out_specs=pl.BlockSpec((tile, HIDDEN), lambda j, i, c: (i, j)),
    )
    return pl.pallas_call(
        weight_grads_kernel,
        grid_spec=grid,
        out_shape=jax.ShapeDtypeStruct((half, GRAD_COLUMNS), BF16),
        compiler_params=pltpu.CompilerParams(vmem_limit_bytes=VMEM_LIMIT),
        cost_estimate=pl.CostEstimate(
            flops=2 * 3 * 2 * rows * half * HIDDEN, bytes_accessed=24 * 1024 * 1024, transcendentals=0
        ),
    )(core, x, x2, dy, dy2, right, right2)


def out_grad_kernel(core_ref, held_ref, left_ref, left2_ref, right_ref, right2_ref, out_ref, total, sem):
    total[...] = (dot_tn(left_ref[...], right_ref[...]) + dot_tn(left2_ref[...], right2_ref[...])).astype(BF16)
    copy = pltpu.make_async_copy(total, out_ref.at[:, pl.ds(3 * HIDDEN, OUT_COLUMNS)], sem)
    copy.start()
    copy.wait()


def out_grad(core, held, left, left2, right, right2):
    rows = left.shape[0]
    half = left2.shape[1]
    whole = lambda i, c: (0, 0)
    grid = pltpu.PrefetchScalarGridSpec(
        num_scalar_prefetch=1,
        grid=(1,),
        in_specs=[
            pl.BlockSpec(memory_space=pl.ANY),
            pl.BlockSpec((rows, half), lambda i, c: (0, c[0])),
            pl.BlockSpec((rows, half), whole),
            pl.BlockSpec((rows, OUT_COLUMNS), whole),
            pl.BlockSpec((rows, OUT_COLUMNS), whole),
        ],
        out_specs=pl.BlockSpec(memory_space=pl.ANY),
        scratch_shapes=[pltpu.VMEM((half, OUT_COLUMNS), BF16), pltpu.SemaphoreType.DMA],
    )
    return pl.pallas_call(
        out_grad_kernel,
        grid_spec=grid,
        out_shape=jax.ShapeDtypeStruct((half, GRAD_COLUMNS), BF16),
        input_output_aliases={1: 0},
        compiler_params=pltpu.CompilerParams(vmem_limit_bytes=VMEM_LIMIT),
        cost_estimate=pl.CostEstimate(
            flops=2 * 2 * rows * half * OUT_COLUMNS, bytes_accessed=4 * 1024 * 1024, transcendentals=0
        ),
    )(core, held, left, left2, right, right2)


def rows_times_kernel(left_ref, right_ref, out_ref):
    out_ref[...] = dot_nt(left_ref[...], right_ref[...]).astype(BF16)


def rows_times(left, right, part):
    rows, depth = left.shape[0], HIDDEN
    width = right.shape[0]
    tile = 512
    return pl.pallas_call(
        rows_times_kernel,
        out_shape=jax.ShapeDtypeStruct((rows, width), BF16),
        grid=(width // tile,),
        in_specs=[
            pl.BlockSpec((rows, depth), lambda i: (0, part)),
            pl.BlockSpec((tile, depth), lambda i: (i, part)),
        ],
        out_specs=pl.BlockSpec((rows, tile), lambda i: (0, i)),
        compiler_params=pltpu.CompilerParams(vmem_limit_bytes=VMEM_LIMIT),
        cost_estimate=pl.CostEstimate(
            flops=2 * rows * depth * width,
            bytes_accessed=2 * (rows * depth + width * depth + rows * width),
            transcendentals=0,
        ),
    )(left, right)


def finish_kernel(
    x_ref, w_ref, dq_ref, own_ref, one_ref, two_ref, cos_ref, sin_ref, norm_ref, grad_ref, dx_ref, gain_ref, dqkv, sums
):
    @pl.when(pl.program_id(0) == 0)
    def _():
        dqkv[:, :512] = dq_ref[...]
        dkv = own_ref[...] + one_ref[...].astype(F32) + two_ref[...].astype(F32)
        turned = turn(dkv, cos_ref[...], -sin_ref[...])
        dqkv[:, 512:] = jnp.where(lane_is_low(dkv.shape, 128), turned, dkv).astype(BF16)

    grads, x = dqkv[...], x_ref[...]
    grad_ref[...] = dot_tn(x, grads).astype(BF16)
    dx = dot_nt(grads, w_ref[...])
    dx_ref[...] = dx.astype(BF16)
    columns = pl.ds(pl.multiple_of(pl.program_id(0) * 512, 512), 512)
    sums[:, columns] = jnp.broadcast_to(
        jnp.sum(dx * x.astype(F32), 0, keepdims=True) / norm_ref[...], (8, 512)
    )

    @pl.when(pl.program_id(0) == 3)
    def _():
        gain_ref[...] = jnp.concatenate(block_major_tiles(in_tiles(sums[...])), 1)[:1]


def finish(normed, weights, dq, own, one, two, cosine, sine, gain):
    rows, width = normed.shape
    tile = 512
    whole = lambda i: (0, 0)
    return pl.pallas_call(
        finish_kernel,
        out_shape=(
            jax.ShapeDtypeStruct((width, 640), BF16),
            jax.ShapeDtypeStruct((rows, width), BF16),
            jax.ShapeDtypeStruct((1, width), F32),
        ),
        grid=(width // tile,),
        in_specs=[
            pl.BlockSpec((rows, tile), lambda i: (0, i)),
            pl.BlockSpec((tile, 640), lambda i: (i, 0)),
            pl.BlockSpec((rows, 512), whole),
            pl.BlockSpec((rows, 128), whole),
            pl.BlockSpec((rows, 128), whole),
            pl.BlockSpec((rows, 128), whole),
            pl.BlockSpec((rows, 128), whole),
            pl.BlockSpec((rows, 128), whole),
            pl.BlockSpec((1, tile), lambda i: (0, i)),
        ],
        out_specs=(
            pl.BlockSpec((tile, 640), lambda i: (i, 0)),
            pl.BlockSpec((rows, tile), lambda i: (0, i)),
            pl.BlockSpec((1, width), whole),
        ),
        scratch_shapes=[pltpu.VMEM((rows, 640), BF16), pltpu.VMEM((8, width), F32)],
        compiler_params=pltpu.CompilerParams(vmem_limit_bytes=VMEM_LIMIT),
        cost_estimate=pl.CostEstimate(
            flops=4 * rows * width * 640, bytes_accessed=11 * 1024 * 1024, transcendentals=0
        ),
    )(normed, weights, dq, own, one, two, cosine, sine, gain)


def per_device(
    tokens,
    segments,
    w_query,
    key_projection,
    value_projection,
    w_out,
    w_gate,
    w_up,
    w_down,
    norm_attn,
    norm_ffn,
    cotangent,
):
    place, core = lax.axis_index("head"), lax.axis_index("core")
    block = (lax.axis_index("y") * 4 + lax.axis_index("x")) * 2 + core
    place_array = place.astype(jnp.int32).reshape(1)
    core_array = core.astype(jnp.int32).reshape(1)
    keep = lax.optimization_barrier

    attention_weights = lax.all_gather(
        jnp.concatenate([w_query, key_projection, value_projection, w_out.T], 1),
        CORE_FIRST,
        axis=0,
        tiled=True,
    )
    ffn_weights = lax.all_gather(
        jnp.concatenate([w_gate, w_up, w_down.T], 1), CORE_FIRST, axis=0, tiled=True
    )
    out_t = attention_weights[:, 640:]

    x_rows, dy_rows, normed_rows, gain_one, gain_two = prepare(
        tokens[0],
        cotangent[0],
        jnp.broadcast_to(norm_attn[None], (16, 2048)),
        jnp.broadcast_to(norm_ffn[None], (16, 2048)),
    )
    gain_one, gain_two = gain_one[:1], gain_two[:1]
    scale_one = scale_of(x_rows)
    normed_one = gather_head(normed_rows)

    row = jnp.arange(512, dtype=jnp.int32)
    positions = block * 512 + ((row // 128 + place) % 4) * 128 + row % 128
    frequency = 10000.0 ** (-jnp.arange(32, dtype=F32) * 2.0 / HEAD_SIZE)
    angles = positions.astype(F32)[:, None] * frequency[None, :]
    cosine, sine = jnp.cos(angles), jnp.sin(angles)
    cosine = jnp.concatenate([cosine] * 4, 1)
    sine = jnp.concatenate([-sine, sine, -sine, sine], 1)

    kv_own = project(project_kv_kernel, normed_one, attention_weights, cosine, sine, 512, 128, 128)
    normed_late, kv_own = keep((normed_one, kv_own))
    kv = (from_block(kv_own, 2), from_block(kv_own, 1), kv_own)
    queries = project(project_q_kernel, normed_late, attention_weights, cosine, sine, 0, 512, 256)

    flat = segments.reshape(-1)
    padded = jnp.concatenate([jnp.full((1024,), -1, jnp.int32), flat])
    qseg = lax.dynamic_slice_in_dim(flat, block * 512, 512, 0).reshape(1, 512)
    kseg = lax.dynamic_slice_in_dim(padded, block * 512, 1536, 0).reshape(1536, 1)

    dy_rows_late, queries, kv = keep((dy_rows, queries, kv))
    dy = gather_head_direct(dy_rows_late)
    attended, lse = attend(place_array, queries, kv, qseg, kseg)
    attended, dy = keep((attended, dy))
    attended_other = shift(attended, "core", 1)
    dy_other = swap_half(dy, core)
    h1 = x_rows + scatter_head(dot_nt(attended, out_t).astype(BF16))
    scale_two = scale_of(h1)
    normed_two = gather_head((h1 * scale_two * gain_two).astype(BF16))
    dact = columns_times(dy, ffn_weights, 2)
    normed_two, dact, attended_other, dy_other = keep((normed_two, dact, attended_other, dy_other))

    gua, dnormed_two = ffn(normed_two, dact, ffn_weights)
    gua_other = shift(gua, "core", 1)
    normed_two_other = swap_half(normed_two, core)
    dnormed_two, (gua_other, normed_two_other) = scatter_head(dnormed_two, (gua_other, normed_two_other))
    held = weight_grads(core_array, normed_two, normed_two_other, dy, dy_other, gua, gua_other)
    held, dnormed_two = keep((held, dnormed_two))

    dh1 = dy_rows.astype(F32) + norm_backward(h1, scale_two, gain_two, dnormed_two)
    grad_gain_two = jnp.sum(dnormed_two * h1 * scale_two, 0, keepdims=True)
    grad_gain_two = to_blocks(jnp.broadcast_to(grad_gain_two, (8, 2048)), F32)[:1]
    dh1_low = gather_head(dh1.astype(BF16))
    late_gua, dnormed_two = keep((gua, dnormed_two))
    out_partial = rows_times(late_gua, ffn_weights, 2)
    out_partial, dh1_low = keep((out_partial, dh1_low))
    dh1_other = swap_half(dh1_low, core)
    dattended = dot_nn(dh1_low, out_t).astype(BF16)
    held = out_grad(core_array, held, dh1_low, dh1_other, attended, attended_other)
    held, dattended = keep((held, dattended))
    grads = lax.psum_scatter(held, ("y", "x"), scatter_dimension=0, tiled=True)

    output = to_blocks(h1 + scatter_head_direct(out_partial), BF16)
    dq, dkv_own, dkv_earlier = attend_back(
        place_array, queries, dattended, lse, kv, qseg, kseg, cosine, sine
    )
    dq, output = keep((dq, output))
    dkv_one = from_block(dkv_earlier[1], -1)
    dkv_two = from_block(dkv_earlier[0], -2)

    grad_qkv, dnormed_one, grad_gain_one = finish(
        normed_one, attention_weights, dq, dkv_own, dkv_one, dkv_two, cosine, sine, gain_one
    )
    dnormed_one = scatter_head(dnormed_one)
    grad_inputs = dh1 + norm_backward(x_rows, scale_one, gain_one, dnormed_one)
    gains = jnp.concatenate([grad_gain_one[0], grad_gain_two[0], jnp.zeros((16 * 640 - 4096,), F32)])
    attention_grads, gains = scatter_blocks(grad_qkv, gains.reshape(16, 640))
    gains = sum_head(gains.reshape(-1)[:4096].reshape(2, 2048))

    return (
        output[None],
        to_blocks(grad_inputs, BF16)[None],
        attention_grads[:, :512],
        attention_grads[:, 512:576],
        attention_grads[:, 576:640],
        grads[:, 3 * HIDDEN :].T.astype(F32),
        grads[:, :HIDDEN].astype(F32),
        grads[:, HIDDEN : 2 * HIDDEN].astype(F32),
        grads[:, 2 * HIDDEN : 3 * HIDDEN].T.astype(F32),
        gains[0],
        gains[1],
    )


def solution(mesh):
    grid = Mesh(mesh.devices.reshape(4, 4, 4, 2), ("head", "y", "x", "core"))
    rows, up, down = P(BLK, "head", None), P(BLK, "head"), P("head", BLK)
    return jax.shard_map(
        per_device,
        mesh=grid,
        in_specs=(rows, P(), up, up, up, down, up, up, down, P(), P(), rows),
        out_specs=(rows, rows, up, up, up, down, up, up, down, P(), P()),
        check_vma=False,
    )
```

```python
import functools

import jax
import jax.numpy as jnp
from jax import lax
from jax.experimental import pallas as pl
from jax.experimental.pallas import tpu as pltpu
from jax.sharding import Mesh
from jax.sharding import PartitionSpec as P

HEAD_SIZE = 64
WINDOW = 1024
EPSILON = 1e-05
BF16 = jnp.bfloat16
F32 = jnp.float32
BLK = ("y", "x", "core")
CORE_FIRST = ("core", "y", "x")
VMEM_LIMIT = 56 * 1024 * 1024


def dot_nn(a, b):
    return jnp.dot(a, b, preferred_element_type=F32)


def dot_nt(a, b):
    return lax.dot_general(a, b, (((1,), (1,)), ((), ())), preferred_element_type=F32)


def dot_tn(a, b):
    return lax.dot_general(a, b, (((0,), (0,)), ((), ())), preferred_element_type=F32)


def shift(value, axis, distance):
    size = lax.axis_size(axis)
    return lax.ppermute(value, axis, [(i, (i + distance) % size) for i in range(size)])


def add_low(a, b):
    return (a.astype(F32) + b.astype(F32)).astype(BF16)


def gather_pieces(rows, beside=None):
    half = rows.shape[0] // 2
    ahead, behind = shift(rows, "head", -1), shift(rows, "head", 1)
    if beside is not None:
        ahead, behind, beside = lax.optimization_barrier((ahead, behind, beside))
    far_top = shift(behind[:half], "head", 1)
    far_bottom = shift(ahead[half:], "head", -1)
    pieces = ahead, far_top, far_bottom, behind
    return pieces if beside is None else (pieces, beside)


def gather_head(rows):
    return jnp.concatenate([rows, *gather_pieces(rows)], 0)


def scatter_pieces(own, ahead, far_top, far_bottom, behind, beside=None):
    half = far_top.shape[0]
    far_top, far_bottom = shift(far_top, "head", 1), shift(far_bottom, "head", -1)
    if beside is not None:
        far_top, far_bottom, beside = lax.optimization_barrier((far_top, far_bottom, beside))
    ahead = jnp.concatenate([add_low(ahead[:half], far_top), ahead[half:]], 0)
    behind = jnp.concatenate([behind[:half], add_low(behind[half:], far_bottom)], 0)
    ahead, behind = shift(ahead, "head", 1), shift(behind, "head", -1)
    total = own.astype(F32) + (ahead.astype(F32) + behind.astype(F32))
    return total if beside is None else (total, beside)


def swap_half(value, core):
    width = value.shape[1] // 2
    return shift(lax.dynamic_slice_in_dim(value, (1 - core) * width, width, 1), "core", 1)


def gather_head_direct(rows):
    ahead, behind, far = shift(rows, "head", -1), shift(rows, "head", 1), shift(rows, "head", 2)
    return jnp.concatenate([rows, ahead, far, behind], 0)


def scatter_head_direct(partial):
    n = partial.shape[0] // 4
    own, ahead, far, behind = (partial[k * n : (k + 1) * n] for k in range(4))
    ahead, behind, far = shift(ahead, "head", 1), shift(behind, "head", -1), shift(far, "head", 2)
    return (own.astype(F32) + far.astype(F32)) + (ahead.astype(F32) + behind.astype(F32))


def scatter_axis(value, extra, axis):
    index = lax.axis_index(axis)
    rows = value.shape[1]

    def send(distance):
        piece = lax.dynamic_index_in_dim(value, (index + distance) % 4, 0, False)
        moved = shift(jnp.concatenate([piece, extra], 0), axis, 2 if distance == 2 else distance)
        return moved.astype(F32)

    own = jnp.concatenate([lax.dynamic_index_in_dim(value, index, 0, False), extra], 0)
    total = (own.astype(F32) + send(1)) + (send(-1) + send(2))
    return total[:rows], total[rows:]


def scatter_blocks(other, own, extra):
    columns = own.shape[1]
    pair = add_low(own, shift(other, "core", 1))
    extra = extra + shift(extra, "core", 1)
    pair = pair.reshape(4, 4, 64, columns).transpose(1, 0, 2, 3).reshape(4, 256, columns)
    part, extra = scatter_axis(pair, extra.astype(BF16), "x")
    part = part.astype(BF16).reshape(4, 64, columns)
    return scatter_axis(part, extra.astype(BF16), "y")


def sum_head(value):
    return (value + shift(value, "head", 1)) + (shift(value, "head", -1) + shift(value, "head", 2))


def from_block(value, distance):
    route = [(i, i + distance) for i in range(32) if 0 <= i + distance < 32]
    return lax.ppermute(value, BLK, route)


def scale_of(values):
    return lax.rsqrt(jnp.mean(values * values, -1, keepdims=True) + EPSILON)


def norm_backward(values, scale, gain, grad):
    weighted = grad * gain
    inner = jnp.mean(weighted * values, -1, keepdims=True)
    return scale * weighted - values * (scale * scale * scale * inner)


def lane_is_low(shape, period):
    return lax.broadcasted_iota(jnp.int32, shape, len(shape) - 1) % period < period // 2


def turn(values, cosine, sine):
    swapped = jnp.where(
        lane_is_low(values.shape, 64), pltpu.roll(values, 96, 1), pltpu.roll(values, 32, 1)
    )
    return values * cosine + swapped * sine


def core_major_tiles(tiles):
    low = lane_is_low(tiles[0].shape, 128)
    rolled = [pltpu.roll(tile, 64, 1) for tile in tiles]
    first = [jnp.where(low, tiles[2 * k], rolled[2 * k + 1]) for k in range(8)]
    second = [jnp.where(low, rolled[2 * k], tiles[2 * k + 1]) for k in range(8)]
    return first + second


def block_major_tiles(tiles):
    low = lane_is_low(tiles[0].shape, 128)
    rolled = [pltpu.roll(tile, 64, 1) for tile in tiles]
    result = []
    for k in range(8):
        result.append(jnp.where(low, tiles[k], rolled[8 + k]))
        result.append(jnp.where(low, rolled[k], tiles[8 + k]))
    return result


def in_tiles(value):
    return [value[:, 128 * k : 128 * k + 128] for k in range(16)]


def prepare_kernel(x_ref, dy_ref, gain_one_ref, gain_two_ref, x_out, dy_out, normed_out, one_out, two_out):
    def convert(ref):
        return jnp.concatenate(core_major_tiles(in_tiles(ref[...].astype(F32))), 1)

    x, gain = convert(x_ref), convert(gain_one_ref)
    one_out[...], two_out[...] = gain, convert(gain_two_ref)
    x_out[...] = x
    dy_out[...] = convert(dy_ref).astype(BF16)
    normed_out[...] = (x * scale_of(x) * gain[:1]).astype(BF16)


def prepare(x, dy, gain_one, gain_two):
    rows, width = x.shape
    return pl.pallas_call(
        prepare_kernel,
        out_shape=(
            jax.ShapeDtypeStruct((rows, width), F32),
            jax.ShapeDtypeStruct((rows, width), BF16),
            jax.ShapeDtypeStruct((rows, width), BF16),
            jax.ShapeDtypeStruct((16, width), F32),
            jax.ShapeDtypeStruct((16, width), F32),
        ),
        compiler_params=pltpu.CompilerParams(vmem_limit_bytes=VMEM_LIMIT),
        cost_estimate=pl.CostEstimate(
            flops=10 * rows * width, bytes_accessed=10 * rows * width, transcendentals=rows
        ),
    )(x, dy, gain_one, gain_two)


def to_blocks_kernel(value_ref, out_ref):
    out_ref[...] = jnp.concatenate(block_major_tiles(in_tiles(value_ref[...])), 1).astype(out_ref.dtype)


def to_blocks(value, dtype):
    return pl.pallas_call(
        to_blocks_kernel,
        out_shape=jax.ShapeDtypeStruct(value.shape, dtype),
        compiler_params=pltpu.CompilerParams(vmem_limit_bytes=VMEM_LIMIT),
        cost_estimate=pl.CostEstimate(flops=2 * value.size, bytes_accessed=6 * value.size, transcendentals=0),
    )(value)


def project_kv_kernel(x_ref, w_ref, cos_ref, sin_ref, kv_ref):
    flat = dot_nn(x_ref[...], w_ref[...])
    turned = turn(flat, cos_ref[...], sin_ref[...])
    kv_ref[...] = jnp.where(lane_is_low(flat.shape, 128), turned, flat).astype(BF16)


def project_q_kernel(x_ref, w_ref, cos_ref, sin_ref, q_ref):
    cosine, sine = cos_ref[...], sin_ref[...]
    wide = dot_nn(x_ref[...], w_ref[...])
    for part in (0, 128):
        turned = turn(wide[:, part : part + 128], cosine, sine)
        q_ref[:, part : part + 128] = (turned * HEAD_SIZE**-0.5).astype(BF16)


def project(kernel, normed, weights, cosine, sine, start, columns, tile):
    rows, width = normed.shape
    whole = lambda i: (0, 0)
    return pl.pallas_call(
        kernel,
        out_shape=jax.ShapeDtypeStruct((rows, columns), BF16),
        grid=(columns // tile,),
        in_specs=[
            pl.BlockSpec((rows, width), whole),
            pl.BlockSpec((width, tile), lambda i: (0, start // tile + i)),
            pl.BlockSpec((rows, 128), whole),
            pl.BlockSpec((rows, 128), whole),
        ],
        out_specs=pl.BlockSpec((rows, tile), lambda i: (0, i)),
        compiler_params=pltpu.CompilerParams(vmem_limit_bytes=VMEM_LIMIT),
        cost_estimate=pl.CostEstimate(
            flops=2 * rows * width * columns,
            bytes_accessed=2 * (rows * width + width * columns + rows * columns),
            transcendentals=0,
        ),
    )(normed, weights, cosine, sine)


KEYS = 1152


def set_up_kernel(place_ref, kv0_ref, kv1_ref, kv2_ref, kk_ref, vv_ref, kvt_ref):
    place = place_ref[0]
    low = lane_is_low((128, 128), 128)
    for block, ref in enumerate((kv0_ref, kv1_ref, kv2_ref)):
        for group in range(4):
            at = pl.multiple_of(lax.rem(group - place + 4, 4) * 128, 128)
            piece = ref[pl.ds(at, 128), :].astype(F32)
            rolled = pltpu.roll(piece, 64, 1)
            to = block * 512 + group * 128
            kk_ref[to : to + 128, :] = jnp.where(low, piece, rolled).astype(BF16)
            vv_ref[to : to + 128, :] = jnp.where(low, rolled, piece).astype(BF16)
            kvt_ref[:, to : to + 128] = piece.T.astype(BF16)


def set_up(place, kv):
    vmem = pl.BlockSpec(memory_space=pltpu.VMEM)
    return pl.pallas_call(
        set_up_kernel,
        out_shape=(
            jax.ShapeDtypeStruct((1536, 128), BF16),
            jax.ShapeDtypeStruct((1536, 128), BF16),
            jax.ShapeDtypeStruct((128, 1536), BF16),
        ),
        in_specs=[pl.BlockSpec(memory_space=pltpu.SMEM), vmem, vmem, vmem],
        out_specs=(vmem, vmem, vmem),
        compiler_params=pltpu.CompilerParams(vmem_limit_bytes=VMEM_LIMIT),
        cost_estimate=pl.CostEstimate(flops=1536 * 128 * 8, bytes_accessed=2 * 1024 * 1024, transcendentals=0),
    )(place, *kv)


def both_heads(pair):
    low = lane_is_low(pair.shape, 128)
    nothing = jnp.zeros_like(pair)
    return jnp.concatenate([jnp.where(low, pair, nothing), jnp.where(low, nothing, pair)], 0)


def side_by_side(transposed):
    return jnp.concatenate([transposed[:, :128], transposed[:, 128:]], 0).T


def mask_of(at, qseg_ref, kseg_ref):
    key = lax.broadcasted_iota(jnp.int32, (KEYS, 128), 0)
    query = lax.broadcasted_iota(jnp.int32, (KEYS, 128), 1)
    distance = query - key + WINDOW
    same = kseg_ref[pl.ds(at, KEYS), :] == qseg_ref[:, pl.ds(at, 128)]
    seen = (distance >= 0) & (distance < WINDOW) & same
    bias = jnp.where(seen, 0.0, -jnp.inf)
    return jnp.concatenate([bias, bias], 1)


def attend_kernel(
    first, step, place_ref, q_ref, kk_ref, kvt_ref, qseg_ref, kseg_ref, w_ref, o_ref, lse_ref, part_ref, bias, held
):
    pair = pl.program_id(1)
    group = lax.rem(place_ref[0] + first + step * pl.program_id(0), 4)
    at = pl.multiple_of(group * 128, 128)

    @pl.when(pair == 0)
    def _():
        bias[...] = mask_of(at, qseg_ref, kseg_ref)

    scores = dot_nt(kk_ref[pl.ds(at, KEYS), :], both_heads(q_ref[...])) + bias[...]
    top = jnp.max(scores, 0, keepdims=True)
    weights = jnp.exp(scores - top)
    total = jnp.sum(weights, 0, keepdims=True)
    result = dot_nn(kvt_ref[64:128, pl.ds(at, KEYS)], weights.astype(BF16)) / total
    lse_ref[0, 0] = top + jnp.log(total)
    result = side_by_side(result).astype(BF16)
    o_ref[...] = result
    held[pair] = result

    @pl.when(pair == 3)
    def _():
        rows = jnp.concatenate([held[k] for k in range(4)], 1)
        part_ref[...] = dot_nt(rows, w_ref[...]).astype(BF16)


def attend(first, step, count, place, queries, kk, kvt, qseg, kseg, out_t):
    whole = lambda g, p, s: (0, 0)
    grid = pltpu.PrefetchScalarGridSpec(
        num_scalar_prefetch=1,
        grid=(count, 4),
        in_specs=[
            pl.BlockSpec((128, 128), lambda g, p, s: (first + step * g, p)),
            pl.BlockSpec((1536, 128), whole),
            pl.BlockSpec((128, 1536), whole),
            pl.BlockSpec((1, 512), whole),
            pl.BlockSpec((1536, 1), whole),
            pl.BlockSpec((2048, 512), whole),
        ],
        out_specs=(
            pl.BlockSpec((128, 128), lambda g, p, s: (g, p)),
            pl.BlockSpec((1, 1, 1, 256), lambda g, p, s: (g, p, 0, 0)),
            pl.BlockSpec((128, 2048), lambda g, p, s: (g, 0)),
        ),
        scratch_shapes=[pltpu.VMEM((KEYS, 256), F32), pltpu.VMEM((4, 128, 128), BF16)],
    )
    return pl.pallas_call(
        functools.partial(attend_kernel, first, step),
        grid_spec=grid,
        out_shape=(
            jax.ShapeDtypeStruct((128 * count, 512), BF16),
            jax.ShapeDtypeStruct((count, 4, 1, 256), F32),
            jax.ShapeDtypeStruct((128 * count, 2048), BF16),
        ),
        compiler_params=pltpu.CompilerParams(vmem_limit_bytes=VMEM_LIMIT),
        cost_estimate=pl.CostEstimate(
            flops=count * 4 * KEYS * 256 * 256 * 2,
            bytes_accessed=3 * 1024 * 1024,
            transcendentals=count * 4 * KEYS * 256,
        ),
    )(place, queries, kk, kvt, qseg, kseg, out_t)


def attend_back_kernel(first, step, last, *refs):
    place_ref, q_ref, dh_ref, w_ref, lse_ref, kk_ref, vv_ref, kvt_ref, qseg_ref, kseg_ref, cos_ref, sin_ref = refs[:12]
    if first == 0:
        dk_in, dv_in, refs = None, None, refs[12:]
    else:
        dk_in, dv_in, refs = refs[12], refs[13], refs[14:]
    dq_ref, one_out, two_out, bias, do_held, dk, dv = refs
    number, pair = pl.program_id(0), pl.program_id(1)
    place = place_ref[0]
    at = pl.multiple_of(lax.rem(place + first + step * number, 4) * 128, 128)

    @pl.when((number == 0) & (pair == 0))
    def _():
        dk[...] = jnp.zeros_like(dk) if dk_in is None else dk_in[...]
        dv[...] = jnp.zeros_like(dv) if dv_in is None else dv_in[...]

    @pl.when(pair == 0)
    def _():
        bias[...] = mask_of(at, qseg_ref, kseg_ref)
        do_rows = dot_nn(dh_ref[...], w_ref[...]).astype(BF16)
        for k in range(4):
            do_held[k] = do_rows[:, 128 * k : 128 * k + 128]

    keys = pl.ds(at, KEYS)
    query, grad = both_heads(q_ref[...]), both_heads(do_held[pair])
    scores = dot_nt(kk_ref[keys, :], query) + bias[...]
    weights = jnp.exp(scores - lse_ref[0, 0])
    grad_weights = dot_nt(vv_ref[keys, :], grad)
    dv[keys, :] += dot_nn(weights.astype(BF16), grad)
    inner = jnp.sum(weights * grad_weights, 0, keepdims=True)
    grad_scores = (weights * (grad_weights - inner)).astype(BF16)
    dk[keys, :] += dot_nn(grad_scores, query)
    grad_query = side_by_side(dot_nn(kvt_ref[0:64, keys], grad_scores)) * HEAD_SIZE**-0.5
    dq_ref[...] = turn(grad_query, cos_ref[...], -sin_ref[...]).astype(BF16)

    @pl.when((number == pl.num_programs(0) - 1) & (pair == 3))
    def _():
        if not last:
            one_out[...], two_out[...] = dk[...], dv[...]
            return
        half = lane_is_low((128, 128), 128)
        for block in range(3):
            for group in range(4):
                to = pl.multiple_of(lax.rem(group - place + 4, 4) * 128, 128)
                frm = slice(block * 512 + group * 128, block * 512 + group * 128 + 128)
                key, value = dk[frm, :], dv[frm, :]
                key = key + pltpu.roll(key, 64, 1)
                value = value + pltpu.roll(value, 64, 1)
                both = jnp.where(half, key, value)
                if block == 2:
                    one_out[pl.ds(to, 128), :] = both
                else:
                    two_out[block, pl.ds(to, 128), :] = both.astype(BF16)


def attend_back(first, step, count, place, queries, dh, out_t, lse, kk, vv, kvt, qseg, kseg, cosine, sine, held):
    last = first == 2
    whole = lambda g, p, s: (0, 0)
    specs = [
        pl.BlockSpec((128, 128), lambda g, p, s: (first + step * g, p)),
        pl.BlockSpec((128, 2048), lambda g, p, s: (g, 0)),
        pl.BlockSpec((2048, 512), whole),
        pl.BlockSpec((1, 1, 1, 256), lambda g, p, s: (g, p, 0, 0)),
        pl.BlockSpec((1536, 128), whole),
        pl.BlockSpec((1536, 128), whole),
        pl.BlockSpec((128, 1536), whole),
        pl.BlockSpec((1, 512), whole),
        pl.BlockSpec((1536, 1), whole),
        pl.BlockSpec((128, 128), lambda g, p, s: (first + step * g, 0)),
        pl.BlockSpec((128, 128), lambda g, p, s: (first + step * g, 0)),
    ] + [pl.BlockSpec((1536, 128), whole)] * len(held)
    if last:
        out_specs = (pl.BlockSpec((512, 128), whole), pl.BlockSpec((2, 512, 128), lambda g, p, s: (0, 0, 0)))
        out_shape = (jax.ShapeDtypeStruct((512, 128), F32), jax.ShapeDtypeStruct((2, 512, 128), BF16))
    else:
        out_specs = (pl.BlockSpec((1536, 128), whole),) * 2
        out_shape = (jax.ShapeDtypeStruct((1536, 128), F32),) * 2
    grid = pltpu.PrefetchScalarGridSpec(
        num_scalar_prefetch=1,
        grid=(count, 4),
        in_specs=specs,
        out_specs=(pl.BlockSpec((128, 128), lambda g, p, s: (g, p)),) + out_specs,
        scratch_shapes=[
            pltpu.VMEM((KEYS, 256), F32),
            pltpu.VMEM((4, 128, 128), BF16),
            pltpu.VMEM((1536, 128), F32),
            pltpu.VMEM((1536, 128), F32),
        ],
    )
    return pl.pallas_call(
        functools.partial(attend_back_kernel, first, step, last),
        grid_spec=grid,
        out_shape=(jax.ShapeDtypeStruct((128 * count, 512), BF16),) + out_shape,
        compiler_params=pltpu.CompilerParams(vmem_limit_bytes=VMEM_LIMIT),
        cost_estimate=pl.CostEstimate(
            flops=count * 4 * KEYS * 256 * 640 * 2,
            bytes_accessed=6 * 1024 * 1024,
            transcendentals=count * 4 * KEYS * 256,
        ),
    )(place, queries, dh, out_t, lse, kk, vv, kvt, qseg, kseg, cosine, sine, *held)


HIDDEN = 1408
GROUPS = [(0, 128), (128, 256), (384, 512), (896, 512)]


def columns_times_kernel(left_ref, right_ref, out_ref):
    out_ref[...] = dot_nn(left_ref[...], right_ref[...])


def columns_times(left, right, part):
    rows, width = left.shape
    return pl.pallas_call(
        columns_times_kernel,
        out_shape=jax.ShapeDtypeStruct((rows, HIDDEN), F32),
        grid=(1,),
        in_specs=[
            pl.BlockSpec((rows, width), lambda i: (0, 0)),
            pl.BlockSpec((width, HIDDEN), lambda i: (0, part)),
        ],
        out_specs=pl.BlockSpec((rows, HIDDEN), lambda i: (0, 0)),
        compiler_params=pltpu.CompilerParams(vmem_limit_bytes=VMEM_LIMIT),
        cost_estimate=pl.CostEstimate(
            flops=2 * rows * width * HIDDEN, bytes_accessed=11 * 1024 * 1024, transcendentals=0
        ),
    )(left, right)


PIECES = [(0, 128), (128, 128), (256, 64), (320, 64), (384, 128)]


def ffn_kernel(*refs):
    x_refs, dact_ref, w_ref, gua_ref, whole_ref, dx_refs = refs[:5], refs[5], refs[6], refs[7], refs[8], refs[9:14]
    x_held, dact_held, w_held, gua, dx, sems, out_sems = refs[14:]
    x_copies = []
    for number, (start, size) in enumerate(PIECES):
        copy = pltpu.make_async_copy(
            x_refs[number], x_held.at[pl.ds(start, size)], sems.at[12 + number]
        )
        copy.start()
        x_copies.append(copy)
    copies = []
    for number, (start, width) in enumerate(GROUPS):
        for part in range(3):
            if part < 2:
                columns = pl.ds(part * HIDDEN + start, width)
                copy = pltpu.make_async_copy(
                    w_ref.at[:, columns], w_held.at[:, columns], sems.at[3 * number + part]
                )
            else:
                columns = pl.ds(start, width)
                copy = pltpu.make_async_copy(
                    dact_ref.at[:, columns], dact_held.at[:, columns], sems.at[3 * number + part]
                )
            copy.start()
            copies.append(copy)
    for copy in x_copies:
        copy.wait()
    results = [pltpu.make_async_copy(x_held, whole_ref, out_sems.at[6])]
    results[0].start()
    x = x_held[...]
    for number, (start, width) in enumerate(GROUPS):
        for part in range(3):
            copies[3 * number + part].wait()
        gate = dot_nn(x, w_held[:, start : start + width])
        up = dot_nn(x, w_held[:, HIDDEN + start : HIDDEN + start + width])
        dact = dact_held[:, start : start + width]
        sig = jax.nn.sigmoid(gate)
        silu = gate * sig
        dgate = dact * up * (sig * (1.0 + gate * (1.0 - sig)))
        gua[:, start : start + width] = dgate.astype(BF16)
        gua[:, HIDDEN + start : HIDDEN + start + width] = (dact * silu).astype(BF16)
        gua[:, 2 * HIDDEN + start : 2 * HIDDEN + start + width] = (silu * up).astype(BF16)
    copy = pltpu.make_async_copy(gua, gua_ref, out_sems.at[5])
    copy.start()
    results.append(copy)
    dgu = gua[:, : 2 * HIDDEN]
    for number in range(4):
        columns = slice(512 * number, 512 * number + 512)
        dx[:, columns] = dot_nt(dgu, w_held[columns, : 2 * HIDDEN]).astype(BF16)
    for number, (start, size) in enumerate(PIECES):
        copy = pltpu.make_async_copy(dx.at[pl.ds(start, size)], dx_refs[number], out_sems.at[number])
        copy.start()
        results.append(copy)
    for copy in results:
        copy.wait()


def ffn(pieces, dact, weights):
    rows, width = dact.shape[0], weights.shape[0]
    anywhere = pl.BlockSpec(memory_space=pl.ANY)
    result = pl.pallas_call(
        ffn_kernel,
        out_shape=(
            jax.ShapeDtypeStruct((rows, 3 * HIDDEN), BF16),
            jax.ShapeDtypeStruct((rows, width), BF16),
            *(jax.ShapeDtypeStruct((size, width), BF16) for _, size in PIECES),
        ),
        in_specs=[anywhere] * 7,
        out_specs=(anywhere,) * 7,
        scratch_shapes=[
            pltpu.VMEM((rows, width), BF16),
            pltpu.VMEM((rows, HIDDEN), F32),
            pltpu.VMEM((width, 2 * HIDDEN), BF16),
            pltpu.VMEM((rows, 3 * HIDDEN), BF16),
            pltpu.VMEM((rows, width), BF16),
            pltpu.SemaphoreType.DMA((17,)),
            pltpu.SemaphoreType.DMA((7,)),
        ],
        compiler_params=pltpu.CompilerParams(vmem_limit_bytes=VMEM_LIMIT),
        cost_estimate=pl.CostEstimate(
            flops=8 * rows * width * HIDDEN,
            bytes_accessed=25 * 1024 * 1024,
            transcendentals=rows * HIDDEN,
        ),
    )(*pieces, dact, weights)
    return result[0], result[1], result[2:]


OUT_COLUMNS = 512
GRAD_COLUMNS = 3 * HIDDEN + OUT_COLUMNS


def weight_grads_kernel(core_ref, x_ref, x2_ref, dy_ref, dy2_ref, right_ref, right2_ref, out_ref):
    part = pl.program_id(0)

    @pl.when(part < 2)
    def _():
        total = dot_tn(x_ref[...], right_ref[...]) + dot_tn(x2_ref[...], right2_ref[...])
        out_ref[...] = total.astype(BF16)

    @pl.when(part == 2)
    def _():
        total = dot_tn(dy_ref[...], right_ref[...]) + dot_tn(dy2_ref[...], right2_ref[...])
        out_ref[...] = total.astype(BF16)


def weight_grads(core, x, x2, dy, dy2, right, right2):
    rows = x.shape[0]
    tile = 512
    half = x2.shape[1]
    tiles = half // tile
    own = lambda j, i, c: (0, c[0] * tiles + i)
    other = lambda j, i, c: (0, i)
    side = lambda j, i, c: (0, j)
    grid = pltpu.PrefetchScalarGridSpec(
        num_scalar_prefetch=1,
        grid=(3, tiles),
        in_specs=[
            pl.BlockSpec((rows, tile), own),
            pl.BlockSpec((rows, tile), other),
            pl.BlockSpec((rows, tile), own),
            pl.BlockSpec((rows, tile), other),
            pl.BlockSpec((rows, HIDDEN), side),
            pl.BlockSpec((rows, HIDDEN), side),
        ],
        out_specs=pl.BlockSpec((tile, HIDDEN), lambda j, i, c: (i, j)),
    )
    return pl.pallas_call(
        weight_grads_kernel,
        grid_spec=grid,
        out_shape=jax.ShapeDtypeStruct((half, GRAD_COLUMNS), BF16),
        compiler_params=pltpu.CompilerParams(vmem_limit_bytes=VMEM_LIMIT),
        cost_estimate=pl.CostEstimate(
            flops=2 * 3 * 2 * rows * half * HIDDEN, bytes_accessed=24 * 1024 * 1024, transcendentals=0
        ),
    )(core, x, x2, dy, dy2, right, right2)


def out_grad_kernel(core_ref, held_ref, left_ref, left2_ref, right_ref, right2_ref, out_ref, total, sem):
    total[...] = (dot_tn(left_ref[...], right_ref[...]) + dot_tn(left2_ref[...], right2_ref[...])).astype(BF16)
    copy = pltpu.make_async_copy(total, out_ref.at[:, pl.ds(3 * HIDDEN, OUT_COLUMNS)], sem)
    copy.start()
    copy.wait()


def out_grad(core, held, left, left2, right, right2):
    rows = left.shape[0]
    half = left2.shape[1]
    whole = lambda i, c: (0, 0)
    grid = pltpu.PrefetchScalarGridSpec(
        num_scalar_prefetch=1,
        grid=(1,),
        in_specs=[
            pl.BlockSpec(memory_space=pl.ANY),
            pl.BlockSpec((rows, half), lambda i, c: (0, c[0])),
            pl.BlockSpec((rows, half), whole),
            pl.BlockSpec((rows, OUT_COLUMNS), whole),
            pl.BlockSpec((rows, OUT_COLUMNS), whole),
        ],
        out_specs=pl.BlockSpec(memory_space=pl.ANY),
        scratch_shapes=[pltpu.VMEM((half, OUT_COLUMNS), BF16), pltpu.SemaphoreType.DMA],
    )
    return pl.pallas_call(
        out_grad_kernel,
        grid_spec=grid,
        out_shape=jax.ShapeDtypeStruct((half, GRAD_COLUMNS), BF16),
        input_output_aliases={1: 0},
        compiler_params=pltpu.CompilerParams(vmem_limit_bytes=VMEM_LIMIT),
        cost_estimate=pl.CostEstimate(
            flops=2 * 2 * rows * half * OUT_COLUMNS, bytes_accessed=4 * 1024 * 1024, transcendentals=0
        ),
    )(core, held, left, left2, right, right2)


def rows_times_kernel(left_ref, right_ref, out_ref):
    out_ref[...] = dot_nt(left_ref[...], right_ref[...]).astype(BF16)


def rows_times(left, right, part):
    rows, depth = left.shape[0], HIDDEN
    width = right.shape[0]
    tile = 512
    return pl.pallas_call(
        rows_times_kernel,
        out_shape=jax.ShapeDtypeStruct((rows, width), BF16),
        grid=(width // tile,),
        in_specs=[
            pl.BlockSpec((rows, depth), lambda i: (0, part)),
            pl.BlockSpec((tile, depth), lambda i: (i, part)),
        ],
        out_specs=pl.BlockSpec((rows, tile), lambda i: (0, i)),
        compiler_params=pltpu.CompilerParams(vmem_limit_bytes=VMEM_LIMIT),
        cost_estimate=pl.CostEstimate(
            flops=2 * rows * depth * width,
            bytes_accessed=2 * (rows * depth + width * depth + rows * width),
            transcendentals=0,
        ),
    )(left, right)


def finish_kernel(
    core_ref,
    x_ref,
    w_ref,
    dq0_ref,
    dq1_ref,
    dq2_ref,
    own_ref,
    one_ref,
    two_ref,
    cos_ref,
    sin_ref,
    norm_ref,
    other_grad_ref,
    own_grad_ref,
    dx_own,
    dx_ahead,
    dx_far_top,
    dx_far_bottom,
    dx_behind,
    gain_ref,
    dqkv,
    sums,
):
    number = pl.program_id(0)

    @pl.when(number == 0)
    def _():
        dqkv[:128, :512] = dq0_ref[...]
        dqkv[128:256, :512] = dq1_ref[:128]
        dqkv[256:384, :512] = dq2_ref[...]
        dqkv[384:, :512] = dq1_ref[128:]
        dkv = own_ref[...] + one_ref[...].astype(F32) + two_ref[...].astype(F32)
        turned = turn(dkv, cos_ref[...], -sin_ref[...])
        dqkv[:, 512:] = jnp.where(lane_is_low(dkv.shape, 128), turned, dkv).astype(BF16)

    grads, x = dqkv[...], x_ref[...]
    weight_grad = dot_tn(x, grads).astype(BF16)

    @pl.when(number < 2)
    def _():
        other_grad_ref[...] = weight_grad

    @pl.when(number >= 2)
    def _():
        own_grad_ref[...] = weight_grad

    dx = dot_nt(grads, w_ref[...])
    for (start, size), ref in zip(PIECES, (dx_own, dx_ahead, dx_far_top, dx_far_bottom, dx_behind)):
        ref[...] = dx[start : start + size].astype(BF16)
    tile = lax.rem(number + 2 * (1 - core_ref[0]), 4)
    columns = pl.ds(pl.multiple_of(tile * 512, 512), 512)
    sums[:, columns] = jnp.broadcast_to(
        jnp.sum(dx * x.astype(F32), 0, keepdims=True) / norm_ref[...], (8, 512)
    )

    @pl.when(number == 3)
    def _():
        gain_ref[...] = jnp.concatenate(block_major_tiles(in_tiles(sums[...])), 1)[:1]


def finish(core, normed, weights, dq, own, one, two, cosine, sine, gain):
    rows, width = normed.shape
    tile = 512
    whole = lambda i, c: (0, 0)
    at = lambda i, c: lax.rem(i + 2 * (1 - c[0]), 4)
    grid = pltpu.PrefetchScalarGridSpec(
        num_scalar_prefetch=1,
        grid=(4,),
        in_specs=[
            pl.BlockSpec((rows, tile), lambda i, c: (0, at(i, c))),
            pl.BlockSpec((tile, 640), lambda i, c: (at(i, c), 0)),
            pl.BlockSpec((128, 512), whole),
            pl.BlockSpec((256, 512), whole),
            pl.BlockSpec((128, 512), whole),
            pl.BlockSpec((rows, 128), whole),
            pl.BlockSpec((rows, 128), whole),
            pl.BlockSpec((rows, 128), whole),
            pl.BlockSpec((rows, 128), whole),
            pl.BlockSpec((rows, 128), whole),
            pl.BlockSpec((1, tile), lambda i, c: (0, at(i, c))),
        ],
        out_specs=(
            pl.BlockSpec((tile, 640), lambda i, c: (jnp.minimum(i, 1), 0)),
            pl.BlockSpec((tile, 640), lambda i, c: (jnp.maximum(i - 2, 0), 0)),
            *(pl.BlockSpec((size, tile), lambda i, c: (0, at(i, c))) for _, size in PIECES),
            pl.BlockSpec((1, width), whole),
        ),
        scratch_shapes=[pltpu.VMEM((rows, 640), BF16), pltpu.VMEM((8, width), F32)],
    )
    result = pl.pallas_call(
        finish_kernel,
        grid_spec=grid,
        out_shape=(
            jax.ShapeDtypeStruct((width // 2, 640), BF16),
            jax.ShapeDtypeStruct((width // 2, 640), BF16),
            *(jax.ShapeDtypeStruct((size, width), BF16) for _, size in PIECES),
            jax.ShapeDtypeStruct((1, width), F32),
        ),
        compiler_params=pltpu.CompilerParams(vmem_limit_bytes=VMEM_LIMIT),
        cost_estimate=pl.CostEstimate(
            flops=4 * rows * width * 640, bytes_accessed=11 * 1024 * 1024, transcendentals=0
        ),
    )(core, normed, weights, *dq, own, one, two, cosine, sine, gain)
    return result[0], result[1], result[2:7], result[7]


def per_device(
    tokens,
    segments,
    w_query,
    key_projection,
    value_projection,
    w_out,
    w_gate,
    w_up,
    w_down,
    norm_attn,
    norm_ffn,
    cotangent,
):
    place, core = lax.axis_index("head"), lax.axis_index("core")
    block = (lax.axis_index("y") * 4 + lax.axis_index("x")) * 2 + core
    place_array = place.astype(jnp.int32).reshape(1)
    core_array = core.astype(jnp.int32).reshape(1)
    keep = lax.optimization_barrier

    attention_weights = lax.all_gather(
        jnp.concatenate([w_query, key_projection, value_projection, w_out.T], 1),
        CORE_FIRST,
        axis=0,
        tiled=True,
    )
    ffn_weights = lax.all_gather(
        jnp.concatenate([w_gate, w_up, w_down.T], 1), CORE_FIRST, axis=0, tiled=True
    )
    out_t = attention_weights[:, 640:]

    x_rows, dy_rows, normed_rows, gain_one, gain_two = prepare(
        tokens[0],
        cotangent[0],
        jnp.broadcast_to(norm_attn[None], (16, 2048)),
        jnp.broadcast_to(norm_ffn[None], (16, 2048)),
    )
    gain_one, gain_two = gain_one[:1], gain_two[:1]
    scale_one = scale_of(x_rows)
    normed_one = gather_head(normed_rows)
    normed_one, dy_rows_late = keep((normed_one, dy_rows))
    dy = gather_head_direct(dy_rows_late)

    row = jnp.arange(512, dtype=jnp.int32)
    positions = block * 512 + ((row // 128 + place) % 4) * 128 + row % 128
    frequency = 10000.0 ** (-jnp.arange(32, dtype=F32) * 2.0 / HEAD_SIZE)
    angles = positions.astype(F32)[:, None] * frequency[None, :]
    cosine, sine = jnp.cos(angles), jnp.sin(angles)
    cosine = jnp.concatenate([cosine] * 4, 1)
    sine = jnp.concatenate([-sine, sine, -sine, sine], 1)

    kv_own = project(project_kv_kernel, normed_one, attention_weights, cosine, sine, 512, 128, 128)
    normed_late, kv_own, dy = keep((normed_one, kv_own, dy))
    kv = (from_block(kv_own, 2), from_block(kv_own, 1), kv_own)
    queries = project(project_q_kernel, normed_late, attention_weights, cosine, sine, 0, 512, 256)

    flat = segments.reshape(-1)
    padded = jnp.concatenate([jnp.full((1024,), -1, jnp.int32), flat])
    qseg = lax.dynamic_slice_in_dim(flat, block * 512, 512, 0).reshape(1, 512)
    kseg = lax.dynamic_slice_in_dim(padded, block * 512, 1536, 0).reshape(1536, 1)

    kk, vv, kvt = set_up(place_array, kv)
    seen = place_array, queries, kk, kvt, qseg, kseg, out_t
    o_far, lse_far, part_far = attend(2, 1, 1, *seen)
    o_near, lse_near, part_near = attend(1, 2, 2, *seen)
    o_own, lse_own, part_own = attend(0, 1, 1, *seen)
    dy_other = swap_half(dy, core)
    attention_sum = scatter_pieces(
        part_own, part_near[:128], part_far[:64], part_far[64:], part_near[128:]
    )
    h1 = x_rows + attention_sum
    scale_two = scale_of(h1)
    normed_rows_two = (h1 * scale_two * gain_two).astype(BF16)
    dact = columns_times(dy, ffn_weights, 2)
    pieces, (dact, dy_other) = gather_pieces(normed_rows_two, (dact, dy_other))

    gua, normed_two, dnormed_two = ffn((normed_rows_two, *pieces), dact, ffn_weights)
    gua_other = shift(gua, "core", 1)
    normed_two_other = swap_half(normed_two, core)
    dnormed_two, (gua_other, normed_two_other) = scatter_pieces(*dnormed_two, (gua_other, normed_two_other))
    held = weight_grads(core_array, normed_two, normed_two_other, dy, dy_other, gua, gua_other)
    held, dnormed_two = keep((held, dnormed_two))

    dh1 = dy_rows.astype(F32) + norm_backward(h1, scale_two, gain_two, dnormed_two)
    dh1_low = dh1.astype(BF16)
    back = kk, vv, kvt, qseg, kseg, cosine, sine
    dq_own, dk, dv = attend_back(0, 1, 1, place_array, queries, dh1_low, out_t, lse_own, *back, ())
    (ahead, far_top, far_bottom, behind), (dk, dv) = gather_pieces(dh1_low, (dk, dv))
    near = jnp.concatenate([ahead, behind], 0)
    dq_near, dk, dv = attend_back(1, 2, 2, place_array, queries, near, out_t, lse_near, *back, (dk, dv))
    far_top, far_bottom, dk, dv = keep((far_top, far_bottom, dk, dv))
    far = jnp.concatenate([far_top, far_bottom], 0)

    dh1_all = jnp.concatenate([dh1_low, ahead, far, behind], 0)
    dh1_other = swap_half(dh1_all, core)
    attended = jnp.concatenate([o_own, o_near[:128], o_far, o_near[128:]], 0)
    attended_other = shift(attended, "core", 1)
    held = out_grad(core_array, held, dh1_all, dh1_other, attended, attended_other)
    grads = lax.psum_scatter(held, ("y", "x"), scatter_dimension=0, tiled=True)

    dq_far, dkv_own, dkv_earlier = attend_back(
        2, 1, 1, place_array, queries, far, out_t, lse_far, *back, (dk, dv)
    )
    dkv_one = from_block(dkv_earlier[1], -1)
    dkv_two = from_block(dkv_earlier[0], -2)
    late_gua, late_dnormed_two, dq_far = keep((gua, dnormed_two, dq_far))
    out_partial = rows_times(late_gua, ffn_weights, 2)
    grad_gain_two = jnp.sum(late_dnormed_two * h1 * scale_two, 0, keepdims=True)
    grad_gain_two = to_blocks(jnp.broadcast_to(grad_gain_two, (8, 2048)), F32)[:1]
    dkv_one, dkv_two, out_partial, grad_gain_two = keep((dkv_one, dkv_two, out_partial, grad_gain_two))

    other_grad, own_grad, dnormed_one, grad_gain_one = finish(
        core_array,
        normed_one,
        attention_weights,
        (dq_own, dq_near, dq_far),
        dkv_own,
        dkv_one,
        dkv_two,
        cosine,
        sine,
        gain_one,
    )
    dnormed_one = scatter_pieces(*dnormed_one)
    grad_inputs = dh1 + norm_backward(x_rows, scale_one, gain_one, dnormed_one)
    gains = jnp.concatenate([grad_gain_one[0], grad_gain_two[0], jnp.zeros((16 * 640 - 4096,), F32)])
    attention_grads, gains = scatter_blocks(other_grad, own_grad, gains.reshape(16, 640))
    gains = sum_head(gains.reshape(-1)[:4096].reshape(2, 2048))
    output = to_blocks(h1 + scatter_head_direct(out_partial), BF16)

    return (
        output[None],
        to_blocks(grad_inputs, BF16)[None],
        attention_grads[:, :512],
        attention_grads[:, 512:576],
        attention_grads[:, 576:640],
        grads[:, 3 * HIDDEN :].T.astype(F32),
        grads[:, :HIDDEN].astype(F32),
        grads[:, HIDDEN : 2 * HIDDEN].astype(F32),
        grads[:, 2 * HIDDEN : 3 * HIDDEN].T.astype(F32),
        gains[0],
        gains[1],
    )


def solution(mesh):
    grid = Mesh(mesh.devices.reshape(4, 4, 4, 2), ("head", "y", "x", "core"))
    rows, up, down = P(BLK, "head", None), P(BLK, "head"), P("head", BLK)
    return jax.shard_map(
        per_device,
        mesh=grid,
        in_specs=(rows, P(), up, up, up, down, up, up, down, P(), P(), rows),
        out_specs=(rows, rows, up, up, up, down, up, up, down, P(), P()),
        check_vma=False,
    )
```

```python
import functools

import jax
import jax.numpy as jnp
from jax import lax
from jax.experimental import pallas as pl
from jax.experimental.pallas import tpu as pltpu
from jax.sharding import Mesh
from jax.sharding import PartitionSpec as P

HEAD_SIZE = 64
WINDOW = 1024
EPSILON = 1e-05
BF16 = jnp.bfloat16
F32 = jnp.float32
BLK = ("y", "x", "core")
CORE_FIRST = ("core", "y", "x")
VMEM_LIMIT = 56 * 1024 * 1024


def dot_nn(a, b):
    return jnp.dot(a, b, preferred_element_type=F32)


def dot_nt(a, b):
    return lax.dot_general(a, b, (((1,), (1,)), ((), ())), preferred_element_type=F32)


def dot_tn(a, b):
    return lax.dot_general(a, b, (((0,), (0,)), ((), ())), preferred_element_type=F32)


def shift(value, axis, distance):
    size = lax.axis_size(axis)
    return lax.ppermute(value, axis, [(i, (i + distance) % size) for i in range(size)])


def add_low(a, b):
    return (a.astype(F32) + b.astype(F32)).astype(BF16)


def gather_pieces(rows, beside=None):
    half = rows.shape[0] // 2
    ahead, behind = shift(rows, "head", -1), shift(rows, "head", 1)
    if beside is not None:
        ahead, behind, beside = lax.optimization_barrier((ahead, behind, beside))
    far_top = shift(behind[:half], "head", 1)
    far_bottom = shift(ahead[half:], "head", -1)
    pieces = ahead, far_top, far_bottom, behind
    return pieces if beside is None else (pieces, beside)


def gather_head(rows):
    return jnp.concatenate([rows, *gather_pieces(rows)], 0)


def scatter_pieces(own, ahead, far_top, far_bottom, behind, beside=None):
    far_top, far_bottom = shift(far_top, "head", 1), shift(far_bottom, "head", -1)
    if beside is not None:
        far_top, far_bottom, beside = lax.optimization_barrier((far_top, far_bottom, beside))
    ahead, behind = add_halves(ahead, behind, far_top, far_bottom)
    pieces = own, shift(ahead, "head", 1), shift(behind, "head", -1)
    return pieces if beside is None else (pieces, beside)


def swap_half(value, core):
    width = value.shape[1] // 2
    return shift(lax.dynamic_slice_in_dim(value, (1 - core) * width, width, 1), "core", 1)


def gather_head_direct(rows):
    ahead, behind, far = shift(rows, "head", -1), shift(rows, "head", 1), shift(rows, "head", 2)
    return jnp.concatenate([rows, ahead, far, behind], 0)


def scatter_direct(own, ahead, far, behind):
    return own, shift(ahead, "head", 1), shift(behind, "head", -1), shift(far, "head", 2)


def exchange(pieces, axis):
    return pieces[0], shift(pieces[1], axis, 1), shift(pieces[2], axis, 2), shift(pieces[3], axis, -1)


def from_block(value, distance):
    route = [(i, i + distance) for i in range(32) if 0 <= i + distance < 32]
    return lax.ppermute(value, BLK, route)


def scale_of(values):
    return lax.rsqrt(jnp.mean(values * values, -1, keepdims=True) + EPSILON)


def lane_is_low(shape, period):
    return lax.broadcasted_iota(jnp.int32, shape, len(shape) - 1) % period < period // 2


def turn(values, cosine, sine):
    swapped = jnp.where(
        lane_is_low(values.shape, 64), pltpu.roll(values, 96, 1), pltpu.roll(values, 32, 1)
    )
    return values * cosine + swapped * sine


def core_major_tiles(tiles):
    low = lane_is_low(tiles[0].shape, 128)
    rolled = [pltpu.roll(tile, 64, 1) for tile in tiles]
    first = [jnp.where(low, tiles[2 * k], rolled[2 * k + 1]) for k in range(8)]
    second = [jnp.where(low, rolled[2 * k], tiles[2 * k + 1]) for k in range(8)]
    return first + second


def block_major_tiles(tiles):
    low = lane_is_low(tiles[0].shape, 128)
    rolled = [pltpu.roll(tile, 64, 1) for tile in tiles]
    result = []
    for k in range(8):
        result.append(jnp.where(low, tiles[k], rolled[8 + k]))
        result.append(jnp.where(low, rolled[k], tiles[8 + k]))
    return result


def in_tiles(value):
    return [value[:, 128 * k : 128 * k + 128] for k in range(16)]


def prepare_kernel(x_ref, dy_ref, gain_one_ref, gain_two_ref, x_out, dy_out, normed_out, one_out, two_out):
    def convert(ref):
        return jnp.concatenate(core_major_tiles(in_tiles(ref[...].astype(F32))), 1)

    x, gain = convert(x_ref), convert(gain_one_ref)
    one_out[...], two_out[...] = gain, convert(gain_two_ref)
    x_out[...] = x
    dy_out[...] = convert(dy_ref).astype(BF16)
    normed_out[...] = (x * scale_of(x) * gain[:1]).astype(BF16)


def prepare(x, dy, gain_one, gain_two):
    rows, width = x.shape
    return pl.pallas_call(
        prepare_kernel,
        out_shape=(
            jax.ShapeDtypeStruct((rows, width), F32),
            jax.ShapeDtypeStruct((rows, width), BF16),
            jax.ShapeDtypeStruct((rows, width), BF16),
            jax.ShapeDtypeStruct((16, width), F32),
            jax.ShapeDtypeStruct((16, width), F32),
        ),
        compiler_params=pltpu.CompilerParams(vmem_limit_bytes=VMEM_LIMIT),
        cost_estimate=pl.CostEstimate(
            flops=10 * rows * width, bytes_accessed=10 * rows * width, transcendentals=rows
        ),
    )(x, dy, gain_one, gain_two)


def to_blocks(value):
    return jnp.concatenate(block_major_tiles(in_tiles(value)), 1)


def small_call(kernel, out_shape, *operands):
    return pl.pallas_call(
        kernel,
        out_shape=tuple(jax.ShapeDtypeStruct(shape, dtype) for shape, dtype in out_shape),
        compiler_params=pltpu.CompilerParams(vmem_limit_bytes=VMEM_LIMIT),
        cost_estimate=pl.CostEstimate(
            flops=sum(x.size for x in operands),
            bytes_accessed=2 * sum(x.size * x.dtype.itemsize for x in operands),
            transcendentals=0,
        ),
    )(*operands)


def total_of(refs):
    values = [ref[...].astype(F32) for ref in refs]
    while len(values) > 1:
        values = [values[0] + values[1]] + values[2:]
    return values[0]


def add_halves_kernel(ahead_ref, behind_ref, top_ref, bottom_ref, ahead_out, behind_out):
    half = top_ref.shape[0]
    ahead_out[:half] = add_low(ahead_ref[:half], top_ref[...])
    ahead_out[half:] = ahead_ref[half:]
    behind_out[:half] = behind_ref[:half]
    behind_out[half:] = add_low(behind_ref[half:], bottom_ref[...])


def add_halves(ahead, behind, top, bottom):
    return small_call(
        add_halves_kernel, ((ahead.shape, BF16), (behind.shape, BF16)), ahead, behind, top, bottom
    )


def join_kernel(x_ref, gain_ref, a_ref, b_ref, c_ref, h_out, normed_out):
    h = x_ref[...] + total_of((a_ref, b_ref, c_ref))
    h_out[...] = h
    normed_out[...] = (h * scale_of(h) * gain_ref[...]).astype(BF16)


def join(x, gain, pieces):
    return small_call(join_kernel, ((x.shape, F32), (x.shape, BF16)), x, gain, *pieces)


def norm_backward(values, gain, grad):
    scale = scale_of(values)
    weighted = grad * gain
    inner = jnp.mean(weighted * values, -1, keepdims=True)
    return scale * weighted - values * (scale * scale * scale * inner), scale


def join_back_kernel(h_ref, dy_ref, gain_ref, a_ref, b_ref, c_ref, dh_out, low_out, grad_out):
    h, grad = h_ref[...], total_of((a_ref, b_ref, c_ref))
    back, scale = norm_backward(h, gain_ref[...], grad)
    dh = dy_ref[...].astype(F32) + back
    dh_out[...] = dh
    low_out[...] = dh.astype(BF16)
    grad_out[...] = to_blocks(jnp.broadcast_to(jnp.sum(grad * h * scale, 0, keepdims=True), (8, h.shape[1])))


def join_back(h, dy, gain, pieces):
    shapes = (h.shape, F32), (h.shape, BF16), ((8, h.shape[1]), F32)
    return small_call(join_back_kernel, shapes, h, dy, gain, *pieces)


def output_kernel(h_ref, a_ref, b_ref, c_ref, d_ref, out_ref):
    out_ref[...] = to_blocks(h_ref[...] + total_of((a_ref, b_ref, c_ref, d_ref))).astype(BF16)


def input_grad_kernel(dh_ref, x_ref, gain_ref, a_ref, b_ref, c_ref, d_ref, out_ref):
    back, _ = norm_backward(x_ref[...], gain_ref[...], total_of((a_ref, b_ref, c_ref, d_ref)))
    out_ref[...] = to_blocks(dh_ref[...] + back).astype(BF16)


GAIN_ROWS, GAIN_COLUMNS = 16, 256


def gain_rows(vector):
    return jnp.concatenate([vector[:, 256 * k : 256 * k + 256] for k in range(8)], 0)


def put_piece(ref, rows, gains):
    count = rows.shape[0]
    ref[:count] = rows
    ref[count:, GAIN_COLUMNS:] = jnp.zeros((GAIN_ROWS, ref.shape[1] - GAIN_COLUMNS), BF16)
    ref[count:, :GAIN_COLUMNS] = gains.astype(BF16)


def pieces_x_kernel(at_ref, wide_ref, wide2_ref, narrow_ref, narrow2_ref, gain_ref, gain2_ref, *out_refs):
    wide = add_low(wide_ref[...], wide2_ref[...]).reshape(256, wide_ref.shape[3])
    narrow = add_low(narrow_ref[...], narrow2_ref[...]).reshape(256, narrow_ref.shape[3])
    rows = jnp.concatenate([wide, narrow], 1)
    gains = gain_ref[...] + gain2_ref[...]
    for number, ref in enumerate(out_refs):

        @pl.when(pl.program_id(0) == number)
        def _():
            put_piece(ref, rows, gains)


def pieces_x(at, wide, wide2, narrow, narrow2, gains, gains2):
    columns = wide.shape[1] + narrow.shape[1]
    pick = lambda d, s: (0, lax.rem(s[0] + d, 4), 0, 0)
    spec = lambda value: pl.BlockSpec((4, 1, 64, value.shape[1]), pick)
    whole = lambda d, s: (0, 0)
    shaped = lambda value: value.reshape(4, 4, 64, value.shape[1])
    grid = pltpu.PrefetchScalarGridSpec(
        num_scalar_prefetch=1,
        grid=(4,),
        in_specs=[spec(wide), spec(wide), spec(narrow), spec(narrow)]
        + [pl.BlockSpec((GAIN_ROWS, GAIN_COLUMNS), whole)] * 2,
        out_specs=(pl.BlockSpec((256 + GAIN_ROWS, columns), whole),) * 4,
    )
    return pl.pallas_call(
        pieces_x_kernel,
        grid_spec=grid,
        out_shape=(jax.ShapeDtypeStruct((256 + GAIN_ROWS, columns), BF16),) * 4,
        compiler_params=pltpu.CompilerParams(vmem_limit_bytes=VMEM_LIMIT),
        cost_estimate=pl.CostEstimate(
            flops=2 * 1024 * columns, bytes_accessed=6 * 1024 * columns, transcendentals=0
        ),
    )(at, shaped(wide), shaped(wide2), shaped(narrow), shaped(narrow2), gains, gains2)


def pieces_y_kernel(at_ref, a_ref, b_ref, c_ref, d_ref, *refs):
    held = refs[4]
    held[...] = total_of((a_ref, b_ref, c_ref, d_ref))
    for number, ref in enumerate(refs[:4]):
        start = pl.multiple_of(lax.rem(at_ref[0] + number, 4) * 64, 64)
        put_piece(ref, held[pl.ds(start, 64), :].astype(BF16), held[256:, :GAIN_COLUMNS])


def pieces_y(at, pieces):
    columns = pieces[0].shape[1]
    vmem = pl.BlockSpec(memory_space=pltpu.VMEM)
    return pl.pallas_call(
        pieces_y_kernel,
        out_shape=(jax.ShapeDtypeStruct((64 + GAIN_ROWS, columns), BF16),) * 4,
        in_specs=[pl.BlockSpec(memory_space=pltpu.SMEM)] + [vmem] * 4,
        out_specs=(vmem,) * 4,
        scratch_shapes=[pltpu.VMEM((256 + GAIN_ROWS, columns), F32)],
        compiler_params=pltpu.CompilerParams(vmem_limit_bytes=VMEM_LIMIT),
        cost_estimate=pl.CostEstimate(
            flops=4 * 272 * columns, bytes_accessed=10 * 272 * columns, transcendentals=0
        ),
    )(at, *pieces)


def attention_grads_kernel(a_ref, b_ref, c_ref, d_ref, out_ref, q_ref, k_ref, v_ref, gain_ref):
    total = total_of((a_ref, b_ref, c_ref, d_ref))
    out_ref[...] = total[:64, :512].T
    q_ref[...] = total[:64, 512:1024]
    k_ref[...] = total[:64, 1024:1088]
    v_ref[...] = total[:64, 1088:]
    gain_ref[...] = total[64:, :GAIN_COLUMNS]


def gains_kernel(a_ref, b_ref, c_ref, d_ref, one_ref, two_ref):
    total = total_of((a_ref, b_ref, c_ref, d_ref))
    one_ref[...] = jnp.concatenate([total[k : k + 1] for k in range(8)], 1)
    two_ref[...] = jnp.concatenate([total[k : k + 1] for k in range(8, 16)], 1)


def project_kv_kernel(x_ref, w_ref, cos_ref, sin_ref, kv_ref):
    flat = dot_nn(x_ref[...], w_ref[...])
    turned = turn(flat, cos_ref[...], sin_ref[...])
    kv_ref[...] = jnp.where(lane_is_low(flat.shape, 128), turned, flat).astype(BF16)


def project_q_kernel(x_ref, w_ref, cos_ref, sin_ref, q_ref):
    cosine, sine = cos_ref[...], sin_ref[...]
    wide = dot_nn(x_ref[...], w_ref[...])
    for part in (0, 128):
        turned = turn(wide[:, part : part + 128], cosine, sine)
        q_ref[:, part : part + 128] = (turned * HEAD_SIZE**-0.5).astype(BF16)


def project(kernel, normed, weights, cosine, sine, start, columns, tile):
    rows, width = normed.shape
    whole = lambda i: (0, 0)
    return pl.pallas_call(
        kernel,
        out_shape=jax.ShapeDtypeStruct((rows, columns), BF16),
        grid=(columns // tile,),
        in_specs=[
            pl.BlockSpec((rows, width), whole),
            pl.BlockSpec((width, tile), lambda i: (0, start // tile + i)),
            pl.BlockSpec((rows, 128), whole),
            pl.BlockSpec((rows, 128), whole),
        ],
        out_specs=pl.BlockSpec((rows, tile), lambda i: (0, i)),
        compiler_params=pltpu.CompilerParams(vmem_limit_bytes=VMEM_LIMIT),
        cost_estimate=pl.CostEstimate(
            flops=2 * rows * width * columns,
            bytes_accessed=2 * (rows * width + width * columns + rows * columns),
            transcendentals=0,
        ),
    )(normed, weights, cosine, sine)


KEYS = 1152


def set_up_kernel(place_ref, kv0_ref, kv1_ref, kv2_ref, kk_ref, vv_ref, kvt_ref):
    place = place_ref[0]
    low = lane_is_low((128, 128), 128)
    for block, ref in enumerate((kv0_ref, kv1_ref, kv2_ref)):
        for group in range(4):
            at = pl.multiple_of(lax.rem(group - place + 4, 4) * 128, 128)
            piece = ref[pl.ds(at, 128), :].astype(F32)
            rolled = pltpu.roll(piece, 64, 1)
            to = block * 512 + group * 128
            kk_ref[to : to + 128, :] = jnp.where(low, piece, rolled).astype(BF16)
            vv_ref[to : to + 128, :] = jnp.where(low, rolled, piece).astype(BF16)
            kvt_ref[:, to : to + 128] = piece.T.astype(BF16)


def set_up(place, kv):
    vmem = pl.BlockSpec(memory_space=pltpu.VMEM)
    return pl.pallas_call(
        set_up_kernel,
        out_shape=(
            jax.ShapeDtypeStruct((1536, 128), BF16),
            jax.ShapeDtypeStruct((1536, 128), BF16),
            jax.ShapeDtypeStruct((128, 1536), BF16),
        ),
        in_specs=[pl.BlockSpec(memory_space=pltpu.SMEM), vmem, vmem, vmem],
        out_specs=(vmem, vmem, vmem),
        compiler_params=pltpu.CompilerParams(vmem_limit_bytes=VMEM_LIMIT),
        cost_estimate=pl.CostEstimate(flops=1536 * 128 * 8, bytes_accessed=2 * 1024 * 1024, transcendentals=0),
    )(place, *kv)


def both_heads(pair):
    low = lane_is_low(pair.shape, 128)
    nothing = jnp.zeros_like(pair)
    return jnp.concatenate([jnp.where(low, pair, nothing), jnp.where(low, nothing, pair)], 0)


def side_by_side(transposed):
    return jnp.concatenate([transposed[:, :128], transposed[:, 128:]], 0).T


def mask_of(at, qseg_ref, kseg_ref):
    key = lax.broadcasted_iota(jnp.int32, (KEYS, 128), 0)
    query = lax.broadcasted_iota(jnp.int32, (KEYS, 128), 1)
    distance = query - key + WINDOW
    same = kseg_ref[pl.ds(at, KEYS), :] == qseg_ref[:, pl.ds(at, 128)]
    seen = (distance >= 0) & (distance < WINDOW) & same
    bias = jnp.where(seen, 0.0, -jnp.inf)
    return jnp.concatenate([bias, bias], 1)


def attend_kernel(
    first, step, place_ref, q_ref, kk_ref, kvt_ref, qseg_ref, kseg_ref, w_ref, o_ref, lse_ref, part_ref, bias, held
):
    pair = pl.program_id(1)
    group = lax.rem(place_ref[0] + first + step * pl.program_id(0), 4)
    at = pl.multiple_of(group * 128, 128)

    @pl.when(pair == 0)
    def _():
        bias[...] = mask_of(at, qseg_ref, kseg_ref)

    scores = dot_nt(kk_ref[pl.ds(at, KEYS), :], both_heads(q_ref[...])) + bias[...]
    top = jnp.max(scores, 0, keepdims=True)
    weights = jnp.exp(scores - top)
    total = jnp.sum(weights, 0, keepdims=True)
    result = dot_nn(kvt_ref[64:128, pl.ds(at, KEYS)], weights.astype(BF16)) / total
    lse_ref[0, 0] = top + jnp.log(total)
    result = side_by_side(result).astype(BF16)
    o_ref[...] = result
    held[pair] = result

    @pl.when(pair == 3)
    def _():
        rows = jnp.concatenate([held[k] for k in range(4)], 1)
        part_ref[...] = dot_nt(rows, w_ref[...]).astype(BF16)


def attend(first, step, count, place, queries, kk, kvt, qseg, kseg, attention_weights):
    whole = lambda g, p, s: (0, 0)
    grid = pltpu.PrefetchScalarGridSpec(
        num_scalar_prefetch=1,
        grid=(count, 4),
        in_specs=[
            pl.BlockSpec((128, 128), lambda g, p, s: (first + step * g, p)),
            pl.BlockSpec((1536, 128), whole),
            pl.BlockSpec((128, 1536), whole),
            pl.BlockSpec((1, 512), whole),
            pl.BlockSpec((1536, 1), whole),
            pl.BlockSpec((2048, 512), whole),
        ],
        out_specs=(
            pl.BlockSpec((128, 128), lambda g, p, s: (g, p)),
            pl.BlockSpec((1, 1, 1, 256), lambda g, p, s: (g, p, 0, 0)),
            pl.BlockSpec((128, 2048), lambda g, p, s: (g, 0)),
        ),
        scratch_shapes=[pltpu.VMEM((KEYS, 256), F32), pltpu.VMEM((4, 128, 128), BF16)],
    )
    return pl.pallas_call(
        functools.partial(attend_kernel, first, step),
        grid_spec=grid,
        out_shape=(
            jax.ShapeDtypeStruct((128 * count, 512), BF16),
            jax.ShapeDtypeStruct((count, 4, 1, 256), F32),
            jax.ShapeDtypeStruct((128 * count, 2048), BF16),
        ),
        compiler_params=pltpu.CompilerParams(vmem_limit_bytes=VMEM_LIMIT),
        cost_estimate=pl.CostEstimate(
            flops=count * 4 * KEYS * 256 * 256 * 2,
            bytes_accessed=3 * 1024 * 1024,
            transcendentals=count * 4 * KEYS * 256,
        ),
    )(place, queries, kk, kvt, qseg, kseg, attention_weights)


def attend_back_kernel(first, step, last, *refs):
    place_ref, q_ref, dh_ref, w_ref, lse_ref, kk_ref, vv_ref, kvt_ref, qseg_ref, kseg_ref, cos_ref, sin_ref = refs[:12]
    if first == 0:
        dk_in, dv_in, refs = None, None, refs[12:]
    else:
        dk_in, dv_in, refs = refs[12], refs[13], refs[14:]
    dq_ref, one_out, two_out, bias, do_held, dk, dv = refs
    number, pair = pl.program_id(0), pl.program_id(1)
    place = place_ref[0]
    at = pl.multiple_of(lax.rem(place + first + step * number, 4) * 128, 128)

    @pl.when((number == 0) & (pair == 0))
    def _():
        dk[...] = jnp.zeros_like(dk) if dk_in is None else dk_in[...]
        dv[...] = jnp.zeros_like(dv) if dv_in is None else dv_in[...]

    @pl.when(pair == 0)
    def _():
        bias[...] = mask_of(at, qseg_ref, kseg_ref)
        do_rows = dot_nn(dh_ref[...], w_ref[...]).astype(BF16)
        for k in range(4):
            do_held[k] = do_rows[:, 128 * k : 128 * k + 128]

    keys = pl.ds(at, KEYS)
    query, grad = both_heads(q_ref[...]), both_heads(do_held[pair])
    scores = dot_nt(kk_ref[keys, :], query) + bias[...]
    weights = jnp.exp(scores - lse_ref[0, 0])
    grad_weights = dot_nt(vv_ref[keys, :], grad)
    dv[keys, :] += dot_nn(weights.astype(BF16), grad)
    inner = jnp.sum(weights * grad_weights, 0, keepdims=True)
    grad_scores = (weights * (grad_weights - inner)).astype(BF16)
    dk[keys, :] += dot_nn(grad_scores, query)
    grad_query = side_by_side(dot_nn(kvt_ref[0:64, keys], grad_scores)) * HEAD_SIZE**-0.5
    dq_ref[...] = turn(grad_query, cos_ref[...], -sin_ref[...]).astype(BF16)

    @pl.when((number == pl.num_programs(0) - 1) & (pair == 3))
    def _():
        if not last:
            one_out[...], two_out[...] = dk[...], dv[...]
            return
        half = lane_is_low((128, 128), 128)
        for block in range(3):
            for group in range(4):
                to = pl.multiple_of(lax.rem(group - place + 4, 4) * 128, 128)
                frm = slice(block * 512 + group * 128, block * 512 + group * 128 + 128)
                key, value = dk[frm, :], dv[frm, :]
                key = key + pltpu.roll(key, 64, 1)
                value = value + pltpu.roll(value, 64, 1)
                both = jnp.where(half, key, value)
                if block == 2:
                    one_out[pl.ds(to, 128), :] = both
                else:
                    two_out[block, pl.ds(to, 128), :] = both.astype(BF16)


def attend_back(first, step, count, place, queries, dh, attention_weights, lse, kk, vv, kvt, qseg, kseg, cosine, sine, held):
    last = first == 2
    whole = lambda g, p, s: (0, 0)
    specs = [
        pl.BlockSpec((128, 128), lambda g, p, s: (first + step * g, p)),
        pl.BlockSpec((128, 2048), lambda g, p, s: (g, 0)),
        pl.BlockSpec((2048, 512), whole),
        pl.BlockSpec((1, 1, 1, 256), lambda g, p, s: (g, p, 0, 0)),
        pl.BlockSpec((1536, 128), whole),
        pl.BlockSpec((1536, 128), whole),
        pl.BlockSpec((128, 1536), whole),
        pl.BlockSpec((1, 512), whole),
        pl.BlockSpec((1536, 1), whole),
        pl.BlockSpec((128, 128), lambda g, p, s: (first + step * g, 0)),
        pl.BlockSpec((128, 128), lambda g, p, s: (first + step * g, 0)),
    ] + [pl.BlockSpec((1536, 128), whole)] * len(held)
    if last:
        out_specs = (pl.BlockSpec((512, 128), whole), pl.BlockSpec((2, 512, 128), lambda g, p, s: (0, 0, 0)))
        out_shape = (jax.ShapeDtypeStruct((512, 128), F32), jax.ShapeDtypeStruct((2, 512, 128), BF16))
    else:
        out_specs = (pl.BlockSpec((1536, 128), whole),) * 2
        out_shape = (jax.ShapeDtypeStruct((1536, 128), F32),) * 2
    grid = pltpu.PrefetchScalarGridSpec(
        num_scalar_prefetch=1,
        grid=(count, 4),
        in_specs=specs,
        out_specs=(pl.BlockSpec((128, 128), lambda g, p, s: (g, p)),) + out_specs,
        scratch_shapes=[
            pltpu.VMEM((KEYS, 256), F32),
            pltpu.VMEM((4, 128, 128), BF16),
            pltpu.VMEM((1536, 128), F32),
            pltpu.VMEM((1536, 128), F32),
        ],
    )
    return pl.pallas_call(
        functools.partial(attend_back_kernel, first, step, last),
        grid_spec=grid,
        out_shape=(jax.ShapeDtypeStruct((128 * count, 512), BF16),) + out_shape,
        compiler_params=pltpu.CompilerParams(vmem_limit_bytes=VMEM_LIMIT),
        cost_estimate=pl.CostEstimate(
            flops=count * 4 * KEYS * 256 * 640 * 2,
            bytes_accessed=6 * 1024 * 1024,
            transcendentals=count * 4 * KEYS * 256,
        ),
    )(place, queries, dh, attention_weights, lse, kk, vv, kvt, qseg, kseg, cosine, sine, *held)


HIDDEN = 1408
GROUPS = [(0, 128), (128, 256), (384, 512), (896, 512)]


def columns_times_kernel(left_ref, right_ref, out_ref):
    out_ref[...] = dot_nn(left_ref[...], right_ref[...])


def columns_times(left, right, part):
    rows, width = left.shape
    return pl.pallas_call(
        columns_times_kernel,
        out_shape=jax.ShapeDtypeStruct((rows, HIDDEN), F32),
        grid=(1,),
        in_specs=[
            pl.BlockSpec((rows, width), lambda i: (0, 0)),
            pl.BlockSpec((width, HIDDEN), lambda i: (0, part)),
        ],
        out_specs=pl.BlockSpec((rows, HIDDEN), lambda i: (0, 0)),
        compiler_params=pltpu.CompilerParams(vmem_limit_bytes=VMEM_LIMIT),
        cost_estimate=pl.CostEstimate(
            flops=2 * rows * width * HIDDEN, bytes_accessed=11 * 1024 * 1024, transcendentals=0
        ),
    )(left, right)


PIECES = [(0, 128), (128, 128), (256, 64), (320, 64), (384, 128)]


def ffn_kernel(*refs):
    x_refs, dact_ref, w_ref, gua_ref, whole_ref, dx_refs = refs[:5], refs[5], refs[6], refs[7], refs[8], refs[9:14]
    x_held, dact_held, w_held, gua, dx, sems, out_sems = refs[14:]
    x_copies = []
    for number, (start, size) in enumerate(PIECES):
        copy = pltpu.make_async_copy(
            x_refs[number], x_held.at[pl.ds(start, size)], sems.at[12 + number]
        )
        copy.start()
        x_copies.append(copy)
    copies = []
    for number, (start, width) in enumerate(GROUPS):
        for part in range(3):
            if part < 2:
                columns = pl.ds(part * HIDDEN + start, width)
                copy = pltpu.make_async_copy(
                    w_ref.at[:, columns], w_held.at[:, columns], sems.at[3 * number + part]
                )
            else:
                columns = pl.ds(start, width)
                copy = pltpu.make_async_copy(
                    dact_ref.at[:, columns], dact_held.at[:, columns], sems.at[3 * number + part]
                )
            copy.start()
            copies.append(copy)
    for copy in x_copies:
        copy.wait()
    results = [pltpu.make_async_copy(x_held, whole_ref, out_sems.at[6])]
    results[0].start()
    x = x_held[...]
    for number, (start, width) in enumerate(GROUPS):
        for part in range(3):
            copies[3 * number + part].wait()
        gate = dot_nn(x, w_held[:, start : start + width])
        up = dot_nn(x, w_held[:, HIDDEN + start : HIDDEN + start + width])
        dact = dact_held[:, start : start + width]
        sig = jax.nn.sigmoid(gate)
        silu = gate * sig
        dgate = dact * up * (sig * (1.0 + gate * (1.0 - sig)))
        gua[:, start : start + width] = dgate.astype(BF16)
        gua[:, HIDDEN + start : HIDDEN + start + width] = (dact * silu).astype(BF16)
        gua[:, 2 * HIDDEN + start : 2 * HIDDEN + start + width] = (silu * up).astype(BF16)
    copy = pltpu.make_async_copy(gua, gua_ref, out_sems.at[5])
    copy.start()
    results.append(copy)
    dgu = gua[:, : 2 * HIDDEN]
    for number in range(4):
        columns = slice(512 * number, 512 * number + 512)
        dx[:, columns] = dot_nt(dgu, w_held[columns, : 2 * HIDDEN]).astype(BF16)
    for number, (start, size) in enumerate(PIECES):
        copy = pltpu.make_async_copy(dx.at[pl.ds(start, size)], dx_refs[number], out_sems.at[number])
        copy.start()
        results.append(copy)
    for copy in results:
        copy.wait()


def ffn(pieces, dact, weights):
    rows, width = dact.shape[0], weights.shape[0]
    anywhere = pl.BlockSpec(memory_space=pl.ANY)
    result = pl.pallas_call(
        ffn_kernel,
        out_shape=(
            jax.ShapeDtypeStruct((rows, 3 * HIDDEN), BF16),
            jax.ShapeDtypeStruct((rows, width), BF16),
            *(jax.ShapeDtypeStruct((size, width), BF16) for _, size in PIECES),
        ),
        in_specs=[anywhere] * 7,
        out_specs=(anywhere,) * 7,
        scratch_shapes=[
            pltpu.VMEM((rows, width), BF16),
            pltpu.VMEM((rows, HIDDEN), F32),
            pltpu.VMEM((width, 2 * HIDDEN), BF16),
            pltpu.VMEM((rows, 3 * HIDDEN), BF16),
            pltpu.VMEM((rows, width), BF16),
            pltpu.SemaphoreType.DMA((17,)),
            pltpu.SemaphoreType.DMA((7,)),
        ],
        compiler_params=pltpu.CompilerParams(vmem_limit_bytes=VMEM_LIMIT),
        cost_estimate=pl.CostEstimate(
            flops=8 * rows * width * HIDDEN,
            bytes_accessed=25 * 1024 * 1024,
            transcendentals=rows * HIDDEN,
        ),
    )(*pieces, dact, weights)
    return result[0], result[1], result[2:]


def weight_grads_kernel(core_ref, x_ref, x2_ref, dy_ref, dy2_ref, right_ref, right2_ref, out_ref):
    part = pl.program_id(0)

    @pl.when(part < 2)
    def _():
        total = dot_tn(x_ref[...], right_ref[...]) + dot_tn(x2_ref[...], right2_ref[...])
        out_ref[...] = total.astype(BF16)

    @pl.when(part == 2)
    def _():
        total = dot_tn(dy_ref[...], right_ref[...]) + dot_tn(dy2_ref[...], right2_ref[...])
        out_ref[...] = total.astype(BF16)


def weight_grads(core, x, x2, dy, dy2, right, right2):
    rows = x.shape[0]
    tile = 512
    half = x2.shape[1]
    tiles = half // tile
    own = lambda j, i, c: (0, c[0] * tiles + i)
    other = lambda j, i, c: (0, i)
    side = lambda j, i, c: (0, j)
    grid = pltpu.PrefetchScalarGridSpec(
        num_scalar_prefetch=1,
        grid=(3, tiles),
        in_specs=[
            pl.BlockSpec((rows, tile), own),
            pl.BlockSpec((rows, tile), other),
            pl.BlockSpec((rows, tile), own),
            pl.BlockSpec((rows, tile), other),
            pl.BlockSpec((rows, HIDDEN), side),
            pl.BlockSpec((rows, HIDDEN), side),
        ],
        out_specs=pl.BlockSpec((tile, HIDDEN), lambda j, i, c: (i, j)),
    )
    return pl.pallas_call(
        weight_grads_kernel,
        grid_spec=grid,
        out_shape=jax.ShapeDtypeStruct((half, 3 * HIDDEN), BF16),
        compiler_params=pltpu.CompilerParams(vmem_limit_bytes=VMEM_LIMIT),
        cost_estimate=pl.CostEstimate(
            flops=2 * 3 * 2 * rows * half * HIDDEN, bytes_accessed=24 * 1024 * 1024, transcendentals=0
        ),
    )(core, x, x2, dy, dy2, right, right2)


def rows_times_kernel(left_ref, right_ref, *out_refs):
    result = dot_nt(left_ref[...], right_ref[...]).astype(BF16)
    for number, ref in enumerate(out_refs):
        ref[...] = result[128 * number : 128 * number + 128]


def rows_times(left, right, part):
    rows, depth = left.shape[0], HIDDEN
    width = right.shape[0]
    tile = 512
    return pl.pallas_call(
        rows_times_kernel,
        out_shape=(jax.ShapeDtypeStruct((128, width), BF16),) * 4,
        grid=(width // tile,),
        in_specs=[
            pl.BlockSpec((rows, depth), lambda i: (0, part)),
            pl.BlockSpec((tile, depth), lambda i: (i, part)),
        ],
        out_specs=(pl.BlockSpec((128, tile), lambda i: (0, i)),) * 4,
        compiler_params=pltpu.CompilerParams(vmem_limit_bytes=VMEM_LIMIT),
        cost_estimate=pl.CostEstimate(
            flops=2 * rows * depth * width,
            bytes_accessed=2 * (rows * depth + width * depth + rows * width),
            transcendentals=0,
        ),
    )(left, right)


def ring_rows(own, near, far):
    return jnp.concatenate([own, near[:128], far, near[128:]], 0)


def put_half(number, value, other_ref, own_ref):
    @pl.when(number < 2)
    def _():
        other_ref[...] = value

    @pl.when(number >= 2)
    def _():
        own_ref[...] = value


def tile_at(i, c):
    return lax.rem(i + 2 * (1 - c[0]), 4)


def half_specs(tile, columns):
    return (
        pl.BlockSpec((tile, columns), lambda i, c: (jnp.minimum(i, 1), 0)),
        pl.BlockSpec((tile, columns), lambda i, c: (jnp.maximum(i - 2, 0), 0)),
    )


def wide_grads_kernel(
    core_ref, x_ref, dh0, dh1, dh2, o0, o1, o2, dq0, dq1, dq2, other_ref, own_ref, o_held, dq_held
):
    number = pl.program_id(0)

    @pl.when(number == 0)
    def _():
        o_held[...] = ring_rows(o0[...], o1[...], o2[...])
        dq_held[...] = ring_rows(dq0[...], dq1[...], dq2[...])

    out = dot_tn(ring_rows(dh0[...], dh1[...], dh2[...]), o_held[...])
    query = dot_tn(x_ref[...], dq_held[...])
    put_half(number, jnp.concatenate([out, query], 1).astype(BF16), other_ref, own_ref)


def wide_grads(core, normed, dh, o, dq):
    rows, width = normed.shape
    tile = 512
    whole = lambda i, c: (0, 0)
    column = lambda i, c: (0, tile_at(i, c))
    small = [pl.BlockSpec((size, 512), whole) for size in (128, 256, 128)]
    grid = pltpu.PrefetchScalarGridSpec(
        num_scalar_prefetch=1,
        grid=(4,),
        in_specs=[pl.BlockSpec((rows, tile), column)]
        + [pl.BlockSpec((size, tile), column) for size in (128, 256, 128)]
        + small
        + small,
        out_specs=half_specs(tile, 1024),
        scratch_shapes=[pltpu.VMEM((rows, 512), BF16), pltpu.VMEM((rows, 512), BF16)],
    )
    return pl.pallas_call(
        wide_grads_kernel,
        grid_spec=grid,
        out_shape=(jax.ShapeDtypeStruct((width // 2, 1024), BF16),) * 2,
        compiler_params=pltpu.CompilerParams(vmem_limit_bytes=VMEM_LIMIT),
        cost_estimate=pl.CostEstimate(
            flops=2 * rows * width * 1024, bytes_accessed=10 * 1024 * 1024, transcendentals=0
        ),
    )(core, normed, *dh, *o, *dq)


def finish_kernel(
    core_ref,
    x_ref,
    w_ref,
    dq0_ref,
    dq1_ref,
    dq2_ref,
    own_ref,
    one_ref,
    two_ref,
    cos_ref,
    sin_ref,
    norm_ref,
    second_ref,
    other_grad_ref,
    own_grad_ref,
    dx_own,
    dx_ahead,
    dx_far,
    dx_behind,
    gain_ref,
    dqkv,
    sums,
):
    number = pl.program_id(0)

    @pl.when(number == 0)
    def _():
        dqkv[:, :512] = ring_rows(dq0_ref[...], dq1_ref[...], dq2_ref[...])
        dkv = own_ref[...] + one_ref[...].astype(F32) + two_ref[...].astype(F32)
        turned = turn(dkv, cos_ref[...], -sin_ref[...])
        dqkv[:, 512:] = jnp.where(lane_is_low(dkv.shape, 128), turned, dkv).astype(BF16)

    x = x_ref[...]
    put_half(number, dot_tn(x, dqkv[:, 512:]).astype(BF16), other_grad_ref, own_grad_ref)
    dx = dot_nt(dqkv[...], w_ref[:, 512:])
    for start, ref in ((0, dx_own), (128, dx_ahead), (256, dx_far), (384, dx_behind)):
        ref[...] = dx[start : start + 128].astype(BF16)
    columns = pl.ds(pl.multiple_of(tile_at(number, core_ref) * 512, 512), 512)
    sums[:, columns] = jnp.broadcast_to(
        jnp.sum(dx * x.astype(F32), 0, keepdims=True) / norm_ref[...], (8, 512)
    )

    @pl.when(number == 3)
    def _():
        gain_ref[:8] = gain_rows(to_blocks(sums[...])[:1])
        gain_ref[8:] = gain_rows(second_ref[:1])


def finish(core, normed, weights, dq, own, one, two, cosine, sine, gain, second):
    rows, width = normed.shape
    tile = 512
    whole = lambda i, c: (0, 0)
    column = lambda i, c: (0, tile_at(i, c))
    narrow = pl.BlockSpec((rows, 128), whole)
    grid = pltpu.PrefetchScalarGridSpec(
        num_scalar_prefetch=1,
        grid=(4,),
        in_specs=[
            pl.BlockSpec((rows, tile), column),
            pl.BlockSpec((tile, 1152), lambda i, c: (tile_at(i, c), 0)),
            pl.BlockSpec((128, 512), whole),
            pl.BlockSpec((256, 512), whole),
            pl.BlockSpec((128, 512), whole),
            narrow,
            narrow,
            narrow,
            narrow,
            narrow,
            pl.BlockSpec((1, tile), column),
            pl.BlockSpec((8, width), whole),
        ],
        out_specs=half_specs(tile, 128)
        + (pl.BlockSpec((128, tile), column),) * 4
        + (pl.BlockSpec((GAIN_ROWS, GAIN_COLUMNS), whole),),
        scratch_shapes=[pltpu.VMEM((rows, 640), BF16), pltpu.VMEM((8, width), F32)],
    )
    result = pl.pallas_call(
        finish_kernel,
        grid_spec=grid,
        out_shape=(jax.ShapeDtypeStruct((width // 2, 128), BF16),) * 2
        + (jax.ShapeDtypeStruct((128, width), BF16),) * 4
        + (jax.ShapeDtypeStruct((GAIN_ROWS, GAIN_COLUMNS), F32),),
        compiler_params=pltpu.CompilerParams(vmem_limit_bytes=VMEM_LIMIT),
        cost_estimate=pl.CostEstimate(
            flops=2 * rows * width * 768, bytes_accessed=10 * 1024 * 1024, transcendentals=0
        ),
    )(core, normed, weights, *dq, own, one, two, cosine, sine, gain, second)
    return result[0], result[1], result[2:6], result[6]


def per_device(
    tokens,
    segments,
    w_query,
    key_projection,
    value_projection,
    w_out,
    w_gate,
    w_up,
    w_down,
    norm_attn,
    norm_ffn,
    cotangent,
):
    place, core = lax.axis_index("head"), lax.axis_index("core")
    block = (lax.axis_index("y") * 4 + lax.axis_index("x")) * 2 + core
    place_array = place.astype(jnp.int32).reshape(1)
    core_array = core.astype(jnp.int32).reshape(1)
    keep = lax.optimization_barrier

    attention_weights = lax.all_gather(
        jnp.concatenate([w_out.T, w_query, key_projection, value_projection], 1),
        CORE_FIRST,
        axis=0,
        tiled=True,
    )
    ffn_weights = lax.all_gather(
        jnp.concatenate([w_gate, w_up, w_down.T], 1), CORE_FIRST, axis=0, tiled=True
    )

    x_rows, dy_rows, normed_rows, gain_one, gain_two = prepare(
        tokens[0],
        cotangent[0],
        jnp.broadcast_to(norm_attn[None], (16, 2048)),
        jnp.broadcast_to(norm_ffn[None], (16, 2048)),
    )
    gain_one, gain_two = gain_one[:1], gain_two[:1]
    normed_one = gather_head(normed_rows)
    normed_one, dy_rows_late = keep((normed_one, dy_rows))
    dy = gather_head_direct(dy_rows_late)

    row = jnp.arange(512, dtype=jnp.int32)
    positions = block * 512 + ((row // 128 + place) % 4) * 128 + row % 128
    frequency = 10000.0 ** (-jnp.arange(32, dtype=F32) * 2.0 / HEAD_SIZE)
    angles = positions.astype(F32)[:, None] * frequency[None, :]
    cosine, sine = jnp.cos(angles), jnp.sin(angles)
    cosine = jnp.concatenate([cosine] * 4, 1)
    sine = jnp.concatenate([-sine, sine, -sine, sine], 1)

    kv_own = project(project_kv_kernel, normed_one, attention_weights, cosine, sine, 1024, 128, 128)
    normed_late, kv_own = keep((normed_one, kv_own))
    kv = (from_block(kv_own, 2), from_block(kv_own, 1), kv_own)
    queries = project(project_q_kernel, normed_late, attention_weights, cosine, sine, 512, 512, 256)

    flat = segments.reshape(-1)
    padded = jnp.concatenate([jnp.full((1024,), -1, jnp.int32), flat])
    qseg = lax.dynamic_slice_in_dim(flat, block * 512, 512, 0).reshape(1, 512)
    kseg = lax.dynamic_slice_in_dim(padded, block * 512, 1536, 0).reshape(1536, 1)

    kv, dy = keep((kv, dy))
    kk, vv, kvt = set_up(place_array, kv)
    seen = place_array, queries, kk, kvt, qseg, kseg, attention_weights
    o_far, lse_far, part_far = attend(2, 1, 1, *seen)
    o_near, lse_near, part_near = attend(1, 2, 2, *seen)
    o_own, lse_own, part_own = attend(0, 1, 1, *seen)
    dy_other = swap_half(dy, core)
    attention_sum = scatter_pieces(
        part_own, part_near[:128], part_far[:64], part_far[64:], part_near[128:]
    )
    h1, normed_rows_two = join(x_rows, gain_two, attention_sum)
    dact = columns_times(dy, ffn_weights, 2)
    pieces, (dact, dy_other) = gather_pieces(normed_rows_two, (dact, dy_other))

    gua, normed_two, dnormed_two = ffn((normed_rows_two, *pieces), dact, ffn_weights)
    gua_other = shift(gua, "core", 1)
    normed_two_other = swap_half(normed_two, core)
    out_pieces = rows_times(gua, ffn_weights, 2)
    dnormed_two, (gua_other, normed_two_other, out_pieces) = scatter_pieces(
        *dnormed_two, (gua_other, normed_two_other, out_pieces)
    )
    out_pieces = scatter_direct(*out_pieces)
    held = weight_grads(core_array, normed_two, normed_two_other, dy, dy_other, gua, gua_other)
    held, dnormed_two = keep((held, dnormed_two))
    grads = lax.psum_scatter(held, ("y", "x"), scatter_dimension=0, tiled=True)

    dh1, dh1_low, grad_gain_two = join_back(h1, dy_rows, gain_two, dnormed_two)
    back = kk, vv, kvt, qseg, kseg, cosine, sine
    dq_own, dk, dv = attend_back(0, 1, 1, place_array, queries, dh1_low, attention_weights, lse_own, *back, ())
    (ahead, far_top, far_bottom, behind), (dk, dv, out_pieces) = gather_pieces(
        dh1_low, (dk, dv, out_pieces)
    )
    near = jnp.concatenate([ahead, behind], 0)
    dq_near, dk, dv = attend_back(
        1, 2, 2, place_array, queries, near, attention_weights, lse_near, *back, (dk, dv)
    )
    far_top, far_bottom, dk, dv = keep((far_top, far_bottom, dk, dv))
    far = jnp.concatenate([far_top, far_bottom], 0)
    dq_far, dkv_own, dkv_earlier = attend_back(
        2, 1, 1, place_array, queries, far, attention_weights, lse_far, *back, (dk, dv)
    )
    dq = dq_own, dq_near, dq_far
    dkv_one = from_block(dkv_earlier[1], -1)
    dkv_two = from_block(dkv_earlier[0], -2)
    wide_other, wide_own = wide_grads(
        core_array, normed_one, (dh1_low, near, far), (o_own, o_near, o_far), dq
    )
    dkv_one, dkv_two, wide_other = keep((dkv_one, dkv_two, wide_other))
    wide_other = shift(wide_other, "core", 1)

    narrow_other, narrow_own, dnormed_one, gains = finish(
        core_array,
        normed_one,
        attention_weights,
        dq,
        dkv_own,
        dkv_one,
        dkv_two,
        cosine,
        sine,
        gain_one,
        grad_gain_two,
    )
    pieces = pieces_x(
        lax.axis_index("x").astype(jnp.int32).reshape(1),
        wide_own,
        wide_other,
        narrow_own,
        shift(narrow_other, "core", 1),
        gains,
        shift(gains, "core", 1),
    )
    pieces, dnormed_one = keep((pieces, dnormed_one))
    pieces = pieces_y(lax.axis_index("y").astype(jnp.int32).reshape(1), exchange(pieces, "x"))
    columns = (512, 64), (64, 512), (64, 64), (64, 64), (GAIN_ROWS, GAIN_COLUMNS)
    grad_out, grad_query, grad_key, grad_value, gains = small_call(
        attention_grads_kernel, [(shape, F32) for shape in columns], *exchange(pieces, "y")
    )
    grad_gain_one, grad_gain_two = small_call(
        gains_kernel, [((1, 2048), F32)] * 2, *exchange([gains] * 4, "head")
    )

    dnormed_one = scatter_direct(*dnormed_one)
    rows = [(x_rows.shape, BF16)]
    (grad_inputs,) = small_call(input_grad_kernel, rows, dh1, x_rows, gain_one, *dnormed_one)
    (output,) = small_call(output_kernel, rows, h1, *out_pieces)
    return (
        output[None],
        grad_inputs[None],
        grad_query,
        grad_key,
        grad_value,
        grad_out,
        grads[:, :HIDDEN].astype(F32),
        grads[:, HIDDEN : 2 * HIDDEN].astype(F32),
        grads[:, 2 * HIDDEN :].T.astype(F32),
        grad_gain_one.reshape(2048),
        grad_gain_two.reshape(2048),
    )


def solution(mesh):
    grid = Mesh(mesh.devices.reshape(4, 4, 4, 2), ("head", "y", "x", "core"))
    rows, up, down = P(BLK, "head", None), P(BLK, "head"), P("head", BLK)
    return jax.shard_map(
        per_device,
        mesh=grid,
        in_specs=(rows, P(), up, up, up, down, up, up, down, P(), P(), rows),
        out_specs=(rows, rows, up, up, up, down, up, up, down, P(), P()),
        check_vma=False,
    )
```

```python
import functools

import jax
import jax.numpy as jnp
from jax import lax
from jax.experimental import pallas as pl
from jax.experimental.pallas import tpu as pltpu
from jax.sharding import Mesh
from jax.sharding import PartitionSpec as P

HEAD_SIZE = 64
WINDOW = 1024
EPSILON = 1e-05
BF16 = jnp.bfloat16
F32 = jnp.float32
BLK = ("y", "x", "core")
CORE_FIRST = ("core", "y", "x")
VMEM_LIMIT = 56 * 1024 * 1024


def dot_nn(a, b):
    return jnp.dot(a, b, preferred_element_type=F32)


def dot_nt(a, b):
    return lax.dot_general(a, b, (((1,), (1,)), ((), ())), preferred_element_type=F32)


def dot_tn(a, b):
    return lax.dot_general(a, b, (((0,), (0,)), ((), ())), preferred_element_type=F32)


def shift(value, axis, distance):
    size = lax.axis_size(axis)
    return lax.ppermute(value, axis, [(i, (i + distance) % size) for i in range(size)])


def add_low(a, b):
    return (a.astype(F32) + b.astype(F32)).astype(BF16)


def gather_pieces(rows):
    return shift(rows, "head", -1), shift(rows, "head", 2), shift(rows, "head", 1)


def gather_head(rows):
    return jnp.concatenate([rows, *gather_pieces(rows)], 0)


def scatter_pieces(own, ahead, far, behind):
    return own, shift(ahead, "head", 1), shift(behind, "head", -1), shift(far, "head", 2)


def swap_half(value, core):
    width = value.shape[1] // 2
    return shift(lax.dynamic_slice_in_dim(value, (1 - core) * width, width, 1), "core", 1)


def exchange(pieces, axis):
    return pieces[0], shift(pieces[1], axis, 1), shift(pieces[2], axis, 2), shift(pieces[3], axis, -1)


def from_block(value, distance):
    route = [(i, i + distance) for i in range(32) if 0 <= i + distance < 32]
    return lax.ppermute(value, BLK, route)


def scale_of(values):
    return lax.rsqrt(jnp.mean(values * values, -1, keepdims=True) + EPSILON)


def lane_is_low(shape, period):
    return lax.broadcasted_iota(jnp.int32, shape, len(shape) - 1) % period < period // 2


def turn(values, cosine, sine):
    swapped = jnp.where(
        lane_is_low(values.shape, 64), pltpu.roll(values, 96, 1), pltpu.roll(values, 32, 1)
    )
    return values * cosine + swapped * sine


def core_major_tiles(tiles):
    low = lane_is_low(tiles[0].shape, 128)
    rolled = [pltpu.roll(tile, 64, 1) for tile in tiles]
    first = [jnp.where(low, tiles[2 * k], rolled[2 * k + 1]) for k in range(8)]
    second = [jnp.where(low, rolled[2 * k], tiles[2 * k + 1]) for k in range(8)]
    return first + second


def block_major_tiles(tiles):
    low = lane_is_low(tiles[0].shape, 128)
    rolled = [pltpu.roll(tile, 64, 1) for tile in tiles]
    result = []
    for k in range(8):
        result.append(jnp.where(low, tiles[k], rolled[8 + k]))
        result.append(jnp.where(low, rolled[k], tiles[8 + k]))
    return result


def in_tiles(value):
    return [value[:, 128 * k : 128 * k + 128] for k in range(16)]


def prepare_kernel(x_ref, dy_ref, gain_one_ref, gain_two_ref, x_out, dy_out, normed_out, one_out, two_out):
    def convert(ref):
        return jnp.concatenate(core_major_tiles(in_tiles(ref[...].astype(F32))), 1)

    x, gain = convert(x_ref), convert(gain_one_ref)
    one_out[...], two_out[...] = gain, convert(gain_two_ref)
    x_out[...] = x
    dy_out[...] = convert(dy_ref).astype(BF16)
    normed_out[...] = (x * scale_of(x) * gain[:1]).astype(BF16)


def prepare(x, dy, gain_one, gain_two):
    rows, width = x.shape
    return pl.pallas_call(
        prepare_kernel,
        out_shape=(
            jax.ShapeDtypeStruct((rows, width), F32),
            jax.ShapeDtypeStruct((rows, width), BF16),
            jax.ShapeDtypeStruct((rows, width), BF16),
            jax.ShapeDtypeStruct((16, width), F32),
            jax.ShapeDtypeStruct((16, width), F32),
        ),
        compiler_params=pltpu.CompilerParams(vmem_limit_bytes=VMEM_LIMIT),
        cost_estimate=pl.CostEstimate(
            flops=10 * rows * width, bytes_accessed=10 * rows * width, transcendentals=rows
        ),
    )(x, dy, gain_one, gain_two)


def to_blocks(value):
    return jnp.concatenate(block_major_tiles(in_tiles(value)), 1)


def small_call(kernel, out_shape, *operands):
    return pl.pallas_call(
        kernel,
        out_shape=tuple(jax.ShapeDtypeStruct(shape, dtype) for shape, dtype in out_shape),
        compiler_params=pltpu.CompilerParams(vmem_limit_bytes=VMEM_LIMIT),
        cost_estimate=pl.CostEstimate(
            flops=sum(x.size for x in operands),
            bytes_accessed=2 * sum(x.size * x.dtype.itemsize for x in operands),
            transcendentals=0,
        ),
    )(*operands)


def total_of(refs):
    values = [ref[...].astype(F32) for ref in refs]
    while len(values) > 1:
        values = [values[0] + values[1]] + values[2:]
    return values[0]


def join_kernel(x_ref, gain_ref, a_ref, b_ref, c_ref, d_ref, h_out, normed_out):
    h = x_ref[...] + total_of((a_ref, b_ref, c_ref, d_ref))
    h_out[...] = h
    normed_out[...] = (h * scale_of(h) * gain_ref[...]).astype(BF16)


def join(x, gain, pieces):
    return small_call(join_kernel, ((x.shape, F32), (x.shape, BF16)), x, gain, *pieces)


def norm_backward(values, gain, grad):
    scale = scale_of(values)
    weighted = grad * gain
    inner = jnp.mean(weighted * values, -1, keepdims=True)
    return scale * weighted - values * (scale * scale * scale * inner), scale


def join_back_kernel(h_ref, dy_ref, gain_ref, a_ref, b_ref, c_ref, d_ref, dh_out, low_out, grad_out):
    h, grad = h_ref[...], total_of((a_ref, b_ref, c_ref, d_ref))
    back, scale = norm_backward(h, gain_ref[...], grad)
    dh = dy_ref[...].astype(F32) + back
    dh_out[...] = dh
    low_out[...] = dh.astype(BF16)
    grad_out[...] = to_blocks(jnp.broadcast_to(jnp.sum(grad * h * scale, 0, keepdims=True), (8, h.shape[1])))


def join_back(h, dy, gain, pieces):
    shapes = (h.shape, F32), (h.shape, BF16), ((8, h.shape[1]), F32)
    return small_call(join_back_kernel, shapes, h, dy, gain, *pieces)


def output_kernel(h_ref, a_ref, b_ref, c_ref, d_ref, out_ref):
    out_ref[...] = to_blocks(h_ref[...] + total_of((a_ref, b_ref, c_ref, d_ref))).astype(BF16)


def input_grad_kernel(dh_ref, x_ref, gain_ref, a_ref, b_ref, c_ref, d_ref, out_ref):
    back, _ = norm_backward(x_ref[...], gain_ref[...], total_of((a_ref, b_ref, c_ref, d_ref)))
    out_ref[...] = to_blocks(dh_ref[...] + back).astype(BF16)


GAIN_ROWS, GAIN_COLUMNS = 16, 256


def gain_rows(vector):
    return jnp.concatenate([vector[:, 256 * k : 256 * k + 256] for k in range(8)], 0)


def put_piece(ref, rows, gains):
    count = rows.shape[0]
    ref[:count] = rows
    ref[count:, GAIN_COLUMNS:] = jnp.zeros((GAIN_ROWS, ref.shape[1] - GAIN_COLUMNS), BF16)
    ref[count:, :GAIN_COLUMNS] = gains.astype(BF16)


def pieces_x_kernel(at_ref, wide_ref, wide2_ref, narrow_ref, narrow2_ref, gain_ref, gain2_ref, *out_refs):
    wide = add_low(wide_ref[...], wide2_ref[...]).reshape(256, wide_ref.shape[3])
    narrow = add_low(narrow_ref[...], narrow2_ref[...]).reshape(256, narrow_ref.shape[3])
    rows = jnp.concatenate([wide, narrow], 1)
    gains = gain_ref[...] + gain2_ref[...]
    for number, ref in enumerate(out_refs):

        @pl.when(pl.program_id(0) == number)
        def _():
            put_piece(ref, rows, gains)


def pieces_x(at, wide, wide2, narrow, narrow2, gains, gains2):
    columns = wide.shape[1] + narrow.shape[1]
    pick = lambda d, s: (0, lax.rem(s[0] + d, 4), 0, 0)
    spec = lambda value: pl.BlockSpec((4, 1, 64, value.shape[1]), pick)
    whole = lambda d, s: (0, 0)
    shaped = lambda value: value.reshape(4, 4, 64, value.shape[1])
    grid = pltpu.PrefetchScalarGridSpec(
        num_scalar_prefetch=1,
        grid=(4,),
        in_specs=[spec(wide), spec(wide), spec(narrow), spec(narrow)]
        + [pl.BlockSpec((GAIN_ROWS, GAIN_COLUMNS), whole)] * 2,
        out_specs=(pl.BlockSpec((256 + GAIN_ROWS, columns), whole),) * 4,
    )
    return pl.pallas_call(
        pieces_x_kernel,
        grid_spec=grid,
        out_shape=(jax.ShapeDtypeStruct((256 + GAIN_ROWS, columns), BF16),) * 4,
        compiler_params=pltpu.CompilerParams(vmem_limit_bytes=VMEM_LIMIT),
        cost_estimate=pl.CostEstimate(
            flops=2 * 1024 * columns, bytes_accessed=6 * 1024 * columns, transcendentals=0
        ),
    )(at, shaped(wide), shaped(wide2), shaped(narrow), shaped(narrow2), gains, gains2)


def pieces_y_kernel(at_ref, a_ref, b_ref, c_ref, d_ref, *refs):
    held = refs[4]
    held[...] = total_of((a_ref, b_ref, c_ref, d_ref))
    for number, ref in enumerate(refs[:4]):
        start = pl.multiple_of(lax.rem(at_ref[0] + number, 4) * 64, 64)
        put_piece(ref, held[pl.ds(start, 64), :].astype(BF16), held[256:, :GAIN_COLUMNS])


def pieces_y(at, pieces):
    columns = pieces[0].shape[1]
    vmem = pl.BlockSpec(memory_space=pltpu.VMEM)
    return pl.pallas_call(
        pieces_y_kernel,
        out_shape=(jax.ShapeDtypeStruct((64 + GAIN_ROWS, columns), BF16),) * 4,
        in_specs=[pl.BlockSpec(memory_space=pltpu.SMEM)] + [vmem] * 4,
        out_specs=(vmem,) * 4,
        scratch_shapes=[pltpu.VMEM((256 + GAIN_ROWS, columns), F32)],
        compiler_params=pltpu.CompilerParams(vmem_limit_bytes=VMEM_LIMIT),
        cost_estimate=pl.CostEstimate(
            flops=4 * 272 * columns, bytes_accessed=10 * 272 * columns, transcendentals=0
        ),
    )(at, *pieces)


def attention_grads_kernel(a_ref, b_ref, c_ref, d_ref, out_ref, q_ref, k_ref, v_ref, gain_ref):
    total = total_of((a_ref, b_ref, c_ref, d_ref))
    out_ref[...] = total[:64, :512].T
    q_ref[...] = total[:64, 512:1024]
    k_ref[...] = total[:64, 1024:1088]
    v_ref[...] = total[:64, 1088:]
    gain_ref[...] = total[64:, :GAIN_COLUMNS]


def gains_kernel(a_ref, b_ref, c_ref, d_ref, one_ref, two_ref):
    total = total_of((a_ref, b_ref, c_ref, d_ref))
    one_ref[...] = jnp.concatenate([total[k : k + 1] for k in range(8)], 1)
    two_ref[...] = jnp.concatenate([total[k : k + 1] for k in range(8, 16)], 1)


def project_kv_kernel(x_ref, w_ref, cos_ref, sin_ref, kv_ref):
    flat = dot_nn(x_ref[...], w_ref[...])
    turned = turn(flat, cos_ref[...], sin_ref[...])
    kv_ref[...] = jnp.where(lane_is_low(flat.shape, 128), turned, flat).astype(BF16)


def project_q_kernel(x_ref, w_ref, cos_ref, sin_ref, q_ref):
    cosine, sine = cos_ref[...], sin_ref[...]
    wide = dot_nn(x_ref[...], w_ref[...])
    for part in (0, 128):
        turned = turn(wide[:, part : part + 128], cosine, sine)
        q_ref[:, part : part + 128] = (turned * HEAD_SIZE**-0.5).astype(BF16)


def project(kernel, normed, weights, cosine, sine, start, columns, tile):
    rows, width = normed.shape
    whole = lambda i: (0, 0)
    return pl.pallas_call(
        kernel,
        out_shape=jax.ShapeDtypeStruct((rows, columns), BF16),
        grid=(columns // tile,),
        in_specs=[
            pl.BlockSpec((rows, width), whole),
            pl.BlockSpec((width, tile), lambda i: (0, start // tile + i)),
            pl.BlockSpec((rows, 128), whole),
            pl.BlockSpec((rows, 128), whole),
        ],
        out_specs=pl.BlockSpec((rows, tile), lambda i: (0, i)),
        compiler_params=pltpu.CompilerParams(vmem_limit_bytes=VMEM_LIMIT),
        cost_estimate=pl.CostEstimate(
            flops=2 * rows * width * columns,
            bytes_accessed=2 * (rows * width + width * columns + rows * columns),
            transcendentals=0,
        ),
    )(normed, weights, cosine, sine)


KEYS = 1152


def set_up_kernel(place_ref, kv0_ref, kv1_ref, kv2_ref, kk_ref, vv_ref, kvt_ref):
    place = place_ref[0]
    low = lane_is_low((128, 128), 128)
    for block, ref in enumerate((kv0_ref, kv1_ref, kv2_ref)):
        for group in range(4):
            at = pl.multiple_of(lax.rem(group - place + 4, 4) * 128, 128)
            piece = ref[pl.ds(at, 128), :].astype(F32)
            rolled = pltpu.roll(piece, 64, 1)
            to = block * 512 + group * 128
            kk_ref[to : to + 128, :] = jnp.where(low, piece, rolled).astype(BF16)
            vv_ref[to : to + 128, :] = jnp.where(low, rolled, piece).astype(BF16)
            kvt_ref[:, to : to + 128] = piece.T.astype(BF16)


def set_up(place, kv):
    vmem = pl.BlockSpec(memory_space=pltpu.VMEM)
    return pl.pallas_call(
        set_up_kernel,
        out_shape=(
            jax.ShapeDtypeStruct((1536, 128), BF16),
            jax.ShapeDtypeStruct((1536, 128), BF16),
            jax.ShapeDtypeStruct((128, 1536), BF16),
        ),
        in_specs=[pl.BlockSpec(memory_space=pltpu.SMEM), vmem, vmem, vmem],
        out_specs=(vmem, vmem, vmem),
        compiler_params=pltpu.CompilerParams(vmem_limit_bytes=VMEM_LIMIT),
        cost_estimate=pl.CostEstimate(flops=1536 * 128 * 8, bytes_accessed=2 * 1024 * 1024, transcendentals=0),
    )(place, *kv)


def both_heads(pair):
    low = lane_is_low(pair.shape, 128)
    nothing = jnp.zeros_like(pair)
    return jnp.concatenate([jnp.where(low, pair, nothing), jnp.where(low, nothing, pair)], 0)


def side_by_side(transposed):
    return jnp.concatenate([transposed[:, :128], transposed[:, 128:]], 0).T


def mask_of(at, qseg_ref, kseg_ref):
    key = lax.broadcasted_iota(jnp.int32, (KEYS, 128), 0)
    query = lax.broadcasted_iota(jnp.int32, (KEYS, 128), 1)
    distance = query - key + WINDOW
    same = kseg_ref[pl.ds(at, KEYS), :] == qseg_ref[:, pl.ds(at, 128)]
    seen = (distance >= 0) & (distance < WINDOW) & same
    bias = jnp.where(seen, 0.0, -jnp.inf)
    return jnp.concatenate([bias, bias], 1)


def attend_kernel(
    first, step, place_ref, q_ref, kk_ref, kvt_ref, qseg_ref, kseg_ref, w_ref, o_ref, lse_ref, part_ref, bias, held
):
    pair = pl.program_id(1)
    group = lax.rem(place_ref[0] + first + step * pl.program_id(0), 4)
    at = pl.multiple_of(group * 128, 128)

    @pl.when(pair == 0)
    def _():
        bias[...] = mask_of(at, qseg_ref, kseg_ref)

    scores = dot_nt(kk_ref[pl.ds(at, KEYS), :], both_heads(q_ref[...])) + bias[...]
    top = jnp.max(scores, 0, keepdims=True)
    weights = jnp.exp(scores - top)
    total = jnp.sum(weights, 0, keepdims=True)
    result = dot_nn(kvt_ref[64:128, pl.ds(at, KEYS)], weights.astype(BF16)) / total
    lse_ref[0, 0] = top + jnp.log(total)
    result = side_by_side(result).astype(BF16)
    o_ref[...] = result
    held[pair] = result

    @pl.when(pair == 3)
    def _():
        rows = jnp.concatenate([held[k] for k in range(4)], 1)
        part_ref[...] = dot_nt(rows, w_ref[...]).astype(BF16)


def attend(first, step, count, place, queries, kk, kvt, qseg, kseg, attention_weights):
    whole = lambda g, p, s: (0, 0)
    grid = pltpu.PrefetchScalarGridSpec(
        num_scalar_prefetch=1,
        grid=(count, 4),
        in_specs=[
            pl.BlockSpec((128, 128), lambda g, p, s: (first + step * g, p)),
            pl.BlockSpec((1536, 128), whole),
            pl.BlockSpec((128, 1536), whole),
            pl.BlockSpec((1, 512), whole),
            pl.BlockSpec((1536, 1), whole),
            pl.BlockSpec((2048, 512), whole),
        ],
        out_specs=(
            pl.BlockSpec((128, 128), lambda g, p, s: (g, p)),
            pl.BlockSpec((1, 1, 1, 256), lambda g, p, s: (g, p, 0, 0)),
            pl.BlockSpec((128, 2048), lambda g, p, s: (g, 0)),
        ),
        scratch_shapes=[pltpu.VMEM((KEYS, 256), F32), pltpu.VMEM((4, 128, 128), BF16)],
    )
    return pl.pallas_call(
        functools.partial(attend_kernel, first, step),
        grid_spec=grid,
        out_shape=(
            jax.ShapeDtypeStruct((128 * count, 512), BF16),
            jax.ShapeDtypeStruct((count, 4, 1, 256), F32),
            jax.ShapeDtypeStruct((128 * count, 2048), BF16),
        ),
        compiler_params=pltpu.CompilerParams(vmem_limit_bytes=VMEM_LIMIT),
        cost_estimate=pl.CostEstimate(
            flops=count * 4 * KEYS * 256 * 256 * 2,
            bytes_accessed=3 * 1024 * 1024,
            transcendentals=count * 4 * KEYS * 256,
        ),
    )(place, queries, kk, kvt, qseg, kseg, attention_weights)


def attend_back_kernel(first, step, last, *refs):
    place_ref, q_ref, dh_ref, w_ref, lse_ref, kk_ref, vv_ref, kvt_ref, qseg_ref, kseg_ref, cos_ref, sin_ref = refs[:12]
    if first == 0:
        dk_in, dv_in, refs = None, None, refs[12:]
    else:
        dk_in, dv_in, refs = refs[12], refs[13], refs[14:]
    dq_ref, one_out, two_out, bias, do_held, dk, dv = refs
    number, pair = pl.program_id(0), pl.program_id(1)
    place = place_ref[0]
    at = pl.multiple_of(lax.rem(place + first + step * number, 4) * 128, 128)

    @pl.when((number == 0) & (pair == 0))
    def _():
        dk[...] = jnp.zeros_like(dk) if dk_in is None else dk_in[...]
        dv[...] = jnp.zeros_like(dv) if dv_in is None else dv_in[...]

    @pl.when(pair == 0)
    def _():
        bias[...] = mask_of(at, qseg_ref, kseg_ref)
        do_rows = dot_nn(dh_ref[...], w_ref[...]).astype(BF16)
        for k in range(4):
            do_held[k] = do_rows[:, 128 * k : 128 * k + 128]

    keys = pl.ds(at, KEYS)
    query, grad = both_heads(q_ref[...]), both_heads(do_held[pair])
    scores = dot_nt(kk_ref[keys, :], query) + bias[...]
    weights = jnp.exp(scores - lse_ref[0, 0])
    grad_weights = dot_nt(vv_ref[keys, :], grad)
    dv[keys, :] += dot_nn(weights.astype(BF16), grad)
    inner = jnp.sum(weights * grad_weights, 0, keepdims=True)
    grad_scores = (weights * (grad_weights - inner)).astype(BF16)
    dk[keys, :] += dot_nn(grad_scores, query)
    grad_query = side_by_side(dot_nn(kvt_ref[0:64, keys], grad_scores)) * HEAD_SIZE**-0.5
    dq_ref[...] = turn(grad_query, cos_ref[...], -sin_ref[...]).astype(BF16)

    @pl.when((number == pl.num_programs(0) - 1) & (pair == 3))
    def _():
        if not last:
            one_out[...], two_out[...] = dk[...], dv[...]
            return
        half = lane_is_low((128, 128), 128)
        for block in range(3):
            for group in range(4):
                to = pl.multiple_of(lax.rem(group - place + 4, 4) * 128, 128)
                frm = slice(block * 512 + group * 128, block * 512 + group * 128 + 128)
                key, value = dk[frm, :], dv[frm, :]
                key = key + pltpu.roll(key, 64, 1)
                value = value + pltpu.roll(value, 64, 1)
                both = jnp.where(half, key, value)
                if block == 2:
                    one_out[pl.ds(to, 128), :] = both
                else:
                    two_out[block, pl.ds(to, 128), :] = both.astype(BF16)


def attend_back(first, step, count, place, queries, dh, attention_weights, lse, kk, vv, kvt, qseg, kseg, cosine, sine, held):
    last = first == 2
    whole = lambda g, p, s: (0, 0)
    specs = [
        pl.BlockSpec((128, 128), lambda g, p, s: (first + step * g, p)),
        pl.BlockSpec((128, 2048), lambda g, p, s: (g, 0)),
        pl.BlockSpec((2048, 512), whole),
        pl.BlockSpec((1, 1, 1, 256), lambda g, p, s: (g, p, 0, 0)),
        pl.BlockSpec((1536, 128), whole),
        pl.BlockSpec((1536, 128), whole),
        pl.BlockSpec((128, 1536), whole),
        pl.BlockSpec((1, 512), whole),
        pl.BlockSpec((1536, 1), whole),
        pl.BlockSpec((128, 128), lambda g, p, s: (first + step * g, 0)),
        pl.BlockSpec((128, 128), lambda g, p, s: (first + step * g, 0)),
    ] + [pl.BlockSpec((1536, 128), whole)] * len(held)
    if last:
        out_specs = (pl.BlockSpec((512, 128), whole), pl.BlockSpec((2, 512, 128), lambda g, p, s: (0, 0, 0)))
        out_shape = (jax.ShapeDtypeStruct((512, 128), F32), jax.ShapeDtypeStruct((2, 512, 128), BF16))
    else:
        out_specs = (pl.BlockSpec((1536, 128), whole),) * 2
        out_shape = (jax.ShapeDtypeStruct((1536, 128), F32),) * 2
    grid = pltpu.PrefetchScalarGridSpec(
        num_scalar_prefetch=1,
        grid=(count, 4),
        in_specs=specs,
        out_specs=(pl.BlockSpec((128, 128), lambda g, p, s: (g, p)),) + out_specs,
        scratch_shapes=[
            pltpu.VMEM((KEYS, 256), F32),
            pltpu.VMEM((4, 128, 128), BF16),
            pltpu.VMEM((1536, 128), F32),
            pltpu.VMEM((1536, 128), F32),
        ],
    )
    return pl.pallas_call(
        functools.partial(attend_back_kernel, first, step, last),
        grid_spec=grid,
        out_shape=(jax.ShapeDtypeStruct((128 * count, 512), BF16),) + out_shape,
        compiler_params=pltpu.CompilerParams(vmem_limit_bytes=VMEM_LIMIT),
        cost_estimate=pl.CostEstimate(
            flops=count * 4 * KEYS * 256 * 640 * 2,
            bytes_accessed=6 * 1024 * 1024,
            transcendentals=count * 4 * KEYS * 256,
        ),
    )(place, queries, dh, attention_weights, lse, kk, vv, kvt, qseg, kseg, cosine, sine, *held)


HIDDEN = 1408
GROUPS = [(0, 128), (128, 256), (384, 512), (896, 512)]


def columns_times_kernel(left_ref, right_ref, out_ref):
    out_ref[...] = dot_nn(left_ref[...], right_ref[...])


def columns_times(left, right, part):
    rows, width = left.shape
    return pl.pallas_call(
        columns_times_kernel,
        out_shape=jax.ShapeDtypeStruct((rows, HIDDEN), F32),
        grid=(1,),
        in_specs=[
            pl.BlockSpec((rows, width), lambda i: (0, 0)),
            pl.BlockSpec((width, HIDDEN), lambda i: (0, part)),
        ],
        out_specs=pl.BlockSpec((rows, HIDDEN), lambda i: (0, 0)),
        compiler_params=pltpu.CompilerParams(vmem_limit_bytes=VMEM_LIMIT),
        cost_estimate=pl.CostEstimate(
            flops=2 * rows * width * HIDDEN, bytes_accessed=11 * 1024 * 1024, transcendentals=0
        ),
    )(left, right)


PIECES = [(0, 128), (128, 128), (256, 128), (384, 128)]


def ffn_kernel(*refs):
    x_refs, dact_ref, w_ref, gua_ref, whole_ref, dx_refs = refs[:4], refs[4], refs[5], refs[6], refs[7], refs[8:12]
    x_held, dact_held, w_held, gua, dx, sems, out_sems = refs[12:]
    x_copies = []
    for number, (start, size) in enumerate(PIECES):
        copy = pltpu.make_async_copy(
            x_refs[number], x_held.at[pl.ds(start, size)], sems.at[12 + number]
        )
        copy.start()
        x_copies.append(copy)
    copies = []
    for number, (start, width) in enumerate(GROUPS):
        for part in range(3):
            if part < 2:
                columns = pl.ds(part * HIDDEN + start, width)
                copy = pltpu.make_async_copy(
                    w_ref.at[:, columns], w_held.at[:, columns], sems.at[3 * number + part]
                )
            else:
                columns = pl.ds(start, width)
                copy = pltpu.make_async_copy(
                    dact_ref.at[:, columns], dact_held.at[:, columns], sems.at[3 * number + part]
                )
            copy.start()
            copies.append(copy)
    for copy in x_copies:
        copy.wait()
    results = [pltpu.make_async_copy(x_held, whole_ref, out_sems.at[5])]
    results[0].start()
    x = x_held[...]
    for number, (start, width) in enumerate(GROUPS):
        for part in range(3):
            copies[3 * number + part].wait()
        gate = dot_nn(x, w_held[:, start : start + width])
        up = dot_nn(x, w_held[:, HIDDEN + start : HIDDEN + start + width])
        dact = dact_held[:, start : start + width]
        sig = jax.nn.sigmoid(gate)
        silu = gate * sig
        dgate = dact * up * (sig * (1.0 + gate * (1.0 - sig)))
        gua[:, start : start + width] = dgate.astype(BF16)
        gua[:, HIDDEN + start : HIDDEN + start + width] = (dact * silu).astype(BF16)
        gua[:, 2 * HIDDEN + start : 2 * HIDDEN + start + width] = (silu * up).astype(BF16)
    copy = pltpu.make_async_copy(gua, gua_ref, out_sems.at[4])
    copy.start()
    results.append(copy)
    dgu = gua[:, : 2 * HIDDEN]
    for number in range(4):
        columns = slice(512 * number, 512 * number + 512)
        dx[:, columns] = dot_nt(dgu, w_held[columns, : 2 * HIDDEN]).astype(BF16)
    for number, (start, size) in enumerate(PIECES):
        copy = pltpu.make_async_copy(dx.at[pl.ds(start, size)], dx_refs[number], out_sems.at[number])
        copy.start()
        results.append(copy)
    for copy in results:
        copy.wait()


def ffn(pieces, dact, weights):
    rows, width = dact.shape[0], weights.shape[0]
    anywhere = pl.BlockSpec(memory_space=pl.ANY)
    result = pl.pallas_call(
        ffn_kernel,
        out_shape=(
            jax.ShapeDtypeStruct((rows, 3 * HIDDEN), BF16),
            jax.ShapeDtypeStruct((rows, width), BF16),
            *(jax.ShapeDtypeStruct((size, width), BF16) for _, size in PIECES),
        ),
        in_specs=[anywhere] * 6,
        out_specs=(anywhere,) * 6,
        scratch_shapes=[
            pltpu.VMEM((rows, width), BF16),
            pltpu.VMEM((rows, HIDDEN), F32),
            pltpu.VMEM((width, 2 * HIDDEN), BF16),
            pltpu.VMEM((rows, 3 * HIDDEN), BF16),
            pltpu.VMEM((rows, width), BF16),
            pltpu.SemaphoreType.DMA((16,)),
            pltpu.SemaphoreType.DMA((6,)),
        ],
        compiler_params=pltpu.CompilerParams(vmem_limit_bytes=VMEM_LIMIT),
        cost_estimate=pl.CostEstimate(
            flops=8 * rows * width * HIDDEN,
            bytes_accessed=25 * 1024 * 1024,
            transcendentals=rows * HIDDEN,
        ),
    )(*pieces, dact, weights)
    return result[0], result[1], result[2:]


def weight_grads_kernel(core_ref, x_ref, x2_ref, dy_ref, dy2_ref, right_ref, right2_ref, out_ref):
    part = pl.program_id(0)

    @pl.when(part < 2)
    def _():
        total = dot_tn(x_ref[...], right_ref[...]) + dot_tn(x2_ref[...], right2_ref[...])
        out_ref[...] = total.astype(BF16)

    @pl.when(part == 2)
    def _():
        total = dot_tn(dy_ref[...], right_ref[...]) + dot_tn(dy2_ref[...], right2_ref[...])
        out_ref[...] = total.astype(BF16)


def weight_grads(core, x, x2, dy, dy2, right, right2):
    rows = x.shape[0]
    tile = 512
    half = x2.shape[1]
    tiles = half // tile
    own = lambda j, i, c: (0, c[0] * tiles + i)
    other = lambda j, i, c: (0, i)
    side = lambda j, i, c: (0, j)
    grid = pltpu.PrefetchScalarGridSpec(
        num_scalar_prefetch=1,
        grid=(3, tiles),
        in_specs=[
            pl.BlockSpec((rows, tile), own),
            pl.BlockSpec((rows, tile), other),
            pl.BlockSpec((rows, tile), own),
            pl.BlockSpec((rows, tile), other),
            pl.BlockSpec((rows, HIDDEN), side),
            pl.BlockSpec((rows, HIDDEN), side),
        ],
        out_specs=pl.BlockSpec((tile, HIDDEN), lambda j, i, c: (i, j)),
    )
    return pl.pallas_call(
        weight_grads_kernel,
        grid_spec=grid,
        out_shape=jax.ShapeDtypeStruct((half, 3 * HIDDEN), BF16),
        compiler_params=pltpu.CompilerParams(vmem_limit_bytes=VMEM_LIMIT),
        cost_estimate=pl.CostEstimate(
            flops=2 * 3 * 2 * rows * half * HIDDEN, bytes_accessed=24 * 1024 * 1024, transcendentals=0
        ),
    )(core, x, x2, dy, dy2, right, right2)


def rows_times_kernel(left_ref, right_ref, *out_refs):
    result = dot_nt(left_ref[...], right_ref[...]).astype(BF16)
    for number, ref in enumerate(out_refs):
        ref[...] = result[128 * number : 128 * number + 128]


def rows_times(left, right, part):
    rows, depth = left.shape[0], HIDDEN
    width = right.shape[0]
    tile = 512
    return pl.pallas_call(
        rows_times_kernel,
        out_shape=(jax.ShapeDtypeStruct((128, width), BF16),) * 4,
        grid=(width // tile,),
        in_specs=[
            pl.BlockSpec((rows, depth), lambda i: (0, part)),
            pl.BlockSpec((tile, depth), lambda i: (i, part)),
        ],
        out_specs=(pl.BlockSpec((128, tile), lambda i: (0, i)),) * 4,
        compiler_params=pltpu.CompilerParams(vmem_limit_bytes=VMEM_LIMIT),
        cost_estimate=pl.CostEstimate(
            flops=2 * rows * depth * width,
            bytes_accessed=2 * (rows * depth + width * depth + rows * width),
            transcendentals=0,
        ),
    )(left, right)


def ring_rows(own, near, far):
    return jnp.concatenate([own, near[:128], far, near[128:]], 0)


def put_half(number, value, other_ref, own_ref):
    @pl.when(number < 2)
    def _():
        other_ref[...] = value

    @pl.when(number >= 2)
    def _():
        own_ref[...] = value


def tile_at(i, c):
    return lax.rem(i + 2 * (1 - c[0]), 4)


def half_specs(tile, columns):
    return (
        pl.BlockSpec((tile, columns), lambda i, c: (jnp.minimum(i, 1), 0)),
        pl.BlockSpec((tile, columns), lambda i, c: (jnp.maximum(i - 2, 0), 0)),
    )


def wide_grads_kernel(
    core_ref, x_ref, dh0, dh1, dh2, o0, o1, o2, dq0, dq1, dq2, other_ref, own_ref, o_held, dq_held
):
    number = pl.program_id(0)

    @pl.when(number == 0)
    def _():
        o_held[...] = ring_rows(o0[...], o1[...], o2[...])
        dq_held[...] = ring_rows(dq0[...], dq1[...], dq2[...])

    out = dot_tn(ring_rows(dh0[...], dh1[...], dh2[...]), o_held[...])
    query = dot_tn(x_ref[...], dq_held[...])
    put_half(number, jnp.concatenate([out, query], 1).astype(BF16), other_ref, own_ref)


def wide_grads(core, normed, dh, o, dq):
    rows, width = normed.shape
    tile = 512
    whole = lambda i, c: (0, 0)
    column = lambda i, c: (0, tile_at(i, c))
    small = [pl.BlockSpec((size, 512), whole) for size in (128, 256, 128)]
    grid = pltpu.PrefetchScalarGridSpec(
        num_scalar_prefetch=1,
        grid=(4,),
        in_specs=[pl.BlockSpec((rows, tile), column)]
        + [pl.BlockSpec((size, tile), column) for size in (128, 256, 128)]
        + small
        + small,
        out_specs=half_specs(tile, 1024),
        scratch_shapes=[pltpu.VMEM((rows, 512), BF16), pltpu.VMEM((rows, 512), BF16)],
    )
    return pl.pallas_call(
        wide_grads_kernel,
        grid_spec=grid,
        out_shape=(jax.ShapeDtypeStruct((width // 2, 1024), BF16),) * 2,
        compiler_params=pltpu.CompilerParams(vmem_limit_bytes=VMEM_LIMIT),
        cost_estimate=pl.CostEstimate(
            flops=2 * rows * width * 1024, bytes_accessed=10 * 1024 * 1024, transcendentals=0
        ),
    )(core, normed, *dh, *o, *dq)


def finish_kernel(
    core_ref,
    x_ref,
    w_ref,
    dq0_ref,
    dq1_ref,
    dq2_ref,
    own_ref,
    one_ref,
    two_ref,
    cos_ref,
    sin_ref,
    norm_ref,
    second_ref,
    other_grad_ref,
    own_grad_ref,
    dx_own,
    dx_ahead,
    dx_far,
    dx_behind,
    gain_ref,
    dqkv,
    sums,
):
    number = pl.program_id(0)

    @pl.when(number == 0)
    def _():
        dqkv[:, :512] = ring_rows(dq0_ref[...], dq1_ref[...], dq2_ref[...])
        dkv = own_ref[...] + one_ref[...].astype(F32) + two_ref[...].astype(F32)
        turned = turn(dkv, cos_ref[...], -sin_ref[...])
        dqkv[:, 512:] = jnp.where(lane_is_low(dkv.shape, 128), turned, dkv).astype(BF16)

    x = x_ref[...]
    put_half(number, dot_tn(x, dqkv[:, 512:]).astype(BF16), other_grad_ref, own_grad_ref)
    dx = dot_nt(dqkv[...], w_ref[:, 512:])
    for start, ref in ((0, dx_own), (128, dx_ahead), (256, dx_far), (384, dx_behind)):
        ref[...] = dx[start : start + 128].astype(BF16)
    columns = pl.ds(pl.multiple_of(tile_at(number, core_ref) * 512, 512), 512)
    sums[:, columns] = jnp.broadcast_to(
        jnp.sum(dx * x.astype(F32), 0, keepdims=True) / norm_ref[...], (8, 512)
    )

    @pl.when(number == 3)
    def _():
        gain_ref[:8] = gain_rows(to_blocks(sums[...])[:1])
        gain_ref[8:] = gain_rows(second_ref[:1])


def finish(core, normed, weights, dq, own, one, two, cosine, sine, gain, second):
    rows, width = normed.shape
    tile = 512
    whole = lambda i, c: (0, 0)
    column = lambda i, c: (0, tile_at(i, c))
    narrow = pl.BlockSpec((rows, 128), whole)
    grid = pltpu.PrefetchScalarGridSpec(
        num_scalar_prefetch=1,
        grid=(4,),
        in_specs=[
            pl.BlockSpec((rows, tile), column),
            pl.BlockSpec((tile, 1152), lambda i, c: (tile_at(i, c), 0)),
            pl.BlockSpec((128, 512), whole),
            pl.BlockSpec((256, 512), whole),
            pl.BlockSpec((128, 512), whole),
            narrow,
            narrow,
            narrow,
            narrow,
            narrow,
            pl.BlockSpec((1, tile), column),
            pl.BlockSpec((8, width), whole),
        ],
        out_specs=half_specs(tile, 128)
        + (pl.BlockSpec((128, tile), column),) * 4
        + (pl.BlockSpec((GAIN_ROWS, GAIN_COLUMNS), whole),),
        scratch_shapes=[pltpu.VMEM((rows, 640), BF16), pltpu.VMEM((8, width), F32)],
    )
    result = pl.pallas_call(
        finish_kernel,
        grid_spec=grid,
        out_shape=(jax.ShapeDtypeStruct((width // 2, 128), BF16),) * 2
        + (jax.ShapeDtypeStruct((128, width), BF16),) * 4
        + (jax.ShapeDtypeStruct((GAIN_ROWS, GAIN_COLUMNS), F32),),
        compiler_params=pltpu.CompilerParams(vmem_limit_bytes=VMEM_LIMIT),
        cost_estimate=pl.CostEstimate(
            flops=2 * rows * width * 768, bytes_accessed=10 * 1024 * 1024, transcendentals=0
        ),
    )(core, normed, weights, *dq, own, one, two, cosine, sine, gain, second)
    return result[0], result[1], result[2:6], result[6]


def per_device(
    tokens,
    segments,
    w_query,
    key_projection,
    value_projection,
    w_out,
    w_gate,
    w_up,
    w_down,
    norm_attn,
    norm_ffn,
    cotangent,
):
    place, core = lax.axis_index("head"), lax.axis_index("core")
    block = (lax.axis_index("y") * 4 + lax.axis_index("x")) * 2 + core
    place_array = place.astype(jnp.int32).reshape(1)
    core_array = core.astype(jnp.int32).reshape(1)
    keep = lax.optimization_barrier

    attention_weights = lax.all_gather(
        jnp.concatenate([w_out.T, w_query, key_projection, value_projection], 1),
        CORE_FIRST,
        axis=0,
        tiled=True,
    )
    ffn_weights = lax.all_gather(
        jnp.concatenate([w_gate, w_up, w_down.T], 1), CORE_FIRST, axis=0, tiled=True
    )

    x_rows, dy_rows, normed_rows, gain_one, gain_two = prepare(
        tokens[0],
        cotangent[0],
        jnp.broadcast_to(norm_attn[None], (16, 2048)),
        jnp.broadcast_to(norm_ffn[None], (16, 2048)),
    )
    gain_one, gain_two = gain_one[:1], gain_two[:1]
    normed_one = gather_head(normed_rows)
    normed_one, dy_rows_late = keep((normed_one, dy_rows))
    dy = gather_head(dy_rows_late)

    row = jnp.arange(512, dtype=jnp.int32)
    positions = block * 512 + ((row // 128 + place) % 4) * 128 + row % 128
    frequency = 10000.0 ** (-jnp.arange(32, dtype=F32) * 2.0 / HEAD_SIZE)
    angles = positions.astype(F32)[:, None] * frequency[None, :]
    cosine, sine = jnp.cos(angles), jnp.sin(angles)
    cosine = jnp.concatenate([cosine] * 4, 1)
    sine = jnp.concatenate([-sine, sine, -sine, sine], 1)

    kv_own = project(project_kv_kernel, normed_one, attention_weights, cosine, sine, 1024, 128, 128)
    normed_late, kv_own = keep((normed_one, kv_own))
    kv = (from_block(kv_own, 2), from_block(kv_own, 1), kv_own)
    queries = project(project_q_kernel, normed_late, attention_weights, cosine, sine, 512, 512, 256)

    flat = segments.reshape(-1)
    padded = jnp.concatenate([jnp.full((1024,), -1, jnp.int32), flat])
    qseg = lax.dynamic_slice_in_dim(flat, block * 512, 512, 0).reshape(1, 512)
    kseg = lax.dynamic_slice_in_dim(padded, block * 512, 1536, 0).reshape(1536, 1)

    kv, dy = keep((kv, dy))
    kk, vv, kvt = set_up(place_array, kv)
    seen = place_array, queries, kk, kvt, qseg, kseg, attention_weights
    o_far, lse_far, part_far = attend(2, 1, 1, *seen)
    o_near, lse_near, part_near = attend(1, 2, 2, *seen)
    o_own, lse_own, part_own = attend(0, 1, 1, *seen)
    dy_other = swap_half(dy, core)
    attention_sum = scatter_pieces(part_own, part_near[:128], part_far, part_near[128:])
    h1, normed_rows_two = join(x_rows, gain_two, attention_sum)
    ahead, far, behind = gather_pieces(normed_rows_two)
    dact = columns_times(dy, ffn_weights, 2)
    dact, dy_other = keep((dact, dy_other))

    gua, normed_two, dnormed_two = ffn((normed_rows_two, ahead, far, behind), dact, ffn_weights)
    dnormed_two = scatter_pieces(*dnormed_two)
    gua_other = shift(gua, "core", 1)
    normed_two_other = swap_half(normed_two, core)
    out_pieces = rows_times(gua, ffn_weights, 2)
    gua_other, normed_two_other, out_pieces = keep((gua_other, normed_two_other, out_pieces))
    held = weight_grads(core_array, normed_two, normed_two_other, dy, dy_other, gua, gua_other)
    held, dnormed_two = keep((held, dnormed_two))
    grads = lax.psum_scatter(held, ("y", "x"), scatter_dimension=0, tiled=True)

    dh1, dh1_low, grad_gain_two = join_back(h1, dy_rows, gain_two, dnormed_two)
    back = kk, vv, kvt, qseg, kseg, cosine, sine
    dq_own, dk, dv = attend_back(0, 1, 1, place_array, queries, dh1_low, attention_weights, lse_own, *back, ())
    ahead, behind = shift(dh1_low, "head", -1), shift(dh1_low, "head", 1)
    ahead, behind, dk, dv, dh1_late, out_pieces = keep((ahead, behind, dk, dv, dh1_low, out_pieces))
    far = shift(dh1_late, "head", 2)
    near = jnp.concatenate([ahead, behind], 0)
    dq_near, dk, dv = attend_back(
        1, 2, 2, place_array, queries, near, attention_weights, lse_near, *back, (dk, dv)
    )
    far, dk, dv, out_pieces = keep((far, dk, dv, out_pieces))
    out_pieces = scatter_pieces(*out_pieces)
    dq_far, dkv_own, dkv_earlier = attend_back(
        2, 1, 1, place_array, queries, far, attention_weights, lse_far, *back, (dk, dv)
    )
    dq = dq_own, dq_near, dq_far
    dkv_one = from_block(dkv_earlier[1], -1)
    dkv_two = from_block(dkv_earlier[0], -2)
    wide_other, wide_own = wide_grads(
        core_array, normed_one, (dh1_low, near, far), (o_own, o_near, o_far), dq
    )
    dkv_one, dkv_two, wide_other, out_pieces = keep((dkv_one, dkv_two, wide_other, out_pieces))
    wide_other = shift(wide_other, "core", 1)

    narrow_other, narrow_own, dnormed_one, gains = finish(
        core_array,
        normed_one,
        attention_weights,
        dq,
        dkv_own,
        dkv_one,
        dkv_two,
        cosine,
        sine,
        gain_one,
        grad_gain_two,
    )
    pieces = pieces_x(
        lax.axis_index("x").astype(jnp.int32).reshape(1),
        wide_own,
        wide_other,
        narrow_own,
        shift(narrow_other, "core", 1),
        gains,
        shift(gains, "core", 1),
    )
    pieces, dnormed_one = keep((pieces, dnormed_one))
    rows = [(x_rows.shape, BF16)]
    (output,) = small_call(output_kernel, rows, h1, *out_pieces)
    grads = (
        grads[:, :HIDDEN].astype(F32),
        grads[:, HIDDEN : 2 * HIDDEN].astype(F32),
        grads[:, 2 * HIDDEN :].T.astype(F32),
    )
    pieces, output, grads = keep((exchange(pieces, "x"), output, grads))
    pieces = pieces_y(lax.axis_index("y").astype(jnp.int32).reshape(1), pieces)
    dnormed_one = scatter_pieces(*dnormed_one)
    (grad_inputs,) = small_call(input_grad_kernel, rows, dh1, x_rows, gain_one, *dnormed_one)
    pieces, grad_inputs = keep((exchange(pieces, "y"), grad_inputs))
    columns = (512, 64), (64, 512), (64, 64), (64, 64), (GAIN_ROWS, GAIN_COLUMNS)
    grad_out, grad_query, grad_key, grad_value, gains = small_call(
        attention_grads_kernel, [(shape, F32) for shape in columns], *pieces
    )
    grad_gain_one, grad_gain_two = small_call(
        gains_kernel, [((1, 2048), F32)] * 2, *exchange([gains] * 4, "head")
    )

    return (
        output[None],
        grad_inputs[None],
        grad_query,
        grad_key,
        grad_value,
        grad_out,
        *grads,
        grad_gain_one.reshape(2048),
        grad_gain_two.reshape(2048),
    )


def solution(mesh):
    grid = Mesh(mesh.devices.reshape(4, 4, 4, 2), ("head", "y", "x", "core"))
    rows, up, down = P(BLK, "head", None), P(BLK, "head"), P("head", BLK)
    return jax.shard_map(
        per_device,
        mesh=grid,
        in_specs=(rows, P(), up, up, up, down, up, up, down, P(), P(), rows),
        out_specs=(rows, rows, up, up, up, down, up, up, down, P(), P()),
        check_vma=False,
    )
```

```python
import functools

import jax
import jax.numpy as jnp
from jax import lax
from jax.experimental import pallas as pl
from jax.experimental.pallas import tpu as pltpu
from jax.sharding import Mesh
from jax.sharding import PartitionSpec as P

HEAD_SIZE = 64
WINDOW = 1024
EPSILON = 1e-05
BF16 = jnp.bfloat16
F32 = jnp.float32
BLK = ("y", "x", "core")
CORE_FIRST = ("core", "y", "x")
VMEM_LIMIT = 56 * 1024 * 1024


def dot_nn(a, b):
    return jnp.dot(a, b, preferred_element_type=F32)


def dot_nt(a, b):
    return lax.dot_general(a, b, (((1,), (1,)), ((), ())), preferred_element_type=F32)


def dot_tn(a, b):
    return lax.dot_general(a, b, (((0,), (0,)), ((), ())), preferred_element_type=F32)


def shift(value, axis, distance):
    size = lax.axis_size(axis)
    return lax.ppermute(value, axis, [(i, (i + distance) % size) for i in range(size)])


def add_low(a, b):
    return (a.astype(F32) + b.astype(F32)).astype(BF16)


def gather_pieces(rows):
    return shift(rows, "head", -1), shift(rows, "head", 2), shift(rows, "head", 1)


def gather_head(rows):
    return jnp.concatenate([rows, *gather_pieces(rows)], 0)


def scatter_pieces(own, ahead, far, behind):
    return own, shift(ahead, "head", 1), shift(behind, "head", -1), shift(far, "head", 2)


def swap_half(value, core):
    width = value.shape[1] // 2
    return shift(lax.dynamic_slice_in_dim(value, (1 - core) * width, width, 1), "core", 1)


def exchange(pieces, axis):
    return pieces[0], shift(pieces[1], axis, 1), shift(pieces[2], axis, 2), shift(pieces[3], axis, -1)


def from_block(value, distance):
    route = [(i, i + distance) for i in range(32) if 0 <= i + distance < 32]
    return lax.ppermute(value, BLK, route)


def scale_of(values):
    return lax.rsqrt(jnp.mean(values * values, -1, keepdims=True) + EPSILON)


def lane_is_low(shape, period):
    return lax.broadcasted_iota(jnp.int32, shape, len(shape) - 1) % period < period // 2


def turn(values, cosine, sine):
    swapped = jnp.where(
        lane_is_low(values.shape, 64), pltpu.roll(values, 96, 1), pltpu.roll(values, 32, 1)
    )
    return values * cosine + swapped * sine


def core_major_tiles(tiles):
    low = lane_is_low(tiles[0].shape, 128)
    rolled = [pltpu.roll(tile, 64, 1) for tile in tiles]
    first = [jnp.where(low, tiles[2 * k], rolled[2 * k + 1]) for k in range(8)]
    second = [jnp.where(low, rolled[2 * k], tiles[2 * k + 1]) for k in range(8)]
    return first + second


def block_major_tiles(tiles):
    low = lane_is_low(tiles[0].shape, 128)
    rolled = [pltpu.roll(tile, 64, 1) for tile in tiles]
    result = []
    for k in range(8):
        result.append(jnp.where(low, tiles[k], rolled[8 + k]))
        result.append(jnp.where(low, rolled[k], tiles[8 + k]))
    return result


def in_tiles(value):
    return [value[:, 128 * k : 128 * k + 128] for k in range(16)]


def prepare_kernel(x_ref, dy_ref, gain_one_ref, gain_two_ref, x_out, dy_out, normed_out, one_out, two_out):
    def convert(ref):
        return jnp.concatenate(core_major_tiles(in_tiles(ref[...].astype(F32))), 1)

    x, gain = convert(x_ref), convert(gain_one_ref)
    one_out[...], two_out[...] = gain, convert(gain_two_ref)
    x_out[...] = x
    dy_out[...] = convert(dy_ref).astype(BF16)
    normed_out[...] = (x * scale_of(x) * gain[:1]).astype(BF16)


def prepare(x, dy, gain_one, gain_two):
    rows, width = x.shape
    return pl.pallas_call(
        prepare_kernel,
        out_shape=(
            jax.ShapeDtypeStruct((rows, width), F32),
            jax.ShapeDtypeStruct((rows, width), BF16),
            jax.ShapeDtypeStruct((rows, width), BF16),
            jax.ShapeDtypeStruct((16, width), F32),
            jax.ShapeDtypeStruct((16, width), F32),
        ),
        compiler_params=pltpu.CompilerParams(vmem_limit_bytes=VMEM_LIMIT),
        cost_estimate=pl.CostEstimate(
            flops=10 * rows * width, bytes_accessed=10 * rows * width, transcendentals=rows
        ),
    )(x, dy, gain_one, gain_two)


def to_blocks(value):
    return jnp.concatenate(block_major_tiles(in_tiles(value)), 1)


def small_call(kernel, out_shape, *operands):
    return pl.pallas_call(
        kernel,
        out_shape=tuple(jax.ShapeDtypeStruct(shape, dtype) for shape, dtype in out_shape),
        compiler_params=pltpu.CompilerParams(vmem_limit_bytes=VMEM_LIMIT),
        cost_estimate=pl.CostEstimate(
            flops=sum(x.size for x in operands),
            bytes_accessed=2 * sum(x.size * x.dtype.itemsize for x in operands),
            transcendentals=0,
        ),
    )(*operands)


def total_of(refs):
    values = [ref[...].astype(F32) for ref in refs]
    while len(values) > 1:
        values = [values[0] + values[1]] + values[2:]
    return values[0]


def join_kernel(x_ref, gain_ref, a_ref, b_ref, c_ref, d_ref, h_out, normed_out):
    h = x_ref[...] + total_of((a_ref, b_ref, c_ref, d_ref))
    h_out[...] = h
    normed_out[...] = (h * scale_of(h) * gain_ref[...]).astype(BF16)


def join(x, gain, pieces):
    return small_call(join_kernel, ((x.shape, F32), (x.shape, BF16)), x, gain, *pieces)


def norm_backward(values, gain, grad):
    scale = scale_of(values)
    weighted = grad * gain
    inner = jnp.mean(weighted * values, -1, keepdims=True)
    return scale * weighted - values * (scale * scale * scale * inner), scale


def join_back_kernel(h_ref, dy_ref, gain_ref, a_ref, b_ref, c_ref, d_ref, dh_out, low_out, grad_out):
    h, grad = h_ref[...], total_of((a_ref, b_ref, c_ref, d_ref))
    back, scale = norm_backward(h, gain_ref[...], grad)
    dh = dy_ref[...].astype(F32) + back
    dh_out[...] = dh
    low_out[...] = dh.astype(BF16)
    grad_out[...] = to_blocks(jnp.broadcast_to(jnp.sum(grad * h * scale, 0, keepdims=True), (8, h.shape[1])))


def join_back(h, dy, gain, pieces):
    shapes = (h.shape, F32), (h.shape, BF16), ((8, h.shape[1]), F32)
    return small_call(join_back_kernel, shapes, h, dy, gain, *pieces)


def output_kernel(h_ref, a_ref, b_ref, c_ref, d_ref, out_ref):
    out_ref[...] = to_blocks(h_ref[...] + total_of((a_ref, b_ref, c_ref, d_ref))).astype(BF16)


def input_grad_kernel(dh_ref, x_ref, gain_ref, a_ref, b_ref, c_ref, d_ref, out_ref):
    back, _ = norm_backward(x_ref[...], gain_ref[...], total_of((a_ref, b_ref, c_ref, d_ref)))
    out_ref[...] = to_blocks(dh_ref[...] + back).astype(BF16)


GAIN_ROWS, GAIN_COLUMNS = 16, 256


def gain_rows(vector):
    return jnp.concatenate([vector[:, 256 * k : 256 * k + 256] for k in range(8)], 0)


def put_piece(ref, rows, gains):
    count = rows.shape[0]
    ref[:count] = rows
    ref[count:, GAIN_COLUMNS:] = jnp.zeros((GAIN_ROWS, ref.shape[1] - GAIN_COLUMNS), BF16)
    ref[count:, :GAIN_COLUMNS] = gains.astype(BF16)


def first_pieces_kernel(
    at_ref, q_ref, q2_ref, kv_ref, kv2_ref, o_ref, o2_ref, gain_ref, gain2_ref, *out_refs
):
    query = add_low(q_ref[...], q2_ref[...]).reshape(256, 512)
    narrow = add_low(kv_ref[...], kv2_ref[...]).reshape(256, 128)
    rows = jnp.concatenate([query, narrow], 1)
    out_rows = add_low(o_ref[...], o2_ref[...]).reshape(256, 512)
    gains = gain_ref[...] + gain2_ref[...]
    for number in range(4):

        @pl.when(pl.program_id(0) == number)
        def _():
            put_piece(out_refs[number], rows, gains)
            out_refs[4 + number][...] = out_rows


def first_pieces(at, wide, wide2, narrow, narrow2, gains, gains2):
    pick_x = lambda column: lambda d, s: (0, lax.rem(s[0] + d, 4), 0, column)
    pick_y = lambda d, s: (lax.rem(s[1] + d, 4), 0, 0, 0)
    whole = lambda d, s: (0, 0)
    shaped = lambda value: value.reshape(4, 4, 64, value.shape[1])
    shapes = [(256 + GAIN_ROWS, 640)] * 4 + [(256, 512)] * 4
    grid = pltpu.PrefetchScalarGridSpec(
        num_scalar_prefetch=1,
        grid=(4,),
        in_specs=[pl.BlockSpec((4, 1, 64, 512), pick_x(1))] * 2
        + [pl.BlockSpec((4, 1, 64, 128), pick_x(0))] * 2
        + [pl.BlockSpec((1, 4, 64, 512), pick_y)] * 2
        + [pl.BlockSpec((GAIN_ROWS, GAIN_COLUMNS), whole)] * 2,
        out_specs=tuple(pl.BlockSpec(shape, whole) for shape in shapes),
    )
    wide, wide2 = shaped(wide), shaped(wide2)
    result = pl.pallas_call(
        first_pieces_kernel,
        grid_spec=grid,
        out_shape=tuple(jax.ShapeDtypeStruct(shape, BF16) for shape in shapes),
        compiler_params=pltpu.CompilerParams(vmem_limit_bytes=VMEM_LIMIT),
        cost_estimate=pl.CostEstimate(
            flops=2 * 1024 * 1152, bytes_accessed=6 * 1024 * 1152, transcendentals=0
        ),
    )(at, wide, wide2, shaped(narrow), shaped(narrow2), wide, wide2, gains, gains2)
    return result[:4], result[4:]


def second_pieces_kernel(at_ref, *refs):
    qkv, out, (held, out_held) = refs[:4], refs[4:8], refs[16:]
    held[...] = total_of(qkv)
    out_held[...] = total_of(out).astype(BF16)
    for number in range(4):
        y = pl.multiple_of(lax.rem(at_ref[1] + number, 4) * 64, 64)
        put_piece(refs[8 + number], held[pl.ds(y, 64), :].astype(BF16), held[256:, :GAIN_COLUMNS])
        x = pl.multiple_of(lax.rem(at_ref[0] + number, 4) * 64, 64)
        refs[12 + number][...] = out_held[pl.ds(x, 64), :]


def second_pieces(at, qkv, out):
    vmem = pl.BlockSpec(memory_space=pltpu.VMEM)
    shapes = [(64 + GAIN_ROWS, 640)] * 4 + [(64, 512)] * 4
    result = pl.pallas_call(
        second_pieces_kernel,
        out_shape=tuple(jax.ShapeDtypeStruct(shape, BF16) for shape in shapes),
        in_specs=[pl.BlockSpec(memory_space=pltpu.SMEM)] + [vmem] * 8,
        out_specs=(vmem,) * 8,
        scratch_shapes=[pltpu.VMEM((256 + GAIN_ROWS, 640), F32), pltpu.VMEM((256, 512), BF16)],
        compiler_params=pltpu.CompilerParams(vmem_limit_bytes=VMEM_LIMIT),
        cost_estimate=pl.CostEstimate(
            flops=4 * 272 * 1152, bytes_accessed=10 * 272 * 1152, transcendentals=0
        ),
    )(at, *qkv, *out)
    return result[:4], result[4:]


def attention_grads_kernel(*refs):
    out_ref, q_ref, k_ref, v_ref, gain_ref = refs[8:]
    total = total_of(refs[:4])
    out_ref[...] = total_of(refs[4:8]).T
    q_ref[...] = total[:64, :512]
    k_ref[...] = total[:64, 512:576]
    v_ref[...] = total[:64, 576:]
    gain_ref[...] = total[64:, :GAIN_COLUMNS]


def gains_kernel(a_ref, b_ref, c_ref, d_ref, one_ref, two_ref):
    total = total_of((a_ref, b_ref, c_ref, d_ref))
    one_ref[...] = jnp.concatenate([total[k : k + 1] for k in range(8)], 1)
    two_ref[...] = jnp.concatenate([total[k : k + 1] for k in range(8, 16)], 1)


def project_kv_kernel(x_ref, w_ref, cos_ref, sin_ref, kv_ref):
    flat = dot_nn(x_ref[...], w_ref[...])
    turned = turn(flat, cos_ref[...], sin_ref[...])
    kv_ref[...] = jnp.where(lane_is_low(flat.shape, 128), turned, flat).astype(BF16)


def project_q_kernel(x_ref, w_ref, cos_ref, sin_ref, q_ref):
    cosine, sine = cos_ref[...], sin_ref[...]
    wide = dot_nn(x_ref[...], w_ref[...])
    for part in (0, 128):
        turned = turn(wide[:, part : part + 128], cosine, sine)
        q_ref[:, part : part + 128] = (turned * HEAD_SIZE**-0.5).astype(BF16)


def project(kernel, normed, weights, cosine, sine, start, columns, tile):
    rows, width = normed.shape
    whole = lambda i: (0, 0)
    return pl.pallas_call(
        kernel,
        out_shape=jax.ShapeDtypeStruct((rows, columns), BF16),
        grid=(columns // tile,),
        in_specs=[
            pl.BlockSpec((rows, width), whole),
            pl.BlockSpec((width, tile), lambda i: (0, start // tile + i)),
            pl.BlockSpec((rows, 128), whole),
            pl.BlockSpec((rows, 128), whole),
        ],
        out_specs=pl.BlockSpec((rows, tile), lambda i: (0, i)),
        compiler_params=pltpu.CompilerParams(vmem_limit_bytes=VMEM_LIMIT),
        cost_estimate=pl.CostEstimate(
            flops=2 * rows * width * columns,
            bytes_accessed=2 * (rows * width + width * columns + rows * columns),
            transcendentals=0,
        ),
    )(normed, weights, cosine, sine)


KEYS = 1152
PAIRS = 4


def set_up_kernel(place_ref, kv0_ref, kv1_ref, kv2_ref, kk_ref, vv_ref, kvt_ref):
    place = place_ref[0]
    low = lane_is_low((128, 128), 128)
    for block, ref in enumerate((kv0_ref, kv1_ref, kv2_ref)):
        for group in range(4):
            at = pl.multiple_of(lax.rem(group - place + 4, 4) * 128, 128)
            piece = ref[pl.ds(at, 128), :].astype(F32)
            rolled = pltpu.roll(piece, 64, 1)
            to = block * 512 + group * 128
            kk_ref[to : to + 128, :] = jnp.where(low, piece, rolled).astype(BF16)
            vv_ref[to : to + 128, :] = jnp.where(low, rolled, piece).astype(BF16)
            kvt_ref[:, to : to + 128] = piece.T.astype(BF16)


def set_up(place, kv):
    vmem = pl.BlockSpec(memory_space=pltpu.VMEM)
    return pl.pallas_call(
        set_up_kernel,
        out_shape=(
            jax.ShapeDtypeStruct((1536, 128), BF16),
            jax.ShapeDtypeStruct((1536, 128), BF16),
            jax.ShapeDtypeStruct((128, 1536), BF16),
        ),
        in_specs=[pl.BlockSpec(memory_space=pltpu.SMEM), vmem, vmem, vmem],
        out_specs=(vmem, vmem, vmem),
        compiler_params=pltpu.CompilerParams(vmem_limit_bytes=VMEM_LIMIT),
        cost_estimate=pl.CostEstimate(flops=1536 * 128 * 8, bytes_accessed=2 * 1024 * 1024, transcendentals=0),
    )(place, *kv)


def both_heads(pair):
    low = lane_is_low(pair.shape, 128)
    nothing = jnp.zeros_like(pair)
    return jnp.concatenate([jnp.where(low, pair, nothing), jnp.where(low, nothing, pair)], 0)


def side_by_side(transposed):
    return jnp.concatenate([transposed[:, :128], transposed[:, 128:]], 0).T


def mask_of(at, low_ref):
    key = lax.broadcasted_iota(jnp.int32, (KEYS, 128), 0)
    query = lax.broadcasted_iota(jnp.int32, (KEYS, 128), 1)
    seen = (key >= low_ref[:, pl.ds(at, 128)] - at) & (key <= query + WINDOW)
    bias = jnp.where(seen, 0.0, -jnp.inf)
    return jnp.concatenate([bias, bias], 1)


def attend_kernel(
    first, step, place_ref, q_ref, kk_ref, kvt_ref, low_ref, w_ref, o_ref, lse_ref, part_ref, bias, held, w_held, sem
):
    group = lax.rem(place_ref[0] + first + step * pl.program_id(0), 4)
    at = pl.multiple_of(group * 128, 128)

    load = pltpu.make_async_copy(w_ref.at[:, pl.ds(0, 512)], w_held, sem)

    @pl.when((pl.program_id(0) == 0) & (pl.program_id(1) == 0))
    def _():
        load.start()

    @pl.when(pl.program_id(1) == 0)
    def _():
        bias[...] = mask_of(at, low_ref)

    keys = pl.ds(at, KEYS)
    for number in range(PAIRS):
        columns = slice(128 * number, 128 * number + 128)
        scores = dot_nt(kk_ref[keys, :], both_heads(q_ref[:, columns])) + bias[...]
        top = jnp.max(scores, 0, keepdims=True)
        weights = jnp.exp(scores - top)
        total = jnp.sum(weights, 0, keepdims=True)
        result = dot_nn(kvt_ref[64:128, keys], weights.astype(BF16)) / total
        lse_ref[0, number] = top + jnp.log(total)
        result = side_by_side(result).astype(BF16)
        o_ref[:, columns] = result
        held[PAIRS * pl.program_id(1) + number] = result

    @pl.when(pl.program_id(1) == 4 // PAIRS - 1)
    def _():
        @pl.when(pl.program_id(0) == 0)
        def _():
            load.wait()

        rows = jnp.concatenate([held[k] for k in range(4)], 1)
        part_ref[...] = dot_nt(rows, w_held[...]).astype(BF16)


def attend(first, step, count, place, queries, kk, kvt, low, attention_weights):
    whole = lambda g, p, s: (0, 0)
    width = 128 * PAIRS
    grid = pltpu.PrefetchScalarGridSpec(
        num_scalar_prefetch=1,
        grid=(count, 4 // PAIRS),
        in_specs=[
            pl.BlockSpec((128, width), lambda g, p, s: (first + step * g, p)),
            pl.BlockSpec((1536, 128), whole),
            pl.BlockSpec((128, 1536), whole),
            pl.BlockSpec((1, 512), whole),
            pl.BlockSpec(memory_space=pl.ANY),
        ],
        out_specs=(
            pl.BlockSpec((128, width), lambda g, p, s: (g, p)),
            pl.BlockSpec((1, PAIRS, 1, 256), lambda g, p, s: (g, p, 0, 0)),
            pl.BlockSpec((128, 2048), lambda g, p, s: (g, 0)),
        ),
        scratch_shapes=[
            pltpu.VMEM((KEYS, 256), F32),
            pltpu.VMEM((4, 128, 128), BF16),
            pltpu.VMEM((2048, 512), BF16),
            pltpu.SemaphoreType.DMA,
        ],
    )
    return pl.pallas_call(
        functools.partial(attend_kernel, first, step),
        grid_spec=grid,
        out_shape=(
            jax.ShapeDtypeStruct((128 * count, 512), BF16),
            jax.ShapeDtypeStruct((count, 4, 1, 256), F32),
            jax.ShapeDtypeStruct((128 * count, 2048), BF16),
        ),
        compiler_params=pltpu.CompilerParams(vmem_limit_bytes=VMEM_LIMIT),
        cost_estimate=pl.CostEstimate(
            flops=count * 4 * KEYS * 256 * 256 * 2,
            bytes_accessed=3 * 1024 * 1024,
            transcendentals=count * 4 * KEYS * 256,
        ),
    )(place, queries, kk, kvt, low, attention_weights)


def attend_back_kernel(first, step, last, *refs):
    place_ref, q_ref, dh_ref, w_ref, lse_ref, kk_ref, vv_ref, kvt_ref, low_ref, cos_ref, sin_ref = refs[:11]
    if first == 0:
        dk_in, dv_in, refs = None, None, refs[11:]
    else:
        dk_in, dv_in, refs = refs[11], refs[12], refs[13:]
    dq_ref, one_out, two_out, bias, do_held, dk, dv, w_held, sem = refs
    number, pair = pl.program_id(0), pl.program_id(1)
    place = place_ref[0]
    at = pl.multiple_of(lax.rem(place + first + step * number, 4) * 128, 128)

    load = pltpu.make_async_copy(w_ref.at[:, pl.ds(0, 512)], w_held, sem)

    @pl.when((number == 0) & (pair == 0))
    def _():
        load.start()
        dk[...] = jnp.zeros_like(dk) if dk_in is None else dk_in[...]
        dv[...] = jnp.zeros_like(dv) if dv_in is None else dv_in[...]

    @pl.when(pair == 0)
    def _():
        bias[...] = mask_of(at, low_ref)

        @pl.when(number == 0)
        def _():
            load.wait()

        do_rows = dot_nn(dh_ref[...], w_held[...]).astype(BF16)
        for k in range(4):
            do_held[k] = do_rows[:, 128 * k : 128 * k + 128]

    keys = pl.ds(at, KEYS)
    queries, grads, all_weights, all_grad_scores = [], [], [], []
    for k in range(PAIRS):
        columns = slice(128 * k, 128 * k + 128)
        query, grad = both_heads(q_ref[:, columns]), both_heads(do_held[PAIRS * pair + k])
        scores = dot_nt(kk_ref[keys, :], query) + bias[...]
        weights = jnp.exp(scores - lse_ref[0, k])
        grad_weights = dot_nt(vv_ref[keys, :], grad)
        inner = jnp.sum(weights * grad_weights, 0, keepdims=True)
        grad_scores = (weights * (grad_weights - inner)).astype(BF16)
        grad_query = side_by_side(dot_nn(kvt_ref[0:64, keys], grad_scores)) * HEAD_SIZE**-0.5
        dq_ref[:, columns] = turn(grad_query, cos_ref[...], -sin_ref[...]).astype(BF16)
        queries.append(query)
        grads.append(grad)
        all_weights.append(weights.astype(BF16))
        all_grad_scores.append(grad_scores)
    join = lambda values, axis: values[0] if PAIRS == 1 else jnp.concatenate(values, axis)
    dv[keys, :] += dot_nn(join(all_weights, 1), join(grads, 0))
    dk[keys, :] += dot_nn(join(all_grad_scores, 1), join(queries, 0))

    @pl.when((number == pl.num_programs(0) - 1) & (pair == 4 // PAIRS - 1))
    def _():
        if not last:
            one_out[...], two_out[...] = dk[...], dv[...]
            return
        half = lane_is_low((128, 128), 128)
        for block in range(3):
            for group in range(4):
                to = pl.multiple_of(lax.rem(group - place + 4, 4) * 128, 128)
                frm = slice(block * 512 + group * 128, block * 512 + group * 128 + 128)
                key, value = dk[frm, :], dv[frm, :]
                key = key + pltpu.roll(key, 64, 1)
                value = value + pltpu.roll(value, 64, 1)
                both = jnp.where(half, key, value)
                if block == 2:
                    one_out[pl.ds(to, 128), :] = both
                else:
                    two_out[block, pl.ds(to, 128), :] = both.astype(BF16)


def attend_back(first, step, count, place, queries, dh, attention_weights, lse, kk, vv, kvt, low, cosine, sine, held):
    last = first == 2
    whole = lambda g, p, s: (0, 0)
    specs = [
        pl.BlockSpec((128, 128 * PAIRS), lambda g, p, s: (first + step * g, p)),
        pl.BlockSpec((128, 2048), lambda g, p, s: (g, 0)),
        pl.BlockSpec(memory_space=pl.ANY),
        pl.BlockSpec((1, PAIRS, 1, 256), lambda g, p, s: (g, p, 0, 0)),
        pl.BlockSpec((1536, 128), whole),
        pl.BlockSpec((1536, 128), whole),
        pl.BlockSpec((128, 1536), whole),
        pl.BlockSpec((1, 512), whole),
        pl.BlockSpec((128, 128), lambda g, p, s: (first + step * g, 0)),
        pl.BlockSpec((128, 128), lambda g, p, s: (first + step * g, 0)),
    ] + [pl.BlockSpec((1536, 128), whole)] * len(held)
    if last:
        out_specs = (pl.BlockSpec((512, 128), whole), pl.BlockSpec((2, 512, 128), lambda g, p, s: (0, 0, 0)))
        out_shape = (jax.ShapeDtypeStruct((512, 128), F32), jax.ShapeDtypeStruct((2, 512, 128), BF16))
    else:
        out_specs = (pl.BlockSpec((1536, 128), whole),) * 2
        out_shape = (jax.ShapeDtypeStruct((1536, 128), F32),) * 2
    grid = pltpu.PrefetchScalarGridSpec(
        num_scalar_prefetch=1,
        grid=(count, 4 // PAIRS),
        in_specs=specs,
        out_specs=(pl.BlockSpec((128, 128 * PAIRS), lambda g, p, s: (g, p)),) + out_specs,
        scratch_shapes=[
            pltpu.VMEM((KEYS, 256), F32),
            pltpu.VMEM((4, 128, 128), BF16),
            pltpu.VMEM((1536, 128), F32),
            pltpu.VMEM((1536, 128), F32),
            pltpu.VMEM((2048, 512), BF16),
            pltpu.SemaphoreType.DMA,
        ],
    )
    return pl.pallas_call(
        functools.partial(attend_back_kernel, first, step, last),
        grid_spec=grid,
        out_shape=(jax.ShapeDtypeStruct((128 * count, 512), BF16),) + out_shape,
        compiler_params=pltpu.CompilerParams(vmem_limit_bytes=VMEM_LIMIT),
        cost_estimate=pl.CostEstimate(
            flops=count * 4 * KEYS * 256 * 640 * 2,
            bytes_accessed=6 * 1024 * 1024,
            transcendentals=count * 4 * KEYS * 256,
        ),
    )(place, queries, dh, attention_weights, lse, kk, vv, kvt, low, cosine, sine, *held)


HIDDEN = 1408
GROUPS = [(0, 128), (128, 256), (384, 512), (896, 512)]


def columns_times_kernel(left_ref, right_ref, out_ref):
    out_ref[...] = dot_nn(left_ref[...], right_ref[...])


def columns_times(left, right, part):
    rows, width = left.shape
    return pl.pallas_call(
        columns_times_kernel,
        out_shape=jax.ShapeDtypeStruct((rows, HIDDEN), F32),
        grid=(1,),
        in_specs=[
            pl.BlockSpec((rows, width), lambda i: (0, 0)),
            pl.BlockSpec((width, HIDDEN), lambda i: (0, part)),
        ],
        out_specs=pl.BlockSpec((rows, HIDDEN), lambda i: (0, 0)),
        compiler_params=pltpu.CompilerParams(vmem_limit_bytes=VMEM_LIMIT),
        cost_estimate=pl.CostEstimate(
            flops=2 * rows * width * HIDDEN, bytes_accessed=11 * 1024 * 1024, transcendentals=0
        ),
    )(left, right)


PIECES = [(0, 128), (128, 128), (256, 128), (384, 128)]


def ffn_kernel(*refs):
    x_refs, dact_ref, w_ref, gua_ref, whole_ref, dx_refs = refs[:4], refs[4], refs[5], refs[6], refs[7], refs[8:12]
    x_held, dact_held, w_held, gua, dx, sems, out_sems = refs[12:]
    x_copies = []
    for number, (start, size) in enumerate(PIECES):
        copy = pltpu.make_async_copy(
            x_refs[number], x_held.at[pl.ds(start, size)], sems.at[12 + number]
        )
        copy.start()
        x_copies.append(copy)
    copies = []
    for number, (start, width) in enumerate(GROUPS):
        for part in range(3):
            if part < 2:
                columns = pl.ds(part * HIDDEN + start, width)
                copy = pltpu.make_async_copy(
                    w_ref.at[:, columns], w_held.at[:, columns], sems.at[3 * number + part]
                )
            else:
                columns = pl.ds(start, width)
                copy = pltpu.make_async_copy(
                    dact_ref.at[:, columns], dact_held.at[:, columns], sems.at[3 * number + part]
                )
            copy.start()
            copies.append(copy)
    for copy in x_copies:
        copy.wait()
    results = [pltpu.make_async_copy(x_held, whole_ref, out_sems.at[5])]
    results[0].start()
    x = x_held[...]
    for number, (start, width) in enumerate(GROUPS):
        for part in range(3):
            copies[3 * number + part].wait()
        gate = dot_nn(x, w_held[:, start : start + width])
        up = dot_nn(x, w_held[:, HIDDEN + start : HIDDEN + start + width])
        dact = dact_held[:, start : start + width]
        sig = jax.nn.sigmoid(gate)
        silu = gate * sig
        dgate = dact * up * (sig * (1.0 + gate * (1.0 - sig)))
        gua[:, start : start + width] = dgate.astype(BF16)
        gua[:, HIDDEN + start : HIDDEN + start + width] = (dact * silu).astype(BF16)
        gua[:, 2 * HIDDEN + start : 2 * HIDDEN + start + width] = (silu * up).astype(BF16)
    copy = pltpu.make_async_copy(gua, gua_ref, out_sems.at[4])
    copy.start()
    results.append(copy)
    dgu = gua[:, : 2 * HIDDEN]
    for number in range(4):
        columns = slice(512 * number, 512 * number + 512)
        dx[:, columns] = dot_nt(dgu, w_held[columns, : 2 * HIDDEN]).astype(BF16)
    for number, (start, size) in enumerate(PIECES):
        copy = pltpu.make_async_copy(dx.at[pl.ds(start, size)], dx_refs[number], out_sems.at[number])
        copy.start()
        results.append(copy)
    for copy in results:
        copy.wait()


def ffn(pieces, dact, weights):
    rows, width = dact.shape[0], weights.shape[0]
    anywhere = pl.BlockSpec(memory_space=pl.ANY)
    result = pl.pallas_call(
        ffn_kernel,
        out_shape=(
            jax.ShapeDtypeStruct((rows, 3 * HIDDEN), BF16),
            jax.ShapeDtypeStruct((rows, width), BF16),
            *(jax.ShapeDtypeStruct((size, width), BF16) for _, size in PIECES),
        ),
        in_specs=[anywhere] * 6,
        out_specs=(anywhere,) * 6,
        scratch_shapes=[
            pltpu.VMEM((rows, width), BF16),
            pltpu.VMEM((rows, HIDDEN), F32),
            pltpu.VMEM((width, 2 * HIDDEN), BF16),
            pltpu.VMEM((rows, 3 * HIDDEN), BF16),
            pltpu.VMEM((rows, width), BF16),
            pltpu.SemaphoreType.DMA((16,)),
            pltpu.SemaphoreType.DMA((6,)),
        ],
        compiler_params=pltpu.CompilerParams(vmem_limit_bytes=VMEM_LIMIT),
        cost_estimate=pl.CostEstimate(
            flops=8 * rows * width * HIDDEN,
            bytes_accessed=25 * 1024 * 1024,
            transcendentals=rows * HIDDEN,
        ),
    )(*pieces, dact, weights)
    return result[0], result[1], result[2:]


def weight_grads_kernel(core_ref, x_ref, x2_ref, dy_ref, dy2_ref, right_ref, right2_ref, out_ref):
    part = pl.program_id(0)

    @pl.when(part < 2)
    def _():
        total = dot_tn(x_ref[...], right_ref[...]) + dot_tn(x2_ref[...], right2_ref[...])
        out_ref[...] = total.astype(BF16)

    @pl.when(part == 2)
    def _():
        total = dot_tn(dy_ref[...], right_ref[...]) + dot_tn(dy2_ref[...], right2_ref[...])
        out_ref[...] = total.astype(BF16)


def weight_grads(core, x, x2, dy, dy2, right, right2):
    rows = x.shape[0]
    tile = 1024
    half = x2.shape[1]
    tiles = half // tile
    own = lambda j, i, c: (0, c[0] * tiles + i)
    other = lambda j, i, c: (0, i)
    side = lambda j, i, c: (0, j)
    grid = pltpu.PrefetchScalarGridSpec(
        num_scalar_prefetch=1,
        grid=(3, tiles),
        in_specs=[
            pl.BlockSpec((rows, tile), own),
            pl.BlockSpec((rows, tile), other),
            pl.BlockSpec((rows, tile), own),
            pl.BlockSpec((rows, tile), other),
            pl.BlockSpec((rows, HIDDEN), side),
            pl.BlockSpec((rows, HIDDEN), side),
        ],
        out_specs=pl.BlockSpec((tile, HIDDEN), lambda j, i, c: (i, j)),
    )
    return pl.pallas_call(
        weight_grads_kernel,
        grid_spec=grid,
        out_shape=jax.ShapeDtypeStruct((half, 3 * HIDDEN), BF16),
        compiler_params=pltpu.CompilerParams(vmem_limit_bytes=VMEM_LIMIT),
        cost_estimate=pl.CostEstimate(
            flops=2 * 3 * 2 * rows * half * HIDDEN, bytes_accessed=24 * 1024 * 1024, transcendentals=0
        ),
    )(core, x, x2, dy, dy2, right, right2)


def rows_times_kernel(left_ref, right_ref, *out_refs):
    result = dot_nt(left_ref[...], right_ref[...]).astype(BF16)
    for number, ref in enumerate(out_refs):
        ref[...] = result[128 * number : 128 * number + 128]


def rows_times(left, right, part):
    rows, depth = left.shape[0], HIDDEN
    width = right.shape[0]
    tile = 512
    return pl.pallas_call(
        rows_times_kernel,
        out_shape=(jax.ShapeDtypeStruct((128, width), BF16),) * 4,
        grid=(width // tile,),
        in_specs=[
            pl.BlockSpec((rows, depth), lambda i: (0, part)),
            pl.BlockSpec((tile, depth), lambda i: (i, part)),
        ],
        out_specs=(pl.BlockSpec((128, tile), lambda i: (0, i)),) * 4,
        compiler_params=pltpu.CompilerParams(vmem_limit_bytes=VMEM_LIMIT),
        cost_estimate=pl.CostEstimate(
            flops=2 * rows * depth * width,
            bytes_accessed=2 * (rows * depth + width * depth + rows * width),
            transcendentals=0,
        ),
    )(left, right)


def ring_rows(own, near, far):
    return jnp.concatenate([own, near[:128], far, near[128:]], 0)


def put_half(number, value, other_ref, own_ref):
    @pl.when(number < 2)
    def _():
        other_ref[...] = value

    @pl.when(number >= 2)
    def _():
        own_ref[...] = value


def tile_at(i, c):
    return lax.rem(i + 2 * (1 - c[0]), 4)


def half_specs(tile, columns):
    return (
        pl.BlockSpec((tile, columns), lambda i, c: (jnp.minimum(i, 1), 0)),
        pl.BlockSpec((tile, columns), lambda i, c: (jnp.maximum(i - 2, 0), 0)),
    )


def wide_grads_kernel(
    core_ref, x_ref, dh0, dh1, dh2, o0, o1, o2, dq0, dq1, dq2, other_ref, own_ref, o_held, dq_held
):
    number = pl.program_id(0)

    @pl.when(number == 0)
    def _():
        o_held[...] = ring_rows(o0[...], o1[...], o2[...])
        dq_held[...] = ring_rows(dq0[...], dq1[...], dq2[...])

    out = dot_tn(ring_rows(dh0[...], dh1[...], dh2[...]), o_held[...])
    query = dot_tn(x_ref[...], dq_held[...])
    put_half(number, jnp.concatenate([out, query], 1).astype(BF16), other_ref, own_ref)


def wide_grads(core, normed, dh, o, dq):
    rows, width = normed.shape
    tile = 512
    whole = lambda i, c: (0, 0)
    column = lambda i, c: (0, tile_at(i, c))
    small = [pl.BlockSpec((size, 512), whole) for size in (128, 256, 128)]
    grid = pltpu.PrefetchScalarGridSpec(
        num_scalar_prefetch=1,
        grid=(4,),
        in_specs=[pl.BlockSpec((rows, tile), column)]
        + [pl.BlockSpec((size, tile), column) for size in (128, 256, 128)]
        + small
        + small,
        out_specs=half_specs(tile, 1024),
        scratch_shapes=[pltpu.VMEM((rows, 512), BF16), pltpu.VMEM((rows, 512), BF16)],
    )
    return pl.pallas_call(
        wide_grads_kernel,
        grid_spec=grid,
        out_shape=(jax.ShapeDtypeStruct((width // 2, 1024), BF16),) * 2,
        compiler_params=pltpu.CompilerParams(vmem_limit_bytes=VMEM_LIMIT),
        cost_estimate=pl.CostEstimate(
            flops=2 * rows * width * 1024, bytes_accessed=10 * 1024 * 1024, transcendentals=0
        ),
    )(core, normed, *dh, *o, *dq)


def finish_kernel(
    core_ref,
    x_ref,
    w_ref,
    dq0_ref,
    dq1_ref,
    dq2_ref,
    own_ref,
    one_ref,
    two_ref,
    cos_ref,
    sin_ref,
    norm_ref,
    second_ref,
    other_grad_ref,
    own_grad_ref,
    dx_own,
    dx_ahead,
    dx_far,
    dx_behind,
    gain_ref,
    dqkv,
    sums,
):
    number = pl.program_id(0)

    @pl.when(number == 0)
    def _():
        dqkv[:, :512] = ring_rows(dq0_ref[...], dq1_ref[...], dq2_ref[...])
        dkv = own_ref[...] + one_ref[...].astype(F32) + two_ref[...].astype(F32)
        turned = turn(dkv, cos_ref[...], -sin_ref[...])
        dqkv[:, 512:] = jnp.where(lane_is_low(dkv.shape, 128), turned, dkv).astype(BF16)

    x = x_ref[...]
    put_half(number, dot_tn(x, dqkv[:, 512:]).astype(BF16), other_grad_ref, own_grad_ref)
    dx = dot_nt(dqkv[...], w_ref[:, 512:])
    for start, ref in ((0, dx_own), (128, dx_ahead), (256, dx_far), (384, dx_behind)):
        ref[...] = dx[start : start + 128].astype(BF16)
    columns = pl.ds(pl.multiple_of(tile_at(number, core_ref) * 512, 512), 512)
    sums[:, columns] = jnp.broadcast_to(
        jnp.sum(dx * x.astype(F32), 0, keepdims=True) / norm_ref[...], (8, 512)
    )

    @pl.when(number == 3)
    def _():
        gain_ref[:8] = gain_rows(to_blocks(sums[...])[:1])
        gain_ref[8:] = gain_rows(second_ref[:1])


def finish(core, normed, weights, dq, own, one, two, cosine, sine, gain, second):
    rows, width = normed.shape
    tile = 512
    whole = lambda i, c: (0, 0)
    column = lambda i, c: (0, tile_at(i, c))
    narrow = pl.BlockSpec((rows, 128), whole)
    grid = pltpu.PrefetchScalarGridSpec(
        num_scalar_prefetch=1,
        grid=(4,),
        in_specs=[
            pl.BlockSpec((rows, tile), column),
            pl.BlockSpec((tile, 1152), lambda i, c: (tile_at(i, c), 0)),
            pl.BlockSpec((128, 512), whole),
            pl.BlockSpec((256, 512), whole),
            pl.BlockSpec((128, 512), whole),
            narrow,
            narrow,
            narrow,
            narrow,
            narrow,
            pl.BlockSpec((1, tile), column),
            pl.BlockSpec((8, width), whole),
        ],
        out_specs=half_specs(tile, 128)
        + (pl.BlockSpec((128, tile), column),) * 4
        + (pl.BlockSpec((GAIN_ROWS, GAIN_COLUMNS), whole),),
        scratch_shapes=[pltpu.VMEM((rows, 640), BF16), pltpu.VMEM((8, width), F32)],
    )
    result = pl.pallas_call(
        finish_kernel,
        grid_spec=grid,
        out_shape=(jax.ShapeDtypeStruct((width // 2, 128), BF16),) * 2
        + (jax.ShapeDtypeStruct((128, width), BF16),) * 4
        + (jax.ShapeDtypeStruct((GAIN_ROWS, GAIN_COLUMNS), F32),),
        compiler_params=pltpu.CompilerParams(vmem_limit_bytes=VMEM_LIMIT),
        cost_estimate=pl.CostEstimate(
            flops=2 * rows * width * 768, bytes_accessed=10 * 1024 * 1024, transcendentals=0
        ),
    )(core, normed, weights, *dq, own, one, two, cosine, sine, gain, second)
    return result[0], result[1], result[2:6], result[6]


def per_device(
    tokens,
    segments,
    w_query,
    key_projection,
    value_projection,
    w_out,
    w_gate,
    w_up,
    w_down,
    norm_attn,
    norm_ffn,
    cotangent,
):
    place, core = lax.axis_index("head"), lax.axis_index("core")
    block = (lax.axis_index("y") * 4 + lax.axis_index("x")) * 2 + core
    place_array = place.astype(jnp.int32).reshape(1)
    core_array = core.astype(jnp.int32).reshape(1)
    keep = lax.optimization_barrier

    attention_weights = lax.all_gather(
        jnp.concatenate([w_out.T, w_query, key_projection, value_projection], 1),
        CORE_FIRST,
        axis=0,
        tiled=True,
    )
    ffn_weights = lax.all_gather(
        jnp.concatenate([w_gate, w_up, w_down.T], 1), CORE_FIRST, axis=0, tiled=True
    )

    x_rows, dy_rows, normed_rows, gain_one, gain_two = prepare(
        tokens[0],
        cotangent[0],
        jnp.broadcast_to(norm_attn[None], (16, 2048)),
        jnp.broadcast_to(norm_ffn[None], (16, 2048)),
    )
    gain_one, gain_two = gain_one[:1], gain_two[:1]
    normed_one = gather_head(normed_rows)
    normed_one, dy_rows_late = keep((normed_one, dy_rows))
    dy_pieces = gather_pieces(dy_rows_late)

    row = jnp.arange(512, dtype=jnp.int32)
    positions = block * 512 + ((row // 128 + place) % 4) * 128 + row % 128
    frequency = 10000.0 ** (-jnp.arange(32, dtype=F32) * 2.0 / HEAD_SIZE)
    angles = positions.astype(F32)[:, None] * frequency[None, :]
    cosine, sine = jnp.cos(angles), jnp.sin(angles)
    cosine = jnp.concatenate([cosine] * 4, 1)
    sine = jnp.concatenate([-sine, sine, -sine, sine], 1)

    kv_own = project(project_kv_kernel, normed_one, attention_weights, cosine, sine, 1024, 128, 128)
    normed_late, kv_own = keep((normed_one, kv_own))
    kv = (from_block(kv_own, 2), from_block(kv_own, 1), kv_own)
    queries = project(project_q_kernel, normed_late, attention_weights, cosine, sine, 512, 512, 256)

    flat = segments.reshape(-1)
    padded = jnp.concatenate([jnp.full((1024,), -1, jnp.int32), flat])
    own = lax.dynamic_slice_in_dim(flat, block * 512, 512, 0)
    window = lax.dynamic_slice_in_dim(padded, block * 512, 1536, 0)
    start = jnp.sum((window[None, :] < own[:, None]).astype(jnp.int32), 1)
    low = jnp.maximum(start, row + 1).reshape(1, 512)

    kk, vv, kvt = set_up(place_array, kv)
    seen = place_array, queries, kk, kvt, low, attention_weights
    o_far, lse_far, part_far = attend(2, 1, 1, *seen)
    part_far, dy_pieces = keep((part_far, dy_pieces))
    dy = jnp.concatenate([dy_rows, *dy_pieces], 0)
    o_near, lse_near, part_near = attend(1, 2, 2, *seen)
    o_own, lse_own, part_own = attend(0, 1, 1, *seen)
    dy_other = swap_half(dy, core)
    attention_sum = scatter_pieces(part_own, part_near[:128], part_far, part_near[128:])
    h1, normed_rows_two = join(x_rows, gain_two, attention_sum)
    ahead, far, behind = gather_pieces(normed_rows_two)
    dact = columns_times(dy, ffn_weights, 2)
    dact, dy_other = keep((dact, dy_other))

    gua, normed_two, dnormed_two = ffn((normed_rows_two, ahead, far, behind), dact, ffn_weights)
    dnormed_two = scatter_pieces(*dnormed_two)
    gua_other = shift(gua, "core", 1)
    normed_two_other = swap_half(normed_two, core)
    out_pieces = rows_times(gua, ffn_weights, 2)
    gua_other, normed_two_other, out_pieces = keep((gua_other, normed_two_other, out_pieces))
    held = weight_grads(core_array, normed_two, normed_two_other, dy, dy_other, gua, gua_other)
    held, dnormed_two = keep((held, dnormed_two))
    grads = lax.psum_scatter(held, ("y", "x"), scatter_dimension=0, tiled=True)

    dh1, dh1_low, grad_gain_two = join_back(h1, dy_rows, gain_two, dnormed_two)
    back = kk, vv, kvt, low, cosine, sine
    dq_own, dk, dv = attend_back(0, 1, 1, place_array, queries, dh1_low, attention_weights, lse_own, *back, ())
    ahead, behind = shift(dh1_low, "head", -1), shift(dh1_low, "head", 1)
    ahead, behind, dk, dv, dh1_late, out_pieces = keep((ahead, behind, dk, dv, dh1_low, out_pieces))
    far = shift(dh1_late, "head", 2)
    near = jnp.concatenate([ahead, behind], 0)
    dq_near, dk, dv = attend_back(
        1, 2, 2, place_array, queries, near, attention_weights, lse_near, *back, (dk, dv)
    )
    far, dk, dv, out_pieces = keep((far, dk, dv, out_pieces))
    out_pieces = scatter_pieces(*out_pieces)
    dq_far, dkv_own, dkv_earlier = attend_back(
        2, 1, 1, place_array, queries, far, attention_weights, lse_far, *back, (dk, dv)
    )
    dq = dq_own, dq_near, dq_far
    dkv_one = from_block(dkv_earlier[1], -1)
    dkv_two = from_block(dkv_earlier[0], -2)
    wide_other, wide_own = wide_grads(
        core_array, normed_one, (dh1_low, near, far), (o_own, o_near, o_far), dq
    )
    dkv_one, dkv_two, wide_other, out_pieces = keep((dkv_one, dkv_two, wide_other, out_pieces))
    wide_other = shift(wide_other, "core", 1)

    narrow_other, narrow_own, dnormed_one, gains = finish(
        core_array,
        normed_one,
        attention_weights,
        dq,
        dkv_own,
        dkv_one,
        dkv_two,
        cosine,
        sine,
        gain_one,
        grad_gain_two,
    )
    at = jnp.stack([lax.axis_index("x"), lax.axis_index("y")]).astype(jnp.int32)
    pieces, out_sums = first_pieces(
        at,
        wide_own,
        wide_other,
        narrow_own,
        shift(narrow_other, "core", 1),
        gains,
        shift(gains, "core", 1),
    )
    pieces, out_sums, dnormed_one = keep((pieces, out_sums, dnormed_one))
    rows = [(x_rows.shape, BF16)]
    (output,) = small_call(output_kernel, rows, h1, *out_pieces)
    grads = (
        grads[:, :HIDDEN].astype(F32),
        grads[:, HIDDEN : 2 * HIDDEN].astype(F32),
        grads[:, 2 * HIDDEN :].T.astype(F32),
    )
    pieces, out_sums, output, grads = keep(
        (exchange(pieces, "x"), exchange(out_sums, "y"), output, grads)
    )
    pieces, out_sums = second_pieces(at, pieces, out_sums)
    dnormed_one = scatter_pieces(*dnormed_one)
    (grad_inputs,) = small_call(input_grad_kernel, rows, dh1, x_rows, gain_one, *dnormed_one)
    pieces, out_sums, grad_inputs = keep((exchange(pieces, "y"), exchange(out_sums, "x"), grad_inputs))
    columns = (512, 64), (64, 512), (64, 64), (64, 64), (GAIN_ROWS, GAIN_COLUMNS)
    grad_out, grad_query, grad_key, grad_value, gains = small_call(
        attention_grads_kernel, [(shape, F32) for shape in columns], *pieces, *out_sums
    )
    grad_gain_one, grad_gain_two = small_call(
        gains_kernel, [((1, 2048), F32)] * 2, *exchange([gains] * 4, "head")
    )

    return (
        output[None],
        grad_inputs[None],
        grad_query,
        grad_key,
        grad_value,
        grad_out,
        *grads,
        grad_gain_one.reshape(2048),
        grad_gain_two.reshape(2048),
    )


def solution(mesh):
    grid = Mesh(mesh.devices.reshape(4, 4, 4, 2), ("head", "y", "x", "core"))
    rows, up, down = P(BLK, "head", None), P(BLK, "head"), P("head", BLK)
    return jax.shard_map(
        per_device,
        mesh=grid,
        in_specs=(rows, P(), up, up, up, down, up, up, down, P(), P(), rows),
        out_specs=(rows, rows, up, up, up, down, up, up, down, P(), P()),
        check_vma=False,
    )
```

```python
import functools

import jax
import jax.numpy as jnp
from jax import lax
from jax.experimental import pallas as pl
from jax.experimental.pallas import tpu as pltpu
from jax.sharding import Mesh
from jax.sharding import PartitionSpec as P

HEAD_SIZE = 64
WINDOW = 1024
HIDDEN = 1408
EPSILON = 1e-05
BF16 = jnp.bfloat16
F32 = jnp.float32
BLK = ("y", "x", "core")
CORE_FIRST = ("core", "y", "x")
VMEM_LIMIT = 56 * 1024 * 1024


def dot_nn(a, b):
    return jnp.dot(a, b, preferred_element_type=F32)


def dot_nt(a, b):
    return lax.dot_general(a, b, (((1,), (1,)), ((), ())), preferred_element_type=F32)


def dot_tn(a, b):
    return lax.dot_general(a, b, (((0,), (0,)), ((), ())), preferred_element_type=F32)


def shift(value, axis, distance):
    size = lax.axis_size(axis)
    return lax.ppermute(value, axis, [(i, (i + distance) % size) for i in range(size)])


def add_low(a, b):
    return (a.astype(F32) + b.astype(F32)).astype(BF16)


def gather_pieces(rows):
    return shift(rows, "head", -1), shift(rows, "head", 2), shift(rows, "head", 1)


def gather_head(rows):
    return jnp.concatenate([rows, *gather_pieces(rows)], 0)


def scatter_pieces(own, ahead, far, behind):
    return own, shift(ahead, "head", 1), shift(behind, "head", -1), shift(far, "head", 2)


def swap_half(value, core):
    width = value.shape[1] // 2
    return shift(lax.dynamic_slice_in_dim(value, (1 - core) * width, width, 1), "core", 1)


def gather_axis(value, axis):
    return jnp.concatenate([value, shift(value, axis, -1), shift(value, axis, 2), shift(value, axis, 1)], 0)


def exchange(pieces, axis):
    return pieces[0], shift(pieces[1], axis, 1), shift(pieces[2], axis, 2), shift(pieces[3], axis, -1)


def from_block(value, distance):
    route = [(i, i + distance) for i in range(32) if 0 <= i + distance < 32]
    return lax.ppermute(value, BLK, route)


def scale_of(values):
    return lax.rsqrt(jnp.mean(values * values, -1, keepdims=True) + EPSILON)


def lane_is_low(shape, period):
    return lax.broadcasted_iota(jnp.int32, shape, len(shape) - 1) % period < period // 2


def turn(values, cosine, sine):
    swapped = jnp.where(
        lane_is_low(values.shape, 64), pltpu.roll(values, 96, 1), pltpu.roll(values, 32, 1)
    )
    return values * cosine + swapped * sine


def core_major_tiles(tiles):
    low = lane_is_low(tiles[0].shape, 128)
    rolled = [pltpu.roll(tile, 64, 1) for tile in tiles]
    first = [jnp.where(low, tiles[2 * k], rolled[2 * k + 1]) for k in range(8)]
    second = [jnp.where(low, rolled[2 * k], tiles[2 * k + 1]) for k in range(8)]
    return first + second


def block_major_tiles(tiles):
    low = lane_is_low(tiles[0].shape, 128)
    rolled = [pltpu.roll(tile, 64, 1) for tile in tiles]
    result = []
    for k in range(8):
        result.append(jnp.where(low, tiles[k], rolled[8 + k]))
        result.append(jnp.where(low, rolled[k], tiles[8 + k]))
    return result


def in_tiles(value):
    return [value[:, 128 * k : 128 * k + 128] for k in range(16)]


def prepare_kernel(x_ref, dy_ref, gain_one_ref, gain_two_ref, x_out, dy_out, normed_out, one_out, two_out):
    def convert(ref):
        return jnp.concatenate(core_major_tiles(in_tiles(ref[...].astype(F32))), 1)

    x, gain = convert(x_ref), convert(gain_one_ref)
    one_out[...], two_out[...] = gain, convert(gain_two_ref)
    x_out[...] = x
    dy_out[...] = convert(dy_ref).astype(BF16)
    normed_out[...] = (x * scale_of(x) * gain[:1]).astype(BF16)


def prepare(x, dy, gain_one, gain_two):
    rows, width = x.shape
    return pl.pallas_call(
        prepare_kernel,
        out_shape=(
            jax.ShapeDtypeStruct((rows, width), F32),
            jax.ShapeDtypeStruct((rows, width), BF16),
            jax.ShapeDtypeStruct((rows, width), BF16),
            jax.ShapeDtypeStruct((16, width), F32),
            jax.ShapeDtypeStruct((16, width), F32),
        ),
        compiler_params=pltpu.CompilerParams(vmem_limit_bytes=VMEM_LIMIT),
        cost_estimate=pl.CostEstimate(
            flops=10 * rows * width, bytes_accessed=10 * rows * width, transcendentals=rows
        ),
    )(x, dy, gain_one, gain_two)


def to_blocks(value):
    return jnp.concatenate(block_major_tiles(in_tiles(value)), 1)


def small_call(kernel, out_shape, *operands):
    return pl.pallas_call(
        kernel,
        out_shape=tuple(jax.ShapeDtypeStruct(shape, dtype) for shape, dtype in out_shape),
        compiler_params=pltpu.CompilerParams(vmem_limit_bytes=VMEM_LIMIT),
        cost_estimate=pl.CostEstimate(
            flops=sum(x.size for x in operands),
            bytes_accessed=2 * sum(x.size * x.dtype.itemsize for x in operands),
            transcendentals=0,
        ),
    )(*operands)


def total_of(refs):
    values = [ref[...].astype(F32) for ref in refs]
    while len(values) > 1:
        values = [values[0] + values[1]] + values[2:]
    return values[0]


def join_kernel(x_ref, gain_ref, a_ref, b_ref, c_ref, d_ref, h_out, normed_out):
    h = x_ref[...] + total_of((a_ref, b_ref, c_ref, d_ref))
    h_out[...] = h
    normed_out[...] = (h * scale_of(h) * gain_ref[...]).astype(BF16)


def join(x, gain, pieces):
    return small_call(join_kernel, ((x.shape, F32), (x.shape, BF16)), x, gain, *pieces)


def norm_backward(values, gain, grad):
    scale = scale_of(values)
    weighted = grad * gain
    inner = jnp.mean(weighted * values, -1, keepdims=True)
    return scale * weighted - values * (scale * scale * scale * inner), scale


def join_back_kernel(h_ref, dy_ref, gain_ref, a_ref, b_ref, c_ref, d_ref, dh_out, low_out, grad_out):
    h, grad = h_ref[...], total_of((a_ref, b_ref, c_ref, d_ref))
    back, scale = norm_backward(h, gain_ref[...], grad)
    dh = dy_ref[...].astype(F32) + back
    dh_out[...] = dh
    low_out[...] = dh.astype(BF16)
    grad_out[...] = to_blocks(jnp.broadcast_to(jnp.sum(grad * h * scale, 0, keepdims=True), (8, h.shape[1])))


def join_back(h, dy, gain, pieces):
    shapes = (h.shape, F32), (h.shape, BF16), ((8, h.shape[1]), F32)
    return small_call(join_back_kernel, shapes, h, dy, gain, *pieces)


def output_kernel(h_ref, a_ref, b_ref, c_ref, d_ref, out_ref):
    out_ref[...] = to_blocks(h_ref[...] + total_of((a_ref, b_ref, c_ref, d_ref))).astype(BF16)


def input_grad_kernel(dh_ref, x_ref, gain_ref, a_ref, b_ref, c_ref, d_ref, out_ref):
    back, _ = norm_backward(x_ref[...], gain_ref[...], total_of((a_ref, b_ref, c_ref, d_ref)))
    out_ref[...] = to_blocks(dh_ref[...] + back).astype(BF16)


GAIN_ROWS, GAIN_COLUMNS = 16, 256


def gain_rows(vector):
    return jnp.concatenate([vector[:, 256 * k : 256 * k + 256] for k in range(8)], 0)


def put_piece(ref, rows, gains):
    count = rows.shape[0]
    ref[:count] = rows
    ref[count:, GAIN_COLUMNS:] = jnp.zeros((GAIN_ROWS, ref.shape[1] - GAIN_COLUMNS), BF16)
    ref[count:, :GAIN_COLUMNS] = gains.astype(BF16)


def first_pieces_kernel(
    at_ref, q_ref, q2_ref, kv_ref, kv2_ref, o_ref, o2_ref, gain_ref, gain2_ref, *out_refs
):
    query = add_low(q_ref[...], q2_ref[...]).reshape(256, 512)
    narrow = add_low(kv_ref[...], kv2_ref[...]).reshape(256, 128)
    rows = jnp.concatenate([query, narrow], 1)
    out_rows = add_low(o_ref[...], o2_ref[...]).reshape(256, 512)
    gains = gain_ref[...] + gain2_ref[...]
    for number in range(4):

        @pl.when(pl.program_id(0) == number)
        def _():
            put_piece(out_refs[number], rows, gains)
            out_refs[4 + number][...] = out_rows


def first_pieces(at, wide, wide2, narrow, narrow2, gains, gains2):
    pick_x = lambda column: lambda d, s: (0, lax.rem(s[0] + d, 4), 0, column)
    pick_y = lambda d, s: (lax.rem(s[1] + d, 4), 0, 0, 0)
    whole = lambda d, s: (0, 0)
    shaped = lambda value: value.reshape(4, 4, 64, value.shape[1])
    shapes = [(256 + GAIN_ROWS, 640)] * 4 + [(256, 512)] * 4
    grid = pltpu.PrefetchScalarGridSpec(
        num_scalar_prefetch=1,
        grid=(4,),
        in_specs=[pl.BlockSpec((4, 1, 64, 512), pick_x(1))] * 2
        + [pl.BlockSpec((4, 1, 64, 128), pick_x(0))] * 2
        + [pl.BlockSpec((1, 4, 64, 512), pick_y)] * 2
        + [pl.BlockSpec((GAIN_ROWS, GAIN_COLUMNS), whole)] * 2,
        out_specs=tuple(pl.BlockSpec(shape, whole) for shape in shapes),
    )
    wide, wide2 = shaped(wide), shaped(wide2)
    result = pl.pallas_call(
        first_pieces_kernel,
        grid_spec=grid,
        out_shape=tuple(jax.ShapeDtypeStruct(shape, BF16) for shape in shapes),
        compiler_params=pltpu.CompilerParams(vmem_limit_bytes=VMEM_LIMIT),
        cost_estimate=pl.CostEstimate(
            flops=2 * 1024 * 1152, bytes_accessed=6 * 1024 * 1152, transcendentals=0
        ),
    )(at, wide, wide2, shaped(narrow), shaped(narrow2), wide, wide2, gains, gains2)
    return result[:4], result[4:]


def second_pieces_kernel(at_ref, *refs):
    qkv, out, (held, out_held) = refs[:4], refs[4:8], refs[16:]
    held[...] = total_of(qkv)
    out_held[...] = total_of(out).astype(BF16)
    for number in range(4):
        y = pl.multiple_of(lax.rem(at_ref[1] + number, 4) * 64, 64)
        put_piece(refs[8 + number], held[pl.ds(y, 64), :].astype(BF16), held[256:, :GAIN_COLUMNS])
        x = pl.multiple_of(lax.rem(at_ref[0] + number, 4) * 64, 64)
        refs[12 + number][...] = out_held[pl.ds(x, 64), :]


def second_pieces(at, qkv, out):
    vmem = pl.BlockSpec(memory_space=pltpu.VMEM)
    shapes = [(64 + GAIN_ROWS, 640)] * 4 + [(64, 512)] * 4
    result = pl.pallas_call(
        second_pieces_kernel,
        out_shape=tuple(jax.ShapeDtypeStruct(shape, BF16) for shape in shapes),
        in_specs=[pl.BlockSpec(memory_space=pltpu.SMEM)] + [vmem] * 8,
        out_specs=(vmem,) * 8,
        scratch_shapes=[pltpu.VMEM((256 + GAIN_ROWS, 640), F32), pltpu.VMEM((256, 512), BF16)],
        compiler_params=pltpu.CompilerParams(vmem_limit_bytes=VMEM_LIMIT),
        cost_estimate=pl.CostEstimate(
            flops=4 * 272 * 1152, bytes_accessed=10 * 272 * 1152, transcendentals=0
        ),
    )(at, *qkv, *out)
    return result[:4], result[4:]


def attention_grads_kernel(*refs):
    out_ref, q_ref, k_ref, v_ref, one_ref, two_ref = refs[8:]
    total = total_of(refs[:4])
    out_ref[...] = total_of(refs[4:8]).T
    q_ref[...] = total[:64, :512]
    k_ref[...] = total[:64, 512:576]
    v_ref[...] = total[:64, 576:]
    gains = total[64:, :GAIN_COLUMNS]
    one_ref[...] = jnp.concatenate([gains[k : k + 1] for k in range(8)], 1)
    two_ref[...] = jnp.concatenate([gains[k : k + 1] for k in range(8, 16)], 1)


def total_kernel(a_ref, b_ref, c_ref, d_ref, out_ref):
    out_ref[...] = total_of((a_ref, b_ref, c_ref, d_ref))


def put_in_order(at_ref, own_ref, other_ref, columns, to_ref, sems):
    x, y, core = at_ref[0], at_ref[1], at_ref[2]
    copies = []
    for number in range(32):
        ref = (own_ref, other_ref)[number // 16]
        to_x, to_y = lax.rem(x + number % 4, 4), lax.rem(y + number // 4 % 4, 4)
        to_core = core if number < 16 else 1 - core
        row = pl.multiple_of(((to_core * 4 + to_y) * 4 + to_x) * 64, 64)
        copy = pltpu.make_async_copy(
            ref.at[pl.ds(number % 16 * 64, 64), columns], to_ref.at[pl.ds(row, 64)], sems.at[number]
        )
        copy.start()
        copies.append(copy)
    return copies


def project_kv_kernel(at_ref, x_ref, own_ref, other_ref, cos_ref, sin_ref, kv_ref, held, sems):
    for copy in put_in_order(at_ref, own_ref, other_ref, pl.ds(512, 128), held, sems):
        copy.wait()
    flat = dot_nn(x_ref[...], held[...])
    turned = turn(flat, cos_ref[...], sin_ref[...])
    kv_ref[...] = jnp.where(lane_is_low(flat.shape, 128), turned, flat).astype(BF16)


def project_q_kernel(at_ref, x_ref, own_ref, other_ref, cos_ref, sin_ref, q_ref, w_ref, held, sems, sem):
    for copy in put_in_order(at_ref, own_ref, other_ref, pl.ds(0, 640), held, sems):
        copy.wait()
    whole = pltpu.make_async_copy(held, w_ref, sem)
    whole.start()
    cosine, sine, x = cos_ref[...], sin_ref[...], x_ref[...]
    for start in (0, 256):
        wide = dot_nn(x, held[:, start : start + 256])
        for part in (0, 128):
            turned = turn(wide[:, part : part + 128], cosine, sine)
            q_ref[:, start + part : start + part + 128] = (turned * HEAD_SIZE**-0.5).astype(BF16)
    whole.wait()


def project(kernel, at, normed, weights, cosine, sine, columns, held_columns, hand_out):
    rows, width = normed.shape
    vmem, anywhere = pl.BlockSpec(memory_space=pltpu.VMEM), pl.BlockSpec(memory_space=pl.ANY)
    out_shape = [jax.ShapeDtypeStruct((rows, columns), BF16)]
    out_specs = [vmem]
    scratch = [pltpu.VMEM((width, held_columns), BF16), pltpu.SemaphoreType.DMA((32,))]
    if hand_out:
        out_shape.append(jax.ShapeDtypeStruct((width, held_columns), BF16))
        out_specs.append(anywhere)
        scratch.append(pltpu.SemaphoreType.DMA)
    return pl.pallas_call(
        kernel,
        out_shape=tuple(out_shape),
        in_specs=[pl.BlockSpec(memory_space=pltpu.SMEM), vmem, anywhere, anywhere, vmem, vmem],
        out_specs=tuple(out_specs),
        scratch_shapes=scratch,
        compiler_params=pltpu.CompilerParams(vmem_limit_bytes=VMEM_LIMIT),
        cost_estimate=pl.CostEstimate(
            flops=2 * rows * width * columns,
            bytes_accessed=2 * (rows * width + width * columns + rows * columns),
            transcendentals=0,
        ),
    )(at, normed, *weights, cosine, sine)


KEYS = 1152
PAIRS = 4


def set_up_kernel(place_ref, kv0_ref, kv1_ref, kv2_ref, kk_ref, vv_ref, kvt_ref):
    place = place_ref[0]
    low = lane_is_low((128, 128), 128)
    for block, ref in enumerate((kv0_ref, kv1_ref, kv2_ref)):
        for group in range(4):
            at = pl.multiple_of(lax.rem(group - place + 4, 4) * 128, 128)
            piece = ref[pl.ds(at, 128), :].astype(F32)
            rolled = pltpu.roll(piece, 64, 1)
            to = block * 512 + group * 128
            kk_ref[to : to + 128, :] = jnp.where(low, piece, rolled).astype(BF16)
            vv_ref[to : to + 128, :] = jnp.where(low, rolled, piece).astype(BF16)
            kvt_ref[:, to : to + 128] = piece.T.astype(BF16)


def set_up(place, kv):
    vmem = pl.BlockSpec(memory_space=pltpu.VMEM)
    return pl.pallas_call(
        set_up_kernel,
        out_shape=(
            jax.ShapeDtypeStruct((1536, 128), BF16),
            jax.ShapeDtypeStruct((1536, 128), BF16),
            jax.ShapeDtypeStruct((128, 1536), BF16),
        ),
        in_specs=[pl.BlockSpec(memory_space=pltpu.SMEM), vmem, vmem, vmem],
        out_specs=(vmem, vmem, vmem),
        compiler_params=pltpu.CompilerParams(vmem_limit_bytes=VMEM_LIMIT),
        cost_estimate=pl.CostEstimate(flops=1536 * 128 * 8, bytes_accessed=2 * 1024 * 1024, transcendentals=0),
    )(place, *kv)


def both_heads(pair):
    low = lane_is_low(pair.shape, 128)
    nothing = jnp.zeros_like(pair)
    return jnp.concatenate([jnp.where(low, pair, nothing), jnp.where(low, nothing, pair)], 0)


def side_by_side(transposed):
    return jnp.concatenate([transposed[:, :128], transposed[:, 128:]], 0).T


def mask_of(at, low_ref):
    key = lax.broadcasted_iota(jnp.int32, (KEYS, 128), 0)
    query = lax.broadcasted_iota(jnp.int32, (KEYS, 128), 1)
    seen = (key >= low_ref[:, pl.ds(at, 128)] - at) & (key <= query + WINDOW)
    bias = jnp.where(seen, 0.0, -jnp.inf)
    return jnp.concatenate([bias, bias], 1)


def attend_kernel(
    first, step, place_ref, q_ref, kk_ref, kvt_ref, low_ref, w_ref, o_ref, lse_ref, part_ref, bias, held, w_held, sem
):
    group = lax.rem(place_ref[0] + first + step * pl.program_id(0), 4)
    at = pl.multiple_of(group * 128, 128)

    load = pltpu.make_async_copy(w_ref.at[:, pl.ds(HIDDEN, 512)], w_held, sem)

    @pl.when((pl.program_id(0) == 0) & (pl.program_id(1) == 0))
    def _():
        load.start()

    @pl.when(pl.program_id(1) == 0)
    def _():
        bias[...] = mask_of(at, low_ref)

    keys = pl.ds(at, KEYS)
    for number in range(PAIRS):
        columns = slice(128 * number, 128 * number + 128)
        scores = dot_nt(kk_ref[keys, :], both_heads(q_ref[:, columns])) + bias[...]
        top = jnp.max(scores, 0, keepdims=True)
        weights = jnp.exp(scores - top)
        total = jnp.sum(weights, 0, keepdims=True)
        result = dot_nn(kvt_ref[64:128, keys], weights.astype(BF16)) / total
        lse_ref[0, number] = top + jnp.log(total)
        result = side_by_side(result).astype(BF16)
        o_ref[:, columns] = result
        held[PAIRS * pl.program_id(1) + number] = result

    @pl.when(pl.program_id(1) == 4 // PAIRS - 1)
    def _():
        @pl.when(pl.program_id(0) == 0)
        def _():
            load.wait()

        rows = jnp.concatenate([held[k] for k in range(4)], 1)
        part_ref[...] = dot_nt(rows, w_held[...]).astype(BF16)


def attend(first, step, count, place, queries, kk, kvt, low, attention_weights):
    whole = lambda g, p, s: (0, 0)
    width = 128 * PAIRS
    grid = pltpu.PrefetchScalarGridSpec(
        num_scalar_prefetch=1,
        grid=(count, 4 // PAIRS),
        in_specs=[
            pl.BlockSpec((128, width), lambda g, p, s: (first + step * g, p)),
            pl.BlockSpec((1536, 128), whole),
            pl.BlockSpec((128, 1536), whole),
            pl.BlockSpec((1, 512), whole),
            pl.BlockSpec(memory_space=pl.ANY),
        ],
        out_specs=(
            pl.BlockSpec((128, width), lambda g, p, s: (g, p)),
            pl.BlockSpec((1, PAIRS, 1, 256), lambda g, p, s: (g, p, 0, 0)),
            pl.BlockSpec((128, 2048), lambda g, p, s: (g, 0)),
        ),
        scratch_shapes=[
            pltpu.VMEM((KEYS, 256), F32),
            pltpu.VMEM((4, 128, 128), BF16),
            pltpu.VMEM((2048, 512), BF16),
            pltpu.SemaphoreType.DMA,
        ],
    )
    return pl.pallas_call(
        functools.partial(attend_kernel, first, step),
        grid_spec=grid,
        out_shape=(
            jax.ShapeDtypeStruct((128 * count, 512), BF16),
            jax.ShapeDtypeStruct((count, 4, 1, 256), F32),
            jax.ShapeDtypeStruct((128 * count, 2048), BF16),
        ),
        compiler_params=pltpu.CompilerParams(vmem_limit_bytes=VMEM_LIMIT),
        cost_estimate=pl.CostEstimate(
            flops=count * 4 * KEYS * 256 * 256 * 2,
            bytes_accessed=3 * 1024 * 1024,
            transcendentals=count * 4 * KEYS * 256,
        ),
    )(place, queries, kk, kvt, low, attention_weights)


def attend_back_kernel(first, step, last, *refs):
    place_ref, q_ref, dh_ref, w_ref, lse_ref, kk_ref, vv_ref, kvt_ref, low_ref, cos_ref, sin_ref = refs[:11]
    if first == 0:
        dk_in, dv_in, refs = None, None, refs[11:]
    else:
        dk_in, dv_in, refs = refs[11], refs[12], refs[13:]
    dq_ref, one_out, two_out, bias, do_held, dk, dv, w_held, sem = refs
    number, pair = pl.program_id(0), pl.program_id(1)
    place = place_ref[0]
    at = pl.multiple_of(lax.rem(place + first + step * number, 4) * 128, 128)

    load = pltpu.make_async_copy(w_ref.at[:, pl.ds(HIDDEN, 512)], w_held, sem)

    @pl.when((number == 0) & (pair == 0))
    def _():
        load.start()
        dk[...] = jnp.zeros_like(dk) if dk_in is None else dk_in[...]
        dv[...] = jnp.zeros_like(dv) if dv_in is None else dv_in[...]

    @pl.when(pair == 0)
    def _():
        bias[...] = mask_of(at, low_ref)

        @pl.when(number == 0)
        def _():
            load.wait()

        do_rows = dot_nn(dh_ref[...], w_held[...]).astype(BF16)
        for k in range(4):
            do_held[k] = do_rows[:, 128 * k : 128 * k + 128]

    keys = pl.ds(at, KEYS)
    queries, grads, all_weights, all_grad_scores = [], [], [], []
    for k in range(PAIRS):
        columns = slice(128 * k, 128 * k + 128)
        query, grad = both_heads(q_ref[:, columns]), both_heads(do_held[PAIRS * pair + k])
        scores = dot_nt(kk_ref[keys, :], query) + bias[...]
        weights = jnp.exp(scores - lse_ref[0, k])
        grad_weights = dot_nt(vv_ref[keys, :], grad)
        inner = jnp.sum(weights * grad_weights, 0, keepdims=True)
        grad_scores = (weights * (grad_weights - inner)).astype(BF16)
        grad_query = side_by_side(dot_nn(kvt_ref[0:64, keys], grad_scores)) * HEAD_SIZE**-0.5
        dq_ref[:, columns] = turn(grad_query, cos_ref[...], -sin_ref[...]).astype(BF16)
        queries.append(query)
        grads.append(grad)
        all_weights.append(weights.astype(BF16))
        all_grad_scores.append(grad_scores)
    join = lambda values, axis: values[0] if PAIRS == 1 else jnp.concatenate(values, axis)
    dv[keys, :] += dot_nn(join(all_weights, 1), join(grads, 0))
    dk[keys, :] += dot_nn(join(all_grad_scores, 1), join(queries, 0))

    @pl.when((number == pl.num_programs(0) - 1) & (pair == 4 // PAIRS - 1))
    def _():
        if not last:
            one_out[...], two_out[...] = dk[...], dv[...]
            return
        half = lane_is_low((128, 128), 128)
        for block in range(3):
            for group in range(4):
                to = pl.multiple_of(lax.rem(group - place + 4, 4) * 128, 128)
                frm = slice(block * 512 + group * 128, block * 512 + group * 128 + 128)
                key, value = dk[frm, :], dv[frm, :]
                key = key + pltpu.roll(key, 64, 1)
                value = value + pltpu.roll(value, 64, 1)
                both = jnp.where(half, key, value)
                if block == 2:
                    one_out[pl.ds(to, 128), :] = both
                else:
                    two_out[block, pl.ds(to, 128), :] = both.astype(BF16)


def attend_back(first, step, count, place, queries, dh, attention_weights, lse, kk, vv, kvt, low, cosine, sine, held):
    last = first == 2
    whole = lambda g, p, s: (0, 0)
    specs = [
        pl.BlockSpec((128, 128 * PAIRS), lambda g, p, s: (first + step * g, p)),
        pl.BlockSpec((128, 2048), lambda g, p, s: (g, 0)),
        pl.BlockSpec(memory_space=pl.ANY),
        pl.BlockSpec((1, PAIRS, 1, 256), lambda g, p, s: (g, p, 0, 0)),
        pl.BlockSpec((1536, 128), whole),
        pl.BlockSpec((1536, 128), whole),
        pl.BlockSpec((128, 1536), whole),
        pl.BlockSpec((1, 512), whole),
        pl.BlockSpec((128, 128), lambda g, p, s: (first + step * g, 0)),
        pl.BlockSpec((128, 128), lambda g, p, s: (first + step * g, 0)),
    ] + [pl.BlockSpec((1536, 128), whole)] * len(held)
    if last:
        out_specs = (pl.BlockSpec((512, 128), whole), pl.BlockSpec((2, 512, 128), lambda g, p, s: (0, 0, 0)))
        out_shape = (jax.ShapeDtypeStruct((512, 128), F32), jax.ShapeDtypeStruct((2, 512, 128), BF16))
    else:
        out_specs = (pl.BlockSpec((1536, 128), whole),) * 2
        out_shape = (jax.ShapeDtypeStruct((1536, 128), F32),) * 2
    grid = pltpu.PrefetchScalarGridSpec(
        num_scalar_prefetch=1,
        grid=(count, 4 // PAIRS),
        in_specs=specs,
        out_specs=(pl.BlockSpec((128, 128 * PAIRS), lambda g, p, s: (g, p)),) + out_specs,
        scratch_shapes=[
            pltpu.VMEM((KEYS, 256), F32),
            pltpu.VMEM((4, 128, 128), BF16),
            pltpu.VMEM((1536, 128), F32),
            pltpu.VMEM((1536, 128), F32),
            pltpu.VMEM((2048, 512), BF16),
            pltpu.SemaphoreType.DMA,
        ],
    )
    return pl.pallas_call(
        functools.partial(attend_back_kernel, first, step, last),
        grid_spec=grid,
        out_shape=(jax.ShapeDtypeStruct((128 * count, 512), BF16),) + out_shape,
        compiler_params=pltpu.CompilerParams(vmem_limit_bytes=VMEM_LIMIT),
        cost_estimate=pl.CostEstimate(
            flops=count * 4 * KEYS * 256 * 640 * 2,
            bytes_accessed=6 * 1024 * 1024,
            transcendentals=count * 4 * KEYS * 256,
        ),
    )(place, queries, dh, attention_weights, lse, kk, vv, kvt, low, cosine, sine, *held)


GROUPS = [(0, 128), (128, 256), (384, 512), (896, 512)]


def columns_times_kernel(left_ref, right_ref, out_ref):
    out_ref[...] = dot_nn(left_ref[...], right_ref[...])


def columns_times(left, right, part):
    rows, width = left.shape
    return pl.pallas_call(
        columns_times_kernel,
        out_shape=jax.ShapeDtypeStruct((rows, HIDDEN), F32),
        grid=(1,),
        in_specs=[
            pl.BlockSpec((rows, width), lambda i: (0, 0)),
            pl.BlockSpec((width, HIDDEN), lambda i: (0, part)),
        ],
        out_specs=pl.BlockSpec((rows, HIDDEN), lambda i: (0, 0)),
        compiler_params=pltpu.CompilerParams(vmem_limit_bytes=VMEM_LIMIT),
        cost_estimate=pl.CostEstimate(
            flops=2 * rows * width * HIDDEN, bytes_accessed=11 * 1024 * 1024, transcendentals=0
        ),
    )(left, right)


PIECES = [(0, 128), (128, 128), (256, 128), (384, 128)]


def ffn_kernel(*refs):
    x_refs, dact_ref, w_ref, gua_ref, whole_ref, dx_refs = refs[:4], refs[4], refs[5], refs[6], refs[7], refs[8:12]
    x_held, dact_held, w_held, gua, dx, sems, out_sems = refs[12:]
    x_copies = []
    for number, (start, size) in enumerate(PIECES):
        copy = pltpu.make_async_copy(
            x_refs[number], x_held.at[pl.ds(start, size)], sems.at[12 + number]
        )
        copy.start()
        x_copies.append(copy)
    copies = []
    for number, (start, width) in enumerate(GROUPS):
        for part in range(3):
            if part < 2:
                columns = pl.ds(part * HIDDEN + start, width)
                copy = pltpu.make_async_copy(
                    w_ref.at[:, columns], w_held.at[:, columns], sems.at[3 * number + part]
                )
            else:
                columns = pl.ds(start, width)
                copy = pltpu.make_async_copy(
                    dact_ref.at[:, columns], dact_held.at[:, columns], sems.at[3 * number + part]
                )
            copy.start()
            copies.append(copy)
    for copy in x_copies:
        copy.wait()
    results = [pltpu.make_async_copy(x_held, whole_ref, out_sems.at[5])]
    results[0].start()
    x = x_held[...]
    for number, (start, width) in enumerate(GROUPS):
        for part in range(3):
            copies[3 * number + part].wait()
        gate = dot_nn(x, w_held[:, start : start + width])
        up = dot_nn(x, w_held[:, HIDDEN + start : HIDDEN + start + width])
        dact = dact_held[:, start : start + width]
        sig = jax.nn.sigmoid(gate)
        silu = gate * sig
        dgate = dact * up * (sig * (1.0 + gate * (1.0 - sig)))
        gua[:, start : start + width] = dgate.astype(BF16)
        gua[:, HIDDEN + start : HIDDEN + start + width] = (dact * silu).astype(BF16)
        gua[:, 2 * HIDDEN + start : 2 * HIDDEN + start + width] = (silu * up).astype(BF16)
    copy = pltpu.make_async_copy(gua, gua_ref, out_sems.at[4])
    copy.start()
    results.append(copy)
    dgu = gua[:, : 2 * HIDDEN]
    for number in range(4):
        columns = slice(512 * number, 512 * number + 512)
        dx[:, columns] = dot_nt(dgu, w_held[columns, : 2 * HIDDEN]).astype(BF16)
    for number, (start, size) in enumerate(PIECES):
        copy = pltpu.make_async_copy(dx.at[pl.ds(start, size)], dx_refs[number], out_sems.at[number])
        copy.start()
        results.append(copy)
    for copy in results:
        copy.wait()


def ffn(pieces, dact, weights):
    rows, width = dact.shape[0], weights.shape[0]
    anywhere = pl.BlockSpec(memory_space=pl.ANY)
    result = pl.pallas_call(
        ffn_kernel,
        out_shape=(
            jax.ShapeDtypeStruct((rows, 3 * HIDDEN), BF16),
            jax.ShapeDtypeStruct((rows, width), BF16),
            *(jax.ShapeDtypeStruct((size, width), BF16) for _, size in PIECES),
        ),
        in_specs=[anywhere] * 6,
        out_specs=(anywhere,) * 6,
        scratch_shapes=[
            pltpu.VMEM((rows, width), BF16),
            pltpu.VMEM((rows, HIDDEN), F32),
            pltpu.VMEM((width, 2 * HIDDEN), BF16),
            pltpu.VMEM((rows, 3 * HIDDEN), BF16),
            pltpu.VMEM((rows, width), BF16),
            pltpu.SemaphoreType.DMA((16,)),
            pltpu.SemaphoreType.DMA((6,)),
        ],
        compiler_params=pltpu.CompilerParams(vmem_limit_bytes=VMEM_LIMIT),
        cost_estimate=pl.CostEstimate(
            flops=8 * rows * width * HIDDEN,
            bytes_accessed=25 * 1024 * 1024,
            transcendentals=rows * HIDDEN,
        ),
    )(*pieces, dact, weights)
    return result[0], result[1], result[2:]


def weight_grads_kernel(core_ref, x_ref, x2_ref, dy_ref, dy2_ref, right_ref, right2_ref, out_ref):
    part = pl.program_id(0)

    @pl.when(part < 2)
    def _():
        total = dot_tn(x_ref[...], right_ref[...]) + dot_tn(x2_ref[...], right2_ref[...])
        out_ref[...] = total.astype(BF16)

    @pl.when(part == 2)
    def _():
        total = dot_tn(dy_ref[...], right_ref[...]) + dot_tn(dy2_ref[...], right2_ref[...])
        out_ref[...] = total.astype(BF16)


def weight_grads(core, x, x2, dy, dy2, right, right2):
    rows = x.shape[0]
    tile = 1024
    half = x2.shape[1]
    tiles = half // tile
    own = lambda j, i, c: (0, c[0] * tiles + i)
    other = lambda j, i, c: (0, i)
    side = lambda j, i, c: (0, j)
    grid = pltpu.PrefetchScalarGridSpec(
        num_scalar_prefetch=1,
        grid=(3, tiles),
        in_specs=[
            pl.BlockSpec((rows, tile), own),
            pl.BlockSpec((rows, tile), other),
            pl.BlockSpec((rows, tile), own),
            pl.BlockSpec((rows, tile), other),
            pl.BlockSpec((rows, HIDDEN), side),
            pl.BlockSpec((rows, HIDDEN), side),
        ],
        out_specs=pl.BlockSpec((tile, HIDDEN), lambda j, i, c: (i, j)),
    )
    return pl.pallas_call(
        weight_grads_kernel,
        grid_spec=grid,
        out_shape=jax.ShapeDtypeStruct((half, 3 * HIDDEN), BF16),
        compiler_params=pltpu.CompilerParams(vmem_limit_bytes=VMEM_LIMIT),
        cost_estimate=pl.CostEstimate(
            flops=2 * 3 * 2 * rows * half * HIDDEN, bytes_accessed=24 * 1024 * 1024, transcendentals=0
        ),
    )(core, x, x2, dy, dy2, right, right2)


def rows_times_kernel(left_ref, right_ref, *out_refs):
    result = dot_nt(left_ref[...], right_ref[...]).astype(BF16)
    for number, ref in enumerate(out_refs):
        ref[...] = result[128 * number : 128 * number + 128]


def rows_times(left, left_part, right, part):
    rows, depth = left.shape[0], HIDDEN
    width = right.shape[0]
    tile = 512
    return pl.pallas_call(
        rows_times_kernel,
        out_shape=(jax.ShapeDtypeStruct((128, width), BF16),) * 4,
        grid=(width // tile,),
        in_specs=[
            pl.BlockSpec((rows, depth), lambda i: (0, left_part)),
            pl.BlockSpec((tile, depth), lambda i: (i, part)),
        ],
        out_specs=(pl.BlockSpec((128, tile), lambda i: (0, i)),) * 4,
        compiler_params=pltpu.CompilerParams(vmem_limit_bytes=VMEM_LIMIT),
        cost_estimate=pl.CostEstimate(
            flops=2 * rows * depth * width,
            bytes_accessed=2 * (rows * depth + width * depth + rows * width),
            transcendentals=0,
        ),
    )(left, right)


def ring_rows(own, near, far):
    return jnp.concatenate([own, near[:128], far, near[128:]], 0)


def put_half(number, value, other_ref, own_ref):
    @pl.when(number < 2)
    def _():
        other_ref[...] = value

    @pl.when(number >= 2)
    def _():
        own_ref[...] = value


def tile_at(i, c):
    return lax.rem(i + 2 * (1 - c[0]), 4)


def half_specs(tile, columns):
    return (
        pl.BlockSpec((tile, columns), lambda i, c: (jnp.minimum(i, 1), 0)),
        pl.BlockSpec((tile, columns), lambda i, c: (jnp.maximum(i - 2, 0), 0)),
    )


def wide_grads_kernel(
    core_ref, x_ref, dh0, dh1, dh2, o0, o1, o2, dq0, dq1, dq2, other_ref, own_ref, o_held, dq_held
):
    number = pl.program_id(0)

    @pl.when(number == 0)
    def _():
        o_held[...] = ring_rows(o0[...], o1[...], o2[...])
        dq_held[...] = ring_rows(dq0[...], dq1[...], dq2[...])

    out = dot_tn(ring_rows(dh0[...], dh1[...], dh2[...]), o_held[...])
    query = dot_tn(x_ref[...], dq_held[...])
    put_half(number, jnp.concatenate([out, query], 1).astype(BF16), other_ref, own_ref)


def wide_grads(core, normed, dh, o, dq):
    rows, width = normed.shape
    tile = 512
    whole = lambda i, c: (0, 0)
    column = lambda i, c: (0, tile_at(i, c))
    small = [pl.BlockSpec((size, 512), whole) for size in (128, 256, 128)]
    grid = pltpu.PrefetchScalarGridSpec(
        num_scalar_prefetch=1,
        grid=(4,),
        in_specs=[pl.BlockSpec((rows, tile), column)]
        + [pl.BlockSpec((size, tile), column) for size in (128, 256, 128)]
        + small
        + small,
        out_specs=half_specs(tile, 1024),
        scratch_shapes=[pltpu.VMEM((rows, 512), BF16), pltpu.VMEM((rows, 512), BF16)],
    )
    return pl.pallas_call(
        wide_grads_kernel,
        grid_spec=grid,
        out_shape=(jax.ShapeDtypeStruct((width // 2, 1024), BF16),) * 2,
        compiler_params=pltpu.CompilerParams(vmem_limit_bytes=VMEM_LIMIT),
        cost_estimate=pl.CostEstimate(
            flops=2 * rows * width * 1024, bytes_accessed=10 * 1024 * 1024, transcendentals=0
        ),
    )(core, normed, *dh, *o, *dq)


def finish_kernel(
    core_ref,
    x_ref,
    w_ref,
    dq0_ref,
    dq1_ref,
    dq2_ref,
    own_ref,
    one_ref,
    two_ref,
    cos_ref,
    sin_ref,
    norm_ref,
    second_ref,
    other_grad_ref,
    own_grad_ref,
    dx_own,
    dx_ahead,
    dx_far,
    dx_behind,
    gain_ref,
    dqkv,
    sums,
):
    number = pl.program_id(0)

    @pl.when(number == 0)
    def _():
        dqkv[:, :512] = ring_rows(dq0_ref[...], dq1_ref[...], dq2_ref[...])
        dkv = own_ref[...] + one_ref[...].astype(F32) + two_ref[...].astype(F32)
        turned = turn(dkv, cos_ref[...], -sin_ref[...])
        dqkv[:, 512:] = jnp.where(lane_is_low(dkv.shape, 128), turned, dkv).astype(BF16)

    x = x_ref[...]
    put_half(number, dot_tn(x, dqkv[:, 512:]).astype(BF16), other_grad_ref, own_grad_ref)
    dx = dot_nt(dqkv[...], w_ref[...])
    for start, ref in ((0, dx_own), (128, dx_ahead), (256, dx_far), (384, dx_behind)):
        ref[...] = dx[start : start + 128].astype(BF16)
    columns = pl.ds(pl.multiple_of(tile_at(number, core_ref) * 512, 512), 512)
    sums[:, columns] = jnp.broadcast_to(
        jnp.sum(dx * x.astype(F32), 0, keepdims=True) / norm_ref[...], (8, 512)
    )

    @pl.when(number == 3)
    def _():
        gain_ref[:8] = gain_rows(to_blocks(sums[...])[:1])
        gain_ref[8:] = gain_rows(second_ref[:1])


def finish(core, normed, weights, dq, own, one, two, cosine, sine, gain, second):
    rows, width = normed.shape
    tile = 512
    whole = lambda i, c: (0, 0)
    column = lambda i, c: (0, tile_at(i, c))
    narrow = pl.BlockSpec((rows, 128), whole)
    grid = pltpu.PrefetchScalarGridSpec(
        num_scalar_prefetch=1,
        grid=(4,),
        in_specs=[
            pl.BlockSpec((rows, tile), column),
            pl.BlockSpec((tile, 640), lambda i, c: (tile_at(i, c), 0)),
            pl.BlockSpec((128, 512), whole),
            pl.BlockSpec((256, 512), whole),
            pl.BlockSpec((128, 512), whole),
            narrow,
            narrow,
            narrow,
            narrow,
            narrow,
            pl.BlockSpec((1, tile), column),
            pl.BlockSpec((8, width), whole),
        ],
        out_specs=half_specs(tile, 128)
        + (pl.BlockSpec((128, tile), column),) * 4
        + (pl.BlockSpec((GAIN_ROWS, GAIN_COLUMNS), whole),),
        scratch_shapes=[pltpu.VMEM((rows, 640), BF16), pltpu.VMEM((8, width), F32)],
    )
    result = pl.pallas_call(
        finish_kernel,
        grid_spec=grid,
        out_shape=(jax.ShapeDtypeStruct((width // 2, 128), BF16),) * 2
        + (jax.ShapeDtypeStruct((128, width), BF16),) * 4
        + (jax.ShapeDtypeStruct((GAIN_ROWS, GAIN_COLUMNS), F32),),
        compiler_params=pltpu.CompilerParams(vmem_limit_bytes=VMEM_LIMIT),
        cost_estimate=pl.CostEstimate(
            flops=2 * rows * width * 768, bytes_accessed=10 * 1024 * 1024, transcendentals=0
        ),
    )(core, normed, weights, *dq, own, one, two, cosine, sine, gain, second)
    return result[0], result[1], result[2:6], result[6]


def per_device(
    tokens,
    segments,
    w_query,
    key_projection,
    value_projection,
    w_out,
    w_gate,
    w_up,
    w_down,
    norm_attn,
    norm_ffn,
    cotangent,
):
    place, core = lax.axis_index("head"), lax.axis_index("core")
    block = (lax.axis_index("y") * 4 + lax.axis_index("x")) * 2 + core
    place_array = place.astype(jnp.int32).reshape(1)
    core_array = core.astype(jnp.int32).reshape(1)
    keep = lax.optimization_barrier

    at = jnp.stack([lax.axis_index("x"), lax.axis_index("y"), core]).astype(jnp.int32)

    qkv_own = gather_axis(jnp.concatenate([w_query, key_projection, value_projection], 1), "x")
    qkv_own = gather_axis(qkv_own, "y")
    qkv_pieces = qkv_own, shift(qkv_own, "core", 1)
    out_weights = lax.all_gather(
        jnp.concatenate([w_down.T, w_out.T], 1), CORE_FIRST, axis=0, tiled=True
    )
    ffn_weights = lax.all_gather(jnp.concatenate([w_gate, w_up], 1), CORE_FIRST, axis=0, tiled=True)

    x_rows, dy_rows, normed_rows, gain_one, gain_two = prepare(
        tokens[0],
        cotangent[0],
        jnp.broadcast_to(norm_attn[None], (16, 2048)),
        jnp.broadcast_to(norm_ffn[None], (16, 2048)),
    )
    gain_one, gain_two = gain_one[:1], gain_two[:1]
    normed_one = gather_head(normed_rows)
    normed_one, dy_rows_late = keep((normed_one, dy_rows))
    dy_pieces = gather_pieces(dy_rows_late)

    row = jnp.arange(512, dtype=jnp.int32)
    positions = block * 512 + ((row // 128 + place) % 4) * 128 + row % 128
    frequency = 10000.0 ** (-jnp.arange(32, dtype=F32) * 2.0 / HEAD_SIZE)
    angles = positions.astype(F32)[:, None] * frequency[None, :]
    cosine, sine = jnp.cos(angles), jnp.sin(angles)
    cosine = jnp.concatenate([cosine] * 4, 1)
    sine = jnp.concatenate([-sine, sine, -sine, sine], 1)

    (kv_own,) = project(
        project_kv_kernel, at, normed_one, qkv_pieces, cosine, sine, 128, 128, False
    )
    normed_late, kv_own = keep((normed_one, kv_own))
    kv = (from_block(kv_own, 2), from_block(kv_own, 1), kv_own)
    queries, qkv_weights = project(
        project_q_kernel, at, normed_late, qkv_pieces, cosine, sine, 512, 640, True
    )

    flat = segments.reshape(-1)
    padded = jnp.concatenate([jnp.full((1024,), -1, jnp.int32), flat])
    own = lax.dynamic_slice_in_dim(flat, block * 512, 512, 0)
    window = lax.dynamic_slice_in_dim(padded, block * 512, 1536, 0)
    start = jnp.sum((window[None, :] < own[:, None]).astype(jnp.int32), 1)
    low = jnp.maximum(start, row + 1).reshape(1, 512)

    kk, vv, kvt = set_up(place_array, kv)
    seen = place_array, queries, kk, kvt, low, out_weights
    o_far, lse_far, part_far = attend(2, 1, 1, *seen)
    part_far, dy_pieces = keep((part_far, dy_pieces))
    dy = jnp.concatenate([dy_rows, *dy_pieces], 0)
    o_near, lse_near, part_near = attend(1, 2, 2, *seen)
    o_own, lse_own, part_own = attend(0, 1, 1, *seen)
    dy_other = swap_half(dy, core)
    attention_sum = scatter_pieces(part_own, part_near[:128], part_far, part_near[128:])
    h1, normed_rows_two = join(x_rows, gain_two, attention_sum)
    ahead, far, behind = gather_pieces(normed_rows_two)
    dact = columns_times(dy, out_weights, 0)
    dact, dy_other = keep((dact, dy_other))

    gua, normed_two, dnormed_two = ffn((normed_rows_two, ahead, far, behind), dact, ffn_weights)
    dnormed_two = scatter_pieces(*dnormed_two)
    gua_other = shift(gua, "core", 1)
    normed_two_other = swap_half(normed_two, core)
    out_pieces = rows_times(gua, 2, out_weights, 0)
    gua_other, normed_two_other, out_pieces = keep((gua_other, normed_two_other, out_pieces))
    held = weight_grads(core_array, normed_two, normed_two_other, dy, dy_other, gua, gua_other)
    held, dnormed_two = keep((held, dnormed_two))
    grads = lax.psum_scatter(held, ("y", "x"), scatter_dimension=0, tiled=True)

    dh1, dh1_low, grad_gain_two = join_back(h1, dy_rows, gain_two, dnormed_two)
    back = kk, vv, kvt, low, cosine, sine
    dq_own, dk, dv = attend_back(0, 1, 1, place_array, queries, dh1_low, out_weights, lse_own, *back, ())
    ahead, behind = shift(dh1_low, "head", -1), shift(dh1_low, "head", 1)
    ahead, behind, dk, dv, dh1_late, out_pieces = keep((ahead, behind, dk, dv, dh1_low, out_pieces))
    far = shift(dh1_late, "head", 2)
    near = jnp.concatenate([ahead, behind], 0)
    dq_near, dk, dv = attend_back(
        1, 2, 2, place_array, queries, near, out_weights, lse_near, *back, (dk, dv)
    )
    far, dk, dv, out_pieces = keep((far, dk, dv, out_pieces))
    out_pieces = scatter_pieces(*out_pieces)
    dq_far, dkv_own, dkv_earlier = attend_back(
        2, 1, 1, place_array, queries, far, out_weights, lse_far, *back, (dk, dv)
    )
    dq = dq_own, dq_near, dq_far
    dkv_one = from_block(dkv_earlier[1], -1)
    dkv_two = from_block(dkv_earlier[0], -2)
    wide_other, wide_own = wide_grads(
        core_array, normed_one, (dh1_low, near, far), (o_own, o_near, o_far), dq
    )
    dkv_one, dkv_two, wide_other, out_pieces = keep((dkv_one, dkv_two, wide_other, out_pieces))
    wide_other = shift(wide_other, "core", 1)

    narrow_other, narrow_own, dnormed_one, gains = finish(
        core_array,
        normed_one,
        qkv_weights,
        dq,
        dkv_own,
        dkv_one,
        dkv_two,
        cosine,
        sine,
        gain_one,
        grad_gain_two,
    )
    (gains,) = small_call(
        total_kernel, [((GAIN_ROWS, GAIN_COLUMNS), F32)], *exchange([gains] * 4, "head")
    )
    pieces, out_sums = first_pieces(
        at,
        wide_own,
        wide_other,
        narrow_own,
        shift(narrow_other, "core", 1),
        gains,
        shift(gains, "core", 1),
    )
    pieces, out_sums, dnormed_one = keep((pieces, out_sums, dnormed_one))
    rows = [(x_rows.shape, BF16)]
    (output,) = small_call(output_kernel, rows, h1, *out_pieces)
    grads = (
        grads[:, :HIDDEN].astype(F32),
        grads[:, HIDDEN : 2 * HIDDEN].astype(F32),
        grads[:, 2 * HIDDEN :].T.astype(F32),
    )
    pieces, out_sums, output, grads = keep(
        (exchange(pieces, "x"), exchange(out_sums, "y"), output, grads)
    )
    pieces, out_sums = second_pieces(at, pieces, out_sums)
    dnormed_one = scatter_pieces(*dnormed_one)
    (grad_inputs,) = small_call(input_grad_kernel, rows, dh1, x_rows, gain_one, *dnormed_one)
    pieces, out_sums, grad_inputs = keep((exchange(pieces, "y"), exchange(out_sums, "x"), grad_inputs))
    columns = (512, 64), (64, 512), (64, 64), (64, 64), (1, 2048), (1, 2048)
    grad_out, grad_query, grad_key, grad_value, grad_gain_one, grad_gain_two = small_call(
        attention_grads_kernel, [(shape, F32) for shape in columns], *pieces, *out_sums
    )

    return (
        output[None],
        grad_inputs[None],
        grad_query,
        grad_key,
        grad_value,
        grad_out,
        *grads,
        grad_gain_one.reshape(2048),
        grad_gain_two.reshape(2048),
    )


def solution(mesh):
    grid = Mesh(mesh.devices.reshape(4, 4, 4, 2), ("head", "y", "x", "core"))
    rows, up, down = P(BLK, "head", None), P(BLK, "head"), P("head", BLK)
    return jax.shard_map(
        per_device,
        mesh=grid,
        in_specs=(rows, P(), up, up, up, down, up, up, down, P(), P(), rows),
        out_specs=(rows, rows, up, up, up, down, up, up, down, P(), P()),
        check_vma=False,
    )
```

```python
import functools

import jax
import jax.numpy as jnp
from jax import lax
from jax.experimental import pallas as pl
from jax.experimental.pallas import tpu as pltpu
from jax.sharding import Mesh
from jax.sharding import PartitionSpec as P

HEAD_SIZE = 64
WINDOW = 1024
HIDDEN = 1408
EPSILON = 1e-05
BF16 = jnp.bfloat16
F32 = jnp.float32
BLK = ("y", "x", "core")
CORE_FIRST = ("core", "y", "x")
VMEM_LIMIT = 56 * 1024 * 1024


def dot_nn(a, b):
    return jnp.dot(a, b, preferred_element_type=F32)


def dot_nt(a, b):
    return lax.dot_general(a, b, (((1,), (1,)), ((), ())), preferred_element_type=F32)


def dot_tn(a, b):
    return lax.dot_general(a, b, (((0,), (0,)), ((), ())), preferred_element_type=F32)


def shift(value, axis, distance):
    size = lax.axis_size(axis)
    return lax.ppermute(value, axis, [(i, (i + distance) % size) for i in range(size)])


def add_low(a, b):
    return (a.astype(F32) + b.astype(F32)).astype(BF16)


def gather_pieces(rows):
    return shift(rows, "head", -1), shift(rows, "head", 2), shift(rows, "head", 1)


def near_pieces(rows):
    return shift(rows, "head", -1), shift(rows, "head", 1)


def far_pieces(ahead, behind):
    half = ahead.shape[0] // 2
    return shift(behind[:half], "head", 1), shift(ahead[half:], "head", -1)


def scatter_pieces(own, ahead, far, behind):
    return own, shift(ahead, "head", 1), shift(behind, "head", -1), shift(far, "head", 2)


def gather_axis(value, axis):
    return jnp.concatenate([value, shift(value, axis, -1), shift(value, axis, 2), shift(value, axis, 1)], 0)


def exchange(pieces, axis):
    return pieces[0], shift(pieces[1], axis, 1), shift(pieces[2], axis, 2), shift(pieces[3], axis, -1)


def from_block(value, distance):
    route = [(i, i + distance) for i in range(32) if 0 <= i + distance < 32]
    return lax.ppermute(value, BLK, route)


def scale_of(values):
    return lax.rsqrt(jnp.mean(values * values, -1, keepdims=True) + EPSILON)


def lane_is_low(shape, period):
    return lax.broadcasted_iota(jnp.int32, shape, len(shape) - 1) % period < period // 2


def turn(values, cosine, sine):
    swapped = jnp.where(
        lane_is_low(values.shape, 64), pltpu.roll(values, 96, 1), pltpu.roll(values, 32, 1)
    )
    return values * cosine + swapped * sine


def core_major_tiles(tiles):
    low = lane_is_low(tiles[0].shape, 128)
    rolled = [pltpu.roll(tile, 64, 1) for tile in tiles]
    first = [jnp.where(low, tiles[2 * k], rolled[2 * k + 1]) for k in range(8)]
    second = [jnp.where(low, rolled[2 * k], tiles[2 * k + 1]) for k in range(8)]
    return first + second


def block_major_tiles(tiles):
    low = lane_is_low(tiles[0].shape, 128)
    rolled = [pltpu.roll(tile, 64, 1) for tile in tiles]
    result = []
    for k in range(8):
        result.append(jnp.where(low, tiles[k], rolled[8 + k]))
        result.append(jnp.where(low, rolled[k], tiles[8 + k]))
    return result


def in_tiles(value):
    return [value[:, 128 * k : 128 * k + 128] for k in range(16)]


def prepare_kernel(x_ref, dy_ref, gain_one_ref, gain_two_ref, x_out, dy_out, normed_out, one_out, two_out):
    def convert(ref):
        return jnp.concatenate(core_major_tiles(in_tiles(ref[...].astype(F32))), 1)

    x, gain = convert(x_ref), convert(gain_one_ref)
    one_out[...], two_out[...] = gain, convert(gain_two_ref)
    x_out[...] = x
    dy_out[...] = convert(dy_ref).astype(BF16)
    normed_out[...] = (x * scale_of(x) * gain[:1]).astype(BF16)


def prepare(x, dy, gain_one, gain_two):
    rows, width = x.shape
    return pl.pallas_call(
        prepare_kernel,
        out_shape=(
            jax.ShapeDtypeStruct((rows, width), F32),
            jax.ShapeDtypeStruct((rows, width), BF16),
            jax.ShapeDtypeStruct((rows, width), BF16),
            jax.ShapeDtypeStruct((16, width), F32),
            jax.ShapeDtypeStruct((16, width), F32),
        ),
        compiler_params=pltpu.CompilerParams(vmem_limit_bytes=VMEM_LIMIT),
        cost_estimate=pl.CostEstimate(
            flops=10 * rows * width, bytes_accessed=10 * rows * width, transcendentals=rows
        ),
    )(x, dy, gain_one, gain_two)


def to_blocks(value):
    return jnp.concatenate(block_major_tiles(in_tiles(value)), 1)


def assemble_kernel(core_ref, own_ref, ahead_ref, top_ref, bottom_ref, behind_ref, out_ref, swap_ref):
    out_ref[:128] = own_ref[...]
    start = 128
    for ref in (ahead_ref, top_ref, bottom_ref, behind_ref):
        size = ref.shape[0]
        out_ref[start : start + size] = jnp.concatenate(
            core_major_tiles(in_tiles(ref[...].astype(F32))), 1
        ).astype(BF16)
        start += size
    swap_ref[...] = jnp.where(core_ref[0] == 0, out_ref[:, 1024:], out_ref[:, :1024])


def assemble(core, own, ahead, far_top, far_bottom, behind):
    vmem = pl.BlockSpec(memory_space=pltpu.VMEM)
    return pl.pallas_call(
        assemble_kernel,
        out_shape=(jax.ShapeDtypeStruct((512, 2048), BF16), jax.ShapeDtypeStruct((512, 1024), BF16)),
        in_specs=[pl.BlockSpec(memory_space=pltpu.SMEM)] + [vmem] * 5,
        out_specs=(vmem, vmem),
        compiler_params=pltpu.CompilerParams(vmem_limit_bytes=VMEM_LIMIT),
        cost_estimate=pl.CostEstimate(
            flops=4 * 512 * 2048, bytes_accessed=5 * 1024 * 1024, transcendentals=0
        ),
    )(core, own, ahead, far_top, far_bottom, behind)


def small_call(kernel, out_shape, *operands):
    return pl.pallas_call(
        kernel,
        out_shape=tuple(jax.ShapeDtypeStruct(shape, dtype) for shape, dtype in out_shape),
        compiler_params=pltpu.CompilerParams(vmem_limit_bytes=VMEM_LIMIT),
        cost_estimate=pl.CostEstimate(
            flops=sum(x.size for x in operands),
            bytes_accessed=2 * sum(x.size * x.dtype.itemsize for x in operands),
            transcendentals=0,
        ),
    )(*operands)


def total_of(refs):
    values = [ref[...].astype(F32) for ref in refs]
    while len(values) > 1:
        values = [values[0] + values[1]] + values[2:]
    return values[0]


def join_kernel(x_ref, gain_ref, a_ref, b_ref, c_ref, d_ref, h_out, normed_out):
    h = x_ref[...] + total_of((a_ref, b_ref, c_ref, d_ref))
    h_out[...] = h
    normed_out[...] = (h * scale_of(h) * gain_ref[:1]).astype(BF16)


def join(x, gain, pieces):
    return small_call(join_kernel, ((x.shape, F32), (x.shape, BF16)), x, gain, *pieces)


def norm_backward(values, gain, grad):
    scale = scale_of(values)
    weighted = grad * gain
    inner = jnp.mean(weighted * values, -1, keepdims=True)
    return scale * weighted - values * (scale * scale * scale * inner), scale


def join_back_kernel(h_ref, dy_ref, gain_ref, a_ref, b_ref, c_ref, d_ref, dh_out, low_out, grad_out):
    h, grad = h_ref[...], total_of((a_ref, b_ref, c_ref, d_ref))
    back, scale = norm_backward(h, gain_ref[:1], grad)
    dh = dy_ref[...].astype(F32) + back
    dh_out[...] = dh
    low_out[...] = dh.astype(BF16)
    grad_out[...] = to_blocks(jnp.broadcast_to(jnp.sum(grad * h * scale, 0, keepdims=True), (8, h.shape[1])))


def join_back(h, dy, gain, pieces):
    shapes = (h.shape, F32), (h.shape, BF16), ((8, h.shape[1]), F32)
    return small_call(join_back_kernel, shapes, h, dy, gain, *pieces)


def output_kernel(h_ref, a_ref, b_ref, c_ref, d_ref, out_ref):
    out_ref[...] = to_blocks(h_ref[...] + total_of((a_ref, b_ref, c_ref, d_ref))).astype(BF16)


def input_grad_kernel(dh_ref, x_ref, gain_ref, grad_ref, out_ref):
    back, _ = norm_backward(x_ref[...], gain_ref[:1], grad_ref[...].astype(F32))
    out_ref[...] = to_blocks(dh_ref[...] + back).astype(BF16)


GAIN_ROWS, GAIN_COLUMNS = 16, 256


def gain_rows(vector):
    return jnp.concatenate([vector[:, 256 * k : 256 * k + 256] for k in range(8)], 0)


def put_piece(ref, rows, gains):
    count = rows.shape[0]
    ref[:count] = rows
    ref[count:, GAIN_COLUMNS:] = jnp.zeros((GAIN_ROWS, ref.shape[1] - GAIN_COLUMNS), BF16)
    ref[count:, :GAIN_COLUMNS] = gains.astype(BF16)


def first_pieces_kernel(
    at_ref, q_ref, q2_ref, kv_ref, kv2_ref, o_ref, o2_ref, *refs
):
    gain_refs, out_refs = refs[:4], refs[4:]
    query = add_low(q_ref[...], q2_ref[...]).reshape(256, 512)
    narrow = add_low(kv_ref[...], kv2_ref[...]).reshape(256, 128)
    rows = jnp.concatenate([query, narrow], 1)
    out_rows = add_low(o_ref[...], o2_ref[...]).reshape(256, 512)
    gains = total_of(gain_refs)
    for number in range(4):

        @pl.when(pl.program_id(0) == number)
        def _():
            put_piece(out_refs[number], rows, gains)
            out_refs[4 + number][...] = out_rows


def first_pieces(at, wide, wide2, narrow, narrow2, gains):
    pick_x = lambda column: lambda d, s: (0, lax.rem(s[0] + d, 4), 0, column)
    pick_y = lambda d, s: (lax.rem(s[1] + d, 4), 0, 0, 0)
    whole = lambda d, s: (0, 0)
    shaped = lambda value: value.reshape(4, 4, 64, value.shape[1])
    shapes = [(256 + GAIN_ROWS, 640)] * 4 + [(256, 512)] * 4
    grid = pltpu.PrefetchScalarGridSpec(
        num_scalar_prefetch=1,
        grid=(4,),
        in_specs=[pl.BlockSpec((4, 1, 64, 512), pick_x(1))] * 2
        + [pl.BlockSpec((4, 1, 64, 128), pick_x(0))] * 2
        + [pl.BlockSpec((1, 4, 64, 512), pick_y)] * 2
        + [pl.BlockSpec((GAIN_ROWS, GAIN_COLUMNS), whole)] * 4,
        out_specs=tuple(pl.BlockSpec(shape, whole) for shape in shapes),
    )
    wide, wide2 = shaped(wide), shaped(wide2)
    result = pl.pallas_call(
        first_pieces_kernel,
        grid_spec=grid,
        out_shape=tuple(jax.ShapeDtypeStruct(shape, BF16) for shape in shapes),
        compiler_params=pltpu.CompilerParams(vmem_limit_bytes=VMEM_LIMIT),
        cost_estimate=pl.CostEstimate(
            flops=2 * 1024 * 1152, bytes_accessed=6 * 1024 * 1152, transcendentals=0
        ),
    )(at, wide, wide2, shaped(narrow), shaped(narrow2), wide, wide2, *gains)
    return result[:4], result[4:]


def second_pieces_kernel(at_ref, *refs):
    qkv, out, (held, out_held) = refs[:4], refs[4:8], refs[16:]
    held[...] = total_of(qkv)
    out_held[...] = total_of(out).astype(BF16)
    for number in range(4):
        y = pl.multiple_of(lax.rem(at_ref[1] + number, 4) * 64, 64)
        put_piece(refs[8 + number], held[pl.ds(y, 64), :].astype(BF16), held[256:, :GAIN_COLUMNS])
        x = pl.multiple_of(lax.rem(at_ref[0] + number, 4) * 64, 64)
        refs[12 + number][...] = out_held[pl.ds(x, 64), :]


def second_pieces(at, qkv, out):
    vmem = pl.BlockSpec(memory_space=pltpu.VMEM)
    shapes = [(64 + GAIN_ROWS, 640)] * 4 + [(64, 512)] * 4
    result = pl.pallas_call(
        second_pieces_kernel,
        out_shape=tuple(jax.ShapeDtypeStruct(shape, BF16) for shape in shapes),
        in_specs=[pl.BlockSpec(memory_space=pltpu.SMEM)] + [vmem] * 8,
        out_specs=(vmem,) * 8,
        scratch_shapes=[pltpu.VMEM((256 + GAIN_ROWS, 640), F32), pltpu.VMEM((256, 512), BF16)],
        compiler_params=pltpu.CompilerParams(vmem_limit_bytes=VMEM_LIMIT),
        cost_estimate=pl.CostEstimate(
            flops=4 * 272 * 1152, bytes_accessed=10 * 272 * 1152, transcendentals=0
        ),
    )(at, *qkv, *out)
    return result[:4], result[4:]


def gains_kernel(a_ref, b_ref, c_ref, d_ref, out_ref):
    values = [ref[64:, :GAIN_COLUMNS].astype(F32) for ref in (a_ref, b_ref, c_ref, d_ref)]
    out_ref[...] = (values[0] + values[1]) + (values[2] + values[3])


def attention_grads_kernel(*refs):
    out_ref, q_ref, k_ref, v_ref, one_ref, two_ref = refs[10:]
    total = total_of(refs[:4])
    out_ref[...] = total_of(refs[4:8]).T
    q_ref[...] = total[:64, :512]
    k_ref[...] = total[:64, 512:576]
    v_ref[...] = total[:64, 576:]
    gains = total_of(refs[8:10])
    one_ref[...] = jnp.concatenate([gains[k : k + 1] for k in range(8)], 1)
    two_ref[...] = jnp.concatenate([gains[k : k + 1] for k in range(8, 16)], 1)


def put_in_order(at_ref, own_ref, other_ref, columns, to_ref, sems):
    x, y, core = at_ref[0], at_ref[1], at_ref[2]
    copies = []
    for number in range(32):
        ref = (own_ref, other_ref)[number // 16]
        to_x, to_y = lax.rem(x + number % 4, 4), lax.rem(y + number // 4 % 4, 4)
        to_core = core if number < 16 else 1 - core
        row = pl.multiple_of(((to_core * 4 + to_y) * 4 + to_x) * 64, 64)
        copy = pltpu.make_async_copy(
            ref.at[pl.ds(number % 16 * 64, 64), columns], to_ref.at[pl.ds(row, 64)], sems.at[number]
        )
        copy.start()
        copies.append(copy)
    return copies


def project_kv_kernel(at_ref, x_ref, own_ref, other_ref, cos_ref, sin_ref, kv_ref, held, sems):
    for copy in put_in_order(at_ref, own_ref, other_ref, pl.ds(512, 128), held, sems):
        copy.wait()
    flat = dot_nn(x_ref[...], held[...])
    turned = turn(flat, cos_ref[...], sin_ref[...])
    kv_ref[...] = jnp.where(lane_is_low(flat.shape, 128), turned, flat).astype(BF16)


def project_q_kernel(at_ref, x_ref, own_ref, other_ref, cos_ref, sin_ref, q_ref, w_ref, held, sems, sem):
    for copy in put_in_order(at_ref, own_ref, other_ref, pl.ds(0, 640), held, sems):
        copy.wait()
    whole = pltpu.make_async_copy(held, w_ref, sem)
    whole.start()
    cosine, sine, x = cos_ref[...], sin_ref[...], x_ref[...]
    for start in (0, 256):
        wide = dot_nn(x, held[:, start : start + 256])
        for part in (0, 128):
            turned = turn(wide[:, part : part + 128], cosine, sine)
            q_ref[:, start + part : start + part + 128] = (turned * HEAD_SIZE**-0.5).astype(BF16)
    whole.wait()


def project(kernel, at, normed, weights, cosine, sine, columns, held_columns, hand_out):
    rows, width = normed.shape
    vmem, anywhere = pl.BlockSpec(memory_space=pltpu.VMEM), pl.BlockSpec(memory_space=pl.ANY)
    out_shape = [jax.ShapeDtypeStruct((rows, columns), BF16)]
    out_specs = [vmem]
    scratch = [pltpu.VMEM((width, held_columns), BF16), pltpu.SemaphoreType.DMA((32,))]
    if hand_out:
        out_shape.append(jax.ShapeDtypeStruct((width, held_columns), BF16))
        out_specs.append(anywhere)
        scratch.append(pltpu.SemaphoreType.DMA)
    return pl.pallas_call(
        kernel,
        out_shape=tuple(out_shape),
        in_specs=[pl.BlockSpec(memory_space=pltpu.SMEM), vmem, anywhere, anywhere, vmem, vmem],
        out_specs=tuple(out_specs),
        scratch_shapes=scratch,
        compiler_params=pltpu.CompilerParams(vmem_limit_bytes=VMEM_LIMIT),
        cost_estimate=pl.CostEstimate(
            flops=2 * rows * width * columns,
            bytes_accessed=2 * (rows * width + width * columns + rows * columns),
            transcendentals=0,
        ),
    )(at, normed, *weights, cosine, sine)


KEYS = 1152
PAIRS = 4


def set_up_kernel(place_ref, kv0_ref, kv1_ref, kv2_ref, kk_ref, vv_ref, kvt_ref):
    place = place_ref[0]
    low = lane_is_low((128, 128), 128)
    for block, ref in enumerate((kv0_ref, kv1_ref, kv2_ref)):
        for group in range(4):
            at = pl.multiple_of(lax.rem(group - place + 4, 4) * 128, 128)
            piece = ref[pl.ds(at, 128), :].astype(F32)
            rolled = pltpu.roll(piece, 64, 1)
            to = block * 512 + group * 128
            kk_ref[to : to + 128, :] = jnp.where(low, piece, rolled).astype(BF16)
            vv_ref[to : to + 128, :] = jnp.where(low, rolled, piece).astype(BF16)
            kvt_ref[:, to : to + 128] = piece.T.astype(BF16)


def set_up(place, kv):
    vmem = pl.BlockSpec(memory_space=pltpu.VMEM)
    return pl.pallas_call(
        set_up_kernel,
        out_shape=(
            jax.ShapeDtypeStruct((1536, 128), BF16),
            jax.ShapeDtypeStruct((1536, 128), BF16),
            jax.ShapeDtypeStruct((128, 1536), BF16),
        ),
        in_specs=[pl.BlockSpec(memory_space=pltpu.SMEM), vmem, vmem, vmem],
        out_specs=(vmem, vmem, vmem),
        compiler_params=pltpu.CompilerParams(vmem_limit_bytes=VMEM_LIMIT),
        cost_estimate=pl.CostEstimate(flops=1536 * 128 * 8, bytes_accessed=2 * 1024 * 1024, transcendentals=0),
    )(place, *kv)


def both_heads(pair):
    low = lane_is_low(pair.shape, 128)
    nothing = jnp.zeros_like(pair)
    return jnp.concatenate([jnp.where(low, pair, nothing), jnp.where(low, nothing, pair)], 0)


def side_by_side(transposed):
    return jnp.concatenate([transposed[:, :128], transposed[:, 128:]], 0).T


def mask_of(at, low_ref):
    key = lax.broadcasted_iota(jnp.int32, (KEYS, 128), 0)
    query = lax.broadcasted_iota(jnp.int32, (KEYS, 128), 1)
    seen = (key >= low_ref[:, pl.ds(at, 128)] - at) & (key <= query + WINDOW)
    bias = jnp.where(seen, 0.0, -jnp.inf)
    return jnp.concatenate([bias, bias], 1)


def attend_kernel(
    first, step, place_ref, q_ref, kk_ref, kvt_ref, low_ref, w_ref, o_ref, lse_ref, *refs
):
    part_refs, (bias, held, w_held, sem) = refs[:-4], refs[-4:]
    group = lax.rem(place_ref[0] + first + step * pl.program_id(0), 4)
    at = pl.multiple_of(group * 128, 128)

    load = pltpu.make_async_copy(w_ref.at[:, pl.ds(HIDDEN, 512)], w_held, sem)

    @pl.when((pl.program_id(0) == 0) & (pl.program_id(1) == 0))
    def _():
        load.start()

    @pl.when(pl.program_id(1) == 0)
    def _():
        bias[...] = mask_of(at, low_ref)

    keys = pl.ds(at, KEYS)
    for number in range(PAIRS):
        columns = slice(128 * number, 128 * number + 128)
        scores = dot_nt(kk_ref[keys, :], both_heads(q_ref[:, columns])) + bias[...]
        top = jnp.max(scores, 0, keepdims=True)
        weights = jnp.exp(scores - top)
        total = jnp.sum(weights, 0, keepdims=True)
        result = dot_nn(kvt_ref[64:128, keys], weights.astype(BF16)) / total
        lse_ref[0, number] = top + jnp.log(total)
        result = side_by_side(result).astype(BF16)
        o_ref[:, columns] = result
        held[PAIRS * pl.program_id(1) + number] = result

    @pl.when(pl.program_id(1) == 4 // PAIRS - 1)
    def _():
        @pl.when(pl.program_id(0) == 0)
        def _():
            load.wait()

        rows = jnp.concatenate([held[k] for k in range(4)], 1)
        part = dot_nt(rows, w_held[...]).astype(BF16)
        for number, ref in enumerate(part_refs):

            @pl.when(pl.program_id(0) == number)
            def _():
                ref[...] = part


def attend(first, step, count, place, queries, kk, kvt, low, weights):
    whole = lambda g, p, s: (0, 0)
    width = 128 * PAIRS
    grid = pltpu.PrefetchScalarGridSpec(
        num_scalar_prefetch=1,
        grid=(count, 4 // PAIRS),
        in_specs=[
            pl.BlockSpec((128, width), lambda g, p, s: (first + step * g, p)),
            pl.BlockSpec((1536, 128), whole),
            pl.BlockSpec((128, 1536), whole),
            pl.BlockSpec((1, 512), whole),
            pl.BlockSpec(memory_space=pl.ANY),
        ],
        out_specs=(
            pl.BlockSpec((128, width), lambda g, p, s: (g, p)),
            pl.BlockSpec((1, PAIRS, 1, 256), lambda g, p, s: (g, p, 0, 0)),
        )
        + (pl.BlockSpec((128, 2048), whole),) * count,
        scratch_shapes=[
            pltpu.VMEM((KEYS, 256), F32),
            pltpu.VMEM((4, 128, 128), BF16),
            pltpu.VMEM((2048, 512), BF16),
            pltpu.SemaphoreType.DMA,
        ],
    )
    return pl.pallas_call(
        functools.partial(attend_kernel, first, step),
        grid_spec=grid,
        out_shape=(
            jax.ShapeDtypeStruct((128 * count, 512), BF16),
            jax.ShapeDtypeStruct((count, 4, 1, 256), F32),
        )
        + (jax.ShapeDtypeStruct((128, 2048), BF16),) * count,
        compiler_params=pltpu.CompilerParams(vmem_limit_bytes=VMEM_LIMIT),
        cost_estimate=pl.CostEstimate(
            flops=count * 4 * KEYS * 256 * 256 * 2,
            bytes_accessed=3 * 1024 * 1024,
            transcendentals=count * 4 * KEYS * 256,
        ),
    )(place, queries, kk, kvt, low, weights)


def attend_back_kernel(first, step, count, *refs):
    last = first == 2
    place_ref, q_ref, w_ref, lse_ref, kk_ref, vv_ref, kvt_ref, low_ref, cos_ref, sin_ref = refs[:10]
    dh_refs, refs = refs[10 : 10 + count], refs[10 + count :]
    dk_in = dv_in = None
    if first > 0:
        dk_in, dv_in, refs = refs[0], refs[1], refs[2:]
    bias, do_held, dk, dv, w_held, sem = refs[-6:]
    dq_ref, outs = refs[0], refs[1:-6]
    number, pair = pl.program_id(0), pl.program_id(1)
    place = place_ref[0]
    at = pl.multiple_of(lax.rem(place + first + step * number, 4) * 128, 128)

    load = pltpu.make_async_copy(w_ref.at[:, pl.ds(HIDDEN, 512)], w_held, sem)

    @pl.when((number == 0) & (pair == 0))
    def _():
        load.start()
        dk[...] = jnp.zeros_like(dk) if dk_in is None else dk_in[...]
        dv[...] = jnp.zeros_like(dv) if dv_in is None else dv_in[...]

    @pl.when(pair == 0)
    def _():
        bias[...] = mask_of(at, low_ref)

        @pl.when(number == 0)
        def _():
            load.wait()

        for k, ref in enumerate(dh_refs):

            @pl.when(number == k)
            def _():
                do_rows = dot_nn(ref[...], w_held[...]).astype(BF16)
                for p in range(4):
                    do_held[p] = do_rows[:, 128 * p : 128 * p + 128]

    keys = pl.ds(at, KEYS)
    queries, grads, all_weights, all_grad_scores = [], [], [], []
    for k in range(PAIRS):
        columns = slice(128 * k, 128 * k + 128)
        query, grad = both_heads(q_ref[:, columns]), both_heads(do_held[PAIRS * pair + k])
        scores = dot_nt(kk_ref[keys, :], query) + bias[...]
        weights = jnp.exp(scores - lse_ref[0, k])
        grad_weights = dot_nt(vv_ref[keys, :], grad)
        inner = jnp.sum(weights * grad_weights, 0, keepdims=True)
        grad_scores = (weights * (grad_weights - inner)).astype(BF16)
        grad_query = side_by_side(dot_nn(kvt_ref[0:64, keys], grad_scores)) * HEAD_SIZE**-0.5
        dq_ref[:, columns] = turn(grad_query, cos_ref[...], -sin_ref[...]).astype(BF16)
        queries.append(query)
        grads.append(grad)
        all_weights.append(weights.astype(BF16))
        all_grad_scores.append(grad_scores)
    join = lambda values, axis: values[0] if PAIRS == 1 else jnp.concatenate(values, axis)
    dv[keys, :] += dot_nn(join(all_weights, 1), join(grads, 0))
    dk[keys, :] += dot_nn(join(all_grad_scores, 1), join(queries, 0))

    @pl.when((number == pl.num_programs(0) - 1) & (pair == 4 // PAIRS - 1))
    def _():
        if not last:
            outs[0][...], outs[1][...] = dk[...], dv[...]
            return
        half = lane_is_low((128, 128), 128)
        for block in range(3):
            for group in range(4):
                to = pl.multiple_of(lax.rem(group - place + 4, 4) * 128, 128)
                frm = slice(block * 512 + group * 128, block * 512 + group * 128 + 128)
                key, value = dk[frm, :], dv[frm, :]
                key = key + pltpu.roll(key, 64, 1)
                value = value + pltpu.roll(value, 64, 1)
                both = jnp.where(half, key, value)
                outs[block][pl.ds(to, 128), :] = both.astype(outs[block].dtype)


def attend_back(first, step, count, place, queries, dh, weights, lse, kk, vv, kvt, low, cosine, sine, held):
    last = first == 2
    whole = lambda g, p, s: (0, 0)
    specs = [
        pl.BlockSpec((128, 128 * PAIRS), lambda g, p, s: (first + step * g, p)),
        pl.BlockSpec(memory_space=pl.ANY),
        pl.BlockSpec((1, PAIRS, 1, 256), lambda g, p, s: (g, p, 0, 0)),
        pl.BlockSpec((1536, 128), whole),
        pl.BlockSpec((1536, 128), whole),
        pl.BlockSpec((128, 1536), whole),
        pl.BlockSpec((1, 512), whole),
        pl.BlockSpec((128, 128), lambda g, p, s: (first + step * g, 0)),
        pl.BlockSpec((128, 128), lambda g, p, s: (first + step * g, 0)),
    ]
    specs += [pl.BlockSpec((128, 2048), whole)] * count + [pl.BlockSpec((1536, 128), whole)] * len(held)
    if last:
        out_specs = (pl.BlockSpec((512, 128), whole),) * 3
        out_shape = tuple(jax.ShapeDtypeStruct((512, 128), dtype) for dtype in (BF16, BF16, F32))
    else:
        out_specs = (pl.BlockSpec((1536, 128), whole),) * 2
        out_shape = (jax.ShapeDtypeStruct((1536, 128), F32),) * 2
    grid = pltpu.PrefetchScalarGridSpec(
        num_scalar_prefetch=1,
        grid=(count, 4 // PAIRS),
        in_specs=specs,
        out_specs=(pl.BlockSpec((128, 128 * PAIRS), lambda g, p, s: (g, p)),) + out_specs,
        scratch_shapes=[
            pltpu.VMEM((KEYS, 256), F32),
            pltpu.VMEM((4, 128, 128), BF16),
            pltpu.VMEM((1536, 128), F32),
            pltpu.VMEM((1536, 128), F32),
            pltpu.VMEM((2048, 512), BF16),
            pltpu.SemaphoreType.DMA,
        ],
    )
    return pl.pallas_call(
        functools.partial(attend_back_kernel, first, step, count),
        grid_spec=grid,
        out_shape=(jax.ShapeDtypeStruct((128 * count, 512), BF16),) + out_shape,
        compiler_params=pltpu.CompilerParams(vmem_limit_bytes=VMEM_LIMIT),
        cost_estimate=pl.CostEstimate(
            flops=count * 4 * KEYS * 256 * 640 * 2,
            bytes_accessed=6 * 1024 * 1024,
            transcendentals=count * 4 * KEYS * 256,
        ),
    )(place, queries, weights, lse, kk, vv, kvt, low, cosine, sine, *dh, *held)


GROUPS = [(0, 128), (128, 256), (384, 512), (896, 512)]


def columns_times_kernel(left_ref, right_ref, out_ref):
    out_ref[...] = dot_nn(left_ref[...], right_ref[...])


def columns_times(left, right, part):
    rows, width = left.shape
    return pl.pallas_call(
        columns_times_kernel,
        out_shape=jax.ShapeDtypeStruct((rows, HIDDEN), F32),
        grid=(1,),
        in_specs=[
            pl.BlockSpec((rows, width), lambda i: (0, 0)),
            pl.BlockSpec((width, HIDDEN), lambda i: (0, part)),
        ],
        out_specs=pl.BlockSpec((rows, HIDDEN), lambda i: (0, 0)),
        compiler_params=pltpu.CompilerParams(vmem_limit_bytes=VMEM_LIMIT),
        cost_estimate=pl.CostEstimate(
            flops=2 * rows * width * HIDDEN, bytes_accessed=11 * 1024 * 1024, transcendentals=0
        ),
    )(left, right)


PIECES = [(0, 128), (128, 128), (256, 128), (384, 128)]


def ffn_kernel(*refs):
    core_ref, x_refs, dact_ref, w_ref = refs[0], refs[1:5], refs[5], refs[6]
    gua_ref, whole_ref, swap_ref, dx_refs = refs[7], refs[8], refs[9], refs[10:14]
    x_held, dact_held, w_held, gua, dx, sems, out_sems = refs[14:]
    x_copies = []
    for number, (start, size) in enumerate(PIECES):
        copy = pltpu.make_async_copy(
            x_refs[number], x_held.at[pl.ds(start, size)], sems.at[12 + number]
        )
        copy.start()
        x_copies.append(copy)
    copies = []
    for number, (start, width) in enumerate(GROUPS):
        for part in range(3):
            if part < 2:
                columns = pl.ds(part * HIDDEN + start, width)
                copy = pltpu.make_async_copy(
                    w_ref.at[:, columns], w_held.at[:, columns], sems.at[3 * number + part]
                )
            else:
                columns = pl.ds(start, width)
                copy = pltpu.make_async_copy(
                    dact_ref.at[:, columns], dact_held.at[:, columns], sems.at[3 * number + part]
                )
            copy.start()
            copies.append(copy)
    for copy in x_copies:
        copy.wait()
    half = pl.multiple_of((1 - core_ref[0]) * 1024, 1024)
    results = [
        pltpu.make_async_copy(x_held, whole_ref, out_sems.at[5]),
        pltpu.make_async_copy(x_held.at[:, pl.ds(half, 1024)], swap_ref, out_sems.at[6]),
    ]
    for copy in results:
        copy.start()
    x = x_held[...]
    for number, (start, width) in enumerate(GROUPS):
        for part in range(3):
            copies[3 * number + part].wait()
        gate = dot_nn(x, w_held[:, start : start + width])
        up = dot_nn(x, w_held[:, HIDDEN + start : HIDDEN + start + width])
        dact = dact_held[:, start : start + width]
        sig = jax.nn.sigmoid(gate)
        silu = gate * sig
        dgate = dact * up * (sig * (1.0 + gate * (1.0 - sig)))
        gua[:, start : start + width] = dgate.astype(BF16)
        gua[:, HIDDEN + start : HIDDEN + start + width] = (dact * silu).astype(BF16)
        gua[:, 2 * HIDDEN + start : 2 * HIDDEN + start + width] = (silu * up).astype(BF16)
    copy = pltpu.make_async_copy(gua, gua_ref, out_sems.at[4])
    copy.start()
    results.append(copy)
    dgu = gua[:, : 2 * HIDDEN]
    for number in range(4):
        columns = slice(512 * number, 512 * number + 512)
        dx[:, columns] = dot_nt(dgu, w_held[columns, : 2 * HIDDEN]).astype(BF16)
    for number, (start, size) in enumerate(PIECES):
        copy = pltpu.make_async_copy(dx.at[pl.ds(start, size)], dx_refs[number], out_sems.at[number])
        copy.start()
        results.append(copy)
    for copy in results:
        copy.wait()


def ffn(core, pieces, dact, weights):
    rows, width = dact.shape[0], weights.shape[0]
    anywhere = pl.BlockSpec(memory_space=pl.ANY)
    result = pl.pallas_call(
        ffn_kernel,
        out_shape=(
            jax.ShapeDtypeStruct((rows, 3 * HIDDEN), BF16),
            jax.ShapeDtypeStruct((rows, width), BF16),
            jax.ShapeDtypeStruct((rows, width // 2), BF16),
            *(jax.ShapeDtypeStruct((size, width), BF16) for _, size in PIECES),
        ),
        in_specs=[pl.BlockSpec(memory_space=pltpu.SMEM)] + [anywhere] * 6,
        out_specs=(anywhere,) * 7,
        scratch_shapes=[
            pltpu.VMEM((rows, width), BF16),
            pltpu.VMEM((rows, HIDDEN), F32),
            pltpu.VMEM((width, 2 * HIDDEN), BF16),
            pltpu.VMEM((rows, 3 * HIDDEN), BF16),
            pltpu.VMEM((rows, width), BF16),
            pltpu.SemaphoreType.DMA((16,)),
            pltpu.SemaphoreType.DMA((7,)),
        ],
        compiler_params=pltpu.CompilerParams(vmem_limit_bytes=VMEM_LIMIT),
        cost_estimate=pl.CostEstimate(
            flops=8 * rows * width * HIDDEN,
            bytes_accessed=25 * 1024 * 1024,
            transcendentals=rows * HIDDEN,
        ),
    )(core, *pieces, dact, weights)
    return result[0], result[1], result[2], result[3:]


def weight_grads_kernel(core_ref, x_ref, x2_ref, dy_ref, dy2_ref, right_ref, right2_ref, out_ref):
    part = pl.program_id(0)

    @pl.when(part < 2)
    def _():
        total = dot_tn(x_ref[...], right_ref[...]) + dot_tn(x2_ref[...], right2_ref[...])
        out_ref[...] = total.astype(BF16)

    @pl.when(part == 2)
    def _():
        total = dot_tn(dy_ref[...], right_ref[...]) + dot_tn(dy2_ref[...], right2_ref[...])
        out_ref[...] = total.astype(BF16)


def weight_grads(core, x, x2, dy, dy2, right, right2):
    rows = x.shape[0]
    tile = 1024
    half = x2.shape[1]
    tiles = half // tile
    own = lambda j, i, c: (0, c[0] * tiles + i)
    other = lambda j, i, c: (0, i)
    side = lambda j, i, c: (0, j)
    grid = pltpu.PrefetchScalarGridSpec(
        num_scalar_prefetch=1,
        grid=(3, tiles),
        in_specs=[
            pl.BlockSpec((rows, tile), own),
            pl.BlockSpec((rows, tile), other),
            pl.BlockSpec((rows, tile), own),
            pl.BlockSpec((rows, tile), other),
            pl.BlockSpec((rows, HIDDEN), side),
            pl.BlockSpec((rows, HIDDEN), side),
        ],
        out_specs=pl.BlockSpec((tile, HIDDEN), lambda j, i, c: (i, j)),
    )
    return pl.pallas_call(
        weight_grads_kernel,
        grid_spec=grid,
        out_shape=jax.ShapeDtypeStruct((half, 3 * HIDDEN), BF16),
        compiler_params=pltpu.CompilerParams(vmem_limit_bytes=VMEM_LIMIT),
        cost_estimate=pl.CostEstimate(
            flops=2 * 3 * 2 * rows * half * HIDDEN, bytes_accessed=24 * 1024 * 1024, transcendentals=0
        ),
    )(core, x, x2, dy, dy2, right, right2)


def rows_times_kernel(left_ref, right_ref, *out_refs):
    result = dot_nt(left_ref[...], right_ref[...]).astype(BF16)
    for number, ref in enumerate(out_refs):
        ref[...] = result[128 * number : 128 * number + 128]


def rows_times(left, left_part, right, part):
    rows, depth = left.shape[0], HIDDEN
    width = right.shape[0]
    tile = 512
    return pl.pallas_call(
        rows_times_kernel,
        out_shape=(jax.ShapeDtypeStruct((128, width), BF16),) * 4,
        grid=(width // tile,),
        in_specs=[
            pl.BlockSpec((rows, depth), lambda i: (0, left_part)),
            pl.BlockSpec((tile, depth), lambda i: (i, part)),
        ],
        out_specs=(pl.BlockSpec((128, tile), lambda i: (0, i)),) * 4,
        compiler_params=pltpu.CompilerParams(vmem_limit_bytes=VMEM_LIMIT),
        cost_estimate=pl.CostEstimate(
            flops=2 * rows * depth * width,
            bytes_accessed=2 * (rows * depth + width * depth + rows * width),
            transcendentals=0,
        ),
    )(left, right)


def ring_rows(own, near, far):
    return jnp.concatenate([own, near[:128], far, near[128:]], 0)


def put_half(number, value, other_ref, own_ref):
    @pl.when(number < 2)
    def _():
        other_ref[...] = value

    @pl.when(number >= 2)
    def _():
        own_ref[...] = value


def tile_at(i, c):
    return lax.rem(i + 2 * (1 - c[0]), 4)


def half_specs(tile, columns):
    return (
        pl.BlockSpec((tile, columns), lambda i, c: (jnp.minimum(i, 1), 0)),
        pl.BlockSpec((tile, columns), lambda i, c: (jnp.maximum(i - 2, 0), 0)),
    )


def wide_grads_kernel(
    core_ref, x_ref, dh0, dh1, dh2, dh3, o0, o1, o2, dq0, dq1, dq2, other_ref, own_ref, o_held, dq_held
):
    number = pl.program_id(0)

    @pl.when(number == 0)
    def _():
        o_held[...] = ring_rows(o0[...], o1[...], o2[...])
        dq_held[...] = ring_rows(dq0[...], dq1[...], dq2[...])

    dh = jnp.concatenate([ref[...] for ref in (dh0, dh1, dh2, dh3)], 0)
    out = dot_tn(dh, o_held[...])
    query = dot_tn(x_ref[...], dq_held[...])
    put_half(number, jnp.concatenate([out, query], 1).astype(BF16), other_ref, own_ref)


def wide_grads(core, normed, dh, o, dq):
    rows, width = normed.shape
    tile = 512
    whole = lambda i, c: (0, 0)
    column = lambda i, c: (0, tile_at(i, c))
    small = [pl.BlockSpec((size, 512), whole) for size in (128, 256, 128)]
    grid = pltpu.PrefetchScalarGridSpec(
        num_scalar_prefetch=1,
        grid=(4,),
        in_specs=[pl.BlockSpec((rows, tile), column)]
        + [pl.BlockSpec((128, tile), column)] * 4
        + small
        + small,
        out_specs=half_specs(tile, 1024),
        scratch_shapes=[pltpu.VMEM((rows, 512), BF16), pltpu.VMEM((rows, 512), BF16)],
    )
    return pl.pallas_call(
        wide_grads_kernel,
        grid_spec=grid,
        out_shape=(jax.ShapeDtypeStruct((width // 2, 1024), BF16),) * 2,
        compiler_params=pltpu.CompilerParams(vmem_limit_bytes=VMEM_LIMIT),
        cost_estimate=pl.CostEstimate(
            flops=2 * rows * width * 1024, bytes_accessed=10 * 1024 * 1024, transcendentals=0
        ),
    )(core, normed, *dh, *o, *dq)


def finish_kernel(
    core_ref,
    x_ref,
    w_ref,
    dq0_ref,
    dq1_ref,
    dq2_ref,
    own_ref,
    one_ref,
    two_ref,
    cos_ref,
    sin_ref,
    norm_ref,
    second_ref,
    other_grad_ref,
    own_grad_ref,
    dx_ref,
    gain_ref,
    dqkv,
    sums,
):
    number = pl.program_id(0)

    @pl.when(number == 0)
    def _():
        dqkv[:, :512] = ring_rows(dq0_ref[...], dq1_ref[...], dq2_ref[...])
        dkv = own_ref[...] + one_ref[...].astype(F32) + two_ref[...].astype(F32)
        turned = turn(dkv, cos_ref[...], -sin_ref[...])
        dqkv[:, 512:] = jnp.where(lane_is_low(dkv.shape, 128), turned, dkv).astype(BF16)

    x = x_ref[...]
    put_half(number, dot_tn(x, dqkv[:, 512:]).astype(BF16), other_grad_ref, own_grad_ref)
    dx = dot_nt(dqkv[...], w_ref[...])
    for piece in range(4):
        row = pl.multiple_of(lax.rem(core_ref[1] + piece, 4) * 128, 128)
        dx_ref[pl.ds(row, 128), :] = dx[128 * piece : 128 * piece + 128].astype(BF16)
    columns = pl.ds(pl.multiple_of(tile_at(number, core_ref) * 512, 512), 512)
    sums[:, columns] = jnp.broadcast_to(
        jnp.sum(dx * x.astype(F32), 0, keepdims=True) / norm_ref[:1], (8, 512)
    )

    @pl.when(number == 3)
    def _():
        gain_ref[:8] = gain_rows(to_blocks(sums[...])[:1])
        gain_ref[8:] = gain_rows(second_ref[:1])


def finish(core, normed, weights, dq, own, one, two, cosine, sine, gain, second):
    rows, width = normed.shape
    tile = 512
    whole = lambda i, c: (0, 0)
    column = lambda i, c: (0, tile_at(i, c))
    narrow = pl.BlockSpec((rows, 128), whole)
    grid = pltpu.PrefetchScalarGridSpec(
        num_scalar_prefetch=1,
        grid=(4,),
        in_specs=[
            pl.BlockSpec((rows, tile), column),
            pl.BlockSpec((tile, 640), lambda i, c: (tile_at(i, c), 0)),
            pl.BlockSpec((128, 512), whole),
            pl.BlockSpec((256, 512), whole),
            pl.BlockSpec((128, 512), whole),
            narrow,
            narrow,
            narrow,
            narrow,
            narrow,
            pl.BlockSpec((16, tile), column),
            pl.BlockSpec((8, width), whole),
        ],
        out_specs=half_specs(tile, 128)
        + (pl.BlockSpec((rows, tile), column),)
        + (pl.BlockSpec((GAIN_ROWS, GAIN_COLUMNS), whole),),
        scratch_shapes=[pltpu.VMEM((rows, 640), BF16), pltpu.VMEM((8, width), F32)],
    )
    result = pl.pallas_call(
        finish_kernel,
        grid_spec=grid,
        out_shape=(jax.ShapeDtypeStruct((width // 2, 128), BF16),) * 2
        + (jax.ShapeDtypeStruct((rows, width), BF16),)
        + (jax.ShapeDtypeStruct((GAIN_ROWS, GAIN_COLUMNS), F32),),
        compiler_params=pltpu.CompilerParams(vmem_limit_bytes=VMEM_LIMIT),
        cost_estimate=pl.CostEstimate(
            flops=2 * rows * width * 768, bytes_accessed=10 * 1024 * 1024, transcendentals=0
        ),
    )(core, normed, weights, *dq, own, one, two, cosine, sine, gain, second)
    return result


def per_device(
    tokens,
    segments,
    w_query,
    key_projection,
    value_projection,
    w_out,
    w_gate,
    w_up,
    w_down,
    norm_attn,
    norm_ffn,
    cotangent,
):
    place, core = lax.axis_index("head"), lax.axis_index("core")
    block = (lax.axis_index("y") * 4 + lax.axis_index("x")) * 2 + core
    place_array = place.astype(jnp.int32).reshape(1)
    core_array = core.astype(jnp.int32).reshape(1)
    core_place = jnp.stack([core, place]).astype(jnp.int32)
    keep = lax.optimization_barrier

    at = jnp.stack([lax.axis_index("x"), lax.axis_index("y"), core]).astype(jnp.int32)

    qkv_own = gather_axis(jnp.concatenate([w_query, key_projection, value_projection], 1), "x")
    qkv_own = gather_axis(qkv_own, "y")
    qkv_pieces = qkv_own, shift(qkv_own, "core", 1)
    out_weights = lax.all_gather(
        jnp.concatenate([w_down.T, w_out.T], 1), CORE_FIRST, axis=0, tiled=True
    )
    ffn_weights = lax.all_gather(jnp.concatenate([w_gate, w_up], 1), CORE_FIRST, axis=0, tiled=True)

    x_rows, dy_rows, normed_rows, gain_one, gain_two = prepare(
        tokens[0],
        cotangent[0],
        jnp.broadcast_to(norm_attn[None], (16, 2048)),
        jnp.broadcast_to(norm_ffn[None], (16, 2048)),
    )
    dy_ahead, dy_behind = near_pieces(cotangent[0])
    normed_rows, dy_ahead, dy_behind = keep((normed_rows, dy_ahead, dy_behind))
    ahead, behind = near_pieces(normed_rows)
    dy_ahead, dy_behind, ahead, behind = keep((dy_ahead, dy_behind, ahead, behind))
    dy_far = far_pieces(dy_ahead, dy_behind)
    normed_one = jnp.concatenate([normed_rows, ahead, *far_pieces(ahead, behind), behind], 0)

    row = jnp.arange(512, dtype=jnp.int32)
    positions = block * 512 + ((row // 128 + place) % 4) * 128 + row % 128
    frequency = 10000.0 ** (-jnp.arange(32, dtype=F32) * 2.0 / HEAD_SIZE)
    angles = positions.astype(F32)[:, None] * frequency[None, :]
    cosine, sine = jnp.cos(angles), jnp.sin(angles)
    cosine = jnp.concatenate([cosine] * 4, 1)
    sine = jnp.concatenate([-sine, sine, -sine, sine], 1)

    (kv_own,) = project(
        project_kv_kernel, at, normed_one, qkv_pieces, cosine, sine, 128, 128, False
    )
    normed_late, kv_own, dy_far = keep((normed_one, kv_own, dy_far))
    kv = (from_block(kv_own, 2), from_block(kv_own, 1), kv_own)
    queries, qkv_weights = project(
        project_q_kernel, at, normed_late, qkv_pieces, cosine, sine, 512, 640, True
    )

    flat = segments.reshape(-1)
    padded = jnp.concatenate([jnp.full((1024,), -1, jnp.int32), flat])
    own = lax.dynamic_slice_in_dim(flat, block * 512, 512, 0)
    window = lax.dynamic_slice_in_dim(padded, block * 512, 1536, 0)
    start = jnp.sum((window[None, :] < own[:, None]).astype(jnp.int32), 1)
    low = jnp.maximum(start, row + 1).reshape(1, 512)

    kk, vv, kvt = set_up(place_array, kv)
    seen = place_array, queries, kk, kvt, low, out_weights
    o_far, lse_far, part_far = attend(2, 1, 1, *seen)
    queries, part_far = keep((queries, part_far))
    part_far = shift(part_far, "head", 2)
    seen = place_array, queries, kk, kvt, low, out_weights
    o_near, lse_near, part_ahead, part_behind = attend(1, 2, 2, *seen)
    dy, dy_swap = assemble(core_array, dy_rows, dy_ahead, *dy_far, dy_behind)
    queries, part_far, part_ahead, part_behind, dy, dy_swap = keep(
        (queries, part_far, part_ahead, part_behind, dy, dy_swap)
    )
    seen = place_array, queries, kk, kvt, low, out_weights
    o_own, lse_own, part_own = attend(0, 1, 1, *seen)
    dy_other = shift(dy_swap, "core", 1)
    attention_sum = part_own, shift(part_ahead, "head", 1), shift(part_behind, "head", -1), part_far
    h1, normed_rows_two = join(x_rows, gain_two, attention_sum)
    ahead, far, behind = gather_pieces(normed_rows_two)
    dact = columns_times(dy, out_weights, 0)
    dact, dy_other = keep((dact, dy_other))

    gua, normed_two, normed_two_swap, dnormed_two = ffn(
        core_array, (normed_rows_two, ahead, far, behind), dact, ffn_weights
    )
    dnormed_two = scatter_pieces(*dnormed_two)
    gua_other = shift(gua, "core", 1)
    normed_two_other = shift(normed_two_swap, "core", 1)
    out_pieces = rows_times(gua, 2, out_weights, 0)
    gua_other, normed_two_other, out_pieces = keep((gua_other, normed_two_other, out_pieces))
    held = weight_grads(core_array, normed_two, normed_two_other, dy, dy_other, gua, gua_other)
    held, dnormed_two = keep((held, dnormed_two))
    grads = lax.psum_scatter(held, ("y", "x"), scatter_dimension=0, tiled=True)

    dh1, dh1_low, grad_gain_two = join_back(h1, dy_rows, gain_two, dnormed_two)
    back = kk, vv, kvt, low, cosine, sine
    dq_own, dk, dv = attend_back(0, 1, 1, place_array, queries, (dh1_low,), out_weights, lse_own, *back, ())
    ahead, behind = shift(dh1_low, "head", -1), shift(dh1_low, "head", 1)
    ahead, behind, dk, dv, dh1_late, out_pieces = keep((ahead, behind, dk, dv, dh1_low, out_pieces))
    far = shift(dh1_late, "head", 2)
    dq_near, dk, dv = attend_back(
        1, 2, 2, place_array, queries, (ahead, behind), out_weights, lse_near, *back, (dk, dv)
    )
    far, dk, dv, out_pieces = keep((far, dk, dv, out_pieces))
    out_pieces = scatter_pieces(*out_pieces)
    dq_far, dkv_first, dkv_second, dkv_own = attend_back(
        2, 1, 1, place_array, queries, (far,), out_weights, lse_far, *back, (dk, dv)
    )
    dq = dq_own, dq_near, dq_far
    dkv_one = from_block(dkv_second, -1)
    dkv_two = from_block(dkv_first, -2)
    wide_other, wide_own = wide_grads(
        core_array, normed_one, (dh1_low, ahead, far, behind), (o_own, o_near, o_far), dq
    )
    dkv_one, dkv_two, wide_other, out_pieces = keep((dkv_one, dkv_two, wide_other, out_pieces))
    wide_other = shift(wide_other, "core", 1)

    narrow_other, narrow_own, dnormed_one, gains = finish(
        core_place,
        normed_one,
        qkv_weights,
        dq,
        dkv_own,
        dkv_one,
        dkv_two,
        cosine,
        sine,
        gain_one,
        grad_gain_two,
    )
    dnormed_one = lax.psum_scatter(dnormed_one, "head", scatter_dimension=0, tiled=True)
    pieces, out_sums = first_pieces(
        at,
        wide_own,
        wide_other,
        narrow_own,
        shift(narrow_other, "core", 1),
        exchange([gains] * 4, "head"),
    )
    rows = [(x_rows.shape, BF16)]
    (output,) = small_call(output_kernel, rows, h1, *out_pieces)
    grads = (
        grads[:, :HIDDEN].astype(F32),
        grads[:, HIDDEN : 2 * HIDDEN].astype(F32),
        grads[:, 2 * HIDDEN :].T.astype(F32),
    )
    pieces, out_sums, output, grads = keep(
        (exchange(pieces, "x"), exchange(out_sums, "y"), output, grads)
    )
    pieces, out_sums = second_pieces(at, pieces, out_sums)
    (grad_inputs,) = small_call(input_grad_kernel, rows, dh1, x_rows, gain_one, dnormed_one)
    pieces, out_sums, grad_inputs = keep((exchange(pieces, "y"), exchange(out_sums, "x"), grad_inputs))
    (gains,) = small_call(gains_kernel, [((GAIN_ROWS, GAIN_COLUMNS), F32)], *pieces)
    columns = (512, 64), (64, 512), (64, 64), (64, 64), (1, 2048), (1, 2048)
    grad_out, grad_query, grad_key, grad_value, grad_gain_one, grad_gain_two = small_call(
        attention_grads_kernel,
        [(shape, F32) for shape in columns],
        *pieces,
        *out_sums,
        gains,
        shift(gains, "core", 1),
    )

    return (
        output[None],
        grad_inputs[None],
        grad_query,
        grad_key,
        grad_value,
        grad_out,
        *grads,
        grad_gain_one.reshape(2048),
        grad_gain_two.reshape(2048),
    )


def solution(mesh):
    grid = Mesh(mesh.devices.reshape(4, 4, 4, 2), ("head", "y", "x", "core"))
    rows, up, down = P(BLK, "head", None), P(BLK, "head"), P("head", BLK)
    return jax.shard_map(
        per_device,
        mesh=grid,
        in_specs=(rows, P(), up, up, up, down, up, up, down, P(), P(), rows),
        out_specs=(rows, rows, up, up, up, down, up, up, down, P(), P()),
        check_vma=False,
    )
```

```python
import functools

import jax
import jax.numpy as jnp
from jax import lax
from jax.experimental import pallas as pl
from jax.experimental.pallas import tpu as pltpu
from jax.sharding import Mesh
from jax.sharding import PartitionSpec as P

HEAD_SIZE = 64
WINDOW = 1024
HIDDEN = 1408
EPSILON = 1e-05
BF16 = jnp.bfloat16
F32 = jnp.float32
BLK = ("y", "x", "core")
CORE_FIRST = ("core", "y", "x")
VMEM_LIMIT = 56 * 1024 * 1024


def dot_nn(a, b):
    return jnp.dot(a, b, preferred_element_type=F32)


def dot_nt(a, b):
    return lax.dot_general(a, b, (((1,), (1,)), ((), ())), preferred_element_type=F32)


def dot_tn(a, b):
    return lax.dot_general(a, b, (((0,), (0,)), ((), ())), preferred_element_type=F32)


def shift(value, axis, distance):
    size = lax.axis_size(axis)
    return lax.ppermute(value, axis, [(i, (i + distance) % size) for i in range(size)])


def add_low(a, b):
    return (a.astype(F32) + b.astype(F32)).astype(BF16)


def gather_pieces(rows):
    return shift(rows, "head", -1), shift(rows, "head", 2), shift(rows, "head", 1)


def near_pieces(rows):
    return shift(rows, "head", -1), shift(rows, "head", 1)


def far_pieces(ahead, behind):
    half = ahead.shape[0] // 2
    return shift(behind[:half], "head", 1), shift(ahead[half:], "head", -1)


def scatter_pieces(own, ahead, far, behind):
    return own, shift(ahead, "head", 1), shift(behind, "head", -1), shift(far, "head", 2)


def gather_axis(value, axis):
    return value, shift(value, axis, -1), shift(value, axis, 2), shift(value, axis, 1)


def exchange(pieces, axis):
    return pieces[0], shift(pieces[1], axis, 1), shift(pieces[2], axis, 2), shift(pieces[3], axis, -1)


def from_block(value, distance):
    route = [(i, i + distance) for i in range(32) if 0 <= i + distance < 32]
    return lax.ppermute(value, BLK, route)


def scale_of(values):
    return lax.rsqrt(jnp.mean(values * values, -1, keepdims=True) + EPSILON)


def lane_is_low(shape, period):
    return lax.broadcasted_iota(jnp.int32, shape, len(shape) - 1) % period < period // 2


def turn(values, cosine, sine):
    swapped = jnp.where(
        lane_is_low(values.shape, 64), pltpu.roll(values, 96, 1), pltpu.roll(values, 32, 1)
    )
    return values * cosine + swapped * sine


def core_major_tiles(tiles):
    low = lane_is_low(tiles[0].shape, 128)
    rolled = [pltpu.roll(tile, 64, 1) for tile in tiles]
    first = [jnp.where(low, tiles[2 * k], rolled[2 * k + 1]) for k in range(8)]
    second = [jnp.where(low, rolled[2 * k], tiles[2 * k + 1]) for k in range(8)]
    return first + second


def block_major_tiles(tiles):
    low = lane_is_low(tiles[0].shape, 128)
    rolled = [pltpu.roll(tile, 64, 1) for tile in tiles]
    result = []
    for k in range(8):
        result.append(jnp.where(low, tiles[k], rolled[8 + k]))
        result.append(jnp.where(low, rolled[k], tiles[8 + k]))
    return result


def in_tiles(value):
    return [value[:, 128 * k : 128 * k + 128] for k in range(16)]


def prepare_kernel(x_ref, dy_ref, gain_one_ref, gain_two_ref, x_out, dy_out, normed_out, one_out, two_out):
    def convert(ref):
        return jnp.concatenate(core_major_tiles(in_tiles(ref[...].astype(F32))), 1)

    x, gain = convert(x_ref), convert(gain_one_ref)
    one_out[...], two_out[...] = gain, convert(gain_two_ref)
    x_out[...] = x
    dy_out[...] = convert(dy_ref).astype(BF16)
    normed_out[...] = (x * scale_of(x) * gain[:1]).astype(BF16)


def prepare(x, dy, gain_one, gain_two):
    rows, width = x.shape
    return pl.pallas_call(
        prepare_kernel,
        out_shape=(
            jax.ShapeDtypeStruct((rows, width), F32),
            jax.ShapeDtypeStruct((rows, width), BF16),
            jax.ShapeDtypeStruct((rows, width), BF16),
            jax.ShapeDtypeStruct((16, width), F32),
            jax.ShapeDtypeStruct((16, width), F32),
        ),
        compiler_params=pltpu.CompilerParams(vmem_limit_bytes=VMEM_LIMIT),
        cost_estimate=pl.CostEstimate(
            flops=10 * rows * width, bytes_accessed=10 * rows * width, transcendentals=rows
        ),
    )(x, dy, gain_one, gain_two)


def to_blocks(value):
    return jnp.concatenate(block_major_tiles(in_tiles(value)), 1)


def assemble_kernel(core_ref, own_ref, ahead_ref, top_ref, bottom_ref, behind_ref, out_ref, swap_ref):
    out_ref[:128] = own_ref[...]
    start = 128
    for ref in (ahead_ref, top_ref, bottom_ref, behind_ref):
        size = ref.shape[0]
        out_ref[start : start + size] = jnp.concatenate(
            core_major_tiles(in_tiles(ref[...].astype(F32))), 1
        ).astype(BF16)
        start += size
    swap_ref[...] = jnp.where(core_ref[0] == 0, out_ref[:, 1024:], out_ref[:, :1024])


def assemble(core, own, ahead, far_top, far_bottom, behind):
    vmem = pl.BlockSpec(memory_space=pltpu.VMEM)
    return pl.pallas_call(
        assemble_kernel,
        out_shape=(jax.ShapeDtypeStruct((512, 2048), BF16), jax.ShapeDtypeStruct((512, 1024), BF16)),
        in_specs=[pl.BlockSpec(memory_space=pltpu.SMEM)] + [vmem] * 5,
        out_specs=(vmem, vmem),
        compiler_params=pltpu.CompilerParams(vmem_limit_bytes=VMEM_LIMIT),
        cost_estimate=pl.CostEstimate(
            flops=4 * 512 * 2048, bytes_accessed=5 * 1024 * 1024, transcendentals=0
        ),
    )(core, own, ahead, far_top, far_bottom, behind)


def small_call(kernel, out_shape, *operands):
    return pl.pallas_call(
        kernel,
        out_shape=tuple(jax.ShapeDtypeStruct(shape, dtype) for shape, dtype in out_shape),
        compiler_params=pltpu.CompilerParams(vmem_limit_bytes=VMEM_LIMIT),
        cost_estimate=pl.CostEstimate(
            flops=sum(x.size for x in operands),
            bytes_accessed=2 * sum(x.size * x.dtype.itemsize for x in operands),
            transcendentals=0,
        ),
    )(*operands)


def total_of(refs):
    values = [ref[...].astype(F32) for ref in refs]
    while len(values) > 1:
        values = [values[0] + values[1]] + values[2:]
    return values[0]


def join_kernel(x_ref, gain_ref, a_ref, b_ref, c_ref, d_ref, h_out, normed_out):
    h = x_ref[...] + total_of((a_ref, b_ref, c_ref, d_ref))
    h_out[...] = h
    normed_out[...] = (h * scale_of(h) * gain_ref[:1]).astype(BF16)


def join(x, gain, pieces):
    return small_call(join_kernel, ((x.shape, F32), (x.shape, BF16)), x, gain, *pieces)


def norm_backward(values, gain, grad):
    scale = scale_of(values)
    weighted = grad * gain
    inner = jnp.mean(weighted * values, -1, keepdims=True)
    return scale * weighted - values * (scale * scale * scale * inner), scale


def join_back_kernel(h_ref, dy_ref, gain_ref, a_ref, b_ref, c_ref, d_ref, dh_out, low_out, grad_out):
    h, grad = h_ref[...], total_of((a_ref, b_ref, c_ref, d_ref))
    back, scale = norm_backward(h, gain_ref[:1], grad)
    dh = dy_ref[...].astype(F32) + back
    dh_out[...] = dh
    low_out[...] = dh.astype(BF16)
    grad_out[...] = to_blocks(jnp.broadcast_to(jnp.sum(grad * h * scale, 0, keepdims=True), (8, h.shape[1])))


def join_back(h, dy, gain, pieces):
    shapes = (h.shape, F32), (h.shape, BF16), ((8, h.shape[1]), F32)
    return small_call(join_back_kernel, shapes, h, dy, gain, *pieces)


def output_kernel(h_ref, a_ref, b_ref, c_ref, d_ref, out_ref):
    out_ref[...] = to_blocks(h_ref[...] + total_of((a_ref, b_ref, c_ref, d_ref))).astype(BF16)


def input_grad_kernel(dh_ref, x_ref, gain_ref, grad_ref, out_ref):
    back, _ = norm_backward(x_ref[...], gain_ref[:1], grad_ref[...].astype(F32))
    out_ref[...] = to_blocks(dh_ref[...] + back).astype(BF16)


GAIN_ROWS, GAIN_COLUMNS = 16, 256


def gain_rows(vector):
    return jnp.concatenate([vector[:, 256 * k : 256 * k + 256] for k in range(8)], 0)


def put_piece(ref, rows, gains):
    count = rows.shape[0]
    ref[:count] = rows
    ref[count:, GAIN_COLUMNS:] = jnp.zeros((GAIN_ROWS, ref.shape[1] - GAIN_COLUMNS), BF16)
    ref[count:, :GAIN_COLUMNS] = gains.astype(BF16)


def first_pieces_kernel(
    at_ref, q_ref, q2_ref, kv_ref, kv2_ref, o_ref, o2_ref, *refs
):
    gain_refs, out_refs = refs[:4], refs[4:]
    query = add_low(q_ref[...], q2_ref[...]).reshape(256, 512)
    narrow = add_low(kv_ref[...], kv2_ref[...]).reshape(256, 128)
    rows = jnp.concatenate([query, narrow], 1)
    out_rows = add_low(o_ref[...], o2_ref[...]).reshape(256, 512)
    gains = total_of(gain_refs)
    for number in range(4):

        @pl.when(pl.program_id(0) == number)
        def _():
            put_piece(out_refs[number], rows, gains)
            out_refs[4 + number][...] = out_rows


def first_pieces(at, wide, wide2, narrow, narrow2, gains):
    pick_x = lambda column: lambda d, s: (0, lax.rem(s[0] + d, 4), 0, column)
    pick_y = lambda d, s: (lax.rem(s[1] + d, 4), 0, 0, 0)
    whole = lambda d, s: (0, 0)
    shaped = lambda value: value.reshape(4, 4, 64, value.shape[1])
    shapes = [(256 + GAIN_ROWS, 640)] * 4 + [(256, 512)] * 4
    grid = pltpu.PrefetchScalarGridSpec(
        num_scalar_prefetch=1,
        grid=(4,),
        in_specs=[pl.BlockSpec((4, 1, 64, 512), pick_x(1))] * 2
        + [pl.BlockSpec((4, 1, 64, 128), pick_x(0))] * 2
        + [pl.BlockSpec((1, 4, 64, 512), pick_y)] * 2
        + [pl.BlockSpec((GAIN_ROWS, GAIN_COLUMNS), whole)] * 4,
        out_specs=tuple(pl.BlockSpec(shape, whole) for shape in shapes),
    )
    wide, wide2 = shaped(wide), shaped(wide2)
    result = pl.pallas_call(
        first_pieces_kernel,
        grid_spec=grid,
        out_shape=tuple(jax.ShapeDtypeStruct(shape, BF16) for shape in shapes),
        compiler_params=pltpu.CompilerParams(vmem_limit_bytes=VMEM_LIMIT),
        cost_estimate=pl.CostEstimate(
            flops=2 * 1024 * 1152, bytes_accessed=6 * 1024 * 1152, transcendentals=0
        ),
    )(at, wide, wide2, shaped(narrow), shaped(narrow2), wide, wide2, *gains)
    return result[:4], result[4:]


def second_pieces_kernel(at_ref, *refs):
    qkv, out, (held, out_held) = refs[:4], refs[4:8], refs[16:]
    held[...] = total_of(qkv)
    out_held[...] = total_of(out).astype(BF16)
    for number in range(4):
        y = pl.multiple_of(lax.rem(at_ref[1] + number, 4) * 64, 64)
        put_piece(refs[8 + number], held[pl.ds(y, 64), :].astype(BF16), held[256:, :GAIN_COLUMNS])
        x = pl.multiple_of(lax.rem(at_ref[0] + number, 4) * 64, 64)
        refs[12 + number][...] = out_held[pl.ds(x, 64), :]


def second_pieces(at, qkv, out):
    vmem = pl.BlockSpec(memory_space=pltpu.VMEM)
    shapes = [(64 + GAIN_ROWS, 640)] * 4 + [(64, 512)] * 4
    result = pl.pallas_call(
        second_pieces_kernel,
        out_shape=tuple(jax.ShapeDtypeStruct(shape, BF16) for shape in shapes),
        in_specs=[pl.BlockSpec(memory_space=pltpu.SMEM)] + [vmem] * 8,
        out_specs=(vmem,) * 8,
        scratch_shapes=[pltpu.VMEM((256 + GAIN_ROWS, 640), F32), pltpu.VMEM((256, 512), BF16)],
        compiler_params=pltpu.CompilerParams(vmem_limit_bytes=VMEM_LIMIT),
        cost_estimate=pl.CostEstimate(
            flops=4 * 272 * 1152, bytes_accessed=10 * 272 * 1152, transcendentals=0
        ),
    )(at, *qkv, *out)
    return result[:4], result[4:]


def gains_kernel(a_ref, b_ref, c_ref, d_ref, out_ref):
    values = [ref[64:, :GAIN_COLUMNS].astype(F32) for ref in (a_ref, b_ref, c_ref, d_ref)]
    out_ref[...] = (values[0] + values[1]) + (values[2] + values[3])


def attention_grads_kernel(*refs):
    out_ref, q_ref, k_ref, v_ref, one_ref, two_ref = refs[10:]
    total = total_of(refs[:4])
    out_ref[...] = total_of(refs[4:8])
    q_ref[...] = total[:64, :512]
    k_ref[...] = total[:64, 512:576]
    v_ref[...] = total[:64, 576:]
    gains = total_of(refs[8:10])
    one_ref[...] = jnp.concatenate([gains[k : k + 1] for k in range(8)], 1)
    two_ref[...] = jnp.concatenate([gains[k : k + 1] for k in range(8, 16)], 1)


def put_in_order(at_ref, own_ref, other_ref, columns, to_ref, sems):
    x, y, core = at_ref[0], at_ref[1], at_ref[2]
    copies = []
    for number in range(32):
        ref = (own_ref, other_ref)[number // 16]
        to_x, to_y = lax.rem(x + number % 4, 4), lax.rem(y + number // 4 % 4, 4)
        to_core = core if number < 16 else 1 - core
        row = pl.multiple_of(((to_core * 4 + to_y) * 4 + to_x) * 64, 64)
        copy = pltpu.make_async_copy(
            ref.at[pl.ds(number % 16 * 64, 64), columns], to_ref.at[pl.ds(row, 64)], sems.at[number]
        )
        copy.start()
        copies.append(copy)
    return copies


def project_kv_kernel(at_ref, x_ref, own_ref, other_ref, cos_ref, sin_ref, kv_ref, held, sems):
    for copy in put_in_order(at_ref, own_ref, other_ref, pl.ds(512, 128), held, sems):
        copy.wait()
    flat = dot_nn(x_ref[...], held[...])
    turned = turn(flat, cos_ref[...], sin_ref[...])
    kv_ref[...] = jnp.where(lane_is_low(flat.shape, 128), turned, flat).astype(BF16)


def project_q_kernel(at_ref, x_ref, own_ref, other_ref, cos_ref, sin_ref, q_ref, w_ref, held, sems, sem):
    for copy in put_in_order(at_ref, own_ref, other_ref, pl.ds(0, 640), held, sems):
        copy.wait()
    whole = pltpu.make_async_copy(held, w_ref, sem)
    whole.start()
    cosine, sine, x = cos_ref[...], sin_ref[...], x_ref[...]
    for start in (0, 256):
        wide = dot_nn(x, held[:, start : start + 256])
        for part in (0, 128):
            turned = turn(wide[:, part : part + 128], cosine, sine)
            q_ref[:, start + part : start + part + 128] = (turned * HEAD_SIZE**-0.5).astype(BF16)
    whole.wait()


def project(kernel, at, normed, weights, cosine, sine, columns, held_columns, hand_out):
    rows, width = normed.shape
    vmem, anywhere = pl.BlockSpec(memory_space=pltpu.VMEM), pl.BlockSpec(memory_space=pl.ANY)
    out_shape = [jax.ShapeDtypeStruct((rows, columns), BF16)]
    out_specs = [vmem]
    scratch = [pltpu.VMEM((width, held_columns), BF16), pltpu.SemaphoreType.DMA((32,))]
    if hand_out:
        out_shape.append(jax.ShapeDtypeStruct((width, held_columns), BF16))
        out_specs.append(anywhere)
        scratch.append(pltpu.SemaphoreType.DMA)
    return pl.pallas_call(
        kernel,
        out_shape=tuple(out_shape),
        in_specs=[pl.BlockSpec(memory_space=pltpu.SMEM), vmem, anywhere, anywhere, vmem, vmem],
        out_specs=tuple(out_specs),
        scratch_shapes=scratch,
        compiler_params=pltpu.CompilerParams(vmem_limit_bytes=VMEM_LIMIT),
        cost_estimate=pl.CostEstimate(
            flops=2 * rows * width * columns,
            bytes_accessed=2 * (rows * width + width * columns + rows * columns),
            transcendentals=0,
        ),
    )(at, normed, *weights, cosine, sine)


KEYS = 1152
PAIRS = 4


def set_up_kernel(place_ref, kv0_ref, kv1_ref, kv2_ref, kk_ref, vv_ref, kvt_ref):
    place = place_ref[0]
    low = lane_is_low((128, 128), 128)
    for block, ref in enumerate((kv0_ref, kv1_ref, kv2_ref)):
        for group in range(4):
            at = pl.multiple_of(lax.rem(group - place + 4, 4) * 128, 128)
            piece = ref[pl.ds(at, 128), :].astype(F32)
            rolled = pltpu.roll(piece, 64, 1)
            to = block * 512 + group * 128
            kk_ref[to : to + 128, :] = jnp.where(low, piece, rolled).astype(BF16)
            vv_ref[to : to + 128, :] = jnp.where(low, rolled, piece).astype(BF16)
            kvt_ref[:, to : to + 128] = piece.T.astype(BF16)


def set_up(place, kv):
    vmem = pl.BlockSpec(memory_space=pltpu.VMEM)
    return pl.pallas_call(
        set_up_kernel,
        out_shape=(
            jax.ShapeDtypeStruct((1536, 128), BF16),
            jax.ShapeDtypeStruct((1536, 128), BF16),
            jax.ShapeDtypeStruct((128, 1536), BF16),
        ),
        in_specs=[pl.BlockSpec(memory_space=pltpu.SMEM), vmem, vmem, vmem],
        out_specs=(vmem, vmem, vmem),
        compiler_params=pltpu.CompilerParams(vmem_limit_bytes=VMEM_LIMIT),
        cost_estimate=pl.CostEstimate(flops=1536 * 128 * 8, bytes_accessed=2 * 1024 * 1024, transcendentals=0),
    )(place, *kv)


def both_heads(pair):
    low = lane_is_low(pair.shape, 128)
    nothing = jnp.zeros_like(pair)
    return jnp.concatenate([jnp.where(low, pair, nothing), jnp.where(low, nothing, pair)], 0)


def side_by_side(transposed):
    return jnp.concatenate([transposed[:, :128], transposed[:, 128:]], 0).T


def mask_of(at, low_ref):
    key = lax.broadcasted_iota(jnp.int32, (KEYS, 128), 0)
    query = lax.broadcasted_iota(jnp.int32, (KEYS, 128), 1)
    seen = (key >= low_ref[:, pl.ds(at, 128)] - at) & (key <= query + WINDOW)
    bias = jnp.where(seen, 0.0, -jnp.inf)
    return jnp.concatenate([bias, bias], 1)


def attend_kernel(
    first, step, place_ref, q_ref, kk_ref, kvt_ref, low_ref, w_ref, o_ref, lse_ref, *refs
):
    part_refs, (bias, held, w_held, sem) = refs[:-4], refs[-4:]
    group = lax.rem(place_ref[0] + first + step * pl.program_id(0), 4)
    at = pl.multiple_of(group * 128, 128)

    load = pltpu.make_async_copy(w_ref.at[:, pl.ds(HIDDEN, 512)], w_held, sem)

    @pl.when((pl.program_id(0) == 0) & (pl.program_id(1) == 0))
    def _():
        load.start()

    @pl.when(pl.program_id(1) == 0)
    def _():
        bias[...] = mask_of(at, low_ref)

    keys = pl.ds(at, KEYS)
    for number in range(PAIRS):
        columns = slice(128 * number, 128 * number + 128)
        scores = dot_nt(kk_ref[keys, :], both_heads(q_ref[:, columns])) + bias[...]
        top = jnp.max(scores, 0, keepdims=True)
        weights = jnp.exp(scores - top)
        total = jnp.sum(weights, 0, keepdims=True)
        result = dot_nn(kvt_ref[64:128, keys], weights.astype(BF16)) / total
        lse_ref[0, number] = top + jnp.log(total)
        result = side_by_side(result).astype(BF16)
        o_ref[:, columns] = result
        held[PAIRS * pl.program_id(1) + number] = result

    @pl.when(pl.program_id(1) == 4 // PAIRS - 1)
    def _():
        @pl.when(pl.program_id(0) == 0)
        def _():
            load.wait()

        rows = jnp.concatenate([held[k] for k in range(4)], 1)
        part = dot_nt(rows, w_held[...]).astype(BF16)
        for number, ref in enumerate(part_refs):

            @pl.when(pl.program_id(0) == number)
            def _():
                ref[...] = part


def attend(first, step, count, place, queries, kk, kvt, low, weights):
    whole = lambda g, p, s: (0, 0)
    width = 128 * PAIRS
    grid = pltpu.PrefetchScalarGridSpec(
        num_scalar_prefetch=1,
        grid=(count, 4 // PAIRS),
        in_specs=[
            pl.BlockSpec((128, width), lambda g, p, s: (first + step * g, p)),
            pl.BlockSpec((1536, 128), whole),
            pl.BlockSpec((128, 1536), whole),
            pl.BlockSpec((1, 512), whole),
            pl.BlockSpec(memory_space=pl.ANY),
        ],
        out_specs=(
            pl.BlockSpec((128, width), lambda g, p, s: (g, p)),
            pl.BlockSpec((1, PAIRS, 1, 256), lambda g, p, s: (g, p, 0, 0)),
        )
        + (pl.BlockSpec((128, 2048), whole),) * count,
        scratch_shapes=[
            pltpu.VMEM((KEYS, 256), F32),
            pltpu.VMEM((4, 128, 128), BF16),
            pltpu.VMEM((2048, 512), BF16),
            pltpu.SemaphoreType.DMA,
        ],
    )
    return pl.pallas_call(
        functools.partial(attend_kernel, first, step),
        grid_spec=grid,
        out_shape=(
            jax.ShapeDtypeStruct((128 * count, 512), BF16),
            jax.ShapeDtypeStruct((count, 4, 1, 256), F32),
        )
        + (jax.ShapeDtypeStruct((128, 2048), BF16),) * count,
        compiler_params=pltpu.CompilerParams(vmem_limit_bytes=VMEM_LIMIT),
        cost_estimate=pl.CostEstimate(
            flops=count * 4 * KEYS * 256 * 256 * 2,
            bytes_accessed=3 * 1024 * 1024,
            transcendentals=count * 4 * KEYS * 256,
        ),
    )(place, queries, kk, kvt, low, weights)


def attend_back_kernel(first, step, count, *refs):
    last = first == 2
    place_ref, q_ref, w_ref, lse_ref, kk_ref, vv_ref, kvt_ref, low_ref, cos_ref, sin_ref = refs[:10]
    o_ref = refs[10]
    dh_refs, refs = refs[11 : 11 + count], refs[11 + count :]
    dk_in = dv_in = None
    if first > 0:
        dk_in, dv_in, refs = refs[0], refs[1], refs[2:]
    bias, do_held, dk, dv, w_held, sem = refs[-6:]
    dq_ref, outs = refs[0], refs[1:-6]
    number, pair = pl.program_id(0), pl.program_id(1)
    place = place_ref[0]
    at = pl.multiple_of(lax.rem(place + first + step * number, 4) * 128, 128)

    load = pltpu.make_async_copy(w_ref.at[:, pl.ds(HIDDEN, 512)], w_held, sem)

    @pl.when((number == 0) & (pair == 0))
    def _():
        load.start()
        dk[...] = jnp.zeros_like(dk) if dk_in is None else dk_in[...]
        dv[...] = jnp.zeros_like(dv) if dv_in is None else dv_in[...]

    @pl.when(pair == 0)
    def _():
        bias[...] = mask_of(at, low_ref)

        @pl.when(number == 0)
        def _():
            load.wait()

        for k, ref in enumerate(dh_refs):

            @pl.when(number == k)
            def _():
                do_rows = dot_nn(ref[...], w_held[...]).astype(BF16)
                for p in range(4):
                    do_held[p] = do_rows[:, 128 * p : 128 * p + 128]

    keys = pl.ds(at, KEYS)
    queries, grads, all_weights, all_grad_scores = [], [], [], []
    for k in range(PAIRS):
        columns = slice(128 * k, 128 * k + 128)
        do_pair = do_held[PAIRS * pair + k]
        query, grad = both_heads(q_ref[:, columns]), both_heads(do_pair)
        scores = dot_nt(kk_ref[keys, :], query) + bias[...]
        weights = jnp.exp(scores - lse_ref[0, k])
        grad_weights = dot_nt(vv_ref[keys, :], grad)
        product = (o_ref[:, columns].astype(F32) * do_pair.astype(F32)).T
        inner = jnp.concatenate(
            [jnp.sum(product[:64], 0, keepdims=True), jnp.sum(product[64:], 0, keepdims=True)], 1
        )
        grad_scores = (weights * (grad_weights - inner)).astype(BF16)
        grad_query = side_by_side(dot_nn(kvt_ref[0:64, keys], grad_scores)) * HEAD_SIZE**-0.5
        dq_ref[:, columns] = turn(grad_query, cos_ref[...], -sin_ref[...]).astype(BF16)
        queries.append(query)
        grads.append(grad)
        all_weights.append(weights.astype(BF16))
        all_grad_scores.append(grad_scores)
    join = lambda values, axis: values[0] if PAIRS == 1 else jnp.concatenate(values, axis)
    dv[keys, :] += dot_nn(join(all_weights, 1), join(grads, 0))
    dk[keys, :] += dot_nn(join(all_grad_scores, 1), join(queries, 0))

    @pl.when((number == pl.num_programs(0) - 1) & (pair == 4 // PAIRS - 1))
    def _():
        if not last:
            outs[0][...], outs[1][...] = dk[...], dv[...]
            return
        half = lane_is_low((128, 128), 128)
        for block in range(3):
            for group in range(4):
                to = pl.multiple_of(lax.rem(group - place + 4, 4) * 128, 128)
                frm = slice(block * 512 + group * 128, block * 512 + group * 128 + 128)
                key, value = dk[frm, :], dv[frm, :]
                key = key + pltpu.roll(key, 64, 1)
                value = value + pltpu.roll(value, 64, 1)
                both = jnp.where(half, key, value)
                outs[block][pl.ds(to, 128), :] = both.astype(outs[block].dtype)


def attend_back(first, step, count, place, queries, o, dh, weights, lse, kk, vv, kvt, low, cosine, sine, held):
    last = first == 2
    whole = lambda g, p, s: (0, 0)
    specs = [
        pl.BlockSpec((128, 128 * PAIRS), lambda g, p, s: (first + step * g, p)),
        pl.BlockSpec(memory_space=pl.ANY),
        pl.BlockSpec((1, PAIRS, 1, 256), lambda g, p, s: (g, p, 0, 0)),
        pl.BlockSpec((1536, 128), whole),
        pl.BlockSpec((1536, 128), whole),
        pl.BlockSpec((128, 1536), whole),
        pl.BlockSpec((1, 512), whole),
        pl.BlockSpec((128, 128), lambda g, p, s: (first + step * g, 0)),
        pl.BlockSpec((128, 128), lambda g, p, s: (first + step * g, 0)),
    ]
    specs += [pl.BlockSpec((128, 128 * PAIRS), lambda g, p, s: (g, p))]
    specs += [pl.BlockSpec((128, 2048), whole)] * count + [pl.BlockSpec((1536, 128), whole)] * len(held)
    if last:
        out_specs = (pl.BlockSpec((512, 128), whole),) * 3
        out_shape = tuple(jax.ShapeDtypeStruct((512, 128), dtype) for dtype in (BF16, BF16, F32))
    else:
        out_specs = (pl.BlockSpec((1536, 128), whole),) * 2
        out_shape = (jax.ShapeDtypeStruct((1536, 128), F32),) * 2
    grid = pltpu.PrefetchScalarGridSpec(
        num_scalar_prefetch=1,
        grid=(count, 4 // PAIRS),
        in_specs=specs,
        out_specs=(pl.BlockSpec((128, 128 * PAIRS), lambda g, p, s: (g, p)),) + out_specs,
        scratch_shapes=[
            pltpu.VMEM((KEYS, 256), F32),
            pltpu.VMEM((4, 128, 128), BF16),
            pltpu.VMEM((1536, 128), F32),
            pltpu.VMEM((1536, 128), F32),
            pltpu.VMEM((2048, 512), BF16),
            pltpu.SemaphoreType.DMA,
        ],
    )
    return pl.pallas_call(
        functools.partial(attend_back_kernel, first, step, count),
        grid_spec=grid,
        out_shape=(jax.ShapeDtypeStruct((128 * count, 512), BF16),) + out_shape,
        compiler_params=pltpu.CompilerParams(vmem_limit_bytes=VMEM_LIMIT),
        cost_estimate=pl.CostEstimate(
            flops=count * 4 * KEYS * 256 * 640 * 2,
            bytes_accessed=6 * 1024 * 1024,
            transcendentals=count * 4 * KEYS * 256,
        ),
    )(place, queries, weights, lse, kk, vv, kvt, low, cosine, sine, o, *dh, *held)


GROUPS = [(0, 128), (128, 256), (384, 512), (896, 512)]


def columns_times_kernel(left_ref, right_ref, out_ref):
    out_ref[...] = dot_nn(left_ref[...], right_ref[...])


def columns_times(left, right, part):
    rows, width = left.shape
    return pl.pallas_call(
        columns_times_kernel,
        out_shape=jax.ShapeDtypeStruct((rows, HIDDEN), F32),
        grid=(1,),
        in_specs=[
            pl.BlockSpec((rows, width), lambda i: (0, 0)),
            pl.BlockSpec((width, HIDDEN), lambda i: (0, part)),
        ],
        out_specs=pl.BlockSpec((rows, HIDDEN), lambda i: (0, 0)),
        compiler_params=pltpu.CompilerParams(vmem_limit_bytes=VMEM_LIMIT),
        cost_estimate=pl.CostEstimate(
            flops=2 * rows * width * HIDDEN, bytes_accessed=11 * 1024 * 1024, transcendentals=0
        ),
    )(left, right)


PIECES = [(0, 128), (128, 128), (256, 128), (384, 128)]


def ffn_kernel(*refs):
    core_ref, x_refs, dact_ref, w_ref = refs[0], refs[1:5], refs[5], refs[6]
    gua_ref, whole_ref, swap_ref, dx_refs = refs[7], refs[8], refs[9], refs[10:14]
    x_held, dact_held, w_held, gua, dx, sems, out_sems = refs[14:]
    x_copies = []
    for number, (start, size) in enumerate(PIECES):
        copy = pltpu.make_async_copy(
            x_refs[number], x_held.at[pl.ds(start, size)], sems.at[12 + number]
        )
        copy.start()
        x_copies.append(copy)
    copies = []
    for number, (start, width) in enumerate(GROUPS):
        for part in range(3):
            if part < 2:
                columns = pl.ds(part * HIDDEN + start, width)
                copy = pltpu.make_async_copy(
                    w_ref.at[:, columns], w_held.at[:, columns], sems.at[3 * number + part]
                )
            else:
                columns = pl.ds(start, width)
                copy = pltpu.make_async_copy(
                    dact_ref.at[:, columns], dact_held.at[:, columns], sems.at[3 * number + part]
                )
            copy.start()
            copies.append(copy)
    for copy in x_copies:
        copy.wait()
    half = pl.multiple_of((1 - core_ref[0]) * 1024, 1024)
    results = [
        pltpu.make_async_copy(x_held, whole_ref, out_sems.at[5]),
        pltpu.make_async_copy(x_held.at[:, pl.ds(half, 1024)], swap_ref, out_sems.at[6]),
    ]
    for copy in results:
        copy.start()
    x = x_held[...]
    for number, (start, width) in enumerate(GROUPS):
        for part in range(3):
            copies[3 * number + part].wait()
        gate = dot_nn(x, w_held[:, start : start + width])
        up = dot_nn(x, w_held[:, HIDDEN + start : HIDDEN + start + width])
        dact = dact_held[:, start : start + width]
        sig = jax.nn.sigmoid(gate)
        silu = gate * sig
        dgate = dact * up * (sig * (1.0 + gate * (1.0 - sig)))
        gua[:, start : start + width] = dgate.astype(BF16)
        gua[:, HIDDEN + start : HIDDEN + start + width] = (dact * silu).astype(BF16)
        gua[:, 2 * HIDDEN + start : 2 * HIDDEN + start + width] = (silu * up).astype(BF16)
    copy = pltpu.make_async_copy(gua, gua_ref, out_sems.at[4])
    copy.start()
    results.append(copy)
    dgu = gua[:, : 2 * HIDDEN]
    for number in range(4):
        columns = slice(512 * number, 512 * number + 512)
        dx[:, columns] = dot_nt(dgu, w_held[columns, : 2 * HIDDEN]).astype(BF16)
    for number, (start, size) in enumerate(PIECES):
        copy = pltpu.make_async_copy(dx.at[pl.ds(start, size)], dx_refs[number], out_sems.at[number])
        copy.start()
        results.append(copy)
    for copy in results:
        copy.wait()


def ffn(core, pieces, dact, weights):
    rows, width = dact.shape[0], weights.shape[0]
    anywhere = pl.BlockSpec(memory_space=pl.ANY)
    result = pl.pallas_call(
        ffn_kernel,
        out_shape=(
            jax.ShapeDtypeStruct((rows, 3 * HIDDEN), BF16),
            jax.ShapeDtypeStruct((rows, width), BF16),
            jax.ShapeDtypeStruct((rows, width // 2), BF16),
            *(jax.ShapeDtypeStruct((size, width), BF16) for _, size in PIECES),
        ),
        in_specs=[pl.BlockSpec(memory_space=pltpu.SMEM)] + [anywhere] * 6,
        out_specs=(anywhere,) * 7,
        scratch_shapes=[
            pltpu.VMEM((rows, width), BF16),
            pltpu.VMEM((rows, HIDDEN), F32),
            pltpu.VMEM((width, 2 * HIDDEN), BF16),
            pltpu.VMEM((rows, 3 * HIDDEN), BF16),
            pltpu.VMEM((rows, width), BF16),
            pltpu.SemaphoreType.DMA((16,)),
            pltpu.SemaphoreType.DMA((7,)),
        ],
        compiler_params=pltpu.CompilerParams(vmem_limit_bytes=VMEM_LIMIT),
        cost_estimate=pl.CostEstimate(
            flops=8 * rows * width * HIDDEN,
            bytes_accessed=25 * 1024 * 1024,
            transcendentals=rows * HIDDEN,
        ),
    )(core, *pieces, dact, weights)
    return result[0], result[1], result[2], result[3:]


def weight_grads_kernel(core_ref, x_ref, x2_ref, dy_ref, dy2_ref, right_ref, right2_ref, out_ref):
    part = pl.program_id(0)

    @pl.when(part < 2)
    def _():
        total = dot_tn(x_ref[...], right_ref[...]) + dot_tn(x2_ref[...], right2_ref[...])
        out_ref[...] = total.astype(BF16)

    @pl.when(part == 2)
    def _():
        total = dot_tn(dy_ref[...], right_ref[...]) + dot_tn(dy2_ref[...], right2_ref[...])
        out_ref[...] = total.astype(BF16)


def weight_grads(core, x, x2, dy, dy2, right, right2):
    rows = x.shape[0]
    tile = 1024
    half = x2.shape[1]
    tiles = half // tile
    own = lambda j, i, c: (0, c[0] * tiles + i)
    other = lambda j, i, c: (0, i)
    side = lambda j, i, c: (0, j)
    grid = pltpu.PrefetchScalarGridSpec(
        num_scalar_prefetch=1,
        grid=(3, tiles),
        in_specs=[
            pl.BlockSpec((rows, tile), own),
            pl.BlockSpec((rows, tile), other),
            pl.BlockSpec((rows, tile), own),
            pl.BlockSpec((rows, tile), other),
            pl.BlockSpec((rows, HIDDEN), side),
            pl.BlockSpec((rows, HIDDEN), side),
        ],
        out_specs=pl.BlockSpec((tile, HIDDEN), lambda j, i, c: (i, j)),
    )
    return pl.pallas_call(
        weight_grads_kernel,
        grid_spec=grid,
        out_shape=jax.ShapeDtypeStruct((half, 3 * HIDDEN), BF16),
        compiler_params=pltpu.CompilerParams(vmem_limit_bytes=VMEM_LIMIT),
        cost_estimate=pl.CostEstimate(
            flops=2 * 3 * 2 * rows * half * HIDDEN, bytes_accessed=24 * 1024 * 1024, transcendentals=0
        ),
    )(core, x, x2, dy, dy2, right, right2)


def rows_times_kernel(left_ref, right_ref, *out_refs):
    result = dot_nt(left_ref[...], right_ref[...]).astype(BF16)
    for number, ref in enumerate(out_refs):
        ref[...] = result[128 * number : 128 * number + 128]


def rows_times(left, left_part, right, part):
    rows, depth = left.shape[0], HIDDEN
    width = right.shape[0]
    tile = 512
    return pl.pallas_call(
        rows_times_kernel,
        out_shape=(jax.ShapeDtypeStruct((128, width), BF16),) * 4,
        grid=(width // tile,),
        in_specs=[
            pl.BlockSpec((rows, depth), lambda i: (0, left_part)),
            pl.BlockSpec((tile, depth), lambda i: (i, part)),
        ],
        out_specs=(pl.BlockSpec((128, tile), lambda i: (0, i)),) * 4,
        compiler_params=pltpu.CompilerParams(vmem_limit_bytes=VMEM_LIMIT),
        cost_estimate=pl.CostEstimate(
            flops=2 * rows * depth * width,
            bytes_accessed=2 * (rows * depth + width * depth + rows * width),
            transcendentals=0,
        ),
    )(left, right)


def ring_rows(own, near, far):
    return jnp.concatenate([own, near[:128], far, near[128:]], 0)


def put_half(number, value, other_ref, own_ref):
    @pl.when(number < 2)
    def _():
        other_ref[...] = value

    @pl.when(number >= 2)
    def _():
        own_ref[...] = value


def tile_at(i, c):
    return lax.rem(i + 2 * (1 - c[0]), 4)


def half_specs(tile, columns):
    return (
        pl.BlockSpec((tile, columns), lambda i, c: (jnp.minimum(i, 1), 0)),
        pl.BlockSpec((tile, columns), lambda i, c: (jnp.maximum(i - 2, 0), 0)),
    )


def wide_grads_kernel(
    core_ref, x_ref, dh0, dh1, dh2, dh3, o0, o1, o2, dq0, dq1, dq2, other_ref, own_ref, o_held, dq_held
):
    number = pl.program_id(0)

    @pl.when(number == 0)
    def _():
        o_held[...] = ring_rows(o0[...], o1[...], o2[...])
        dq_held[...] = ring_rows(dq0[...], dq1[...], dq2[...])

    dh = jnp.concatenate([ref[...] for ref in (dh0, dh1, dh2, dh3)], 0)
    out = dot_tn(dh, o_held[...])
    query = dot_tn(x_ref[...], dq_held[...])
    put_half(number, jnp.concatenate([out, query], 1).astype(BF16), other_ref, own_ref)


def wide_grads(core, normed, dh, o, dq):
    rows, width = normed.shape
    tile = 512
    whole = lambda i, c: (0, 0)
    column = lambda i, c: (0, tile_at(i, c))
    small = [pl.BlockSpec((size, 512), whole) for size in (128, 256, 128)]
    grid = pltpu.PrefetchScalarGridSpec(
        num_scalar_prefetch=1,
        grid=(4,),
        in_specs=[pl.BlockSpec((rows, tile), column)]
        + [pl.BlockSpec((128, tile), column)] * 4
        + small
        + small,
        out_specs=half_specs(tile, 1024),
        scratch_shapes=[pltpu.VMEM((rows, 512), BF16), pltpu.VMEM((rows, 512), BF16)],
    )
    return pl.pallas_call(
        wide_grads_kernel,
        grid_spec=grid,
        out_shape=(jax.ShapeDtypeStruct((width // 2, 1024), BF16),) * 2,
        compiler_params=pltpu.CompilerParams(vmem_limit_bytes=VMEM_LIMIT),
        cost_estimate=pl.CostEstimate(
            flops=2 * rows * width * 1024, bytes_accessed=10 * 1024 * 1024, transcendentals=0
        ),
    )(core, normed, *dh, *o, *dq)


def finish_kernel(
    core_ref,
    x_ref,
    w_ref,
    dq0_ref,
    dq1_ref,
    dq2_ref,
    own_ref,
    one_ref,
    two_ref,
    cos_ref,
    sin_ref,
    norm_ref,
    second_ref,
    other_grad_ref,
    own_grad_ref,
    dx_ref,
    gain_ref,
    dqkv,
    sums,
):
    number = pl.program_id(0)

    @pl.when(number == 0)
    def _():
        dqkv[:, :512] = ring_rows(dq0_ref[...], dq1_ref[...], dq2_ref[...])
        dkv = own_ref[...] + one_ref[...].astype(F32) + two_ref[...].astype(F32)
        turned = turn(dkv, cos_ref[...], -sin_ref[...])
        dqkv[:, 512:] = jnp.where(lane_is_low(dkv.shape, 128), turned, dkv).astype(BF16)

    x = x_ref[...]
    put_half(number, dot_tn(x, dqkv[:, 512:]).astype(BF16), other_grad_ref, own_grad_ref)
    dx = dot_nt(dqkv[...], w_ref[...])
    for piece in range(4):
        row = pl.multiple_of(lax.rem(core_ref[1] + piece, 4) * 128, 128)
        dx_ref[pl.ds(row, 128), :] = dx[128 * piece : 128 * piece + 128].astype(BF16)
    columns = pl.ds(pl.multiple_of(tile_at(number, core_ref) * 512, 512), 512)
    sums[:, columns] = jnp.broadcast_to(
        jnp.sum(dx * x.astype(F32), 0, keepdims=True) / norm_ref[:1], (8, 512)
    )

    @pl.when(number == 3)
    def _():
        gain_ref[:8] = gain_rows(to_blocks(sums[...])[:1])
        gain_ref[8:] = gain_rows(second_ref[:1])


def finish(core, normed, weights, dq, own, one, two, cosine, sine, gain, second):
    rows, width = normed.shape
    tile = 512
    whole = lambda i, c: (0, 0)
    column = lambda i, c: (0, tile_at(i, c))
    narrow = pl.BlockSpec((rows, 128), whole)
    grid = pltpu.PrefetchScalarGridSpec(
        num_scalar_prefetch=1,
        grid=(4,),
        in_specs=[
            pl.BlockSpec((rows, tile), column),
            pl.BlockSpec((tile, 640), lambda i, c: (tile_at(i, c), 0)),
            pl.BlockSpec((128, 512), whole),
            pl.BlockSpec((256, 512), whole),
            pl.BlockSpec((128, 512), whole),
            narrow,
            narrow,
            narrow,
            narrow,
            narrow,
            pl.BlockSpec((16, tile), column),
            pl.BlockSpec((8, width), whole),
        ],
        out_specs=half_specs(tile, 128)
        + (pl.BlockSpec((rows, tile), column),)
        + (pl.BlockSpec((GAIN_ROWS, GAIN_COLUMNS), whole),),
        scratch_shapes=[pltpu.VMEM((rows, 640), BF16), pltpu.VMEM((8, width), F32)],
    )
    result = pl.pallas_call(
        finish_kernel,
        grid_spec=grid,
        out_shape=(jax.ShapeDtypeStruct((width // 2, 128), BF16),) * 2
        + (jax.ShapeDtypeStruct((rows, width), BF16),)
        + (jax.ShapeDtypeStruct((GAIN_ROWS, GAIN_COLUMNS), F32),),
        compiler_params=pltpu.CompilerParams(vmem_limit_bytes=VMEM_LIMIT),
        cost_estimate=pl.CostEstimate(
            flops=2 * rows * width * 768, bytes_accessed=10 * 1024 * 1024, transcendentals=0
        ),
    )(core, normed, weights, *dq, own, one, two, cosine, sine, gain, second)
    return result


def per_device(
    tokens,
    segments,
    w_query,
    key_projection,
    value_projection,
    w_out,
    w_gate,
    w_up,
    w_down,
    norm_attn,
    norm_ffn,
    cotangent,
):
    place, core = lax.axis_index("head"), lax.axis_index("core")
    block = (lax.axis_index("y") * 4 + lax.axis_index("x")) * 2 + core
    place_array = place.astype(jnp.int32).reshape(1)
    core_array = core.astype(jnp.int32).reshape(1)
    core_place = jnp.stack([core, place]).astype(jnp.int32)
    keep = lax.optimization_barrier

    at = jnp.stack([lax.axis_index("x"), lax.axis_index("y"), core]).astype(jnp.int32)

    out_weights = lax.all_gather(
        jnp.concatenate([w_down.T, w_out.T], 1), CORE_FIRST, axis=0, tiled=True
    )
    ffn_weights = lax.all_gather(jnp.concatenate([w_gate, w_up], 1), CORE_FIRST, axis=0, tiled=True)

    x_rows, dy_rows, normed_rows, gain_one, gain_two = prepare(
        tokens[0],
        cotangent[0],
        jnp.broadcast_to(norm_attn[None], (16, 2048)),
        jnp.broadcast_to(norm_ffn[None], (16, 2048)),
    )
    normed_rows, w_query = keep((normed_rows, w_query))
    ahead, behind = near_pieces(normed_rows)
    qkv_own = gather_axis(jnp.concatenate([w_query, key_projection, value_projection], 1), "x")
    qkv_own = gather_axis(jnp.concatenate(qkv_own, 0), "y")
    far = far_pieces(ahead, behind)
    qkv_own, far = keep((qkv_own, far))
    qkv_own = jnp.concatenate(qkv_own, 0)
    qkv_pieces = qkv_own, shift(qkv_own, "core", 1)
    normed_one = jnp.concatenate([normed_rows, ahead, *far, behind], 0)
    dy_raw, far = keep((cotangent[0], far))
    dy_ahead, dy_behind = near_pieces(dy_raw)
    dy_far = far_pieces(dy_ahead, dy_behind)

    row = jnp.arange(512, dtype=jnp.int32)
    positions = block * 512 + ((row // 128 + place) % 4) * 128 + row % 128
    frequency = 10000.0 ** (-jnp.arange(32, dtype=F32) * 2.0 / HEAD_SIZE)
    angles = positions.astype(F32)[:, None] * frequency[None, :]
    cosine, sine = jnp.cos(angles), jnp.sin(angles)
    cosine = jnp.concatenate([cosine] * 4, 1)
    sine = jnp.concatenate([-sine, sine, -sine, sine], 1)

    (kv_own,) = project(
        project_kv_kernel, at, normed_one, qkv_pieces, cosine, sine, 128, 128, False
    )
    normed_late, kv_own = keep((normed_one, kv_own))
    kv = (from_block(kv_own, 2), from_block(kv_own, 1), kv_own)
    queries, qkv_weights = project(
        project_q_kernel, at, normed_late, qkv_pieces, cosine, sine, 512, 640, True
    )

    flat = segments.reshape(-1)
    padded = jnp.concatenate([jnp.full((1024,), -1, jnp.int32), flat])
    own = lax.dynamic_slice_in_dim(flat, block * 512, 512, 0)
    window = lax.dynamic_slice_in_dim(padded, block * 512, 1536, 0)
    start = jnp.sum((window[None, :] < own[:, None]).astype(jnp.int32), 1)
    low = jnp.maximum(start, row + 1).reshape(1, 512)

    kk, vv, kvt = set_up(place_array, kv)
    seen = place_array, queries, kk, kvt, low, out_weights
    o_far, lse_far, part_far = attend(2, 1, 1, *seen)
    queries, part_far = keep((queries, part_far))
    part_far = shift(part_far, "head", 2)
    seen = place_array, queries, kk, kvt, low, out_weights
    o_near, lse_near, part_ahead, part_behind = attend(1, 2, 2, *seen)
    queries, part_far, part_ahead, part_behind = keep((queries, part_far, part_ahead, part_behind))
    seen = place_array, queries, kk, kvt, low, out_weights
    o_own, lse_own, part_own = attend(0, 1, 1, *seen)
    o_own, dy_far = keep((o_own, dy_far))
    dy, dy_swap = assemble(core_array, dy_rows, dy_ahead, *dy_far, dy_behind)
    dy_other = shift(dy_swap, "core", 1)
    attention_sum = part_own, shift(part_ahead, "head", 1), shift(part_behind, "head", -1), part_far
    h1, normed_rows_two = join(x_rows, gain_two, attention_sum)
    ahead, far, behind = gather_pieces(normed_rows_two)
    dact = columns_times(dy, out_weights, 0)
    dact, dy_other = keep((dact, dy_other))

    gua, normed_two, normed_two_swap, dnormed_two = ffn(
        core_array, (normed_rows_two, ahead, far, behind), dact, ffn_weights
    )
    dnormed_two = scatter_pieces(*dnormed_two)
    gua_other = shift(gua, "core", 1)
    normed_two_other = shift(normed_two_swap, "core", 1)
    out_pieces = rows_times(gua, 2, out_weights, 0)
    gua_other, normed_two_other, out_pieces = keep((gua_other, normed_two_other, out_pieces))
    held = weight_grads(core_array, normed_two, normed_two_other, dy, dy_other, gua, gua_other)
    held, dnormed_two = keep((held, dnormed_two))
    grads = lax.psum_scatter(held, ("y", "x"), scatter_dimension=0, tiled=True)

    dh1, dh1_low, grad_gain_two = join_back(h1, dy_rows, gain_two, dnormed_two)
    back = kk, vv, kvt, low, cosine, sine
    dq_own, dk, dv = attend_back(0, 1, 1, place_array, queries, o_own, (dh1_low,), out_weights, lse_own, *back, ())
    ahead, behind = shift(dh1_low, "head", -1), shift(dh1_low, "head", 1)
    ahead, behind, dk, dv, dh1_late, out_pieces = keep((ahead, behind, dk, dv, dh1_low, out_pieces))
    far = shift(dh1_late, "head", 2)
    dq_near, dk, dv = attend_back(
        1, 2, 2, place_array, queries, o_near, (ahead, behind), out_weights, lse_near, *back, (dk, dv)
    )
    far, dk, dv, out_pieces = keep((far, dk, dv, out_pieces))
    out_pieces = scatter_pieces(*out_pieces)
    dq_far, dkv_first, dkv_second, dkv_own = attend_back(
        2, 1, 1, place_array, queries, o_far, (far,), out_weights, lse_far, *back, (dk, dv)
    )
    dq = dq_own, dq_near, dq_far
    dkv_one = from_block(dkv_second, -1)
    dkv_two = from_block(dkv_first, -2)
    wide_other, wide_own = wide_grads(
        core_array, normed_one, (dh1_low, ahead, far, behind), (o_own, o_near, o_far), dq
    )
    dkv_one, dkv_two, wide_other, out_pieces = keep((dkv_one, dkv_two, wide_other, out_pieces))
    wide_other = shift(wide_other, "core", 1)

    narrow_other, narrow_own, dnormed_one, gains = finish(
        core_place,
        normed_one,
        qkv_weights,
        dq,
        dkv_own,
        dkv_one,
        dkv_two,
        cosine,
        sine,
        gain_one,
        grad_gain_two,
    )
    dnormed_one = lax.psum_scatter(dnormed_one, "head", scatter_dimension=0, tiled=True)
    pieces, out_sums = first_pieces(
        at,
        wide_own,
        wide_other,
        narrow_own,
        shift(narrow_other, "core", 1),
        exchange([gains] * 4, "head"),
    )
    rows = [(x_rows.shape, BF16)]
    (output,) = small_call(output_kernel, rows, h1, *out_pieces)
    grads = (
        grads[:, :HIDDEN].astype(F32),
        grads[:, HIDDEN : 2 * HIDDEN].astype(F32),
        grads[:, 2 * HIDDEN :].T.astype(F32),
    )
    pieces, out_sums, output, grads = keep(
        (exchange(pieces, "x"), exchange(out_sums, "y"), output, grads)
    )
    pieces, out_sums = second_pieces(at, pieces, out_sums)
    (grad_inputs,) = small_call(input_grad_kernel, rows, dh1, x_rows, gain_one, dnormed_one)
    pieces, out_sums, grad_inputs = keep((exchange(pieces, "y"), exchange(out_sums, "x"), grad_inputs))
    (gains,) = small_call(gains_kernel, [((GAIN_ROWS, GAIN_COLUMNS), F32)], *pieces)
    columns = (64, 512), (64, 512), (64, 64), (64, 64), (1, 2048), (1, 2048)
    grad_out, grad_query, grad_key, grad_value, grad_gain_one, grad_gain_two = small_call(
        attention_grads_kernel,
        [(shape, F32) for shape in columns],
        *pieces,
        *out_sums,
        gains,
        shift(gains, "core", 1),
    )

    return (
        output[None],
        grad_inputs[None],
        grad_query,
        grad_key,
        grad_value,
        grad_out.T,
        *grads,
        grad_gain_one.reshape(2048),
        grad_gain_two.reshape(2048),
    )


def solution(mesh):
    grid = Mesh(mesh.devices.reshape(4, 4, 4, 2), ("head", "y", "x", "core"))
    rows, up, down = P(BLK, "head", None), P(BLK, "head"), P("head", BLK)
    return jax.shard_map(
        per_device,
        mesh=grid,
        in_specs=(rows, P(), up, up, up, down, up, up, down, P(), P(), rows),
        out_specs=(rows, rows, up, up, up, down, up, up, down, P(), P()),
        check_vma=False,
    )
```

```python
import functools

import jax
import jax.numpy as jnp
from jax import lax
from jax.experimental import pallas as pl
from jax.experimental.pallas import tpu as pltpu
from jax.sharding import Mesh
from jax.sharding import PartitionSpec as P

HEAD_SIZE = 64
WINDOW = 1024
HIDDEN = 1408
EPSILON = 1e-05
BF16 = jnp.bfloat16
F32 = jnp.float32
BLK = ("y", "x", "core")
CORE_FIRST = ("core", "y", "x")
VMEM_LIMIT = 63 * 1024 * 1024


def dot_nn(a, b):
    return jnp.dot(a, b, preferred_element_type=F32)


def dot_nt(a, b):
    return lax.dot_general(a, b, (((1,), (1,)), ((), ())), preferred_element_type=F32)


def dot_tn(a, b):
    return lax.dot_general(a, b, (((0,), (0,)), ((), ())), preferred_element_type=F32)


def shift(value, axis, distance):
    size = lax.axis_size(axis)
    return lax.ppermute(value, axis, [(i, (i + distance) % size) for i in range(size)])


def add_low(a, b):
    return (a.astype(F32) + b.astype(F32)).astype(BF16)


def gather_pieces(rows):
    return shift(rows, "head", -1), shift(rows, "head", 2), shift(rows, "head", 1)


def near_pieces(rows):
    return shift(rows, "head", -1), shift(rows, "head", 1)


def far_pieces(ahead, behind):
    half = ahead.shape[0] // 2
    return shift(behind[:half], "head", 1), shift(ahead[half:], "head", -1)


def scatter_pieces(own, ahead, far, behind):
    return own, shift(ahead, "head", 1), shift(behind, "head", -1), shift(far, "head", 2)


def gather_axis(value, axis):
    return value, shift(value, axis, -1), shift(value, axis, 2), shift(value, axis, 1)


def exchange(pieces, axis):
    return pieces[0], shift(pieces[1], axis, 1), shift(pieces[2], axis, 2), shift(pieces[3], axis, -1)


def from_block(value, distance):
    route = [(i, i + distance) for i in range(32) if 0 <= i + distance < 32]
    return lax.ppermute(value, BLK, route)


def scale_of(values):
    return lax.rsqrt(jnp.mean(values * values, -1, keepdims=True) + EPSILON)


def lane_is_low(shape, period):
    return lax.broadcasted_iota(jnp.int32, shape, len(shape) - 1) % period < period // 2


def turn(values, cosine, sine):
    swapped = jnp.where(
        lane_is_low(values.shape, 64), pltpu.roll(values, 96, 1), pltpu.roll(values, 32, 1)
    )
    return values * cosine + swapped * sine


def core_major_tiles(tiles):
    low = lane_is_low(tiles[0].shape, 128)
    rolled = [pltpu.roll(tile, 64, 1) for tile in tiles]
    first = [jnp.where(low, tiles[2 * k], rolled[2 * k + 1]) for k in range(8)]
    second = [jnp.where(low, rolled[2 * k], tiles[2 * k + 1]) for k in range(8)]
    return first + second


def block_major_tiles(tiles):
    low = lane_is_low(tiles[0].shape, 128)
    rolled = [pltpu.roll(tile, 64, 1) for tile in tiles]
    result = []
    for k in range(8):
        result.append(jnp.where(low, tiles[k], rolled[8 + k]))
        result.append(jnp.where(low, rolled[k], tiles[8 + k]))
    return result


def in_tiles(value):
    return [value[:, 128 * k : 128 * k + 128] for k in range(16)]


def prepare_kernel(x_ref, dy_ref, gain_ref, x_out, dy_out, normed_out, gain_out):
    def convert(ref):
        return jnp.concatenate(core_major_tiles(in_tiles(ref[...].astype(F32))), 1)

    x, gains = convert(x_ref), convert(gain_ref)
    gain_out[...] = gains
    x_out[...] = x
    dy_out[...] = convert(dy_ref).astype(BF16)
    normed_out[...] = (x * scale_of(x) * gains[:1]).astype(BF16)


def prepare(x, dy, gains):
    rows, width = x.shape
    return pl.pallas_call(
        prepare_kernel,
        out_shape=(
            jax.ShapeDtypeStruct((rows, width), F32),
            jax.ShapeDtypeStruct((rows, width), BF16),
            jax.ShapeDtypeStruct((rows, width), BF16),
            jax.ShapeDtypeStruct(gains.shape, F32),
        ),
        compiler_params=pltpu.CompilerParams(vmem_limit_bytes=VMEM_LIMIT),
        cost_estimate=pl.CostEstimate(
            flops=10 * rows * width, bytes_accessed=10 * rows * width, transcendentals=rows
        ),
    )(x, dy, gains)


def to_blocks(value):
    return jnp.concatenate(block_major_tiles(in_tiles(value)), 1)


def assemble_kernel(core_ref, own_ref, ahead_ref, top_ref, bottom_ref, behind_ref, out_ref, swap_ref):
    out_ref[:128] = own_ref[...]
    start = 128
    for ref in (ahead_ref, top_ref, bottom_ref, behind_ref):
        size = ref.shape[0]
        out_ref[start : start + size] = jnp.concatenate(
            core_major_tiles(in_tiles(ref[...].astype(F32))), 1
        ).astype(BF16)
        start += size
    swap_ref[...] = jnp.where(core_ref[0] == 0, out_ref[:, 1024:], out_ref[:, :1024])


def assemble(core, own, ahead, far_top, far_bottom, behind):
    vmem = pl.BlockSpec(memory_space=pltpu.VMEM)
    return pl.pallas_call(
        assemble_kernel,
        out_shape=(jax.ShapeDtypeStruct((512, 2048), BF16), jax.ShapeDtypeStruct((512, 1024), BF16)),
        in_specs=[pl.BlockSpec(memory_space=pltpu.SMEM)] + [vmem] * 5,
        out_specs=(vmem, vmem),
        compiler_params=pltpu.CompilerParams(vmem_limit_bytes=VMEM_LIMIT),
        cost_estimate=pl.CostEstimate(
            flops=4 * 512 * 2048, bytes_accessed=5 * 1024 * 1024, transcendentals=0
        ),
    )(core, own, ahead, far_top, far_bottom, behind)


def small_call(kernel, out_shape, *operands):
    return pl.pallas_call(
        kernel,
        out_shape=tuple(jax.ShapeDtypeStruct(shape, dtype) for shape, dtype in out_shape),
        compiler_params=pltpu.CompilerParams(vmem_limit_bytes=VMEM_LIMIT),
        cost_estimate=pl.CostEstimate(
            flops=sum(x.size for x in operands),
            bytes_accessed=2 * sum(x.size * x.dtype.itemsize for x in operands),
            transcendentals=0,
        ),
    )(*operands)


def total_of(refs):
    values = [ref[...].astype(F32) for ref in refs]
    while len(values) > 1:
        values = [values[0] + values[1]] + values[2:]
    return values[0]


def join_kernel(x_ref, gain_ref, a_ref, b_ref, c_ref, d_ref, h_out, normed_out):
    h = x_ref[...] + total_of((a_ref, b_ref, c_ref, d_ref))
    h_out[...] = h
    normed_out[...] = (h * scale_of(h) * gain_ref[1:2]).astype(BF16)


def join(x, gain, pieces):
    return small_call(join_kernel, ((x.shape, F32), (x.shape, BF16)), x, gain, *pieces)


def norm_backward(values, gain, grad):
    scale = scale_of(values)
    weighted = grad * gain
    inner = jnp.mean(weighted * values, -1, keepdims=True)
    return scale * weighted - values * (scale * scale * scale * inner), scale


def join_back_kernel(h_ref, dy_ref, gain_ref, a_ref, b_ref, c_ref, d_ref, dh_out, low_out, grad_out):
    h, grad = h_ref[...], total_of((a_ref, b_ref, c_ref, d_ref))
    back, scale = norm_backward(h, gain_ref[1:2], grad)
    dh = dy_ref[...].astype(F32) + back
    dh_out[...] = dh
    low_out[...] = dh.astype(BF16)
    grad_out[...] = to_blocks(jnp.broadcast_to(jnp.sum(grad * h * scale, 0, keepdims=True), (8, h.shape[1])))


def join_back(h, dy, gain, pieces):
    shapes = (h.shape, F32), (h.shape, BF16), ((8, h.shape[1]), F32)
    return small_call(join_back_kernel, shapes, h, dy, gain, *pieces)


def output_kernel(h_ref, a_ref, b_ref, c_ref, d_ref, out_ref):
    out_ref[...] = to_blocks(h_ref[...] + total_of((a_ref, b_ref, c_ref, d_ref))).astype(BF16)


def input_grad_kernel(dh_ref, x_ref, gain_ref, grad_ref, out_ref):
    back, _ = norm_backward(x_ref[...], gain_ref[:1], grad_ref[...].astype(F32))
    out_ref[...] = to_blocks(dh_ref[...] + back).astype(BF16)


GAIN_ROWS, GAIN_COLUMNS = 16, 256


def gain_rows(vector):
    return jnp.concatenate([vector[:, 256 * k : 256 * k + 256] for k in range(8)], 0)


def put_piece(ref, rows, gains):
    count = rows.shape[0]
    ref[:count] = rows
    ref[count:, GAIN_COLUMNS:] = jnp.zeros((GAIN_ROWS, ref.shape[1] - GAIN_COLUMNS), BF16)
    ref[count:, :GAIN_COLUMNS] = gains.astype(BF16)


def first_pieces_kernel(
    at_ref, q_ref, q2_ref, kv_ref, kv2_ref, o_ref, o2_ref, *refs
):
    gain_refs, out_refs = refs[:4], refs[4:]
    query = add_low(q_ref[...], q2_ref[...]).reshape(256, 512)
    narrow = add_low(kv_ref[...], kv2_ref[...]).reshape(256, 128)
    rows = jnp.concatenate([query, narrow], 1)
    out_rows = add_low(o_ref[...], o2_ref[...]).reshape(256, 512)
    gains = total_of(gain_refs)
    for number in range(4):

        @pl.when(pl.program_id(0) == number)
        def _():
            put_piece(out_refs[number], rows, gains)
            out_refs[4 + number][...] = out_rows


def first_pieces(at, wide, wide2, narrow, narrow2, gains):
    pick_x = lambda column: lambda d, s: (0, lax.rem(s[0] + d, 4), 0, column)
    pick_y = lambda d, s: (lax.rem(s[1] + d, 4), 0, 0, 0)
    whole = lambda d, s: (0, 0)
    shaped = lambda value: value.reshape(4, 4, 64, value.shape[1])
    shapes = [(256 + GAIN_ROWS, 640)] * 4 + [(256, 512)] * 4
    grid = pltpu.PrefetchScalarGridSpec(
        num_scalar_prefetch=1,
        grid=(4,),
        in_specs=[pl.BlockSpec((4, 1, 64, 512), pick_x(1))] * 2
        + [pl.BlockSpec((4, 1, 64, 128), pick_x(0))] * 2
        + [pl.BlockSpec((1, 4, 64, 512), pick_y)] * 2
        + [pl.BlockSpec((GAIN_ROWS, GAIN_COLUMNS), whole)] * 4,
        out_specs=tuple(pl.BlockSpec(shape, whole) for shape in shapes),
    )
    wide, wide2 = shaped(wide), shaped(wide2)
    result = pl.pallas_call(
        first_pieces_kernel,
        grid_spec=grid,
        out_shape=tuple(jax.ShapeDtypeStruct(shape, BF16) for shape in shapes),
        compiler_params=pltpu.CompilerParams(vmem_limit_bytes=VMEM_LIMIT),
        cost_estimate=pl.CostEstimate(
            flops=2 * 1024 * 1152, bytes_accessed=6 * 1024 * 1152, transcendentals=0
        ),
    )(at, wide, wide2, shaped(narrow), shaped(narrow2), wide, wide2, *gains)
    return result[:4], result[4:]


def second_pieces_kernel(at_ref, *refs):
    qkv, out, (held, out_held) = refs[:4], refs[4:8], refs[16:]
    held[...] = total_of(qkv)
    out_held[...] = total_of(out).astype(BF16)
    for number in range(4):
        y = pl.multiple_of(lax.rem(at_ref[1] + number, 4) * 64, 64)
        put_piece(refs[8 + number], held[pl.ds(y, 64), :].astype(BF16), held[256:, :GAIN_COLUMNS])
        x = pl.multiple_of(lax.rem(at_ref[0] + number, 4) * 64, 64)
        refs[12 + number][...] = out_held[pl.ds(x, 64), :]


def second_pieces(at, qkv, out):
    vmem = pl.BlockSpec(memory_space=pltpu.VMEM)
    shapes = [(64 + GAIN_ROWS, 640)] * 4 + [(64, 512)] * 4
    result = pl.pallas_call(
        second_pieces_kernel,
        out_shape=tuple(jax.ShapeDtypeStruct(shape, BF16) for shape in shapes),
        in_specs=[pl.BlockSpec(memory_space=pltpu.SMEM)] + [vmem] * 8,
        out_specs=(vmem,) * 8,
        scratch_shapes=[pltpu.VMEM((256 + GAIN_ROWS, 640), F32), pltpu.VMEM((256, 512), BF16)],
        compiler_params=pltpu.CompilerParams(vmem_limit_bytes=VMEM_LIMIT),
        cost_estimate=pl.CostEstimate(
            flops=4 * 272 * 1152, bytes_accessed=10 * 272 * 1152, transcendentals=0
        ),
    )(at, *qkv, *out)
    return result[:4], result[4:]


def gains_kernel(a_ref, b_ref, c_ref, d_ref, out_ref):
    values = [ref[64:, :GAIN_COLUMNS].astype(F32) for ref in (a_ref, b_ref, c_ref, d_ref)]
    out_ref[...] = (values[0] + values[1]) + (values[2] + values[3])


def attention_grads_kernel(*refs):
    out_ref, q_ref, k_ref, v_ref, one_ref, two_ref = refs[10:]
    total = total_of(refs[:4])
    out_ref[...] = total_of(refs[4:8])
    q_ref[...] = total[:64, :512]
    k_ref[...] = total[:64, 512:576]
    v_ref[...] = total[:64, 576:]
    gains = total_of(refs[8:10])
    one_ref[...] = jnp.concatenate([gains[k : k + 1] for k in range(8)], 1)
    two_ref[...] = jnp.concatenate([gains[k : k + 1] for k in range(8, 16)], 1)


def put_in_order(at_ref, own_ref, other_ref, columns, to_ref, sems):
    x, y, core = at_ref[0], at_ref[1], at_ref[2]
    copies = []
    for number in range(32):
        ref = (own_ref, other_ref)[number // 16]
        to_x, to_y = lax.rem(x + number % 4, 4), lax.rem(y + number // 4 % 4, 4)
        to_core = core if number < 16 else 1 - core
        row = pl.multiple_of(((to_core * 4 + to_y) * 4 + to_x) * 64, 64)
        copy = pltpu.make_async_copy(
            ref.at[pl.ds(number % 16 * 64, 64), columns], to_ref.at[pl.ds(row, 64)], sems.at[number]
        )
        copy.start()
        copies.append(copy)
    return copies


def project_kv_kernel(at_ref, x_ref, own_ref, other_ref, cos_ref, sin_ref, kv_ref, held, sems):
    for copy in put_in_order(at_ref, own_ref, other_ref, pl.ds(512, 128), held, sems):
        copy.wait()
    flat = dot_nn(x_ref[...], held[...])
    turned = turn(flat, cos_ref[...], sin_ref[...])
    kv_ref[...] = jnp.where(lane_is_low(flat.shape, 128), turned, flat).astype(BF16)


def project_q_kernel(at_ref, x_ref, own_ref, other_ref, cos_ref, sin_ref, q_ref, w_ref, held, sems, sem):
    for copy in put_in_order(at_ref, own_ref, other_ref, pl.ds(0, 640), held, sems):
        copy.wait()
    whole = pltpu.make_async_copy(held, w_ref, sem)
    whole.start()
    cosine, sine, x = cos_ref[...], sin_ref[...], x_ref[...]
    for start in (0, 256):
        wide = dot_nn(x, held[:, start : start + 256])
        for part in (0, 128):
            turned = turn(wide[:, part : part + 128], cosine, sine)
            q_ref[:, start + part : start + part + 128] = (turned * HEAD_SIZE**-0.5).astype(BF16)
    whole.wait()


def project(kernel, at, normed, weights, cosine, sine, columns, held_columns, hand_out):
    rows, width = normed.shape
    vmem, anywhere = pl.BlockSpec(memory_space=pltpu.VMEM), pl.BlockSpec(memory_space=pl.ANY)
    out_shape = [jax.ShapeDtypeStruct((rows, columns), BF16)]
    out_specs = [vmem]
    scratch = [pltpu.VMEM((width, held_columns), BF16), pltpu.SemaphoreType.DMA((32,))]
    if hand_out:
        out_shape.append(jax.ShapeDtypeStruct((width, held_columns), BF16))
        out_specs.append(anywhere)
        scratch.append(pltpu.SemaphoreType.DMA)
    return pl.pallas_call(
        kernel,
        out_shape=tuple(out_shape),
        in_specs=[pl.BlockSpec(memory_space=pltpu.SMEM), vmem, anywhere, anywhere, vmem, vmem],
        out_specs=tuple(out_specs),
        scratch_shapes=scratch,
        compiler_params=pltpu.CompilerParams(vmem_limit_bytes=VMEM_LIMIT),
        cost_estimate=pl.CostEstimate(
            flops=2 * rows * width * columns,
            bytes_accessed=2 * (rows * width + width * columns + rows * columns),
            transcendentals=0,
        ),
    )(at, normed, *weights, cosine, sine)


KEYS = 1152
PAIRS = 4


def set_up_kernel(place_ref, kv0_ref, kv1_ref, kv2_ref, kk_ref, vv_ref, kvt_ref):
    place = place_ref[0]
    low = lane_is_low((128, 128), 128)
    for block, ref in enumerate((kv0_ref, kv1_ref, kv2_ref)):
        for group in range(4):
            at = pl.multiple_of(lax.rem(group - place + 4, 4) * 128, 128)
            piece = ref[pl.ds(at, 128), :].astype(F32)
            rolled = pltpu.roll(piece, 64, 1)
            to = block * 512 + group * 128
            kk_ref[to : to + 128, :] = jnp.where(low, piece, rolled).astype(BF16)
            vv_ref[to : to + 128, :] = jnp.where(low, rolled, piece).astype(BF16)
            kvt_ref[:, to : to + 128] = piece.T.astype(BF16)


def set_up(place, kv):
    vmem = pl.BlockSpec(memory_space=pltpu.VMEM)
    return pl.pallas_call(
        set_up_kernel,
        out_shape=(
            jax.ShapeDtypeStruct((1536, 128), BF16),
            jax.ShapeDtypeStruct((1536, 128), BF16),
            jax.ShapeDtypeStruct((128, 1536), BF16),
        ),
        in_specs=[pl.BlockSpec(memory_space=pltpu.SMEM), vmem, vmem, vmem],
        out_specs=(vmem, vmem, vmem),
        compiler_params=pltpu.CompilerParams(vmem_limit_bytes=VMEM_LIMIT),
        cost_estimate=pl.CostEstimate(flops=1536 * 128 * 8, bytes_accessed=2 * 1024 * 1024, transcendentals=0),
    )(place, *kv)


def both_heads(pair):
    low = lane_is_low(pair.shape, 128)
    nothing = jnp.zeros_like(pair)
    return jnp.concatenate([jnp.where(low, pair, nothing), jnp.where(low, nothing, pair)], 0)


def side_by_side(transposed):
    return jnp.concatenate([transposed[:, :128], transposed[:, 128:]], 0).T


def mask_of(at, low_ref):
    key = lax.broadcasted_iota(jnp.int32, (KEYS, 128), 0)
    query = lax.broadcasted_iota(jnp.int32, (KEYS, 128), 1)
    seen = (key >= low_ref[:, pl.ds(at, 128)] - at) & (key <= query + WINDOW)
    bias = jnp.where(seen, 0.0, -jnp.inf)
    return jnp.concatenate([bias, bias], 1)


def attend_kernel(
    first, step, place_ref, q_ref, kk_ref, kvt_ref, low_ref, w_ref, o_ref, lse_ref, *refs
):
    part_refs, (bias, held, w_held, sem) = refs[:-4], refs[-4:]
    group = lax.rem(place_ref[0] + first + step * pl.program_id(0), 4)
    at = pl.multiple_of(group * 128, 128)

    load = pltpu.make_async_copy(w_ref.at[:, pl.ds(HIDDEN, 512)], w_held, sem)

    @pl.when((pl.program_id(0) == 0) & (pl.program_id(1) == 0))
    def _():
        load.start()

    @pl.when(pl.program_id(1) == 0)
    def _():
        bias[...] = mask_of(at, low_ref)

    keys = pl.ds(at, KEYS)
    for number in range(PAIRS):
        columns = slice(128 * number, 128 * number + 128)
        scores = dot_nt(kk_ref[keys, :], both_heads(q_ref[:, columns])) + bias[...]
        top = jnp.max(scores, 0, keepdims=True)
        weights = jnp.exp(scores - top)
        total = jnp.sum(weights, 0, keepdims=True)
        result = dot_nn(kvt_ref[64:128, keys], weights.astype(BF16)) / total
        lse_ref[0, number] = top + jnp.log(total)
        result = side_by_side(result).astype(BF16)
        o_ref[:, columns] = result
        held[PAIRS * pl.program_id(1) + number] = result

    @pl.when(pl.program_id(1) == 4 // PAIRS - 1)
    def _():
        @pl.when(pl.program_id(0) == 0)
        def _():
            load.wait()

        rows = jnp.concatenate([held[k] for k in range(4)], 1)
        part = dot_nt(rows, w_held[...]).astype(BF16)
        for number, ref in enumerate(part_refs):

            @pl.when(pl.program_id(0) == number)
            def _():
                ref[...] = part


def attend(first, step, count, place, queries, kk, kvt, low, weights):
    whole = lambda g, p, s: (0, 0)
    width = 128 * PAIRS
    grid = pltpu.PrefetchScalarGridSpec(
        num_scalar_prefetch=1,
        grid=(count, 4 // PAIRS),
        in_specs=[
            pl.BlockSpec((128, width), lambda g, p, s: (first + step * g, p)),
            pl.BlockSpec((1536, 128), whole),
            pl.BlockSpec((128, 1536), whole),
            pl.BlockSpec((1, 512), whole),
            pl.BlockSpec(memory_space=pl.ANY),
        ],
        out_specs=(
            pl.BlockSpec((128, width), lambda g, p, s: (g, p)),
            pl.BlockSpec((1, PAIRS, 1, 256), lambda g, p, s: (g, p, 0, 0)),
        )
        + (pl.BlockSpec((128, 2048), whole),) * count,
        scratch_shapes=[
            pltpu.VMEM((KEYS, 256), F32),
            pltpu.VMEM((4, 128, 128), BF16),
            pltpu.VMEM((2048, 512), BF16),
            pltpu.SemaphoreType.DMA,
        ],
    )
    return pl.pallas_call(
        functools.partial(attend_kernel, first, step),
        grid_spec=grid,
        out_shape=(
            jax.ShapeDtypeStruct((128 * count, 512), BF16),
            jax.ShapeDtypeStruct((count, 4, 1, 256), F32),
        )
        + (jax.ShapeDtypeStruct((128, 2048), BF16),) * count,
        compiler_params=pltpu.CompilerParams(vmem_limit_bytes=VMEM_LIMIT),
        cost_estimate=pl.CostEstimate(
            flops=count * 4 * KEYS * 256 * 256 * 2,
            bytes_accessed=3 * 1024 * 1024,
            transcendentals=count * 4 * KEYS * 256,
        ),
    )(place, queries, kk, kvt, low, weights)


def attend_back_kernel(first, step, count, *refs):
    last = first == 2
    place_ref, q_ref, w_ref, lse_ref, kk_ref, vv_ref, kvt_ref, low_ref, cos_ref, sin_ref = refs[:10]
    o_ref = refs[10]
    dh_refs, refs = refs[11 : 11 + count], refs[11 + count :]
    dk_in = dv_in = None
    if first > 0:
        dk_in, dv_in, refs = refs[0], refs[1], refs[2:]
    bias, do_held, dk, dv, w_held, sem = refs[-6:]
    dq_ref, outs = refs[0], refs[1:-6]
    number, pair = pl.program_id(0), pl.program_id(1)
    place = place_ref[0]
    at = pl.multiple_of(lax.rem(place + first + step * number, 4) * 128, 128)

    load = pltpu.make_async_copy(w_ref.at[:, pl.ds(HIDDEN, 512)], w_held, sem)

    @pl.when((number == 0) & (pair == 0))
    def _():
        load.start()
        dk[...] = jnp.zeros_like(dk) if dk_in is None else dk_in[...]
        dv[...] = jnp.zeros_like(dv) if dv_in is None else dv_in[...]

    @pl.when(pair == 0)
    def _():
        bias[...] = mask_of(at, low_ref)

        @pl.when(number == 0)
        def _():
            load.wait()

        for k, ref in enumerate(dh_refs):

            @pl.when(number == k)
            def _():
                do_rows = dot_nn(ref[...], w_held[...]).astype(BF16)
                for p in range(4):
                    do_held[p] = do_rows[:, 128 * p : 128 * p + 128]

    keys = pl.ds(at, KEYS)
    queries, grads, all_weights, all_grad_scores = [], [], [], []
    for k in range(PAIRS):
        columns = slice(128 * k, 128 * k + 128)
        do_pair = do_held[PAIRS * pair + k]
        query, grad = both_heads(q_ref[:, columns]), both_heads(do_pair)
        scores = dot_nt(kk_ref[keys, :], query) + bias[...]
        weights = jnp.exp(scores - lse_ref[0, k])
        grad_weights = dot_nt(vv_ref[keys, :], grad)
        product = (o_ref[:, columns].astype(F32) * do_pair.astype(F32)).T
        inner = jnp.concatenate(
            [jnp.sum(product[:64], 0, keepdims=True), jnp.sum(product[64:], 0, keepdims=True)], 1
        )
        grad_scores = (weights * (grad_weights - inner)).astype(BF16)
        grad_query = side_by_side(dot_nn(kvt_ref[0:64, keys], grad_scores)) * HEAD_SIZE**-0.5
        dq_ref[:, columns] = turn(grad_query, cos_ref[...], -sin_ref[...]).astype(BF16)
        queries.append(query)
        grads.append(grad)
        all_weights.append(weights.astype(BF16))
        all_grad_scores.append(grad_scores)
    join = lambda values, axis: values[0] if PAIRS == 1 else jnp.concatenate(values, axis)
    dv[keys, :] += dot_nn(join(all_weights, 1), join(grads, 0))
    dk[keys, :] += dot_nn(join(all_grad_scores, 1), join(queries, 0))

    @pl.when((number == pl.num_programs(0) - 1) & (pair == 4 // PAIRS - 1))
    def _():
        if not last:
            outs[0][...], outs[1][...] = dk[...], dv[...]
            return
        half = lane_is_low((128, 128), 128)
        for block in range(3):
            for group in range(4):
                to = pl.multiple_of(lax.rem(group - place + 4, 4) * 128, 128)
                frm = slice(block * 512 + group * 128, block * 512 + group * 128 + 128)
                key, value = dk[frm, :], dv[frm, :]
                key = key + pltpu.roll(key, 64, 1)
                value = value + pltpu.roll(value, 64, 1)
                both = jnp.where(half, key, value)
                outs[block][pl.ds(to, 128), :] = both.astype(outs[block].dtype)


def attend_back(first, step, count, place, queries, o, dh, weights, lse, kk, vv, kvt, low, cosine, sine, held):
    last = first == 2
    whole = lambda g, p, s: (0, 0)
    specs = [
        pl.BlockSpec((128, 128 * PAIRS), lambda g, p, s: (first + step * g, p)),
        pl.BlockSpec(memory_space=pl.ANY),
        pl.BlockSpec((1, PAIRS, 1, 256), lambda g, p, s: (g, p, 0, 0)),
        pl.BlockSpec((1536, 128), whole),
        pl.BlockSpec((1536, 128), whole),
        pl.BlockSpec((128, 1536), whole),
        pl.BlockSpec((1, 512), whole),
        pl.BlockSpec((128, 128), lambda g, p, s: (first + step * g, 0)),
        pl.BlockSpec((128, 128), lambda g, p, s: (first + step * g, 0)),
    ]
    specs += [pl.BlockSpec((128, 128 * PAIRS), lambda g, p, s: (g, p))]
    specs += [pl.BlockSpec((128, 2048), whole)] * count + [pl.BlockSpec((1536, 128), whole)] * len(held)
    if last:
        out_specs = (pl.BlockSpec((512, 128), whole),) * 3
        out_shape = tuple(jax.ShapeDtypeStruct((512, 128), dtype) for dtype in (BF16, BF16, F32))
    else:
        out_specs = (pl.BlockSpec((1536, 128), whole),) * 2
        out_shape = (jax.ShapeDtypeStruct((1536, 128), F32),) * 2
    grid = pltpu.PrefetchScalarGridSpec(
        num_scalar_prefetch=1,
        grid=(count, 4 // PAIRS),
        in_specs=specs,
        out_specs=(pl.BlockSpec((128, 128 * PAIRS), lambda g, p, s: (g, p)),) + out_specs,
        scratch_shapes=[
            pltpu.VMEM((KEYS, 256), F32),
            pltpu.VMEM((4, 128, 128), BF16),
            pltpu.VMEM((1536, 128), F32),
            pltpu.VMEM((1536, 128), F32),
            pltpu.VMEM((2048, 512), BF16),
            pltpu.SemaphoreType.DMA,
        ],
    )
    return pl.pallas_call(
        functools.partial(attend_back_kernel, first, step, count),
        grid_spec=grid,
        out_shape=(jax.ShapeDtypeStruct((128 * count, 512), BF16),) + out_shape,
        compiler_params=pltpu.CompilerParams(vmem_limit_bytes=VMEM_LIMIT),
        cost_estimate=pl.CostEstimate(
            flops=count * 4 * KEYS * 256 * 640 * 2,
            bytes_accessed=6 * 1024 * 1024,
            transcendentals=count * 4 * KEYS * 256,
        ),
    )(place, queries, weights, lse, kk, vv, kvt, low, cosine, sine, o, *dh, *held)


GROUPS = [(0, 128), (128, 256), (384, 512), (896, 512)]


def columns_times_kernel(left_ref, right_ref, out_ref):
    out_ref[...] = dot_nn(left_ref[...], right_ref[...])


def columns_times(left, right, part):
    rows, width = left.shape
    return pl.pallas_call(
        columns_times_kernel,
        out_shape=jax.ShapeDtypeStruct((rows, HIDDEN), F32),
        grid=(1,),
        in_specs=[
            pl.BlockSpec((rows, width), lambda i: (0, 0)),
            pl.BlockSpec((width, HIDDEN), lambda i: (0, part)),
        ],
        out_specs=pl.BlockSpec((rows, HIDDEN), lambda i: (0, 0)),
        compiler_params=pltpu.CompilerParams(vmem_limit_bytes=VMEM_LIMIT),
        cost_estimate=pl.CostEstimate(
            flops=2 * rows * width * HIDDEN, bytes_accessed=11 * 1024 * 1024, transcendentals=0
        ),
    )(left, right)


PIECES = [(0, 128), (128, 128), (256, 128), (384, 128)]


def ffn_kernel(*refs):
    core_ref, x_refs, dact_ref, w_ref = refs[0], refs[1:5], refs[5], refs[6]
    gua_ref, whole_ref, swap_ref, dx_refs = refs[7], refs[8], refs[9], refs[10:14]
    x_held, dact_held, w_held, gua, dx, sems, out_sems = refs[14:]
    x_copies = []
    for number, (start, size) in enumerate(PIECES):
        copy = pltpu.make_async_copy(
            x_refs[number], x_held.at[pl.ds(start, size)], sems.at[12 + number]
        )
        copy.start()
        x_copies.append(copy)
    copies = []
    for number, (start, width) in enumerate(GROUPS):
        for part in range(3):
            if part < 2:
                columns = pl.ds(part * HIDDEN + start, width)
                copy = pltpu.make_async_copy(
                    w_ref.at[:, columns], w_held.at[:, columns], sems.at[3 * number + part]
                )
            else:
                columns = pl.ds(start, width)
                copy = pltpu.make_async_copy(
                    dact_ref.at[:, columns], dact_held.at[:, columns], sems.at[3 * number + part]
                )
            copy.start()
            copies.append(copy)
    for copy in x_copies:
        copy.wait()
    half = pl.multiple_of((1 - core_ref[0]) * 1024, 1024)
    results = [
        pltpu.make_async_copy(x_held, whole_ref, out_sems.at[5]),
        pltpu.make_async_copy(x_held.at[:, pl.ds(half, 1024)], swap_ref, out_sems.at[6]),
    ]
    for copy in results:
        copy.start()
    x = x_held[...]
    for number, (start, width) in enumerate(GROUPS):
        for part in range(3):
            copies[3 * number + part].wait()
        gate = dot_nn(x, w_held[:, start : start + width])
        up = dot_nn(x, w_held[:, HIDDEN + start : HIDDEN + start + width])
        dact = dact_held[:, start : start + width]
        sig = jax.nn.sigmoid(gate)
        silu = gate * sig
        dgate = dact * up * (sig * (1.0 + gate * (1.0 - sig)))
        gua[:, start : start + width] = dgate.astype(BF16)
        gua[:, HIDDEN + start : HIDDEN + start + width] = (dact * silu).astype(BF16)
        gua[:, 2 * HIDDEN + start : 2 * HIDDEN + start + width] = (silu * up).astype(BF16)
    copy = pltpu.make_async_copy(gua, gua_ref, out_sems.at[4])
    copy.start()
    results.append(copy)
    dgu = gua[:, : 2 * HIDDEN]
    for number in range(4):
        columns = slice(512 * number, 512 * number + 512)
        dx[:, columns] = dot_nt(dgu, w_held[columns, : 2 * HIDDEN]).astype(BF16)
    for number, (start, size) in enumerate(PIECES):
        copy = pltpu.make_async_copy(dx.at[pl.ds(start, size)], dx_refs[number], out_sems.at[number])
        copy.start()
        results.append(copy)
    for copy in results:
        copy.wait()


def ffn(core, pieces, dact, weights):
    rows, width = dact.shape[0], weights.shape[0]
    anywhere = pl.BlockSpec(memory_space=pl.ANY)
    result = pl.pallas_call(
        ffn_kernel,
        out_shape=(
            jax.ShapeDtypeStruct((rows, 3 * HIDDEN), BF16),
            jax.ShapeDtypeStruct((rows, width), BF16),
            jax.ShapeDtypeStruct((rows, width // 2), BF16),
            *(jax.ShapeDtypeStruct((size, width), BF16) for _, size in PIECES),
        ),
        in_specs=[pl.BlockSpec(memory_space=pltpu.SMEM)] + [anywhere] * 6,
        out_specs=(anywhere,) * 7,
        scratch_shapes=[
            pltpu.VMEM((rows, width), BF16),
            pltpu.VMEM((rows, HIDDEN), F32),
            pltpu.VMEM((width, 2 * HIDDEN), BF16),
            pltpu.VMEM((rows, 3 * HIDDEN), BF16),
            pltpu.VMEM((rows, width), BF16),
            pltpu.SemaphoreType.DMA((16,)),
            pltpu.SemaphoreType.DMA((7,)),
        ],
        compiler_params=pltpu.CompilerParams(vmem_limit_bytes=VMEM_LIMIT),
        cost_estimate=pl.CostEstimate(
            flops=8 * rows * width * HIDDEN,
            bytes_accessed=25 * 1024 * 1024,
            transcendentals=rows * HIDDEN,
        ),
    )(core, *pieces, dact, weights)
    return result[0], result[1], result[2], result[3:]


def weight_grads_kernel(core_ref, x_ref, x2_ref, dy_ref, dy2_ref, right_ref, right2_ref, out_ref):
    part = pl.program_id(0)

    @pl.when(part < 2)
    def _():
        total = dot_tn(x_ref[...], right_ref[...]) + dot_tn(x2_ref[...], right2_ref[...])
        out_ref[...] = total.astype(BF16)

    @pl.when(part == 2)
    def _():
        total = dot_tn(dy_ref[...], right_ref[...]) + dot_tn(dy2_ref[...], right2_ref[...])
        out_ref[...] = total.astype(BF16)


def weight_grads(core, x, x2, dy, dy2, right, right2):
    rows = x.shape[0]
    tile = 1024
    half = x2.shape[1]
    tiles = half // tile
    own = lambda j, i, c: (0, c[0] * tiles + i)
    other = lambda j, i, c: (0, i)
    side = lambda j, i, c: (0, j)
    grid = pltpu.PrefetchScalarGridSpec(
        num_scalar_prefetch=1,
        grid=(3, tiles),
        in_specs=[
            pl.BlockSpec((rows, tile), own),
            pl.BlockSpec((rows, tile), other),
            pl.BlockSpec((rows, tile), own),
            pl.BlockSpec((rows, tile), other),
            pl.BlockSpec((rows, HIDDEN), side),
            pl.BlockSpec((rows, HIDDEN), side),
        ],
        out_specs=pl.BlockSpec((tile, HIDDEN), lambda j, i, c: (i, j)),
    )
    return pl.pallas_call(
        weight_grads_kernel,
        grid_spec=grid,
        out_shape=jax.ShapeDtypeStruct((half, 3 * HIDDEN), BF16),
        compiler_params=pltpu.CompilerParams(vmem_limit_bytes=VMEM_LIMIT),
        cost_estimate=pl.CostEstimate(
            flops=2 * 3 * 2 * rows * half * HIDDEN, bytes_accessed=24 * 1024 * 1024, transcendentals=0
        ),
    )(core, x, x2, dy, dy2, right, right2)


def rows_times_kernel(left_ref, right_ref, *out_refs):
    result = dot_nt(left_ref[...], right_ref[...]).astype(BF16)
    for number, ref in enumerate(out_refs):
        ref[...] = result[128 * number : 128 * number + 128]


def rows_times(left, left_part, right, part):
    rows, depth = left.shape[0], HIDDEN
    width = right.shape[0]
    tile = 512
    return pl.pallas_call(
        rows_times_kernel,
        out_shape=(jax.ShapeDtypeStruct((128, width), BF16),) * 4,
        grid=(width // tile,),
        in_specs=[
            pl.BlockSpec((rows, depth), lambda i: (0, left_part)),
            pl.BlockSpec((tile, depth), lambda i: (i, part)),
        ],
        out_specs=(pl.BlockSpec((128, tile), lambda i: (0, i)),) * 4,
        compiler_params=pltpu.CompilerParams(vmem_limit_bytes=VMEM_LIMIT),
        cost_estimate=pl.CostEstimate(
            flops=2 * rows * depth * width,
            bytes_accessed=2 * (rows * depth + width * depth + rows * width),
            transcendentals=0,
        ),
    )(left, right)


def ring_rows(own, near, far):
    return jnp.concatenate([own, near[:128], far, near[128:]], 0)


def put_half(number, value, other_ref, own_ref):
    @pl.when(number < 2)
    def _():
        other_ref[...] = value

    @pl.when(number >= 2)
    def _():
        own_ref[...] = value


def tile_at(i, c):
    return lax.rem(i + 2 * (1 - c[0]), 4)


def half_specs(tile, columns):
    return (
        pl.BlockSpec((tile, columns), lambda i, c: (jnp.minimum(i, 1), 0)),
        pl.BlockSpec((tile, columns), lambda i, c: (jnp.maximum(i - 2, 0), 0)),
    )


def wide_grads_kernel(
    core_ref, x_ref, dh0, dh1, dh2, dh3, o0, o1, o2, dq0, dq1, dq2, other_ref, own_ref, o_held, dq_held
):
    number = pl.program_id(0)

    @pl.when(number == 0)
    def _():
        o_held[...] = ring_rows(o0[...], o1[...], o2[...])
        dq_held[...] = ring_rows(dq0[...], dq1[...], dq2[...])

    dh = jnp.concatenate([ref[...] for ref in (dh0, dh1, dh2, dh3)], 0)
    out = dot_tn(dh, o_held[...])
    query = dot_tn(x_ref[...], dq_held[...])
    put_half(number, jnp.concatenate([out, query], 1).astype(BF16), other_ref, own_ref)


def wide_grads(core, normed, dh, o, dq):
    rows, width = normed.shape
    tile = 512
    whole = lambda i, c: (0, 0)
    column = lambda i, c: (0, tile_at(i, c))
    small = [pl.BlockSpec((size, 512), whole) for size in (128, 256, 128)]
    grid = pltpu.PrefetchScalarGridSpec(
        num_scalar_prefetch=1,
        grid=(4,),
        in_specs=[pl.BlockSpec((rows, tile), column)]
        + [pl.BlockSpec((128, tile), column)] * 4
        + small
        + small,
        out_specs=half_specs(tile, 1024),
        scratch_shapes=[pltpu.VMEM((rows, 512), BF16), pltpu.VMEM((rows, 512), BF16)],
    )
    return pl.pallas_call(
        wide_grads_kernel,
        grid_spec=grid,
        out_shape=(jax.ShapeDtypeStruct((width // 2, 1024), BF16),) * 2,
        compiler_params=pltpu.CompilerParams(vmem_limit_bytes=VMEM_LIMIT),
        cost_estimate=pl.CostEstimate(
            flops=2 * rows * width * 1024, bytes_accessed=10 * 1024 * 1024, transcendentals=0
        ),
    )(core, normed, *dh, *o, *dq)


def finish_kernel(
    core_ref,
    x_ref,
    w_ref,
    dq0_ref,
    dq1_ref,
    dq2_ref,
    own_ref,
    one_ref,
    two_ref,
    cos_ref,
    sin_ref,
    norm_ref,
    second_ref,
    other_grad_ref,
    own_grad_ref,
    dx_ref,
    gain_ref,
    dqkv,
    sums,
):
    number = pl.program_id(0)

    @pl.when(number == 0)
    def _():
        dqkv[:, :512] = ring_rows(dq0_ref[...], dq1_ref[...], dq2_ref[...])
        dkv = own_ref[...] + one_ref[...].astype(F32) + two_ref[...].astype(F32)
        turned = turn(dkv, cos_ref[...], -sin_ref[...])
        dqkv[:, 512:] = jnp.where(lane_is_low(dkv.shape, 128), turned, dkv).astype(BF16)

    x = x_ref[...]
    put_half(number, dot_tn(x, dqkv[:, 512:]).astype(BF16), other_grad_ref, own_grad_ref)
    dx = dot_nt(dqkv[...], w_ref[...])
    for piece in range(4):
        row = pl.multiple_of(lax.rem(core_ref[1] + piece, 4) * 128, 128)
        dx_ref[pl.ds(row, 128), :] = dx[128 * piece : 128 * piece + 128].astype(BF16)
    columns = pl.ds(pl.multiple_of(tile_at(number, core_ref) * 512, 512), 512)
    sums[:, columns] = jnp.broadcast_to(
        jnp.sum(dx * x.astype(F32), 0, keepdims=True) / norm_ref[:1], (8, 512)
    )

    @pl.when(number == 3)
    def _():
        gain_ref[:8] = gain_rows(to_blocks(sums[...])[:1])
        gain_ref[8:] = gain_rows(second_ref[:1])


def finish(core, normed, weights, dq, own, one, two, cosine, sine, gain, second):
    rows, width = normed.shape
    tile = 512
    whole = lambda i, c: (0, 0)
    column = lambda i, c: (0, tile_at(i, c))
    narrow = pl.BlockSpec((rows, 128), whole)
    grid = pltpu.PrefetchScalarGridSpec(
        num_scalar_prefetch=1,
        grid=(4,),
        in_specs=[
            pl.BlockSpec((rows, tile), column),
            pl.BlockSpec((tile, 640), lambda i, c: (tile_at(i, c), 0)),
            pl.BlockSpec((128, 512), whole),
            pl.BlockSpec((256, 512), whole),
            pl.BlockSpec((128, 512), whole),
            narrow,
            narrow,
            narrow,
            narrow,
            narrow,
            pl.BlockSpec((2, tile), column),
            pl.BlockSpec((8, width), whole),
        ],
        out_specs=half_specs(tile, 128)
        + (pl.BlockSpec((rows, tile), column),)
        + (pl.BlockSpec((GAIN_ROWS, GAIN_COLUMNS), whole),),
        scratch_shapes=[pltpu.VMEM((rows, 640), BF16), pltpu.VMEM((8, width), F32)],
    )
    result = pl.pallas_call(
        finish_kernel,
        grid_spec=grid,
        out_shape=(jax.ShapeDtypeStruct((width // 2, 128), BF16),) * 2
        + (jax.ShapeDtypeStruct((rows, width), BF16),)
        + (jax.ShapeDtypeStruct((GAIN_ROWS, GAIN_COLUMNS), F32),),
        compiler_params=pltpu.CompilerParams(vmem_limit_bytes=VMEM_LIMIT),
        cost_estimate=pl.CostEstimate(
            flops=2 * rows * width * 768, bytes_accessed=10 * 1024 * 1024, transcendentals=0
        ),
    )(core, normed, weights, *dq, own, one, two, cosine, sine, gain, second)
    return result


def per_device(
    tokens,
    segments,
    w_query,
    key_projection,
    value_projection,
    w_out,
    w_gate,
    w_up,
    w_down,
    norm_attn,
    norm_ffn,
    cotangent,
):
    place, core = lax.axis_index("head"), lax.axis_index("core")
    block = (lax.axis_index("y") * 4 + lax.axis_index("x")) * 2 + core
    place_array = place.astype(jnp.int32).reshape(1)
    core_array = core.astype(jnp.int32).reshape(1)
    core_place = jnp.stack([core, place]).astype(jnp.int32)
    keep = lax.optimization_barrier

    at = jnp.stack([lax.axis_index("x"), lax.axis_index("y"), core]).astype(jnp.int32)

    out_weights = lax.all_gather(
        jnp.concatenate([w_down.T, w_out.T], 1), CORE_FIRST, axis=0, tiled=True
    )
    ffn_weights = lax.all_gather(jnp.concatenate([w_gate, w_up], 1), CORE_FIRST, axis=0, tiled=True)

    x_rows, dy_rows, normed_rows, gains = prepare(
        tokens[0], cotangent[0], jnp.stack([norm_attn, norm_ffn]).astype(F32)
    )
    normed_rows, w_query = keep((normed_rows, w_query))
    ahead, behind = near_pieces(normed_rows)
    qkv_own = gather_axis(jnp.concatenate([w_query, key_projection, value_projection], 1), "x")
    qkv_own = gather_axis(jnp.concatenate(qkv_own, 0), "y")
    far = far_pieces(ahead, behind)
    qkv_own, far = keep((qkv_own, far))
    qkv_own = jnp.concatenate(qkv_own, 0)
    qkv_pieces = qkv_own, shift(qkv_own, "core", 1)
    normed_one = jnp.concatenate([normed_rows, ahead, *far, behind], 0)
    dy_raw, far = keep((cotangent[0], far))
    dy_ahead, dy_behind = near_pieces(dy_raw)
    dy_far = far_pieces(dy_ahead, dy_behind)

    row = jnp.arange(512, dtype=jnp.int32)
    positions = block * 512 + ((row // 128 + place) % 4) * 128 + row % 128
    frequency = 10000.0 ** (-jnp.arange(32, dtype=F32) * 2.0 / HEAD_SIZE)
    angles = positions.astype(F32)[:, None] * frequency[None, :]
    cosine, sine = jnp.cos(angles), jnp.sin(angles)
    cosine = jnp.concatenate([cosine] * 4, 1)
    sine = jnp.concatenate([-sine, sine, -sine, sine], 1)

    (kv_own,) = project(
        project_kv_kernel, at, normed_one, qkv_pieces, cosine, sine, 128, 128, False
    )
    normed_late, kv_own = keep((normed_one, kv_own))
    kv = (from_block(kv_own, 2), from_block(kv_own, 1), kv_own)
    queries, qkv_weights = project(
        project_q_kernel, at, normed_late, qkv_pieces, cosine, sine, 512, 640, True
    )

    flat = segments.reshape(-1)
    padded = jnp.concatenate([jnp.full((1024,), -1, jnp.int32), flat])
    own = lax.dynamic_slice_in_dim(flat, block * 512, 512, 0)
    window = lax.dynamic_slice_in_dim(padded, block * 512, 1536, 0)
    start = jnp.sum((window[None, :] < own[:, None]).astype(jnp.int32), 1)
    low = jnp.maximum(start, row + 1).reshape(1, 512)

    kk, vv, kvt = set_up(place_array, kv)
    seen = place_array, queries, kk, kvt, low, out_weights
    o_far, lse_far, part_far = attend(2, 1, 1, *seen)
    queries, part_far = keep((queries, part_far))
    part_far = shift(part_far, "head", 2)
    seen = place_array, queries, kk, kvt, low, out_weights
    o_near, lse_near, part_ahead, part_behind = attend(1, 2, 2, *seen)
    queries, part_far, part_ahead, part_behind = keep((queries, part_far, part_ahead, part_behind))
    seen = place_array, queries, kk, kvt, low, out_weights
    o_own, lse_own, part_own = attend(0, 1, 1, *seen)
    o_own, dy_far = keep((o_own, dy_far))
    dy, dy_swap = assemble(core_array, dy_rows, dy_ahead, *dy_far, dy_behind)
    dy_other = shift(dy_swap, "core", 1)
    attention_sum = part_own, shift(part_ahead, "head", 1), shift(part_behind, "head", -1), part_far
    h1, normed_rows_two = join(x_rows, gains, attention_sum)
    ahead, far, behind = gather_pieces(normed_rows_two)
    dact = columns_times(dy, out_weights, 0)
    dact, dy_other = keep((dact, dy_other))

    gua, normed_two, normed_two_swap, dnormed_two = ffn(
        core_array, (normed_rows_two, ahead, far, behind), dact, ffn_weights
    )
    dnormed_two = scatter_pieces(*dnormed_two)
    gua_other = shift(gua, "core", 1)
    normed_two_other = shift(normed_two_swap, "core", 1)
    out_pieces = rows_times(gua, 2, out_weights, 0)
    gua_other, normed_two_other, out_pieces = keep((gua_other, normed_two_other, out_pieces))
    held = weight_grads(core_array, normed_two, normed_two_other, dy, dy_other, gua, gua_other)
    held, dnormed_two = keep((held, dnormed_two))
    grads = lax.psum_scatter(held, ("y", "x"), scatter_dimension=0, tiled=True)

    dh1, dh1_low, grad_gain_two = join_back(h1, dy_rows, gains, dnormed_two)
    back = kk, vv, kvt, low, cosine, sine
    dq_own, dk, dv = attend_back(0, 1, 1, place_array, queries, o_own, (dh1_low,), out_weights, lse_own, *back, ())
    ahead, behind = shift(dh1_low, "head", -1), shift(dh1_low, "head", 1)
    ahead, behind, dk, dv, dh1_late, out_pieces = keep((ahead, behind, dk, dv, dh1_low, out_pieces))
    far = shift(dh1_late, "head", 2)
    dq_near, dk, dv = attend_back(
        1, 2, 2, place_array, queries, o_near, (ahead, behind), out_weights, lse_near, *back, (dk, dv)
    )
    far, dk, dv, out_pieces = keep((far, dk, dv, out_pieces))
    out_pieces = scatter_pieces(*out_pieces)
    dq_far, dkv_first, dkv_second, dkv_own = attend_back(
        2, 1, 1, place_array, queries, o_far, (far,), out_weights, lse_far, *back, (dk, dv)
    )
    dq = dq_own, dq_near, dq_far
    dkv_one = from_block(dkv_second, -1)
    dkv_two = from_block(dkv_first, -2)
    wide_other, wide_own = wide_grads(
        core_array, normed_one, (dh1_low, ahead, far, behind), (o_own, o_near, o_far), dq
    )
    dkv_one, dkv_two, wide_other, out_pieces = keep((dkv_one, dkv_two, wide_other, out_pieces))
    wide_other = shift(wide_other, "core", 1)

    narrow_other, narrow_own, dnormed_one, gain_grads = finish(
        core_place,
        normed_one,
        qkv_weights,
        dq,
        dkv_own,
        dkv_one,
        dkv_two,
        cosine,
        sine,
        gains,
        grad_gain_two,
    )
    dnormed_one = lax.psum_scatter(dnormed_one, "head", scatter_dimension=0, tiled=True)
    pieces, out_sums = first_pieces(
        at,
        wide_own,
        wide_other,
        narrow_own,
        shift(narrow_other, "core", 1),
        exchange([gain_grads] * 4, "head"),
    )
    rows = [(x_rows.shape, BF16)]
    (output,) = small_call(output_kernel, rows, h1, *out_pieces)
    grads = (
        grads[:, :HIDDEN].astype(F32),
        grads[:, HIDDEN : 2 * HIDDEN].astype(F32),
        grads[:, 2 * HIDDEN :].T.astype(F32),
    )
    pieces, out_sums, output, grads = keep(
        (exchange(pieces, "x"), exchange(out_sums, "y"), output, grads)
    )
    pieces, out_sums = second_pieces(at, pieces, out_sums)
    (grad_inputs,) = small_call(input_grad_kernel, rows, dh1, x_rows, gains, dnormed_one)
    pieces, out_sums, grad_inputs = keep((exchange(pieces, "y"), exchange(out_sums, "x"), grad_inputs))
    (gain_grads,) = small_call(gains_kernel, [((GAIN_ROWS, GAIN_COLUMNS), F32)], *pieces)
    columns = (64, 512), (64, 512), (64, 64), (64, 64), (1, 2048), (1, 2048)
    grad_out, grad_query, grad_key, grad_value, grad_gain_one, grad_gain_two = small_call(
        attention_grads_kernel,
        [(shape, F32) for shape in columns],
        *pieces,
        *out_sums,
        gain_grads,
        shift(gain_grads, "core", 1),
    )

    return (
        output[None],
        grad_inputs[None],
        grad_query,
        grad_key,
        grad_value,
        grad_out.T,
        *grads,
        grad_gain_one.reshape(2048),
        grad_gain_two.reshape(2048),
    )


def solution(mesh):
    grid = Mesh(mesh.devices.reshape(4, 4, 4, 2), ("head", "y", "x", "core"))
    rows, up, down = P(BLK, "head", None), P(BLK, "head"), P("head", BLK)
    return jax.shard_map(
        per_device,
        mesh=grid,
        in_specs=(rows, P(), up, up, up, down, up, up, down, P(), P(), rows),
        out_specs=(rows, rows, up, up, up, down, up, up, down, P(), P()),
        check_vma=False,
    )
```

```python
import functools

import jax
import jax.numpy as jnp
from jax import lax
from jax.experimental import pallas as pl
from jax.experimental.pallas import tpu as pltpu
from jax.sharding import Mesh
from jax.sharding import PartitionSpec as P

HEAD_SIZE = 64
WINDOW = 1024
HIDDEN = 1408
EPSILON = 1e-05
BF16 = jnp.bfloat16
F32 = jnp.float32
BLK = ("y", "x", "core")
CORE_FIRST = ("core", "y", "x")
VMEM_LIMIT = 63 * 1024 * 1024


def dot_nn(a, b):
    return jnp.dot(a, b, preferred_element_type=F32)


def dot_nt(a, b):
    return lax.dot_general(a, b, (((1,), (1,)), ((), ())), preferred_element_type=F32)


def dot_tn(a, b):
    return lax.dot_general(a, b, (((0,), (0,)), ((), ())), preferred_element_type=F32)


def shift(value, axis, distance):
    size = lax.axis_size(axis)
    return lax.ppermute(value, axis, [(i, (i + distance) % size) for i in range(size)])


def add_low(a, b):
    return (a.astype(F32) + b.astype(F32)).astype(BF16)


def gather_pieces(rows):
    return shift(rows, "head", -1), shift(rows, "head", 2), shift(rows, "head", 1)


def near_pieces(rows):
    return shift(rows, "head", -1), shift(rows, "head", 1)


def far_pieces(ahead, behind):
    half = ahead.shape[0] // 2
    return shift(behind[:half], "head", 1), shift(ahead[half:], "head", -1)


def scatter_pieces(own, ahead, far, behind):
    return own, shift(ahead, "head", 1), shift(behind, "head", -1), shift(far, "head", 2)


def gather_axis(value, axis):
    return value, shift(value, axis, -1), shift(value, axis, 2), shift(value, axis, 1)


def exchange(pieces, axis):
    return pieces[0], shift(pieces[1], axis, 1), shift(pieces[2], axis, 2), shift(pieces[3], axis, -1)


def from_block(value, distance):
    route = [(i, i + distance) for i in range(32) if 0 <= i + distance < 32]
    return lax.ppermute(value, BLK, route)


def scale_of(values):
    return lax.rsqrt(jnp.mean(values * values, -1, keepdims=True) + EPSILON)


def lane_is_low(shape, period):
    return lax.broadcasted_iota(jnp.int32, shape, len(shape) - 1) % period < period // 2


def turn(values, cosine, sine):
    swapped = jnp.where(
        lane_is_low(values.shape, 64), pltpu.roll(values, 96, 1), pltpu.roll(values, 32, 1)
    )
    return values * cosine + swapped * sine


def core_major_tiles(tiles):
    low = lane_is_low(tiles[0].shape, 128)
    rolled = [pltpu.roll(tile, 64, 1) for tile in tiles]
    first = [jnp.where(low, tiles[2 * k], rolled[2 * k + 1]) for k in range(8)]
    second = [jnp.where(low, rolled[2 * k], tiles[2 * k + 1]) for k in range(8)]
    return first + second


def block_major_tiles(tiles):
    low = lane_is_low(tiles[0].shape, 128)
    rolled = [pltpu.roll(tile, 64, 1) for tile in tiles]
    result = []
    for k in range(8):
        result.append(jnp.where(low, tiles[k], rolled[8 + k]))
        result.append(jnp.where(low, rolled[k], tiles[8 + k]))
    return result


def in_tiles(value):
    return [value[:, 128 * k : 128 * k + 128] for k in range(16)]


def prepare_kernel(x_ref, dy_ref, gain_ref, x_out, dy_out, normed_out, gain_out):
    def convert(ref):
        return jnp.concatenate(core_major_tiles(in_tiles(ref[...].astype(F32))), 1)

    x, gains = convert(x_ref), convert(gain_ref)
    gain_out[...] = gains
    x_out[...] = x
    dy_out[...] = convert(dy_ref).astype(BF16)
    normed_out[...] = (x * scale_of(x) * gains[:1]).astype(BF16)


def prepare(x, dy, gains):
    rows, width = x.shape
    return pl.pallas_call(
        prepare_kernel,
        out_shape=(
            jax.ShapeDtypeStruct((rows, width), F32),
            jax.ShapeDtypeStruct((rows, width), BF16),
            jax.ShapeDtypeStruct((rows, width), BF16),
            jax.ShapeDtypeStruct(gains.shape, F32),
        ),
        compiler_params=pltpu.CompilerParams(vmem_limit_bytes=VMEM_LIMIT),
        cost_estimate=pl.CostEstimate(
            flops=10 * rows * width, bytes_accessed=10 * rows * width, transcendentals=rows
        ),
    )(x, dy, gains)


def to_blocks(value):
    return jnp.concatenate(block_major_tiles(in_tiles(value)), 1)


def assemble_kernel(core_ref, own_ref, ahead_ref, top_ref, bottom_ref, behind_ref, out_ref, swap_ref):
    out_ref[:128] = own_ref[...]
    start = 128
    for ref in (ahead_ref, top_ref, bottom_ref, behind_ref):
        size = ref.shape[0]
        out_ref[start : start + size] = jnp.concatenate(
            core_major_tiles(in_tiles(ref[...].astype(F32))), 1
        ).astype(BF16)
        start += size
    swap_ref[...] = jnp.where(core_ref[0] == 0, out_ref[:, 1024:], out_ref[:, :1024])


def assemble(core, own, ahead, far_top, far_bottom, behind):
    vmem = pl.BlockSpec(memory_space=pltpu.VMEM)
    return pl.pallas_call(
        assemble_kernel,
        out_shape=(jax.ShapeDtypeStruct((512, 2048), BF16), jax.ShapeDtypeStruct((512, 1024), BF16)),
        in_specs=[pl.BlockSpec(memory_space=pltpu.SMEM)] + [vmem] * 5,
        out_specs=(vmem, vmem),
        compiler_params=pltpu.CompilerParams(vmem_limit_bytes=VMEM_LIMIT),
        cost_estimate=pl.CostEstimate(
            flops=4 * 512 * 2048, bytes_accessed=5 * 1024 * 1024, transcendentals=0
        ),
    )(core, own, ahead, far_top, far_bottom, behind)


def small_call(kernel, out_shape, *operands):
    return pl.pallas_call(
        kernel,
        out_shape=tuple(jax.ShapeDtypeStruct(shape, dtype) for shape, dtype in out_shape),
        compiler_params=pltpu.CompilerParams(vmem_limit_bytes=VMEM_LIMIT),
        cost_estimate=pl.CostEstimate(
            flops=sum(x.size for x in operands),
            bytes_accessed=2 * sum(x.size * x.dtype.itemsize for x in operands),
            transcendentals=0,
        ),
    )(*operands)


def total_of(refs):
    values = [ref[...].astype(F32) for ref in refs]
    while len(values) > 1:
        values = [values[0] + values[1]] + values[2:]
    return values[0]


def join_kernel(x_ref, gain_ref, a_ref, b_ref, c_ref, d_ref, h_out, top_out, bottom_out):
    h = x_ref[...] + total_of((a_ref, b_ref, c_ref, d_ref))
    h_out[...] = h
    normed = (h * scale_of(h) * gain_ref[1:2]).astype(BF16)
    half = h.shape[0] // 2
    top_out[...], bottom_out[...] = normed[:half], normed[half:]


def join(x, gain, pieces):
    half = x.shape[0] // 2, x.shape[1]
    return small_call(join_kernel, ((x.shape, F32), (half, BF16), (half, BF16)), x, gain, *pieces)


def norm_backward(values, gain, grad):
    scale = scale_of(values)
    weighted = grad * gain
    inner = jnp.mean(weighted * values, -1, keepdims=True)
    return scale * weighted - values * (scale * scale * scale * inner), scale


def join_back_kernel(h_ref, dy_ref, gain_ref, a_ref, b_ref, c_ref, d_ref, dh_out, low_out, grad_out):
    h, grad = h_ref[...], total_of((a_ref, b_ref, c_ref, d_ref))
    back, scale = norm_backward(h, gain_ref[1:2], grad)
    dh = dy_ref[...].astype(F32) + back
    dh_out[...] = dh
    low_out[...] = dh.astype(BF16)
    grad_out[...] = to_blocks(jnp.broadcast_to(jnp.sum(grad * h * scale, 0, keepdims=True), (8, h.shape[1])))


def join_back(h, dy, gain, pieces):
    shapes = (h.shape, F32), (h.shape, BF16), ((8, h.shape[1]), F32)
    return small_call(join_back_kernel, shapes, h, dy, gain, *pieces)


def output_kernel(h_ref, a_ref, b_ref, c_ref, d_ref, out_ref):
    out_ref[...] = to_blocks(h_ref[...] + total_of((a_ref, b_ref, c_ref, d_ref))).astype(BF16)


def input_grad_kernel(dh_ref, x_ref, gain_ref, grad_ref, out_ref):
    back, _ = norm_backward(x_ref[...], gain_ref[:1], grad_ref[...].astype(F32))
    out_ref[...] = to_blocks(dh_ref[...] + back).astype(BF16)


GAIN_ROWS, GAIN_COLUMNS = 16, 256


def gain_rows(vector):
    return jnp.concatenate([vector[:, 256 * k : 256 * k + 256] for k in range(8)], 0)


def put_piece(ref, rows, gains):
    count = rows.shape[0]
    ref[:count] = rows
    ref[count:, GAIN_COLUMNS:] = jnp.zeros((GAIN_ROWS, ref.shape[1] - GAIN_COLUMNS), BF16)
    ref[count:, :GAIN_COLUMNS] = gains.astype(BF16)


def first_pieces_kernel(
    at_ref, q_ref, q2_ref, kv_ref, kv2_ref, o_ref, o2_ref, *refs
):
    gain_refs, out_refs = refs[:4], refs[4:]
    query = add_low(q_ref[...], q2_ref[...]).reshape(256, 512)
    narrow = add_low(kv_ref[...], kv2_ref[...]).reshape(256, 128)
    rows = jnp.concatenate([query, narrow], 1)
    out_rows = add_low(o_ref[...], o2_ref[...]).reshape(256, 512)
    gains = total_of(gain_refs)
    for number in range(4):

        @pl.when(pl.program_id(0) == number)
        def _():
            put_piece(out_refs[number], rows, gains)
            out_refs[4 + number][...] = out_rows


def first_pieces(at, wide, wide2, narrow, narrow2, gains):
    pick_x = lambda column: lambda d, s: (0, lax.rem(s[0] + d, 4), 0, column)
    pick_y = lambda d, s: (lax.rem(s[1] + d, 4), 0, 0, 0)
    whole = lambda d, s: (0, 0)
    shaped = lambda value: value.reshape(4, 4, 64, value.shape[1])
    shapes = [(256 + GAIN_ROWS, 640)] * 4 + [(256, 512)] * 4
    grid = pltpu.PrefetchScalarGridSpec(
        num_scalar_prefetch=1,
        grid=(4,),
        in_specs=[pl.BlockSpec((4, 1, 64, 512), pick_x(1))] * 2
        + [pl.BlockSpec((4, 1, 64, 128), pick_x(0))] * 2
        + [pl.BlockSpec((1, 4, 64, 512), pick_y)] * 2
        + [pl.BlockSpec((GAIN_ROWS, GAIN_COLUMNS), whole)] * 4,
        out_specs=tuple(pl.BlockSpec(shape, whole) for shape in shapes),
    )
    wide, wide2 = shaped(wide), shaped(wide2)
    result = pl.pallas_call(
        first_pieces_kernel,
        grid_spec=grid,
        out_shape=tuple(jax.ShapeDtypeStruct(shape, BF16) for shape in shapes),
        compiler_params=pltpu.CompilerParams(vmem_limit_bytes=VMEM_LIMIT),
        cost_estimate=pl.CostEstimate(
            flops=2 * 1024 * 1152, bytes_accessed=6 * 1024 * 1152, transcendentals=0
        ),
    )(at, wide, wide2, shaped(narrow), shaped(narrow2), wide, wide2, *gains)
    return result[:4], result[4:]


def second_pieces_kernel(at_ref, *refs):
    qkv, out, (held, out_held) = refs[:4], refs[4:8], refs[16:]
    held[...] = total_of(qkv)
    out_held[...] = total_of(out).astype(BF16)
    for number in range(4):
        y = pl.multiple_of(lax.rem(at_ref[1] + number, 4) * 64, 64)
        put_piece(refs[8 + number], held[pl.ds(y, 64), :].astype(BF16), held[256:, :GAIN_COLUMNS])
        x = pl.multiple_of(lax.rem(at_ref[0] + number, 4) * 64, 64)
        refs[12 + number][...] = out_held[pl.ds(x, 64), :]


def second_pieces(at, qkv, out):
    vmem = pl.BlockSpec(memory_space=pltpu.VMEM)
    shapes = [(64 + GAIN_ROWS, 640)] * 4 + [(64, 512)] * 4
    result = pl.pallas_call(
        second_pieces_kernel,
        out_shape=tuple(jax.ShapeDtypeStruct(shape, BF16) for shape in shapes),
        in_specs=[pl.BlockSpec(memory_space=pltpu.SMEM)] + [vmem] * 8,
        out_specs=(vmem,) * 8,
        scratch_shapes=[pltpu.VMEM((256 + GAIN_ROWS, 640), F32), pltpu.VMEM((256, 512), BF16)],
        compiler_params=pltpu.CompilerParams(vmem_limit_bytes=VMEM_LIMIT),
        cost_estimate=pl.CostEstimate(
            flops=4 * 272 * 1152, bytes_accessed=10 * 272 * 1152, transcendentals=0
        ),
    )(at, *qkv, *out)
    return result[:4], result[4:]


def gains_kernel(a_ref, b_ref, c_ref, d_ref, out_ref):
    values = [ref[64:, :GAIN_COLUMNS].astype(F32) for ref in (a_ref, b_ref, c_ref, d_ref)]
    out_ref[...] = (values[0] + values[1]) + (values[2] + values[3])


def attention_grads_kernel(*refs):
    out_ref, q_ref, k_ref, v_ref, one_ref, two_ref = refs[10:]
    total = total_of(refs[:4])
    out_ref[...] = total_of(refs[4:8])
    q_ref[...] = total[:64, :512]
    k_ref[...] = total[:64, 512:576]
    v_ref[...] = total[:64, 576:]
    gains = total_of(refs[8:10])
    one_ref[...] = jnp.concatenate([gains[k : k + 1] for k in range(8)], 1)
    two_ref[...] = jnp.concatenate([gains[k : k + 1] for k in range(8, 16)], 1)


def put_in_order(at_ref, own_ref, other_ref, columns, to_ref, sems):
    x, y, core = at_ref[0], at_ref[1], at_ref[2]
    copies = []
    for number in range(32):
        ref = (own_ref, other_ref)[number // 16]
        to_x, to_y = lax.rem(x + number % 4, 4), lax.rem(y + number // 4 % 4, 4)
        to_core = core if number < 16 else 1 - core
        row = pl.multiple_of(((to_core * 4 + to_y) * 4 + to_x) * 64, 64)
        copy = pltpu.make_async_copy(
            ref.at[pl.ds(number % 16 * 64, 64), columns], to_ref.at[pl.ds(row, 64)], sems.at[number]
        )
        copy.start()
        copies.append(copy)
    return copies


def project_kv_kernel(at_ref, x_ref, own_ref, other_ref, cos_ref, sin_ref, kv_ref, held, sems):
    for copy in put_in_order(at_ref, own_ref, other_ref, pl.ds(512, 128), held, sems):
        copy.wait()
    flat = dot_nn(x_ref[...], held[...])
    turned = turn(flat, cos_ref[...], sin_ref[...])
    kv_ref[...] = jnp.where(lane_is_low(flat.shape, 128), turned, flat).astype(BF16)


def project_q_kernel(at_ref, x_ref, own_ref, other_ref, cos_ref, sin_ref, q_ref, w_ref, held, sems, sem):
    for copy in put_in_order(at_ref, own_ref, other_ref, pl.ds(0, 640), held, sems):
        copy.wait()
    whole = pltpu.make_async_copy(held, w_ref, sem)
    whole.start()
    cosine, sine, x = cos_ref[...], sin_ref[...], x_ref[...]
    for start in (0, 256):
        wide = dot_nn(x, held[:, start : start + 256])
        for part in (0, 128):
            turned = turn(wide[:, part : part + 128], cosine, sine)
            q_ref[:, start + part : start + part + 128] = (turned * HEAD_SIZE**-0.5).astype(BF16)
    whole.wait()


def project(kernel, at, normed, weights, cosine, sine, columns, held_columns, hand_out):
    rows, width = normed.shape
    vmem, anywhere = pl.BlockSpec(memory_space=pltpu.VMEM), pl.BlockSpec(memory_space=pl.ANY)
    out_shape = [jax.ShapeDtypeStruct((rows, columns), BF16)]
    out_specs = [vmem]
    scratch = [pltpu.VMEM((width, held_columns), BF16), pltpu.SemaphoreType.DMA((32,))]
    if hand_out:
        out_shape.append(jax.ShapeDtypeStruct((width, held_columns), BF16))
        out_specs.append(anywhere)
        scratch.append(pltpu.SemaphoreType.DMA)
    return pl.pallas_call(
        kernel,
        out_shape=tuple(out_shape),
        in_specs=[pl.BlockSpec(memory_space=pltpu.SMEM), vmem, anywhere, anywhere, vmem, vmem],
        out_specs=tuple(out_specs),
        scratch_shapes=scratch,
        compiler_params=pltpu.CompilerParams(vmem_limit_bytes=VMEM_LIMIT),
        cost_estimate=pl.CostEstimate(
            flops=2 * rows * width * columns,
            bytes_accessed=2 * (rows * width + width * columns + rows * columns),
            transcendentals=0,
        ),
    )(at, normed, *weights, cosine, sine)


KEYS = 1152
PAIRS = 4


def set_up_kernel(place_ref, kv0_ref, kv1_ref, kv2_ref, kk_ref, vv_ref, kvt_ref):
    place = place_ref[0]
    low = lane_is_low((128, 128), 128)
    for block, ref in enumerate((kv0_ref, kv1_ref, kv2_ref)):
        for group in range(4):
            at = pl.multiple_of(lax.rem(group - place + 4, 4) * 128, 128)
            piece = ref[pl.ds(at, 128), :].astype(F32)
            rolled = pltpu.roll(piece, 64, 1)
            to = block * 512 + group * 128
            kk_ref[to : to + 128, :] = jnp.where(low, piece, rolled).astype(BF16)
            vv_ref[to : to + 128, :] = jnp.where(low, rolled, piece).astype(BF16)
            kvt_ref[:, to : to + 128] = piece.T.astype(BF16)


def set_up(place, kv):
    vmem = pl.BlockSpec(memory_space=pltpu.VMEM)
    return pl.pallas_call(
        set_up_kernel,
        out_shape=(
            jax.ShapeDtypeStruct((1536, 128), BF16),
            jax.ShapeDtypeStruct((1536, 128), BF16),
            jax.ShapeDtypeStruct((128, 1536), BF16),
        ),
        in_specs=[pl.BlockSpec(memory_space=pltpu.SMEM), vmem, vmem, vmem],
        out_specs=(vmem, vmem, vmem),
        compiler_params=pltpu.CompilerParams(vmem_limit_bytes=VMEM_LIMIT),
        cost_estimate=pl.CostEstimate(flops=1536 * 128 * 8, bytes_accessed=2 * 1024 * 1024, transcendentals=0),
    )(place, *kv)


def both_heads(pair):
    low = lane_is_low(pair.shape, 128)
    nothing = jnp.zeros_like(pair)
    return jnp.concatenate([jnp.where(low, pair, nothing), jnp.where(low, nothing, pair)], 0)


def side_by_side(transposed):
    return jnp.concatenate([transposed[:, :128], transposed[:, 128:]], 0).T


def mask_of(at, low_ref):
    key = lax.broadcasted_iota(jnp.int32, (KEYS, 128), 0)
    query = lax.broadcasted_iota(jnp.int32, (KEYS, 128), 1)
    seen = (key >= low_ref[:, pl.ds(at, 128)] - at) & (key <= query + WINDOW)
    bias = jnp.where(seen, 0.0, -jnp.inf)
    return jnp.concatenate([bias, bias], 1)


def attend_kernel(
    first, step, place_ref, q_ref, kk_ref, kvt_ref, low_ref, w_ref, o_ref, lse_ref, *refs
):
    part_refs, (bias, held, w_held, sem) = refs[:-4], refs[-4:]
    group = lax.rem(place_ref[0] + first + step * pl.program_id(0), 4)
    at = pl.multiple_of(group * 128, 128)

    load = pltpu.make_async_copy(w_ref.at[:, pl.ds(HIDDEN, 512)], w_held, sem)

    @pl.when((pl.program_id(0) == 0) & (pl.program_id(1) == 0))
    def _():
        load.start()

    @pl.when(pl.program_id(1) == 0)
    def _():
        bias[...] = mask_of(at, low_ref)

    keys = pl.ds(at, KEYS)
    for number in range(PAIRS):
        columns = slice(128 * number, 128 * number + 128)
        scores = dot_nt(kk_ref[keys, :], both_heads(q_ref[:, columns])) + bias[...]
        top = jnp.max(scores, 0, keepdims=True)
        weights = jnp.exp(scores - top)
        total = jnp.sum(weights, 0, keepdims=True)
        result = dot_nn(kvt_ref[64:128, keys], weights.astype(BF16)) / total
        lse_ref[0, number] = top + jnp.log(total)
        result = side_by_side(result).astype(BF16)
        o_ref[:, columns] = result
        held[PAIRS * pl.program_id(1) + number] = result

    @pl.when(pl.program_id(1) == 4 // PAIRS - 1)
    def _():
        @pl.when(pl.program_id(0) == 0)
        def _():
            load.wait()

        rows = jnp.concatenate([held[k] for k in range(4)], 1)
        part = dot_nt(rows, w_held[...]).astype(BF16)
        for number, ref in enumerate(part_refs):

            @pl.when(pl.program_id(0) == number)
            def _():
                ref[...] = part


def attend(first, step, count, place, queries, kk, kvt, low, weights):
    whole = lambda g, p, s: (0, 0)
    width = 128 * PAIRS
    grid = pltpu.PrefetchScalarGridSpec(
        num_scalar_prefetch=1,
        grid=(count, 4 // PAIRS),
        in_specs=[
            pl.BlockSpec((128, width), lambda g, p, s: (first + step * g, p)),
            pl.BlockSpec((1536, 128), whole),
            pl.BlockSpec((128, 1536), whole),
            pl.BlockSpec((1, 512), whole),
            pl.BlockSpec(memory_space=pl.ANY),
        ],
        out_specs=(
            pl.BlockSpec((128, width), lambda g, p, s: (g, p)),
            pl.BlockSpec((1, PAIRS, 1, 256), lambda g, p, s: (g, p, 0, 0)),
        )
        + (pl.BlockSpec((128, 2048), whole),) * count,
        scratch_shapes=[
            pltpu.VMEM((KEYS, 256), F32),
            pltpu.VMEM((4, 128, 128), BF16),
            pltpu.VMEM((2048, 512), BF16),
            pltpu.SemaphoreType.DMA,
        ],
    )
    return pl.pallas_call(
        functools.partial(attend_kernel, first, step),
        grid_spec=grid,
        out_shape=(
            jax.ShapeDtypeStruct((128 * count, 512), BF16),
            jax.ShapeDtypeStruct((count, 4, 1, 256), F32),
        )
        + (jax.ShapeDtypeStruct((128, 2048), BF16),) * count,
        compiler_params=pltpu.CompilerParams(vmem_limit_bytes=VMEM_LIMIT),
        cost_estimate=pl.CostEstimate(
            flops=count * 4 * KEYS * 256 * 256 * 2,
            bytes_accessed=3 * 1024 * 1024,
            transcendentals=count * 4 * KEYS * 256,
        ),
    )(place, queries, kk, kvt, low, weights)


def attend_back_kernel(first, step, count, *refs):
    last = first == 2
    place_ref, q_ref, w_ref, lse_ref, kk_ref, vv_ref, kvt_ref, low_ref, cos_ref, sin_ref = refs[:10]
    o_ref = refs[10]
    dh_refs, refs = refs[11 : 11 + count], refs[11 + count :]
    dk_in = dv_in = None
    if first > 0:
        dk_in, dv_in, refs = refs[0], refs[1], refs[2:]
    bias, do_held, dk, dv, w_held, sem = refs[-6:]
    dq_ref, outs = refs[0], refs[1:-6]
    number, pair = pl.program_id(0), pl.program_id(1)
    place = place_ref[0]
    at = pl.multiple_of(lax.rem(place + first + step * number, 4) * 128, 128)

    load = pltpu.make_async_copy(w_ref.at[:, pl.ds(HIDDEN, 512)], w_held, sem)

    @pl.when((number == 0) & (pair == 0))
    def _():
        load.start()
        dk[...] = jnp.zeros_like(dk) if dk_in is None else dk_in[...]
        dv[...] = jnp.zeros_like(dv) if dv_in is None else dv_in[...]

    @pl.when(pair == 0)
    def _():
        bias[...] = mask_of(at, low_ref)

        @pl.when(number == 0)
        def _():
            load.wait()

        for k, ref in enumerate(dh_refs):

            @pl.when(number == k)
            def _():
                do_rows = dot_nn(ref[...], w_held[...]).astype(BF16)
                for p in range(4):
                    do_held[p] = do_rows[:, 128 * p : 128 * p + 128]

    keys = pl.ds(at, KEYS)
    queries, grads, all_weights, all_grad_scores = [], [], [], []
    for k in range(PAIRS):
        columns = slice(128 * k, 128 * k + 128)
        do_pair = do_held[PAIRS * pair + k]
        query, grad = both_heads(q_ref[:, columns]), both_heads(do_pair)
        scores = dot_nt(kk_ref[keys, :], query) + bias[...]
        weights = jnp.exp(scores - lse_ref[0, k])
        grad_weights = dot_nt(vv_ref[keys, :], grad)
        product = (o_ref[:, columns].astype(F32) * do_pair.astype(F32)).T
        inner = jnp.concatenate(
            [jnp.sum(product[:64], 0, keepdims=True), jnp.sum(product[64:], 0, keepdims=True)], 1
        )
        grad_scores = (weights * (grad_weights - inner)).astype(BF16)
        grad_query = side_by_side(dot_nn(kvt_ref[0:64, keys], grad_scores)) * HEAD_SIZE**-0.5
        dq_ref[:, columns] = turn(grad_query, cos_ref[...], -sin_ref[...]).astype(BF16)
        queries.append(query)
        grads.append(grad)
        all_weights.append(weights.astype(BF16))
        all_grad_scores.append(grad_scores)
    join = lambda values, axis: values[0] if PAIRS == 1 else jnp.concatenate(values, axis)
    dv[keys, :] += dot_nn(join(all_weights, 1), join(grads, 0))
    dk[keys, :] += dot_nn(join(all_grad_scores, 1), join(queries, 0))

    @pl.when((number == pl.num_programs(0) - 1) & (pair == 4 // PAIRS - 1))
    def _():
        if not last:
            outs[0][...], outs[1][...] = dk[...], dv[...]
            return
        half = lane_is_low((128, 128), 128)
        for block in range(3):
            for group in range(4):
                to = pl.multiple_of(lax.rem(group - place + 4, 4) * 128, 128)
                frm = slice(block * 512 + group * 128, block * 512 + group * 128 + 128)
                key, value = dk[frm, :], dv[frm, :]
                key = key + pltpu.roll(key, 64, 1)
                value = value + pltpu.roll(value, 64, 1)
                both = jnp.where(half, key, value)
                outs[block][pl.ds(to, 128), :] = both.astype(outs[block].dtype)


def attend_back(first, step, count, place, queries, o, dh, weights, lse, kk, vv, kvt, low, cosine, sine, held):
    last = first == 2
    whole = lambda g, p, s: (0, 0)
    specs = [
        pl.BlockSpec((128, 128 * PAIRS), lambda g, p, s: (first + step * g, p)),
        pl.BlockSpec(memory_space=pl.ANY),
        pl.BlockSpec((1, PAIRS, 1, 256), lambda g, p, s: (g, p, 0, 0)),
        pl.BlockSpec((1536, 128), whole),
        pl.BlockSpec((1536, 128), whole),
        pl.BlockSpec((128, 1536), whole),
        pl.BlockSpec((1, 512), whole),
        pl.BlockSpec((128, 128), lambda g, p, s: (first + step * g, 0)),
        pl.BlockSpec((128, 128), lambda g, p, s: (first + step * g, 0)),
    ]
    specs += [pl.BlockSpec((128, 128 * PAIRS), lambda g, p, s: (g, p))]
    specs += [pl.BlockSpec((128, 2048), whole)] * count + [pl.BlockSpec((1536, 128), whole)] * len(held)
    if last:
        out_specs = (pl.BlockSpec((512, 128), whole),) * 3
        out_shape = tuple(jax.ShapeDtypeStruct((512, 128), dtype) for dtype in (BF16, BF16, F32))
    else:
        out_specs = (pl.BlockSpec((1536, 128), whole),) * 2
        out_shape = (jax.ShapeDtypeStruct((1536, 128), F32),) * 2
    grid = pltpu.PrefetchScalarGridSpec(
        num_scalar_prefetch=1,
        grid=(count, 4 // PAIRS),
        in_specs=specs,
        out_specs=(pl.BlockSpec((128, 128 * PAIRS), lambda g, p, s: (g, p)),) + out_specs,
        scratch_shapes=[
            pltpu.VMEM((KEYS, 256), F32),
            pltpu.VMEM((4, 128, 128), BF16),
            pltpu.VMEM((1536, 128), F32),
            pltpu.VMEM((1536, 128), F32),
            pltpu.VMEM((2048, 512), BF16),
            pltpu.SemaphoreType.DMA,
        ],
    )
    return pl.pallas_call(
        functools.partial(attend_back_kernel, first, step, count),
        grid_spec=grid,
        out_shape=(jax.ShapeDtypeStruct((128 * count, 512), BF16),) + out_shape,
        compiler_params=pltpu.CompilerParams(vmem_limit_bytes=VMEM_LIMIT),
        cost_estimate=pl.CostEstimate(
            flops=count * 4 * KEYS * 256 * 640 * 2,
            bytes_accessed=6 * 1024 * 1024,
            transcendentals=count * 4 * KEYS * 256,
        ),
    )(place, queries, weights, lse, kk, vv, kvt, low, cosine, sine, o, *dh, *held)


GROUPS = [(0, 128), (128, 256), (384, 512), (896, 512)]


def columns_times_kernel(left_ref, right_ref, out_ref):
    out_ref[...] = dot_nn(left_ref[...], right_ref[...])


def columns_times(left, right, part):
    rows, width = left.shape
    return pl.pallas_call(
        columns_times_kernel,
        out_shape=jax.ShapeDtypeStruct((rows, HIDDEN), F32),
        grid=(1,),
        in_specs=[
            pl.BlockSpec((rows, width), lambda i: (0, 0)),
            pl.BlockSpec((width, HIDDEN), lambda i: (0, part)),
        ],
        out_specs=pl.BlockSpec((rows, HIDDEN), lambda i: (0, 0)),
        compiler_params=pltpu.CompilerParams(vmem_limit_bytes=VMEM_LIMIT),
        cost_estimate=pl.CostEstimate(
            flops=2 * rows * width * HIDDEN, bytes_accessed=11 * 1024 * 1024, transcendentals=0
        ),
    )(left, right)


PIECES = [(0, 128), (128, 128), (256, 128), (384, 128)]


def ffn_kernel(*refs):
    core_ref, x_refs, dact_ref, w_ref = refs[0], refs[1:9], refs[9], refs[10]
    gua_ref, whole_ref, swap_ref, dx_refs = refs[11], refs[12], refs[13], refs[14:18]
    x_held, dact_held, w_held, gua, dx, sems, out_sems = refs[18:]
    x_copies = []
    for number in range(8):
        copy = pltpu.make_async_copy(
            x_refs[number], x_held.at[pl.ds(64 * number, 64)], sems.at[12 + number]
        )
        copy.start()
        x_copies.append(copy)
    copies = []
    for number, (start, width) in enumerate(GROUPS):
        for part in range(3):
            if part < 2:
                columns = pl.ds(part * HIDDEN + start, width)
                copy = pltpu.make_async_copy(
                    w_ref.at[:, columns], w_held.at[:, columns], sems.at[3 * number + part]
                )
            else:
                columns = pl.ds(start, width)
                copy = pltpu.make_async_copy(
                    dact_ref.at[:, columns], dact_held.at[:, columns], sems.at[3 * number + part]
                )
            copy.start()
            copies.append(copy)
    for copy in x_copies:
        copy.wait()
    half = pl.multiple_of((1 - core_ref[0]) * 1024, 1024)
    results = [
        pltpu.make_async_copy(x_held, whole_ref, out_sems.at[5]),
        pltpu.make_async_copy(x_held.at[:, pl.ds(half, 1024)], swap_ref, out_sems.at[6]),
    ]
    for copy in results:
        copy.start()
    x = x_held[...]
    for number, (start, width) in enumerate(GROUPS):
        for part in range(3):
            copies[3 * number + part].wait()
        gate = dot_nn(x, w_held[:, start : start + width])
        up = dot_nn(x, w_held[:, HIDDEN + start : HIDDEN + start + width])
        dact = dact_held[:, start : start + width]
        sig = jax.nn.sigmoid(gate)
        silu = gate * sig
        dgate = dact * up * (sig * (1.0 + gate * (1.0 - sig)))
        gua[:, start : start + width] = dgate.astype(BF16)
        gua[:, HIDDEN + start : HIDDEN + start + width] = (dact * silu).astype(BF16)
        gua[:, 2 * HIDDEN + start : 2 * HIDDEN + start + width] = (silu * up).astype(BF16)
    copy = pltpu.make_async_copy(gua, gua_ref, out_sems.at[4])
    copy.start()
    results.append(copy)
    dgu = gua[:, : 2 * HIDDEN]
    for number in range(4):
        columns = slice(512 * number, 512 * number + 512)
        dx[:, columns] = dot_nt(dgu, w_held[columns, : 2 * HIDDEN]).astype(BF16)
    for number, (start, size) in enumerate(PIECES):
        copy = pltpu.make_async_copy(dx.at[pl.ds(start, size)], dx_refs[number], out_sems.at[number])
        copy.start()
        results.append(copy)
    for copy in results:
        copy.wait()


def ffn(core, pieces, dact, weights):
    rows, width = dact.shape[0], weights.shape[0]
    anywhere = pl.BlockSpec(memory_space=pl.ANY)
    result = pl.pallas_call(
        ffn_kernel,
        out_shape=(
            jax.ShapeDtypeStruct((rows, 3 * HIDDEN), BF16),
            jax.ShapeDtypeStruct((rows, width), BF16),
            jax.ShapeDtypeStruct((rows, width // 2), BF16),
            *(jax.ShapeDtypeStruct((size, width), BF16) for _, size in PIECES),
        ),
        in_specs=[pl.BlockSpec(memory_space=pltpu.SMEM)] + [anywhere] * 10,
        out_specs=(anywhere,) * 7,
        scratch_shapes=[
            pltpu.VMEM((rows, width), BF16),
            pltpu.VMEM((rows, HIDDEN), F32),
            pltpu.VMEM((width, 2 * HIDDEN), BF16),
            pltpu.VMEM((rows, 3 * HIDDEN), BF16),
            pltpu.VMEM((rows, width), BF16),
            pltpu.SemaphoreType.DMA((20,)),
            pltpu.SemaphoreType.DMA((7,)),
        ],
        compiler_params=pltpu.CompilerParams(vmem_limit_bytes=VMEM_LIMIT),
        cost_estimate=pl.CostEstimate(
            flops=8 * rows * width * HIDDEN,
            bytes_accessed=25 * 1024 * 1024,
            transcendentals=rows * HIDDEN,
        ),
    )(core, *pieces, dact, weights)
    return result[0], result[1], result[2], result[3:]


def weight_grads_kernel(core_ref, x_ref, x2_ref, dy_ref, dy2_ref, right_ref, right2_ref, out_ref):
    part = pl.program_id(0)

    @pl.when(part < 2)
    def _():
        total = dot_tn(x_ref[...], right_ref[...]) + dot_tn(x2_ref[...], right2_ref[...])
        out_ref[...] = total.astype(BF16)

    @pl.when(part == 2)
    def _():
        total = dot_tn(dy_ref[...], right_ref[...]) + dot_tn(dy2_ref[...], right2_ref[...])
        out_ref[...] = total.astype(BF16)


def weight_grads(core, x, x2, dy, dy2, right, right2):
    rows = x.shape[0]
    tile = 1024
    half = x2.shape[1]
    tiles = half // tile
    own = lambda j, i, c: (0, c[0] * tiles + i)
    other = lambda j, i, c: (0, i)
    side = lambda j, i, c: (0, j)
    grid = pltpu.PrefetchScalarGridSpec(
        num_scalar_prefetch=1,
        grid=(3, tiles),
        in_specs=[
            pl.BlockSpec((rows, tile), own),
            pl.BlockSpec((rows, tile), other),
            pl.BlockSpec((rows, tile), own),
            pl.BlockSpec((rows, tile), other),
            pl.BlockSpec((rows, HIDDEN), side),
            pl.BlockSpec((rows, HIDDEN), side),
        ],
        out_specs=pl.BlockSpec((tile, HIDDEN), lambda j, i, c: (i, j)),
    )
    return pl.pallas_call(
        weight_grads_kernel,
        grid_spec=grid,
        out_shape=jax.ShapeDtypeStruct((half, 3 * HIDDEN), BF16),
        compiler_params=pltpu.CompilerParams(vmem_limit_bytes=VMEM_LIMIT),
        cost_estimate=pl.CostEstimate(
            flops=2 * 3 * 2 * rows * half * HIDDEN, bytes_accessed=24 * 1024 * 1024, transcendentals=0
        ),
    )(core, x, x2, dy, dy2, right, right2)


def rows_times_kernel(left_ref, right_ref, *out_refs):
    result = dot_nt(left_ref[...], right_ref[...]).astype(BF16)
    for number, ref in enumerate(out_refs):
        ref[...] = result[128 * number : 128 * number + 128]


def rows_times(left, left_part, right, part):
    rows, depth = left.shape[0], HIDDEN
    width = right.shape[0]
    tile = 512
    return pl.pallas_call(
        rows_times_kernel,
        out_shape=(jax.ShapeDtypeStruct((128, width), BF16),) * 4,
        grid=(width // tile,),
        in_specs=[
            pl.BlockSpec((rows, depth), lambda i: (0, left_part)),
            pl.BlockSpec((tile, depth), lambda i: (i, part)),
        ],
        out_specs=(pl.BlockSpec((128, tile), lambda i: (0, i)),) * 4,
        compiler_params=pltpu.CompilerParams(vmem_limit_bytes=VMEM_LIMIT),
        cost_estimate=pl.CostEstimate(
            flops=2 * rows * depth * width,
            bytes_accessed=2 * (rows * depth + width * depth + rows * width),
            transcendentals=0,
        ),
    )(left, right)


def ring_rows(own, near, far):
    return jnp.concatenate([own, near[:128], far, near[128:]], 0)


def put_half(number, value, other_ref, own_ref):
    @pl.when(number < 2)
    def _():
        other_ref[...] = value

    @pl.when(number >= 2)
    def _():
        own_ref[...] = value


def tile_at(i, c):
    return lax.rem(i + 2 * (1 - c[0]), 4)


def half_specs(tile, columns):
    return (
        pl.BlockSpec((tile, columns), lambda i, c: (jnp.minimum(i, 1), 0)),
        pl.BlockSpec((tile, columns), lambda i, c: (jnp.maximum(i - 2, 0), 0)),
    )


def wide_grads_kernel(
    core_ref, x_ref, dh0, dh1, dh2, dh3, o0, o1, o2, dq0, dq1, dq2, other_ref, own_ref, o_held, dq_held
):
    number = pl.program_id(0)

    @pl.when(number == 0)
    def _():
        o_held[...] = ring_rows(o0[...], o1[...], o2[...])
        dq_held[...] = ring_rows(dq0[...], dq1[...], dq2[...])

    dh = jnp.concatenate([ref[...] for ref in (dh0, dh1, dh2, dh3)], 0)
    out = dot_tn(dh, o_held[...])
    query = dot_tn(x_ref[...], dq_held[...])
    put_half(number, jnp.concatenate([out, query], 1).astype(BF16), other_ref, own_ref)


def wide_grads(core, normed, dh, o, dq):
    rows, width = normed.shape
    tile = 512
    whole = lambda i, c: (0, 0)
    column = lambda i, c: (0, tile_at(i, c))
    small = [pl.BlockSpec((size, 512), whole) for size in (128, 256, 128)]
    grid = pltpu.PrefetchScalarGridSpec(
        num_scalar_prefetch=1,
        grid=(4,),
        in_specs=[pl.BlockSpec((rows, tile), column)]
        + [pl.BlockSpec((128, tile), column)] * 4
        + small
        + small,
        out_specs=half_specs(tile, 1024),
        scratch_shapes=[pltpu.VMEM((rows, 512), BF16), pltpu.VMEM((rows, 512), BF16)],
    )
    return pl.pallas_call(
        wide_grads_kernel,
        grid_spec=grid,
        out_shape=(jax.ShapeDtypeStruct((width // 2, 1024), BF16),) * 2,
        compiler_params=pltpu.CompilerParams(vmem_limit_bytes=VMEM_LIMIT),
        cost_estimate=pl.CostEstimate(
            flops=2 * rows * width * 1024, bytes_accessed=10 * 1024 * 1024, transcendentals=0
        ),
    )(core, normed, *dh, *o, *dq)


def finish_kernel(
    core_ref,
    x_ref,
    w_ref,
    dq0_ref,
    dq1_ref,
    dq2_ref,
    own_ref,
    one_ref,
    two_ref,
    cos_ref,
    sin_ref,
    norm_ref,
    second_ref,
    other_grad_ref,
    own_grad_ref,
    dx_ref,
    gain_ref,
    dqkv,
    sums,
):
    number = pl.program_id(0)

    @pl.when(number == 0)
    def _():
        dqkv[:, :512] = ring_rows(dq0_ref[...], dq1_ref[...], dq2_ref[...])
        dkv = own_ref[...] + one_ref[...].astype(F32) + two_ref[...].astype(F32)
        turned = turn(dkv, cos_ref[...], -sin_ref[...])
        dqkv[:, 512:] = jnp.where(lane_is_low(dkv.shape, 128), turned, dkv).astype(BF16)

    x = x_ref[...]
    put_half(number, dot_tn(x, dqkv[:, 512:]).astype(BF16), other_grad_ref, own_grad_ref)
    dx = dot_nt(dqkv[...], w_ref[...])
    for piece in range(4):
        row = pl.multiple_of(lax.rem(core_ref[1] + piece, 4) * 128, 128)
        dx_ref[pl.ds(row, 128), :] = dx[128 * piece : 128 * piece + 128].astype(BF16)
    columns = pl.ds(pl.multiple_of(tile_at(number, core_ref) * 512, 512), 512)
    sums[:, columns] = jnp.broadcast_to(
        jnp.sum(dx * x.astype(F32), 0, keepdims=True) / norm_ref[:1], (8, 512)
    )

    @pl.when(number == 3)
    def _():
        gain_ref[:8] = gain_rows(to_blocks(sums[...])[:1])
        gain_ref[8:] = gain_rows(second_ref[:1])


def finish(core, normed, weights, dq, own, one, two, cosine, sine, gain, second):
    rows, width = normed.shape
    tile = 512
    whole = lambda i, c: (0, 0)
    column = lambda i, c: (0, tile_at(i, c))
    narrow = pl.BlockSpec((rows, 128), whole)
    grid = pltpu.PrefetchScalarGridSpec(
        num_scalar_prefetch=1,
        grid=(4,),
        in_specs=[
            pl.BlockSpec((rows, tile), column),
            pl.BlockSpec((tile, 640), lambda i, c: (tile_at(i, c), 0)),
            pl.BlockSpec((128, 512), whole),
            pl.BlockSpec((256, 512), whole),
            pl.BlockSpec((128, 512), whole),
            narrow,
            narrow,
            narrow,
            narrow,
            narrow,
            pl.BlockSpec((2, tile), column),
            pl.BlockSpec((8, width), whole),
        ],
        out_specs=half_specs(tile, 128)
        + (pl.BlockSpec((rows, tile), column),)
        + (pl.BlockSpec((GAIN_ROWS, GAIN_COLUMNS), whole),),
        scratch_shapes=[pltpu.VMEM((rows, 640), BF16), pltpu.VMEM((8, width), F32)],
    )
    result = pl.pallas_call(
        finish_kernel,
        grid_spec=grid,
        out_shape=(jax.ShapeDtypeStruct((width // 2, 128), BF16),) * 2
        + (jax.ShapeDtypeStruct((rows, width), BF16),)
        + (jax.ShapeDtypeStruct((GAIN_ROWS, GAIN_COLUMNS), F32),),
        compiler_params=pltpu.CompilerParams(vmem_limit_bytes=VMEM_LIMIT),
        cost_estimate=pl.CostEstimate(
            flops=2 * rows * width * 768, bytes_accessed=10 * 1024 * 1024, transcendentals=0
        ),
    )(core, normed, weights, *dq, own, one, two, cosine, sine, gain, second)
    return result


def per_device(
    tokens,
    segments,
    w_query,
    key_projection,
    value_projection,
    w_out,
    w_gate,
    w_up,
    w_down,
    norm_attn,
    norm_ffn,
    cotangent,
):
    place, core = lax.axis_index("head"), lax.axis_index("core")
    block = (lax.axis_index("y") * 4 + lax.axis_index("x")) * 2 + core
    place_array = place.astype(jnp.int32).reshape(1)
    core_array = core.astype(jnp.int32).reshape(1)
    core_place = jnp.stack([core, place]).astype(jnp.int32)
    keep = lax.optimization_barrier

    at = jnp.stack([lax.axis_index("x"), lax.axis_index("y"), core]).astype(jnp.int32)

    out_weights = lax.all_gather(
        jnp.concatenate([w_down.T, w_out.T], 1), CORE_FIRST, axis=0, tiled=True
    )
    ffn_weights = lax.all_gather(jnp.concatenate([w_gate, w_up], 1), CORE_FIRST, axis=0, tiled=True)

    x_rows, dy_rows, normed_rows, gains = prepare(
        tokens[0], cotangent[0], jnp.stack([norm_attn, norm_ffn]).astype(F32)
    )
    normed_rows, w_query = keep((normed_rows, w_query))
    ahead, behind = near_pieces(normed_rows)
    qkv_own = gather_axis(jnp.concatenate([w_query, key_projection, value_projection], 1), "x")
    qkv_own = gather_axis(jnp.concatenate(qkv_own, 0), "y")
    far = far_pieces(ahead, behind)
    qkv_own, far = keep((qkv_own, far))
    qkv_own = jnp.concatenate(qkv_own, 0)
    qkv_pieces = qkv_own, shift(qkv_own, "core", 1)
    normed_one = jnp.concatenate([normed_rows, ahead, *far, behind], 0)
    dy_raw, far = keep((cotangent[0], far))
    dy_ahead, dy_behind = near_pieces(dy_raw)
    dy_far = far_pieces(dy_ahead, dy_behind)

    row = jnp.arange(512, dtype=jnp.int32)
    positions = block * 512 + ((row // 128 + place) % 4) * 128 + row % 128
    frequency = 10000.0 ** (-jnp.arange(32, dtype=F32) * 2.0 / HEAD_SIZE)
    angles = positions.astype(F32)[:, None] * frequency[None, :]
    cosine, sine = jnp.cos(angles), jnp.sin(angles)
    cosine = jnp.concatenate([cosine] * 4, 1)
    sine = jnp.concatenate([-sine, sine, -sine, sine], 1)

    (kv_own,) = project(
        project_kv_kernel, at, normed_one, qkv_pieces, cosine, sine, 128, 128, False
    )
    normed_late, kv_own = keep((normed_one, kv_own))
    kv = (from_block(kv_own, 2), from_block(kv_own, 1), kv_own)
    queries, qkv_weights = project(
        project_q_kernel, at, normed_late, qkv_pieces, cosine, sine, 512, 640, True
    )

    flat = segments.reshape(-1)
    padded = jnp.concatenate([jnp.full((1024,), -1, jnp.int32), flat])
    own = lax.dynamic_slice_in_dim(flat, block * 512, 512, 0)
    window = lax.dynamic_slice_in_dim(padded, block * 512, 1536, 0)
    start = jnp.sum((window[None, :] < own[:, None]).astype(jnp.int32), 1)
    low = jnp.maximum(start, row + 1).reshape(1, 512)

    kk, vv, kvt = set_up(place_array, kv)
    seen = place_array, queries, kk, kvt, low, out_weights
    o_far, lse_far, part_far = attend(2, 1, 1, *seen)
    queries, part_far = keep((queries, part_far))
    part_far = shift(part_far, "head", 2)
    seen = place_array, queries, kk, kvt, low, out_weights
    o_near, lse_near, part_ahead, part_behind = attend(1, 2, 2, *seen)
    queries, part_far, part_ahead, part_behind = keep((queries, part_far, part_ahead, part_behind))
    seen = place_array, queries, kk, kvt, low, out_weights
    o_own, lse_own, part_own = attend(0, 1, 1, *seen)
    o_own, dy_far = keep((o_own, dy_far))
    dy, dy_swap = assemble(core_array, dy_rows, dy_ahead, *dy_far, dy_behind)
    dy_other = shift(dy_swap, "core", 1)
    attention_sum = part_own, shift(part_ahead, "head", 1), shift(part_behind, "head", -1), part_far
    h1, top, bottom = join(x_rows, gains, attention_sum)
    behind_top, ahead_bottom = shift(top, "head", 1), shift(bottom, "head", -1)
    ahead_top, behind_bottom = shift(top, "head", -1), shift(bottom, "head", 1)
    behind_top, ahead_bottom, dy = keep((behind_top, ahead_bottom, dy))
    far_top, far_bottom = shift(behind_top, "head", 1), shift(ahead_bottom, "head", -1)
    rows_two = top, bottom, ahead_top, ahead_bottom, far_top, far_bottom, behind_top, behind_bottom
    dact = columns_times(dy, out_weights, 0)
    dact, dy_other = keep((dact, dy_other))

    gua, normed_two, normed_two_swap, dnormed_two = ffn(
        core_array, rows_two, dact, ffn_weights
    )
    dnormed_two = scatter_pieces(*dnormed_two)
    gua_other = shift(gua, "core", 1)
    normed_two_other = shift(normed_two_swap, "core", 1)
    out_pieces = rows_times(gua, 2, out_weights, 0)
    gua_other, normed_two_other, out_pieces = keep((gua_other, normed_two_other, out_pieces))
    held = weight_grads(core_array, normed_two, normed_two_other, dy, dy_other, gua, gua_other)
    held, dnormed_two = keep((held, dnormed_two))
    grads = lax.psum_scatter(held, ("y", "x"), scatter_dimension=0, tiled=True)

    dh1, dh1_low, grad_gain_two = join_back(h1, dy_rows, gains, dnormed_two)
    back = kk, vv, kvt, low, cosine, sine
    dq_own, dk, dv = attend_back(0, 1, 1, place_array, queries, o_own, (dh1_low,), out_weights, lse_own, *back, ())
    ahead, behind = shift(dh1_low, "head", -1), shift(dh1_low, "head", 1)
    ahead, behind, dk, dv, dh1_late, out_pieces = keep((ahead, behind, dk, dv, dh1_low, out_pieces))
    far = shift(dh1_late, "head", 2)
    dq_near, dk, dv = attend_back(
        1, 2, 2, place_array, queries, o_near, (ahead, behind), out_weights, lse_near, *back, (dk, dv)
    )
    far, dk, dv, out_pieces = keep((far, dk, dv, out_pieces))
    out_pieces = scatter_pieces(*out_pieces)
    dq_far, dkv_first, dkv_second, dkv_own = attend_back(
        2, 1, 1, place_array, queries, o_far, (far,), out_weights, lse_far, *back, (dk, dv)
    )
    dq = dq_own, dq_near, dq_far
    dkv_one = from_block(dkv_second, -1)
    dkv_two = from_block(dkv_first, -2)
    wide_other, wide_own = wide_grads(
        core_array, normed_one, (dh1_low, ahead, far, behind), (o_own, o_near, o_far), dq
    )
    dkv_one, dkv_two, wide_other, out_pieces = keep((dkv_one, dkv_two, wide_other, out_pieces))
    wide_other = shift(wide_other, "core", 1)

    narrow_other, narrow_own, dnormed_one, gain_grads = finish(
        core_place,
        normed_one,
        qkv_weights,
        dq,
        dkv_own,
        dkv_one,
        dkv_two,
        cosine,
        sine,
        gains,
        grad_gain_two,
    )
    dnormed_one = lax.psum_scatter(dnormed_one, "head", scatter_dimension=0, tiled=True)
    gain_grads = exchange([gain_grads] * 4, "head")
    rows = [(x_rows.shape, BF16)]
    (output,) = small_call(output_kernel, rows, h1, *out_pieces)
    gain_grads, output = keep((gain_grads, output))
    pieces, out_sums = first_pieces(
        at, wide_own, wide_other, narrow_own, shift(narrow_other, "core", 1), gain_grads
    )
    grads = (
        grads[:, :HIDDEN].astype(F32),
        grads[:, HIDDEN : 2 * HIDDEN].astype(F32),
        grads[:, 2 * HIDDEN :].T.astype(F32),
    )
    pieces, out_sums, grads = keep((exchange(pieces, "x"), exchange(out_sums, "y"), grads))
    pieces, out_sums = second_pieces(at, pieces, out_sums)
    (grad_inputs,) = small_call(input_grad_kernel, rows, dh1, x_rows, gains, dnormed_one)
    pieces, out_sums, grad_inputs = keep((exchange(pieces, "y"), exchange(out_sums, "x"), grad_inputs))
    (gain_grads,) = small_call(gains_kernel, [((GAIN_ROWS, GAIN_COLUMNS), F32)], *pieces)
    columns = (64, 512), (64, 512), (64, 64), (64, 64), (1, 2048), (1, 2048)
    grad_out, grad_query, grad_key, grad_value, grad_gain_one, grad_gain_two = small_call(
        attention_grads_kernel,
        [(shape, F32) for shape in columns],
        *pieces,
        *out_sums,
        gain_grads,
        shift(gain_grads, "core", 1),
    )

    return (
        output[None],
        grad_inputs[None],
        grad_query,
        grad_key,
        grad_value,
        grad_out.T,
        *grads,
        grad_gain_one.reshape(2048),
        grad_gain_two.reshape(2048),
    )


def solution(mesh):
    grid = Mesh(mesh.devices.reshape(4, 4, 4, 2), ("head", "y", "x", "core"))
    rows, up, down = P(BLK, "head", None), P(BLK, "head"), P("head", BLK)
    return jax.shard_map(
        per_device,
        mesh=grid,
        in_specs=(rows, P(), up, up, up, down, up, up, down, P(), P(), rows),
        out_specs=(rows, rows, up, up, up, down, up, up, down, P(), P()),
        check_vma=False,
    )
```

```python
import functools

import jax
import jax.numpy as jnp
from jax import lax
from jax.experimental import pallas as pl
from jax.experimental.pallas import tpu as pltpu
from jax.sharding import Mesh
from jax.sharding import PartitionSpec as P

HEAD_SIZE = 64
WINDOW = 1024
HIDDEN = 1408
EPSILON = 1e-05
BF16 = jnp.bfloat16
F32 = jnp.float32
BLK = ("y", "x", "core")
CORE_FIRST = ("core", "y", "x")
VMEM_LIMIT = 63 * 1024 * 1024


def dot_nn(a, b):
    return jnp.dot(a, b, preferred_element_type=F32)


def dot_nt(a, b):
    return lax.dot_general(a, b, (((1,), (1,)), ((), ())), preferred_element_type=F32)


def dot_tn(a, b):
    return lax.dot_general(a, b, (((0,), (0,)), ((), ())), preferred_element_type=F32)


def shift(value, axis, distance):
    size = lax.axis_size(axis)
    return lax.ppermute(value, axis, [(i, (i + distance) % size) for i in range(size)])


def add_low(a, b):
    return (a.astype(F32) + b.astype(F32)).astype(BF16)


def gather_pieces(rows):
    return shift(rows, "head", -1), shift(rows, "head", 2), shift(rows, "head", 1)


def near_pieces(rows):
    return shift(rows, "head", -1), shift(rows, "head", 1)


def far_pieces(ahead, behind):
    half = ahead.shape[0] // 2
    return shift(behind[:half], "head", 1), shift(ahead[half:], "head", -1)


def scatter_pieces(own, ahead, far, behind):
    return own, shift(ahead, "head", 1), shift(behind, "head", -1), shift(far, "head", 2)


def gather_axis(value, axis):
    return value, shift(value, axis, -1), shift(value, axis, 2), shift(value, axis, 1)


def exchange(pieces, axis):
    return pieces[0], shift(pieces[1], axis, 1), shift(pieces[2], axis, 2), shift(pieces[3], axis, -1)


def from_block(value, distance):
    route = [(i, i + distance) for i in range(32) if 0 <= i + distance < 32]
    return lax.ppermute(value, BLK, route)


def scale_of(values):
    return lax.rsqrt(jnp.mean(values * values, -1, keepdims=True) + EPSILON)


def x_of(code):
    return lax.shift_right_logical(code[0], 5)


def y_of(code):
    return lax.shift_right_logical(code[0], 3) & 3


def core_of(code):
    return lax.shift_right_logical(code[0], 2) & 1


def place_of(code):
    return code[0] & 3


def lane_is_low(shape, period):
    return lax.broadcasted_iota(jnp.int32, shape, len(shape) - 1) % period < period // 2


def turn(values, cosine, sine):
    swapped = jnp.where(
        lane_is_low(values.shape, 64), pltpu.roll(values, 96, 1), pltpu.roll(values, 32, 1)
    )
    return values * cosine + swapped * sine


def core_major_tiles(tiles):
    low = lane_is_low(tiles[0].shape, 128)
    rolled = [pltpu.roll(tile, 64, 1) for tile in tiles]
    first = [jnp.where(low, tiles[2 * k], rolled[2 * k + 1]) for k in range(8)]
    second = [jnp.where(low, rolled[2 * k], tiles[2 * k + 1]) for k in range(8)]
    return first + second


def block_major_tiles(tiles):
    low = lane_is_low(tiles[0].shape, 128)
    rolled = [pltpu.roll(tile, 64, 1) for tile in tiles]
    result = []
    for k in range(8):
        result.append(jnp.where(low, tiles[k], rolled[8 + k]))
        result.append(jnp.where(low, rolled[k], tiles[8 + k]))
    return result


def in_tiles(value):
    return [value[:, 128 * k : 128 * k + 128] for k in range(16)]


def prepare_kernel(x_ref, dy_ref, gain_ref, x_out, dy_out, normed_out, gain_out):
    def convert(ref):
        return jnp.concatenate(core_major_tiles(in_tiles(ref[...].astype(F32))), 1)

    x, gains = convert(x_ref), convert(gain_ref)
    gain_out[...] = gains
    x_out[...] = x
    dy_out[...] = convert(dy_ref).astype(BF16)
    normed_out[...] = (x * scale_of(x) * gains[:1]).astype(BF16)


def prepare(x, dy, gains):
    rows, width = x.shape
    return pl.pallas_call(
        prepare_kernel,
        out_shape=(
            jax.ShapeDtypeStruct((rows, width), F32),
            jax.ShapeDtypeStruct((rows, width), BF16),
            jax.ShapeDtypeStruct((rows, width), BF16),
            jax.ShapeDtypeStruct(gains.shape, F32),
        ),
        compiler_params=pltpu.CompilerParams(vmem_limit_bytes=VMEM_LIMIT),
        cost_estimate=pl.CostEstimate(
            flops=10 * rows * width, bytes_accessed=10 * rows * width, transcendentals=rows
        ),
    )(x, dy, gains)


def to_blocks(value):
    return jnp.concatenate(block_major_tiles(in_tiles(value)), 1)


def assemble_kernel(core_ref, own_ref, ahead_ref, far_ref, behind_ref, out_ref, swap_ref):
    out_ref[:128] = own_ref[...]
    start = 128
    for ref in (ahead_ref, far_ref, behind_ref):
        size = ref.shape[0]
        out_ref[start : start + size] = jnp.concatenate(
            core_major_tiles(in_tiles(ref[...].astype(F32))), 1
        ).astype(BF16)
        start += size
    swap_ref[...] = jnp.where(core_of(core_ref) == 0, out_ref[:, 1024:], out_ref[:, :1024])


def assemble(core, own, ahead, far, behind):
    vmem = pl.BlockSpec(memory_space=pltpu.VMEM)
    return pl.pallas_call(
        assemble_kernel,
        out_shape=(jax.ShapeDtypeStruct((512, 2048), BF16), jax.ShapeDtypeStruct((512, 1024), BF16)),
        in_specs=[pl.BlockSpec(memory_space=pltpu.SMEM)] + [vmem] * 4,
        out_specs=(vmem, vmem),
        compiler_params=pltpu.CompilerParams(vmem_limit_bytes=VMEM_LIMIT),
        cost_estimate=pl.CostEstimate(
            flops=4 * 512 * 2048, bytes_accessed=5 * 1024 * 1024, transcendentals=0
        ),
    )(core, own, ahead, far, behind)


def small_call(kernel, out_shape, *operands):
    return pl.pallas_call(
        kernel,
        out_shape=tuple(jax.ShapeDtypeStruct(shape, dtype) for shape, dtype in out_shape),
        compiler_params=pltpu.CompilerParams(vmem_limit_bytes=VMEM_LIMIT),
        cost_estimate=pl.CostEstimate(
            flops=sum(x.size for x in operands),
            bytes_accessed=2 * sum(x.size * x.dtype.itemsize for x in operands),
            transcendentals=0,
        ),
    )(*operands)


def total_of(refs):
    values = [ref[...].astype(F32) for ref in refs]
    while len(values) > 1:
        values = [values[0] + values[1]] + values[2:]
    return values[0]


def join_kernel(x_ref, gain_ref, a_ref, b_ref, c_ref, d_ref, h_out, top_out, bottom_out):
    h = x_ref[...] + total_of((a_ref, b_ref, c_ref, d_ref))
    h_out[...] = h
    normed = (h * scale_of(h) * gain_ref[1:2]).astype(BF16)
    half = h.shape[0] // 2
    top_out[...], bottom_out[...] = normed[:half], normed[half:]


def join(x, gain, pieces):
    half = x.shape[0] // 2, x.shape[1]
    return small_call(join_kernel, ((x.shape, F32), (half, BF16), (half, BF16)), x, gain, *pieces)


def norm_backward(values, gain, grad):
    scale = scale_of(values)
    weighted = grad * gain
    inner = jnp.mean(weighted * values, -1, keepdims=True)
    return scale * weighted - values * (scale * scale * scale * inner), scale


def join_back_kernel(h_ref, dy_ref, gain_ref, a_ref, b_ref, c_ref, d_ref, dh_out, low_out, grad_out):
    h, grad = h_ref[...], total_of((a_ref, b_ref, c_ref, d_ref))
    back, scale = norm_backward(h, gain_ref[1:2], grad)
    dh = dy_ref[...].astype(F32) + back
    dh_out[...] = dh
    low_out[...] = dh.astype(BF16)
    grad_out[...] = to_blocks(jnp.broadcast_to(jnp.sum(grad * h * scale, 0, keepdims=True), (8, h.shape[1])))


def join_back(h, dy, gain, pieces):
    shapes = (h.shape, F32), (h.shape, BF16), ((8, h.shape[1]), F32)
    return small_call(join_back_kernel, shapes, h, dy, gain, *pieces)


def output_kernel(h_ref, a_ref, b_ref, c_ref, d_ref, out_ref):
    out_ref[...] = to_blocks(h_ref[...] + total_of((a_ref, b_ref, c_ref, d_ref))).astype(BF16)


def input_grad_kernel(dh_ref, x_ref, gain_ref, grad_ref, out_ref):
    back, _ = norm_backward(x_ref[...], gain_ref[:1], grad_ref[...].astype(F32))
    out_ref[...] = to_blocks(dh_ref[...] + back).astype(BF16)


GAIN_ROWS, GAIN_COLUMNS = 16, 256


def gain_rows(vector):
    return jnp.concatenate([vector[:, 256 * k : 256 * k + 256] for k in range(8)], 0)


def put_piece(ref, rows, gains):
    count = rows.shape[0]
    ref[:count] = rows
    ref[count:, GAIN_COLUMNS:] = jnp.zeros((GAIN_ROWS, ref.shape[1] - GAIN_COLUMNS), BF16)
    ref[count:, :GAIN_COLUMNS] = gains.astype(BF16)


def first_pieces_kernel(
    at_ref, q_ref, q2_ref, kv_ref, kv2_ref, o_ref, o2_ref, *refs
):
    gain_refs, out_refs = refs[:4], refs[4:]
    query = add_low(q_ref[...], q2_ref[...]).reshape(256, 512)
    narrow = add_low(kv_ref[...], kv2_ref[...]).reshape(256, 128)
    rows = jnp.concatenate([query, narrow], 1)
    out_rows = add_low(o_ref[...], o2_ref[...]).reshape(256, 512)
    gains = total_of(gain_refs)
    gains = gains[:GAIN_ROWS] + gains[GAIN_ROWS:]
    for number in range(4):

        @pl.when(pl.program_id(0) == number)
        def _():
            put_piece(out_refs[number], rows, gains)
            out_refs[4 + number][...] = out_rows


def first_pieces(at, wide, wide2, narrow, narrow2, gains):
    pick_x = lambda column: lambda d, s: (0, lax.rem(x_of(s) + d, 4), 0, column)
    pick_y = lambda d, s: (lax.rem(y_of(s) + d, 4), 0, 0, 0)
    whole = lambda d, s: (0, 0)
    shaped = lambda value: value.reshape(4, 4, 64, value.shape[1])
    shapes = [(256 + GAIN_ROWS, 640)] * 4 + [(256, 512)] * 4
    grid = pltpu.PrefetchScalarGridSpec(
        num_scalar_prefetch=1,
        grid=(4,),
        in_specs=[pl.BlockSpec((4, 1, 64, 512), pick_x(1))] * 2
        + [pl.BlockSpec((4, 1, 64, 128), pick_x(0))] * 2
        + [pl.BlockSpec((1, 4, 64, 512), pick_y)] * 2
        + [pl.BlockSpec((2 * GAIN_ROWS, GAIN_COLUMNS), whole)] * 4,
        out_specs=tuple(pl.BlockSpec(shape, whole) for shape in shapes),
    )
    wide, wide2 = shaped(wide), shaped(wide2)
    result = pl.pallas_call(
        first_pieces_kernel,
        grid_spec=grid,
        out_shape=tuple(jax.ShapeDtypeStruct(shape, BF16) for shape in shapes),
        compiler_params=pltpu.CompilerParams(vmem_limit_bytes=VMEM_LIMIT),
        cost_estimate=pl.CostEstimate(
            flops=2 * 1024 * 1152, bytes_accessed=6 * 1024 * 1152, transcendentals=0
        ),
    )(at, wide, wide2, shaped(narrow), shaped(narrow2), wide, wide2, *gains)
    return result[:4], result[4:]


def second_pieces_kernel(at_ref, *refs):
    qkv, out, (held, out_held) = refs[:4], refs[4:8], refs[16:]
    held[...] = total_of(qkv)
    out_held[...] = total_of(out).astype(BF16)
    for number in range(4):
        y = pl.multiple_of(lax.rem(y_of(at_ref) + number, 4) * 64, 64)
        put_piece(refs[8 + number], held[pl.ds(y, 64), :].astype(BF16), held[256:, :GAIN_COLUMNS])
        x = pl.multiple_of(lax.rem(x_of(at_ref) + number, 4) * 64, 64)
        refs[12 + number][...] = out_held[pl.ds(x, 64), :]


def second_pieces(at, qkv, out):
    vmem = pl.BlockSpec(memory_space=pltpu.VMEM)
    shapes = [(64 + GAIN_ROWS, 640)] * 4 + [(64, 512)] * 4
    result = pl.pallas_call(
        second_pieces_kernel,
        out_shape=tuple(jax.ShapeDtypeStruct(shape, BF16) for shape in shapes),
        in_specs=[pl.BlockSpec(memory_space=pltpu.SMEM)] + [vmem] * 8,
        out_specs=(vmem,) * 8,
        scratch_shapes=[pltpu.VMEM((256 + GAIN_ROWS, 640), F32), pltpu.VMEM((256, 512), BF16)],
        compiler_params=pltpu.CompilerParams(vmem_limit_bytes=VMEM_LIMIT),
        cost_estimate=pl.CostEstimate(
            flops=4 * 272 * 1152, bytes_accessed=10 * 272 * 1152, transcendentals=0
        ),
    )(at, *qkv, *out)
    return result[:4], result[4:]


def attention_grads_kernel(*refs):
    out_ref, q_ref, k_ref, v_ref, one_ref, two_ref = refs[8:]
    total = total_of(refs[:4])
    out_ref[...] = total_of(refs[4:8])
    q_ref[...] = total[:64, :512]
    k_ref[...] = total[:64, 512:576]
    v_ref[...] = total[:64, 576:]
    gains = total[64:, :GAIN_COLUMNS]
    one_ref[...] = jnp.concatenate([gains[k : k + 1] for k in range(8)], 1)
    two_ref[...] = jnp.concatenate([gains[k : k + 1] for k in range(8, 16)], 1)


def put_in_order(at_ref, own_ref, other_ref, columns, to_ref, sems):
    x, y, core = x_of(at_ref), y_of(at_ref), core_of(at_ref)
    copies = []
    for number in range(32):
        ref = (own_ref, other_ref)[number // 16]
        to_x, to_y = lax.rem(x + number % 4, 4), lax.rem(y + number // 4 % 4, 4)
        to_core = core if number < 16 else 1 - core
        row = pl.multiple_of(((to_core * 4 + to_y) * 4 + to_x) * 64, 64)
        copy = pltpu.make_async_copy(
            ref.at[pl.ds(number % 16 * 64, 64), columns], to_ref.at[pl.ds(row, 64)], sems.at[number]
        )
        copy.start()
        copies.append(copy)
    return copies


def project_kv_kernel(at_ref, x_ref, own_ref, other_ref, cos_ref, sin_ref, kv_ref, held, sems):
    for copy in put_in_order(at_ref, own_ref, other_ref, pl.ds(512, 128), held, sems):
        copy.wait()
    flat = dot_nn(x_ref[...], held[...])
    turned = turn(flat, cos_ref[...], sin_ref[...])
    kv_ref[...] = jnp.where(lane_is_low(flat.shape, 128), turned, flat).astype(BF16)


def project_q_kernel(at_ref, x_ref, own_ref, other_ref, cos_ref, sin_ref, q_ref, w_ref, held, sems, sem):
    for copy in put_in_order(at_ref, own_ref, other_ref, pl.ds(0, 640), held, sems):
        copy.wait()
    whole = pltpu.make_async_copy(held, w_ref, sem)
    whole.start()
    cosine, sine, x = cos_ref[...], sin_ref[...], x_ref[...]
    for start in (0, 256):
        wide = dot_nn(x, held[:, start : start + 256])
        for part in (0, 128):
            turned = turn(wide[:, part : part + 128], cosine, sine)
            q_ref[:, start + part : start + part + 128] = (turned * HEAD_SIZE**-0.5).astype(BF16)
    whole.wait()


def project(kernel, at, normed, weights, cosine, sine, columns, held_columns, hand_out):
    rows, width = normed.shape
    vmem, anywhere = pl.BlockSpec(memory_space=pltpu.VMEM), pl.BlockSpec(memory_space=pl.ANY)
    out_shape = [jax.ShapeDtypeStruct((rows, columns), BF16)]
    out_specs = [vmem]
    scratch = [pltpu.VMEM((width, held_columns), BF16), pltpu.SemaphoreType.DMA((32,))]
    if hand_out:
        out_shape.append(jax.ShapeDtypeStruct((width, held_columns), BF16))
        out_specs.append(anywhere)
        scratch.append(pltpu.SemaphoreType.DMA)
    return pl.pallas_call(
        kernel,
        out_shape=tuple(out_shape),
        in_specs=[pl.BlockSpec(memory_space=pltpu.SMEM), vmem, anywhere, anywhere, vmem, vmem],
        out_specs=tuple(out_specs),
        scratch_shapes=scratch,
        compiler_params=pltpu.CompilerParams(vmem_limit_bytes=VMEM_LIMIT),
        cost_estimate=pl.CostEstimate(
            flops=2 * rows * width * columns,
            bytes_accessed=2 * (rows * width + width * columns + rows * columns),
            transcendentals=0,
        ),
    )(at, normed, *weights, cosine, sine)


KEYS = 1152
PAIRS = 4


def set_up_kernel(place_ref, kv0_ref, kv1_ref, kv2_ref, kk_ref, vv_ref, kvt_ref):
    place = place_of(place_ref)
    low = lane_is_low((128, 128), 128)
    for block, ref in enumerate((kv0_ref, kv1_ref, kv2_ref)):
        for group in range(4):
            at = pl.multiple_of(lax.rem(group - place + 4, 4) * 128, 128)
            piece = ref[pl.ds(at, 128), :].astype(F32)
            rolled = pltpu.roll(piece, 64, 1)
            to = block * 512 + group * 128
            kk_ref[to : to + 128, :] = jnp.where(low, piece, rolled).astype(BF16)
            vv_ref[to : to + 128, :] = jnp.where(low, rolled, piece).astype(BF16)
            kvt_ref[:, to : to + 128] = piece.T.astype(BF16)


def set_up(place, kv):
    vmem = pl.BlockSpec(memory_space=pltpu.VMEM)
    return pl.pallas_call(
        set_up_kernel,
        out_shape=(
            jax.ShapeDtypeStruct((1536, 128), BF16),
            jax.ShapeDtypeStruct((1536, 128), BF16),
            jax.ShapeDtypeStruct((128, 1536), BF16),
        ),
        in_specs=[pl.BlockSpec(memory_space=pltpu.SMEM), vmem, vmem, vmem],
        out_specs=(vmem, vmem, vmem),
        compiler_params=pltpu.CompilerParams(vmem_limit_bytes=VMEM_LIMIT),
        cost_estimate=pl.CostEstimate(flops=1536 * 128 * 8, bytes_accessed=2 * 1024 * 1024, transcendentals=0),
    )(place, *kv)


def both_heads(pair):
    low = lane_is_low(pair.shape, 128)
    nothing = jnp.zeros_like(pair)
    return jnp.concatenate([jnp.where(low, pair, nothing), jnp.where(low, nothing, pair)], 0)


def side_by_side(transposed):
    return jnp.concatenate([transposed[:, :128], transposed[:, 128:]], 0).T


def mask_of(at, low_ref):
    key = lax.broadcasted_iota(jnp.int32, (KEYS, 128), 0)
    query = lax.broadcasted_iota(jnp.int32, (KEYS, 128), 1)
    seen = (key >= low_ref[:, pl.ds(at, 128)] - at) & (key <= query + WINDOW)
    bias = jnp.where(seen, 0.0, -jnp.inf)
    return jnp.concatenate([bias, bias], 1)


def attend_kernel(
    first, step, place_ref, q_ref, kk_ref, kvt_ref, low_ref, w_ref, o_ref, lse_ref, *refs
):
    part_refs, (bias, held, w_held, sem) = refs[:-4], refs[-4:]
    group = lax.rem(place_of(place_ref) + first + step * pl.program_id(0), 4)
    at = pl.multiple_of(group * 128, 128)

    load = pltpu.make_async_copy(w_ref.at[:, pl.ds(HIDDEN, 512)], w_held, sem)

    @pl.when((pl.program_id(0) == 0) & (pl.program_id(1) == 0))
    def _():
        load.start()

    @pl.when(pl.program_id(1) == 0)
    def _():
        bias[...] = mask_of(at, low_ref)

    keys = pl.ds(at, KEYS)
    for number in range(PAIRS):
        columns = slice(128 * number, 128 * number + 128)
        scores = dot_nt(kk_ref[keys, :], both_heads(q_ref[:, columns])) + bias[...]
        top = jnp.max(scores, 0, keepdims=True)
        weights = jnp.exp(scores - top)
        total = jnp.sum(weights, 0, keepdims=True)
        result = dot_nn(kvt_ref[64:128, keys], weights.astype(BF16)) / total
        lse_ref[0, number] = top + jnp.log(total)
        result = side_by_side(result).astype(BF16)
        o_ref[:, columns] = result
        held[PAIRS * pl.program_id(1) + number] = result

    @pl.when(pl.program_id(1) == 4 // PAIRS - 1)
    def _():
        @pl.when(pl.program_id(0) == 0)
        def _():
            load.wait()

        rows = jnp.concatenate([held[k] for k in range(4)], 1)
        part = dot_nt(rows, w_held[...]).astype(BF16)
        for number, ref in enumerate(part_refs):

            @pl.when(pl.program_id(0) == number)
            def _():
                ref[...] = part


def attend(first, step, count, place, queries, kk, kvt, low, weights):
    whole = lambda g, p, s: (0, 0)
    width = 128 * PAIRS
    grid = pltpu.PrefetchScalarGridSpec(
        num_scalar_prefetch=1,
        grid=(count, 4 // PAIRS),
        in_specs=[
            pl.BlockSpec((128, width), lambda g, p, s: (first + step * g, p)),
            pl.BlockSpec((1536, 128), whole),
            pl.BlockSpec((128, 1536), whole),
            pl.BlockSpec((1, 512), whole),
            pl.BlockSpec(memory_space=pl.ANY),
        ],
        out_specs=(
            pl.BlockSpec((128, width), lambda g, p, s: (g, p)),
            pl.BlockSpec((1, PAIRS, 1, 256), lambda g, p, s: (g, p, 0, 0)),
        )
        + (pl.BlockSpec((128, 2048), whole),) * count,
        scratch_shapes=[
            pltpu.VMEM((KEYS, 256), F32),
            pltpu.VMEM((4, 128, 128), BF16),
            pltpu.VMEM((2048, 512), BF16),
            pltpu.SemaphoreType.DMA,
        ],
    )
    return pl.pallas_call(
        functools.partial(attend_kernel, first, step),
        grid_spec=grid,
        out_shape=(
            jax.ShapeDtypeStruct((128 * count, 512), BF16),
            jax.ShapeDtypeStruct((count, 4, 1, 256), F32),
        )
        + (jax.ShapeDtypeStruct((128, 2048), BF16),) * count,
        compiler_params=pltpu.CompilerParams(vmem_limit_bytes=VMEM_LIMIT),
        cost_estimate=pl.CostEstimate(
            flops=count * 4 * KEYS * 256 * 256 * 2,
            bytes_accessed=3 * 1024 * 1024,
            transcendentals=count * 4 * KEYS * 256,
        ),
    )(place, queries, kk, kvt, low, weights)


def attend_back_kernel(first, step, count, *refs):
    last = first == 2
    place_ref, q_ref, w_ref, lse_ref, kk_ref, vv_ref, kvt_ref, low_ref, cos_ref, sin_ref = refs[:10]
    o_ref = refs[10]
    dh_refs, refs = refs[11 : 11 + count], refs[11 + count :]
    dk_in = dv_in = None
    if first > 0:
        dk_in, dv_in, refs = refs[0], refs[1], refs[2:]
    bias, do_held, dk, dv, w_held, sem = refs[-6:]
    dq_ref, outs = refs[0], refs[1:-6]
    number, pair = pl.program_id(0), pl.program_id(1)
    place = place_of(place_ref)
    at = pl.multiple_of(lax.rem(place + first + step * number, 4) * 128, 128)

    load = pltpu.make_async_copy(w_ref.at[:, pl.ds(HIDDEN, 512)], w_held, sem)

    @pl.when((number == 0) & (pair == 0))
    def _():
        load.start()
        dk[...] = jnp.zeros_like(dk) if dk_in is None else dk_in[...]
        dv[...] = jnp.zeros_like(dv) if dv_in is None else dv_in[...]

    @pl.when(pair == 0)
    def _():
        bias[...] = mask_of(at, low_ref)

        @pl.when(number == 0)
        def _():
            load.wait()

        for k, ref in enumerate(dh_refs):

            @pl.when(number == k)
            def _():
                do_rows = dot_nn(ref[...], w_held[...]).astype(BF16)
                for p in range(4):
                    do_held[p] = do_rows[:, 128 * p : 128 * p + 128]

    keys = pl.ds(at, KEYS)
    queries, grads, all_weights, all_grad_scores = [], [], [], []
    for k in range(PAIRS):
        columns = slice(128 * k, 128 * k + 128)
        do_pair = do_held[PAIRS * pair + k]
        query, grad = both_heads(q_ref[:, columns]), both_heads(do_pair)
        scores = dot_nt(kk_ref[keys, :], query) + bias[...]
        weights = jnp.exp(scores - lse_ref[0, k])
        grad_weights = dot_nt(vv_ref[keys, :], grad)
        product = (o_ref[:, columns].astype(F32) * do_pair.astype(F32)).T
        inner = jnp.concatenate(
            [jnp.sum(product[:64], 0, keepdims=True), jnp.sum(product[64:], 0, keepdims=True)], 1
        )
        grad_scores = (weights * (grad_weights - inner)).astype(BF16)
        grad_query = side_by_side(dot_nn(kvt_ref[0:64, keys], grad_scores)) * HEAD_SIZE**-0.5
        dq_ref[:, columns] = turn(grad_query, cos_ref[...], -sin_ref[...]).astype(BF16)
        queries.append(query)
        grads.append(grad)
        all_weights.append(weights.astype(BF16))
        all_grad_scores.append(grad_scores)
    join = lambda values, axis: values[0] if PAIRS == 1 else jnp.concatenate(values, axis)
    dv[keys, :] += dot_nn(join(all_weights, 1), join(grads, 0))
    dk[keys, :] += dot_nn(join(all_grad_scores, 1), join(queries, 0))

    @pl.when((number == pl.num_programs(0) - 1) & (pair == 4 // PAIRS - 1))
    def _():
        if not last:
            outs[0][...], outs[1][...] = dk[...], dv[...]
            return
        half = lane_is_low((128, 128), 128)
        for block in range(3):
            for group in range(4):
                to = pl.multiple_of(lax.rem(group - place + 4, 4) * 128, 128)
                frm = slice(block * 512 + group * 128, block * 512 + group * 128 + 128)
                key, value = dk[frm, :], dv[frm, :]
                key = key + pltpu.roll(key, 64, 1)
                value = value + pltpu.roll(value, 64, 1)
                both = jnp.where(half, key, value)
                outs[block][pl.ds(to, 128), :] = both.astype(outs[block].dtype)


def attend_back(first, step, count, place, queries, o, dh, weights, lse, kk, vv, kvt, low, cosine, sine, held):
    last = first == 2
    whole = lambda g, p, s: (0, 0)
    specs = [
        pl.BlockSpec((128, 128 * PAIRS), lambda g, p, s: (first + step * g, p)),
        pl.BlockSpec(memory_space=pl.ANY),
        pl.BlockSpec((1, PAIRS, 1, 256), lambda g, p, s: (g, p, 0, 0)),
        pl.BlockSpec((1536, 128), whole),
        pl.BlockSpec((1536, 128), whole),
        pl.BlockSpec((128, 1536), whole),
        pl.BlockSpec((1, 512), whole),
        pl.BlockSpec((128, 128), lambda g, p, s: (first + step * g, 0)),
        pl.BlockSpec((128, 128), lambda g, p, s: (first + step * g, 0)),
    ]
    specs += [pl.BlockSpec((128, 128 * PAIRS), lambda g, p, s: (g, p))]
    specs += [pl.BlockSpec((128, 2048), whole)] * count + [pl.BlockSpec((1536, 128), whole)] * len(held)
    if last:
        out_specs = (pl.BlockSpec((512, 128), whole),) * 3
        out_shape = tuple(jax.ShapeDtypeStruct((512, 128), dtype) for dtype in (BF16, BF16, F32))
    else:
        out_specs = (pl.BlockSpec((1536, 128), whole),) * 2
        out_shape = (jax.ShapeDtypeStruct((1536, 128), F32),) * 2
    grid = pltpu.PrefetchScalarGridSpec(
        num_scalar_prefetch=1,
        grid=(count, 4 // PAIRS),
        in_specs=specs,
        out_specs=(pl.BlockSpec((128, 128 * PAIRS), lambda g, p, s: (g, p)),) + out_specs,
        scratch_shapes=[
            pltpu.VMEM((KEYS, 256), F32),
            pltpu.VMEM((4, 128, 128), BF16),
            pltpu.VMEM((1536, 128), F32),
            pltpu.VMEM((1536, 128), F32),
            pltpu.VMEM((2048, 512), BF16),
            pltpu.SemaphoreType.DMA,
        ],
    )
    return pl.pallas_call(
        functools.partial(attend_back_kernel, first, step, count),
        grid_spec=grid,
        out_shape=(jax.ShapeDtypeStruct((128 * count, 512), BF16),) + out_shape,
        compiler_params=pltpu.CompilerParams(vmem_limit_bytes=VMEM_LIMIT),
        cost_estimate=pl.CostEstimate(
            flops=count * 4 * KEYS * 256 * 640 * 2,
            bytes_accessed=6 * 1024 * 1024,
            transcendentals=count * 4 * KEYS * 256,
        ),
    )(place, queries, weights, lse, kk, vv, kvt, low, cosine, sine, o, *dh, *held)


GROUPS = [(0, 128), (128, 256), (384, 512), (896, 512)]


def columns_times_kernel(left_ref, right_ref, out_ref, left, right, out, sems, out_sems):
    load = pltpu.make_async_copy(left_ref, left, sems.at[len(GROUPS)])
    load.start()
    copies, results = [], []
    for number, (start, width) in enumerate(GROUPS):
        columns = pl.ds(start, width)
        copy = pltpu.make_async_copy(right_ref.at[:, columns], right.at[:, columns], sems.at[number])
        copy.start()
        copies.append(copy)
    load.wait()
    value = left[...]
    for number, (start, width) in enumerate(GROUPS):
        copies[number].wait()
        out[:, start : start + width] = dot_nn(value, right[:, start : start + width])
        columns = pl.ds(start, width)
        copy = pltpu.make_async_copy(out.at[:, columns], out_ref.at[:, columns], out_sems.at[number])
        copy.start()
        results.append(copy)
    for copy in results:
        copy.wait()


def columns_times(left, right):
    rows, width = left.shape
    anywhere = pl.BlockSpec(memory_space=pl.ANY)
    return pl.pallas_call(
        columns_times_kernel,
        out_shape=jax.ShapeDtypeStruct((rows, HIDDEN), F32),
        in_specs=[anywhere, anywhere],
        out_specs=anywhere,
        scratch_shapes=[
            pltpu.VMEM((rows, width), BF16),
            pltpu.VMEM((width, HIDDEN), BF16),
            pltpu.VMEM((rows, HIDDEN), F32),
            pltpu.SemaphoreType.DMA((len(GROUPS) + 1,)),
            pltpu.SemaphoreType.DMA((len(GROUPS),)),
        ],
        compiler_params=pltpu.CompilerParams(vmem_limit_bytes=VMEM_LIMIT),
        cost_estimate=pl.CostEstimate(
            flops=2 * rows * width * HIDDEN, bytes_accessed=11 * 1024 * 1024, transcendentals=0
        ),
    )(left, right)


PIECES = [(0, 128), (128, 128), (256, 128), (384, 128)]


def ffn_kernel(*refs):
    core_ref, x_refs, dact_ref, w_ref = refs[0], refs[1:9], refs[9], refs[10]
    gua_ref, whole_ref, swap_ref, dx_refs = refs[11], refs[12], refs[13], refs[14:18]
    x_held, dact_held, w_held, gua, dx, sems, out_sems = refs[18:]
    x_copies = []
    for number in range(8):
        copy = pltpu.make_async_copy(
            x_refs[number], x_held.at[pl.ds(64 * number, 64)], sems.at[12 + number]
        )
        copy.start()
        x_copies.append(copy)
    copies = []
    for number, (start, width) in enumerate(GROUPS):
        for part in range(3):
            if part < 2:
                columns = pl.ds(part * HIDDEN + start, width)
                copy = pltpu.make_async_copy(
                    w_ref.at[:, columns], w_held.at[:, columns], sems.at[3 * number + part]
                )
            else:
                columns = pl.ds(start, width)
                copy = pltpu.make_async_copy(
                    dact_ref.at[:, columns], dact_held.at[:, columns], sems.at[3 * number + part]
                )
            copy.start()
            copies.append(copy)
    for copy in x_copies:
        copy.wait()
    half = pl.multiple_of((1 - core_of(core_ref)) * 1024, 1024)
    results = [
        pltpu.make_async_copy(x_held, whole_ref, out_sems.at[5]),
        pltpu.make_async_copy(x_held.at[:, pl.ds(half, 1024)], swap_ref, out_sems.at[6]),
    ]
    for copy in results:
        copy.start()
    x = x_held[...]
    for number, (start, width) in enumerate(GROUPS):
        for part in range(3):
            copies[3 * number + part].wait()
        gate = dot_nn(x, w_held[:, start : start + width])
        up = dot_nn(x, w_held[:, HIDDEN + start : HIDDEN + start + width])
        dact = dact_held[:, start : start + width]
        sig = jax.nn.sigmoid(gate)
        silu = gate * sig
        dgate = dact * up * (sig * (1.0 + gate * (1.0 - sig)))
        gua[:, start : start + width] = dgate.astype(BF16)
        gua[:, HIDDEN + start : HIDDEN + start + width] = (dact * silu).astype(BF16)
        gua[:, 2 * HIDDEN + start : 2 * HIDDEN + start + width] = (silu * up).astype(BF16)
    copy = pltpu.make_async_copy(gua, gua_ref, out_sems.at[4])
    copy.start()
    results.append(copy)
    dgu = gua[:, : 2 * HIDDEN]
    for number in range(4):
        columns = slice(512 * number, 512 * number + 512)
        dx[:, columns] = dot_nt(dgu, w_held[columns, : 2 * HIDDEN]).astype(BF16)
    for number, (start, size) in enumerate(PIECES):
        copy = pltpu.make_async_copy(dx.at[pl.ds(start, size)], dx_refs[number], out_sems.at[number])
        copy.start()
        results.append(copy)
    for copy in results:
        copy.wait()


def ffn(core, pieces, dact, weights):
    rows, width = dact.shape[0], weights.shape[0]
    anywhere = pl.BlockSpec(memory_space=pl.ANY)
    result = pl.pallas_call(
        ffn_kernel,
        out_shape=(
            jax.ShapeDtypeStruct((rows, 3 * HIDDEN), BF16),
            jax.ShapeDtypeStruct((rows, width), BF16),
            jax.ShapeDtypeStruct((rows, width // 2), BF16),
            *(jax.ShapeDtypeStruct((size, width), BF16) for _, size in PIECES),
        ),
        in_specs=[pl.BlockSpec(memory_space=pltpu.SMEM)] + [anywhere] * 10,
        out_specs=(anywhere,) * 7,
        scratch_shapes=[
            pltpu.VMEM((rows, width), BF16),
            pltpu.VMEM((rows, HIDDEN), F32),
            pltpu.VMEM((width, 2 * HIDDEN), BF16),
            pltpu.VMEM((rows, 3 * HIDDEN), BF16),
            pltpu.VMEM((rows, width), BF16),
            pltpu.SemaphoreType.DMA((20,)),
            pltpu.SemaphoreType.DMA((7,)),
        ],
        compiler_params=pltpu.CompilerParams(vmem_limit_bytes=VMEM_LIMIT),
        cost_estimate=pl.CostEstimate(
            flops=8 * rows * width * HIDDEN,
            bytes_accessed=25 * 1024 * 1024,
            transcendentals=rows * HIDDEN,
        ),
    )(core, *pieces, dact, weights)
    return result[0], result[1], result[2], result[3:]


def weight_grads_kernel(core_ref, x_ref, x2_ref, dy_ref, dy2_ref, right_ref, right2_ref, out_ref):
    part = pl.program_id(0)

    @pl.when(part < 2)
    def _():
        total = dot_tn(x_ref[...], right_ref[...]) + dot_tn(x2_ref[...], right2_ref[...])
        out_ref[...] = total.astype(BF16)

    @pl.when(part == 2)
    def _():
        total = dot_tn(dy_ref[...], right_ref[...]) + dot_tn(dy2_ref[...], right2_ref[...])
        out_ref[...] = total.astype(BF16)


def weight_grads(core, x, x2, dy, dy2, right, right2):
    rows = x.shape[0]
    tile = 1024
    half = x2.shape[1]
    tiles = half // tile
    own = lambda j, i, c: (0, core_of(c) * tiles + i)
    other = lambda j, i, c: (0, i)
    side = lambda j, i, c: (0, j)
    grid = pltpu.PrefetchScalarGridSpec(
        num_scalar_prefetch=1,
        grid=(3, tiles),
        in_specs=[
            pl.BlockSpec((rows, tile), own),
            pl.BlockSpec((rows, tile), other),
            pl.BlockSpec((rows, tile), own),
            pl.BlockSpec((rows, tile), other),
            pl.BlockSpec((rows, HIDDEN), side),
            pl.BlockSpec((rows, HIDDEN), side),
        ],
        out_specs=pl.BlockSpec((tile, HIDDEN), lambda j, i, c: (i, j)),
    )
    return pl.pallas_call(
        weight_grads_kernel,
        grid_spec=grid,
        out_shape=jax.ShapeDtypeStruct((half, 3 * HIDDEN), BF16),
        compiler_params=pltpu.CompilerParams(vmem_limit_bytes=VMEM_LIMIT),
        cost_estimate=pl.CostEstimate(
            flops=2 * 3 * 2 * rows * half * HIDDEN, bytes_accessed=24 * 1024 * 1024, transcendentals=0
        ),
    )(core, x, x2, dy, dy2, right, right2)


def rows_times_kernel(left_ref, right_ref, *out_refs):
    result = dot_nt(left_ref[...], right_ref[...]).astype(BF16)
    for number, ref in enumerate(out_refs):
        ref[...] = result[128 * number : 128 * number + 128]


def rows_times(left, left_part, right, part):
    rows, depth = left.shape[0], HIDDEN
    width = right.shape[0]
    tile = 512
    return pl.pallas_call(
        rows_times_kernel,
        out_shape=(jax.ShapeDtypeStruct((128, width), BF16),) * 4,
        grid=(width // tile,),
        in_specs=[
            pl.BlockSpec((rows, depth), lambda i: (0, left_part)),
            pl.BlockSpec((tile, depth), lambda i: (i, part)),
        ],
        out_specs=(pl.BlockSpec((128, tile), lambda i: (0, i)),) * 4,
        compiler_params=pltpu.CompilerParams(vmem_limit_bytes=VMEM_LIMIT),
        cost_estimate=pl.CostEstimate(
            flops=2 * rows * depth * width,
            bytes_accessed=2 * (rows * depth + width * depth + rows * width),
            transcendentals=0,
        ),
    )(left, right)


def ring_rows(own, near, far):
    return jnp.concatenate([own, near[:128], far, near[128:]], 0)


def put_half(number, value, other_ref, own_ref):
    @pl.when(number < 2)
    def _():
        other_ref[...] = value

    @pl.when(number >= 2)
    def _():
        own_ref[...] = value


def tile_at(i, c):
    return lax.rem(i + 2 * (1 - core_of(c)), 4)


def half_specs(tile, columns):
    return (
        pl.BlockSpec((tile, columns), lambda i, c: (jnp.minimum(i, 1), 0)),
        pl.BlockSpec((tile, columns), lambda i, c: (jnp.maximum(i - 2, 0), 0)),
    )


def wide_grads_kernel(
    core_ref, x_ref, dh0, dh1, dh2, dh3, o0, o1, o2, dq0, dq1, dq2, other_ref, own_ref, o_held, dq_held
):
    number = pl.program_id(0)

    @pl.when(number == 0)
    def _():
        o_held[...] = ring_rows(o0[...], o1[...], o2[...])
        dq_held[...] = ring_rows(dq0[...], dq1[...], dq2[...])

    dh = jnp.concatenate([ref[...] for ref in (dh0, dh1, dh2, dh3)], 0)
    out = dot_tn(dh, o_held[...])
    query = dot_tn(x_ref[...], dq_held[...])
    put_half(number, jnp.concatenate([out, query], 1).astype(BF16), other_ref, own_ref)


def wide_grads(core, normed, dh, o, dq):
    rows, width = normed.shape
    tile = 512
    whole = lambda i, c: (0, 0)
    column = lambda i, c: (0, tile_at(i, c))
    small = [pl.BlockSpec((size, 512), whole) for size in (128, 256, 128)]
    grid = pltpu.PrefetchScalarGridSpec(
        num_scalar_prefetch=1,
        grid=(4,),
        in_specs=[pl.BlockSpec((rows, tile), column)]
        + [pl.BlockSpec((128, tile), column)] * 4
        + small
        + small,
        out_specs=half_specs(tile, 1024),
        scratch_shapes=[pltpu.VMEM((rows, 512), BF16), pltpu.VMEM((rows, 512), BF16)],
    )
    return pl.pallas_call(
        wide_grads_kernel,
        grid_spec=grid,
        out_shape=(jax.ShapeDtypeStruct((width // 2, 1024), BF16),) * 2,
        compiler_params=pltpu.CompilerParams(vmem_limit_bytes=VMEM_LIMIT),
        cost_estimate=pl.CostEstimate(
            flops=2 * rows * width * 1024, bytes_accessed=10 * 1024 * 1024, transcendentals=0
        ),
    )(core, normed, *dh, *o, *dq)


def finish_kernel(
    core_ref,
    x_ref,
    w_ref,
    dq0_ref,
    dq1_ref,
    dq2_ref,
    own_ref,
    one_ref,
    two_ref,
    cos_ref,
    sin_ref,
    norm_ref,
    second_ref,
    other_grad_ref,
    own_grad_ref,
    dx_ref,
    gain_ref,
    dqkv,
    sums,
):
    number = pl.program_id(0)

    @pl.when(number == 0)
    def _():
        dqkv[:, :512] = ring_rows(dq0_ref[...], dq1_ref[...], dq2_ref[...])
        dkv = own_ref[...] + one_ref[...].astype(F32) + two_ref[...].astype(F32)
        turned = turn(dkv, cos_ref[...], -sin_ref[...])
        dqkv[:, 512:] = jnp.where(lane_is_low(dkv.shape, 128), turned, dkv).astype(BF16)

    x = x_ref[...]
    put_half(number, dot_tn(x, dqkv[:, 512:]).astype(BF16), other_grad_ref, own_grad_ref)
    dx = dot_nt(dqkv[...], w_ref[...])
    for piece in range(4):
        row = pl.multiple_of(lax.rem(place_of(core_ref) + piece, 4) * 128, 128)
        dx_ref[pl.ds(row, 128), :] = dx[128 * piece : 128 * piece + 128].astype(BF16)
    columns = pl.ds(pl.multiple_of(tile_at(number, core_ref) * 512, 512), 512)
    sums[:, columns] = jnp.broadcast_to(
        jnp.sum(dx * x.astype(F32), 0, keepdims=True) / norm_ref[:1], (8, 512)
    )

    @pl.when(number == 3)
    def _():
        gain_ref[:8] = gain_rows(to_blocks(sums[...])[:1])
        gain_ref[8:] = gain_rows(second_ref[:1])


def finish(core, normed, weights, dq, own, one, two, cosine, sine, gain, second):
    rows, width = normed.shape
    tile = 512
    whole = lambda i, c: (0, 0)
    column = lambda i, c: (0, tile_at(i, c))
    narrow = pl.BlockSpec((rows, 128), whole)
    grid = pltpu.PrefetchScalarGridSpec(
        num_scalar_prefetch=1,
        grid=(4,),
        in_specs=[
            pl.BlockSpec((rows, tile), column),
            pl.BlockSpec((tile, 640), lambda i, c: (tile_at(i, c), 0)),
            pl.BlockSpec((128, 512), whole),
            pl.BlockSpec((256, 512), whole),
            pl.BlockSpec((128, 512), whole),
            narrow,
            narrow,
            narrow,
            narrow,
            narrow,
            pl.BlockSpec((2, tile), column),
            pl.BlockSpec((8, width), whole),
        ],
        out_specs=half_specs(tile, 128)
        + (pl.BlockSpec((rows, tile), column),)
        + (pl.BlockSpec((GAIN_ROWS, GAIN_COLUMNS), whole),),
        scratch_shapes=[pltpu.VMEM((rows, 640), BF16), pltpu.VMEM((8, width), F32)],
    )
    result = pl.pallas_call(
        finish_kernel,
        grid_spec=grid,
        out_shape=(jax.ShapeDtypeStruct((width // 2, 128), BF16),) * 2
        + (jax.ShapeDtypeStruct((rows, width), BF16),)
        + (jax.ShapeDtypeStruct((GAIN_ROWS, GAIN_COLUMNS), F32),),
        compiler_params=pltpu.CompilerParams(vmem_limit_bytes=VMEM_LIMIT),
        cost_estimate=pl.CostEstimate(
            flops=2 * rows * width * 768, bytes_accessed=10 * 1024 * 1024, transcendentals=0
        ),
    )(core, normed, weights, *dq, own, one, two, cosine, sine, gain, second)
    return result


def per_device(
    tokens,
    segments,
    w_query,
    key_projection,
    value_projection,
    w_out,
    w_gate,
    w_up,
    w_down,
    norm_attn,
    norm_ffn,
    cotangent,
):
    place, core = lax.axis_index("head"), lax.axis_index("core")
    block = (lax.axis_index("y") * 4 + lax.axis_index("x")) * 2 + core
    code = (((lax.axis_index("x") * 4 + lax.axis_index("y")) * 2 + core) * 4 + place).astype(jnp.int32)
    code = code.reshape(1)
    keep = lax.optimization_barrier


    out_weights = lax.all_gather(
        jnp.concatenate([w_down.T, w_out.T], 1), CORE_FIRST, axis=0, tiled=True
    )
    ffn_weights = lax.all_gather(jnp.concatenate([w_gate, w_up], 1), CORE_FIRST, axis=0, tiled=True)

    x_rows, dy_rows, normed_rows, gains = prepare(
        tokens[0], cotangent[0], jnp.stack([norm_attn, norm_ffn]).astype(F32)
    )
    normed_rows, w_query = keep((normed_rows, w_query))
    ahead, behind = near_pieces(normed_rows)
    qkv_own = gather_axis(jnp.concatenate([w_query, key_projection, value_projection], 1), "x")
    qkv_own = gather_axis(jnp.concatenate(qkv_own, 0), "y")
    far = far_pieces(ahead, behind)
    qkv_own, far = keep((qkv_own, far))
    qkv_own = jnp.concatenate(qkv_own, 0)
    qkv_pieces = qkv_own, shift(qkv_own, "core", 1)
    normed_one = jnp.concatenate([normed_rows, ahead, *far, behind], 0)
    dy_raw, far = keep((cotangent[0], far))
    dy_pieces = gather_pieces(dy_raw)

    row = jnp.arange(512, dtype=jnp.int32)
    positions = block * 512 + ((row // 128 + place) % 4) * 128 + row % 128
    frequency = 10000.0 ** (-jnp.arange(32, dtype=F32) * 2.0 / HEAD_SIZE)
    angles = positions.astype(F32)[:, None] * frequency[None, :]
    cosine, sine = jnp.cos(angles), jnp.sin(angles)
    cosine = jnp.concatenate([cosine] * 4, 1)
    sine = jnp.concatenate([-sine, sine, -sine, sine], 1)

    (kv_own,) = project(
        project_kv_kernel, code, normed_one, qkv_pieces, cosine, sine, 128, 128, False
    )
    normed_late, kv_own = keep((normed_one, kv_own))
    kv = (from_block(kv_own, 2), from_block(kv_own, 1), kv_own)
    queries, qkv_weights = project(
        project_q_kernel, code, normed_late, qkv_pieces, cosine, sine, 512, 640, True
    )

    flat = segments.reshape(-1)
    padded = jnp.concatenate([jnp.full((1024,), -1, jnp.int32), flat])
    own = lax.dynamic_slice_in_dim(flat, block * 512, 512, 0)
    window = lax.dynamic_slice_in_dim(padded, block * 512, 1536, 0)
    start = jnp.sum((window[None, :] < own[:, None]).astype(jnp.int32), 1)
    low = jnp.maximum(start, row + 1).reshape(1, 512)

    kk, vv, kvt = set_up(code, kv)
    seen = code, queries, kk, kvt, low, out_weights
    o_far, lse_far, part_far = attend(2, 1, 1, *seen)
    queries, part_far, dy_pieces = keep((queries, part_far, dy_pieces))
    part_far = shift(part_far, "head", 2)
    seen = code, queries, kk, kvt, low, out_weights
    o_near, lse_near, part_ahead, part_behind = attend(1, 2, 2, *seen)
    queries, part_far, part_ahead, part_behind = keep((queries, part_far, part_ahead, part_behind))
    seen = code, queries, kk, kvt, low, out_weights
    o_own, lse_own, part_own = attend(0, 1, 1, *seen)
    dy, dy_swap = assemble(code, dy_rows, *dy_pieces)
    dy_other = shift(dy_swap, "core", 1)
    attention_sum = part_own, shift(part_ahead, "head", 1), shift(part_behind, "head", -1), part_far
    h1, top, bottom = join(x_rows, gains, attention_sum)
    behind_top, ahead_bottom = shift(top, "head", 1), shift(bottom, "head", -1)
    ahead_top, behind_bottom = shift(top, "head", -1), shift(bottom, "head", 1)
    behind_top, ahead_bottom, dy = keep((behind_top, ahead_bottom, dy))
    far_top, far_bottom = shift(behind_top, "head", 1), shift(ahead_bottom, "head", -1)
    rows_two = top, bottom, ahead_top, ahead_bottom, far_top, far_bottom, behind_top, behind_bottom
    dact = columns_times(dy, out_weights)
    dact, dy_other = keep((dact, dy_other))

    gua, normed_two, normed_two_swap, dnormed_two = ffn(
        code, rows_two, dact, ffn_weights
    )
    dnormed_two = scatter_pieces(*dnormed_two)
    gua_other = shift(gua, "core", 1)
    normed_two_other = shift(normed_two_swap, "core", 1)
    out_pieces = rows_times(gua, 2, out_weights, 0)
    gua_other, normed_two_other, out_pieces = keep((gua_other, normed_two_other, out_pieces))
    held = weight_grads(code, normed_two, normed_two_other, dy, dy_other, gua, gua_other)
    held, dnormed_two = keep((held, dnormed_two))
    grads = lax.psum_scatter(held, ("y", "x"), scatter_dimension=0, tiled=True)

    dh1, dh1_low, grad_gain_two = join_back(h1, dy_rows, gains, dnormed_two)
    back = kk, vv, kvt, low, cosine, sine
    dq_own, dk, dv = attend_back(0, 1, 1, code, queries, o_own, (dh1_low,), out_weights, lse_own, *back, ())
    ahead, behind = shift(dh1_low, "head", -1), shift(dh1_low, "head", 1)
    ahead, behind, dk, dv, dh1_late, out_pieces = keep((ahead, behind, dk, dv, dh1_low, out_pieces))
    far = shift(dh1_late, "head", 2)
    dq_near, dk, dv = attend_back(
        1, 2, 2, code, queries, o_near, (ahead, behind), out_weights, lse_near, *back, (dk, dv)
    )
    far, dk, dv, out_pieces = keep((far, dk, dv, out_pieces))
    out_pieces = scatter_pieces(*out_pieces)
    dq_far, dkv_first, dkv_second, dkv_own = attend_back(
        2, 1, 1, code, queries, o_far, (far,), out_weights, lse_far, *back, (dk, dv)
    )
    dq = dq_own, dq_near, dq_far
    dkv_one = from_block(dkv_second, -1)
    dkv_two = from_block(dkv_first, -2)
    wide_other, wide_own = wide_grads(
        code, normed_one, (dh1_low, ahead, far, behind), (o_own, o_near, o_far), dq
    )
    dkv_one, dkv_two, wide_other, out_pieces = keep((dkv_one, dkv_two, wide_other, out_pieces))
    wide_other = shift(wide_other, "core", 1)

    narrow_other, narrow_own, dnormed_one, gain_grads = finish(
        code,
        normed_one,
        qkv_weights,
        dq,
        dkv_own,
        dkv_one,
        dkv_two,
        cosine,
        sine,
        gains,
        grad_gain_two,
    )
    dnormed_one = lax.psum_scatter(dnormed_one, "head", scatter_dimension=0, tiled=True)
    gain_grads = jnp.concatenate([gain_grads, shift(gain_grads, "core", 1)], 0)
    gain_grads = exchange([gain_grads] * 4, "head")
    rows = [(x_rows.shape, BF16)]
    (output,) = small_call(output_kernel, rows, h1, *out_pieces)
    gain_grads, output = keep((gain_grads, output))
    pieces, out_sums = first_pieces(
        code, wide_own, wide_other, narrow_own, shift(narrow_other, "core", 1), gain_grads
    )
    grads = (
        grads[:, :HIDDEN].astype(F32),
        grads[:, HIDDEN : 2 * HIDDEN].astype(F32),
        grads[:, 2 * HIDDEN :].T.astype(F32),
    )
    pieces, out_sums, grads = keep((exchange(pieces, "x"), exchange(out_sums, "y"), grads))
    pieces, out_sums = second_pieces(code, pieces, out_sums)
    (grad_inputs,) = small_call(input_grad_kernel, rows, dh1, x_rows, gains, dnormed_one)
    pieces, out_sums, grad_inputs = keep((exchange(pieces, "y"), exchange(out_sums, "x"), grad_inputs))
    columns = (64, 512), (64, 512), (64, 64), (64, 64), (1, 2048), (1, 2048)
    grad_out, grad_query, grad_key, grad_value, grad_gain_one, grad_gain_two = small_call(
        attention_grads_kernel,
        [(shape, F32) for shape in columns],
        *pieces,
        *out_sums,
    )

    return (
        output[None],
        grad_inputs[None],
        grad_query,
        grad_key,
        grad_value,
        grad_out.T,
        *grads,
        grad_gain_one.reshape(2048),
        grad_gain_two.reshape(2048),
    )


def solution(mesh):
    grid = Mesh(mesh.devices.reshape(4, 4, 4, 2), ("head", "y", "x", "core"))
    rows, up, down = P(BLK, "head", None), P(BLK, "head"), P("head", BLK)
    return jax.shard_map(
        per_device,
        mesh=grid,
        in_specs=(rows, P(), up, up, up, down, up, up, down, P(), P(), rows),
        out_specs=(rows, rows, up, up, up, down, up, up, down, P(), P()),
        check_vma=False,
    )
```

```python
import functools

import jax
import jax.numpy as jnp
from jax import lax
from jax.experimental import pallas as pl
from jax.experimental.pallas import tpu as pltpu
from jax.sharding import Mesh
from jax.sharding import PartitionSpec as P

HEAD_SIZE = 64
WINDOW = 1024
HIDDEN = 1408
EPSILON = 1e-05
BF16 = jnp.bfloat16
F32 = jnp.float32
BLK = ("y", "x", "core")
CORE_FIRST = ("core", "y", "x")
VMEM_LIMIT = 63 * 1024 * 1024


def dot_nn(a, b):
    return jnp.dot(a, b, preferred_element_type=F32)


def dot_nt(a, b):
    return lax.dot_general(a, b, (((1,), (1,)), ((), ())), preferred_element_type=F32)


def dot_tn(a, b):
    return lax.dot_general(a, b, (((0,), (0,)), ((), ())), preferred_element_type=F32)


def shift(value, axis, distance):
    size = lax.axis_size(axis)
    return lax.ppermute(value, axis, [(i, (i + distance) % size) for i in range(size)])


def add_low(a, b):
    return (a.astype(F32) + b.astype(F32)).astype(BF16)


def gather_pieces(rows):
    return shift(rows, "head", -1), shift(rows, "head", 2), shift(rows, "head", 1)


def near_pieces(rows):
    return shift(rows, "head", -1), shift(rows, "head", 1)


def far_pieces(ahead, behind):
    half = ahead.shape[0] // 2
    return shift(behind[:half], "head", 1), shift(ahead[half:], "head", -1)


def scatter_pieces(own, ahead, far, behind):
    return own, shift(ahead, "head", 1), shift(behind, "head", -1), shift(far, "head", 2)


def gather_axis(value, axis):
    return value, shift(value, axis, -1), shift(value, axis, 2), shift(value, axis, 1)


def exchange(pieces, axis):
    return pieces[0], shift(pieces[1], axis, 1), shift(pieces[2], axis, 2), shift(pieces[3], axis, -1)


def from_block(value, distance):
    route = [(i, i + distance) for i in range(32) if 0 <= i + distance < 32]
    return lax.ppermute(value, BLK, route)


def scale_of(values):
    return lax.rsqrt(jnp.mean(values * values, -1, keepdims=True) + EPSILON)


def x_of(code):
    return lax.shift_right_logical(code[0], 5)


def y_of(code):
    return lax.shift_right_logical(code[0], 3) & 3


def core_of(code):
    return lax.shift_right_logical(code[0], 2) & 1


def place_of(code):
    return code[0] & 3


def lane_is_low(shape, period):
    return lax.broadcasted_iota(jnp.int32, shape, len(shape) - 1) % period < period // 2


def turn(values, cosine, sine):
    swapped = jnp.where(
        lane_is_low(values.shape, 64), pltpu.roll(values, 96, 1), pltpu.roll(values, 32, 1)
    )
    return values * cosine + swapped * sine


def core_major_tiles(tiles):
    low = lane_is_low(tiles[0].shape, 128)
    rolled = [pltpu.roll(tile, 64, 1) for tile in tiles]
    first = [jnp.where(low, tiles[2 * k], rolled[2 * k + 1]) for k in range(8)]
    second = [jnp.where(low, rolled[2 * k], tiles[2 * k + 1]) for k in range(8)]
    return first + second


def block_major_tiles(tiles):
    low = lane_is_low(tiles[0].shape, 128)
    rolled = [pltpu.roll(tile, 64, 1) for tile in tiles]
    result = []
    for k in range(8):
        result.append(jnp.where(low, tiles[k], rolled[8 + k]))
        result.append(jnp.where(low, rolled[k], tiles[8 + k]))
    return result


def in_tiles(value):
    return [value[:, 128 * k : 128 * k + 128] for k in range(16)]


def prepare_kernel(x_ref, dy_ref, gain_ref, x_out, dy_out, normed_out, gain_out):
    def convert(ref):
        return jnp.concatenate(core_major_tiles(in_tiles(ref[...].astype(F32))), 1)

    x, gains = convert(x_ref), convert(gain_ref)
    gain_out[...] = gains
    x_out[...] = x
    dy_out[...] = convert(dy_ref).astype(BF16)
    normed_out[...] = (x * scale_of(x) * gains[:1]).astype(BF16)


def prepare(x, dy, gains):
    rows, width = x.shape
    return pl.pallas_call(
        prepare_kernel,
        out_shape=(
            jax.ShapeDtypeStruct((rows, width), F32),
            jax.ShapeDtypeStruct((rows, width), BF16),
            jax.ShapeDtypeStruct((rows, width), BF16),
            jax.ShapeDtypeStruct(gains.shape, F32),
        ),
        compiler_params=pltpu.CompilerParams(vmem_limit_bytes=VMEM_LIMIT),
        cost_estimate=pl.CostEstimate(
            flops=10 * rows * width, bytes_accessed=10 * rows * width, transcendentals=rows
        ),
    )(x, dy, gains)


def to_blocks(value):
    return jnp.concatenate(block_major_tiles(in_tiles(value)), 1)


def assemble_kernel(core_ref, own_ref, ahead_ref, far_ref, behind_ref, out_ref, swap_ref):
    out_ref[:128] = own_ref[...]
    start = 128
    for ref in (ahead_ref, far_ref, behind_ref):
        size = ref.shape[0]
        out_ref[start : start + size] = jnp.concatenate(
            core_major_tiles(in_tiles(ref[...].astype(F32))), 1
        ).astype(BF16)
        start += size
    swap_ref[...] = jnp.where(core_of(core_ref) == 0, out_ref[:, 1024:], out_ref[:, :1024])


def assemble(core, own, ahead, far, behind):
    vmem = pl.BlockSpec(memory_space=pltpu.VMEM)
    return pl.pallas_call(
        assemble_kernel,
        out_shape=(jax.ShapeDtypeStruct((512, 2048), BF16), jax.ShapeDtypeStruct((512, 1024), BF16)),
        in_specs=[pl.BlockSpec(memory_space=pltpu.SMEM)] + [vmem] * 4,
        out_specs=(vmem, vmem),
        compiler_params=pltpu.CompilerParams(vmem_limit_bytes=VMEM_LIMIT),
        cost_estimate=pl.CostEstimate(
            flops=4 * 512 * 2048, bytes_accessed=5 * 1024 * 1024, transcendentals=0
        ),
    )(core, own, ahead, far, behind)


def small_call(kernel, out_shape, *operands):
    return pl.pallas_call(
        kernel,
        out_shape=tuple(jax.ShapeDtypeStruct(shape, dtype) for shape, dtype in out_shape),
        compiler_params=pltpu.CompilerParams(vmem_limit_bytes=VMEM_LIMIT),
        cost_estimate=pl.CostEstimate(
            flops=sum(x.size for x in operands),
            bytes_accessed=2 * sum(x.size * x.dtype.itemsize for x in operands),
            transcendentals=0,
        ),
    )(*operands)


def total_of(refs):
    values = [ref[...].astype(F32) for ref in refs]
    while len(values) > 1:
        values = [values[0] + values[1]] + values[2:]
    return values[0]


def join_kernel(x_ref, gain_ref, a_ref, b_ref, c_ref, d_ref, h_out, top_out, bottom_out):
    h = x_ref[...] + total_of((a_ref, b_ref, c_ref, d_ref))
    h_out[...] = h
    normed = (h * scale_of(h) * gain_ref[1:2]).astype(BF16)
    half = h.shape[0] // 2
    top_out[...], bottom_out[...] = normed[:half], normed[half:]


def join(x, gain, pieces):
    half = x.shape[0] // 2, x.shape[1]
    return small_call(join_kernel, ((x.shape, F32), (half, BF16), (half, BF16)), x, gain, *pieces)


def norm_backward(values, gain, grad):
    scale = scale_of(values)
    weighted = grad * gain
    inner = jnp.mean(weighted * values, -1, keepdims=True)
    return scale * weighted - values * (scale * scale * scale * inner), scale


def join_back_kernel(h_ref, dy_ref, gain_ref, a_ref, b_ref, c_ref, d_ref, dh_out, low_out, grad_out):
    h, grad = h_ref[...], total_of((a_ref, b_ref, c_ref, d_ref))
    back, scale = norm_backward(h, gain_ref[1:2], grad)
    dh = dy_ref[...].astype(F32) + back
    dh_out[...] = dh
    low_out[...] = dh.astype(BF16)
    grad_out[...] = to_blocks(jnp.broadcast_to(jnp.sum(grad * h * scale, 0, keepdims=True), (8, h.shape[1])))


def join_back(h, dy, gain, pieces):
    shapes = (h.shape, F32), (h.shape, BF16), ((8, h.shape[1]), F32)
    return small_call(join_back_kernel, shapes, h, dy, gain, *pieces)


def output_kernel(h_ref, a_ref, b_ref, c_ref, d_ref, out_ref):
    out_ref[...] = to_blocks(h_ref[...] + total_of((a_ref, b_ref, c_ref, d_ref))).astype(BF16)


def input_grad_kernel(dh_ref, x_ref, gain_ref, grad_ref, out_ref):
    back, _ = norm_backward(x_ref[...], gain_ref[:1], grad_ref[...].astype(F32))
    out_ref[...] = to_blocks(dh_ref[...] + back).astype(BF16)


GAIN_ROWS, GAIN_COLUMNS = 16, 256


def gain_rows(vector):
    return jnp.concatenate([vector[:, 256 * k : 256 * k + 256] for k in range(8)], 0)


def put_piece(ref, rows, gains):
    count = rows.shape[0]
    ref[:count] = rows
    ref[count:, GAIN_COLUMNS:] = jnp.zeros((GAIN_ROWS, ref.shape[1] - GAIN_COLUMNS), BF16)
    ref[count:, :GAIN_COLUMNS] = gains.astype(BF16)


def first_pieces_kernel(
    at_ref, q_ref, q2_ref, kv_ref, kv2_ref, o_ref, o2_ref, *refs
):
    gain_refs, out_refs = refs[:4], refs[4:]
    query = add_low(q_ref[...], q2_ref[...]).reshape(256, 512)
    narrow = add_low(kv_ref[...], kv2_ref[...]).reshape(256, 128)
    rows = jnp.concatenate([query, narrow], 1)
    out_rows = add_low(o_ref[...], o2_ref[...]).reshape(256, 512)
    gains = total_of(gain_refs)
    gains = gains[:GAIN_ROWS] + gains[GAIN_ROWS:]
    for number in range(4):

        @pl.when(pl.program_id(0) == number)
        def _():
            put_piece(out_refs[number], rows, gains)
            out_refs[4 + number][...] = out_rows


def first_pieces(at, wide, wide2, narrow, narrow2, gains):
    pick_x = lambda column: lambda d, s: (0, lax.rem(x_of(s) + d, 4), 0, column)
    pick_y = lambda d, s: (lax.rem(y_of(s) + d, 4), 0, 0, 0)
    whole = lambda d, s: (0, 0)
    shaped = lambda value: value.reshape(4, 4, 64, value.shape[1])
    shapes = [(256 + GAIN_ROWS, 640)] * 4 + [(256, 512)] * 4
    grid = pltpu.PrefetchScalarGridSpec(
        num_scalar_prefetch=1,
        grid=(4,),
        in_specs=[pl.BlockSpec((4, 1, 64, 512), pick_x(1))] * 2
        + [pl.BlockSpec((4, 1, 64, 128), pick_x(0))] * 2
        + [pl.BlockSpec((1, 4, 64, 512), pick_y)] * 2
        + [pl.BlockSpec((2 * GAIN_ROWS, GAIN_COLUMNS), whole)] * 4,
        out_specs=tuple(pl.BlockSpec(shape, whole) for shape in shapes),
    )
    wide, wide2 = shaped(wide), shaped(wide2)
    result = pl.pallas_call(
        first_pieces_kernel,
        grid_spec=grid,
        out_shape=tuple(jax.ShapeDtypeStruct(shape, BF16) for shape in shapes),
        compiler_params=pltpu.CompilerParams(vmem_limit_bytes=VMEM_LIMIT),
        cost_estimate=pl.CostEstimate(
            flops=2 * 1024 * 1152, bytes_accessed=6 * 1024 * 1152, transcendentals=0
        ),
    )(at, wide, wide2, shaped(narrow), shaped(narrow2), wide, wide2, *gains)
    return result[:4], result[4:]


def second_pieces_kernel(at_ref, *refs):
    qkv, out, (held, out_held) = refs[:4], refs[4:8], refs[16:]
    held[...] = total_of(qkv)
    out_held[...] = total_of(out).astype(BF16)
    for number in range(4):
        y = pl.multiple_of(lax.rem(y_of(at_ref) + number, 4) * 64, 64)
        put_piece(refs[8 + number], held[pl.ds(y, 64), :].astype(BF16), held[256:, :GAIN_COLUMNS])
        x = pl.multiple_of(lax.rem(x_of(at_ref) + number, 4) * 64, 64)
        refs[12 + number][...] = out_held[pl.ds(x, 64), :]


def second_pieces(at, qkv, out):
    vmem = pl.BlockSpec(memory_space=pltpu.VMEM)
    shapes = [(64 + GAIN_ROWS, 640)] * 4 + [(64, 512)] * 4
    result = pl.pallas_call(
        second_pieces_kernel,
        out_shape=tuple(jax.ShapeDtypeStruct(shape, BF16) for shape in shapes),
        in_specs=[pl.BlockSpec(memory_space=pltpu.SMEM)] + [vmem] * 8,
        out_specs=(vmem,) * 8,
        scratch_shapes=[pltpu.VMEM((256 + GAIN_ROWS, 640), F32), pltpu.VMEM((256, 512), BF16)],
        compiler_params=pltpu.CompilerParams(vmem_limit_bytes=VMEM_LIMIT),
        cost_estimate=pl.CostEstimate(
            flops=4 * 272 * 1152, bytes_accessed=10 * 272 * 1152, transcendentals=0
        ),
    )(at, *qkv, *out)
    return result[:4], result[4:]


def attention_grads_kernel(*refs):
    out_ref, q_ref, k_ref, v_ref, one_ref, two_ref = refs[8:]
    total = total_of(refs[:4])
    out_ref[...] = total_of(refs[4:8])
    q_ref[...] = total[:64, :512]
    k_ref[...] = total[:64, 512:576]
    v_ref[...] = total[:64, 576:]
    gains = total[64:, :GAIN_COLUMNS]
    one_ref[...] = jnp.concatenate([gains[k : k + 1] for k in range(8)], 1)
    two_ref[...] = jnp.concatenate([gains[k : k + 1] for k in range(8, 16)], 1)


def put_in_order(at_ref, piece_refs, columns, to_ref, sems):
    x, y, core = x_of(at_ref), y_of(at_ref), core_of(at_ref)
    copies = []
    for number in range(32):
        to_x, to_y = lax.rem(x + number % 4, 4), lax.rem(y + number // 4 % 4, 4)
        to_core = core if number < 16 else 1 - core
        row = pl.multiple_of(((to_core * 4 + to_y) * 4 + to_x) * 64, 64)
        copy = pltpu.make_async_copy(
            piece_refs[number // 4].at[pl.ds(number % 4 * 64, 64), columns],
            to_ref.at[pl.ds(row, 64)],
            sems.at[number],
        )
        copy.start()
        copies.append(copy)
    return copies


RING_PIECES = [(0, 128), (128, 128), (256, 64), (320, 64), (384, 128)]


def project_kv_kernel(at_ref, *refs):
    x_refs, piece_refs, (cos_ref, sin_ref, kv_ref, whole_ref) = refs[:5], refs[5:13], refs[13:17]
    x_held, held, sems, x_sems = refs[17:]
    copies = []
    for number, (start, size) in enumerate(RING_PIECES):
        copy = pltpu.make_async_copy(x_refs[number], x_held.at[pl.ds(start, size)], x_sems.at[number])
        copy.start()
        copies.append(copy)
    copies += put_in_order(at_ref, piece_refs, pl.ds(512, 128), held, sems)
    for copy in copies:
        copy.wait()
    whole = pltpu.make_async_copy(x_held, whole_ref, x_sems.at[len(RING_PIECES)])
    whole.start()
    flat = dot_nn(x_held[...], held[...])
    turned = turn(flat, cos_ref[...], sin_ref[...])
    kv_ref[...] = jnp.where(lane_is_low(flat.shape, 128), turned, flat).astype(BF16)
    whole.wait()


def project_kv(at, x_pieces, weights, cosine, sine):
    rows, width = 512, x_pieces[0].shape[1]
    vmem, anywhere = pl.BlockSpec(memory_space=pltpu.VMEM), pl.BlockSpec(memory_space=pl.ANY)
    return pl.pallas_call(
        project_kv_kernel,
        out_shape=(jax.ShapeDtypeStruct((rows, 128), BF16), jax.ShapeDtypeStruct((rows, width), BF16)),
        in_specs=[pl.BlockSpec(memory_space=pltpu.SMEM)] + [anywhere] * 13 + [vmem, vmem],
        out_specs=(vmem, anywhere),
        scratch_shapes=[
            pltpu.VMEM((rows, width), BF16),
            pltpu.VMEM((width, 128), BF16),
            pltpu.SemaphoreType.DMA((32,)),
            pltpu.SemaphoreType.DMA((len(RING_PIECES) + 1,)),
        ],
        compiler_params=pltpu.CompilerParams(vmem_limit_bytes=VMEM_LIMIT),
        cost_estimate=pl.CostEstimate(
            flops=2 * rows * width * 128, bytes_accessed=5 * 1024 * 1024, transcendentals=0
        ),
    )(at, *x_pieces, *weights, cosine, sine)


def project_q_kernel(at_ref, x_ref, *refs):
    piece_refs, (cos_ref, sin_ref, q_ref, w_ref, held, sems, sem) = refs[:8], refs[8:]
    for copy in put_in_order(at_ref, piece_refs, pl.ds(0, 640), held, sems):
        copy.wait()
    whole = pltpu.make_async_copy(held, w_ref, sem)
    whole.start()
    cosine, sine, x = cos_ref[...], sin_ref[...], x_ref[...]
    for start in (0, 256):
        wide = dot_nn(x, held[:, start : start + 256])
        for part in (0, 128):
            turned = turn(wide[:, part : part + 128], cosine, sine)
            q_ref[:, start + part : start + part + 128] = (turned * HEAD_SIZE**-0.5).astype(BF16)
    whole.wait()


def project_q(at, normed, weights, cosine, sine):
    rows, width = normed.shape
    vmem, anywhere = pl.BlockSpec(memory_space=pltpu.VMEM), pl.BlockSpec(memory_space=pl.ANY)
    return pl.pallas_call(
        project_q_kernel,
        out_shape=(jax.ShapeDtypeStruct((rows, 512), BF16), jax.ShapeDtypeStruct((width, 640), BF16)),
        in_specs=[pl.BlockSpec(memory_space=pltpu.SMEM), vmem] + [anywhere] * 8 + [vmem, vmem],
        out_specs=(vmem, anywhere),
        scratch_shapes=[
            pltpu.VMEM((width, 640), BF16),
            pltpu.SemaphoreType.DMA((32,)),
            pltpu.SemaphoreType.DMA,
        ],
        compiler_params=pltpu.CompilerParams(vmem_limit_bytes=VMEM_LIMIT),
        cost_estimate=pl.CostEstimate(
            flops=2 * rows * width * 512, bytes_accessed=7 * 1024 * 1024, transcendentals=0
        ),
    )(at, normed, *weights, cosine, sine)


KEYS = 1152
PAIRS = 4


def set_up_kernel(place_ref, kv0_ref, kv1_ref, kv2_ref, kk_ref, vv_ref, kvt_ref):
    place = place_of(place_ref)
    low = lane_is_low((128, 128), 128)
    for block, ref in enumerate((kv0_ref, kv1_ref, kv2_ref)):
        for group in range(4):
            at = pl.multiple_of(lax.rem(group - place + 4, 4) * 128, 128)
            piece = ref[pl.ds(at, 128), :].astype(F32)
            rolled = pltpu.roll(piece, 64, 1)
            to = block * 512 + group * 128
            kk_ref[to : to + 128, :] = jnp.where(low, piece, rolled).astype(BF16)
            vv_ref[to : to + 128, :] = jnp.where(low, rolled, piece).astype(BF16)
            kvt_ref[:, to : to + 128] = piece.T.astype(BF16)


def set_up(place, kv):
    vmem = pl.BlockSpec(memory_space=pltpu.VMEM)
    return pl.pallas_call(
        set_up_kernel,
        out_shape=(
            jax.ShapeDtypeStruct((1536, 128), BF16),
            jax.ShapeDtypeStruct((1536, 128), BF16),
            jax.ShapeDtypeStruct((128, 1536), BF16),
        ),
        in_specs=[pl.BlockSpec(memory_space=pltpu.SMEM), vmem, vmem, vmem],
        out_specs=(vmem, vmem, vmem),
        compiler_params=pltpu.CompilerParams(vmem_limit_bytes=VMEM_LIMIT),
        cost_estimate=pl.CostEstimate(flops=1536 * 128 * 8, bytes_accessed=2 * 1024 * 1024, transcendentals=0),
    )(place, *kv)


def both_heads(pair):
    low = lane_is_low(pair.shape, 128)
    nothing = jnp.zeros_like(pair)
    return jnp.concatenate([jnp.where(low, pair, nothing), jnp.where(low, nothing, pair)], 0)


def side_by_side(transposed):
    return jnp.concatenate([transposed[:, :128], transposed[:, 128:]], 0).T


def mask_of(at, low_ref):
    key = lax.broadcasted_iota(jnp.int32, (KEYS, 128), 0)
    query = lax.broadcasted_iota(jnp.int32, (KEYS, 128), 1)
    seen = (key >= low_ref[:, pl.ds(at, 128)] - at) & (key <= query + WINDOW)
    bias = jnp.where(seen, 0.0, -jnp.inf)
    return jnp.concatenate([bias, bias], 1)


def attend_kernel(
    first, step, place_ref, q_ref, kk_ref, kvt_ref, low_ref, w_ref, o_ref, lse_ref, *refs
):
    part_refs, (bias, held, w_held, sem) = refs[:-4], refs[-4:]
    group = lax.rem(place_of(place_ref) + first + step * pl.program_id(0), 4)
    at = pl.multiple_of(group * 128, 128)

    load = pltpu.make_async_copy(w_ref.at[:, pl.ds(HIDDEN, 512)], w_held, sem)

    @pl.when((pl.program_id(0) == 0) & (pl.program_id(1) == 0))
    def _():
        load.start()

    @pl.when(pl.program_id(1) == 0)
    def _():
        bias[...] = mask_of(at, low_ref)

    keys = pl.ds(at, KEYS)
    for number in range(PAIRS):
        columns = slice(128 * number, 128 * number + 128)
        scores = dot_nt(kk_ref[keys, :], both_heads(q_ref[:, columns])) + bias[...]
        top = jnp.max(scores, 0, keepdims=True)
        weights = jnp.exp(scores - top)
        total = jnp.sum(weights, 0, keepdims=True)
        result = dot_nn(kvt_ref[64:128, keys], weights.astype(BF16)) / total
        lse_ref[0, number] = top + jnp.log(total)
        result = side_by_side(result).astype(BF16)
        o_ref[:, columns] = result
        held[PAIRS * pl.program_id(1) + number] = result

    @pl.when(pl.program_id(1) == 4 // PAIRS - 1)
    def _():
        @pl.when(pl.program_id(0) == 0)
        def _():
            load.wait()

        rows = jnp.concatenate([held[k] for k in range(4)], 1)
        part = dot_nt(rows, w_held[...]).astype(BF16)
        for number, ref in enumerate(part_refs):

            @pl.when(pl.program_id(0) == number)
            def _():
                ref[...] = part


def attend(first, step, count, place, queries, kk, kvt, low, weights):
    whole = lambda g, p, s: (0, 0)
    width = 128 * PAIRS
    grid = pltpu.PrefetchScalarGridSpec(
        num_scalar_prefetch=1,
        grid=(count, 4 // PAIRS),
        in_specs=[
            pl.BlockSpec((128, width), lambda g, p, s: (first + step * g, p)),
            pl.BlockSpec((1536, 128), whole),
            pl.BlockSpec((128, 1536), whole),
            pl.BlockSpec((1, 512), whole),
            pl.BlockSpec(memory_space=pl.ANY),
        ],
        out_specs=(
            pl.BlockSpec((128, width), lambda g, p, s: (g, p)),
            pl.BlockSpec((1, PAIRS, 1, 256), lambda g, p, s: (g, p, 0, 0)),
        )
        + (pl.BlockSpec((128, 2048), whole),) * count,
        scratch_shapes=[
            pltpu.VMEM((KEYS, 256), F32),
            pltpu.VMEM((4, 128, 128), BF16),
            pltpu.VMEM((2048, 512), BF16),
            pltpu.SemaphoreType.DMA,
        ],
    )
    return pl.pallas_call(
        functools.partial(attend_kernel, first, step),
        grid_spec=grid,
        out_shape=(
            jax.ShapeDtypeStruct((128 * count, 512), BF16),
            jax.ShapeDtypeStruct((count, 4, 1, 256), F32),
        )
        + (jax.ShapeDtypeStruct((128, 2048), BF16),) * count,
        compiler_params=pltpu.CompilerParams(vmem_limit_bytes=VMEM_LIMIT),
        cost_estimate=pl.CostEstimate(
            flops=count * 4 * KEYS * 256 * 256 * 2,
            bytes_accessed=3 * 1024 * 1024,
            transcendentals=count * 4 * KEYS * 256,
        ),
    )(place, queries, kk, kvt, low, weights)


def attend_back_kernel(first, step, count, *refs):
    last = first == 2
    place_ref, q_ref, w_ref, lse_ref, kk_ref, vv_ref, kvt_ref, low_ref, cos_ref, sin_ref = refs[:10]
    o_ref = refs[10]
    dh_refs, refs = refs[11 : 11 + count], refs[11 + count :]
    dk_in = dv_in = None
    if first > 0:
        dk_in, dv_in, refs = refs[0], refs[1], refs[2:]
    bias, do_held, dk, dv, w_held, sem = refs[-6:]
    dq_ref, outs = refs[0], refs[1:-6]
    number, pair = pl.program_id(0), pl.program_id(1)
    place = place_of(place_ref)
    at = pl.multiple_of(lax.rem(place + first + step * number, 4) * 128, 128)

    load = pltpu.make_async_copy(w_ref.at[:, pl.ds(HIDDEN, 512)], w_held, sem)

    @pl.when((number == 0) & (pair == 0))
    def _():
        load.start()
        dk[...] = jnp.zeros_like(dk) if dk_in is None else dk_in[...]
        dv[...] = jnp.zeros_like(dv) if dv_in is None else dv_in[...]

    @pl.when(pair == 0)
    def _():
        bias[...] = mask_of(at, low_ref)

        @pl.when(number == 0)
        def _():
            load.wait()

        for k, ref in enumerate(dh_refs):

            @pl.when(number == k)
            def _():
                do_rows = dot_nn(ref[...], w_held[...]).astype(BF16)
                for p in range(4):
                    do_held[p] = do_rows[:, 128 * p : 128 * p + 128]

    keys = pl.ds(at, KEYS)
    queries, grads, all_weights, all_grad_scores = [], [], [], []
    for k in range(PAIRS):
        columns = slice(128 * k, 128 * k + 128)
        do_pair = do_held[PAIRS * pair + k]
        query, grad = both_heads(q_ref[:, columns]), both_heads(do_pair)
        scores = dot_nt(kk_ref[keys, :], query) + bias[...]
        weights = jnp.exp(scores - lse_ref[0, k])
        grad_weights = dot_nt(vv_ref[keys, :], grad)
        product = (o_ref[:, columns].astype(F32) * do_pair.astype(F32)).T
        inner = jnp.concatenate(
            [jnp.sum(product[:64], 0, keepdims=True), jnp.sum(product[64:], 0, keepdims=True)], 1
        )
        grad_scores = (weights * (grad_weights - inner)).astype(BF16)
        grad_query = side_by_side(dot_nn(kvt_ref[0:64, keys], grad_scores)) * HEAD_SIZE**-0.5
        dq_ref[:, columns] = turn(grad_query, cos_ref[...], -sin_ref[...]).astype(BF16)
        queries.append(query)
        grads.append(grad)
        all_weights.append(weights.astype(BF16))
        all_grad_scores.append(grad_scores)
    join = lambda values, axis: values[0] if PAIRS == 1 else jnp.concatenate(values, axis)
    dv[keys, :] += dot_nn(join(all_weights, 1), join(grads, 0))
    dk[keys, :] += dot_nn(join(all_grad_scores, 1), join(queries, 0))

    @pl.when((number == pl.num_programs(0) - 1) & (pair == 4 // PAIRS - 1))
    def _():
        if not last:
            outs[0][...], outs[1][...] = dk[...], dv[...]
            return
        half = lane_is_low((128, 128), 128)
        for block in range(3):
            for group in range(4):
                to = pl.multiple_of(lax.rem(group - place + 4, 4) * 128, 128)
                frm = slice(block * 512 + group * 128, block * 512 + group * 128 + 128)
                key, value = dk[frm, :], dv[frm, :]
                key = key + pltpu.roll(key, 64, 1)
                value = value + pltpu.roll(value, 64, 1)
                both = jnp.where(half, key, value)
                outs[block][pl.ds(to, 128), :] = both.astype(outs[block].dtype)


def attend_back(first, step, count, place, queries, o, dh, weights, lse, kk, vv, kvt, low, cosine, sine, held):
    last = first == 2
    whole = lambda g, p, s: (0, 0)
    specs = [
        pl.BlockSpec((128, 128 * PAIRS), lambda g, p, s: (first + step * g, p)),
        pl.BlockSpec(memory_space=pl.ANY),
        pl.BlockSpec((1, PAIRS, 1, 256), lambda g, p, s: (g, p, 0, 0)),
        pl.BlockSpec((1536, 128), whole),
        pl.BlockSpec((1536, 128), whole),
        pl.BlockSpec((128, 1536), whole),
        pl.BlockSpec((1, 512), whole),
        pl.BlockSpec((128, 128), lambda g, p, s: (first + step * g, 0)),
        pl.BlockSpec((128, 128), lambda g, p, s: (first + step * g, 0)),
    ]
    specs += [pl.BlockSpec((128, 128 * PAIRS), lambda g, p, s: (g, p))]
    specs += [pl.BlockSpec((128, 2048), whole)] * count + [pl.BlockSpec((1536, 128), whole)] * len(held)
    if last:
        out_specs = (pl.BlockSpec((512, 128), whole),) * 3
        out_shape = tuple(jax.ShapeDtypeStruct((512, 128), dtype) for dtype in (BF16, BF16, F32))
    else:
        out_specs = (pl.BlockSpec((1536, 128), whole),) * 2
        out_shape = (jax.ShapeDtypeStruct((1536, 128), F32),) * 2
    grid = pltpu.PrefetchScalarGridSpec(
        num_scalar_prefetch=1,
        grid=(count, 4 // PAIRS),
        in_specs=specs,
        out_specs=(pl.BlockSpec((128, 128 * PAIRS), lambda g, p, s: (g, p)),) + out_specs,
        scratch_shapes=[
            pltpu.VMEM((KEYS, 256), F32),
            pltpu.VMEM((4, 128, 128), BF16),
            pltpu.VMEM((1536, 128), F32),
            pltpu.VMEM((1536, 128), F32),
            pltpu.VMEM((2048, 512), BF16),
            pltpu.SemaphoreType.DMA,
        ],
    )
    return pl.pallas_call(
        functools.partial(attend_back_kernel, first, step, count),
        grid_spec=grid,
        out_shape=(jax.ShapeDtypeStruct((128 * count, 512), BF16),) + out_shape,
        compiler_params=pltpu.CompilerParams(vmem_limit_bytes=VMEM_LIMIT),
        cost_estimate=pl.CostEstimate(
            flops=count * 4 * KEYS * 256 * 640 * 2,
            bytes_accessed=6 * 1024 * 1024,
            transcendentals=count * 4 * KEYS * 256,
        ),
    )(place, queries, weights, lse, kk, vv, kvt, low, cosine, sine, o, *dh, *held)


GROUPS = [(0, 128), (128, 256), (384, 512), (896, 512)]


def columns_times_kernel(left_ref, right_ref, out_ref, left, right, out, sems, out_sems):
    load = pltpu.make_async_copy(left_ref, left, sems.at[len(GROUPS)])
    load.start()
    copies, results = [], []
    for number, (start, width) in enumerate(GROUPS):
        columns = pl.ds(start, width)
        copy = pltpu.make_async_copy(right_ref.at[:, columns], right.at[:, columns], sems.at[number])
        copy.start()
        copies.append(copy)
    load.wait()
    value = left[...]
    for number, (start, width) in enumerate(GROUPS):
        copies[number].wait()
        out[:, start : start + width] = dot_nn(value, right[:, start : start + width])
        columns = pl.ds(start, width)
        copy = pltpu.make_async_copy(out.at[:, columns], out_ref.at[:, columns], out_sems.at[number])
        copy.start()
        results.append(copy)
    for copy in results:
        copy.wait()


def columns_times(left, right):
    rows, width = left.shape
    anywhere = pl.BlockSpec(memory_space=pl.ANY)
    return pl.pallas_call(
        columns_times_kernel,
        out_shape=jax.ShapeDtypeStruct((rows, HIDDEN), F32),
        in_specs=[anywhere, anywhere],
        out_specs=anywhere,
        scratch_shapes=[
            pltpu.VMEM((rows, width), BF16),
            pltpu.VMEM((width, HIDDEN), BF16),
            pltpu.VMEM((rows, HIDDEN), F32),
            pltpu.SemaphoreType.DMA((len(GROUPS) + 1,)),
            pltpu.SemaphoreType.DMA((len(GROUPS),)),
        ],
        compiler_params=pltpu.CompilerParams(vmem_limit_bytes=VMEM_LIMIT),
        cost_estimate=pl.CostEstimate(
            flops=2 * rows * width * HIDDEN, bytes_accessed=11 * 1024 * 1024, transcendentals=0
        ),
    )(left, right)


PIECES = [(0, 128), (128, 128), (256, 128), (384, 128)]


def ffn_kernel(*refs):
    core_ref, x_refs, dact_ref, w_ref = refs[0], refs[1:9], refs[9], refs[10]
    gua_ref, whole_ref, swap_ref, dx_refs = refs[11], refs[12], refs[13], refs[14:18]
    x_held, dact_held, w_held, gua, dx, sems, out_sems = refs[18:]
    x_copies = []
    for number in range(8):
        copy = pltpu.make_async_copy(
            x_refs[number], x_held.at[pl.ds(64 * number, 64)], sems.at[12 + number]
        )
        copy.start()
        x_copies.append(copy)
    copies = []
    for number, (start, width) in enumerate(GROUPS):
        for part in range(3):
            if part < 2:
                columns = pl.ds(part * HIDDEN + start, width)
                copy = pltpu.make_async_copy(
                    w_ref.at[:, columns], w_held.at[:, columns], sems.at[3 * number + part]
                )
            else:
                columns = pl.ds(start, width)
                copy = pltpu.make_async_copy(
                    dact_ref.at[:, columns], dact_held.at[:, columns], sems.at[3 * number + part]
                )
            copy.start()
            copies.append(copy)
    for copy in x_copies:
        copy.wait()
    half = pl.multiple_of((1 - core_of(core_ref)) * 1024, 1024)
    results = [
        pltpu.make_async_copy(x_held, whole_ref, out_sems.at[5]),
        pltpu.make_async_copy(x_held.at[:, pl.ds(half, 1024)], swap_ref, out_sems.at[6]),
    ]
    for copy in results:
        copy.start()
    x = x_held[...]
    for number, (start, width) in enumerate(GROUPS):
        for part in range(3):
            copies[3 * number + part].wait()
        gate = dot_nn(x, w_held[:, start : start + width])
        up = dot_nn(x, w_held[:, HIDDEN + start : HIDDEN + start + width])
        dact = dact_held[:, start : start + width]
        sig = jax.nn.sigmoid(gate)
        silu = gate * sig
        dgate = dact * up * (sig * (1.0 + gate * (1.0 - sig)))
        gua[:, start : start + width] = dgate.astype(BF16)
        gua[:, HIDDEN + start : HIDDEN + start + width] = (dact * silu).astype(BF16)
        gua[:, 2 * HIDDEN + start : 2 * HIDDEN + start + width] = (silu * up).astype(BF16)
    copy = pltpu.make_async_copy(gua, gua_ref, out_sems.at[4])
    copy.start()
    results.append(copy)
    dgu = gua[:, : 2 * HIDDEN]
    for number in range(4):
        columns = slice(512 * number, 512 * number + 512)
        dx[:, columns] = dot_nt(dgu, w_held[columns, : 2 * HIDDEN]).astype(BF16)
    for number, (start, size) in enumerate(PIECES):
        copy = pltpu.make_async_copy(dx.at[pl.ds(start, size)], dx_refs[number], out_sems.at[number])
        copy.start()
        results.append(copy)
    for copy in results:
        copy.wait()


def ffn(core, pieces, dact, weights):
    rows, width = dact.shape[0], weights.shape[0]
    anywhere = pl.BlockSpec(memory_space=pl.ANY)
    result = pl.pallas_call(
        ffn_kernel,
        out_shape=(
            jax.ShapeDtypeStruct((rows, 3 * HIDDEN), BF16),
            jax.ShapeDtypeStruct((rows, width), BF16),
            jax.ShapeDtypeStruct((rows, width // 2), BF16),
            *(jax.ShapeDtypeStruct((size, width), BF16) for _, size in PIECES),
        ),
        in_specs=[pl.BlockSpec(memory_space=pltpu.SMEM)] + [anywhere] * 10,
        out_specs=(anywhere,) * 7,
        scratch_shapes=[
            pltpu.VMEM((rows, width), BF16),
            pltpu.VMEM((rows, HIDDEN), F32),
            pltpu.VMEM((width, 2 * HIDDEN), BF16),
            pltpu.VMEM((rows, 3 * HIDDEN), BF16),
            pltpu.VMEM((rows, width), BF16),
            pltpu.SemaphoreType.DMA((20,)),
            pltpu.SemaphoreType.DMA((7,)),
        ],
        compiler_params=pltpu.CompilerParams(vmem_limit_bytes=VMEM_LIMIT),
        cost_estimate=pl.CostEstimate(
            flops=8 * rows * width * HIDDEN,
            bytes_accessed=25 * 1024 * 1024,
            transcendentals=rows * HIDDEN,
        ),
    )(core, *pieces, dact, weights)
    return result[0], result[1], result[2], result[3:]


def weight_grads_kernel(core_ref, x_ref, x2_ref, dy_ref, dy2_ref, right_ref, right2_ref, out_ref):
    part = pl.program_id(0)

    @pl.when(part < 2)
    def _():
        total = dot_tn(x_ref[...], right_ref[...]) + dot_tn(x2_ref[...], right2_ref[...])
        out_ref[...] = total.astype(BF16)

    @pl.when(part == 2)
    def _():
        total = dot_tn(dy_ref[...], right_ref[...]) + dot_tn(dy2_ref[...], right2_ref[...])
        out_ref[...] = total.astype(BF16)


def weight_grads(core, x, x2, dy, dy2, right, right2):
    rows = x.shape[0]
    tile = 1024
    half = x2.shape[1]
    tiles = half // tile
    own = lambda j, i, c: (0, core_of(c) * tiles + i)
    other = lambda j, i, c: (0, i)
    side = lambda j, i, c: (0, j)
    grid = pltpu.PrefetchScalarGridSpec(
        num_scalar_prefetch=1,
        grid=(3, tiles),
        in_specs=[
            pl.BlockSpec((rows, tile), own),
            pl.BlockSpec((rows, tile), other),
            pl.BlockSpec((rows, tile), own),
            pl.BlockSpec((rows, tile), other),
            pl.BlockSpec((rows, HIDDEN), side),
            pl.BlockSpec((rows, HIDDEN), side),
        ],
        out_specs=pl.BlockSpec((tile, HIDDEN), lambda j, i, c: (i, j)),
    )
    return pl.pallas_call(
        weight_grads_kernel,
        grid_spec=grid,
        out_shape=jax.ShapeDtypeStruct((half, 3 * HIDDEN), BF16),
        compiler_params=pltpu.CompilerParams(vmem_limit_bytes=VMEM_LIMIT),
        cost_estimate=pl.CostEstimate(
            flops=2 * 3 * 2 * rows * half * HIDDEN, bytes_accessed=24 * 1024 * 1024, transcendentals=0
        ),
    )(core, x, x2, dy, dy2, right, right2)


def rows_times_kernel(left_ref, right_ref, *out_refs):
    result = dot_nt(left_ref[...], right_ref[...]).astype(BF16)
    for number, ref in enumerate(out_refs):
        ref[...] = result[128 * number : 128 * number + 128]


def rows_times(left, left_part, right, part):
    rows, depth = left.shape[0], HIDDEN
    width = right.shape[0]
    tile = 512
    return pl.pallas_call(
        rows_times_kernel,
        out_shape=(jax.ShapeDtypeStruct((128, width), BF16),) * 4,
        grid=(width // tile,),
        in_specs=[
            pl.BlockSpec((rows, depth), lambda i: (0, left_part)),
            pl.BlockSpec((tile, depth), lambda i: (i, part)),
        ],
        out_specs=(pl.BlockSpec((128, tile), lambda i: (0, i)),) * 4,
        compiler_params=pltpu.CompilerParams(vmem_limit_bytes=VMEM_LIMIT),
        cost_estimate=pl.CostEstimate(
            flops=2 * rows * depth * width,
            bytes_accessed=2 * (rows * depth + width * depth + rows * width),
            transcendentals=0,
        ),
    )(left, right)


def ring_rows(own, near, far):
    return jnp.concatenate([own, near[:128], far, near[128:]], 0)


def put_half(number, value, other_ref, own_ref):
    @pl.when(number < 2)
    def _():
        other_ref[...] = value

    @pl.when(number >= 2)
    def _():
        own_ref[...] = value


def tile_at(i, c):
    return lax.rem(i + 2 * (1 - core_of(c)), 4)


def half_specs(tile, columns):
    return (
        pl.BlockSpec((tile, columns), lambda i, c: (jnp.minimum(i, 1), 0)),
        pl.BlockSpec((tile, columns), lambda i, c: (jnp.maximum(i - 2, 0), 0)),
    )


def wide_grads_kernel(
    core_ref, x_ref, dh0, dh1, dh2, dh3, o0, o1, o2, dq0, dq1, dq2, other_ref, own_ref, o_held, dq_held
):
    number = pl.program_id(0)

    @pl.when(number == 0)
    def _():
        o_held[...] = ring_rows(o0[...], o1[...], o2[...])
        dq_held[...] = ring_rows(dq0[...], dq1[...], dq2[...])

    dh = jnp.concatenate([ref[...] for ref in (dh0, dh1, dh2, dh3)], 0)
    out = dot_tn(dh, o_held[...])
    query = dot_tn(x_ref[...], dq_held[...])
    put_half(number, jnp.concatenate([out, query], 1).astype(BF16), other_ref, own_ref)


def wide_grads(core, normed, dh, o, dq):
    rows, width = normed.shape
    tile = 512
    whole = lambda i, c: (0, 0)
    column = lambda i, c: (0, tile_at(i, c))
    small = [pl.BlockSpec((size, 512), whole) for size in (128, 256, 128)]
    grid = pltpu.PrefetchScalarGridSpec(
        num_scalar_prefetch=1,
        grid=(4,),
        in_specs=[pl.BlockSpec((rows, tile), column)]
        + [pl.BlockSpec((128, tile), column)] * 4
        + small
        + small,
        out_specs=half_specs(tile, 1024),
        scratch_shapes=[pltpu.VMEM((rows, 512), BF16), pltpu.VMEM((rows, 512), BF16)],
    )
    return pl.pallas_call(
        wide_grads_kernel,
        grid_spec=grid,
        out_shape=(jax.ShapeDtypeStruct((width // 2, 1024), BF16),) * 2,
        compiler_params=pltpu.CompilerParams(vmem_limit_bytes=VMEM_LIMIT),
        cost_estimate=pl.CostEstimate(
            flops=2 * rows * width * 1024, bytes_accessed=10 * 1024 * 1024, transcendentals=0
        ),
    )(core, normed, *dh, *o, *dq)


def finish_kernel(
    core_ref,
    x_ref,
    w_ref,
    dq0_ref,
    dq1_ref,
    dq2_ref,
    own_ref,
    one_ref,
    two_ref,
    cos_ref,
    sin_ref,
    norm_ref,
    second_ref,
    other_grad_ref,
    own_grad_ref,
    dx_ref,
    gain_ref,
    dqkv,
    sums,
):
    number = pl.program_id(0)

    @pl.when(number == 0)
    def _():
        dqkv[:, :512] = ring_rows(dq0_ref[...], dq1_ref[...], dq2_ref[...])
        dkv = own_ref[...] + one_ref[...].astype(F32) + two_ref[...].astype(F32)
        turned = turn(dkv, cos_ref[...], -sin_ref[...])
        dqkv[:, 512:] = jnp.where(lane_is_low(dkv.shape, 128), turned, dkv).astype(BF16)

    x = x_ref[...]
    put_half(number, dot_tn(x, dqkv[:, 512:]).astype(BF16), other_grad_ref, own_grad_ref)
    dx = dot_nt(dqkv[...], w_ref[...])
    for piece in range(4):
        row = pl.multiple_of(lax.rem(place_of(core_ref) + piece, 4) * 128, 128)
        dx_ref[pl.ds(row, 128), :] = dx[128 * piece : 128 * piece + 128].astype(BF16)
    columns = pl.ds(pl.multiple_of(tile_at(number, core_ref) * 512, 512), 512)
    sums[:, columns] = jnp.broadcast_to(
        jnp.sum(dx * x.astype(F32), 0, keepdims=True) / norm_ref[:1], (8, 512)
    )

    @pl.when(number == 3)
    def _():
        gain_ref[:8] = gain_rows(to_blocks(sums[...])[:1])
        gain_ref[8:] = gain_rows(second_ref[:1])


def finish(core, normed, weights, dq, own, one, two, cosine, sine, gain, second):
    rows, width = normed.shape
    tile = 512
    whole = lambda i, c: (0, 0)
    column = lambda i, c: (0, tile_at(i, c))
    narrow = pl.BlockSpec((rows, 128), whole)
    grid = pltpu.PrefetchScalarGridSpec(
        num_scalar_prefetch=1,
        grid=(4,),
        in_specs=[
            pl.BlockSpec((rows, tile), column),
            pl.BlockSpec((tile, 640), lambda i, c: (tile_at(i, c), 0)),
            pl.BlockSpec((128, 512), whole),
            pl.BlockSpec((256, 512), whole),
            pl.BlockSpec((128, 512), whole),
            narrow,
            narrow,
            narrow,
            narrow,
            narrow,
            pl.BlockSpec((2, tile), column),
            pl.BlockSpec((8, width), whole),
        ],
        out_specs=half_specs(tile, 128)
        + (pl.BlockSpec((rows, tile), column),)
        + (pl.BlockSpec((GAIN_ROWS, GAIN_COLUMNS), whole),),
        scratch_shapes=[pltpu.VMEM((rows, 640), BF16), pltpu.VMEM((8, width), F32)],
    )
    result = pl.pallas_call(
        finish_kernel,
        grid_spec=grid,
        out_shape=(jax.ShapeDtypeStruct((width // 2, 128), BF16),) * 2
        + (jax.ShapeDtypeStruct((rows, width), BF16),)
        + (jax.ShapeDtypeStruct((GAIN_ROWS, GAIN_COLUMNS), F32),),
        compiler_params=pltpu.CompilerParams(vmem_limit_bytes=VMEM_LIMIT),
        cost_estimate=pl.CostEstimate(
            flops=2 * rows * width * 768, bytes_accessed=10 * 1024 * 1024, transcendentals=0
        ),
    )(core, normed, weights, *dq, own, one, two, cosine, sine, gain, second)
    return result


def per_device(
    tokens,
    segments,
    w_query,
    key_projection,
    value_projection,
    w_out,
    w_gate,
    w_up,
    w_down,
    norm_attn,
    norm_ffn,
    cotangent,
):
    place, core = lax.axis_index("head"), lax.axis_index("core")
    block = (lax.axis_index("y") * 4 + lax.axis_index("x")) * 2 + core
    code = (((lax.axis_index("x") * 4 + lax.axis_index("y")) * 2 + core) * 4 + place).astype(jnp.int32)
    code = code.reshape(1)
    keep = lax.optimization_barrier


    out_weights = lax.all_gather(
        jnp.concatenate([w_down.T, w_out.T], 1), CORE_FIRST, axis=0, tiled=True
    )
    ffn_weights = lax.all_gather(jnp.concatenate([w_gate, w_up], 1), CORE_FIRST, axis=0, tiled=True)

    x_rows, dy_rows, normed_rows, gains = prepare(
        tokens[0], cotangent[0], jnp.stack([norm_attn, norm_ffn]).astype(F32)
    )
    row = jnp.arange(512, dtype=jnp.int32)
    positions = block * 512 + ((row // 128 + place) % 4) * 128 + row % 128
    frequency = 10000.0 ** (-jnp.arange(32, dtype=F32) * 2.0 / HEAD_SIZE)
    angles = positions.astype(F32)[:, None] * frequency[None, :]
    cosine, sine = jnp.cos(angles), jnp.sin(angles)
    cosine = jnp.concatenate([cosine] * 4, 1)
    sine = jnp.concatenate([-sine, sine, -sine, sine], 1)

    flat = segments.reshape(-1)
    padded = jnp.concatenate([jnp.full((1024,), -1, jnp.int32), flat])
    own = lax.dynamic_slice_in_dim(flat, block * 512, 512, 0)
    window = lax.dynamic_slice_in_dim(padded, block * 512, 1536, 0)
    start = jnp.sum((window[None, :] < own[:, None]).astype(jnp.int32), 1)
    low = jnp.maximum(start, row + 1).reshape(1, 512)

    normed_rows, w_query = keep((normed_rows, w_query))
    ahead, behind = near_pieces(normed_rows)
    qkv_own = gather_axis(jnp.concatenate([w_query, key_projection, value_projection], 1), "x")
    qkv_own = gather_axis(jnp.concatenate(qkv_own, 0), "y")
    far = far_pieces(ahead, behind)
    qkv_own, far, cosine, sine, low = keep((qkv_own, far, cosine, sine, low))
    qkv_pieces = *qkv_own, *(shift(piece, "core", 1) for piece in qkv_own)
    kv_own, normed_one = project_kv(code, (normed_rows, ahead, *far, behind), qkv_pieces, cosine, sine)
    normed_late, kv_own, dy_raw = keep((normed_one, kv_own, cotangent[0]))
    dy_pieces = gather_pieces(dy_raw)
    kv = (from_block(kv_own, 2), from_block(kv_own, 1), kv_own)
    queries, qkv_weights = project_q(code, normed_late, qkv_pieces, cosine, sine)

    kk, vv, kvt = set_up(code, kv)
    seen = code, queries, kk, kvt, low, out_weights
    o_far, lse_far, part_far = attend(2, 1, 1, *seen)
    queries, part_far, dy_pieces = keep((queries, part_far, dy_pieces))
    part_far = shift(part_far, "head", 2)
    seen = code, queries, kk, kvt, low, out_weights
    o_near, lse_near, part_ahead, part_behind = attend(1, 2, 2, *seen)
    queries, part_far, part_ahead, part_behind = keep((queries, part_far, part_ahead, part_behind))
    seen = code, queries, kk, kvt, low, out_weights
    o_own, lse_own, part_own = attend(0, 1, 1, *seen)
    dy, dy_swap = assemble(code, dy_rows, *dy_pieces)
    dy_other = shift(dy_swap, "core", 1)
    attention_sum = part_own, shift(part_ahead, "head", 1), shift(part_behind, "head", -1), part_far
    h1, top, bottom = join(x_rows, gains, attention_sum)
    behind_top, ahead_bottom = shift(top, "head", 1), shift(bottom, "head", -1)
    ahead_top, behind_bottom = shift(top, "head", -1), shift(bottom, "head", 1)
    behind_top, ahead_bottom, dy = keep((behind_top, ahead_bottom, dy))
    far_top, far_bottom = shift(behind_top, "head", 1), shift(ahead_bottom, "head", -1)
    rows_two = top, bottom, ahead_top, ahead_bottom, far_top, far_bottom, behind_top, behind_bottom
    dact = columns_times(dy, out_weights)
    dact, dy_other = keep((dact, dy_other))

    gua, normed_two, normed_two_swap, dnormed_two = ffn(
        code, rows_two, dact, ffn_weights
    )
    dnormed_two = scatter_pieces(*dnormed_two)
    gua_other = shift(gua, "core", 1)
    normed_two_other = shift(normed_two_swap, "core", 1)
    out_pieces = rows_times(gua, 2, out_weights, 0)
    gua_other, normed_two_other, out_pieces = keep((gua_other, normed_two_other, out_pieces))
    held = weight_grads(code, normed_two, normed_two_other, dy, dy_other, gua, gua_other)
    held, dnormed_two = keep((held, dnormed_two))
    grads = lax.psum_scatter(held, ("y", "x"), scatter_dimension=0, tiled=True)

    dh1, dh1_low, grad_gain_two = join_back(h1, dy_rows, gains, dnormed_two)
    back = kk, vv, kvt, low, cosine, sine
    dq_own, dk, dv = attend_back(0, 1, 1, code, queries, o_own, (dh1_low,), out_weights, lse_own, *back, ())
    ahead, behind = shift(dh1_low, "head", -1), shift(dh1_low, "head", 1)
    ahead, behind, dk, dv, dh1_late, out_pieces = keep((ahead, behind, dk, dv, dh1_low, out_pieces))
    far = shift(dh1_late, "head", 2)
    dq_near, dk, dv = attend_back(
        1, 2, 2, code, queries, o_near, (ahead, behind), out_weights, lse_near, *back, (dk, dv)
    )
    far, dk, dv, out_pieces = keep((far, dk, dv, out_pieces))
    out_pieces = scatter_pieces(*out_pieces)
    dq_far, dkv_first, dkv_second, dkv_own = attend_back(
        2, 1, 1, code, queries, o_far, (far,), out_weights, lse_far, *back, (dk, dv)
    )
    dq = dq_own, dq_near, dq_far
    dkv_one = from_block(dkv_second, -1)
    dkv_two = from_block(dkv_first, -2)
    wide_other, wide_own = wide_grads(
        code, normed_one, (dh1_low, ahead, far, behind), (o_own, o_near, o_far), dq
    )
    dkv_one, dkv_two, wide_other, out_pieces = keep((dkv_one, dkv_two, wide_other, out_pieces))
    wide_other = shift(wide_other, "core", 1)

    narrow_other, narrow_own, dnormed_one, gain_grads = finish(
        code,
        normed_one,
        qkv_weights,
        dq,
        dkv_own,
        dkv_one,
        dkv_two,
        cosine,
        sine,
        gains,
        grad_gain_two,
    )
    dnormed_one = lax.psum_scatter(dnormed_one, "head", scatter_dimension=0, tiled=True)
    gain_grads = jnp.concatenate([gain_grads, shift(gain_grads, "core", 1)], 0)
    gain_grads = exchange([gain_grads] * 4, "head")
    rows = [(x_rows.shape, BF16)]
    (output,) = small_call(output_kernel, rows, h1, *out_pieces)
    gain_grads, output = keep((gain_grads, output))
    pieces, out_sums = first_pieces(
        code, wide_own, wide_other, narrow_own, shift(narrow_other, "core", 1), gain_grads
    )
    grads = (
        grads[:, :HIDDEN].astype(F32),
        grads[:, HIDDEN : 2 * HIDDEN].astype(F32),
        grads[:, 2 * HIDDEN :].T.astype(F32),
    )
    pieces, out_sums, grads = keep((exchange(pieces, "x"), exchange(out_sums, "y"), grads))
    pieces, out_sums = second_pieces(code, pieces, out_sums)
    (grad_inputs,) = small_call(input_grad_kernel, rows, dh1, x_rows, gains, dnormed_one)
    pieces, out_sums, grad_inputs = keep((exchange(pieces, "y"), exchange(out_sums, "x"), grad_inputs))
    columns = (64, 512), (64, 512), (64, 64), (64, 64), (1, 2048), (1, 2048)
    grad_out, grad_query, grad_key, grad_value, grad_gain_one, grad_gain_two = small_call(
        attention_grads_kernel,
        [(shape, F32) for shape in columns],
        *pieces,
        *out_sums,
    )

    return (
        output[None],
        grad_inputs[None],
        grad_query,
        grad_key,
        grad_value,
        grad_out.T,
        *grads,
        grad_gain_one.reshape(2048),
        grad_gain_two.reshape(2048),
    )


def solution(mesh):
    grid = Mesh(mesh.devices.reshape(4, 4, 4, 2), ("head", "y", "x", "core"))
    rows, up, down = P(BLK, "head", None), P(BLK, "head"), P("head", BLK)
    return jax.shard_map(
        per_device,
        mesh=grid,
        in_specs=(rows, P(), up, up, up, down, up, up, down, P(), P(), rows),
        out_specs=(rows, rows, up, up, up, down, up, up, down, P(), P()),
        check_vma=False,
    )
```

```python
import functools

import jax
import jax.numpy as jnp
from jax import lax
from jax.experimental import pallas as pl
from jax.experimental.pallas import tpu as pltpu
from jax.sharding import Mesh
from jax.sharding import PartitionSpec as P

HEAD_SIZE = 64
WINDOW = 1024
HIDDEN = 1408
EPSILON = 1e-05
BF16 = jnp.bfloat16
F32 = jnp.float32
BLK = ("y", "x", "core")
CORE_FIRST = ("core", "y", "x")
VMEM_LIMIT = 63 * 1024 * 1024


def dot_nn(a, b):
    return jnp.dot(a, b, preferred_element_type=F32)


def dot_nt(a, b):
    return lax.dot_general(a, b, (((1,), (1,)), ((), ())), preferred_element_type=F32)


def dot_tn(a, b):
    return lax.dot_general(a, b, (((0,), (0,)), ((), ())), preferred_element_type=F32)


def shift(value, axis, distance):
    size = lax.axis_size(axis)
    return lax.ppermute(value, axis, [(i, (i + distance) % size) for i in range(size)])


def add_low(a, b):
    return (a.astype(F32) + b.astype(F32)).astype(BF16)


def gather_pieces(rows):
    return shift(rows, "head", -1), shift(rows, "head", 2), shift(rows, "head", 1)


def near_pieces(rows):
    return shift(rows, "head", -1), shift(rows, "head", 1)


def far_pieces(ahead, behind):
    half = ahead.shape[0] // 2
    return shift(behind[:half], "head", 1), shift(ahead[half:], "head", -1)


def scatter_pieces(own, ahead, far, behind):
    return own, shift(ahead, "head", 1), shift(behind, "head", -1), shift(far, "head", 2)


def gather_axis(value, axis):
    return value, shift(value, axis, -1), shift(value, axis, 2), shift(value, axis, 1)


def exchange(pieces, axis):
    return pieces[0], shift(pieces[1], axis, 1), shift(pieces[2], axis, 2), shift(pieces[3], axis, -1)


def from_block(value, distance):
    route = [(i, i + distance) for i in range(32) if 0 <= i + distance < 32]
    return lax.ppermute(value, BLK, route)


def scale_of(values):
    return lax.rsqrt(jnp.mean(values * values, -1, keepdims=True) + EPSILON)


def x_of(code):
    return lax.shift_right_logical(code[0], 5)


def y_of(code):
    return lax.shift_right_logical(code[0], 3) & 3


def core_of(code):
    return lax.shift_right_logical(code[0], 2) & 1


def place_of(code):
    return code[0] & 3


def lane_is_low(shape, period):
    return lax.broadcasted_iota(jnp.int32, shape, len(shape) - 1) % period < period // 2


def turn(values, cosine, sine):
    swapped = jnp.where(
        lane_is_low(values.shape, 64), pltpu.roll(values, 96, 1), pltpu.roll(values, 32, 1)
    )
    return values * cosine + swapped * sine


def core_major_tiles(tiles):
    low = lane_is_low(tiles[0].shape, 128)
    rolled = [pltpu.roll(tile, 64, 1) for tile in tiles]
    first = [jnp.where(low, tiles[2 * k], rolled[2 * k + 1]) for k in range(8)]
    second = [jnp.where(low, rolled[2 * k], tiles[2 * k + 1]) for k in range(8)]
    return first + second


def block_major_tiles(tiles):
    low = lane_is_low(tiles[0].shape, 128)
    rolled = [pltpu.roll(tile, 64, 1) for tile in tiles]
    result = []
    for k in range(8):
        result.append(jnp.where(low, tiles[k], rolled[8 + k]))
        result.append(jnp.where(low, rolled[k], tiles[8 + k]))
    return result


def in_tiles(value):
    return [value[:, 128 * k : 128 * k + 128] for k in range(16)]


def prepare_kernel(x_ref, dy_ref, gain_ref, x_out, dy_out, normed_out, gain_out):
    def convert(ref):
        return jnp.concatenate(core_major_tiles(in_tiles(ref[...].astype(F32))), 1)

    x, gains = convert(x_ref), convert(gain_ref)
    gain_out[...] = gains
    x_out[...] = x
    dy_out[...] = convert(dy_ref).astype(BF16)
    normed_out[...] = (x * scale_of(x) * gains[:1]).astype(BF16)


def prepare(x, dy, gains):
    rows, width = x.shape
    return pl.pallas_call(
        prepare_kernel,
        out_shape=(
            jax.ShapeDtypeStruct((rows, width), F32),
            jax.ShapeDtypeStruct((rows, width), BF16),
            jax.ShapeDtypeStruct((rows, width), BF16),
            jax.ShapeDtypeStruct(gains.shape, F32),
        ),
        compiler_params=pltpu.CompilerParams(vmem_limit_bytes=VMEM_LIMIT),
        cost_estimate=pl.CostEstimate(
            flops=10 * rows * width, bytes_accessed=10 * rows * width, transcendentals=rows
        ),
    )(x, dy, gains)


def to_blocks(value):
    return jnp.concatenate(block_major_tiles(in_tiles(value)), 1)


def assemble_kernel(core_ref, own_ref, ahead_ref, far_ref, behind_ref, out_ref, swap_ref):
    out_ref[:128] = own_ref[...]
    start = 128
    for ref in (ahead_ref, far_ref, behind_ref):
        size = ref.shape[0]
        out_ref[start : start + size] = jnp.concatenate(
            core_major_tiles(in_tiles(ref[...].astype(F32))), 1
        ).astype(BF16)
        start += size
    swap_ref[...] = jnp.where(core_of(core_ref) == 0, out_ref[:, 1024:], out_ref[:, :1024])


def assemble(core, own, ahead, far, behind):
    vmem = pl.BlockSpec(memory_space=pltpu.VMEM)
    return pl.pallas_call(
        assemble_kernel,
        out_shape=(jax.ShapeDtypeStruct((512, 2048), BF16), jax.ShapeDtypeStruct((512, 1024), BF16)),
        in_specs=[pl.BlockSpec(memory_space=pltpu.SMEM)] + [vmem] * 4,
        out_specs=(vmem, vmem),
        compiler_params=pltpu.CompilerParams(vmem_limit_bytes=VMEM_LIMIT),
        cost_estimate=pl.CostEstimate(
            flops=4 * 512 * 2048, bytes_accessed=5 * 1024 * 1024, transcendentals=0
        ),
    )(core, own, ahead, far, behind)


def small_call(kernel, out_shape, *operands):
    return pl.pallas_call(
        kernel,
        out_shape=tuple(jax.ShapeDtypeStruct(shape, dtype) for shape, dtype in out_shape),
        compiler_params=pltpu.CompilerParams(vmem_limit_bytes=VMEM_LIMIT),
        cost_estimate=pl.CostEstimate(
            flops=sum(x.size for x in operands),
            bytes_accessed=2 * sum(x.size * x.dtype.itemsize for x in operands),
            transcendentals=0,
        ),
    )(*operands)


def total_of(refs):
    values = [ref[...].astype(F32) for ref in refs]
    while len(values) > 1:
        values = [values[0] + values[1]] + values[2:]
    return values[0]


def join_kernel(x_ref, gain_ref, a_ref, b_ref, c_ref, d_ref, h_out, top_out, bottom_out):
    h = x_ref[...] + total_of((a_ref, b_ref, c_ref, d_ref))
    h_out[...] = h
    normed = (h * scale_of(h) * gain_ref[1:2]).astype(BF16)
    half = h.shape[0] // 2
    top_out[...], bottom_out[...] = normed[:half], normed[half:]


def join(x, gain, pieces):
    half = x.shape[0] // 2, x.shape[1]
    return small_call(join_kernel, ((x.shape, F32), (half, BF16), (half, BF16)), x, gain, *pieces)


def norm_backward(values, gain, grad):
    scale = scale_of(values)
    weighted = grad * gain
    inner = jnp.mean(weighted * values, -1, keepdims=True)
    return scale * weighted - values * (scale * scale * scale * inner), scale


def join_back_kernel(h_ref, dy_ref, gain_ref, a_ref, b_ref, c_ref, d_ref, dh_out, low_out, grad_out):
    h, grad = h_ref[...], total_of((a_ref, b_ref, c_ref, d_ref))
    back, scale = norm_backward(h, gain_ref[1:2], grad)
    dh = dy_ref[...].astype(F32) + back
    dh_out[...] = dh
    low_out[...] = dh.astype(BF16)
    grad_out[...] = to_blocks(jnp.broadcast_to(jnp.sum(grad * h * scale, 0, keepdims=True), (8, h.shape[1])))


def join_back(h, dy, gain, pieces):
    shapes = (h.shape, F32), (h.shape, BF16), ((8, h.shape[1]), F32)
    return small_call(join_back_kernel, shapes, h, dy, gain, *pieces)


def output_kernel(h_ref, a_ref, b_ref, c_ref, d_ref, out_ref):
    out_ref[...] = to_blocks(h_ref[...] + total_of((a_ref, b_ref, c_ref, d_ref))).astype(BF16)


def input_grad_kernel(dh_ref, x_ref, gain_ref, grad_ref, out_ref):
    back, _ = norm_backward(x_ref[...], gain_ref[:1], grad_ref[...].astype(F32))
    out_ref[...] = to_blocks(dh_ref[...] + back).astype(BF16)


GAIN_ROWS, GAIN_COLUMNS = 16, 256


def gain_rows(vector):
    return jnp.concatenate([vector[:, 256 * k : 256 * k + 256] for k in range(8)], 0)


def put_piece(ref, rows, gains):
    count = rows.shape[0]
    ref[:count] = rows
    ref[count:, GAIN_COLUMNS:] = jnp.zeros((GAIN_ROWS, ref.shape[1] - GAIN_COLUMNS), BF16)
    ref[count:, :GAIN_COLUMNS] = gains.astype(BF16)


def first_pieces_kernel(
    at_ref, q_ref, q2_ref, kv_ref, kv2_ref, o_ref, o2_ref, *refs
):
    gain_refs, out_refs = refs[:4], refs[4:]
    query = add_low(q_ref[...], q2_ref[...]).reshape(256, 512)
    narrow = add_low(kv_ref[...], kv2_ref[...]).reshape(256, 128)
    rows = jnp.concatenate([query, narrow], 1)
    out_rows = add_low(o_ref[...], o2_ref[...]).reshape(256, 512)
    gains = total_of(gain_refs)
    gains = gains[:GAIN_ROWS] + gains[GAIN_ROWS:]
    for number in range(4):

        @pl.when(pl.program_id(0) == number)
        def _():
            put_piece(out_refs[number], rows, gains)
            out_refs[4 + number][...] = out_rows


def first_pieces(at, wide, wide2, narrow, narrow2, gains):
    pick_x = lambda column: lambda d, s: (0, lax.rem(x_of(s) + d, 4), 0, column)
    pick_y = lambda d, s: (lax.rem(y_of(s) + d, 4), 0, 0, 0)
    whole = lambda d, s: (0, 0)
    shaped = lambda value: value.reshape(4, 4, 64, value.shape[1])
    shapes = [(256 + GAIN_ROWS, 640)] * 4 + [(256, 512)] * 4
    grid = pltpu.PrefetchScalarGridSpec(
        num_scalar_prefetch=1,
        grid=(4,),
        in_specs=[pl.BlockSpec((4, 1, 64, 512), pick_x(1))] * 2
        + [pl.BlockSpec((4, 1, 64, 128), pick_x(0))] * 2
        + [pl.BlockSpec((1, 4, 64, 512), pick_y)] * 2
        + [pl.BlockSpec((2 * GAIN_ROWS, GAIN_COLUMNS), whole)] * 4,
        out_specs=tuple(pl.BlockSpec(shape, whole) for shape in shapes),
    )
    wide, wide2 = shaped(wide), shaped(wide2)
    result = pl.pallas_call(
        first_pieces_kernel,
        grid_spec=grid,
        out_shape=tuple(jax.ShapeDtypeStruct(shape, BF16) for shape in shapes),
        compiler_params=pltpu.CompilerParams(vmem_limit_bytes=VMEM_LIMIT),
        cost_estimate=pl.CostEstimate(
            flops=2 * 1024 * 1152, bytes_accessed=6 * 1024 * 1152, transcendentals=0
        ),
    )(at, wide, wide2, shaped(narrow), shaped(narrow2), wide, wide2, *gains)
    return result[:4], result[4:]


def second_qkv_kernel(at_ref, a_ref, b_ref, c_ref, d_ref, *refs):
    held = refs[4]
    held[...] = total_of((a_ref, b_ref, c_ref, d_ref))
    for number, ref in enumerate(refs[:4]):
        row = pl.multiple_of(lax.rem(y_of(at_ref) + number, 4) * 64, 64)
        put_piece(ref, held[pl.ds(row, 64), :].astype(BF16), held[256:, :GAIN_COLUMNS])


def second_out_kernel(at_ref, a_ref, b_ref, c_ref, d_ref, *refs):
    held = refs[4]
    held[...] = total_of((a_ref, b_ref, c_ref, d_ref)).astype(BF16)
    for number, ref in enumerate(refs[:4]):
        row = pl.multiple_of(lax.rem(x_of(at_ref) + number, 4) * 64, 64)
        ref[...] = held[pl.ds(row, 64), :]


def second_pieces(kernel, shape, held_type, at, pieces):
    vmem = pl.BlockSpec(memory_space=pltpu.VMEM)
    return pl.pallas_call(
        kernel,
        out_shape=(jax.ShapeDtypeStruct(shape, BF16),) * 4,
        in_specs=[pl.BlockSpec(memory_space=pltpu.SMEM)] + [vmem] * 4,
        out_specs=(vmem,) * 4,
        scratch_shapes=[pltpu.VMEM(pieces[0].shape, held_type)],
        compiler_params=pltpu.CompilerParams(vmem_limit_bytes=VMEM_LIMIT),
        cost_estimate=pl.CostEstimate(
            flops=4 * pieces[0].size, bytes_accessed=10 * pieces[0].size, transcendentals=0
        ),
    )(at, *pieces)


def attention_grads_kernel(*refs):
    out_ref, q_ref, k_ref, v_ref, one_ref, two_ref = refs[8:]
    total = total_of(refs[:4])
    out_ref[...] = total_of(refs[4:8])
    q_ref[...] = total[:64, :512]
    k_ref[...] = total[:64, 512:576]
    v_ref[...] = total[:64, 576:]
    gains = total[64:, :GAIN_COLUMNS]
    one_ref[...] = jnp.concatenate([gains[k : k + 1] for k in range(8)], 1)
    two_ref[...] = jnp.concatenate([gains[k : k + 1] for k in range(8, 16)], 1)


def put_in_order(at_ref, piece_refs, columns, to_ref, sems):
    x, y, core = x_of(at_ref), y_of(at_ref), core_of(at_ref)
    copies = []
    for number in range(32):
        to_x, to_y = lax.rem(x + number % 4, 4), lax.rem(y + number // 4 % 4, 4)
        to_core = core if number < 16 else 1 - core
        row = pl.multiple_of(((to_core * 4 + to_y) * 4 + to_x) * 64, 64)
        copy = pltpu.make_async_copy(
            piece_refs[number // 4].at[pl.ds(number % 4 * 64, 64), columns],
            to_ref.at[pl.ds(row, 64)],
            sems.at[number],
        )
        copy.start()
        copies.append(copy)
    return copies


RING_PIECES = [(0, 128), (128, 128), (256, 64), (320, 64), (384, 128)]


def project_kv_kernel(at_ref, *refs):
    x_refs, piece_refs, (cos_ref, sin_ref, kv_ref, whole_ref) = refs[:5], refs[5:13], refs[13:17]
    x_held, held, sems, x_sems = refs[17:]
    copies = []
    for number, (start, size) in enumerate(RING_PIECES):
        copy = pltpu.make_async_copy(x_refs[number], x_held.at[pl.ds(start, size)], x_sems.at[number])
        copy.start()
        copies.append(copy)
    copies += put_in_order(at_ref, piece_refs, pl.ds(512, 128), held, sems)
    for copy in copies:
        copy.wait()
    whole = pltpu.make_async_copy(x_held, whole_ref, x_sems.at[len(RING_PIECES)])
    whole.start()
    flat = dot_nn(x_held[...], held[...])
    turned = turn(flat, cos_ref[...], sin_ref[...])
    kv_ref[...] = jnp.where(lane_is_low(flat.shape, 128), turned, flat).astype(BF16)
    whole.wait()


def project_kv(at, x_pieces, weights, cosine, sine):
    rows, width = 512, x_pieces[0].shape[1]
    vmem, anywhere = pl.BlockSpec(memory_space=pltpu.VMEM), pl.BlockSpec(memory_space=pl.ANY)
    return pl.pallas_call(
        project_kv_kernel,
        out_shape=(jax.ShapeDtypeStruct((rows, 128), BF16), jax.ShapeDtypeStruct((rows, width), BF16)),
        in_specs=[pl.BlockSpec(memory_space=pltpu.SMEM)] + [anywhere] * 13 + [vmem, vmem],
        out_specs=(vmem, anywhere),
        scratch_shapes=[
            pltpu.VMEM((rows, width), BF16),
            pltpu.VMEM((width, 128), BF16),
            pltpu.SemaphoreType.DMA((32,)),
            pltpu.SemaphoreType.DMA((len(RING_PIECES) + 1,)),
        ],
        compiler_params=pltpu.CompilerParams(vmem_limit_bytes=VMEM_LIMIT),
        cost_estimate=pl.CostEstimate(
            flops=2 * rows * width * 128, bytes_accessed=5 * 1024 * 1024, transcendentals=0
        ),
    )(at, *x_pieces, *weights, cosine, sine)


def project_q_kernel(at_ref, x_ref, *refs):
    piece_refs, (cos_ref, sin_ref, q_ref, w_ref, held, sems, sem) = refs[:8], refs[8:]
    for copy in put_in_order(at_ref, piece_refs, pl.ds(0, 640), held, sems):
        copy.wait()
    whole = pltpu.make_async_copy(held, w_ref, sem)
    whole.start()
    cosine, sine, x = cos_ref[...], sin_ref[...], x_ref[...]
    for start in (0, 256):
        wide = dot_nn(x, held[:, start : start + 256])
        for part in (0, 128):
            turned = turn(wide[:, part : part + 128], cosine, sine)
            q_ref[:, start + part : start + part + 128] = (turned * HEAD_SIZE**-0.5).astype(BF16)
    whole.wait()


def project_q(at, normed, weights, cosine, sine):
    rows, width = normed.shape
    vmem, anywhere = pl.BlockSpec(memory_space=pltpu.VMEM), pl.BlockSpec(memory_space=pl.ANY)
    return pl.pallas_call(
        project_q_kernel,
        out_shape=(jax.ShapeDtypeStruct((rows, 512), BF16), jax.ShapeDtypeStruct((width, 640), BF16)),
        in_specs=[pl.BlockSpec(memory_space=pltpu.SMEM), vmem] + [anywhere] * 8 + [vmem, vmem],
        out_specs=(vmem, anywhere),
        scratch_shapes=[
            pltpu.VMEM((width, 640), BF16),
            pltpu.SemaphoreType.DMA((32,)),
            pltpu.SemaphoreType.DMA,
        ],
        compiler_params=pltpu.CompilerParams(vmem_limit_bytes=VMEM_LIMIT),
        cost_estimate=pl.CostEstimate(
            flops=2 * rows * width * 512, bytes_accessed=7 * 1024 * 1024, transcendentals=0
        ),
    )(at, normed, *weights, cosine, sine)


KEYS = 1152
PAIRS = 4


def set_up_kernel(place_ref, kv0_ref, kv1_ref, kv2_ref, kk_ref, vv_ref, kvt_ref):
    place = place_of(place_ref)
    low = lane_is_low((128, 128), 128)
    for block, ref in enumerate((kv0_ref, kv1_ref, kv2_ref)):
        for group in range(4):
            at = pl.multiple_of(lax.rem(group - place + 4, 4) * 128, 128)
            piece = ref[pl.ds(at, 128), :].astype(F32)
            rolled = pltpu.roll(piece, 64, 1)
            to = block * 512 + group * 128
            kk_ref[to : to + 128, :] = jnp.where(low, piece, rolled).astype(BF16)
            vv_ref[to : to + 128, :] = jnp.where(low, rolled, piece).astype(BF16)
            kvt_ref[:, to : to + 128] = piece.T.astype(BF16)


def set_up(place, kv):
    vmem = pl.BlockSpec(memory_space=pltpu.VMEM)
    return pl.pallas_call(
        set_up_kernel,
        out_shape=(
            jax.ShapeDtypeStruct((1536, 128), BF16),
            jax.ShapeDtypeStruct((1536, 128), BF16),
            jax.ShapeDtypeStruct((128, 1536), BF16),
        ),
        in_specs=[pl.BlockSpec(memory_space=pltpu.SMEM), vmem, vmem, vmem],
        out_specs=(vmem, vmem, vmem),
        compiler_params=pltpu.CompilerParams(vmem_limit_bytes=VMEM_LIMIT),
        cost_estimate=pl.CostEstimate(flops=1536 * 128 * 8, bytes_accessed=2 * 1024 * 1024, transcendentals=0),
    )(place, *kv)


def both_heads(pair):
    low = lane_is_low(pair.shape, 128)
    nothing = jnp.zeros_like(pair)
    return jnp.concatenate([jnp.where(low, pair, nothing), jnp.where(low, nothing, pair)], 0)


def side_by_side(transposed):
    return jnp.concatenate([transposed[:, :128], transposed[:, 128:]], 0).T


def mask_of(at, low_ref):
    key = lax.broadcasted_iota(jnp.int32, (KEYS, 128), 0)
    query = lax.broadcasted_iota(jnp.int32, (KEYS, 128), 1)
    seen = (key >= low_ref[:, pl.ds(at, 128)] - at) & (key <= query + WINDOW)
    bias = jnp.where(seen, 0.0, -jnp.inf)
    return jnp.concatenate([bias, bias], 1)


def attend_kernel(
    first, step, place_ref, q_ref, kk_ref, kvt_ref, low_ref, w_ref, o_ref, lse_ref, *refs
):
    part_refs, (bias, held, w_held, sem) = refs[:-4], refs[-4:]
    group = lax.rem(place_of(place_ref) + first + step * pl.program_id(0), 4)
    at = pl.multiple_of(group * 128, 128)

    load = pltpu.make_async_copy(w_ref.at[:, pl.ds(HIDDEN, 512)], w_held, sem)

    @pl.when((pl.program_id(0) == 0) & (pl.program_id(1) == 0))
    def _():
        load.start()

    @pl.when(pl.program_id(1) == 0)
    def _():
        bias[...] = mask_of(at, low_ref)

    keys = pl.ds(at, KEYS)
    for number in range(PAIRS):
        columns = slice(128 * number, 128 * number + 128)
        scores = dot_nt(kk_ref[keys, :], both_heads(q_ref[:, columns])) + bias[...]
        top = jnp.max(scores, 0, keepdims=True)
        weights = jnp.exp(scores - top)
        total = jnp.sum(weights, 0, keepdims=True)
        result = dot_nn(kvt_ref[64:128, keys], weights.astype(BF16)) / total
        lse_ref[0, number] = top + jnp.log(total)
        result = side_by_side(result).astype(BF16)
        o_ref[:, columns] = result
        held[PAIRS * pl.program_id(1) + number] = result

    @pl.when(pl.program_id(1) == 4 // PAIRS - 1)
    def _():
        @pl.when(pl.program_id(0) == 0)
        def _():
            load.wait()

        rows = jnp.concatenate([held[k] for k in range(4)], 1)
        part = dot_nt(rows, w_held[...]).astype(BF16)
        for number, ref in enumerate(part_refs):

            @pl.when(pl.program_id(0) == number)
            def _():
                ref[...] = part


def attend(first, step, count, place, queries, kk, kvt, low, weights):
    whole = lambda g, p, s: (0, 0)
    width = 128 * PAIRS
    grid = pltpu.PrefetchScalarGridSpec(
        num_scalar_prefetch=1,
        grid=(count, 4 // PAIRS),
        in_specs=[
            pl.BlockSpec((128, width), lambda g, p, s: (first + step * g, p)),
            pl.BlockSpec((1536, 128), whole),
            pl.BlockSpec((128, 1536), whole),
            pl.BlockSpec((1, 512), whole),
            pl.BlockSpec(memory_space=pl.ANY),
        ],
        out_specs=(
            pl.BlockSpec((128, width), lambda g, p, s: (g, p)),
            pl.BlockSpec((1, PAIRS, 1, 256), lambda g, p, s: (g, p, 0, 0)),
        )
        + (pl.BlockSpec((128, 2048), whole),) * count,
        scratch_shapes=[
            pltpu.VMEM((KEYS, 256), F32),
            pltpu.VMEM((4, 128, 128), BF16),
            pltpu.VMEM((2048, 512), BF16),
            pltpu.SemaphoreType.DMA,
        ],
    )
    return pl.pallas_call(
        functools.partial(attend_kernel, first, step),
        grid_spec=grid,
        out_shape=(
            jax.ShapeDtypeStruct((128 * count, 512), BF16),
            jax.ShapeDtypeStruct((count, 4, 1, 256), F32),
        )
        + (jax.ShapeDtypeStruct((128, 2048), BF16),) * count,
        compiler_params=pltpu.CompilerParams(vmem_limit_bytes=VMEM_LIMIT),
        cost_estimate=pl.CostEstimate(
            flops=count * 4 * KEYS * 256 * 256 * 2,
            bytes_accessed=3 * 1024 * 1024,
            transcendentals=count * 4 * KEYS * 256,
        ),
    )(place, queries, kk, kvt, low, weights)


def attend_back_kernel(first, step, count, *refs):
    last = first == 2
    place_ref, q_ref, w_ref, lse_ref, kk_ref, vv_ref, kvt_ref, low_ref, cos_ref, sin_ref = refs[:10]
    o_ref = refs[10]
    dh_refs, refs = refs[11 : 11 + count], refs[11 + count :]
    dk_in = dv_in = None
    if first > 0:
        dk_in, dv_in, refs = refs[0], refs[1], refs[2:]
    bias, do_held, dk, dv, w_held, sem = refs[-6:]
    dq_ref, outs = refs[0], refs[1:-6]
    number, pair = pl.program_id(0), pl.program_id(1)
    place = place_of(place_ref)
    at = pl.multiple_of(lax.rem(place + first + step * number, 4) * 128, 128)

    load = pltpu.make_async_copy(w_ref.at[:, pl.ds(HIDDEN, 512)], w_held, sem)

    @pl.when((number == 0) & (pair == 0))
    def _():
        load.start()
        dk[...] = jnp.zeros_like(dk) if dk_in is None else dk_in[...]
        dv[...] = jnp.zeros_like(dv) if dv_in is None else dv_in[...]

    @pl.when(pair == 0)
    def _():
        bias[...] = mask_of(at, low_ref)

        @pl.when(number == 0)
        def _():
            load.wait()

        for k, ref in enumerate(dh_refs):

            @pl.when(number == k)
            def _():
                do_rows = dot_nn(ref[...], w_held[...]).astype(BF16)
                for p in range(4):
                    do_held[p] = do_rows[:, 128 * p : 128 * p + 128]

    keys = pl.ds(at, KEYS)
    queries, grads, all_weights, all_grad_scores = [], [], [], []
    for k in range(PAIRS):
        columns = slice(128 * k, 128 * k + 128)
        do_pair = do_held[PAIRS * pair + k]
        query, grad = both_heads(q_ref[:, columns]), both_heads(do_pair)
        scores = dot_nt(kk_ref[keys, :], query) + bias[...]
        weights = jnp.exp(scores - lse_ref[0, k])
        grad_weights = dot_nt(vv_ref[keys, :], grad)
        product = (o_ref[:, columns].astype(F32) * do_pair.astype(F32)).T
        inner = jnp.concatenate(
            [jnp.sum(product[:64], 0, keepdims=True), jnp.sum(product[64:], 0, keepdims=True)], 1
        )
        grad_scores = (weights * (grad_weights - inner)).astype(BF16)
        grad_query = side_by_side(dot_nn(kvt_ref[0:64, keys], grad_scores)) * HEAD_SIZE**-0.5
        dq_ref[:, columns] = turn(grad_query, cos_ref[...], -sin_ref[...]).astype(BF16)
        queries.append(query)
        grads.append(grad)
        all_weights.append(weights.astype(BF16))
        all_grad_scores.append(grad_scores)
    join = lambda values, axis: values[0] if PAIRS == 1 else jnp.concatenate(values, axis)
    dv[keys, :] += dot_nn(join(all_weights, 1), join(grads, 0))
    dk[keys, :] += dot_nn(join(all_grad_scores, 1), join(queries, 0))

    @pl.when((number == pl.num_programs(0) - 1) & (pair == 4 // PAIRS - 1))
    def _():
        if not last:
            outs[0][...], outs[1][...] = dk[...], dv[...]
            return
        half = lane_is_low((128, 128), 128)
        for block in range(3):
            for group in range(4):
                to = pl.multiple_of(lax.rem(group - place + 4, 4) * 128, 128)
                frm = slice(block * 512 + group * 128, block * 512 + group * 128 + 128)
                key, value = dk[frm, :], dv[frm, :]
                key = key + pltpu.roll(key, 64, 1)
                value = value + pltpu.roll(value, 64, 1)
                both = jnp.where(half, key, value)
                outs[block][pl.ds(to, 128), :] = both.astype(outs[block].dtype)


def attend_back(first, step, count, place, queries, o, dh, weights, lse, kk, vv, kvt, low, cosine, sine, held):
    last = first == 2
    whole = lambda g, p, s: (0, 0)
    specs = [
        pl.BlockSpec((128, 128 * PAIRS), lambda g, p, s: (first + step * g, p)),
        pl.BlockSpec(memory_space=pl.ANY),
        pl.BlockSpec((1, PAIRS, 1, 256), lambda g, p, s: (g, p, 0, 0)),
        pl.BlockSpec((1536, 128), whole),
        pl.BlockSpec((1536, 128), whole),
        pl.BlockSpec((128, 1536), whole),
        pl.BlockSpec((1, 512), whole),
        pl.BlockSpec((128, 128), lambda g, p, s: (first + step * g, 0)),
        pl.BlockSpec((128, 128), lambda g, p, s: (first + step * g, 0)),
    ]
    specs += [pl.BlockSpec((128, 128 * PAIRS), lambda g, p, s: (g, p))]
    specs += [pl.BlockSpec((128, 2048), whole)] * count + [pl.BlockSpec((1536, 128), whole)] * len(held)
    if last:
        out_specs = (pl.BlockSpec((512, 128), whole),) * 3
        out_shape = tuple(jax.ShapeDtypeStruct((512, 128), dtype) for dtype in (BF16, BF16, F32))
    else:
        out_specs = (pl.BlockSpec((1536, 128), whole),) * 2
        out_shape = (jax.ShapeDtypeStruct((1536, 128), F32),) * 2
    grid = pltpu.PrefetchScalarGridSpec(
        num_scalar_prefetch=1,
        grid=(count, 4 // PAIRS),
        in_specs=specs,
        out_specs=(pl.BlockSpec((128, 128 * PAIRS), lambda g, p, s: (g, p)),) + out_specs,
        scratch_shapes=[
            pltpu.VMEM((KEYS, 256), F32),
            pltpu.VMEM((4, 128, 128), BF16),
            pltpu.VMEM((1536, 128), F32),
            pltpu.VMEM((1536, 128), F32),
            pltpu.VMEM((2048, 512), BF16),
            pltpu.SemaphoreType.DMA,
        ],
    )
    return pl.pallas_call(
        functools.partial(attend_back_kernel, first, step, count),
        grid_spec=grid,
        out_shape=(jax.ShapeDtypeStruct((128 * count, 512), BF16),) + out_shape,
        compiler_params=pltpu.CompilerParams(vmem_limit_bytes=VMEM_LIMIT),
        cost_estimate=pl.CostEstimate(
            flops=count * 4 * KEYS * 256 * 640 * 2,
            bytes_accessed=6 * 1024 * 1024,
            transcendentals=count * 4 * KEYS * 256,
        ),
    )(place, queries, weights, lse, kk, vv, kvt, low, cosine, sine, o, *dh, *held)


GROUPS = [(0, 128), (128, 256), (384, 512), (896, 512)]


def columns_times_kernel(left_ref, right_ref, out_ref, left, right, out, sems, out_sems):
    load = pltpu.make_async_copy(left_ref, left, sems.at[len(GROUPS)])
    load.start()
    copies, results = [], []
    for number, (start, width) in enumerate(GROUPS):
        columns = pl.ds(start, width)
        copy = pltpu.make_async_copy(right_ref.at[:, columns], right.at[:, columns], sems.at[number])
        copy.start()
        copies.append(copy)
    load.wait()
    value = left[...]
    for number, (start, width) in enumerate(GROUPS):
        copies[number].wait()
        out[:, start : start + width] = dot_nn(value, right[:, start : start + width])
        columns = pl.ds(start, width)
        copy = pltpu.make_async_copy(out.at[:, columns], out_ref.at[:, columns], out_sems.at[number])
        copy.start()
        results.append(copy)
    for copy in results:
        copy.wait()


def columns_times(left, right):
    rows, width = left.shape
    anywhere = pl.BlockSpec(memory_space=pl.ANY)
    return pl.pallas_call(
        columns_times_kernel,
        out_shape=jax.ShapeDtypeStruct((rows, HIDDEN), F32),
        in_specs=[anywhere, anywhere],
        out_specs=anywhere,
        scratch_shapes=[
            pltpu.VMEM((rows, width), BF16),
            pltpu.VMEM((width, HIDDEN), BF16),
            pltpu.VMEM((rows, HIDDEN), F32),
            pltpu.SemaphoreType.DMA((len(GROUPS) + 1,)),
            pltpu.SemaphoreType.DMA((len(GROUPS),)),
        ],
        compiler_params=pltpu.CompilerParams(vmem_limit_bytes=VMEM_LIMIT),
        cost_estimate=pl.CostEstimate(
            flops=2 * rows * width * HIDDEN, bytes_accessed=11 * 1024 * 1024, transcendentals=0
        ),
    )(left, right)


PIECES = [(0, 128), (128, 128), (256, 128), (384, 128)]


def ffn_kernel(*refs):
    core_ref, x_refs, dact_ref, w_ref = refs[0], refs[1:9], refs[9], refs[10]
    gua_ref, whole_ref, swap_ref, dx_refs = refs[11], refs[12], refs[13], refs[14:18]
    x_held, dact_held, w_held, gua, dx, sems, out_sems = refs[18:]
    x_copies = []
    for number in range(8):
        copy = pltpu.make_async_copy(
            x_refs[number], x_held.at[pl.ds(64 * number, 64)], sems.at[12 + number]
        )
        copy.start()
        x_copies.append(copy)
    copies = []
    for number, (start, width) in enumerate(GROUPS):
        for part in range(3):
            if part < 2:
                columns = pl.ds(part * HIDDEN + start, width)
                copy = pltpu.make_async_copy(
                    w_ref.at[:, columns], w_held.at[:, columns], sems.at[3 * number + part]
                )
            else:
                columns = pl.ds(start, width)
                copy = pltpu.make_async_copy(
                    dact_ref.at[:, columns], dact_held.at[:, columns], sems.at[3 * number + part]
                )
            copy.start()
            copies.append(copy)
    for copy in x_copies:
        copy.wait()
    half = pl.multiple_of((1 - core_of(core_ref)) * 1024, 1024)
    results = [
        pltpu.make_async_copy(x_held, whole_ref, out_sems.at[5]),
        pltpu.make_async_copy(x_held.at[:, pl.ds(half, 1024)], swap_ref, out_sems.at[6]),
    ]
    for copy in results:
        copy.start()
    x = x_held[...]
    for number, (start, width) in enumerate(GROUPS):
        for part in range(3):
            copies[3 * number + part].wait()
        gate = dot_nn(x, w_held[:, start : start + width])
        up = dot_nn(x, w_held[:, HIDDEN + start : HIDDEN + start + width])
        dact = dact_held[:, start : start + width]
        sig = jax.nn.sigmoid(gate)
        silu = gate * sig
        dgate = dact * up * (sig * (1.0 + gate * (1.0 - sig)))
        gua[:, start : start + width] = dgate.astype(BF16)
        gua[:, HIDDEN + start : HIDDEN + start + width] = (dact * silu).astype(BF16)
        gua[:, 2 * HIDDEN + start : 2 * HIDDEN + start + width] = (silu * up).astype(BF16)
    copy = pltpu.make_async_copy(gua, gua_ref, out_sems.at[4])
    copy.start()
    results.append(copy)
    dgu = gua[:, : 2 * HIDDEN]
    for number in range(4):
        columns = slice(512 * number, 512 * number + 512)
        dx[:, columns] = dot_nt(dgu, w_held[columns, : 2 * HIDDEN]).astype(BF16)
        for piece, (start, size) in enumerate(PIECES):
            copy = pltpu.make_async_copy(
                dx.at[pl.ds(start, size), pl.ds(512 * number, 512)],
                dx_refs[piece].at[:, pl.ds(512 * number, 512)],
                out_sems.at[7 + 4 * number + piece],
            )
            copy.start()
            results.append(copy)
    for copy in results:
        copy.wait()


def ffn(core, pieces, dact, weights):
    rows, width = dact.shape[0], weights.shape[0]
    anywhere = pl.BlockSpec(memory_space=pl.ANY)
    result = pl.pallas_call(
        ffn_kernel,
        out_shape=(
            jax.ShapeDtypeStruct((rows, 3 * HIDDEN), BF16),
            jax.ShapeDtypeStruct((rows, width), BF16),
            jax.ShapeDtypeStruct((rows, width // 2), BF16),
            *(jax.ShapeDtypeStruct((size, width), BF16) for _, size in PIECES),
        ),
        in_specs=[pl.BlockSpec(memory_space=pltpu.SMEM)] + [anywhere] * 10,
        out_specs=(anywhere,) * 7,
        scratch_shapes=[
            pltpu.VMEM((rows, width), BF16),
            pltpu.VMEM((rows, HIDDEN), F32),
            pltpu.VMEM((width, 2 * HIDDEN), BF16),
            pltpu.VMEM((rows, 3 * HIDDEN), BF16),
            pltpu.VMEM((rows, width), BF16),
            pltpu.SemaphoreType.DMA((20,)),
            pltpu.SemaphoreType.DMA((23,)),
        ],
        compiler_params=pltpu.CompilerParams(vmem_limit_bytes=VMEM_LIMIT),
        cost_estimate=pl.CostEstimate(
            flops=8 * rows * width * HIDDEN,
            bytes_accessed=25 * 1024 * 1024,
            transcendentals=rows * HIDDEN,
        ),
    )(core, *pieces, dact, weights)
    return result[0], result[1], result[2], result[3:]


def weight_grads_kernel(core_ref, x_ref, x2_ref, dy_ref, dy2_ref, right_ref, right2_ref, out_ref, dy, dy2, sems):
    part = pl.program_id(0)
    half = dy.shape[1]
    start = pl.multiple_of(core_of(core_ref) * half, half)
    loads = (
        pltpu.make_async_copy(dy_ref.at[:, pl.ds(start, half)], dy, sems.at[0]),
        pltpu.make_async_copy(dy2_ref, dy2, sems.at[1]),
    )

    @pl.when(part == 0)
    def _():
        for load in loads:
            load.start()

    @pl.when(part < 2)
    def _():
        total = dot_tn(x_ref[...], right_ref[...]) + dot_tn(x2_ref[...], right2_ref[...])
        out_ref[...] = total.astype(BF16)

    @pl.when(part == 2)
    def _():
        for load in loads:
            load.wait()
        total = dot_tn(dy[...], right_ref[...]) + dot_tn(dy2[...], right2_ref[...])
        out_ref[...] = total.astype(BF16)


def weight_grads(core, x, x2, dy, dy2, right, right2):
    rows, half = x2.shape
    anywhere = pl.BlockSpec(memory_space=pl.ANY)
    side = lambda j, c: (0, j)
    grid = pltpu.PrefetchScalarGridSpec(
        num_scalar_prefetch=1,
        grid=(3,),
        in_specs=[
            pl.BlockSpec((rows, half), lambda j, c: (0, core_of(c))),
            pl.BlockSpec((rows, half), lambda j, c: (0, 0)),
            anywhere,
            anywhere,
            pl.BlockSpec((rows, HIDDEN), side),
            pl.BlockSpec((rows, HIDDEN), side),
        ],
        out_specs=pl.BlockSpec((half, HIDDEN), side),
        scratch_shapes=[
            pltpu.VMEM((rows, half), BF16),
            pltpu.VMEM((rows, half), BF16),
            pltpu.SemaphoreType.DMA((2,)),
        ],
    )
    return pl.pallas_call(
        weight_grads_kernel,
        grid_spec=grid,
        out_shape=jax.ShapeDtypeStruct((half, 3 * HIDDEN), BF16),
        compiler_params=pltpu.CompilerParams(vmem_limit_bytes=VMEM_LIMIT),
        cost_estimate=pl.CostEstimate(
            flops=2 * 3 * 2 * rows * half * HIDDEN, bytes_accessed=24 * 1024 * 1024, transcendentals=0
        ),
    )(core, x, x2, dy, dy2, right, right2)


def rows_times_kernel(left_ref, right_ref, *out_refs):
    result = dot_nt(left_ref[...], right_ref[...]).astype(BF16)
    for number, ref in enumerate(out_refs):
        ref[...] = result[128 * number : 128 * number + 128]


def rows_times(left, left_part, right, part):
    rows, depth = left.shape[0], HIDDEN
    width = right.shape[0]
    tile = 512
    return pl.pallas_call(
        rows_times_kernel,
        out_shape=(jax.ShapeDtypeStruct((128, width), BF16),) * 4,
        grid=(width // tile,),
        in_specs=[
            pl.BlockSpec((rows, depth), lambda i: (0, left_part)),
            pl.BlockSpec((tile, depth), lambda i: (i, part)),
        ],
        out_specs=(pl.BlockSpec((128, tile), lambda i: (0, i)),) * 4,
        compiler_params=pltpu.CompilerParams(vmem_limit_bytes=VMEM_LIMIT),
        cost_estimate=pl.CostEstimate(
            flops=2 * rows * depth * width,
            bytes_accessed=2 * (rows * depth + width * depth + rows * width),
            transcendentals=0,
        ),
    )(left, right)


def ring_rows(own, near, far):
    return jnp.concatenate([own, near[:128], far, near[128:]], 0)


def put_half(number, value, other_ref, own_ref):
    @pl.when(number < 2)
    def _():
        other_ref[...] = value

    @pl.when(number >= 2)
    def _():
        own_ref[...] = value


def tile_at(i, c):
    return lax.rem(i + 2 * (1 - core_of(c)), 4)


def half_specs(tile, columns):
    return (
        pl.BlockSpec((tile, columns), lambda i, c: (jnp.minimum(i, 1), 0)),
        pl.BlockSpec((tile, columns), lambda i, c: (jnp.maximum(i - 2, 0), 0)),
    )


def wide_grads_kernel(
    core_ref, x_ref, dh0, dh1, dh2, dh3, o0, o1, o2, dq0, dq1, dq2, other_ref, own_ref, o_held, dq_held
):
    number = pl.program_id(0)

    @pl.when(number == 0)
    def _():
        o_held[...] = ring_rows(o0[...], o1[...], o2[...])
        dq_held[...] = ring_rows(dq0[...], dq1[...], dq2[...])

    dh = jnp.concatenate([ref[...] for ref in (dh0, dh1, dh2, dh3)], 0)
    out = dot_tn(dh, o_held[...])
    query = dot_tn(x_ref[...], dq_held[...])
    put_half(number, jnp.concatenate([out, query], 1).astype(BF16), other_ref, own_ref)


def wide_grads(core, normed, dh, o, dq):
    rows, width = normed.shape
    tile = 512
    whole = lambda i, c: (0, 0)
    column = lambda i, c: (0, tile_at(i, c))
    small = [pl.BlockSpec((size, 512), whole) for size in (128, 256, 128)]
    grid = pltpu.PrefetchScalarGridSpec(
        num_scalar_prefetch=1,
        grid=(4,),
        in_specs=[pl.BlockSpec((rows, tile), column)]
        + [pl.BlockSpec((128, tile), column)] * 4
        + small
        + small,
        out_specs=half_specs(tile, 1024),
        scratch_shapes=[pltpu.VMEM((rows, 512), BF16), pltpu.VMEM((rows, 512), BF16)],
    )
    return pl.pallas_call(
        wide_grads_kernel,
        grid_spec=grid,
        out_shape=(jax.ShapeDtypeStruct((width // 2, 1024), BF16),) * 2,
        compiler_params=pltpu.CompilerParams(vmem_limit_bytes=VMEM_LIMIT),
        cost_estimate=pl.CostEstimate(
            flops=2 * rows * width * 1024, bytes_accessed=10 * 1024 * 1024, transcendentals=0
        ),
    )(core, normed, *dh, *o, *dq)


def finish_kernel(
    core_ref,
    x_ref,
    w_ref,
    dq0_ref,
    dq1_ref,
    dq2_ref,
    own_ref,
    one_ref,
    two_ref,
    cos_ref,
    sin_ref,
    norm_ref,
    second_ref,
    other_grad_ref,
    own_grad_ref,
    dx_ref,
    gain_ref,
    dqkv,
    sums,
):
    number = pl.program_id(0)

    @pl.when(number == 0)
    def _():
        dqkv[:, :512] = ring_rows(dq0_ref[...], dq1_ref[...], dq2_ref[...])
        dkv = own_ref[...] + one_ref[...].astype(F32) + two_ref[...].astype(F32)
        turned = turn(dkv, cos_ref[...], -sin_ref[...])
        dqkv[:, 512:] = jnp.where(lane_is_low(dkv.shape, 128), turned, dkv).astype(BF16)

    x = x_ref[...]
    put_half(number, dot_tn(x, dqkv[:, 512:]).astype(BF16), other_grad_ref, own_grad_ref)
    dx = dot_nt(dqkv[...], w_ref[...])
    for piece in range(4):
        row = pl.multiple_of(lax.rem(place_of(core_ref) + piece, 4) * 128, 128)
        dx_ref[pl.ds(row, 128), :] = dx[128 * piece : 128 * piece + 128].astype(BF16)
    columns = pl.ds(pl.multiple_of(tile_at(number, core_ref) * 512, 512), 512)
    sums[:, columns] = jnp.broadcast_to(
        jnp.sum(dx * x.astype(F32), 0, keepdims=True) / norm_ref[:1], (8, 512)
    )

    @pl.when(number == 3)
    def _():
        gain_ref[:8] = gain_rows(to_blocks(sums[...])[:1])
        gain_ref[8:] = gain_rows(second_ref[:1])


def finish(core, normed, weights, dq, own, one, two, cosine, sine, gain, second):
    rows, width = normed.shape
    tile = 512
    whole = lambda i, c: (0, 0)
    column = lambda i, c: (0, tile_at(i, c))
    narrow = pl.BlockSpec((rows, 128), whole)
    grid = pltpu.PrefetchScalarGridSpec(
        num_scalar_prefetch=1,
        grid=(4,),
        in_specs=[
            pl.BlockSpec((rows, tile), column),
            pl.BlockSpec((tile, 640), lambda i, c: (tile_at(i, c), 0)),
            pl.BlockSpec((128, 512), whole),
            pl.BlockSpec((256, 512), whole),
            pl.BlockSpec((128, 512), whole),
            narrow,
            narrow,
            narrow,
            narrow,
            narrow,
            pl.BlockSpec((2, tile), column),
            pl.BlockSpec((8, width), whole),
        ],
        out_specs=half_specs(tile, 128)
        + (pl.BlockSpec((rows, tile), column),)
        + (pl.BlockSpec((GAIN_ROWS, GAIN_COLUMNS), whole),),
        scratch_shapes=[pltpu.VMEM((rows, 640), BF16), pltpu.VMEM((8, width), F32)],
    )
    result = pl.pallas_call(
        finish_kernel,
        grid_spec=grid,
        out_shape=(jax.ShapeDtypeStruct((width // 2, 128), BF16),) * 2
        + (jax.ShapeDtypeStruct((rows, width), BF16),)
        + (jax.ShapeDtypeStruct((GAIN_ROWS, GAIN_COLUMNS), F32),),
        compiler_params=pltpu.CompilerParams(vmem_limit_bytes=VMEM_LIMIT),
        cost_estimate=pl.CostEstimate(
            flops=2 * rows * width * 768, bytes_accessed=10 * 1024 * 1024, transcendentals=0
        ),
    )(core, normed, weights, *dq, own, one, two, cosine, sine, gain, second)
    return result


def per_device(
    tokens,
    segments,
    w_query,
    key_projection,
    value_projection,
    w_out,
    w_gate,
    w_up,
    w_down,
    norm_attn,
    norm_ffn,
    cotangent,
):
    place, core = lax.axis_index("head"), lax.axis_index("core")
    block = (lax.axis_index("y") * 4 + lax.axis_index("x")) * 2 + core
    code = (((lax.axis_index("x") * 4 + lax.axis_index("y")) * 2 + core) * 4 + place).astype(jnp.int32)
    code = code.reshape(1)
    keep = lax.optimization_barrier


    out_weights = lax.all_gather(
        jnp.concatenate([w_down.T, w_out.T], 1), CORE_FIRST, axis=0, tiled=True
    )
    ffn_weights = lax.all_gather(jnp.concatenate([w_gate, w_up], 1), CORE_FIRST, axis=0, tiled=True)

    x_rows, dy_rows, normed_rows, gains = prepare(
        tokens[0], cotangent[0], jnp.stack([norm_attn, norm_ffn]).astype(F32)
    )
    row = jnp.arange(512, dtype=jnp.int32)
    positions = block * 512 + ((row // 128 + place) % 4) * 128 + row % 128
    frequency = 10000.0 ** (-jnp.arange(32, dtype=F32) * 2.0 / HEAD_SIZE)
    angles = positions.astype(F32)[:, None] * frequency[None, :]
    cosine, sine = jnp.cos(angles), jnp.sin(angles)
    cosine = jnp.concatenate([cosine] * 4, 1)
    sine = jnp.concatenate([-sine, sine, -sine, sine], 1)

    flat = segments.reshape(-1)
    padded = jnp.concatenate([jnp.full((1024,), -1, jnp.int32), flat])
    own = lax.dynamic_slice_in_dim(flat, block * 512, 512, 0)
    window = lax.dynamic_slice_in_dim(padded, block * 512, 1536, 0)
    start = jnp.sum((window[None, :] < own[:, None]).astype(jnp.int32), 1)
    low = jnp.maximum(start, row + 1).reshape(1, 512)

    normed_rows, w_query = keep((normed_rows, w_query))
    ahead, behind = near_pieces(normed_rows)
    qkv_own = gather_axis(jnp.concatenate([w_query, key_projection, value_projection], 1), "x")
    qkv_own = gather_axis(jnp.concatenate(qkv_own, 0), "y")
    far = far_pieces(ahead, behind)
    qkv_own, far, cosine, sine, low = keep((qkv_own, far, cosine, sine, low))
    qkv_pieces = *qkv_own, *(shift(piece, "core", 1) for piece in qkv_own)
    kv_own, normed_one = project_kv(code, (normed_rows, ahead, *far, behind), qkv_pieces, cosine, sine)
    normed_late, kv_own, dy_raw = keep((normed_one, kv_own, cotangent[0]))
    dy_pieces = gather_pieces(dy_raw)
    kv = (from_block(kv_own, 2), from_block(kv_own, 1), kv_own)
    queries, qkv_weights = project_q(code, normed_late, qkv_pieces, cosine, sine)

    kk, vv, kvt = set_up(code, kv)
    seen = code, queries, kk, kvt, low, out_weights
    o_far, lse_far, part_far = attend(2, 1, 1, *seen)
    queries, part_far, dy_pieces = keep((queries, part_far, dy_pieces))
    part_far = shift(part_far, "head", 2)
    seen = code, queries, kk, kvt, low, out_weights
    o_near, lse_near, part_ahead, part_behind = attend(1, 2, 2, *seen)
    queries, part_far, part_ahead, part_behind = keep((queries, part_far, part_ahead, part_behind))
    seen = code, queries, kk, kvt, low, out_weights
    o_own, lse_own, part_own = attend(0, 1, 1, *seen)
    dy, dy_swap = assemble(code, dy_rows, *dy_pieces)
    dy_other = shift(dy_swap, "core", 1)
    attention_sum = part_own, shift(part_ahead, "head", 1), shift(part_behind, "head", -1), part_far
    h1, top, bottom = join(x_rows, gains, attention_sum)
    behind_top, ahead_bottom = shift(top, "head", 1), shift(bottom, "head", -1)
    ahead_top, behind_bottom = shift(top, "head", -1), shift(bottom, "head", 1)
    behind_top, ahead_bottom, dy = keep((behind_top, ahead_bottom, dy))
    far_top, far_bottom = shift(behind_top, "head", 1), shift(ahead_bottom, "head", -1)
    rows_two = top, bottom, ahead_top, ahead_bottom, far_top, far_bottom, behind_top, behind_bottom
    dact = columns_times(dy, out_weights)
    dact, dy_other = keep((dact, dy_other))

    gua, normed_two, normed_two_swap, dnormed_two = ffn(
        code, rows_two, dact, ffn_weights
    )
    dnormed_two = scatter_pieces(*dnormed_two)
    gua_other = shift(gua, "core", 1)
    normed_two_other = shift(normed_two_swap, "core", 1)
    out_pieces = rows_times(gua, 2, out_weights, 0)
    gua_other, normed_two_other, out_pieces = keep((gua_other, normed_two_other, out_pieces))
    held = weight_grads(code, normed_two, normed_two_other, dy, dy_other, gua, gua_other)
    held, dnormed_two = keep((held, dnormed_two))
    grads = lax.psum_scatter(held, ("y", "x"), scatter_dimension=0, tiled=True)

    dh1, dh1_low, grad_gain_two = join_back(h1, dy_rows, gains, dnormed_two)
    back = kk, vv, kvt, low, cosine, sine
    dq_own, dk, dv = attend_back(0, 1, 1, code, queries, o_own, (dh1_low,), out_weights, lse_own, *back, ())
    ahead, behind = shift(dh1_low, "head", -1), shift(dh1_low, "head", 1)
    ahead, behind, dk, dv, dh1_late, out_pieces = keep((ahead, behind, dk, dv, dh1_low, out_pieces))
    far = shift(dh1_late, "head", 2)
    dq_near, dk, dv = attend_back(
        1, 2, 2, code, queries, o_near, (ahead, behind), out_weights, lse_near, *back, (dk, dv)
    )
    far, dk, dv, out_pieces = keep((far, dk, dv, out_pieces))
    out_pieces = scatter_pieces(*out_pieces)
    dq_far, dkv_first, dkv_second, dkv_own = attend_back(
        2, 1, 1, code, queries, o_far, (far,), out_weights, lse_far, *back, (dk, dv)
    )
    dq = dq_own, dq_near, dq_far
    dkv_one = from_block(dkv_second, -1)
    dkv_two = from_block(dkv_first, -2)
    wide_other, wide_own = wide_grads(
        code, normed_one, (dh1_low, ahead, far, behind), (o_own, o_near, o_far), dq
    )
    dkv_one, dkv_two, wide_other, out_pieces = keep((dkv_one, dkv_two, wide_other, out_pieces))
    wide_other = shift(wide_other, "core", 1)

    narrow_other, narrow_own, dnormed_one, gain_grads = finish(
        code,
        normed_one,
        qkv_weights,
        dq,
        dkv_own,
        dkv_one,
        dkv_two,
        cosine,
        sine,
        gains,
        grad_gain_two,
    )
    dnormed_one = lax.psum_scatter(dnormed_one, "head", scatter_dimension=0, tiled=True)
    gain_grads = jnp.concatenate([gain_grads, shift(gain_grads, "core", 1)], 0)
    gain_grads = exchange([gain_grads] * 4, "head")
    rows = [(x_rows.shape, BF16)]
    (output,) = small_call(output_kernel, rows, h1, *out_pieces)
    gain_grads, output = keep((gain_grads, output))
    pieces, out_sums = first_pieces(
        code, wide_own, wide_other, narrow_own, shift(narrow_other, "core", 1), gain_grads
    )
    grads = (
        grads[:, :HIDDEN].astype(F32),
        grads[:, HIDDEN : 2 * HIDDEN].astype(F32),
        grads[:, 2 * HIDDEN :].T.astype(F32),
    )
    pieces, grads = keep((exchange(pieces, "x"), grads))
    pieces = second_pieces(second_qkv_kernel, (64 + GAIN_ROWS, 640), F32, code, pieces)
    out_sums, pieces = keep((exchange(out_sums, "y"), pieces))
    out_sums = second_pieces(second_out_kernel, (64, 512), BF16, code, out_sums)
    (grad_inputs,) = small_call(input_grad_kernel, rows, dh1, x_rows, gains, dnormed_one)
    pieces, out_sums, grad_inputs = keep((exchange(pieces, "y"), exchange(out_sums, "x"), grad_inputs))
    columns = (64, 512), (64, 512), (64, 64), (64, 64), (1, 2048), (1, 2048)
    grad_out, grad_query, grad_key, grad_value, grad_gain_one, grad_gain_two = small_call(
        attention_grads_kernel,
        [(shape, F32) for shape in columns],
        *pieces,
        *out_sums,
    )

    return (
        output[None],
        grad_inputs[None],
        grad_query,
        grad_key,
        grad_value,
        grad_out.T,
        *grads,
        grad_gain_one.reshape(2048),
        grad_gain_two.reshape(2048),
    )


def solution(mesh):
    grid = Mesh(mesh.devices.reshape(4, 4, 4, 2), ("head", "y", "x", "core"))
    rows, up, down = P(BLK, "head", None), P(BLK, "head"), P("head", BLK)
    return jax.shard_map(
        per_device,
        mesh=grid,
        in_specs=(rows, P(), up, up, up, down, up, up, down, P(), P(), rows),
        out_specs=(rows, rows, up, up, up, down, up, up, down, P(), P()),
        check_vma=False,
    )
```

```python
import functools

import jax
import jax.numpy as jnp
from jax import lax
from jax.experimental import pallas as pl
from jax.experimental.pallas import tpu as pltpu
from jax.sharding import Mesh
from jax.sharding import PartitionSpec as P

HEAD_SIZE = 64
WINDOW = 1024
HIDDEN = 1408
EPSILON = 1e-05
BF16 = jnp.bfloat16
F32 = jnp.float32
BLK = ("y", "x", "core")
CORE_FIRST = ("core", "y", "x")
VMEM_LIMIT = 63 * 1024 * 1024


def dot_nn(a, b):
    return jnp.dot(a, b, preferred_element_type=F32)


def dot_nt(a, b):
    return lax.dot_general(a, b, (((1,), (1,)), ((), ())), preferred_element_type=F32)


def dot_tn(a, b):
    return lax.dot_general(a, b, (((0,), (0,)), ((), ())), preferred_element_type=F32)


def shift(value, axis, distance):
    size = lax.axis_size(axis)
    return lax.ppermute(value, axis, [(i, (i + distance) % size) for i in range(size)])


def add_low(a, b):
    return (a.astype(F32) + b.astype(F32)).astype(BF16)


def gather_pieces(rows):
    return shift(rows, "head", -1), shift(rows, "head", 2), shift(rows, "head", 1)


def near_pieces(rows):
    return shift(rows, "head", -1), shift(rows, "head", 1)


def far_pieces(ahead, behind):
    half = ahead.shape[0] // 2
    return shift(behind[:half], "head", 1), shift(ahead[half:], "head", -1)


def scatter_pieces(own, ahead, far, behind):
    return own, shift(ahead, "head", 1), shift(behind, "head", -1), shift(far, "head", 2)


def gather_axis(value, axis):
    return value, shift(value, axis, -1), shift(value, axis, 2), shift(value, axis, 1)


def exchange(pieces, axis):
    return pieces[0], shift(pieces[1], axis, 1), shift(pieces[2], axis, 2), shift(pieces[3], axis, -1)


def from_block(value, distance):
    route = [(i, i + distance) for i in range(32) if 0 <= i + distance < 32]
    return lax.ppermute(value, BLK, route)


def scale_of(values):
    return lax.rsqrt(jnp.mean(values * values, -1, keepdims=True) + EPSILON)


def x_of(code):
    return lax.shift_right_logical(code[0], 5)


def y_of(code):
    return lax.shift_right_logical(code[0], 3) & 3


def core_of(code):
    return lax.shift_right_logical(code[0], 2) & 1


def place_of(code):
    return code[0] & 3


def lane_is_low(shape, period):
    return lax.broadcasted_iota(jnp.int32, shape, len(shape) - 1) % period < period // 2


def turn(values, cosine, sine):
    swapped = jnp.where(
        lane_is_low(values.shape, 64), pltpu.roll(values, 96, 1), pltpu.roll(values, 32, 1)
    )
    return values * cosine + swapped * sine


def core_major_tiles(tiles):
    low = lane_is_low(tiles[0].shape, 128)
    rolled = [pltpu.roll(tile, 64, 1) for tile in tiles]
    first = [jnp.where(low, tiles[2 * k], rolled[2 * k + 1]) for k in range(8)]
    second = [jnp.where(low, rolled[2 * k], tiles[2 * k + 1]) for k in range(8)]
    return first + second


def block_major_tiles(tiles):
    low = lane_is_low(tiles[0].shape, 128)
    rolled = [pltpu.roll(tile, 64, 1) for tile in tiles]
    result = []
    for k in range(8):
        result.append(jnp.where(low, tiles[k], rolled[8 + k]))
        result.append(jnp.where(low, rolled[k], tiles[8 + k]))
    return result


def in_tiles(value):
    return [value[:, 128 * k : 128 * k + 128] for k in range(16)]


def prepare_kernel(x_ref, dy_ref, gain_ref, x_out, dy_out, normed_out, gain_out):
    def convert(ref):
        return jnp.concatenate(core_major_tiles(in_tiles(ref[...].astype(F32))), 1)

    x, gains = convert(x_ref), convert(gain_ref)
    gain_out[...] = gains
    x_out[...] = x
    dy_out[...] = convert(dy_ref).astype(BF16)
    normed_out[...] = (x * scale_of(x) * gains[:1]).astype(BF16)


def prepare(x, dy, gains):
    rows, width = x.shape
    return pl.pallas_call(
        prepare_kernel,
        out_shape=(
            jax.ShapeDtypeStruct((rows, width), F32),
            jax.ShapeDtypeStruct((rows, width), BF16),
            jax.ShapeDtypeStruct((rows, width), BF16),
            jax.ShapeDtypeStruct(gains.shape, F32),
        ),
        compiler_params=pltpu.CompilerParams(vmem_limit_bytes=VMEM_LIMIT),
        cost_estimate=pl.CostEstimate(
            flops=10 * rows * width, bytes_accessed=10 * rows * width, transcendentals=rows
        ),
    )(x, dy, gains)


def to_blocks(value):
    return jnp.concatenate(block_major_tiles(in_tiles(value)), 1)


def assemble_kernel(core_ref, own_ref, ahead_ref, far_ref, behind_ref, out_ref, swap_ref):
    out_ref[:128] = own_ref[...]
    start = 128
    for ref in (ahead_ref, far_ref, behind_ref):
        size = ref.shape[0]
        out_ref[start : start + size] = jnp.concatenate(
            core_major_tiles(in_tiles(ref[...].astype(F32))), 1
        ).astype(BF16)
        start += size
    swap_ref[...] = jnp.where(core_of(core_ref) == 0, out_ref[:, 1024:], out_ref[:, :1024])


def assemble(core, own, ahead, far, behind):
    vmem = pl.BlockSpec(memory_space=pltpu.VMEM)
    return pl.pallas_call(
        assemble_kernel,
        out_shape=(jax.ShapeDtypeStruct((512, 2048), BF16), jax.ShapeDtypeStruct((512, 1024), BF16)),
        in_specs=[pl.BlockSpec(memory_space=pltpu.SMEM)] + [vmem] * 4,
        out_specs=(vmem, vmem),
        compiler_params=pltpu.CompilerParams(vmem_limit_bytes=VMEM_LIMIT),
        cost_estimate=pl.CostEstimate(
            flops=4 * 512 * 2048, bytes_accessed=5 * 1024 * 1024, transcendentals=0
        ),
    )(core, own, ahead, far, behind)


def small_call(kernel, out_shape, *operands):
    return pl.pallas_call(
        kernel,
        out_shape=tuple(jax.ShapeDtypeStruct(shape, dtype) for shape, dtype in out_shape),
        compiler_params=pltpu.CompilerParams(vmem_limit_bytes=VMEM_LIMIT),
        cost_estimate=pl.CostEstimate(
            flops=sum(x.size for x in operands),
            bytes_accessed=2 * sum(x.size * x.dtype.itemsize for x in operands),
            transcendentals=0,
        ),
    )(*operands)


def total_of(refs):
    values = [ref[...].astype(F32) for ref in refs]
    while len(values) > 1:
        values = [values[0] + values[1]] + values[2:]
    return values[0]


def join_kernel(x_ref, gain_ref, a_ref, b_ref, c_ref, d_ref, h_out, top_out, bottom_out):
    h = x_ref[...] + total_of((a_ref, b_ref, c_ref, d_ref))
    h_out[...] = h
    normed = (h * scale_of(h) * gain_ref[1:2]).astype(BF16)
    half = h.shape[0] // 2
    top_out[...], bottom_out[...] = normed[:half], normed[half:]


def join(x, gain, pieces):
    half = x.shape[0] // 2, x.shape[1]
    return small_call(join_kernel, ((x.shape, F32), (half, BF16), (half, BF16)), x, gain, *pieces)


def norm_backward(values, gain, grad):
    scale = scale_of(values)
    weighted = grad * gain
    inner = jnp.mean(weighted * values, -1, keepdims=True)
    return scale * weighted - values * (scale * scale * scale * inner), scale


def join_back_kernel(h_ref, dy_ref, gain_ref, a_ref, b_ref, c_ref, d_ref, dh_out, low_out, grad_out):
    h, grad = h_ref[...], total_of((a_ref, b_ref, c_ref, d_ref))
    back, scale = norm_backward(h, gain_ref[1:2], grad)
    dh = dy_ref[...].astype(F32) + back
    dh_out[...] = dh
    low_out[...] = dh.astype(BF16)
    grad_out[...] = to_blocks(jnp.broadcast_to(jnp.sum(grad * h * scale, 0, keepdims=True), (8, h.shape[1])))


def join_back(h, dy, gain, pieces):
    shapes = (h.shape, F32), (h.shape, BF16), ((8, h.shape[1]), F32)
    return small_call(join_back_kernel, shapes, h, dy, gain, *pieces)


def output_kernel(h_ref, a_ref, b_ref, c_ref, d_ref, out_ref):
    out_ref[...] = to_blocks(h_ref[...] + total_of((a_ref, b_ref, c_ref, d_ref))).astype(BF16)


def input_grad_kernel(dh_ref, x_ref, gain_ref, grad_ref, out_ref):
    back, _ = norm_backward(x_ref[...], gain_ref[:1], grad_ref[...].astype(F32))
    out_ref[...] = to_blocks(dh_ref[...] + back).astype(BF16)


GAIN_ROWS, GAIN_COLUMNS = 16, 256


def gain_rows(vector):
    return jnp.concatenate([vector[:, 256 * k : 256 * k + 256] for k in range(8)], 0)


def put_piece(ref, rows, gains):
    count = rows.shape[0]
    ref[:count] = rows
    ref[count:, GAIN_COLUMNS:] = jnp.zeros((GAIN_ROWS, ref.shape[1] - GAIN_COLUMNS), BF16)
    ref[count:, :GAIN_COLUMNS] = gains.astype(BF16)


def first_pieces_kernel(
    at_ref, q_ref, q2_ref, kv_ref, kv2_ref, o_ref, o2_ref, *refs
):
    gain_refs, out_refs = refs[:4], refs[4:]
    query = add_low(q_ref[...], q2_ref[...]).reshape(256, 512)
    narrow = add_low(kv_ref[...], kv2_ref[...]).reshape(256, 128)
    rows = jnp.concatenate([query, narrow], 1)
    out_rows = add_low(o_ref[...], o2_ref[...]).reshape(256, 512)
    gains = total_of(gain_refs)
    for number in range(4):

        @pl.when(pl.program_id(0) == number)
        def _():
            put_piece(out_refs[number], rows, gains)
            out_refs[4 + number][...] = out_rows


def first_pieces(at, wide, wide2, narrow, narrow2, gains):
    pick_x = lambda column: lambda d, s: (0, lax.rem(x_of(s) + d, 4), 0, column)
    pick_y = lambda d, s: (lax.rem(y_of(s) + d, 4), 0, 0, 0)
    whole = lambda d, s: (0, 0)
    shaped = lambda value: value.reshape(4, 4, 64, value.shape[1])
    shapes = [(256 + GAIN_ROWS, 640)] * 4 + [(256, 512)] * 4
    grid = pltpu.PrefetchScalarGridSpec(
        num_scalar_prefetch=1,
        grid=(4,),
        in_specs=[pl.BlockSpec((4, 1, 64, 512), pick_x(1))] * 2
        + [pl.BlockSpec((4, 1, 64, 128), pick_x(0))] * 2
        + [pl.BlockSpec((1, 4, 64, 512), pick_y)] * 2
        + [pl.BlockSpec((GAIN_ROWS, GAIN_COLUMNS), whole)] * 4,
        out_specs=tuple(pl.BlockSpec(shape, whole) for shape in shapes),
    )
    wide, wide2 = shaped(wide), shaped(wide2)
    result = pl.pallas_call(
        first_pieces_kernel,
        grid_spec=grid,
        out_shape=tuple(jax.ShapeDtypeStruct(shape, BF16) for shape in shapes),
        compiler_params=pltpu.CompilerParams(vmem_limit_bytes=VMEM_LIMIT),
        cost_estimate=pl.CostEstimate(
            flops=2 * 1024 * 1152, bytes_accessed=6 * 1024 * 1152, transcendentals=0
        ),
    )(at, wide, wide2, shaped(narrow), shaped(narrow2), wide, wide2, *gains)
    return result[:4], result[4:]


def second_pieces_kernel(at_ref, *refs):
    qkv, out, (held, out_held) = refs[:4], refs[4:8], refs[16:]
    held[...] = total_of(qkv)
    out_held[...] = total_of(out).astype(BF16)
    for number in range(4):
        y = pl.multiple_of(lax.rem(y_of(at_ref) + number, 4) * 64, 64)
        put_piece(refs[8 + number], held[pl.ds(y, 64), :].astype(BF16), held[256:, :GAIN_COLUMNS])
        x = pl.multiple_of(lax.rem(x_of(at_ref) + number, 4) * 64, 64)
        refs[12 + number][...] = out_held[pl.ds(x, 64), :]


def second_pieces(at, qkv, out):
    vmem = pl.BlockSpec(memory_space=pltpu.VMEM)
    shapes = [(64 + GAIN_ROWS, 640)] * 4 + [(64, 512)] * 4
    result = pl.pallas_call(
        second_pieces_kernel,
        out_shape=tuple(jax.ShapeDtypeStruct(shape, BF16) for shape in shapes),
        in_specs=[pl.BlockSpec(memory_space=pltpu.SMEM)] + [vmem] * 8,
        out_specs=(vmem,) * 8,
        scratch_shapes=[pltpu.VMEM((256 + GAIN_ROWS, 640), F32), pltpu.VMEM((256, 512), BF16)],
        compiler_params=pltpu.CompilerParams(vmem_limit_bytes=VMEM_LIMIT),
        cost_estimate=pl.CostEstimate(
            flops=4 * 272 * 1152, bytes_accessed=10 * 272 * 1152, transcendentals=0
        ),
    )(at, *qkv, *out)
    return result[:4], result[4:]


def gains_kernel(a_ref, b_ref, c_ref, d_ref, out_ref):
    values = [ref[64:, :GAIN_COLUMNS].astype(F32) for ref in (a_ref, b_ref, c_ref, d_ref)]
    out_ref[...] = (values[0] + values[1]) + (values[2] + values[3])


def attention_grads_kernel(*refs):
    out_ref, q_ref, k_ref, v_ref, one_ref, two_ref = refs[10:]
    total = total_of(refs[:4])
    out_ref[...] = total_of(refs[4:8])
    q_ref[...] = total[:64, :512]
    k_ref[...] = total[:64, 512:576]
    v_ref[...] = total[:64, 576:]
    gains = total_of(refs[8:10])
    one_ref[...] = jnp.concatenate([gains[k : k + 1] for k in range(8)], 1)
    two_ref[...] = jnp.concatenate([gains[k : k + 1] for k in range(8, 16)], 1)


def put_in_order(at_ref, piece_refs, columns, to_ref, sems):
    x, y, core = x_of(at_ref), y_of(at_ref), core_of(at_ref)
    copies = []
    for number in range(32):
        to_x, to_y = lax.rem(x + number % 4, 4), lax.rem(y + number // 4 % 4, 4)
        to_core = core if number < 16 else 1 - core
        row = pl.multiple_of(((to_core * 4 + to_y) * 4 + to_x) * 64, 64)
        copy = pltpu.make_async_copy(
            piece_refs[number // 4].at[pl.ds(number % 4 * 64, 64), columns],
            to_ref.at[pl.ds(row, 64)],
            sems.at[number],
        )
        copy.start()
        copies.append(copy)
    return copies


RING_PIECES = [(0, 128), (128, 128), (256, 64), (320, 64), (384, 128)]


def project_kv_kernel(at_ref, *refs):
    x_refs, piece_refs, (cos_ref, sin_ref, kv_ref, whole_ref) = refs[:5], refs[5:13], refs[13:17]
    x_held, held, sems, x_sems = refs[17:]
    copies = []
    for number, (start, size) in enumerate(RING_PIECES):
        copy = pltpu.make_async_copy(x_refs[number], x_held.at[pl.ds(start, size)], x_sems.at[number])
        copy.start()
        copies.append(copy)
    copies += put_in_order(at_ref, piece_refs, pl.ds(512, 128), held, sems)
    for copy in copies:
        copy.wait()
    whole = pltpu.make_async_copy(x_held, whole_ref, x_sems.at[len(RING_PIECES)])
    whole.start()
    flat = dot_nn(x_held[...], held[...])
    turned = turn(flat, cos_ref[...], sin_ref[...])
    kv_ref[...] = jnp.where(lane_is_low(flat.shape, 128), turned, flat).astype(BF16)
    whole.wait()


def project_kv(at, x_pieces, weights, cosine, sine):
    rows, width = 512, x_pieces[0].shape[1]
    vmem, anywhere = pl.BlockSpec(memory_space=pltpu.VMEM), pl.BlockSpec(memory_space=pl.ANY)
    return pl.pallas_call(
        project_kv_kernel,
        out_shape=(jax.ShapeDtypeStruct((rows, 128), BF16), jax.ShapeDtypeStruct((rows, width), BF16)),
        in_specs=[pl.BlockSpec(memory_space=pltpu.SMEM)] + [anywhere] * 13 + [vmem, vmem],
        out_specs=(vmem, anywhere),
        scratch_shapes=[
            pltpu.VMEM((rows, width), BF16),
            pltpu.VMEM((width, 128), BF16),
            pltpu.SemaphoreType.DMA((32,)),
            pltpu.SemaphoreType.DMA((len(RING_PIECES) + 1,)),
        ],
        compiler_params=pltpu.CompilerParams(vmem_limit_bytes=VMEM_LIMIT),
        cost_estimate=pl.CostEstimate(
            flops=2 * rows * width * 128, bytes_accessed=5 * 1024 * 1024, transcendentals=0
        ),
    )(at, *x_pieces, *weights, cosine, sine)


def project_q_kernel(at_ref, x_ref, *refs):
    piece_refs, (cos_ref, sin_ref, q_ref, w_ref, held, sems, sem) = refs[:8], refs[8:]
    for copy in put_in_order(at_ref, piece_refs, pl.ds(0, 640), held, sems):
        copy.wait()
    whole = pltpu.make_async_copy(held, w_ref, sem)
    whole.start()
    cosine, sine, x = cos_ref[...], sin_ref[...], x_ref[...]
    for start in (0, 256):
        wide = dot_nn(x, held[:, start : start + 256])
        for part in (0, 128):
            turned = turn(wide[:, part : part + 128], cosine, sine)
            q_ref[:, start + part : start + part + 128] = (turned * HEAD_SIZE**-0.5).astype(BF16)
    whole.wait()


def project_q(at, normed, weights, cosine, sine):
    rows, width = normed.shape
    vmem, anywhere = pl.BlockSpec(memory_space=pltpu.VMEM), pl.BlockSpec(memory_space=pl.ANY)
    return pl.pallas_call(
        project_q_kernel,
        out_shape=(jax.ShapeDtypeStruct((rows, 512), BF16), jax.ShapeDtypeStruct((width, 640), BF16)),
        in_specs=[pl.BlockSpec(memory_space=pltpu.SMEM), vmem] + [anywhere] * 8 + [vmem, vmem],
        out_specs=(vmem, anywhere),
        scratch_shapes=[
            pltpu.VMEM((width, 640), BF16),
            pltpu.SemaphoreType.DMA((32,)),
            pltpu.SemaphoreType.DMA,
        ],
        compiler_params=pltpu.CompilerParams(vmem_limit_bytes=VMEM_LIMIT),
        cost_estimate=pl.CostEstimate(
            flops=2 * rows * width * 512, bytes_accessed=7 * 1024 * 1024, transcendentals=0
        ),
    )(at, normed, *weights, cosine, sine)


KEYS = 1152
PAIRS = 4


def set_up_kernel(place_ref, kv0_ref, kv1_ref, kv2_ref, kk_ref, vv_ref, kvt_ref):
    place = place_of(place_ref)
    low = lane_is_low((128, 128), 128)
    for block, ref in enumerate((kv0_ref, kv1_ref, kv2_ref)):
        for group in range(4):
            at = pl.multiple_of(lax.rem(group - place + 4, 4) * 128, 128)
            piece = ref[pl.ds(at, 128), :].astype(F32)
            rolled = pltpu.roll(piece, 64, 1)
            to = block * 512 + group * 128
            kk_ref[to : to + 128, :] = jnp.where(low, piece, rolled).astype(BF16)
            vv_ref[to : to + 128, :] = jnp.where(low, rolled, piece).astype(BF16)
            kvt_ref[:, to : to + 128] = piece.T.astype(BF16)


def set_up(place, kv):
    vmem = pl.BlockSpec(memory_space=pltpu.VMEM)
    return pl.pallas_call(
        set_up_kernel,
        out_shape=(
            jax.ShapeDtypeStruct((1536, 128), BF16),
            jax.ShapeDtypeStruct((1536, 128), BF16),
            jax.ShapeDtypeStruct((128, 1536), BF16),
        ),
        in_specs=[pl.BlockSpec(memory_space=pltpu.SMEM), vmem, vmem, vmem],
        out_specs=(vmem, vmem, vmem),
        compiler_params=pltpu.CompilerParams(vmem_limit_bytes=VMEM_LIMIT),
        cost_estimate=pl.CostEstimate(flops=1536 * 128 * 8, bytes_accessed=2 * 1024 * 1024, transcendentals=0),
    )(place, *kv)


def both_heads(pair):
    low = lane_is_low(pair.shape, 128)
    nothing = jnp.zeros_like(pair)
    return jnp.concatenate([jnp.where(low, pair, nothing), jnp.where(low, nothing, pair)], 0)


def side_by_side(transposed):
    return jnp.concatenate([transposed[:, :128], transposed[:, 128:]], 0).T


def mask_of(at, low_ref):
    key = lax.broadcasted_iota(jnp.int32, (KEYS, 128), 0)
    query = lax.broadcasted_iota(jnp.int32, (KEYS, 128), 1)
    seen = (key >= low_ref[:, pl.ds(at, 128)] - at) & (key <= query + WINDOW)
    bias = jnp.where(seen, 0.0, -jnp.inf)
    return jnp.concatenate([bias, bias], 1)


def attend_kernel(
    first, step, place_ref, q_ref, kk_ref, kvt_ref, low_ref, w_ref, o_ref, lse_ref, *refs
):
    part_refs, (bias, held, w_held, sem) = refs[:-4], refs[-4:]
    group = lax.rem(place_of(place_ref) + first + step * pl.program_id(0), 4)
    at = pl.multiple_of(group * 128, 128)

    load = pltpu.make_async_copy(w_ref.at[:, pl.ds(HIDDEN, 512)], w_held, sem)

    @pl.when((pl.program_id(0) == 0) & (pl.program_id(1) == 0))
    def _():
        load.start()

    @pl.when(pl.program_id(1) == 0)
    def _():
        bias[...] = mask_of(at, low_ref)

    keys = pl.ds(at, KEYS)
    for number in range(PAIRS):
        columns = slice(128 * number, 128 * number + 128)
        scores = dot_nt(kk_ref[keys, :], both_heads(q_ref[:, columns])) + bias[...]
        top = jnp.max(scores, 0, keepdims=True)
        weights = jnp.exp(scores - top)
        total = jnp.sum(weights, 0, keepdims=True)
        result = dot_nn(kvt_ref[64:128, keys], weights.astype(BF16)) / total
        lse_ref[0, number] = top + jnp.log(total)
        result = side_by_side(result).astype(BF16)
        o_ref[:, columns] = result
        held[PAIRS * pl.program_id(1) + number] = result

    @pl.when(pl.program_id(1) == 4 // PAIRS - 1)
    def _():
        @pl.when(pl.program_id(0) == 0)
        def _():
            load.wait()

        rows = jnp.concatenate([held[k] for k in range(4)], 1)
        part = dot_nt(rows, w_held[...]).astype(BF16)
        for number, ref in enumerate(part_refs):

            @pl.when(pl.program_id(0) == number)
            def _():
                ref[...] = part


def attend(first, step, count, place, queries, kk, kvt, low, weights):
    whole = lambda g, p, s: (0, 0)
    width = 128 * PAIRS
    grid = pltpu.PrefetchScalarGridSpec(
        num_scalar_prefetch=1,
        grid=(count, 4 // PAIRS),
        in_specs=[
            pl.BlockSpec((128, width), lambda g, p, s: (first + step * g, p)),
            pl.BlockSpec((1536, 128), whole),
            pl.BlockSpec((128, 1536), whole),
            pl.BlockSpec((1, 512), whole),
            pl.BlockSpec(memory_space=pl.ANY),
        ],
        out_specs=(
            pl.BlockSpec((128, width), lambda g, p, s: (g, p)),
            pl.BlockSpec((1, PAIRS, 1, 256), lambda g, p, s: (g, p, 0, 0)),
        )
        + (pl.BlockSpec((128, 2048), whole),) * count,
        scratch_shapes=[
            pltpu.VMEM((KEYS, 256), F32),
            pltpu.VMEM((4, 128, 128), BF16),
            pltpu.VMEM((2048, 512), BF16),
            pltpu.SemaphoreType.DMA,
        ],
    )
    return pl.pallas_call(
        functools.partial(attend_kernel, first, step),
        grid_spec=grid,
        out_shape=(
            jax.ShapeDtypeStruct((128 * count, 512), BF16),
            jax.ShapeDtypeStruct((count, 4, 1, 256), F32),
        )
        + (jax.ShapeDtypeStruct((128, 2048), BF16),) * count,
        compiler_params=pltpu.CompilerParams(vmem_limit_bytes=VMEM_LIMIT),
        cost_estimate=pl.CostEstimate(
            flops=count * 4 * KEYS * 256 * 256 * 2,
            bytes_accessed=3 * 1024 * 1024,
            transcendentals=count * 4 * KEYS * 256,
        ),
    )(place, queries, kk, kvt, low, weights)


def attend_back_kernel(first, step, count, *refs):
    last = first == 2
    place_ref, q_ref, w_ref, lse_ref, kk_ref, vv_ref, kvt_ref, low_ref, cos_ref, sin_ref = refs[:10]
    o_ref = refs[10]
    dh_refs, refs = refs[11 : 11 + count], refs[11 + count :]
    dk_in = dv_in = None
    if first > 0:
        dk_in, dv_in, refs = refs[0], refs[1], refs[2:]
    bias, do_held, dk, dv, w_held, sem = refs[-6:]
    dq_ref, outs = refs[0], refs[1:-6]
    number, pair = pl.program_id(0), pl.program_id(1)
    place = place_of(place_ref)
    at = pl.multiple_of(lax.rem(place + first + step * number, 4) * 128, 128)

    load = pltpu.make_async_copy(w_ref.at[:, pl.ds(HIDDEN, 512)], w_held, sem)

    @pl.when((number == 0) & (pair == 0))
    def _():
        load.start()
        dk[...] = jnp.zeros_like(dk) if dk_in is None else dk_in[...]
        dv[...] = jnp.zeros_like(dv) if dv_in is None else dv_in[...]

    @pl.when(pair == 0)
    def _():
        bias[...] = mask_of(at, low_ref)

        @pl.when(number == 0)
        def _():
            load.wait()

        for k, ref in enumerate(dh_refs):

            @pl.when(number == k)
            def _():
                do_rows = dot_nn(ref[...], w_held[...]).astype(BF16)
                for p in range(4):
                    do_held[p] = do_rows[:, 128 * p : 128 * p + 128]

    keys = pl.ds(at, KEYS)
    queries, grads, all_weights, all_grad_scores = [], [], [], []
    for k in range(PAIRS):
        columns = slice(128 * k, 128 * k + 128)
        do_pair = do_held[PAIRS * pair + k]
        query, grad = both_heads(q_ref[:, columns]), both_heads(do_pair)
        scores = dot_nt(kk_ref[keys, :], query) + bias[...]
        weights = jnp.exp(scores - lse_ref[0, k])
        grad_weights = dot_nt(vv_ref[keys, :], grad)
        product = (o_ref[:, columns].astype(F32) * do_pair.astype(F32)).T
        inner = jnp.concatenate(
            [jnp.sum(product[:64], 0, keepdims=True), jnp.sum(product[64:], 0, keepdims=True)], 1
        )
        grad_scores = (weights * (grad_weights - inner)).astype(BF16)
        grad_query = side_by_side(dot_nn(kvt_ref[0:64, keys], grad_scores)) * HEAD_SIZE**-0.5
        dq_ref[:, columns] = turn(grad_query, cos_ref[...], -sin_ref[...]).astype(BF16)
        queries.append(query)
        grads.append(grad)
        all_weights.append(weights.astype(BF16))
        all_grad_scores.append(grad_scores)
    join = lambda values, axis: values[0] if PAIRS == 1 else jnp.concatenate(values, axis)
    dv[keys, :] += dot_nn(join(all_weights, 1), join(grads, 0))
    dk[keys, :] += dot_nn(join(all_grad_scores, 1), join(queries, 0))

    @pl.when((number == pl.num_programs(0) - 1) & (pair == 4 // PAIRS - 1))
    def _():
        if not last:
            outs[0][...], outs[1][...] = dk[...], dv[...]
            return
        half = lane_is_low((128, 128), 128)
        for block in range(3):
            for group in range(4):
                to = pl.multiple_of(lax.rem(group - place + 4, 4) * 128, 128)
                frm = slice(block * 512 + group * 128, block * 512 + group * 128 + 128)
                key, value = dk[frm, :], dv[frm, :]
                key = key + pltpu.roll(key, 64, 1)
                value = value + pltpu.roll(value, 64, 1)
                both = jnp.where(half, key, value)
                outs[block][pl.ds(to, 128), :] = both.astype(outs[block].dtype)


def attend_back(first, step, count, place, queries, o, dh, weights, lse, kk, vv, kvt, low, cosine, sine, held):
    last = first == 2
    whole = lambda g, p, s: (0, 0)
    specs = [
        pl.BlockSpec((128, 128 * PAIRS), lambda g, p, s: (first + step * g, p)),
        pl.BlockSpec(memory_space=pl.ANY),
        pl.BlockSpec((1, PAIRS, 1, 256), lambda g, p, s: (g, p, 0, 0)),
        pl.BlockSpec((1536, 128), whole),
        pl.BlockSpec((1536, 128), whole),
        pl.BlockSpec((128, 1536), whole),
        pl.BlockSpec((1, 512), whole),
        pl.BlockSpec((128, 128), lambda g, p, s: (first + step * g, 0)),
        pl.BlockSpec((128, 128), lambda g, p, s: (first + step * g, 0)),
    ]
    specs += [pl.BlockSpec((128, 128 * PAIRS), lambda g, p, s: (g, p))]
    specs += [pl.BlockSpec((128, 2048), whole)] * count + [pl.BlockSpec((1536, 128), whole)] * len(held)
    if last:
        out_specs = (pl.BlockSpec((512, 128), whole),) * 3
        out_shape = tuple(jax.ShapeDtypeStruct((512, 128), dtype) for dtype in (BF16, BF16, F32))
    else:
        out_specs = (pl.BlockSpec((1536, 128), whole),) * 2
        out_shape = (jax.ShapeDtypeStruct((1536, 128), F32),) * 2
    grid = pltpu.PrefetchScalarGridSpec(
        num_scalar_prefetch=1,
        grid=(count, 4 // PAIRS),
        in_specs=specs,
        out_specs=(pl.BlockSpec((128, 128 * PAIRS), lambda g, p, s: (g, p)),) + out_specs,
        scratch_shapes=[
            pltpu.VMEM((KEYS, 256), F32),
            pltpu.VMEM((4, 128, 128), BF16),
            pltpu.VMEM((1536, 128), F32),
            pltpu.VMEM((1536, 128), F32),
            pltpu.VMEM((2048, 512), BF16),
            pltpu.SemaphoreType.DMA,
        ],
    )
    return pl.pallas_call(
        functools.partial(attend_back_kernel, first, step, count),
        grid_spec=grid,
        out_shape=(jax.ShapeDtypeStruct((128 * count, 512), BF16),) + out_shape,
        compiler_params=pltpu.CompilerParams(vmem_limit_bytes=VMEM_LIMIT),
        cost_estimate=pl.CostEstimate(
            flops=count * 4 * KEYS * 256 * 640 * 2,
            bytes_accessed=6 * 1024 * 1024,
            transcendentals=count * 4 * KEYS * 256,
        ),
    )(place, queries, weights, lse, kk, vv, kvt, low, cosine, sine, o, *dh, *held)


GROUPS = [(0, 128), (128, 256), (384, 512), (896, 512)]


def columns_times_kernel(left_ref, right_ref, out_ref, left, right, out, sems, out_sems):
    load = pltpu.make_async_copy(left_ref, left, sems.at[len(GROUPS)])
    load.start()
    copies, results = [], []
    for number, (start, width) in enumerate(GROUPS):
        columns = pl.ds(start, width)
        copy = pltpu.make_async_copy(right_ref.at[:, columns], right.at[:, columns], sems.at[number])
        copy.start()
        copies.append(copy)
    load.wait()
    value = left[...]
    for number, (start, width) in enumerate(GROUPS):
        copies[number].wait()
        out[:, start : start + width] = dot_nn(value, right[:, start : start + width])
        columns = pl.ds(start, width)
        copy = pltpu.make_async_copy(out.at[:, columns], out_ref.at[:, columns], out_sems.at[number])
        copy.start()
        results.append(copy)
    for copy in results:
        copy.wait()


def columns_times(left, right):
    rows, width = left.shape
    anywhere = pl.BlockSpec(memory_space=pl.ANY)
    return pl.pallas_call(
        columns_times_kernel,
        out_shape=jax.ShapeDtypeStruct((rows, HIDDEN), F32),
        in_specs=[anywhere, anywhere],
        out_specs=anywhere,
        scratch_shapes=[
            pltpu.VMEM((rows, width), BF16),
            pltpu.VMEM((width, HIDDEN), BF16),
            pltpu.VMEM((rows, HIDDEN), F32),
            pltpu.SemaphoreType.DMA((len(GROUPS) + 1,)),
            pltpu.SemaphoreType.DMA((len(GROUPS),)),
        ],
        compiler_params=pltpu.CompilerParams(vmem_limit_bytes=VMEM_LIMIT),
        cost_estimate=pl.CostEstimate(
            flops=2 * rows * width * HIDDEN, bytes_accessed=11 * 1024 * 1024, transcendentals=0
        ),
    )(left, right)


PIECES = [(0, 128), (128, 128), (256, 128), (384, 128)]


def ffn_kernel(*refs):
    core_ref, x_refs, dact_ref, w_ref = refs[0], refs[1:9], refs[9], refs[10]
    gua_ref, whole_ref, swap_ref, dx_refs = refs[11], refs[12], refs[13], refs[14:18]
    x_held, dact_held, w_held, gua, dx, sems, out_sems = refs[18:]
    x_copies = []
    for number in range(8):
        copy = pltpu.make_async_copy(
            x_refs[number], x_held.at[pl.ds(64 * number, 64)], sems.at[12 + number]
        )
        copy.start()
        x_copies.append(copy)
    copies = []
    for number, (start, width) in enumerate(GROUPS):
        for part in range(3):
            if part < 2:
                columns = pl.ds(part * HIDDEN + start, width)
                copy = pltpu.make_async_copy(
                    w_ref.at[:, columns], w_held.at[:, columns], sems.at[3 * number + part]
                )
            else:
                columns = pl.ds(start, width)
                copy = pltpu.make_async_copy(
                    dact_ref.at[:, columns], dact_held.at[:, columns], sems.at[3 * number + part]
                )
            copy.start()
            copies.append(copy)
    for copy in x_copies:
        copy.wait()
    half = pl.multiple_of((1 - core_of(core_ref)) * 1024, 1024)
    results = [
        pltpu.make_async_copy(x_held, whole_ref, out_sems.at[5]),
        pltpu.make_async_copy(x_held.at[:, pl.ds(half, 1024)], swap_ref, out_sems.at[6]),
    ]
    for copy in results:
        copy.start()
    x = x_held[...]
    for number, (start, width) in enumerate(GROUPS):
        for part in range(3):
            copies[3 * number + part].wait()
        gate = dot_nn(x, w_held[:, start : start + width])
        up = dot_nn(x, w_held[:, HIDDEN + start : HIDDEN + start + width])
        dact = dact_held[:, start : start + width]
        sig = jax.nn.sigmoid(gate)
        silu = gate * sig
        dgate = dact * up * (sig * (1.0 + gate * (1.0 - sig)))
        gua[:, start : start + width] = dgate.astype(BF16)
        gua[:, HIDDEN + start : HIDDEN + start + width] = (dact * silu).astype(BF16)
        gua[:, 2 * HIDDEN + start : 2 * HIDDEN + start + width] = (silu * up).astype(BF16)
    copy = pltpu.make_async_copy(gua, gua_ref, out_sems.at[4])
    copy.start()
    results.append(copy)
    dgu = gua[:, : 2 * HIDDEN]
    for number in range(4):
        columns = slice(512 * number, 512 * number + 512)
        dx[:, columns] = dot_nt(dgu, w_held[columns, : 2 * HIDDEN]).astype(BF16)
        for piece, (start, size) in enumerate(PIECES):
            copy = pltpu.make_async_copy(
                dx.at[pl.ds(start, size), pl.ds(512 * number, 512)],
                dx_refs[piece].at[:, pl.ds(512 * number, 512)],
                out_sems.at[7 + 4 * number + piece],
            )
            copy.start()
            results.append(copy)
    for copy in results:
        copy.wait()


def ffn(core, pieces, dact, weights):
    rows, width = dact.shape[0], weights.shape[0]
    anywhere = pl.BlockSpec(memory_space=pl.ANY)
    result = pl.pallas_call(
        ffn_kernel,
        out_shape=(
            jax.ShapeDtypeStruct((rows, 3 * HIDDEN), BF16),
            jax.ShapeDtypeStruct((rows, width), BF16),
            jax.ShapeDtypeStruct((rows, width // 2), BF16),
            *(jax.ShapeDtypeStruct((size, width), BF16) for _, size in PIECES),
        ),
        in_specs=[pl.BlockSpec(memory_space=pltpu.SMEM)] + [anywhere] * 10,
        out_specs=(anywhere,) * 7,
        scratch_shapes=[
            pltpu.VMEM((rows, width), BF16),
            pltpu.VMEM((rows, HIDDEN), F32),
            pltpu.VMEM((width, 2 * HIDDEN), BF16),
            pltpu.VMEM((rows, 3 * HIDDEN), BF16),
            pltpu.VMEM((rows, width), BF16),
            pltpu.SemaphoreType.DMA((20,)),
            pltpu.SemaphoreType.DMA((23,)),
        ],
        compiler_params=pltpu.CompilerParams(vmem_limit_bytes=VMEM_LIMIT),
        cost_estimate=pl.CostEstimate(
            flops=8 * rows * width * HIDDEN,
            bytes_accessed=25 * 1024 * 1024,
            transcendentals=rows * HIDDEN,
        ),
    )(core, *pieces, dact, weights)
    return result[0], result[1], result[2], result[3:]


def weight_grads_kernel(core_ref, x_ref, x2_ref, dy_ref, dy2_ref, right_ref, right2_ref, out_ref, dy, dy2, sems):
    part = pl.program_id(0)
    half = dy.shape[1]
    start = pl.multiple_of(core_of(core_ref) * half, half)
    loads = (
        pltpu.make_async_copy(dy_ref.at[:, pl.ds(start, half)], dy, sems.at[0]),
        pltpu.make_async_copy(dy2_ref, dy2, sems.at[1]),
    )

    @pl.when(part == 0)
    def _():
        for load in loads:
            load.start()

    @pl.when(part < 2)
    def _():
        total = dot_tn(x_ref[...], right_ref[...]) + dot_tn(x2_ref[...], right2_ref[...])
        out_ref[...] = total.astype(BF16)

    @pl.when(part == 2)
    def _():
        for load in loads:
            load.wait()
        total = dot_tn(dy[...], right_ref[...]) + dot_tn(dy2[...], right2_ref[...])
        out_ref[...] = total.astype(BF16)


def weight_grads(core, x, x2, dy, dy2, right, right2):
    rows, half = x2.shape
    anywhere = pl.BlockSpec(memory_space=pl.ANY)
    side = lambda j, c: (0, j)
    grid = pltpu.PrefetchScalarGridSpec(
        num_scalar_prefetch=1,
        grid=(3,),
        in_specs=[
            pl.BlockSpec((rows, half), lambda j, c: (0, core_of(c))),
            pl.BlockSpec((rows, half), lambda j, c: (0, 0)),
            anywhere,
            anywhere,
            pl.BlockSpec((rows, HIDDEN), side),
            pl.BlockSpec((rows, HIDDEN), side),
        ],
        out_specs=pl.BlockSpec((half, HIDDEN), side),
        scratch_shapes=[
            pltpu.VMEM((rows, half), BF16),
            pltpu.VMEM((rows, half), BF16),
            pltpu.SemaphoreType.DMA((2,)),
        ],
    )
    return pl.pallas_call(
        weight_grads_kernel,
        grid_spec=grid,
        out_shape=jax.ShapeDtypeStruct((half, 3 * HIDDEN), BF16),
        compiler_params=pltpu.CompilerParams(vmem_limit_bytes=VMEM_LIMIT),
        cost_estimate=pl.CostEstimate(
            flops=2 * 3 * 2 * rows * half * HIDDEN, bytes_accessed=24 * 1024 * 1024, transcendentals=0
        ),
    )(core, x, x2, dy, dy2, right, right2)


def rows_times_kernel(left_ref, right_ref, *out_refs):
    result = dot_nt(left_ref[...], right_ref[...]).astype(BF16)
    for number, ref in enumerate(out_refs):
        ref[...] = result[128 * number : 128 * number + 128]


def rows_times(left, left_part, right, part):
    rows, depth = left.shape[0], HIDDEN
    width = right.shape[0]
    tile = 512
    return pl.pallas_call(
        rows_times_kernel,
        out_shape=(jax.ShapeDtypeStruct((128, width), BF16),) * 4,
        grid=(width // tile,),
        in_specs=[
            pl.BlockSpec((rows, depth), lambda i: (0, left_part)),
            pl.BlockSpec((tile, depth), lambda i: (i, part)),
        ],
        out_specs=(pl.BlockSpec((128, tile), lambda i: (0, i)),) * 4,
        compiler_params=pltpu.CompilerParams(vmem_limit_bytes=VMEM_LIMIT),
        cost_estimate=pl.CostEstimate(
            flops=2 * rows * depth * width,
            bytes_accessed=2 * (rows * depth + width * depth + rows * width),
            transcendentals=0,
        ),
    )(left, right)


def ring_rows(own, near, far):
    return jnp.concatenate([own, near[:128], far, near[128:]], 0)


def put_half(number, value, other_ref, own_ref):
    @pl.when(number < 2)
    def _():
        other_ref[...] = value

    @pl.when(number >= 2)
    def _():
        own_ref[...] = value


def tile_at(i, c):
    return lax.rem(i + 2 * (1 - core_of(c)), 4)


def half_specs(tile, columns):
    return (
        pl.BlockSpec((tile, columns), lambda i, c: (jnp.minimum(i, 1), 0)),
        pl.BlockSpec((tile, columns), lambda i, c: (jnp.maximum(i - 2, 0), 0)),
    )


def wide_grads_kernel(
    core_ref, x_ref, dh0, dh1, dh2, dh3, o0, o1, o2, dq0, dq1, dq2, other_ref, own_ref, o_held, dq_held
):
    number = pl.program_id(0)

    @pl.when(number == 0)
    def _():
        o_held[...] = ring_rows(o0[...], o1[...], o2[...])
        dq_held[...] = ring_rows(dq0[...], dq1[...], dq2[...])

    dh = jnp.concatenate([ref[...] for ref in (dh0, dh1, dh2, dh3)], 0)
    out = dot_tn(dh, o_held[...])
    query = dot_tn(x_ref[...], dq_held[...])
    put_half(number, jnp.concatenate([out, query], 1).astype(BF16), other_ref, own_ref)


def wide_grads(core, normed, dh, o, dq):
    rows, width = normed.shape
    tile = 512
    whole = lambda i, c: (0, 0)
    column = lambda i, c: (0, tile_at(i, c))
    small = [pl.BlockSpec((size, 512), whole) for size in (128, 256, 128)]
    grid = pltpu.PrefetchScalarGridSpec(
        num_scalar_prefetch=1,
        grid=(4,),
        in_specs=[pl.BlockSpec((rows, tile), column)]
        + [pl.BlockSpec((128, tile), column)] * 4
        + small
        + small,
        out_specs=half_specs(tile, 1024),
        scratch_shapes=[pltpu.VMEM((rows, 512), BF16), pltpu.VMEM((rows, 512), BF16)],
    )
    return pl.pallas_call(
        wide_grads_kernel,
        grid_spec=grid,
        out_shape=(jax.ShapeDtypeStruct((width // 2, 1024), BF16),) * 2,
        compiler_params=pltpu.CompilerParams(vmem_limit_bytes=VMEM_LIMIT),
        cost_estimate=pl.CostEstimate(
            flops=2 * rows * width * 1024, bytes_accessed=10 * 1024 * 1024, transcendentals=0
        ),
    )(core, normed, *dh, *o, *dq)


def finish_kernel(
    core_ref,
    x_ref,
    w_ref,
    dq0_ref,
    dq1_ref,
    dq2_ref,
    own_ref,
    one_ref,
    two_ref,
    cos_ref,
    sin_ref,
    norm_ref,
    second_ref,
    other_grad_ref,
    own_grad_ref,
    dx_ref,
    gain_ref,
    dqkv,
    sums,
):
    number = pl.program_id(0)

    @pl.when(number == 0)
    def _():
        dqkv[:, :512] = ring_rows(dq0_ref[...], dq1_ref[...], dq2_ref[...])
        dkv = own_ref[...] + one_ref[...].astype(F32) + two_ref[...].astype(F32)
        turned = turn(dkv, cos_ref[...], -sin_ref[...])
        dqkv[:, 512:] = jnp.where(lane_is_low(dkv.shape, 128), turned, dkv).astype(BF16)

    x = x_ref[...]
    put_half(number, dot_tn(x, dqkv[:, 512:]).astype(BF16), other_grad_ref, own_grad_ref)
    dx = dot_nt(dqkv[...], w_ref[...])
    for piece in range(4):
        row = pl.multiple_of(lax.rem(place_of(core_ref) + piece, 4) * 128, 128)
        dx_ref[pl.ds(row, 128), :] = dx[128 * piece : 128 * piece + 128].astype(BF16)
    columns = pl.ds(pl.multiple_of(tile_at(number, core_ref) * 512, 512), 512)
    sums[:, columns] = jnp.broadcast_to(
        jnp.sum(dx * x.astype(F32), 0, keepdims=True) / norm_ref[:1], (8, 512)
    )

    @pl.when(number == 3)
    def _():
        gain_ref[:8] = gain_rows(to_blocks(sums[...])[:1])
        gain_ref[8:] = gain_rows(second_ref[:1])


def finish(core, normed, weights, dq, own, one, two, cosine, sine, gain, second):
    rows, width = normed.shape
    tile = 512
    whole = lambda i, c: (0, 0)
    column = lambda i, c: (0, tile_at(i, c))
    narrow = pl.BlockSpec((rows, 128), whole)
    grid = pltpu.PrefetchScalarGridSpec(
        num_scalar_prefetch=1,
        grid=(4,),
        in_specs=[
            pl.BlockSpec((rows, tile), column),
            pl.BlockSpec((tile, 640), lambda i, c: (tile_at(i, c), 0)),
            pl.BlockSpec((128, 512), whole),
            pl.BlockSpec((256, 512), whole),
            pl.BlockSpec((128, 512), whole),
            narrow,
            narrow,
            narrow,
            narrow,
            narrow,
            pl.BlockSpec((2, tile), column),
            pl.BlockSpec((8, width), whole),
        ],
        out_specs=half_specs(tile, 128)
        + (pl.BlockSpec((rows, tile), column),)
        + (pl.BlockSpec((GAIN_ROWS, GAIN_COLUMNS), whole),),
        scratch_shapes=[pltpu.VMEM((rows, 640), BF16), pltpu.VMEM((8, width), F32)],
    )
    result = pl.pallas_call(
        finish_kernel,
        grid_spec=grid,
        out_shape=(jax.ShapeDtypeStruct((width // 2, 128), BF16),) * 2
        + (jax.ShapeDtypeStruct((rows, width), BF16),)
        + (jax.ShapeDtypeStruct((GAIN_ROWS, GAIN_COLUMNS), F32),),
        compiler_params=pltpu.CompilerParams(vmem_limit_bytes=VMEM_LIMIT),
        cost_estimate=pl.CostEstimate(
            flops=2 * rows * width * 768, bytes_accessed=10 * 1024 * 1024, transcendentals=0
        ),
    )(core, normed, weights, *dq, own, one, two, cosine, sine, gain, second)
    return result


def per_device(
    tokens,
    segments,
    w_query,
    key_projection,
    value_projection,
    w_out,
    w_gate,
    w_up,
    w_down,
    norm_attn,
    norm_ffn,
    cotangent,
):
    place, core = lax.axis_index("head"), lax.axis_index("core")
    block = (lax.axis_index("y") * 4 + lax.axis_index("x")) * 2 + core
    code = (((lax.axis_index("x") * 4 + lax.axis_index("y")) * 2 + core) * 4 + place).astype(jnp.int32)
    code = code.reshape(1)
    keep = lax.optimization_barrier


    out_weights = lax.all_gather(
        jnp.concatenate([w_down.T, w_out.T], 1), CORE_FIRST, axis=0, tiled=True
    )
    ffn_weights = lax.all_gather(jnp.concatenate([w_gate, w_up], 1), CORE_FIRST, axis=0, tiled=True)

    x_rows, dy_rows, normed_rows, gains = prepare(
        tokens[0], cotangent[0], jnp.stack([norm_attn, norm_ffn]).astype(F32)
    )
    row = jnp.arange(512, dtype=jnp.int32)
    positions = block * 512 + ((row // 128 + place) % 4) * 128 + row % 128
    frequency = 10000.0 ** (-jnp.arange(32, dtype=F32) * 2.0 / HEAD_SIZE)
    angles = positions.astype(F32)[:, None] * frequency[None, :]
    cosine, sine = jnp.cos(angles), jnp.sin(angles)
    cosine = jnp.concatenate([cosine] * 4, 1)
    sine = jnp.concatenate([-sine, sine, -sine, sine], 1)

    flat = segments.reshape(-1)
    padded = jnp.concatenate([jnp.full((1024,), -1, jnp.int32), flat])
    own = lax.dynamic_slice_in_dim(flat, block * 512, 512, 0)
    window = lax.dynamic_slice_in_dim(padded, block * 512, 1536, 0)
    start = jnp.sum((window[None, :] < own[:, None]).astype(jnp.int32), 1)
    low = jnp.maximum(start, row + 1).reshape(1, 512)

    normed_rows, w_query = keep((normed_rows, w_query))
    ahead, behind = near_pieces(normed_rows)
    qkv_own = gather_axis(jnp.concatenate([w_query, key_projection, value_projection], 1), "x")
    qkv_own = gather_axis(jnp.concatenate(qkv_own, 0), "y")
    far = far_pieces(ahead, behind)
    qkv_own, far, cosine, sine, low = keep((qkv_own, far, cosine, sine, low))
    qkv_pieces = *qkv_own, *(shift(piece, "core", 1) for piece in qkv_own)
    kv_own, normed_one = project_kv(code, (normed_rows, ahead, *far, behind), qkv_pieces, cosine, sine)
    normed_late, kv_own, dy_raw = keep((normed_one, kv_own, cotangent[0]))
    dy_pieces = gather_pieces(dy_raw)
    kv = (from_block(kv_own, 2), from_block(kv_own, 1), kv_own)
    queries, qkv_weights = project_q(code, normed_late, qkv_pieces, cosine, sine)

    kk, vv, kvt = set_up(code, kv)
    seen = code, queries, kk, kvt, low, out_weights
    o_far, lse_far, part_far = attend(2, 1, 1, *seen)
    queries, part_far, dy_pieces = keep((queries, part_far, dy_pieces))
    part_far = shift(part_far, "head", 2)
    seen = code, queries, kk, kvt, low, out_weights
    o_near, lse_near, part_ahead, part_behind = attend(1, 2, 2, *seen)
    queries, part_far, part_ahead, part_behind = keep((queries, part_far, part_ahead, part_behind))
    seen = code, queries, kk, kvt, low, out_weights
    o_own, lse_own, part_own = attend(0, 1, 1, *seen)
    dy, dy_swap = assemble(code, dy_rows, *dy_pieces)
    dy_other = shift(dy_swap, "core", 1)
    attention_sum = part_own, shift(part_ahead, "head", 1), shift(part_behind, "head", -1), part_far
    h1, top, bottom = join(x_rows, gains, attention_sum)
    behind_top, ahead_bottom = shift(top, "head", 1), shift(bottom, "head", -1)
    ahead_top, behind_bottom = shift(top, "head", -1), shift(bottom, "head", 1)
    behind_top, ahead_bottom, dy = keep((behind_top, ahead_bottom, dy))
    far_top, far_bottom = shift(behind_top, "head", 1), shift(ahead_bottom, "head", -1)
    rows_two = top, bottom, ahead_top, ahead_bottom, far_top, far_bottom, behind_top, behind_bottom
    dact = columns_times(dy, out_weights)
    dact, dy_other = keep((dact, dy_other))

    gua, normed_two, normed_two_swap, dnormed_two = ffn(
        code, rows_two, dact, ffn_weights
    )
    dnormed_two = scatter_pieces(*dnormed_two)
    gua_other = shift(gua, "core", 1)
    normed_two_other = shift(normed_two_swap, "core", 1)
    out_pieces = rows_times(gua, 2, out_weights, 0)
    gua_other, normed_two_other, out_pieces = keep((gua_other, normed_two_other, out_pieces))
    held = weight_grads(code, normed_two, normed_two_other, dy, dy_other, gua, gua_other)
    held, dnormed_two = keep((held, dnormed_two))
    grads = lax.psum_scatter(held, ("y", "x"), scatter_dimension=0, tiled=True)

    dh1, dh1_low, grad_gain_two = join_back(h1, dy_rows, gains, dnormed_two)
    back = kk, vv, kvt, low, cosine, sine
    dq_own, dk, dv = attend_back(0, 1, 1, code, queries, o_own, (dh1_low,), out_weights, lse_own, *back, ())
    ahead, behind = shift(dh1_low, "head", -1), shift(dh1_low, "head", 1)
    ahead, behind, dk, dv, dh1_late, out_pieces = keep((ahead, behind, dk, dv, dh1_low, out_pieces))
    far = shift(dh1_late, "head", 2)
    dq_near, dk, dv = attend_back(
        1, 2, 2, code, queries, o_near, (ahead, behind), out_weights, lse_near, *back, (dk, dv)
    )
    far, dk, dv, out_pieces = keep((far, dk, dv, out_pieces))
    out_pieces = scatter_pieces(*out_pieces)
    dq_far, dkv_first, dkv_second, dkv_own = attend_back(
        2, 1, 1, code, queries, o_far, (far,), out_weights, lse_far, *back, (dk, dv)
    )
    dq = dq_own, dq_near, dq_far
    dkv_one = from_block(dkv_second, -1)
    dkv_two = from_block(dkv_first, -2)
    wide_other, wide_own = wide_grads(
        code, normed_one, (dh1_low, ahead, far, behind), (o_own, o_near, o_far), dq
    )
    dkv_one, dkv_two, wide_other, out_pieces = keep((dkv_one, dkv_two, wide_other, out_pieces))
    wide_other = shift(wide_other, "core", 1)

    narrow_other, narrow_own, dnormed_one, gain_grads = finish(
        code,
        normed_one,
        qkv_weights,
        dq,
        dkv_own,
        dkv_one,
        dkv_two,
        cosine,
        sine,
        gains,
        grad_gain_two,
    )
    dnormed_one = lax.psum_scatter(dnormed_one, "head", scatter_dimension=0, tiled=True)
    gain_grads = exchange([gain_grads] * 4, "head")
    rows = [(x_rows.shape, BF16)]
    (output,) = small_call(output_kernel, rows, h1, *out_pieces)
    gain_grads, output = keep((gain_grads, output))
    pieces, out_sums = first_pieces(
        code, wide_own, wide_other, narrow_own, shift(narrow_other, "core", 1), gain_grads
    )
    grads = (
        grads[:, :HIDDEN].astype(F32),
        grads[:, HIDDEN : 2 * HIDDEN].astype(F32),
        grads[:, 2 * HIDDEN :].T.astype(F32),
    )
    pieces, out_sums, grads = keep((exchange(pieces, "x"), exchange(out_sums, "y"), grads))
    pieces, out_sums = second_pieces(code, pieces, out_sums)
    (grad_inputs,) = small_call(input_grad_kernel, rows, dh1, x_rows, gains, dnormed_one)
    pieces, out_sums, grad_inputs = keep((exchange(pieces, "y"), exchange(out_sums, "x"), grad_inputs))
    (gain_grads,) = small_call(gains_kernel, [((GAIN_ROWS, GAIN_COLUMNS), F32)], *pieces)
    columns = (64, 512), (64, 512), (64, 64), (64, 64), (1, 2048), (1, 2048)
    grad_out, grad_query, grad_key, grad_value, grad_gain_one, grad_gain_two = small_call(
        attention_grads_kernel,
        [(shape, F32) for shape in columns],
        *pieces,
        *out_sums,
        gain_grads,
        shift(gain_grads, "core", 1),
    )

    return (
        output[None],
        grad_inputs[None],
        grad_query,
        grad_key,
        grad_value,
        grad_out.T,
        *grads,
        grad_gain_one.reshape(2048),
        grad_gain_two.reshape(2048),
    )


def solution(mesh):
    grid = Mesh(mesh.devices.reshape(4, 4, 4, 2), ("head", "y", "x", "core"))
    rows, up, down = P(BLK, "head", None), P(BLK, "head"), P("head", BLK)
    return jax.shard_map(
        per_device,
        mesh=grid,
        in_specs=(rows, P(), up, up, up, down, up, up, down, P(), P(), rows),
        out_specs=(rows, rows, up, up, up, down, up, up, down, P(), P()),
        check_vma=False,
    )
```

```python
import functools

import jax
import jax.numpy as jnp
from jax import lax
from jax.experimental import pallas as pl
from jax.experimental.pallas import tpu as pltpu
from jax.sharding import Mesh
from jax.sharding import PartitionSpec as P

HEAD_SIZE = 64
WINDOW = 1024
HIDDEN = 1408
EPSILON = 1e-05
BF16 = jnp.bfloat16
F32 = jnp.float32
BLK = ("y", "x", "core")
CORE_FIRST = ("core", "y", "x")
VMEM_LIMIT = 63 * 1024 * 1024


def dot_nn(a, b):
    return jnp.dot(a, b, preferred_element_type=F32)


def dot_nt(a, b):
    return lax.dot_general(a, b, (((1,), (1,)), ((), ())), preferred_element_type=F32)


def dot_tn(a, b):
    return lax.dot_general(a, b, (((0,), (0,)), ((), ())), preferred_element_type=F32)


def shift(value, axis, distance):
    size = lax.axis_size(axis)
    return lax.ppermute(value, axis, [(i, (i + distance) % size) for i in range(size)])


def add_low(a, b):
    return (a.astype(F32) + b.astype(F32)).astype(BF16)


def gather_pieces(rows):
    return shift(rows, "head", -1), shift(rows, "head", 2), shift(rows, "head", 1)


def near_pieces(rows):
    return shift(rows, "head", -1), shift(rows, "head", 1)


def far_pieces(ahead, behind):
    half = ahead.shape[0] // 2
    return shift(behind[:half], "head", 1), shift(ahead[half:], "head", -1)


def scatter_pieces(own, ahead, far, behind):
    return own, shift(ahead, "head", 1), shift(behind, "head", -1), shift(far, "head", 2)


def gather_axis(value, axis):
    return value, shift(value, axis, -1), shift(value, axis, 2), shift(value, axis, 1)


def exchange(pieces, axis):
    return pieces[0], shift(pieces[1], axis, 1), shift(pieces[2], axis, 2), shift(pieces[3], axis, -1)


def from_block(value, distance):
    route = [(i, i + distance) for i in range(32) if 0 <= i + distance < 32]
    return lax.ppermute(value, BLK, route)


def scale_of(values):
    return lax.rsqrt(jnp.mean(values * values, -1, keepdims=True) + EPSILON)


def x_of(code):
    return lax.shift_right_logical(code[0], 5)


def y_of(code):
    return lax.shift_right_logical(code[0], 3) & 3


def core_of(code):
    return lax.shift_right_logical(code[0], 2) & 1


def place_of(code):
    return code[0] & 3


def lane_is_low(shape, period):
    return lax.broadcasted_iota(jnp.int32, shape, len(shape) - 1) % period < period // 2


def turn(values, cosine, sine):
    swapped = jnp.where(
        lane_is_low(values.shape, 64), pltpu.roll(values, 96, 1), pltpu.roll(values, 32, 1)
    )
    return values * cosine + swapped * sine


def core_major_tiles(tiles):
    low = lane_is_low(tiles[0].shape, 128)
    rolled = [pltpu.roll(tile, 64, 1) for tile in tiles]
    first = [jnp.where(low, tiles[2 * k], rolled[2 * k + 1]) for k in range(8)]
    second = [jnp.where(low, rolled[2 * k], tiles[2 * k + 1]) for k in range(8)]
    return first + second


def block_major_tiles(tiles):
    low = lane_is_low(tiles[0].shape, 128)
    rolled = [pltpu.roll(tile, 64, 1) for tile in tiles]
    result = []
    for k in range(8):
        result.append(jnp.where(low, tiles[k], rolled[8 + k]))
        result.append(jnp.where(low, rolled[k], tiles[8 + k]))
    return result


def in_tiles(value):
    return [value[:, 128 * k : 128 * k + 128] for k in range(16)]


def prepare_kernel(x_ref, dy_ref, gain_ref, x_out, dy_out, normed_out, gain_out):
    def convert(ref):
        return jnp.concatenate(core_major_tiles(in_tiles(ref[...].astype(F32))), 1)

    x, gains = convert(x_ref), convert(gain_ref)
    gain_out[...] = gains
    x_out[...] = x
    dy_out[...] = convert(dy_ref).astype(BF16)
    normed_out[...] = (x * scale_of(x) * gains[:1]).astype(BF16)


def prepare(x, dy, gains):
    rows, width = x.shape
    return pl.pallas_call(
        prepare_kernel,
        out_shape=(
            jax.ShapeDtypeStruct((rows, width), F32),
            jax.ShapeDtypeStruct((rows, width), BF16),
            jax.ShapeDtypeStruct((rows, width), BF16),
            jax.ShapeDtypeStruct(gains.shape, F32),
        ),
        compiler_params=pltpu.CompilerParams(vmem_limit_bytes=VMEM_LIMIT),
        cost_estimate=pl.CostEstimate(
            flops=10 * rows * width, bytes_accessed=10 * rows * width, transcendentals=rows
        ),
    )(x, dy, gains)


def to_blocks(value):
    return jnp.concatenate(block_major_tiles(in_tiles(value)), 1)


def assemble_kernel(core_ref, own_ref, ahead_ref, far_ref, behind_ref, out_ref, swap_ref):
    out_ref[:128] = own_ref[...]
    start = 128
    for ref in (ahead_ref, far_ref, behind_ref):
        size = ref.shape[0]
        out_ref[start : start + size] = jnp.concatenate(
            core_major_tiles(in_tiles(ref[...].astype(F32))), 1
        ).astype(BF16)
        start += size
    swap_ref[...] = jnp.where(core_of(core_ref) == 0, out_ref[:, 1024:], out_ref[:, :1024])


def assemble(core, own, ahead, far, behind):
    vmem = pl.BlockSpec(memory_space=pltpu.VMEM)
    return pl.pallas_call(
        assemble_kernel,
        out_shape=(jax.ShapeDtypeStruct((512, 2048), BF16), jax.ShapeDtypeStruct((512, 1024), BF16)),
        in_specs=[pl.BlockSpec(memory_space=pltpu.SMEM)] + [vmem] * 4,
        out_specs=(vmem, vmem),
        compiler_params=pltpu.CompilerParams(vmem_limit_bytes=VMEM_LIMIT),
        cost_estimate=pl.CostEstimate(
            flops=4 * 512 * 2048, bytes_accessed=5 * 1024 * 1024, transcendentals=0
        ),
    )(core, own, ahead, far, behind)


def small_call(kernel, out_shape, *operands):
    return pl.pallas_call(
        kernel,
        out_shape=tuple(jax.ShapeDtypeStruct(shape, dtype) for shape, dtype in out_shape),
        compiler_params=pltpu.CompilerParams(vmem_limit_bytes=VMEM_LIMIT),
        cost_estimate=pl.CostEstimate(
            flops=sum(x.size for x in operands),
            bytes_accessed=2 * sum(x.size * x.dtype.itemsize for x in operands),
            transcendentals=0,
        ),
    )(*operands)


def total_of(refs):
    values = [ref[...].astype(F32) for ref in refs]
    while len(values) > 1:
        values = [values[0] + values[1]] + values[2:]
    return values[0]


def join_kernel(x_ref, gain_ref, a_ref, b_ref, c_ref, d_ref, h_out, top_out, bottom_out):
    h = x_ref[...] + total_of((a_ref, b_ref, c_ref, d_ref))
    h_out[...] = h
    normed = (h * scale_of(h) * gain_ref[1:2]).astype(BF16)
    half = h.shape[0] // 2
    top_out[...], bottom_out[...] = normed[:half], normed[half:]


def join(x, gain, pieces):
    half = x.shape[0] // 2, x.shape[1]
    return small_call(join_kernel, ((x.shape, F32), (half, BF16), (half, BF16)), x, gain, *pieces)


def norm_backward(values, gain, grad):
    scale = scale_of(values)
    weighted = grad * gain
    inner = jnp.mean(weighted * values, -1, keepdims=True)
    return scale * weighted - values * (scale * scale * scale * inner), scale


def join_back_kernel(h_ref, dy_ref, gain_ref, a_ref, b_ref, c_ref, d_ref, dh_out, low_out, grad_out):
    h, grad = h_ref[...], total_of((a_ref, b_ref, c_ref, d_ref))
    back, scale = norm_backward(h, gain_ref[1:2], grad)
    dh = dy_ref[...].astype(F32) + back
    dh_out[...] = dh
    low_out[...] = dh.astype(BF16)
    grad_out[...] = to_blocks(jnp.broadcast_to(jnp.sum(grad * h * scale, 0, keepdims=True), (8, h.shape[1])))


def join_back(h, dy, gain, pieces):
    shapes = (h.shape, F32), (h.shape, BF16), ((8, h.shape[1]), F32)
    return small_call(join_back_kernel, shapes, h, dy, gain, *pieces)


def output_kernel(h_ref, a_ref, b_ref, c_ref, d_ref, out_ref):
    out_ref[...] = to_blocks(h_ref[...] + total_of((a_ref, b_ref, c_ref, d_ref))).astype(BF16)


def input_grad_kernel(dh_ref, x_ref, gain_ref, grad_ref, out_ref):
    back, _ = norm_backward(x_ref[...], gain_ref[:1], grad_ref[...].astype(F32))
    out_ref[...] = to_blocks(dh_ref[...] + back).astype(BF16)


GAIN_ROWS, GAIN_COLUMNS = 16, 256


def gain_rows(vector):
    return jnp.concatenate([vector[:, 256 * k : 256 * k + 256] for k in range(8)], 0)


def put_piece(ref, rows, gains):
    count = rows.shape[0]
    ref[:count] = rows
    ref[count:, GAIN_COLUMNS:] = jnp.zeros((GAIN_ROWS, ref.shape[1] - GAIN_COLUMNS), BF16)
    ref[count:, :GAIN_COLUMNS] = gains.astype(BF16)


def first_pieces_kernel(
    at_ref, q_ref, q2_ref, kv_ref, kv2_ref, o_ref, o2_ref, *refs
):
    gain_refs, out_refs = refs[:4], refs[4:]
    query = add_low(q_ref[...], q2_ref[...]).reshape(256, 512)
    narrow = add_low(kv_ref[...], kv2_ref[...]).reshape(256, 128)
    rows = jnp.concatenate([query, narrow], 1)
    out_rows = add_low(o_ref[...], o2_ref[...]).reshape(256, 512)
    gains = total_of(gain_refs)
    for number in range(4):

        @pl.when(pl.program_id(0) == number)
        def _():
            put_piece(out_refs[number], rows, gains)
            out_refs[4 + number][...] = out_rows


def first_pieces(at, wide, wide2, narrow, narrow2, gains):
    pick_x = lambda column: lambda d, s: (0, lax.rem(x_of(s) + d, 4), 0, column)
    pick_y = lambda d, s: (lax.rem(y_of(s) + d, 4), 0, 0, 0)
    whole = lambda d, s: (0, 0)
    shaped = lambda value: value.reshape(4, 4, 64, value.shape[1])
    shapes = [(256 + GAIN_ROWS, 640)] * 4 + [(256, 512)] * 4
    grid = pltpu.PrefetchScalarGridSpec(
        num_scalar_prefetch=1,
        grid=(4,),
        in_specs=[pl.BlockSpec((4, 1, 64, 512), pick_x(1))] * 2
        + [pl.BlockSpec((4, 1, 64, 128), pick_x(0))] * 2
        + [pl.BlockSpec((1, 4, 64, 512), pick_y)] * 2
        + [pl.BlockSpec((GAIN_ROWS, GAIN_COLUMNS), whole)] * 4,
        out_specs=tuple(pl.BlockSpec(shape, whole) for shape in shapes),
    )
    wide, wide2 = shaped(wide), shaped(wide2)
    result = pl.pallas_call(
        first_pieces_kernel,
        grid_spec=grid,
        out_shape=tuple(jax.ShapeDtypeStruct(shape, BF16) for shape in shapes),
        compiler_params=pltpu.CompilerParams(vmem_limit_bytes=VMEM_LIMIT),
        cost_estimate=pl.CostEstimate(
            flops=2 * 1024 * 1152, bytes_accessed=6 * 1024 * 1152, transcendentals=0
        ),
    )(at, wide, wide2, shaped(narrow), shaped(narrow2), wide, wide2, *gains)
    return result[:4], result[4:]


def second_pieces_kernel(at_ref, *refs):
    qkv, out, (held, out_held) = refs[:4], refs[4:8], refs[16:]
    held[...] = total_of(qkv)
    out_held[...] = total_of(out).astype(BF16)
    for number in range(4):
        y = pl.multiple_of(lax.rem(y_of(at_ref) + number, 4) * 64, 64)
        put_piece(refs[8 + number], held[pl.ds(y, 64), :].astype(BF16), held[256:, :GAIN_COLUMNS])
        x = pl.multiple_of(lax.rem(x_of(at_ref) + number, 4) * 64, 64)
        refs[12 + number][...] = out_held[pl.ds(x, 64), :]


def second_pieces(at, qkv, out):
    vmem = pl.BlockSpec(memory_space=pltpu.VMEM)
    shapes = [(64 + GAIN_ROWS, 640)] * 4 + [(64, 512)] * 4
    result = pl.pallas_call(
        second_pieces_kernel,
        out_shape=tuple(jax.ShapeDtypeStruct(shape, BF16) for shape in shapes),
        in_specs=[pl.BlockSpec(memory_space=pltpu.SMEM)] + [vmem] * 8,
        out_specs=(vmem,) * 8,
        scratch_shapes=[pltpu.VMEM((256 + GAIN_ROWS, 640), F32), pltpu.VMEM((256, 512), BF16)],
        compiler_params=pltpu.CompilerParams(vmem_limit_bytes=VMEM_LIMIT),
        cost_estimate=pl.CostEstimate(
            flops=4 * 272 * 1152, bytes_accessed=10 * 272 * 1152, transcendentals=0
        ),
    )(at, *qkv, *out)
    return result[:4], result[4:]


def gains_kernel(a_ref, b_ref, c_ref, d_ref, out_ref):
    values = [ref[64:, :GAIN_COLUMNS].astype(F32) for ref in (a_ref, b_ref, c_ref, d_ref)]
    out_ref[...] = (values[0] + values[1]) + (values[2] + values[3])


def attention_grads_kernel(*refs):
    out_ref, q_ref, k_ref, v_ref, one_ref, two_ref = refs[10:]
    total = total_of(refs[:4])
    out_ref[...] = total_of(refs[4:8])
    q_ref[...] = total[:64, :512]
    k_ref[...] = total[:64, 512:576]
    v_ref[...] = total[:64, 576:]
    gains = total_of(refs[8:10])
    one_ref[...] = jnp.concatenate([gains[k : k + 1] for k in range(8)], 1)
    two_ref[...] = jnp.concatenate([gains[k : k + 1] for k in range(8, 16)], 1)


def put_in_order(at_ref, piece_refs, columns, to_ref, sems):
    x, y, core = x_of(at_ref), y_of(at_ref), core_of(at_ref)
    copies = []
    for number in range(32):
        to_x, to_y = lax.rem(x + number % 4, 4), lax.rem(y + number // 4 % 4, 4)
        to_core = core if number < 16 else 1 - core
        row = pl.multiple_of(((to_core * 4 + to_y) * 4 + to_x) * 64, 64)
        copy = pltpu.make_async_copy(
            piece_refs[number // 4].at[pl.ds(number % 4 * 64, 64), columns],
            to_ref.at[pl.ds(row, 64)],
            sems.at[number],
        )
        copy.start()
        copies.append(copy)
    return copies


RING_PIECES = [(0, 128), (128, 128), (256, 64), (320, 64), (384, 128)]


def project_kv_kernel(at_ref, *refs):
    x_refs, piece_refs, (cos_ref, sin_ref, kv_ref, whole_ref) = refs[:5], refs[5:13], refs[13:17]
    x_held, held, sems, x_sems = refs[17:]
    copies = []
    for number, (start, size) in enumerate(RING_PIECES):
        copy = pltpu.make_async_copy(x_refs[number], x_held.at[pl.ds(start, size)], x_sems.at[number])
        copy.start()
        copies.append(copy)
    copies += put_in_order(at_ref, piece_refs, pl.ds(512, 128), held, sems)
    for copy in copies:
        copy.wait()
    whole = pltpu.make_async_copy(x_held, whole_ref, x_sems.at[len(RING_PIECES)])
    whole.start()
    flat = dot_nn(x_held[...], held[...])
    turned = turn(flat, cos_ref[...], sin_ref[...])
    kv_ref[...] = jnp.where(lane_is_low(flat.shape, 128), turned, flat).astype(BF16)
    whole.wait()


def project_kv(at, x_pieces, weights, cosine, sine):
    rows, width = 512, x_pieces[0].shape[1]
    vmem, anywhere = pl.BlockSpec(memory_space=pltpu.VMEM), pl.BlockSpec(memory_space=pl.ANY)
    return pl.pallas_call(
        project_kv_kernel,
        out_shape=(jax.ShapeDtypeStruct((rows, 128), BF16), jax.ShapeDtypeStruct((rows, width), BF16)),
        in_specs=[pl.BlockSpec(memory_space=pltpu.SMEM)] + [anywhere] * 13 + [vmem, vmem],
        out_specs=(vmem, anywhere),
        scratch_shapes=[
            pltpu.VMEM((rows, width), BF16),
            pltpu.VMEM((width, 128), BF16),
            pltpu.SemaphoreType.DMA((32,)),
            pltpu.SemaphoreType.DMA((len(RING_PIECES) + 1,)),
        ],
        compiler_params=pltpu.CompilerParams(vmem_limit_bytes=VMEM_LIMIT),
        cost_estimate=pl.CostEstimate(
            flops=2 * rows * width * 128, bytes_accessed=5 * 1024 * 1024, transcendentals=0
        ),
    )(at, *x_pieces, *weights, cosine, sine)


def project_q_kernel(at_ref, x_ref, *refs):
    piece_refs, (cos_ref, sin_ref, q_ref, w_ref, held, sems, sem) = refs[:8], refs[8:]
    for copy in put_in_order(at_ref, piece_refs, pl.ds(0, 640), held, sems):
        copy.wait()
    whole = pltpu.make_async_copy(held, w_ref, sem)
    whole.start()
    cosine, sine, x = cos_ref[...], sin_ref[...], x_ref[...]
    for start in (0, 256):
        wide = dot_nn(x, held[:, start : start + 256])
        for part in (0, 128):
            turned = turn(wide[:, part : part + 128], cosine, sine)
            q_ref[:, start + part : start + part + 128] = (turned * HEAD_SIZE**-0.5).astype(BF16)
    whole.wait()


def project_q(at, normed, weights, cosine, sine):
    rows, width = normed.shape
    vmem, anywhere = pl.BlockSpec(memory_space=pltpu.VMEM), pl.BlockSpec(memory_space=pl.ANY)
    return pl.pallas_call(
        project_q_kernel,
        out_shape=(jax.ShapeDtypeStruct((rows, 512), BF16), jax.ShapeDtypeStruct((width, 640), BF16)),
        in_specs=[pl.BlockSpec(memory_space=pltpu.SMEM), vmem] + [anywhere] * 8 + [vmem, vmem],
        out_specs=(vmem, anywhere),
        scratch_shapes=[
            pltpu.VMEM((width, 640), BF16),
            pltpu.SemaphoreType.DMA((32,)),
            pltpu.SemaphoreType.DMA,
        ],
        compiler_params=pltpu.CompilerParams(vmem_limit_bytes=VMEM_LIMIT),
        cost_estimate=pl.CostEstimate(
            flops=2 * rows * width * 512, bytes_accessed=7 * 1024 * 1024, transcendentals=0
        ),
    )(at, normed, *weights, cosine, sine)


KEYS = 1152
PAIRS = 4


def set_up_kernel(place_ref, kv0_ref, kv1_ref, kv2_ref, kk_ref, vv_ref, kvt_ref):
    place = place_of(place_ref)
    low = lane_is_low((128, 128), 128)
    for block, ref in enumerate((kv0_ref, kv1_ref, kv2_ref)):
        for group in range(4):
            at = pl.multiple_of(lax.rem(group - place + 4, 4) * 128, 128)
            piece = ref[pl.ds(at, 128), :].astype(F32)
            rolled = pltpu.roll(piece, 64, 1)
            to = block * 512 + group * 128
            kk_ref[to : to + 128, :] = jnp.where(low, piece, rolled).astype(BF16)
            vv_ref[to : to + 128, :] = jnp.where(low, rolled, piece).astype(BF16)
            kvt_ref[:, to : to + 128] = piece.T.astype(BF16)


def set_up(place, kv):
    vmem = pl.BlockSpec(memory_space=pltpu.VMEM)
    return pl.pallas_call(
        set_up_kernel,
        out_shape=(
            jax.ShapeDtypeStruct((1536, 128), BF16),
            jax.ShapeDtypeStruct((1536, 128), BF16),
            jax.ShapeDtypeStruct((128, 1536), BF16),
        ),
        in_specs=[pl.BlockSpec(memory_space=pltpu.SMEM), vmem, vmem, vmem],
        out_specs=(vmem, vmem, vmem),
        compiler_params=pltpu.CompilerParams(vmem_limit_bytes=VMEM_LIMIT),
        cost_estimate=pl.CostEstimate(flops=1536 * 128 * 8, bytes_accessed=2 * 1024 * 1024, transcendentals=0),
    )(place, *kv)


def both_heads(pair):
    low = lane_is_low(pair.shape, 128)
    nothing = jnp.zeros_like(pair)
    return jnp.concatenate([jnp.where(low, pair, nothing), jnp.where(low, nothing, pair)], 0)


def side_by_side(transposed):
    return jnp.concatenate([transposed[:, :128], transposed[:, 128:]], 0).T


def mask_of(at, low_ref):
    key = lax.broadcasted_iota(jnp.int32, (KEYS, 128), 0)
    query = lax.broadcasted_iota(jnp.int32, (KEYS, 128), 1)
    seen = (key >= low_ref[:, pl.ds(at, 128)] - at) & (key <= query + WINDOW)
    bias = jnp.where(seen, 0.0, -jnp.inf)
    return jnp.concatenate([bias, bias], 1)


def attend_kernel(
    first, step, place_ref, q_ref, kk_ref, kvt_ref, low_ref, w_ref, o_ref, lse_ref, *refs
):
    part_refs, (bias, held, w_held, sem) = refs[:-4], refs[-4:]
    group = lax.rem(place_of(place_ref) + first + step * pl.program_id(0), 4)
    at = pl.multiple_of(group * 128, 128)

    load = pltpu.make_async_copy(w_ref.at[:, pl.ds(HIDDEN, 512)], w_held, sem)

    @pl.when((pl.program_id(0) == 0) & (pl.program_id(1) == 0))
    def _():
        load.start()

    @pl.when(pl.program_id(1) == 0)
    def _():
        bias[...] = mask_of(at, low_ref)

    keys = pl.ds(at, KEYS)
    for number in range(PAIRS):
        columns = slice(128 * number, 128 * number + 128)
        scores = dot_nt(kk_ref[keys, :], both_heads(q_ref[:, columns])) + bias[...]
        top = jnp.max(scores, 0, keepdims=True)
        weights = jnp.exp(scores - top)
        total = jnp.sum(weights, 0, keepdims=True)
        result = dot_nn(kvt_ref[64:128, keys], weights.astype(BF16)) / total
        lse_ref[0, number] = top + jnp.log(total)
        result = side_by_side(result).astype(BF16)
        o_ref[:, columns] = result
        held[PAIRS * pl.program_id(1) + number] = result

    @pl.when(pl.program_id(1) == 4 // PAIRS - 1)
    def _():
        @pl.when(pl.program_id(0) == 0)
        def _():
            load.wait()

        rows = jnp.concatenate([held[k] for k in range(4)], 1)
        part = dot_nt(rows, w_held[...]).astype(BF16)
        for number, ref in enumerate(part_refs):

            @pl.when(pl.program_id(0) == number)
            def _():
                ref[...] = part


def attend(first, step, count, place, queries, kk, kvt, low, weights):
    whole = lambda g, p, s: (0, 0)
    width = 128 * PAIRS
    grid = pltpu.PrefetchScalarGridSpec(
        num_scalar_prefetch=1,
        grid=(count, 4 // PAIRS),
        in_specs=[
            pl.BlockSpec((128, width), lambda g, p, s: (first + step * g, p)),
            pl.BlockSpec((1536, 128), whole),
            pl.BlockSpec((128, 1536), whole),
            pl.BlockSpec((1, 512), whole),
            pl.BlockSpec(memory_space=pl.ANY),
        ],
        out_specs=(
            pl.BlockSpec((128, width), lambda g, p, s: (g, p)),
            pl.BlockSpec((1, PAIRS, 1, 256), lambda g, p, s: (g, p, 0, 0)),
        )
        + (pl.BlockSpec((128, 2048), whole),) * count,
        scratch_shapes=[
            pltpu.VMEM((KEYS, 256), F32),
            pltpu.VMEM((4, 128, 128), BF16),
            pltpu.VMEM((2048, 512), BF16),
            pltpu.SemaphoreType.DMA,
        ],
    )
    return pl.pallas_call(
        functools.partial(attend_kernel, first, step),
        grid_spec=grid,
        out_shape=(
            jax.ShapeDtypeStruct((128 * count, 512), BF16),
            jax.ShapeDtypeStruct((count, 4, 1, 256), F32),
        )
        + (jax.ShapeDtypeStruct((128, 2048), BF16),) * count,
        compiler_params=pltpu.CompilerParams(vmem_limit_bytes=VMEM_LIMIT),
        cost_estimate=pl.CostEstimate(
            flops=count * 4 * KEYS * 256 * 256 * 2,
            bytes_accessed=3 * 1024 * 1024,
            transcendentals=count * 4 * KEYS * 256,
        ),
    )(place, queries, kk, kvt, low, weights)


def attend_back_kernel(first, step, count, *refs):
    last = first == 2
    place_ref, q_ref, w_ref, lse_ref, kk_ref, vv_ref, kvt_ref, low_ref, cos_ref, sin_ref = refs[:10]
    o_ref = refs[10]
    dh_refs, refs = refs[11 : 11 + count], refs[11 + count :]
    dk_in = dv_in = None
    if first > 0:
        dk_in, dv_in, refs = refs[0], refs[1], refs[2:]
    bias, do_held, dk, dv, w_held, sem = refs[-6:]
    dq_ref, outs = refs[0], refs[1:-6]
    number, pair = pl.program_id(0), pl.program_id(1)
    place = place_of(place_ref)
    at = pl.multiple_of(lax.rem(place + first + step * number, 4) * 128, 128)

    load = pltpu.make_async_copy(w_ref.at[:, pl.ds(HIDDEN, 512)], w_held, sem)

    @pl.when((number == 0) & (pair == 0))
    def _():
        load.start()
        dk[...] = jnp.zeros_like(dk) if dk_in is None else dk_in[...]
        dv[...] = jnp.zeros_like(dv) if dv_in is None else dv_in[...]

    @pl.when(pair == 0)
    def _():
        bias[...] = mask_of(at, low_ref)

        @pl.when(number == 0)
        def _():
            load.wait()

        for k, ref in enumerate(dh_refs):

            @pl.when(number == k)
            def _():
                do_rows = dot_nn(ref[...], w_held[...]).astype(BF16)
                for p in range(4):
                    do_held[p] = do_rows[:, 128 * p : 128 * p + 128]

    keys = pl.ds(at, KEYS)
    queries, grads, all_weights, all_grad_scores = [], [], [], []
    for k in range(PAIRS):
        columns = slice(128 * k, 128 * k + 128)
        do_pair = do_held[PAIRS * pair + k]
        query, grad = both_heads(q_ref[:, columns]), both_heads(do_pair)
        scores = dot_nt(kk_ref[keys, :], query) + bias[...]
        weights = jnp.exp(scores - lse_ref[0, k])
        grad_weights = dot_nt(vv_ref[keys, :], grad)
        product = (o_ref[:, columns].astype(F32) * do_pair.astype(F32)).T
        inner = jnp.concatenate(
            [jnp.sum(product[:64], 0, keepdims=True), jnp.sum(product[64:], 0, keepdims=True)], 1
        )
        grad_scores = (weights * (grad_weights - inner)).astype(BF16)
        grad_query = side_by_side(dot_nn(kvt_ref[0:64, keys], grad_scores)) * HEAD_SIZE**-0.5
        dq_ref[:, columns] = turn(grad_query, cos_ref[...], -sin_ref[...]).astype(BF16)
        queries.append(query)
        grads.append(grad)
        all_weights.append(weights.astype(BF16))
        all_grad_scores.append(grad_scores)
    join = lambda values, axis: values[0] if PAIRS == 1 else jnp.concatenate(values, axis)
    dv[keys, :] += dot_nn(join(all_weights, 1), join(grads, 0))
    dk[keys, :] += dot_nn(join(all_grad_scores, 1), join(queries, 0))

    @pl.when((number == pl.num_programs(0) - 1) & (pair == 4 // PAIRS - 1))
    def _():
        if not last:
            outs[0][...], outs[1][...] = dk[...], dv[...]
            return
        half = lane_is_low((128, 128), 128)
        for block in range(3):
            for group in range(4):
                to = pl.multiple_of(lax.rem(group - place + 4, 4) * 128, 128)
                frm = slice(block * 512 + group * 128, block * 512 + group * 128 + 128)
                key, value = dk[frm, :], dv[frm, :]
                key = key + pltpu.roll(key, 64, 1)
                value = value + pltpu.roll(value, 64, 1)
                both = jnp.where(half, key, value)
                outs[block][pl.ds(to, 128), :] = both.astype(outs[block].dtype)


def attend_back(first, step, count, place, queries, o, dh, weights, lse, kk, vv, kvt, low, cosine, sine, held):
    last = first == 2
    whole = lambda g, p, s: (0, 0)
    specs = [
        pl.BlockSpec((128, 128 * PAIRS), lambda g, p, s: (first + step * g, p)),
        pl.BlockSpec(memory_space=pl.ANY),
        pl.BlockSpec((1, PAIRS, 1, 256), lambda g, p, s: (g, p, 0, 0)),
        pl.BlockSpec((1536, 128), whole),
        pl.BlockSpec((1536, 128), whole),
        pl.BlockSpec((128, 1536), whole),
        pl.BlockSpec((1, 512), whole),
        pl.BlockSpec((128, 128), lambda g, p, s: (first + step * g, 0)),
        pl.BlockSpec((128, 128), lambda g, p, s: (first + step * g, 0)),
    ]
    specs += [pl.BlockSpec((128, 128 * PAIRS), lambda g, p, s: (g, p))]
    specs += [pl.BlockSpec((128, 2048), whole)] * count + [pl.BlockSpec((1536, 128), whole)] * len(held)
    if last:
        out_specs = (pl.BlockSpec((512, 128), whole),) * 3
        out_shape = tuple(jax.ShapeDtypeStruct((512, 128), dtype) for dtype in (BF16, BF16, F32))
    else:
        out_specs = (pl.BlockSpec((1536, 128), whole),) * 2
        out_shape = (jax.ShapeDtypeStruct((1536, 128), F32),) * 2
    grid = pltpu.PrefetchScalarGridSpec(
        num_scalar_prefetch=1,
        grid=(count, 4 // PAIRS),
        in_specs=specs,
        out_specs=(pl.BlockSpec((128, 128 * PAIRS), lambda g, p, s: (g, p)),) + out_specs,
        scratch_shapes=[
            pltpu.VMEM((KEYS, 256), F32),
            pltpu.VMEM((4, 128, 128), BF16),
            pltpu.VMEM((1536, 128), F32),
            pltpu.VMEM((1536, 128), F32),
            pltpu.VMEM((2048, 512), BF16),
            pltpu.SemaphoreType.DMA,
        ],
    )
    return pl.pallas_call(
        functools.partial(attend_back_kernel, first, step, count),
        grid_spec=grid,
        out_shape=(jax.ShapeDtypeStruct((128 * count, 512), BF16),) + out_shape,
        compiler_params=pltpu.CompilerParams(vmem_limit_bytes=VMEM_LIMIT),
        cost_estimate=pl.CostEstimate(
            flops=count * 4 * KEYS * 256 * 640 * 2,
            bytes_accessed=6 * 1024 * 1024,
            transcendentals=count * 4 * KEYS * 256,
        ),
    )(place, queries, weights, lse, kk, vv, kvt, low, cosine, sine, o, *dh, *held)


GROUPS = [(0, 128), (128, 256), (384, 512), (896, 512)]


def columns_times_kernel(left_ref, right_ref, out_ref, left, right, out, sems, out_sems):
    load = pltpu.make_async_copy(left_ref, left, sems.at[len(GROUPS)])
    load.start()
    copies, results = [], []
    for number, (start, width) in enumerate(GROUPS):
        columns = pl.ds(start, width)
        copy = pltpu.make_async_copy(right_ref.at[:, columns], right.at[:, columns], sems.at[number])
        copy.start()
        copies.append(copy)
    load.wait()
    value = left[...]
    for number, (start, width) in enumerate(GROUPS):
        copies[number].wait()
        out[:, start : start + width] = dot_nn(value, right[:, start : start + width])
        columns = pl.ds(start, width)
        copy = pltpu.make_async_copy(out.at[:, columns], out_ref.at[:, columns], out_sems.at[number])
        copy.start()
        results.append(copy)
    for copy in results:
        copy.wait()


def columns_times(left, right):
    rows, width = left.shape
    anywhere = pl.BlockSpec(memory_space=pl.ANY)
    return pl.pallas_call(
        columns_times_kernel,
        out_shape=jax.ShapeDtypeStruct((rows, HIDDEN), F32),
        in_specs=[anywhere, anywhere],
        out_specs=anywhere,
        scratch_shapes=[
            pltpu.VMEM((rows, width), BF16),
            pltpu.VMEM((width, HIDDEN), BF16),
            pltpu.VMEM((rows, HIDDEN), F32),
            pltpu.SemaphoreType.DMA((len(GROUPS) + 1,)),
            pltpu.SemaphoreType.DMA((len(GROUPS),)),
        ],
        compiler_params=pltpu.CompilerParams(vmem_limit_bytes=VMEM_LIMIT),
        cost_estimate=pl.CostEstimate(
            flops=2 * rows * width * HIDDEN, bytes_accessed=11 * 1024 * 1024, transcendentals=0
        ),
    )(left, right)


PIECES = [(0, 128), (128, 128), (256, 128), (384, 128)]


def ffn_kernel(*refs):
    core_ref, x_refs, dact_ref, w_ref = refs[0], refs[1:9], refs[9], refs[10]
    gua_ref, whole_ref, swap_ref, dx_refs = refs[11], refs[12], refs[13], refs[14:18]
    x_held, dact_held, w_held, gua, dx, sems, out_sems = refs[18:]
    x_copies = []
    for number in range(8):
        copy = pltpu.make_async_copy(
            x_refs[number], x_held.at[pl.ds(64 * number, 64)], sems.at[12 + number]
        )
        copy.start()
        x_copies.append(copy)
    copies = []
    for number, (start, width) in enumerate(GROUPS):
        for part in range(3):
            if part < 2:
                columns = pl.ds(part * HIDDEN + start, width)
                copy = pltpu.make_async_copy(
                    w_ref.at[:, columns], w_held.at[:, columns], sems.at[3 * number + part]
                )
            else:
                columns = pl.ds(start, width)
                copy = pltpu.make_async_copy(
                    dact_ref.at[:, columns], dact_held.at[:, columns], sems.at[3 * number + part]
                )
            copy.start()
            copies.append(copy)
    for copy in x_copies:
        copy.wait()
    half = pl.multiple_of((1 - core_of(core_ref)) * 1024, 1024)
    results = [
        pltpu.make_async_copy(x_held, whole_ref, out_sems.at[5]),
        pltpu.make_async_copy(x_held.at[:, pl.ds(half, 1024)], swap_ref, out_sems.at[6]),
    ]
    for copy in results:
        copy.start()
    x = x_held[...]
    for number, (start, width) in enumerate(GROUPS):
        for part in range(3):
            copies[3 * number + part].wait()
        gate = dot_nn(x, w_held[:, start : start + width])
        up = dot_nn(x, w_held[:, HIDDEN + start : HIDDEN + start + width])
        dact = dact_held[:, start : start + width]
        sig = jax.nn.sigmoid(gate)
        silu = gate * sig
        dgate = dact * up * (sig * (1.0 + gate * (1.0 - sig)))
        gua[:, start : start + width] = dgate.astype(BF16)
        gua[:, HIDDEN + start : HIDDEN + start + width] = (dact * silu).astype(BF16)
        gua[:, 2 * HIDDEN + start : 2 * HIDDEN + start + width] = (silu * up).astype(BF16)
    copy = pltpu.make_async_copy(gua, gua_ref, out_sems.at[4])
    copy.start()
    results.append(copy)
    dgu = gua[:, : 2 * HIDDEN]
    for number in range(4):
        columns = slice(512 * number, 512 * number + 512)
        dx[:, columns] = dot_nt(dgu, w_held[columns, : 2 * HIDDEN]).astype(BF16)
        for piece, (start, size) in enumerate(PIECES):
            copy = pltpu.make_async_copy(
                dx.at[pl.ds(start, size), pl.ds(512 * number, 512)],
                dx_refs[piece].at[:, pl.ds(512 * number, 512)],
                out_sems.at[7 + 4 * number + piece],
            )
            copy.start()
            results.append(copy)
    for copy in results:
        copy.wait()


def ffn(core, pieces, dact, weights):
    rows, width = dact.shape[0], weights.shape[0]
    anywhere = pl.BlockSpec(memory_space=pl.ANY)
    result = pl.pallas_call(
        ffn_kernel,
        out_shape=(
            jax.ShapeDtypeStruct((rows, 3 * HIDDEN), BF16),
            jax.ShapeDtypeStruct((rows, width), BF16),
            jax.ShapeDtypeStruct((rows, width // 2), BF16),
            *(jax.ShapeDtypeStruct((size, width), BF16) for _, size in PIECES),
        ),
        in_specs=[pl.BlockSpec(memory_space=pltpu.SMEM)] + [anywhere] * 10,
        out_specs=(anywhere,) * 7,
        scratch_shapes=[
            pltpu.VMEM((rows, width), BF16),
            pltpu.VMEM((rows, HIDDEN), F32),
            pltpu.VMEM((width, 2 * HIDDEN), BF16),
            pltpu.VMEM((rows, 3 * HIDDEN), BF16),
            pltpu.VMEM((rows, width), BF16),
            pltpu.SemaphoreType.DMA((20,)),
            pltpu.SemaphoreType.DMA((23,)),
        ],
        compiler_params=pltpu.CompilerParams(vmem_limit_bytes=VMEM_LIMIT),
        cost_estimate=pl.CostEstimate(
            flops=8 * rows * width * HIDDEN,
            bytes_accessed=25 * 1024 * 1024,
            transcendentals=rows * HIDDEN,
        ),
    )(core, *pieces, dact, weights)
    return result[0], result[1], result[2], result[3:]


def weight_grads_kernel(core_ref, x_ref, x2_ref, dy_ref, dy2_ref, right_ref, right2_ref, out_ref, dy, dy2, sems):
    part = pl.program_id(0)
    half = dy.shape[1]
    start = pl.multiple_of(core_of(core_ref) * half, half)
    loads = (
        pltpu.make_async_copy(dy_ref.at[:, pl.ds(start, half)], dy, sems.at[0]),
        pltpu.make_async_copy(dy2_ref, dy2, sems.at[1]),
    )

    @pl.when(part == 0)
    def _():
        for load in loads:
            load.start()

    @pl.when(part < 2)
    def _():
        total = dot_tn(x_ref[...], right_ref[...]) + dot_tn(x2_ref[...], right2_ref[...])
        out_ref[...] = total.astype(BF16)

    @pl.when(part == 2)
    def _():
        for load in loads:
            load.wait()
        total = dot_tn(dy[...], right_ref[...]) + dot_tn(dy2[...], right2_ref[...])
        out_ref[...] = total.astype(BF16)


def weight_grads(core, x, x2, dy, dy2, right, right2):
    rows, half = x2.shape
    anywhere = pl.BlockSpec(memory_space=pl.ANY)
    side = lambda j, c: (0, j)
    grid = pltpu.PrefetchScalarGridSpec(
        num_scalar_prefetch=1,
        grid=(3,),
        in_specs=[
            pl.BlockSpec((rows, half), lambda j, c: (0, core_of(c))),
            pl.BlockSpec((rows, half), lambda j, c: (0, 0)),
            anywhere,
            anywhere,
            pl.BlockSpec((rows, HIDDEN), side),
            pl.BlockSpec((rows, HIDDEN), side),
        ],
        out_specs=pl.BlockSpec((half, HIDDEN), side),
        scratch_shapes=[
            pltpu.VMEM((rows, half), BF16),
            pltpu.VMEM((rows, half), BF16),
            pltpu.SemaphoreType.DMA((2,)),
        ],
    )
    return pl.pallas_call(
        weight_grads_kernel,
        grid_spec=grid,
        out_shape=jax.ShapeDtypeStruct((half, 3 * HIDDEN), BF16),
        compiler_params=pltpu.CompilerParams(vmem_limit_bytes=VMEM_LIMIT),
        cost_estimate=pl.CostEstimate(
            flops=2 * 3 * 2 * rows * half * HIDDEN, bytes_accessed=24 * 1024 * 1024, transcendentals=0
        ),
    )(core, x, x2, dy, dy2, right, right2)


def rows_times_kernel(left_ref, right_ref, *out_refs):
    result = dot_nt(left_ref[...], right_ref[...]).astype(BF16)
    for number, ref in enumerate(out_refs):
        ref[...] = result[128 * number : 128 * number + 128]


def rows_times(left, left_part, right, part):
    rows, depth = left.shape[0], HIDDEN
    width = right.shape[0]
    tile = 512
    return pl.pallas_call(
        rows_times_kernel,
        out_shape=(jax.ShapeDtypeStruct((128, width), BF16),) * 4,
        grid=(width // tile,),
        in_specs=[
            pl.BlockSpec((rows, depth), lambda i: (0, left_part)),
            pl.BlockSpec((tile, depth), lambda i: (i, part)),
        ],
        out_specs=(pl.BlockSpec((128, tile), lambda i: (0, i)),) * 4,
        compiler_params=pltpu.CompilerParams(vmem_limit_bytes=VMEM_LIMIT),
        cost_estimate=pl.CostEstimate(
            flops=2 * rows * depth * width,
            bytes_accessed=2 * (rows * depth + width * depth + rows * width),
            transcendentals=0,
        ),
    )(left, right)


def ring_rows(own, near, far):
    return jnp.concatenate([own, near[:128], far, near[128:]], 0)


def put_half(number, value, other_ref, own_ref):
    @pl.when(number < 2)
    def _():
        other_ref[...] = value

    @pl.when(number >= 2)
    def _():
        own_ref[...] = value


def tile_at(i, c):
    return lax.rem(i + 2 * (1 - core_of(c)), 4)


def half_specs(tile, columns):
    return (
        pl.BlockSpec((tile, columns), lambda i, c: (jnp.minimum(i, 1), 0)),
        pl.BlockSpec((tile, columns), lambda i, c: (jnp.maximum(i - 2, 0), 0)),
    )


def wide_grads_kernel(
    core_ref, x_ref, dh0, dh1, dh2, dh3, o0, o1, o2, dq0, dq1, dq2, other_ref, own_ref, o_held, dq_held
):
    number = pl.program_id(0)

    @pl.when(number == 0)
    def _():
        o_held[...] = ring_rows(o0[...], o1[...], o2[...])
        dq_held[...] = ring_rows(dq0[...], dq1[...], dq2[...])

    dh = jnp.concatenate([ref[...] for ref in (dh0, dh1, dh2, dh3)], 0)
    out = dot_tn(dh, o_held[...])
    query = dot_tn(x_ref[...], dq_held[...])
    put_half(number, jnp.concatenate([out, query], 1).astype(BF16), other_ref, own_ref)


def wide_grads(core, normed, dh, o, dq):
    rows, width = normed.shape
    tile = 512
    whole = lambda i, c: (0, 0)
    column = lambda i, c: (0, tile_at(i, c))
    small = [pl.BlockSpec((size, 512), whole) for size in (128, 256, 128)]
    grid = pltpu.PrefetchScalarGridSpec(
        num_scalar_prefetch=1,
        grid=(4,),
        in_specs=[pl.BlockSpec((rows, tile), column)]
        + [pl.BlockSpec((128, tile), column)] * 4
        + small
        + small,
        out_specs=half_specs(tile, 1024),
        scratch_shapes=[pltpu.VMEM((rows, 512), BF16), pltpu.VMEM((rows, 512), BF16)],
    )
    return pl.pallas_call(
        wide_grads_kernel,
        grid_spec=grid,
        out_shape=(jax.ShapeDtypeStruct((width // 2, 1024), BF16),) * 2,
        compiler_params=pltpu.CompilerParams(vmem_limit_bytes=VMEM_LIMIT),
        cost_estimate=pl.CostEstimate(
            flops=2 * rows * width * 1024, bytes_accessed=10 * 1024 * 1024, transcendentals=0
        ),
    )(core, normed, *dh, *o, *dq)


def finish_kernel(
    core_ref,
    x_ref,
    w_ref,
    dq0_ref,
    dq1_ref,
    dq2_ref,
    own_ref,
    one_ref,
    two_ref,
    cos_ref,
    sin_ref,
    norm_ref,
    second_ref,
    other_grad_ref,
    own_grad_ref,
    dx_ref,
    gain_ref,
    dqkv,
    sums,
):
    number = pl.program_id(0)

    @pl.when(number == 0)
    def _():
        dqkv[:, :512] = ring_rows(dq0_ref[...], dq1_ref[...], dq2_ref[...])
        dkv = own_ref[...] + one_ref[...].astype(F32) + two_ref[...].astype(F32)
        turned = turn(dkv, cos_ref[...], -sin_ref[...])
        dqkv[:, 512:] = jnp.where(lane_is_low(dkv.shape, 128), turned, dkv).astype(BF16)

    x = x_ref[...]
    put_half(number, dot_tn(x, dqkv[:, 512:]).astype(BF16), other_grad_ref, own_grad_ref)
    dx = dot_nt(dqkv[...], w_ref[...])
    for piece in range(4):
        row = pl.multiple_of(lax.rem(place_of(core_ref) + piece, 4) * 128, 128)
        dx_ref[pl.ds(row, 128), :] = dx[128 * piece : 128 * piece + 128].astype(BF16)
    columns = pl.ds(pl.multiple_of(tile_at(number, core_ref) * 512, 512), 512)
    sums[:, columns] = jnp.broadcast_to(
        jnp.sum(dx * x.astype(F32), 0, keepdims=True) / norm_ref[:1], (8, 512)
    )

    @pl.when(number == 3)
    def _():
        gain_ref[:8] = gain_rows(to_blocks(sums[...])[:1])
        gain_ref[8:] = gain_rows(second_ref[:1])


def finish(core, normed, weights, dq, own, one, two, cosine, sine, gain, second):
    rows, width = normed.shape
    tile = 512
    whole = lambda i, c: (0, 0)
    column = lambda i, c: (0, tile_at(i, c))
    narrow = pl.BlockSpec((rows, 128), whole)
    grid = pltpu.PrefetchScalarGridSpec(
        num_scalar_prefetch=1,
        grid=(4,),
        in_specs=[
            pl.BlockSpec((rows, tile), column),
            pl.BlockSpec((tile, 640), lambda i, c: (tile_at(i, c), 0)),
            pl.BlockSpec((128, 512), whole),
            pl.BlockSpec((256, 512), whole),
            pl.BlockSpec((128, 512), whole),
            narrow,
            narrow,
            narrow,
            narrow,
            narrow,
            pl.BlockSpec((2, tile), column),
            pl.BlockSpec((8, width), whole),
        ],
        out_specs=half_specs(tile, 128)
        + (pl.BlockSpec((rows, tile), column),)
        + (pl.BlockSpec((GAIN_ROWS, GAIN_COLUMNS), whole),),
        scratch_shapes=[pltpu.VMEM((rows, 640), BF16), pltpu.VMEM((8, width), F32)],
    )
    result = pl.pallas_call(
        finish_kernel,
        grid_spec=grid,
        out_shape=(jax.ShapeDtypeStruct((width // 2, 128), BF16),) * 2
        + (jax.ShapeDtypeStruct((rows, width), BF16),)
        + (jax.ShapeDtypeStruct((GAIN_ROWS, GAIN_COLUMNS), F32),),
        compiler_params=pltpu.CompilerParams(vmem_limit_bytes=VMEM_LIMIT),
        cost_estimate=pl.CostEstimate(
            flops=2 * rows * width * 768, bytes_accessed=10 * 1024 * 1024, transcendentals=0
        ),
    )(core, normed, weights, *dq, own, one, two, cosine, sine, gain, second)
    return result


def per_device(
    tokens,
    segments,
    w_query,
    key_projection,
    value_projection,
    w_out,
    w_gate,
    w_up,
    w_down,
    norm_attn,
    norm_ffn,
    cotangent,
):
    place, core = lax.axis_index("head"), lax.axis_index("core")
    block = (lax.axis_index("y") * 4 + lax.axis_index("x")) * 2 + core
    code = (((lax.axis_index("x") * 4 + lax.axis_index("y")) * 2 + core) * 4 + place).astype(jnp.int32)
    code = code.reshape(1)
    keep = lax.optimization_barrier


    out_weights = lax.all_gather(
        jnp.concatenate([w_down.T, w_out.T], 1), CORE_FIRST, axis=0, tiled=True
    )
    ffn_weights = lax.all_gather(jnp.concatenate([w_gate, w_up], 1), CORE_FIRST, axis=0, tiled=True)

    x_rows, dy_rows, normed_rows, gains = prepare(
        tokens[0], cotangent[0], jnp.stack([norm_attn, norm_ffn]).astype(F32)
    )
    row = jnp.arange(512, dtype=jnp.int32)
    positions = block * 512 + ((row // 128 + place) % 4) * 128 + row % 128
    frequency = 10000.0 ** (-jnp.arange(32, dtype=F32) * 2.0 / HEAD_SIZE)
    angles = positions.astype(F32)[:, None] * frequency[None, :]
    cosine, sine = jnp.cos(angles), jnp.sin(angles)
    cosine = jnp.concatenate([cosine] * 4, 1)
    sine = jnp.concatenate([-sine, sine, -sine, sine], 1)

    flat = segments.reshape(-1)
    padded = jnp.concatenate([jnp.full((1024,), -1, jnp.int32), flat])
    own = lax.dynamic_slice_in_dim(flat, block * 512, 512, 0)
    window = lax.dynamic_slice_in_dim(padded, block * 512, 1536, 0)
    start = jnp.sum((window[None, :] < own[:, None]).astype(jnp.int32), 1)
    low = jnp.maximum(start, row + 1).reshape(1, 512)

    normed_rows, w_query = keep((normed_rows, w_query))
    ahead, behind = near_pieces(normed_rows)
    qkv_own = gather_axis(jnp.concatenate([w_query, key_projection, value_projection], 1), "x")
    qkv_own = gather_axis(jnp.concatenate(qkv_own, 0), "y")
    far = far_pieces(ahead, behind)
    qkv_own, far, cosine, sine, low = keep((qkv_own, far, cosine, sine, low))
    qkv_pieces = *qkv_own, *(shift(piece, "core", 1) for piece in qkv_own)
    kv_own, normed_one = project_kv(code, (normed_rows, ahead, *far, behind), qkv_pieces, cosine, sine)
    normed_late, kv_own, dy_raw = keep((normed_one, kv_own, cotangent[0]))
    dy_pieces = gather_pieces(dy_raw)
    kv = (from_block(kv_own, 2), from_block(kv_own, 1), kv_own)
    queries, qkv_weights = project_q(code, normed_late, qkv_pieces, cosine, sine)

    kk, vv, kvt = set_up(code, kv)
    seen = code, queries, kk, kvt, low, out_weights
    o_far, lse_far, part_far = attend(2, 1, 1, *seen)
    queries, part_far, dy_pieces = keep((queries, part_far, dy_pieces))
    part_far = shift(part_far, "head", 2)
    seen = code, queries, kk, kvt, low, out_weights
    o_near, lse_near, part_ahead, part_behind = attend(1, 2, 2, *seen)
    queries, part_far, part_ahead, part_behind = keep((queries, part_far, part_ahead, part_behind))
    seen = code, queries, kk, kvt, low, out_weights
    o_own, lse_own, part_own = attend(0, 1, 1, *seen)
    dy, dy_swap = assemble(code, dy_rows, *dy_pieces)
    dy_other = shift(dy_swap, "core", 1)
    attention_sum = part_own, shift(part_ahead, "head", 1), shift(part_behind, "head", -1), part_far
    h1, top, bottom = join(x_rows, gains, attention_sum)
    behind_top, ahead_bottom = shift(top, "head", 1), shift(bottom, "head", -1)
    ahead_top, behind_bottom = shift(top, "head", -1), shift(bottom, "head", 1)
    behind_top, ahead_bottom, dy = keep((behind_top, ahead_bottom, dy))
    far_top, far_bottom = shift(behind_top, "head", 1), shift(ahead_bottom, "head", -1)
    rows_two = top, bottom, ahead_top, ahead_bottom, far_top, far_bottom, behind_top, behind_bottom
    dact = columns_times(dy, out_weights)
    dact, dy_other = keep((dact, dy_other))

    gua, normed_two, normed_two_swap, dnormed_two = ffn(
        code, rows_two, dact, ffn_weights
    )
    dnormed_two = scatter_pieces(*dnormed_two)
    gua_other = shift(gua, "core", 1)
    normed_two_other = shift(normed_two_swap, "core", 1)
    out_pieces = rows_times(gua, 2, out_weights, 0)
    gua_other, normed_two_other, out_pieces = keep((gua_other, normed_two_other, out_pieces))
    held = weight_grads(code, normed_two, normed_two_other, dy, dy_other, gua, gua_other)
    held, dnormed_two = keep((held, dnormed_two))
    grads = lax.psum_scatter(held, ("y", "x"), scatter_dimension=0, tiled=True)

    dh1, dh1_low, grad_gain_two = join_back(h1, dy_rows, gains, dnormed_two)
    back = kk, vv, kvt, low, cosine, sine
    dq_own, dk, dv = attend_back(0, 1, 1, code, queries, o_own, (dh1_low,), out_weights, lse_own, *back, ())
    ahead, behind = shift(dh1_low, "head", -1), shift(dh1_low, "head", 1)
    ahead, behind, dk, dv, dh1_late, out_pieces = keep((ahead, behind, dk, dv, dh1_low, out_pieces))
    far = shift(dh1_late, "head", 2)
    dq_near, dk, dv = attend_back(
        1, 2, 2, code, queries, o_near, (ahead, behind), out_weights, lse_near, *back, (dk, dv)
    )
    far, dk, dv, out_pieces = keep((far, dk, dv, out_pieces))
    out_pieces = scatter_pieces(*out_pieces)
    dq_far, dkv_first, dkv_second, dkv_own = attend_back(
        2, 1, 1, code, queries, o_far, (far,), out_weights, lse_far, *back, (dk, dv)
    )
    dq = dq_own, dq_near, dq_far
    dkv_one = from_block(dkv_second, -1)
    dkv_two = from_block(dkv_first, -2)
    wide_other, wide_own = wide_grads(
        code, normed_one, (dh1_low, ahead, far, behind), (o_own, o_near, o_far), dq
    )
    dkv_one, dkv_two, wide_other, out_pieces = keep((dkv_one, dkv_two, wide_other, out_pieces))
    wide_other = shift(wide_other, "core", 1)

    narrow_other, narrow_own, dnormed_one, gain_grads = finish(
        code,
        normed_one,
        qkv_weights,
        dq,
        dkv_own,
        dkv_one,
        dkv_two,
        cosine,
        sine,
        gains,
        grad_gain_two,
    )
    dnormed_one = lax.psum_scatter(dnormed_one, "head", scatter_dimension=0, tiled=True)
    gain_grads = exchange([gain_grads] * 4, "head")
    rows = [(x_rows.shape, BF16)]
    (output,) = small_call(output_kernel, rows, h1, *out_pieces)
    gain_grads, output = keep((gain_grads, output))
    pieces, out_sums = first_pieces(
        code, wide_own, wide_other, narrow_own, shift(narrow_other, "core", 1), gain_grads
    )
    grads = (
        grads[:, :HIDDEN].astype(F32),
        grads[:, HIDDEN : 2 * HIDDEN].astype(F32),
        grads[:, 2 * HIDDEN :].T.astype(F32),
    )
    pieces, out_sums, grads = keep((exchange(pieces, "x"), exchange(out_sums, "y"), grads))
    pieces, out_sums = second_pieces(code, pieces, out_sums)
    pieces, out_sums = exchange(pieces, "y"), exchange(out_sums, "x")
    (gain_grads,) = small_call(gains_kernel, [((GAIN_ROWS, GAIN_COLUMNS), F32)], *pieces)
    gain_grads, dnormed_one, out_sums = keep((gain_grads, dnormed_one, out_sums))
    gain_grads_other = shift(gain_grads, "core", 1)
    (grad_inputs,) = small_call(input_grad_kernel, rows, dh1, x_rows, gains, dnormed_one)
    gain_grads_other, grad_inputs = keep((gain_grads_other, grad_inputs))
    columns = (64, 512), (64, 512), (64, 64), (64, 64), (1, 2048), (1, 2048)
    grad_out, grad_query, grad_key, grad_value, grad_gain_one, grad_gain_two = small_call(
        attention_grads_kernel,
        [(shape, F32) for shape in columns],
        *pieces,
        *out_sums,
        gain_grads,
        gain_grads_other,
    )

    return (
        output[None],
        grad_inputs[None],
        grad_query,
        grad_key,
        grad_value,
        grad_out.T,
        *grads,
        grad_gain_one.reshape(2048),
        grad_gain_two.reshape(2048),
    )


def solution(mesh):
    grid = Mesh(mesh.devices.reshape(4, 4, 4, 2), ("head", "y", "x", "core"))
    rows, up, down = P(BLK, "head", None), P(BLK, "head"), P("head", BLK)
    return jax.shard_map(
        per_device,
        mesh=grid,
        in_specs=(rows, P(), up, up, up, down, up, up, down, P(), P(), rows),
        out_specs=(rows, rows, up, up, up, down, up, up, down, P(), P()),
        check_vma=False,
    )
```

```python
import functools

import jax
import jax.numpy as jnp
from jax import lax
from jax.experimental import pallas as pl
from jax.experimental.pallas import tpu as pltpu
from jax.sharding import Mesh
from jax.sharding import PartitionSpec as P

HEAD_SIZE = 64
WINDOW = 1024
HIDDEN = 1408
EPSILON = 1e-05
BF16 = jnp.bfloat16
F32 = jnp.float32
BLK = ("y", "x", "core")
CORE_FIRST = ("core", "y", "x")
VMEM_LIMIT = 63 * 1024 * 1024


def dot_nn(a, b):
    return jnp.dot(a, b, preferred_element_type=F32)


def dot_nt(a, b):
    return lax.dot_general(a, b, (((1,), (1,)), ((), ())), preferred_element_type=F32)


def dot_tn(a, b):
    return lax.dot_general(a, b, (((0,), (0,)), ((), ())), preferred_element_type=F32)


def shift(value, axis, distance):
    size = lax.axis_size(axis)
    return lax.ppermute(value, axis, [(i, (i + distance) % size) for i in range(size)])


def add_low(a, b):
    return (a.astype(F32) + b.astype(F32)).astype(BF16)


def gather_pieces(rows):
    return shift(rows, "head", -1), shift(rows, "head", 2), shift(rows, "head", 1)


def near_pieces(rows):
    return shift(rows, "head", -1), shift(rows, "head", 1)


def far_pieces(ahead, behind):
    half = ahead.shape[0] // 2
    return shift(behind[:half], "head", 1), shift(ahead[half:], "head", -1)


def scatter_pieces(own, ahead, far, behind):
    return own, shift(ahead, "head", 1), shift(behind, "head", -1), shift(far, "head", 2)


def gather_axis(value, axis):
    return value, shift(value, axis, -1), shift(value, axis, 2), shift(value, axis, 1)


def exchange(pieces, axis):
    return pieces[0], shift(pieces[1], axis, 1), shift(pieces[2], axis, 2), shift(pieces[3], axis, -1)


def from_block(value, distance):
    route = [(i, i + distance) for i in range(32) if 0 <= i + distance < 32]
    return lax.ppermute(value, BLK, route)


def scale_of(values):
    return lax.rsqrt(jnp.mean(values * values, -1, keepdims=True) + EPSILON)


def x_of(code):
    return lax.shift_right_logical(code[0], 5)


def y_of(code):
    return lax.shift_right_logical(code[0], 3) & 3


def core_of(code):
    return lax.shift_right_logical(code[0], 2) & 1


def place_of(code):
    return code[0] & 3


def lane_is_low(shape, period):
    return lax.broadcasted_iota(jnp.int32, shape, len(shape) - 1) % period < period // 2


def turn(values, cosine, sine):
    swapped = jnp.where(
        lane_is_low(values.shape, 64), pltpu.roll(values, 96, 1), pltpu.roll(values, 32, 1)
    )
    return values * cosine + swapped * sine


def core_major_tiles(tiles):
    low = lane_is_low(tiles[0].shape, 128)
    rolled = [pltpu.roll(tile, 64, 1) for tile in tiles]
    first = [jnp.where(low, tiles[2 * k], rolled[2 * k + 1]) for k in range(8)]
    second = [jnp.where(low, rolled[2 * k], tiles[2 * k + 1]) for k in range(8)]
    return first + second


def block_major_tiles(tiles):
    low = lane_is_low(tiles[0].shape, 128)
    rolled = [pltpu.roll(tile, 64, 1) for tile in tiles]
    result = []
    for k in range(8):
        result.append(jnp.where(low, tiles[k], rolled[8 + k]))
        result.append(jnp.where(low, rolled[k], tiles[8 + k]))
    return result


def in_tiles(value):
    return [value[:, 128 * k : 128 * k + 128] for k in range(16)]


def prepare_kernel(x_ref, dy_ref, gain_ref, x_out, dy_out, normed_out, gain_out):
    def convert(ref):
        return jnp.concatenate(core_major_tiles(in_tiles(ref[...].astype(F32))), 1)

    x, gains = convert(x_ref), convert(gain_ref)
    gain_out[...] = gains
    x_out[...] = x
    dy_out[...] = convert(dy_ref).astype(BF16)
    normed_out[...] = (x * scale_of(x) * gains[:1]).astype(BF16)


def prepare(x, dy, gains):
    rows, width = x.shape
    return pl.pallas_call(
        prepare_kernel,
        out_shape=(
            jax.ShapeDtypeStruct((rows, width), F32),
            jax.ShapeDtypeStruct((rows, width), BF16),
            jax.ShapeDtypeStruct((rows, width), BF16),
            jax.ShapeDtypeStruct(gains.shape, F32),
        ),
        compiler_params=pltpu.CompilerParams(vmem_limit_bytes=VMEM_LIMIT),
        cost_estimate=pl.CostEstimate(
            flops=10 * rows * width, bytes_accessed=10 * rows * width, transcendentals=rows
        ),
    )(x, dy, gains)


def to_blocks(value):
    return jnp.concatenate(block_major_tiles(in_tiles(value)), 1)


def assemble_kernel(core_ref, own_ref, ahead_ref, far_ref, behind_ref, out_ref, swap_ref):
    out_ref[:128] = own_ref[...]
    start = 128
    for ref in (ahead_ref, far_ref, behind_ref):
        size = ref.shape[0]
        out_ref[start : start + size] = jnp.concatenate(
            core_major_tiles(in_tiles(ref[...].astype(F32))), 1
        ).astype(BF16)
        start += size
    swap_ref[...] = jnp.where(core_of(core_ref) == 0, out_ref[:, 1024:], out_ref[:, :1024])


def assemble(core, own, ahead, far, behind):
    vmem = pl.BlockSpec(memory_space=pltpu.VMEM)
    return pl.pallas_call(
        assemble_kernel,
        out_shape=(jax.ShapeDtypeStruct((512, 2048), BF16), jax.ShapeDtypeStruct((512, 1024), BF16)),
        in_specs=[pl.BlockSpec(memory_space=pltpu.SMEM)] + [vmem] * 4,
        out_specs=(vmem, vmem),
        compiler_params=pltpu.CompilerParams(vmem_limit_bytes=VMEM_LIMIT),
        cost_estimate=pl.CostEstimate(
            flops=4 * 512 * 2048, bytes_accessed=5 * 1024 * 1024, transcendentals=0
        ),
    )(core, own, ahead, far, behind)


def small_call(kernel, out_shape, *operands):
    return pl.pallas_call(
        kernel,
        out_shape=tuple(jax.ShapeDtypeStruct(shape, dtype) for shape, dtype in out_shape),
        compiler_params=pltpu.CompilerParams(vmem_limit_bytes=VMEM_LIMIT),
        cost_estimate=pl.CostEstimate(
            flops=sum(x.size for x in operands),
            bytes_accessed=2 * sum(x.size * x.dtype.itemsize for x in operands),
            transcendentals=0,
        ),
    )(*operands)


def total_of(refs):
    values = [ref[...].astype(F32) for ref in refs]
    while len(values) > 1:
        values = [values[0] + values[1]] + values[2:]
    return values[0]


def join_kernel(x_ref, gain_ref, a_ref, b_ref, c_ref, d_ref, h_out, top_out, bottom_out):
    h = x_ref[...] + total_of((a_ref, b_ref, c_ref, d_ref))
    h_out[...] = h
    normed = (h * scale_of(h) * gain_ref[1:2]).astype(BF16)
    half = h.shape[0] // 2
    top_out[...], bottom_out[...] = normed[:half], normed[half:]


def join(x, gain, pieces):
    half = x.shape[0] // 2, x.shape[1]
    return small_call(join_kernel, ((x.shape, F32), (half, BF16), (half, BF16)), x, gain, *pieces)


def norm_backward(values, gain, grad):
    scale = scale_of(values)
    weighted = grad * gain
    inner = jnp.mean(weighted * values, -1, keepdims=True)
    return scale * weighted - values * (scale * scale * scale * inner), scale


def join_back_kernel(h_ref, dy_ref, gain_ref, a_ref, b_ref, c_ref, d_ref, dh_out, low_out, grad_out):
    h, grad = h_ref[...], total_of((a_ref, b_ref, c_ref, d_ref))
    back, scale = norm_backward(h, gain_ref[1:2], grad)
    dh = dy_ref[...].astype(F32) + back
    dh_out[...] = dh
    low_out[...] = dh.astype(BF16)
    grad_out[...] = to_blocks(jnp.broadcast_to(jnp.sum(grad * h * scale, 0, keepdims=True), (8, h.shape[1])))


def join_back(h, dy, gain, pieces):
    shapes = (h.shape, F32), (h.shape, BF16), ((8, h.shape[1]), F32)
    return small_call(join_back_kernel, shapes, h, dy, gain, *pieces)


def output_kernel(h_ref, a_ref, b_ref, c_ref, d_ref, out_ref):
    out_ref[...] = to_blocks(h_ref[...] + total_of((a_ref, b_ref, c_ref, d_ref))).astype(BF16)


def input_grad_kernel(dh_ref, x_ref, gain_ref, grad_ref, out_ref):
    back, _ = norm_backward(x_ref[...], gain_ref[:1], grad_ref[...].astype(F32))
    out_ref[...] = to_blocks(dh_ref[...] + back).astype(BF16)


GAIN_ROWS, GAIN_COLUMNS = 16, 256


def gain_rows(vector):
    return jnp.concatenate([vector[:, 256 * k : 256 * k + 256] for k in range(8)], 0)


def put_piece(ref, rows, gains):
    count = rows.shape[0]
    ref[:count] = rows
    ref[count:, GAIN_COLUMNS:] = jnp.zeros((GAIN_ROWS, ref.shape[1] - GAIN_COLUMNS), BF16)
    ref[count:, :GAIN_COLUMNS] = gains.astype(BF16)


def first_pieces_kernel(
    at_ref, q_ref, q2_ref, kv_ref, kv2_ref, o_ref, o2_ref, *refs
):
    gain_refs, out_refs = refs[:4], refs[4:]
    query = add_low(q_ref[...], q2_ref[...]).reshape(256, 512)
    narrow = add_low(kv_ref[...], kv2_ref[...]).reshape(256, 128)
    rows = jnp.concatenate([query, narrow], 1)
    out_rows = add_low(o_ref[...], o2_ref[...]).reshape(256, 512)
    gains = total_of(gain_refs)
    for number in range(4):

        @pl.when(pl.program_id(0) == number)
        def _():
            put_piece(out_refs[number], rows, gains)
            out_refs[4 + number][...] = out_rows


def first_pieces(at, wide, wide2, narrow, narrow2, gains):
    pick_x = lambda column: lambda d, s: (0, lax.rem(x_of(s) + d, 4), 0, column)
    pick_y = lambda d, s: (lax.rem(y_of(s) + d, 4), 0, 0, 0)
    whole = lambda d, s: (0, 0)
    shaped = lambda value: value.reshape(4, 4, 64, value.shape[1])
    shapes = [(256 + GAIN_ROWS, 640)] * 4 + [(256, 512)] * 4
    grid = pltpu.PrefetchScalarGridSpec(
        num_scalar_prefetch=1,
        grid=(4,),
        in_specs=[pl.BlockSpec((4, 1, 64, 512), pick_x(1))] * 2
        + [pl.BlockSpec((4, 1, 64, 128), pick_x(0))] * 2
        + [pl.BlockSpec((1, 4, 64, 512), pick_y)] * 2
        + [pl.BlockSpec((GAIN_ROWS, GAIN_COLUMNS), whole)] * 4,
        out_specs=tuple(pl.BlockSpec(shape, whole) for shape in shapes),
    )
    wide, wide2 = shaped(wide), shaped(wide2)
    result = pl.pallas_call(
        first_pieces_kernel,
        grid_spec=grid,
        out_shape=tuple(jax.ShapeDtypeStruct(shape, BF16) for shape in shapes),
        compiler_params=pltpu.CompilerParams(vmem_limit_bytes=VMEM_LIMIT),
        cost_estimate=pl.CostEstimate(
            flops=2 * 1024 * 1152, bytes_accessed=6 * 1024 * 1152, transcendentals=0
        ),
    )(at, wide, wide2, shaped(narrow), shaped(narrow2), wide, wide2, *gains)
    return result[:4], result[4:]


def second_pieces_kernel(at_ref, *refs):
    qkv, out, (held, out_held) = refs[:4], refs[4:8], refs[16:]
    held[...] = total_of(qkv)
    out_held[...] = total_of(out).astype(BF16)
    for number in range(4):
        y = pl.multiple_of(lax.rem(y_of(at_ref) + number, 4) * 64, 64)
        put_piece(refs[8 + number], held[pl.ds(y, 64), :].astype(BF16), held[256:, :GAIN_COLUMNS])
        x = pl.multiple_of(lax.rem(x_of(at_ref) + number, 4) * 64, 64)
        refs[12 + number][...] = out_held[pl.ds(x, 64), :]


def second_pieces(at, qkv, out):
    vmem = pl.BlockSpec(memory_space=pltpu.VMEM)
    shapes = [(64 + GAIN_ROWS, 640)] * 4 + [(64, 512)] * 4
    result = pl.pallas_call(
        second_pieces_kernel,
        out_shape=tuple(jax.ShapeDtypeStruct(shape, BF16) for shape in shapes),
        in_specs=[pl.BlockSpec(memory_space=pltpu.SMEM)] + [vmem] * 8,
        out_specs=(vmem,) * 8,
        scratch_shapes=[pltpu.VMEM((256 + GAIN_ROWS, 640), F32), pltpu.VMEM((256, 512), BF16)],
        compiler_params=pltpu.CompilerParams(vmem_limit_bytes=VMEM_LIMIT),
        cost_estimate=pl.CostEstimate(
            flops=4 * 272 * 1152, bytes_accessed=10 * 272 * 1152, transcendentals=0
        ),
    )(at, *qkv, *out)
    return result[:4], result[4:]


def gains_kernel(a_ref, b_ref, c_ref, d_ref, out_ref):
    values = [ref[64:, :GAIN_COLUMNS].astype(F32) for ref in (a_ref, b_ref, c_ref, d_ref)]
    out_ref[...] = (values[0] + values[1]) + (values[2] + values[3])


def attention_grads_kernel(*refs):
    out_ref, q_ref, k_ref, v_ref, one_ref, two_ref = refs[10:]
    total = total_of(refs[:4])
    out_ref[...] = total_of(refs[4:8])
    q_ref[...] = total[:64, :512]
    k_ref[...] = total[:64, 512:576]
    v_ref[...] = total[:64, 576:]
    gains = total_of(refs[8:10])
    one_ref[...] = jnp.concatenate([gains[k : k + 1] for k in range(8)], 1)
    two_ref[...] = jnp.concatenate([gains[k : k + 1] for k in range(8, 16)], 1)


def put_in_order(at_ref, piece_refs, columns, to_ref, sems):
    x, y, core = x_of(at_ref), y_of(at_ref), core_of(at_ref)
    copies = []
    for number in range(32):
        to_x, to_y = lax.rem(x + number % 4, 4), lax.rem(y + number // 4 % 4, 4)
        to_core = core if number < 16 else 1 - core
        row = pl.multiple_of(((to_core * 4 + to_y) * 4 + to_x) * 64, 64)
        copy = pltpu.make_async_copy(
            piece_refs[number // 4].at[pl.ds(number % 4 * 64, 64), columns],
            to_ref.at[pl.ds(row, 64)],
            sems.at[number],
        )
        copy.start()
        copies.append(copy)
    return copies


RING_PIECES = [(0, 128), (128, 128), (256, 64), (320, 64), (384, 128)]


def project_kv_kernel(at_ref, *refs):
    x_refs, piece_refs, (cos_ref, sin_ref, kv_ref, whole_ref) = refs[:5], refs[5:13], refs[13:17]
    x_held, held, sems, x_sems = refs[17:]
    copies = []
    for number, (start, size) in enumerate(RING_PIECES):
        copy = pltpu.make_async_copy(x_refs[number], x_held.at[pl.ds(start, size)], x_sems.at[number])
        copy.start()
        copies.append(copy)
    copies += put_in_order(at_ref, piece_refs, pl.ds(512, 128), held, sems)
    for copy in copies:
        copy.wait()
    whole = pltpu.make_async_copy(x_held, whole_ref, x_sems.at[len(RING_PIECES)])
    whole.start()
    flat = dot_nn(x_held[...], held[...])
    turned = turn(flat, cos_ref[...], sin_ref[...])
    kv_ref[...] = jnp.where(lane_is_low(flat.shape, 128), turned, flat).astype(BF16)
    whole.wait()


def project_kv(at, x_pieces, weights, cosine, sine):
    rows, width = 512, x_pieces[0].shape[1]
    vmem, anywhere = pl.BlockSpec(memory_space=pltpu.VMEM), pl.BlockSpec(memory_space=pl.ANY)
    return pl.pallas_call(
        project_kv_kernel,
        out_shape=(jax.ShapeDtypeStruct((rows, 128), BF16), jax.ShapeDtypeStruct((rows, width), BF16)),
        in_specs=[pl.BlockSpec(memory_space=pltpu.SMEM)] + [anywhere] * 13 + [vmem, vmem],
        out_specs=(vmem, anywhere),
        scratch_shapes=[
            pltpu.VMEM((rows, width), BF16),
            pltpu.VMEM((width, 128), BF16),
            pltpu.SemaphoreType.DMA((32,)),
            pltpu.SemaphoreType.DMA((len(RING_PIECES) + 1,)),
        ],
        compiler_params=pltpu.CompilerParams(vmem_limit_bytes=VMEM_LIMIT),
        cost_estimate=pl.CostEstimate(
            flops=2 * rows * width * 128, bytes_accessed=5 * 1024 * 1024, transcendentals=0
        ),
    )(at, *x_pieces, *weights, cosine, sine)


def project_q_kernel(at_ref, x_ref, *refs):
    piece_refs, (cos_ref, sin_ref, q_ref, w_ref, held, sems, sem) = refs[:8], refs[8:]
    for copy in put_in_order(at_ref, piece_refs, pl.ds(0, 640), held, sems):
        copy.wait()
    whole = pltpu.make_async_copy(held, w_ref, sem)
    whole.start()
    cosine, sine, x = cos_ref[...], sin_ref[...], x_ref[...]
    for start in (0, 256):
        wide = dot_nn(x, held[:, start : start + 256])
        for part in (0, 128):
            turned = turn(wide[:, part : part + 128], cosine, sine)
            q_ref[:, start + part : start + part + 128] = (turned * HEAD_SIZE**-0.5).astype(BF16)
    whole.wait()


def project_q(at, normed, weights, cosine, sine):
    rows, width = normed.shape
    vmem, anywhere = pl.BlockSpec(memory_space=pltpu.VMEM), pl.BlockSpec(memory_space=pl.ANY)
    return pl.pallas_call(
        project_q_kernel,
        out_shape=(jax.ShapeDtypeStruct((rows, 512), BF16), jax.ShapeDtypeStruct((width, 640), BF16)),
        in_specs=[pl.BlockSpec(memory_space=pltpu.SMEM), vmem] + [anywhere] * 8 + [vmem, vmem],
        out_specs=(vmem, anywhere),
        scratch_shapes=[
            pltpu.VMEM((width, 640), BF16),
            pltpu.SemaphoreType.DMA((32,)),
            pltpu.SemaphoreType.DMA,
        ],
        compiler_params=pltpu.CompilerParams(vmem_limit_bytes=VMEM_LIMIT),
        cost_estimate=pl.CostEstimate(
            flops=2 * rows * width * 512, bytes_accessed=7 * 1024 * 1024, transcendentals=0
        ),
    )(at, normed, *weights, cosine, sine)


KEYS = 1152
PAIRS = 4


def set_up_kernel(place_ref, kv0_ref, kv1_ref, kv2_ref, kk_ref, vv_ref, kvt_ref):
    place = place_of(place_ref)
    low = lane_is_low((128, 128), 128)
    for block, ref in enumerate((kv0_ref, kv1_ref, kv2_ref)):
        for group in range(4):
            at = pl.multiple_of(lax.rem(group - place + 4, 4) * 128, 128)
            piece = ref[pl.ds(at, 128), :].astype(F32)
            rolled = pltpu.roll(piece, 64, 1)
            to = block * 512 + group * 128
            kk_ref[to : to + 128, :] = jnp.where(low, piece, rolled).astype(BF16)
            vv_ref[to : to + 128, :] = jnp.where(low, rolled, piece).astype(BF16)
            kvt_ref[:, to : to + 128] = piece.T.astype(BF16)


def set_up(place, kv):
    vmem = pl.BlockSpec(memory_space=pltpu.VMEM)
    return pl.pallas_call(
        set_up_kernel,
        out_shape=(
            jax.ShapeDtypeStruct((1536, 128), BF16),
            jax.ShapeDtypeStruct((1536, 128), BF16),
            jax.ShapeDtypeStruct((128, 1536), BF16),
        ),
        in_specs=[pl.BlockSpec(memory_space=pltpu.SMEM), vmem, vmem, vmem],
        out_specs=(vmem, vmem, vmem),
        compiler_params=pltpu.CompilerParams(vmem_limit_bytes=VMEM_LIMIT),
        cost_estimate=pl.CostEstimate(flops=1536 * 128 * 8, bytes_accessed=2 * 1024 * 1024, transcendentals=0),
    )(place, *kv)


def both_heads(pair):
    low = lane_is_low(pair.shape, 128)
    nothing = jnp.zeros_like(pair)
    return jnp.concatenate([jnp.where(low, pair, nothing), jnp.where(low, nothing, pair)], 0)


def side_by_side(transposed):
    return jnp.concatenate([transposed[:, :128], transposed[:, 128:]], 0).T


def mask_of(at, low_ref):
    key = lax.broadcasted_iota(jnp.int32, (KEYS, 128), 0)
    query = lax.broadcasted_iota(jnp.int32, (KEYS, 128), 1)
    seen = (key >= low_ref[:, pl.ds(at, 128)] - at) & (key <= query + WINDOW)
    bias = jnp.where(seen, 0.0, -jnp.inf)
    return jnp.concatenate([bias, bias], 1)


def attend_kernel(
    first, step, place_ref, q_ref, kk_ref, kvt_ref, low_ref, w_ref, o_ref, lse_ref, *refs
):
    part_refs, (bias, held, w_held, sem) = refs[:-4], refs[-4:]
    group = lax.rem(place_of(place_ref) + first + step * pl.program_id(0), 4)
    at = pl.multiple_of(group * 128, 128)

    load = pltpu.make_async_copy(w_ref.at[:, pl.ds(HIDDEN, 512)], w_held, sem)

    @pl.when((pl.program_id(0) == 0) & (pl.program_id(1) == 0))
    def _():
        load.start()

    @pl.when(pl.program_id(1) == 0)
    def _():
        bias[...] = mask_of(at, low_ref)

    keys = pl.ds(at, KEYS)
    for number in range(PAIRS):
        columns = slice(128 * number, 128 * number + 128)
        scores = dot_nt(kk_ref[keys, :], both_heads(q_ref[:, columns])) + bias[...]
        top = jnp.max(scores, 0, keepdims=True)
        weights = jnp.exp(scores - top)
        total = jnp.sum(weights, 0, keepdims=True)
        result = dot_nn(kvt_ref[64:128, keys], weights.astype(BF16)) / total
        lse_ref[0, number] = top + jnp.log(total)
        result = side_by_side(result).astype(BF16)
        o_ref[:, columns] = result
        held[PAIRS * pl.program_id(1) + number] = result

    @pl.when(pl.program_id(1) == 4 // PAIRS - 1)
    def _():
        @pl.when(pl.program_id(0) == 0)
        def _():
            load.wait()

        rows = jnp.concatenate([held[k] for k in range(4)], 1)
        part = dot_nt(rows, w_held[...]).astype(BF16)
        for number, ref in enumerate(part_refs):

            @pl.when(pl.program_id(0) == number)
            def _():
                ref[...] = part


def attend(first, step, count, place, queries, kk, kvt, low, weights):
    whole = lambda g, p, s: (0, 0)
    width = 128 * PAIRS
    grid = pltpu.PrefetchScalarGridSpec(
        num_scalar_prefetch=1,
        grid=(count, 4 // PAIRS),
        in_specs=[
            pl.BlockSpec((128, width), lambda g, p, s: (first + step * g, p)),
            pl.BlockSpec((1536, 128), whole),
            pl.BlockSpec((128, 1536), whole),
            pl.BlockSpec((1, 512), whole),
            pl.BlockSpec(memory_space=pl.ANY),
        ],
        out_specs=(
            pl.BlockSpec((128, width), lambda g, p, s: (g, p)),
            pl.BlockSpec((1, PAIRS, 1, 256), lambda g, p, s: (g, p, 0, 0)),
        )
        + (pl.BlockSpec((128, 2048), whole),) * count,
        scratch_shapes=[
            pltpu.VMEM((KEYS, 256), F32),
            pltpu.VMEM((4, 128, 128), BF16),
            pltpu.VMEM((2048, 512), BF16),
            pltpu.SemaphoreType.DMA,
        ],
    )
    return pl.pallas_call(
        functools.partial(attend_kernel, first, step),
        grid_spec=grid,
        out_shape=(
            jax.ShapeDtypeStruct((128 * count, 512), BF16),
            jax.ShapeDtypeStruct((count, 4, 1, 256), F32),
        )
        + (jax.ShapeDtypeStruct((128, 2048), BF16),) * count,
        compiler_params=pltpu.CompilerParams(vmem_limit_bytes=VMEM_LIMIT),
        cost_estimate=pl.CostEstimate(
            flops=count * 4 * KEYS * 256 * 256 * 2,
            bytes_accessed=3 * 1024 * 1024,
            transcendentals=count * 4 * KEYS * 256,
        ),
    )(place, queries, kk, kvt, low, weights)


def attend_back_kernel(first, step, count, *refs):
    last = first == 2
    place_ref, q_ref, w_ref, lse_ref, kk_ref, vv_ref, kvt_ref, low_ref, cos_ref, sin_ref = refs[:10]
    o_ref = refs[10]
    dh_refs, refs = refs[11 : 11 + count], refs[11 + count :]
    dk_in = dv_in = None
    if first > 0:
        dk_in, dv_in, refs = refs[0], refs[1], refs[2:]
    bias, do_held, dk, dv, w_held, sem = refs[-6:]
    dq_ref, outs = refs[0], refs[1:-6]
    number, pair = pl.program_id(0), pl.program_id(1)
    place = place_of(place_ref)
    at = pl.multiple_of(lax.rem(place + first + step * number, 4) * 128, 128)

    load = pltpu.make_async_copy(w_ref.at[:, pl.ds(HIDDEN, 512)], w_held, sem)

    @pl.when((number == 0) & (pair == 0))
    def _():
        load.start()
        dk[...] = jnp.zeros_like(dk) if dk_in is None else dk_in[...]
        dv[...] = jnp.zeros_like(dv) if dv_in is None else dv_in[...]

    @pl.when(pair == 0)
    def _():
        bias[...] = mask_of(at, low_ref)

        @pl.when(number == 0)
        def _():
            load.wait()

        for k, ref in enumerate(dh_refs):

            @pl.when(number == k)
            def _():
                do_rows = dot_nn(ref[...], w_held[...]).astype(BF16)
                for p in range(4):
                    do_held[p] = do_rows[:, 128 * p : 128 * p + 128]

    keys = pl.ds(at, KEYS)
    queries, grads, all_weights, all_grad_scores = [], [], [], []
    for k in range(PAIRS):
        columns = slice(128 * k, 128 * k + 128)
        do_pair = do_held[PAIRS * pair + k]
        query, grad = both_heads(q_ref[:, columns]), both_heads(do_pair)
        scores = dot_nt(kk_ref[keys, :], query) + bias[...]
        weights = jnp.exp(scores - lse_ref[0, k])
        grad_weights = dot_nt(vv_ref[keys, :], grad)
        product = (o_ref[:, columns].astype(F32) * do_pair.astype(F32)).T
        inner = jnp.concatenate(
            [jnp.sum(product[:64], 0, keepdims=True), jnp.sum(product[64:], 0, keepdims=True)], 1
        )
        grad_scores = (weights * (grad_weights - inner)).astype(BF16)
        grad_query = side_by_side(dot_nn(kvt_ref[0:64, keys], grad_scores)) * HEAD_SIZE**-0.5
        dq_ref[:, columns] = turn(grad_query, cos_ref[...], -sin_ref[...]).astype(BF16)
        queries.append(query)
        grads.append(grad)
        all_weights.append(weights.astype(BF16))
        all_grad_scores.append(grad_scores)
    join = lambda values, axis: values[0] if PAIRS == 1 else jnp.concatenate(values, axis)
    dv[keys, :] += dot_nn(join(all_weights, 1), join(grads, 0))
    dk[keys, :] += dot_nn(join(all_grad_scores, 1), join(queries, 0))

    @pl.when((number == pl.num_programs(0) - 1) & (pair == 4 // PAIRS - 1))
    def _():
        if not last:
            outs[0][...], outs[1][...] = dk[...], dv[...]
            return
        half = lane_is_low((128, 128), 128)
        for block in range(3):
            for group in range(4):
                to = pl.multiple_of(lax.rem(group - place + 4, 4) * 128, 128)
                frm = slice(block * 512 + group * 128, block * 512 + group * 128 + 128)
                key, value = dk[frm, :], dv[frm, :]
                key = key + pltpu.roll(key, 64, 1)
                value = value + pltpu.roll(value, 64, 1)
                both = jnp.where(half, key, value)
                outs[block][pl.ds(to, 128), :] = both.astype(outs[block].dtype)


def attend_back(first, step, count, place, queries, o, dh, weights, lse, kk, vv, kvt, low, cosine, sine, held):
    last = first == 2
    whole = lambda g, p, s: (0, 0)
    specs = [
        pl.BlockSpec((128, 128 * PAIRS), lambda g, p, s: (first + step * g, p)),
        pl.BlockSpec(memory_space=pl.ANY),
        pl.BlockSpec((1, PAIRS, 1, 256), lambda g, p, s: (g, p, 0, 0)),
        pl.BlockSpec((1536, 128), whole),
        pl.BlockSpec((1536, 128), whole),
        pl.BlockSpec((128, 1536), whole),
        pl.BlockSpec((1, 512), whole),
        pl.BlockSpec((128, 128), lambda g, p, s: (first + step * g, 0)),
        pl.BlockSpec((128, 128), lambda g, p, s: (first + step * g, 0)),
    ]
    specs += [pl.BlockSpec((128, 128 * PAIRS), lambda g, p, s: (g, p))]
    specs += [pl.BlockSpec((128, 2048), whole)] * count + [pl.BlockSpec((1536, 128), whole)] * len(held)
    if last:
        out_specs = (pl.BlockSpec((512, 128), whole),) * 3
        out_shape = tuple(jax.ShapeDtypeStruct((512, 128), dtype) for dtype in (BF16, BF16, F32))
    else:
        out_specs = (pl.BlockSpec((1536, 128), whole),) * 2
        out_shape = (jax.ShapeDtypeStruct((1536, 128), F32),) * 2
    grid = pltpu.PrefetchScalarGridSpec(
        num_scalar_prefetch=1,
        grid=(count, 4 // PAIRS),
        in_specs=specs,
        out_specs=(pl.BlockSpec((128, 128 * PAIRS), lambda g, p, s: (g, p)),) + out_specs,
        scratch_shapes=[
            pltpu.VMEM((KEYS, 256), F32),
            pltpu.VMEM((4, 128, 128), BF16),
            pltpu.VMEM((1536, 128), F32),
            pltpu.VMEM((1536, 128), F32),
            pltpu.VMEM((2048, 512), BF16),
            pltpu.SemaphoreType.DMA,
        ],
    )
    return pl.pallas_call(
        functools.partial(attend_back_kernel, first, step, count),
        grid_spec=grid,
        out_shape=(jax.ShapeDtypeStruct((128 * count, 512), BF16),) + out_shape,
        compiler_params=pltpu.CompilerParams(vmem_limit_bytes=VMEM_LIMIT),
        cost_estimate=pl.CostEstimate(
            flops=count * 4 * KEYS * 256 * 640 * 2,
            bytes_accessed=6 * 1024 * 1024,
            transcendentals=count * 4 * KEYS * 256,
        ),
    )(place, queries, weights, lse, kk, vv, kvt, low, cosine, sine, o, *dh, *held)


GROUPS = [(0, 128), (128, 256), (384, 512), (896, 512)]


def columns_times_kernel(left_ref, right_ref, out_ref, left, right, out, sems, out_sems):
    load = pltpu.make_async_copy(left_ref, left, sems.at[len(GROUPS)])
    load.start()
    copies, results = [], []
    for number, (start, width) in enumerate(GROUPS):
        columns = pl.ds(start, width)
        copy = pltpu.make_async_copy(right_ref.at[:, columns], right.at[:, columns], sems.at[number])
        copy.start()
        copies.append(copy)
    load.wait()
    value = left[...]
    for number, (start, width) in enumerate(GROUPS):
        copies[number].wait()
        out[:, start : start + width] = dot_nn(value, right[:, start : start + width]).astype(BF16)
        columns = pl.ds(start, width)
        copy = pltpu.make_async_copy(out.at[:, columns], out_ref.at[:, columns], out_sems.at[number])
        copy.start()
        results.append(copy)
    for copy in results:
        copy.wait()


def columns_times(left, right):
    rows, width = left.shape
    anywhere = pl.BlockSpec(memory_space=pl.ANY)
    return pl.pallas_call(
        columns_times_kernel,
        out_shape=jax.ShapeDtypeStruct((rows, HIDDEN), BF16),
        in_specs=[anywhere, anywhere],
        out_specs=anywhere,
        scratch_shapes=[
            pltpu.VMEM((rows, width), BF16),
            pltpu.VMEM((width, HIDDEN), BF16),
            pltpu.VMEM((rows, HIDDEN), BF16),
            pltpu.SemaphoreType.DMA((len(GROUPS) + 1,)),
            pltpu.SemaphoreType.DMA((len(GROUPS),)),
        ],
        compiler_params=pltpu.CompilerParams(vmem_limit_bytes=VMEM_LIMIT),
        cost_estimate=pl.CostEstimate(
            flops=2 * rows * width * HIDDEN, bytes_accessed=11 * 1024 * 1024, transcendentals=0
        ),
    )(left, right)


PIECES = [(0, 128), (128, 128), (256, 128), (384, 128)]


def ffn_kernel(*refs):
    core_ref, x_refs, dact_ref, w_ref = refs[0], refs[1:9], refs[9], refs[10]
    gua_ref, whole_ref, swap_ref, dx_refs = refs[11], refs[12], refs[13], refs[14:18]
    x_held, dact_held, w_held, gua, dx, sems, out_sems = refs[18:]
    x_copies = []
    for number in range(8):
        copy = pltpu.make_async_copy(
            x_refs[number], x_held.at[pl.ds(64 * number, 64)], sems.at[12 + number]
        )
        copy.start()
        x_copies.append(copy)
    copies = []
    for number, (start, width) in enumerate(GROUPS):
        for part in range(3):
            if part < 2:
                columns = pl.ds(part * HIDDEN + start, width)
                copy = pltpu.make_async_copy(
                    w_ref.at[:, columns], w_held.at[:, columns], sems.at[3 * number + part]
                )
            else:
                columns = pl.ds(start, width)
                copy = pltpu.make_async_copy(
                    dact_ref.at[:, columns], dact_held.at[:, columns], sems.at[3 * number + part]
                )
            copy.start()
            copies.append(copy)
    for copy in x_copies:
        copy.wait()
    half = pl.multiple_of((1 - core_of(core_ref)) * 1024, 1024)
    results = [
        pltpu.make_async_copy(x_held, whole_ref, out_sems.at[5]),
        pltpu.make_async_copy(x_held.at[:, pl.ds(half, 1024)], swap_ref, out_sems.at[6]),
    ]
    for copy in results:
        copy.start()
    x = x_held[...]
    for number, (start, width) in enumerate(GROUPS):
        for part in range(3):
            copies[3 * number + part].wait()
        gate = dot_nn(x, w_held[:, start : start + width])
        up = dot_nn(x, w_held[:, HIDDEN + start : HIDDEN + start + width])
        dact = dact_held[:, start : start + width].astype(F32)
        sig = jax.nn.sigmoid(gate)
        silu = gate * sig
        dgate = dact * up * (sig * (1.0 + gate * (1.0 - sig)))
        gua[:, start : start + width] = dgate.astype(BF16)
        gua[:, HIDDEN + start : HIDDEN + start + width] = (dact * silu).astype(BF16)
        gua[:, 2 * HIDDEN + start : 2 * HIDDEN + start + width] = (silu * up).astype(BF16)
    copy = pltpu.make_async_copy(gua, gua_ref, out_sems.at[4])
    copy.start()
    results.append(copy)
    dgu = gua[:, : 2 * HIDDEN]
    for number in range(4):
        columns = slice(512 * number, 512 * number + 512)
        dx[:, columns] = dot_nt(dgu, w_held[columns, : 2 * HIDDEN]).astype(BF16)
        for piece, (start, size) in enumerate(PIECES):
            copy = pltpu.make_async_copy(
                dx.at[pl.ds(start, size), pl.ds(512 * number, 512)],
                dx_refs[piece].at[:, pl.ds(512 * number, 512)],
                out_sems.at[7 + 4 * number + piece],
            )
            copy.start()
            results.append(copy)
    for copy in results:
        copy.wait()


def ffn(core, pieces, dact, weights):
    rows, width = dact.shape[0], weights.shape[0]
    anywhere = pl.BlockSpec(memory_space=pl.ANY)
    result = pl.pallas_call(
        ffn_kernel,
        out_shape=(
            jax.ShapeDtypeStruct((rows, 3 * HIDDEN), BF16),
            jax.ShapeDtypeStruct((rows, width), BF16),
            jax.ShapeDtypeStruct((rows, width // 2), BF16),
            *(jax.ShapeDtypeStruct((size, width), BF16) for _, size in PIECES),
        ),
        in_specs=[pl.BlockSpec(memory_space=pltpu.SMEM)] + [anywhere] * 10,
        out_specs=(anywhere,) * 7,
        scratch_shapes=[
            pltpu.VMEM((rows, width), BF16),
            pltpu.VMEM((rows, HIDDEN), BF16),
            pltpu.VMEM((width, 2 * HIDDEN), BF16),
            pltpu.VMEM((rows, 3 * HIDDEN), BF16),
            pltpu.VMEM((rows, width), BF16),
            pltpu.SemaphoreType.DMA((20,)),
            pltpu.SemaphoreType.DMA((23,)),
        ],
        compiler_params=pltpu.CompilerParams(vmem_limit_bytes=VMEM_LIMIT),
        cost_estimate=pl.CostEstimate(
            flops=8 * rows * width * HIDDEN,
            bytes_accessed=25 * 1024 * 1024,
            transcendentals=rows * HIDDEN,
        ),
    )(core, *pieces, dact, weights)
    return result[0], result[1], result[2], result[3:]


def weight_grads_kernel(core_ref, x_ref, x2_ref, dy_ref, dy2_ref, right_ref, right2_ref, out_ref, dy, dy2, sems):
    part = pl.program_id(0)
    half = dy.shape[1]
    start = pl.multiple_of(core_of(core_ref) * half, half)
    loads = (
        pltpu.make_async_copy(dy_ref.at[:, pl.ds(start, half)], dy, sems.at[0]),
        pltpu.make_async_copy(dy2_ref, dy2, sems.at[1]),
    )

    @pl.when(part == 0)
    def _():
        for load in loads:
            load.start()

    @pl.when(part < 2)
    def _():
        total = dot_tn(x_ref[...], right_ref[...]) + dot_tn(x2_ref[...], right2_ref[...])
        out_ref[...] = total.astype(BF16)

    @pl.when(part == 2)
    def _():
        for load in loads:
            load.wait()
        total = dot_tn(dy[...], right_ref[...]) + dot_tn(dy2[...], right2_ref[...])
        out_ref[...] = total.astype(BF16)


def weight_grads(core, x, x2, dy, dy2, right, right2):
    rows, half = x2.shape
    anywhere = pl.BlockSpec(memory_space=pl.ANY)
    side = lambda j, c: (0, j)
    grid = pltpu.PrefetchScalarGridSpec(
        num_scalar_prefetch=1,
        grid=(3,),
        in_specs=[
            pl.BlockSpec((rows, half), lambda j, c: (0, core_of(c))),
            pl.BlockSpec((rows, half), lambda j, c: (0, 0)),
            anywhere,
            anywhere,
            pl.BlockSpec((rows, HIDDEN), side),
            pl.BlockSpec((rows, HIDDEN), side),
        ],
        out_specs=pl.BlockSpec((half, HIDDEN), side),
        scratch_shapes=[
            pltpu.VMEM((rows, half), BF16),
            pltpu.VMEM((rows, half), BF16),
            pltpu.SemaphoreType.DMA((2,)),
        ],
    )
    return pl.pallas_call(
        weight_grads_kernel,
        grid_spec=grid,
        out_shape=jax.ShapeDtypeStruct((half, 3 * HIDDEN), BF16),
        compiler_params=pltpu.CompilerParams(vmem_limit_bytes=VMEM_LIMIT),
        cost_estimate=pl.CostEstimate(
            flops=2 * 3 * 2 * rows * half * HIDDEN, bytes_accessed=24 * 1024 * 1024, transcendentals=0
        ),
    )(core, x, x2, dy, dy2, right, right2)


def rows_times_kernel(left_ref, right_ref, *out_refs):
    result = dot_nt(left_ref[...], right_ref[...]).astype(BF16)
    for number, ref in enumerate(out_refs):
        ref[...] = result[128 * number : 128 * number + 128]


def rows_times(left, left_part, right, part):
    rows, depth = left.shape[0], HIDDEN
    width = right.shape[0]
    tile = 512
    return pl.pallas_call(
        rows_times_kernel,
        out_shape=(jax.ShapeDtypeStruct((128, width), BF16),) * 4,
        grid=(width // tile,),
        in_specs=[
            pl.BlockSpec((rows, depth), lambda i: (0, left_part)),
            pl.BlockSpec((tile, depth), lambda i: (i, part)),
        ],
        out_specs=(pl.BlockSpec((128, tile), lambda i: (0, i)),) * 4,
        compiler_params=pltpu.CompilerParams(vmem_limit_bytes=VMEM_LIMIT),
        cost_estimate=pl.CostEstimate(
            flops=2 * rows * depth * width,
            bytes_accessed=2 * (rows * depth + width * depth + rows * width),
            transcendentals=0,
        ),
    )(left, right)


def ring_rows(own, near, far):
    return jnp.concatenate([own, near[:128], far, near[128:]], 0)


def put_half(number, value, other_ref, own_ref):
    @pl.when(number < 2)
    def _():
        other_ref[...] = value

    @pl.when(number >= 2)
    def _():
        own_ref[...] = value


def tile_at(i, c):
    return lax.rem(i + 2 * (1 - core_of(c)), 4)


def half_specs(tile, columns):
    return (
        pl.BlockSpec((tile, columns), lambda i, c: (jnp.minimum(i, 1), 0)),
        pl.BlockSpec((tile, columns), lambda i, c: (jnp.maximum(i - 2, 0), 0)),
    )


def wide_grads_kernel(
    core_ref, x_ref, dh0, dh1, dh2, dh3, o0, o1, o2, dq0, dq1, dq2, other_ref, own_ref, o_held, dq_held
):
    number = pl.program_id(0)

    @pl.when(number == 0)
    def _():
        o_held[...] = ring_rows(o0[...], o1[...], o2[...])
        dq_held[...] = ring_rows(dq0[...], dq1[...], dq2[...])

    dh = jnp.concatenate([ref[...] for ref in (dh0, dh1, dh2, dh3)], 0)
    out = dot_tn(dh, o_held[...])
    query = dot_tn(x_ref[...], dq_held[...])
    put_half(number, jnp.concatenate([out, query], 1).astype(BF16), other_ref, own_ref)


def wide_grads(core, normed, dh, o, dq):
    rows, width = normed.shape
    tile = 512
    whole = lambda i, c: (0, 0)
    column = lambda i, c: (0, tile_at(i, c))
    small = [pl.BlockSpec((size, 512), whole) for size in (128, 256, 128)]
    grid = pltpu.PrefetchScalarGridSpec(
        num_scalar_prefetch=1,
        grid=(4,),
        in_specs=[pl.BlockSpec((rows, tile), column)]
        + [pl.BlockSpec((128, tile), column)] * 4
        + small
        + small,
        out_specs=half_specs(tile, 1024),
        scratch_shapes=[pltpu.VMEM((rows, 512), BF16), pltpu.VMEM((rows, 512), BF16)],
    )
    return pl.pallas_call(
        wide_grads_kernel,
        grid_spec=grid,
        out_shape=(jax.ShapeDtypeStruct((width // 2, 1024), BF16),) * 2,
        compiler_params=pltpu.CompilerParams(vmem_limit_bytes=VMEM_LIMIT),
        cost_estimate=pl.CostEstimate(
            flops=2 * rows * width * 1024, bytes_accessed=10 * 1024 * 1024, transcendentals=0
        ),
    )(core, normed, *dh, *o, *dq)


def finish_kernel(
    core_ref,
    x_ref,
    w_ref,
    dq0_ref,
    dq1_ref,
    dq2_ref,
    own_ref,
    one_ref,
    two_ref,
    cos_ref,
    sin_ref,
    norm_ref,
    second_ref,
    other_grad_ref,
    own_grad_ref,
    dx_ref,
    gain_ref,
    dqkv,
    sums,
):
    number = pl.program_id(0)

    @pl.when(number == 0)
    def _():
        dqkv[:, :512] = ring_rows(dq0_ref[...], dq1_ref[...], dq2_ref[...])
        dkv = own_ref[...] + one_ref[...].astype(F32) + two_ref[...].astype(F32)
        turned = turn(dkv, cos_ref[...], -sin_ref[...])
        dqkv[:, 512:] = jnp.where(lane_is_low(dkv.shape, 128), turned, dkv).astype(BF16)

    x = x_ref[...]
    put_half(number, dot_tn(x, dqkv[:, 512:]).astype(BF16), other_grad_ref, own_grad_ref)
    dx = dot_nt(dqkv[...], w_ref[...])
    for piece in range(4):
        row = pl.multiple_of(lax.rem(place_of(core_ref) + piece, 4) * 128, 128)
        dx_ref[pl.ds(row, 128), :] = dx[128 * piece : 128 * piece + 128].astype(BF16)
    columns = pl.ds(pl.multiple_of(tile_at(number, core_ref) * 512, 512), 512)
    sums[:, columns] = jnp.broadcast_to(
        jnp.sum(dx * x.astype(F32), 0, keepdims=True) / norm_ref[:1], (8, 512)
    )

    @pl.when(number == 3)
    def _():
        gain_ref[:8] = gain_rows(to_blocks(sums[...])[:1])
        gain_ref[8:] = gain_rows(second_ref[:1])


def finish(core, normed, weights, dq, own, one, two, cosine, sine, gain, second):
    rows, width = normed.shape
    tile = 512
    whole = lambda i, c: (0, 0)
    column = lambda i, c: (0, tile_at(i, c))
    narrow = pl.BlockSpec((rows, 128), whole)
    grid = pltpu.PrefetchScalarGridSpec(
        num_scalar_prefetch=1,
        grid=(4,),
        in_specs=[
            pl.BlockSpec((rows, tile), column),
            pl.BlockSpec((tile, 640), lambda i, c: (tile_at(i, c), 0)),
            pl.BlockSpec((128, 512), whole),
            pl.BlockSpec((256, 512), whole),
            pl.BlockSpec((128, 512), whole),
            narrow,
            narrow,
            narrow,
            narrow,
            narrow,
            pl.BlockSpec((2, tile), column),
            pl.BlockSpec((8, width), whole),
        ],
        out_specs=half_specs(tile, 128)
        + (pl.BlockSpec((rows, tile), column),)
        + (pl.BlockSpec((GAIN_ROWS, GAIN_COLUMNS), whole),),
        scratch_shapes=[pltpu.VMEM((rows, 640), BF16), pltpu.VMEM((8, width), F32)],
    )
    result = pl.pallas_call(
        finish_kernel,
        grid_spec=grid,
        out_shape=(jax.ShapeDtypeStruct((width // 2, 128), BF16),) * 2
        + (jax.ShapeDtypeStruct((rows, width), BF16),)
        + (jax.ShapeDtypeStruct((GAIN_ROWS, GAIN_COLUMNS), F32),),
        compiler_params=pltpu.CompilerParams(vmem_limit_bytes=VMEM_LIMIT),
        cost_estimate=pl.CostEstimate(
            flops=2 * rows * width * 768, bytes_accessed=10 * 1024 * 1024, transcendentals=0
        ),
    )(core, normed, weights, *dq, own, one, two, cosine, sine, gain, second)
    return result


def per_device(
    tokens,
    segments,
    w_query,
    key_projection,
    value_projection,
    w_out,
    w_gate,
    w_up,
    w_down,
    norm_attn,
    norm_ffn,
    cotangent,
):
    place, core = lax.axis_index("head"), lax.axis_index("core")
    block = (lax.axis_index("y") * 4 + lax.axis_index("x")) * 2 + core
    code = (((lax.axis_index("x") * 4 + lax.axis_index("y")) * 2 + core) * 4 + place).astype(jnp.int32)
    code = code.reshape(1)
    keep = lax.optimization_barrier


    out_weights = lax.all_gather(
        jnp.concatenate([w_down.T, w_out.T], 1), CORE_FIRST, axis=0, tiled=True
    )
    ffn_weights = lax.all_gather(jnp.concatenate([w_gate, w_up], 1), CORE_FIRST, axis=0, tiled=True)

    x_rows, dy_rows, normed_rows, gains = prepare(
        tokens[0], cotangent[0], jnp.stack([norm_attn, norm_ffn]).astype(F32)
    )
    row = jnp.arange(512, dtype=jnp.int32)
    positions = block * 512 + ((row // 128 + place) % 4) * 128 + row % 128
    frequency = 10000.0 ** (-jnp.arange(32, dtype=F32) * 2.0 / HEAD_SIZE)
    angles = positions.astype(F32)[:, None] * frequency[None, :]
    cosine, sine = jnp.cos(angles), jnp.sin(angles)
    cosine = jnp.concatenate([cosine] * 4, 1)
    sine = jnp.concatenate([-sine, sine, -sine, sine], 1)

    flat = segments.reshape(-1)
    padded = jnp.concatenate([jnp.full((1024,), -1, jnp.int32), flat])
    own = lax.dynamic_slice_in_dim(flat, block * 512, 512, 0)
    window = lax.dynamic_slice_in_dim(padded, block * 512, 1536, 0)
    start = jnp.sum((window[None, :] < own[:, None]).astype(jnp.int32), 1)
    low = jnp.maximum(start, row + 1).reshape(1, 512)

    normed_rows, w_query = keep((normed_rows, w_query))
    ahead, behind = near_pieces(normed_rows)
    qkv_own = gather_axis(jnp.concatenate([w_query, key_projection, value_projection], 1), "x")
    qkv_own = gather_axis(jnp.concatenate(qkv_own, 0), "y")
    far = far_pieces(ahead, behind)
    qkv_own, far, cosine, sine, low = keep((qkv_own, far, cosine, sine, low))
    qkv_pieces = *qkv_own, *(shift(piece, "core", 1) for piece in qkv_own)
    kv_own, normed_one = project_kv(code, (normed_rows, ahead, *far, behind), qkv_pieces, cosine, sine)
    normed_late, kv_own, dy_raw = keep((normed_one, kv_own, cotangent[0]))
    dy_pieces = gather_pieces(dy_raw)
    kv = (from_block(kv_own, 2), from_block(kv_own, 1), kv_own)
    queries, qkv_weights = project_q(code, normed_late, qkv_pieces, cosine, sine)

    kk, vv, kvt = set_up(code, kv)
    seen = code, queries, kk, kvt, low, out_weights
    o_far, lse_far, part_far = attend(2, 1, 1, *seen)
    queries, part_far, dy_pieces = keep((queries, part_far, dy_pieces))
    part_far = shift(part_far, "head", 2)
    seen = code, queries, kk, kvt, low, out_weights
    o_near, lse_near, part_ahead, part_behind = attend(1, 2, 2, *seen)
    queries, part_far, part_ahead, part_behind = keep((queries, part_far, part_ahead, part_behind))
    seen = code, queries, kk, kvt, low, out_weights
    o_own, lse_own, part_own = attend(0, 1, 1, *seen)
    dy, dy_swap = assemble(code, dy_rows, *dy_pieces)
    dy_other = shift(dy_swap, "core", 1)
    attention_sum = part_own, shift(part_ahead, "head", 1), shift(part_behind, "head", -1), part_far
    h1, top, bottom = join(x_rows, gains, attention_sum)
    behind_top, ahead_bottom = shift(top, "head", 1), shift(bottom, "head", -1)
    ahead_top, behind_bottom = shift(top, "head", -1), shift(bottom, "head", 1)
    behind_top, ahead_bottom, dy = keep((behind_top, ahead_bottom, dy))
    far_top, far_bottom = shift(behind_top, "head", 1), shift(ahead_bottom, "head", -1)
    rows_two = top, bottom, ahead_top, ahead_bottom, far_top, far_bottom, behind_top, behind_bottom
    dact = columns_times(dy, out_weights)
    dact, dy_other = keep((dact, dy_other))

    gua, normed_two, normed_two_swap, dnormed_two = ffn(
        code, rows_two, dact, ffn_weights
    )
    dnormed_two = scatter_pieces(*dnormed_two)
    gua_other = shift(gua, "core", 1)
    normed_two_other = shift(normed_two_swap, "core", 1)
    out_pieces = rows_times(gua, 2, out_weights, 0)
    gua_other, normed_two_other, out_pieces = keep((gua_other, normed_two_other, out_pieces))
    held = weight_grads(code, normed_two, normed_two_other, dy, dy_other, gua, gua_other)
    held, dnormed_two = keep((held, dnormed_two))
    grads = lax.psum_scatter(held, ("y", "x"), scatter_dimension=0, tiled=True)

    dh1, dh1_low, grad_gain_two = join_back(h1, dy_rows, gains, dnormed_two)
    back = kk, vv, kvt, low, cosine, sine
    dq_own, dk, dv = attend_back(0, 1, 1, code, queries, o_own, (dh1_low,), out_weights, lse_own, *back, ())
    ahead, behind = shift(dh1_low, "head", -1), shift(dh1_low, "head", 1)
    ahead, behind, dk, dv, dh1_late, out_pieces = keep((ahead, behind, dk, dv, dh1_low, out_pieces))
    far = shift(dh1_late, "head", 2)
    dq_near, dk, dv = attend_back(
        1, 2, 2, code, queries, o_near, (ahead, behind), out_weights, lse_near, *back, (dk, dv)
    )
    far, dk, dv, out_pieces = keep((far, dk, dv, out_pieces))
    out_pieces = scatter_pieces(*out_pieces)
    dq_far, dkv_first, dkv_second, dkv_own = attend_back(
        2, 1, 1, code, queries, o_far, (far,), out_weights, lse_far, *back, (dk, dv)
    )
    dq = dq_own, dq_near, dq_far
    dkv_one = from_block(dkv_second, -1)
    dkv_two = from_block(dkv_first, -2)
    wide_other, wide_own = wide_grads(
        code, normed_one, (dh1_low, ahead, far, behind), (o_own, o_near, o_far), dq
    )
    dkv_one, dkv_two, wide_other, out_pieces = keep((dkv_one, dkv_two, wide_other, out_pieces))
    wide_other = shift(wide_other, "core", 1)

    narrow_other, narrow_own, dnormed_one, gain_grads = finish(
        code,
        normed_one,
        qkv_weights,
        dq,
        dkv_own,
        dkv_one,
        dkv_two,
        cosine,
        sine,
        gains,
        grad_gain_two,
    )
    dnormed_one = lax.psum_scatter(dnormed_one, "head", scatter_dimension=0, tiled=True)
    gain_grads = exchange([gain_grads] * 4, "head")
    rows = [(x_rows.shape, BF16)]
    (output,) = small_call(output_kernel, rows, h1, *out_pieces)
    gain_grads, output = keep((gain_grads, output))
    pieces, out_sums = first_pieces(
        code, wide_own, wide_other, narrow_own, shift(narrow_other, "core", 1), gain_grads
    )
    grads = (
        grads[:, :HIDDEN].astype(F32),
        grads[:, HIDDEN : 2 * HIDDEN].astype(F32),
        grads[:, 2 * HIDDEN :].T.astype(F32),
    )
    pieces, out_sums, grads = keep((exchange(pieces, "x"), exchange(out_sums, "y"), grads))
    pieces, out_sums = second_pieces(code, pieces, out_sums)
    (grad_inputs,) = small_call(input_grad_kernel, rows, dh1, x_rows, gains, dnormed_one)
    pieces, out_sums, grad_inputs = keep((exchange(pieces, "y"), exchange(out_sums, "x"), grad_inputs))
    (gain_grads,) = small_call(gains_kernel, [((GAIN_ROWS, GAIN_COLUMNS), F32)], *pieces)
    columns = (64, 512), (64, 512), (64, 64), (64, 64), (1, 2048), (1, 2048)
    grad_out, grad_query, grad_key, grad_value, grad_gain_one, grad_gain_two = small_call(
        attention_grads_kernel,
        [(shape, F32) for shape in columns],
        *pieces,
        *out_sums,
        gain_grads,
        shift(gain_grads, "core", 1),
    )

    return (
        output[None],
        grad_inputs[None],
        grad_query,
        grad_key,
        grad_value,
        grad_out.T,
        *grads,
        grad_gain_one.reshape(2048),
        grad_gain_two.reshape(2048),
    )


def solution(mesh):
    grid = Mesh(mesh.devices.reshape(4, 4, 4, 2), ("head", "y", "x", "core"))
    rows, up, down = P(BLK, "head", None), P(BLK, "head"), P("head", BLK)
    return jax.shard_map(
        per_device,
        mesh=grid,
        in_specs=(rows, P(), up, up, up, down, up, up, down, P(), P(), rows),
        out_specs=(rows, rows, up, up, up, down, up, up, down, P(), P()),
        check_vma=False,
    )
```
